32 devices in a mesh: dp: 2 (over core), context: 4 (over y, x), expert: 4 (over z).
Axes of the slice: x: 2, y: 2, z: 4, core: 2. Of those that a mesh axis runs over, the one named last changes fastest.
Arguments:
- layer_input: bfloat16 [2, 2048, 2048], P('dp', ('context', 'expert')), may hold values from -6 to 6
- grad_output: bfloat16 [2, 2048, 2048], P('dp', ('context', 'expert')), may hold values from -6 to 6
- attn_gain: float32 [2048], replicated, may hold values from 0.5 to 1.5
- query_weight: bfloat16 [2048, 4096], P(None, 'expert'), may hold values from -0.125 to 0.125
- key_weight: bfloat16 [2048, 512], P(None, 'expert'), may hold values from -0.125 to 0.125
- value_weight: bfloat16 [2048, 512], P(None, 'expert'), may hold values from -0.125 to 0.125
- q_gain: float32 [128], replicated, may hold values from 0.25 to 1.75
- k_gain: float32 [128], replicated, may hold values from 0.25 to 1.75
- output_weight: bfloat16 [4096, 2048], P('expert'), may hold values from -1.75 to 1.75
- mlp_gain: float32 [2048], replicated, may hold values from 0.5 to 1.5
- router: bfloat16 [2048, 32], replicated, may hold values from -0.0625 to 0.0625
- w_gate: bfloat16 [32, 2048, 768], P(('dp', 'context', 'expert')), may hold values from -0.125 to 0.125
- w_up: bfloat16 [32, 2048, 768], P(('dp', 'context', 'expert')), may hold values from -0.125 to 0.125
- w_down: bfloat16 [32, 768, 2048], P(('dp', 'context', 'expert')), may hold values from -0.875 to 0.875
- routes: int32 [2, 2048, 8], P('dp', ('context', 'expert')), may hold values from 0 to 31, all different within a row; in each aligned block of 128 rows (0 to 127, 128 to 255, ..., all dimensions but the last counted through in order) at most 36 rows name the same one
- half_order: int32 [8], replicated, may hold values from 0 to 7, each once
Outputs:
- layer_output: bfloat16 [2, 2048, 2048], P('dp', ('context', 'expert'))
- grad_input: float32 [2, 2048, 2048], P('dp', ('context', 'expert'))
- grad_attn_gain: float32 [2048], replicated
- grad_w_query: float32 [2048, 4096], P(None, 'expert')
- grad_w_key: float32 [2048, 512], P(None, 'expert')
- grad_w_value: float32 [2048, 512], P(None, 'expert')
- grad_q_gain: float32 [128], replicated
- grad_k_gain: float32 [128], replicated
- grad_w_out: float32 [4096, 2048], P('expert')
- grad_mlp_gain: float32 [2048], replicated
- grad_router: float32 [2048, 32], replicated
- grad_w_gate: float32 [32, 2048, 768], P(('dp', 'context', 'expert'))
- grad_w_up: float32 [32, 2048, 768], P(('dp', 'context', 'expert'))
- grad_w_down: float32 [32, 768, 2048], P(('dp', 'context', 'expert'))
The draws below stay inside these ranges and needn't reach their ends.
Inputs may be any that keep to these rules, and one draw needn't show every extreme that they name: `routes`: each token names 8 different experts. In each aligned block of 128 tokens (the tokens of one device) no expert is named by more than 36 of them, a bound that some block reaches. `half_order`: each half-block appears once.
All inputs are finite; a program needn't handle non-finite values.
Results may differ from the reference program's by a relative error of at most 0.02.
Values may be sent and summed in bfloat16 or wider, within the bound.
No kernel may reach another device: no remote copies, remote signals or barrier semaphores. Data moves between devices by JAX's collectives and lax.ppermute only.
A program may use at most 320 MiB of HBM per device.

```python
import math
import jax
import jax.numpy as jnp
import numpy as np
from jax import lax

D = 2048
QUERY_HEADS = 32
KEY_VALUE_HEADS = 4
HEAD_WIDTH = 128
FF = 768
TOP = 8
TOK_DEV = 128
EXPERTS = 32
CAP = 36
SEQS = 2
SEQ = 2048
HALF = 256
HALVES = 8


def levels(rng, dims, split, low, largest):
    loudness = 1.0
    for position, blocks in split:
        steps = jax.random.uniform(jax.random.fold_in(jax.random.fold_in(rng, 6), position), (blocks,), jnp.float32, low / len(split), largest / len(split))
        loudness = loudness * jnp.repeat(jnp.exp(steps), dims[position] // blocks).reshape((-1,) + (1,) * (len(dims) - 1 - position))
    return loudness


def routed_block(rng, own, number, rows, amount, top, bound, slope):
    order = jax.random.permutation(rng, amount)
    heavy_load, ordinary = portions_of(amount, rows * top, bound, slope, True), portions_of(amount, rows * top, bound, slope, False)
    places = jnp.arange(amount)

    def named(lengths, turn):
        used = int((lengths > 0).sum())
        fixed = max(1, used // 4)
        passed = fixed + (places - fixed + turn * (used - fixed)) % max(1, amount - fixed)
        return jnp.zeros((amount,), jnp.int32).at[order[jnp.where(places < fixed, places, passed)]].set(jnp.asarray(lengths, jnp.int32))

    lengths = jnp.where(number % 4 == 0, named(heavy_load, number // 4), named(ordinary, number - number // 4 - 1))
    mixed = jax.random.permutation(jax.random.fold_in(own, 3), amount)
    giver, sink = mixed[0:amount // 2 * 2:2], mixed[1:amount // 2 * 2:2]
    room = jnp.minimum(lengths[giver] - 1, bound - lengths[sink]) // 2
    room = jnp.where((giver == order[0]) | (sink == order[0]) | (lengths[sink] == 0), 0, jnp.maximum(room, 0))
    passed = jax.random.randint(jax.random.fold_in(own, 4), (amount // 2,), 0, 1 << 20) % (room + 1)
    lengths = lengths.at[giver].add(-passed).at[sink].add(passed)
    members = jnp.searchsorted(jnp.cumsum(lengths), jnp.arange(rows * top), side="right").astype(jnp.int32)
    listing = members.reshape(top, rows).T
    listing = listing[jax.random.permutation(jax.random.fold_in(own, 1), rows)]
    turn = jax.random.randint(jax.random.fold_in(own, 2), (rows, 1), 0, top)
    return jnp.take_along_axis(listing, (jnp.arange(top)[None, :] + turn) % top, axis=1)


def portions_of(count, total, reach, skew, full):
    loads = [(1 << 20) // math.isqrt(rank ** skew) + 1 for rank in range(1, count + 1)]
    largest = reach if full else min(reach, max(-(-total // count), total * loads[0] // sum(loads)))
    least = 1 if total - largest >= count - 1 else 0
    counts, rest = [largest] + [least] * (count - 1), total - largest - least * (count - 1)
    while rest > 0:
        candidates = [i for i in range(1, count) if counts[i] < largest] or [i for i in range(1, count) if counts[i] < reach]
        pool, budget = sum([loads[i] for i in candidates]), rest
        for i in candidates:
            extra = min(reach - counts[i], max(1, budget * loads[i] // pool), rest)
            counts[i] = counts[i] + extra
            rest = rest - extra
    return np.array(counts)


def normal_values(rng, dims, scale, limit, split=(), kind=jnp.bfloat16):
    loudness = levels(rng, dims, split, -0.22, 0.18) if split else 1.0
    array = jax.random.normal(rng, dims, jnp.float32) * scale * loudness
    return jnp.minimum(jnp.maximum(array, -limit), limit).astype(kind)


def setup_inputs(seed: int = 0) -> dict:
    arg_keys = jax.random.split(jax.random.key(seed), 17)
    layer_input = normal_values(arg_keys[0], (SEQS, SEQ, D), 1.0, 6.0, ((0, 2), (1, 16)))
    grad_output = normal_values(arg_keys[1], (SEQS, SEQ, D), 1.0, 6.0, ((0, 2), (1, 16)))
    attn_gain = jnp.clip(1.0 + 0.1 * jax.random.normal(arg_keys[2], (D,), jnp.float32), 0.5, 1.5)
    query_weight = normal_values(arg_keys[3], (D, QUERY_HEADS * HEAD_WIDTH), D ** -0.5, 0.125, ((1, 4),))
    key_weight = normal_values(arg_keys[4], (D, KEY_VALUE_HEADS * HEAD_WIDTH), D ** -0.5, 0.125, ((1, 4),))
    value_weight = normal_values(arg_keys[5], (D, KEY_VALUE_HEADS * HEAD_WIDTH), D ** -0.5, 0.125, ((1, 4),))
    q_gain = jnp.clip(1.0 + 0.15 * jax.random.normal(arg_keys[6], (HEAD_WIDTH,), jnp.float32), 0.25, 1.75)
    k_gain = jnp.clip(1.0 + 0.15 * jax.random.normal(arg_keys[7], (HEAD_WIDTH,), jnp.float32), 0.25, 1.75)
    output_weight = normal_values(arg_keys[8], (QUERY_HEADS * HEAD_WIDTH, D), (max(1, 6 * QUERY_HEADS * HEAD_WIDTH // SEQ)) ** -0.5, 1.75, ((0, 4),))
    mlp_gain = jnp.clip(1.0 + 0.1 * jax.random.normal(arg_keys[9], (D,), jnp.float32), 0.5, 1.5)
    router = normal_values(arg_keys[10], (D, EXPERTS), (4 * D) ** -0.5, 0.0625)
    w_gate = normal_values(arg_keys[11], (EXPERTS, D, FF), D ** -0.5, 0.125, ((0, 32),))
    w_up = normal_values(arg_keys[12], (EXPERTS, D, FF), D ** -0.5, 0.125, ((0, 32),))
    w_down = normal_values(arg_keys[13], (EXPERTS, FF, D), (FF // 16) ** -0.5, 0.875, ((0, 32),))
    routes_keys = jax.random.split(jax.random.fold_in(arg_keys[14], 1), SEQS * SEQ // TOK_DEV)
    routes_turns = jax.random.permutation(jax.random.fold_in(arg_keys[14], 3), SEQS * SEQ // TOK_DEV)
    routes = jax.vmap(lambda own, number: routed_block(jax.random.fold_in(arg_keys[14], 2), own, number, TOK_DEV, EXPERTS, TOP, CAP, 0))(routes_keys, routes_turns).reshape((SEQS, SEQ, TOP))
    half_order = jax.random.permutation(arg_keys[15], HALVES).astype(jnp.int32)
    return {"layer_input": layer_input, "grad_output": grad_output, "attn_gain": attn_gain, "query_weight": query_weight, "key_weight": key_weight, "value_weight": value_weight, "q_gain": q_gain, "k_gain": k_gain, "output_weight": output_weight, "mlp_gain": mlp_gain, "router": router, "w_gate": w_gate, "w_up": w_up, "w_down": w_down, "routes": routes, "half_order": half_order}


HIGH_PRECISION = lax.Precision.HIGHEST
EPS = 1e-06
THETA = 1000000.0

@jax.custom_vjp
def low_precision(v):
    return lax.optimization_barrier(v.astype(jnp.bfloat16)).astype(jnp.float32)

@jax.custom_vjp
def low_precision_back(v):
    return v

def low_keep(v):
    return (low_precision(v), None)

def low_pass(kept, grad):
    return (grad,)

def back_keep(v):
    return (v, None)

def back_low(kept, grad):
    return (low_precision(grad),)
low_precision.defvjp(low_keep, low_pass)
low_precision_back.defvjp(back_keep, back_low)

def rms_norm(value_rows, gain):
    return value_rows * lax.rsqrt(lax.optimization_barrier(jnp.mean(value_rows * value_rows, axis=-1, keepdims=True)) + EPS) * gain

def rotate(value_rows, angles):
    half_size = value_rows.shape[-1] // 2
    cosine = jnp.cos(angles)[:, None, :]
    sine = jnp.sin(angles)[:, None, :]
    first = value_rows[..., :half_size]
    second = value_rows[..., half_size:]
    return jnp.concatenate([first * cosine - second * sine, second * cosine + first * sine], axis=-1)

def frequencies(positions):
    steps = jnp.arange(0, HEAD_WIDTH, 2).astype(jnp.float32) / HEAD_WIDTH
    return positions.astype(jnp.float32)[:, None] * jnp.power(THETA, -steps)[None, :]

def attend(queries, keys, value_rows, positions):
    block_length = queries.shape[0]
    step_len = math.gcd(block_length, 256)
    group = QUERY_HEADS // KEY_VALUE_HEADS
    score_scale = HEAD_WIDTH ** (-0.5)
    query_blocks = queries.reshape(block_length // step_len, step_len, KEY_VALUE_HEADS, group, HEAD_WIDTH)
    pos_blocks = positions.reshape(block_length // step_len, step_len)

    @jax.checkpoint
    def one_block(pair):
        query_block, query_pos = pair
        scores = low_precision_back(jnp.einsum('qkgd,skd->kgqs', query_block, keys, precision=HIGH_PRECISION) * score_scale)
        allowed = positions[None, :] <= query_pos[:, None]
        scores = jnp.where(allowed[None, None], scores, -1e+30)
        peak = lax.optimization_barrier(jnp.max(scores, axis=-1, keepdims=True))
        weights = jnp.exp(scores - peak)
        probs = weights / lax.optimization_barrier(jnp.sum(weights, axis=-1, keepdims=True))
        result = jnp.einsum('kgqs,skd->qkgd', low_precision(probs), value_rows, precision=HIGH_PRECISION)
        return result.reshape(step_len, QUERY_HEADS * HEAD_WIDTH)
    return lax.map(one_block, (query_blocks, pos_blocks)).reshape(block_length, QUERY_HEADS * HEAD_WIDTH)

def layer(x_in, attn_gain, query_weight, key_weight, value_weight, q_gain, k_gain, output_weight, mlp_gain, router, w_gate, w_up, w_down, positions, route_rows, slot_of, token_of):
    sequence_count, block_length, width = x_in.shape
    angles = frequencies(positions)
    normed_input = low_precision(rms_norm(x_in, attn_gain))
    query_projected = low_precision_back(jnp.einsum('oqg,gm->oqm', normed_input, query_weight, precision=HIGH_PRECISION)).reshape(sequence_count, block_length, QUERY_HEADS, HEAD_WIDTH)
    queries = low_precision(rotate(rms_norm(query_projected, q_gain), angles))
    key_projected = jnp.einsum('oqg,gm->oqm', normed_input, key_weight, precision=HIGH_PRECISION).reshape(sequence_count, block_length, KEY_VALUE_HEADS, HEAD_WIDTH)
    keys = low_precision(rotate(rms_norm(key_projected, k_gain), angles))
    value_rows = low_precision(jnp.einsum('oqg,gm->oqm', normed_input, value_weight, precision=HIGH_PRECISION)).reshape(sequence_count, block_length, KEY_VALUE_HEADS, HEAD_WIDTH)
    attended_output = jnp.stack([attend(queries[member], keys[member], value_rows[member], positions) for member in range(sequence_count)])
    attended_output = low_precision(low_precision_back(attended_output))
    attention_output = low_precision_back(jnp.einsum('iqn,nz->iqz', attended_output, output_weight, precision=HIGH_PRECISION))
    hidden = x_in + attention_output
    mixed = low_precision(rms_norm(hidden, mlp_gain)).reshape(sequence_count * block_length, width)
    logits = jnp.dot(mixed, router, precision=HIGH_PRECISION)
    probs = jax.nn.softmax(logits, axis=-1)
    chosen = jnp.take_along_axis(probs, route_rows, axis=1)
    gates = chosen / lax.optimization_barrier(jnp.sum(chosen, axis=1, keepdims=True))
    padded = jnp.concatenate([mixed, jnp.zeros((1, width), jnp.float32)], axis=0)

    @jax.checkpoint
    def expert(parts):
        gate_w, up_w, down_w, rows_index = parts
        copies = low_precision_back(padded[rows_index])
        pre_gate = low_precision_back(jnp.dot(copies, gate_w, precision=HIGH_PRECISION))
        pre_up = low_precision_back(jnp.dot(copies, up_w, precision=HIGH_PRECISION))
        act = low_precision(jax.nn.silu(pre_gate) * pre_up)
        return low_precision(low_precision_back(jnp.dot(act, down_w, precision=HIGH_PRECISION)))
    returned = lax.map(expert, (w_gate, w_up, w_down, token_of)).reshape(-1, width)
    total = hidden.reshape(sequence_count * block_length, width)
    for route in range(TOP):
        total = total + gates[:, route:route + 1] * returned[slot_of[:, route]]
    return total.reshape(sequence_count, block_length, width)

def reference(layer_input, grad_output, attn_gain, query_weight, key_weight, value_weight, q_gain, k_gain, output_weight, mlp_gain, router, w_gate, w_up, w_down, routes, half_order):
    block_length = layer_input.shape[1]
    seq_rows = jnp.arange(block_length, dtype=jnp.int32)
    positions = half_order[seq_rows // HALF] * HALF + seq_rows % HALF
    flat_ids = routes.reshape(-1)
    n_blocks = flat_ids.shape[0] // (TOK_DEV * TOP)
    block_ids = flat_ids.reshape(n_blocks, TOK_DEV * TOP)
    hits = (block_ids[:, :, None] == jnp.arange(EXPERTS, dtype=jnp.int32)[None, None, :]).astype(jnp.int32)
    ranks = lax.optimization_barrier(jnp.sum((jnp.cumsum(hits, axis=1) - hits) * hits, axis=2))
    slots = block_ids * (n_blocks * CAP) + jnp.arange(n_blocks, dtype=jnp.int32)[:, None] * CAP + ranks
    token_ids = jnp.arange(n_blocks * TOK_DEV * TOP, dtype=jnp.int32) // TOP
    token_of = jnp.full((EXPERTS * n_blocks * CAP,), n_blocks * TOK_DEV, jnp.int32)
    token_of = token_of.at[slots.reshape(-1)].set(token_ids).reshape(EXPERTS, n_blocks * CAP)
    slot_of = slots.reshape(-1, TOP).astype(jnp.int32)
    route_rows = routes.reshape(-1, TOP)

    def forward(x_in, attn_gain_in, query_in, key_in, value_in, q_gain_in, k_gain_in, out_in, mlp_gain_in, router_in, gate_in, up_in, down_in):
        return layer(x_in, attn_gain_in, query_in, key_in, value_in, q_gain_in, k_gain_in, out_in, mlp_gain_in, router_in, gate_in, up_in, down_in, positions, route_rows, slot_of, token_of)
    total, pullback = jax.vjp(forward, layer_input.astype(jnp.float32), attn_gain.astype(jnp.float32), query_weight.astype(jnp.float32), key_weight.astype(jnp.float32), value_weight.astype(jnp.float32), q_gain.astype(jnp.float32), k_gain.astype(jnp.float32), output_weight.astype(jnp.float32), mlp_gain.astype(jnp.float32), router.astype(jnp.float32), w_gate.astype(jnp.float32), w_up.astype(jnp.float32), w_down.astype(jnp.float32))
    grads = pullback(grad_output.astype(jnp.float32))
    return (total.astype(jnp.bfloat16), grads[0], grads[1], grads[2], grads[3], grads[4], grads[5], grads[6], grads[7], grads[8], grads[9], grads[10], grads[11], grads[12])
```

```python
import functools
import math

import jax
import jax.numpy as jnp
from jax import lax
from jax.experimental import pallas as pl
from jax.experimental.pallas import tpu as pltpu
from jax.sharding import PartitionSpec as P

EPS = 1e-06
THETA = 1000000.0
TILE = 256
VMEM_BYTES = 56 * 1024 * 1024
LOG2E = math.log2(math.e)
LOW = jnp.bfloat16
F32 = jnp.float32
ALL_AXES = ("dp", "context", "expert")
GROUP_AXES = ("dp", "context")


def dot_nn(a, b):
    return lax.dot_general(a, b, (((1,), (0,)), ((), ())), preferred_element_type=F32)


def dot_nt(a, b):
    return lax.dot_general(a, b, (((1,), (1,)), ((), ())), preferred_element_type=F32)


def dot_tn(a, b):
    return lax.dot_general(a, b, (((0,), (0,)), ((), ())), preferred_element_type=F32)


def params(**more):
    return pltpu.CompilerParams(vmem_limit_bytes=VMEM_BYTES, **more)


def cost(flops, nbytes, exps=0):
    return pl.CostEstimate(flops=int(flops), bytes_accessed=int(nbytes), transcendentals=int(exps))


def head_forward(u, gain, cos2, sin2):
    rr = lax.rsqrt(jnp.mean(u * u, axis=-1, keepdims=True) + EPS)
    y = u * rr * gain
    return y * cos2 + pltpu.roll(y, 64, 1) * sin2


def head_backward(gy, u, gain, cos2, sin2):
    g = gy * cos2 - pltpu.roll(gy, 64, 1) * sin2
    rr = lax.rsqrt(jnp.mean(u * u, axis=-1, keepdims=True) + EPS)
    n = u * rr
    gn = g * gain
    grad = rr * (gn - n * jnp.mean(gn * n, axis=-1, keepdims=True))
    return grad, jnp.sum(g * n, axis=0, keepdims=True)


def query_kernel(x_ref, w_ref, gain_ref, cos_ref, sin_ref, rot_ref, proj_ref):
    tiles, heads, rows, size = rot_ref.shape
    acc = dot_nn(x_ref[...], w_ref[...])
    for h in range(heads):
        u = acc[:, h * size : (h + 1) * size]
        rot = head_forward(u, gain_ref[...], cos_ref[...], sin_ref[...])
        proj_ref[:, h] = u.reshape(tiles, rows, size)
        rot_ref[:, h] = rot.astype(LOW).reshape(tiles, rows, size)


def project_queries(normed, weight, gain, cos2, sin2):
    block, width = normed.shape
    size = cos2.shape[1]
    heads = weight.shape[1] // size
    tiles = block // TILE
    whole = lambda i: (0, 0)
    per = lambda i: (0, i, 0, 0)
    shape = (tiles, heads, TILE, size)
    return pl.pallas_call(
        query_kernel,
        grid=(heads // 2,),
        in_specs=[
            pl.BlockSpec((block, width), whole),
            pl.BlockSpec((width, 2 * size), lambda i: (0, i)),
            pl.BlockSpec((1, size), whole),
            pl.BlockSpec((block, size), whole),
            pl.BlockSpec((block, size), whole),
        ],
        out_specs=[pl.BlockSpec((tiles, 2, TILE, size), per)] * 2,
        out_shape=[jax.ShapeDtypeStruct(shape, LOW), jax.ShapeDtypeStruct(shape, F32)],
        compiler_params=params(),
        cost_estimate=cost(2 * block * width * heads * size, 12e6),
    )(normed, weight, gain[None], cos2, sin2)


def key_kernel(factor, x_ref, w_ref, gain_ref, cos_ref, sin_ref, kv_ref, proj_ref):
    size = proj_ref.shape[1]
    acc = dot_nn(x_ref[...], w_ref[...])
    u = acc[:, :size]
    rot = head_forward(u, gain_ref[...], cos_ref[...], sin_ref[...])
    proj_ref[...] = u
    kv_ref[:, :size] = (rot * factor).astype(LOW)
    kv_ref[:, size:] = acc[:, size:].astype(LOW)


def project_keys(normed, weight, gain, cos2, sin2, factor):
    block, width = normed.shape
    size = cos2.shape[1]
    return pl.pallas_call(
        functools.partial(key_kernel, factor),
        out_shape=[
            jax.ShapeDtypeStruct((block, 2 * size), LOW),
            jax.ShapeDtypeStruct((block, size), F32),
        ],
        compiler_params=params(),
        cost_estimate=cost(4 * block * width * size, 4e6),
    )(normed, weight, gain[None], cos2, sin2)


def attend_kernel(qpos_ref, kidx_ref, q_ref, kv_ref, out_ref, inv_ref, acc_ref):
    heads, rows, size = q_ref.shape[1:]
    last = qpos_ref[pl.program_id(0)]
    acc_ref[...] = jnp.zeros_like(acc_ref)
    ones = jnp.ones((rows, size), LOW)

    def step(place, masked):
        start = pl.multiple_of(kidx_ref[place] * rows, rows)
        keys = kv_ref[pl.ds(start, rows), :size]
        values = jnp.concatenate([kv_ref[pl.ds(start, rows), size:], ones], axis=1)
        for h in range(heads):
            e = jnp.exp2(dot_nt(q_ref[0, h], keys))
            if masked:
                qi = lax.broadcasted_iota(jnp.int32, e.shape, 0)
                ki = lax.broadcasted_iota(jnp.int32, e.shape, 1)
                e = jnp.where(ki <= qi, e, 0.0)
            acc_ref[h] += dot_nn(e.astype(LOW), values)

    lax.fori_loop(0, last, lambda p, c: (step(p, False), c)[1], 0)
    step(last, True)
    for h in range(heads):
        inv = 1.0 / acc_ref[h, :, size:]
        inv_ref[0, h] = inv
        out_ref[:, h * size : (h + 1) * size] = (acc_ref[h, :, :size] * inv).astype(LOW)


def attend(qpos, kidx, queries, kv):
    tiles, heads, rows, size = queries.shape
    seq = kv.shape[0]
    return pl.pallas_call(
        attend_kernel,
        grid_spec=pltpu.PrefetchScalarGridSpec(
            num_scalar_prefetch=2,
            grid=(tiles,),
            in_specs=[
                pl.BlockSpec((1, heads, rows, size), lambda i, a, b: (i, 0, 0, 0)),
                pl.BlockSpec((seq, 2 * size), lambda i, a, b: (0, 0)),
            ],
            out_specs=[
                pl.BlockSpec((rows, heads * size), lambda i, a, b: (i, 0)),
                pl.BlockSpec((1, heads, rows, size), lambda i, a, b: (i, 0, 0, 0)),
            ],
            scratch_shapes=[pltpu.VMEM((heads, rows, 2 * size), F32)],
        ),
        out_shape=[
            jax.ShapeDtypeStruct((tiles * rows, heads * size), LOW),
            jax.ShapeDtypeStruct((tiles, heads, rows, size), F32),
        ],
        compiler_params=params(),
        cost_estimate=cost(
            6 * tiles * rows * heads * seq * size, 8e6, tiles * rows * heads * seq
        ),
    )(qpos, kidx, queries, kv)


def grad_out_kernel(g_ref, w_ref, o_ref, inv_ref, do_ref, centre_ref):
    tiles, heads, rows, size = do_ref.shape
    acc = dot_nt(g_ref[...], w_ref[...])
    ones = jnp.ones((8, size), F32)
    for t in range(tiles):
        for h in range(heads):
            part = slice(t * rows, (t + 1) * rows), slice(h * size, (h + 1) * size)
            low = (acc[part] * inv_ref[t, h]).astype(LOW)
            do_ref[t, h] = low
            product = low.astype(F32) * o_ref[part].astype(F32)
            centre_ref[t, h] = lax.dot_general(
                ones,
                product,
                (((1,), (1,)), ((), ())),
                precision=lax.Precision.HIGHEST,
                preferred_element_type=F32,
            )


def grad_attended(grad_rows, weight, attended, inverse):
    tiles, heads, rows, size = inverse.shape
    block, width = grad_rows.shape
    return pl.pallas_call(
        grad_out_kernel,
        grid=(heads // 2,),
        in_specs=[
            pl.BlockSpec((block, width), lambda i: (0, 0)),
            pl.BlockSpec((2 * size, width), lambda i: (i, 0)),
            pl.BlockSpec((block, 2 * size), lambda i: (0, i)),
            pl.BlockSpec((tiles, 2, rows, size), lambda i: (0, i, 0, 0)),
        ],
        out_specs=[
            pl.BlockSpec((tiles, 2, rows, size), lambda i: (0, i, 0, 0)),
            pl.BlockSpec((tiles, 2, 8, rows), lambda i: (0, i, 0, 0)),
        ],
        out_shape=[
            jax.ShapeDtypeStruct((tiles, heads, rows, size), LOW),
            jax.ShapeDtypeStruct((tiles, heads, 8, rows), F32),
        ],
        compiler_params=params(),
        cost_estimate=cost(2 * block * width * heads * size, 12e6),
    )(grad_rows, weight, attended, inverse)


def attend_back_kernel(
    qpos_ref,
    kidx_ref,
    q_ref,
    do_ref,
    centre_ref,
    kv_ref,
    proj_ref,
    gain_ref,
    cos_ref,
    sin_ref,
    dkv_ref,
    dq_ref,
    dgain_ref,
    acc_ref,
):
    heads, rows, size = q_ref.shape[1:]
    last = qpos_ref[pl.program_id(0)]

    @pl.when(pl.program_id(0) == 0)
    def _():
        dkv_ref[...] = jnp.zeros_like(dkv_ref)
        dgain_ref[...] = jnp.zeros_like(dgain_ref)

    acc_ref[...] = jnp.zeros_like(acc_ref)

    def step(place, masked):
        start = pl.multiple_of(kidx_ref[place] * rows, rows)
        keys = kv_ref[pl.ds(start, rows), :size]
        values = kv_ref[pl.ds(start, rows), size:]
        dk = dkv_ref[pl.ds(start, rows), :size]
        dv = dkv_ref[pl.ds(start, rows), size:]
        for h in range(heads):
            query, grad = q_ref[0, h], do_ref[0, h]
            e = jnp.exp2(dot_nt(keys, query))
            if masked:
                ki = lax.broadcasted_iota(jnp.int32, e.shape, 0)
                qi = lax.broadcasted_iota(jnp.int32, e.shape, 1)
                e = jnp.where(ki <= qi, e, 0.0)
            ds = (e * (dot_nt(values, grad) - centre_ref[0, h, 0:1])).astype(LOW)
            dv += dot_nn(e.astype(LOW), grad)
            dk += dot_nn(ds, query)
            acc_ref[h] += dot_tn(ds, keys)
        dkv_ref[pl.ds(start, rows), :size] = dk
        dkv_ref[pl.ds(start, rows), size:] = dv

    lax.fori_loop(0, last, lambda p, c: (step(p, False), c)[1], 0)
    step(last, True)
    total = jnp.zeros((1, size), F32)
    for h in range(heads):
        grad, gain_part = head_backward(
            acc_ref[h] * (1.0 / LOG2E), proj_ref[0, h], gain_ref[...], cos_ref[...], sin_ref[...]
        )
        dq_ref[:, h * size : (h + 1) * size] = grad.astype(LOW)
        total += gain_part
    dgain_ref[...] += total


def attend_back(qpos, kidx, queries, grads, centre, kv, proj, gain, cos2, sin2):
    tiles, heads, rows, size = queries.shape
    seq = kv.shape[0]
    per = pl.BlockSpec((1, heads, rows, size), lambda i, a, b: (i, 0, 0, 0))
    flat = lambda i, a, b: (0, 0)
    rowwise = lambda i, a, b: (i, 0)
    return pl.pallas_call(
        attend_back_kernel,
        grid_spec=pltpu.PrefetchScalarGridSpec(
            num_scalar_prefetch=2,
            grid=(tiles,),
            in_specs=[
                per,
                per,
                pl.BlockSpec((1, heads, 8, rows), lambda i, a, b: (i, 0, 0, 0)),
                pl.BlockSpec((seq, 2 * size), flat),
                per,
                pl.BlockSpec((1, size), flat),
                pl.BlockSpec((rows, size), rowwise),
                pl.BlockSpec((rows, size), rowwise),
            ],
            out_specs=[
                pl.BlockSpec((seq, 2 * size), flat),
                pl.BlockSpec((rows, heads * size), rowwise),
                pl.BlockSpec((1, size), flat),
            ],
            scratch_shapes=[pltpu.VMEM((heads, rows, size), F32)],
        ),
        out_shape=[
            jax.ShapeDtypeStruct((seq, 2 * size), F32),
            jax.ShapeDtypeStruct((tiles * rows, heads * size), LOW),
            jax.ShapeDtypeStruct((1, size), F32),
        ],
        compiler_params=params(),
        cost_estimate=cost(
            15 * tiles * rows * heads * seq * size, 12e6, tiles * rows * heads * seq
        ),
    )(qpos, kidx, queries, grads, centre, kv, proj, gain[None], cos2, sin2)


def sum_small(flat):
    n = lax.axis_size(ALL_AXES)
    length = flat.shape[0]
    each = -(-length // (n * 128)) * 128
    parts = jnp.pad(flat, (0, n * each - length)).reshape(n, each)
    parts = lax.all_to_all(parts, ALL_AXES, split_axis=0, concat_axis=0, tiled=True)
    own = jnp.sum(parts, axis=0, keepdims=True)
    whole = lax.all_to_all(
        jnp.broadcast_to(own, (n, each)), ALL_AXES, split_axis=0, concat_axis=0, tiled=True
    )
    return whole.reshape(-1)[:length]


def sum_groups(grad):
    rows, columns = grad.shape
    n_dp, n_context = lax.axis_size("dp"), lax.axis_size("context")
    part = lax.all_to_all(
        grad.reshape(n_dp, rows // n_dp, columns), "dp", split_axis=0, concat_axis=0, tiled=True
    )
    part = jnp.sum(part.astype(F32), axis=0).astype(LOW)
    each = rows // n_dp // n_context
    part = lax.all_to_all(
        part.reshape(n_context, each, columns),
        "context",
        split_axis=0,
        concat_axis=0,
        tiled=True,
    )
    part = jnp.sum(part.astype(F32), axis=0).astype(LOW)
    part = lax.all_to_all(
        jnp.broadcast_to(part[None], (n_context, each, columns)),
        "context",
        split_axis=0,
        concat_axis=0,
        tiled=True,
    )
    part = lax.all_to_all(
        jnp.broadcast_to(part[None], (n_dp, n_context, each, columns)),
        "dp",
        split_axis=0,
        concat_axis=0,
        tiled=True,
    )
    return part.reshape(rows, columns).astype(F32)


def norm_parts(rows):
    rr = lax.rsqrt(jnp.mean(rows * rows, axis=-1, keepdims=True) + EPS)
    return rows * rr, rr


def norm_back(grad, normal, rr, gain):
    weighted = grad * gain
    return rr * (weighted - normal * jnp.mean(weighted * normal, axis=-1, keepdims=True))


def on_device(
    layer_input,
    grad_output,
    attn_gain,
    query_weight,
    key_weight,
    value_weight,
    q_gain,
    k_gain,
    output_weight,
    mlp_gain,
    router,
    w_gate,
    w_up,
    w_down,
    routes,
    half_order,
):
    n_context = lax.axis_size("context")
    n_expert = lax.axis_size("expert")
    n_groups = lax.axis_size(GROUP_AXES)
    tok_dev, width = layer_input.shape[1:]
    size = q_gain.shape[0]
    kv_total = key_weight.shape[1] * n_expert
    group_dev = n_expert // (kv_total // size)
    kv_index = lax.axis_index("expert") // group_dev
    block = tok_dev * n_expert
    seq = block * n_context
    half = block // 2
    experts = router.shape[1]
    top = routes.shape[2]
    capacity = max(2, (tok_dev * top * 9 + 8 * experts - 1) // (8 * experts))
    cap_col = capacity * n_expert
    scale = size ** (-0.5)

    seq_rows = jnp.arange(seq, dtype=jnp.int32)
    context = lax.axis_index("context")
    own_halves = lax.dynamic_slice_in_dim(half_order, 2 * context, 2)
    own_pos = (own_halves[:, None] * half + jnp.arange(half, dtype=jnp.int32)[None]).reshape(-1)
    per_half = half // TILE
    tile_pos = (half_order[:, None] * per_half + jnp.arange(per_half, dtype=jnp.int32)).reshape(-1)
    kidx = jnp.sum(
        (tile_pos[None, :] == jnp.arange(seq // TILE, dtype=jnp.int32)[:, None])
        * jnp.arange(seq // TILE, dtype=jnp.int32)[None, :],
        axis=1,
    ).astype(jnp.int32)
    qpos = lax.dynamic_slice_in_dim(tile_pos, context * (block // TILE), block // TILE)
    freq = jnp.power(THETA, -jnp.arange(0, size, 2).astype(F32) / size)
    angles = own_pos.astype(F32)[:, None] * freq[None, :]
    cosine, sine = jnp.cos(angles), jnp.sin(angles)
    cos2 = jnp.concatenate([cosine, cosine], axis=1)
    sin2 = jnp.concatenate([-sine, sine], axis=1)

    x_rows = layer_input[0].astype(F32)
    x_normal, x_rr = norm_parts(x_rows)
    normed_rows = lax.all_gather(
        (x_normal * attn_gain).astype(LOW), "expert", axis=0, tiled=True
    )
    if group_dev == 1:
        kv_weights = jnp.concatenate([key_weight, value_weight], axis=1)
    else:
        key_whole = lax.all_gather(key_weight, "expert", axis=1, tiled=True)
        value_whole = lax.all_gather(value_weight, "expert", axis=1, tiled=True)
        kv_weights = jnp.concatenate(
            [
                lax.dynamic_slice_in_dim(key_whole, kv_index * size, size, 1),
                lax.dynamic_slice_in_dim(value_whole, kv_index * size, size, 1),
            ],
            axis=1,
        )
    own_kv, key_proj = project_keys(normed_rows, kv_weights, k_gain, cos2, sin2, scale * LOG2E)
    kv_whole = lax.all_gather(own_kv, "context", axis=0, tiled=True)
    queries, query_proj = project_queries(normed_rows, query_weight, q_gain, cos2, sin2)

    grad_low = grad_output[0]
    routes_col = lax.all_gather(routes[0], "expert", axis=0, tiled=True)
    grad_col = lax.all_gather(grad_low, "expert", axis=0, tiled=True)
    group_ids = (
        jnp.arange(n_groups, dtype=jnp.int32) * n_expert + lax.axis_index("expert")
    )
    col_hits = jnp.any(routes_col[:, :, None] == group_ids[None, None, :], axis=1)
    earlier = jnp.tril(jnp.ones((tok_dev, tok_dev), LOW), -1)
    col_ranks = jnp.einsum(
        "ts,zsd->ztd",
        earlier,
        col_hits.astype(LOW).reshape(n_expert, tok_dev, n_groups),
        preferred_element_type=F32,
    ).astype(jnp.int32)
    col_slots = (
        col_ranks + (jnp.arange(n_expert, dtype=jnp.int32) * capacity)[:, None, None]
    ).reshape(block, n_groups)
    col_slots = jnp.where(col_hits, col_slots, -1)
    spread = (
        (col_slots.T[:, None, :] == jnp.arange(cap_col, dtype=jnp.int32)[None, :, None])
        .astype(LOW)
        .reshape(n_groups * cap_col, block)
    )

    def to_experts(rows_col):
        rows = dot_nn(spread, rows_col).astype(LOW).reshape(n_groups, cap_col, width)
        rows = lax.all_to_all(rows, GROUP_AXES, split_axis=0, concat_axis=0, tiled=True)
        return rows.reshape(n_groups * cap_col, width)

    def from_experts(rows):
        rows = lax.all_to_all(
            rows.reshape(n_groups, cap_col, width),
            GROUP_AXES,
            split_axis=0,
            concat_axis=0,
            tiled=True,
        ).reshape(n_groups * cap_col, width)
        return lax.psum_scatter(
            dot_tn(spread, rows).astype(LOW), "expert", scatter_dimension=0, tiled=True
        ).astype(F32)

    attended, inverse = attend(qpos, kidx, queries, kv_whole)
    attn_rows = lax.psum_scatter(
        dot_nn(attended, output_weight).astype(LOW), "expert", scatter_dimension=0, tiled=True
    ).astype(F32)

    grad_x = to_experts(grad_col)
    act_pull = dot_nt(grad_x, w_down[0])

    hidden = x_rows + attn_rows
    h_normal, h_rr = norm_parts(hidden)
    mixed = (h_normal * mlp_gain).astype(LOW)
    mixed_col = lax.all_gather(mixed, "expert", axis=0, tiled=True)
    logits = dot_nn(mixed, router)
    own_mask = jnp.any(
        routes[0][:, :, None] == jnp.arange(experts, dtype=jnp.int32)[None, None, :], axis=1
    )
    own_ranks = dot_nn(earlier, own_mask.astype(LOW)).astype(jnp.int32)
    own_slots = jnp.where(own_mask, own_ranks, -1)
    own_spread = own_slots.T[:, None, :] == jnp.arange(capacity, dtype=jnp.int32)[None, :, None]
    probs = jax.nn.softmax(logits, axis=-1)
    chosen = jnp.where(own_mask, probs, 0.0)
    chosen_sum = jnp.sum(chosen, axis=1, keepdims=True)
    gates = chosen / chosen_sum
    gate_slots = jnp.sum(jnp.where(own_spread, gates.T[:, None, :], 0.0), axis=2)
    gate_rows = lax.all_to_all(gate_slots, ALL_AXES, split_axis=0, concat_axis=0, tiled=True)
    gate_rows = gate_rows.reshape(-1, 1)

    x = to_experts(mixed_col)
    pre_gate = dot_nn(x, w_gate[0])
    pre_up = dot_nn(x, w_up[0])
    sig = jax.nn.sigmoid(pre_gate)
    silu = pre_gate * sig
    act = (silu * pre_up).astype(LOW)
    gate_grads = jnp.sum(act.astype(F32) * act_pull, axis=1)
    grad_act = gate_rows * act_pull
    gate_low = (grad_act * pre_up * (sig * (1.0 + pre_gate * (1.0 - sig)))).astype(LOW)
    up_low = (grad_act * silu).astype(LOW)
    copies = (dot_nt(gate_low, w_gate[0]) + dot_nt(up_low, w_up[0])).astype(LOW)
    gate_back = lax.all_to_all(
        gate_grads.reshape(-1, capacity), ALL_AXES, split_axis=0, concat_axis=0, tiled=True
    )
    grad_mixed = from_experts(copies)
    returned = (dot_nn(act, w_down[0]) * gate_rows).astype(LOW)
    grad_ret = (grad_x.astype(F32) * gate_rows).astype(LOW)
    grad_w_down = dot_tn(act, grad_ret)
    grad_w_gate = dot_tn(x, gate_low)
    grad_w_up = dot_tn(x, up_low)

    grad_gates = jnp.sum(jnp.where(own_spread, gate_back[:, :, None], 0.0), axis=1).T
    centred = grad_gates - jnp.sum(grad_gates * gates, axis=1, keepdims=True)
    centred = jnp.where(own_mask, centred / chosen_sum, 0.0)
    grad_logits = probs * (centred - jnp.sum(centred * chosen, axis=1, keepdims=True))
    high = lax.Precision.HIGHEST
    grad_mixed = grad_mixed + jnp.einsum(
        "te,de->td", grad_logits, router.astype(F32), precision=high
    )
    grad_router = jnp.einsum("te,td->ed", grad_logits, mixed.astype(F32), precision=high)
    grad_rows = grad_low.astype(F32)
    grad_hidden = grad_rows + norm_back(grad_mixed, h_normal, h_rr, mlp_gain)
    grad_mlp_gain = jnp.sum(grad_mixed * h_normal, axis=0)

    grad_attn = lax.all_gather(grad_hidden.astype(LOW), "expert", axis=0, tiled=True)
    grad_o, centre = grad_attended(grad_attn, output_weight, attended, inverse)
    grad_w_out = sum_groups(dot_tn(attended, grad_attn).astype(LOW))
    grad_kv, grad_q, grad_q_gain = attend_back(
        qpos, kidx, queries, grad_o, centre, kv_whole, query_proj, q_gain, cos2, sin2
    )
    grad_kv = lax.psum_scatter(
        grad_kv.astype(LOW), "context", scatter_dimension=0, tiled=True
    ).astype(F32)
    grad_w_query = sum_groups(dot_tn(normed_rows, grad_q).astype(LOW))

    output_rows = hidden + from_experts(returned)

    gk = grad_kv[:, :size] * scale
    roll = lambda v: jnp.concatenate([v[:, size // 2 :], v[:, : size // 2]], axis=1)
    gk = gk * cos2 - roll(gk) * sin2
    k_normal, k_rr = norm_parts(key_proj)
    grad_k_gain = jnp.sum(gk * k_normal, axis=0)
    gk = norm_back(gk, k_normal, k_rr, k_gain)
    kv_grads = jnp.concatenate([gk, grad_kv[:, size:]], axis=1).astype(LOW)

    grad_normed = dot_nt(grad_q, query_weight) + dot_nt(kv_grads, kv_weights)
    grad_attn_gain = jnp.sum(grad_normed * normed_rows.astype(F32), axis=0) / attn_gain
    grad_normed = lax.psum_scatter(
        grad_normed.astype(LOW), "expert", scatter_dimension=0, tiled=True
    ).astype(F32)
    grad_w_kv = dot_tn(normed_rows, kv_grads).astype(LOW)
    if group_dev == 1:
        grad_w_kv = sum_groups(grad_w_kv)
        grad_w_key, grad_w_value = grad_w_kv[:, :size], grad_w_kv[:, size:]
    else:
        blank = jnp.zeros((width, kv_total), LOW)
        pieces = []
        for part in (grad_w_kv[:, :size], grad_w_kv[:, size:]):
            padded = lax.dynamic_update_slice(blank, part, (0, kv_index * size))
            pieces.append(
                lax.psum_scatter(padded, "expert", scatter_dimension=1, tiled=True)
            )
        grad_w_key, grad_w_value = (
            lax.psum(piece, GROUP_AXES).astype(F32) for piece in pieces
        )
    grad_input = grad_hidden + norm_back(grad_normed, x_normal, x_rr, attn_gain)

    small = [grad_attn_gain, grad_mlp_gain, grad_q_gain[0], grad_k_gain, grad_router.reshape(-1)]
    summed = sum_small(jnp.concatenate(small))
    pieces = []
    offset = 0
    for part in small:
        pieces.append(summed[offset : offset + part.shape[0]])
        offset += part.shape[0]
    grad_attn_gain, grad_mlp_gain, grad_q_gain, grad_k_gain, grad_router = pieces
    return (
        output_rows.astype(LOW)[None],
        grad_input[None],
        grad_attn_gain,
        grad_w_query,
        grad_w_key,
        grad_w_value,
        grad_q_gain,
        grad_k_gain,
        grad_w_out,
        grad_mlp_gain,
        grad_router.reshape(experts, width).T,
        grad_w_gate[None],
        grad_w_up[None],
        grad_w_down[None],
    )


def solution(mesh):
    rows = P("dp", ("context", "expert"), None)
    expert = P(ALL_AXES, None, None)
    columns = P(None, "expert")
    in_specs = (
        rows,
        rows,
        P(),
        columns,
        columns,
        columns,
        P(),
        P(),
        P("expert", None),
        P(),
        P(),
        expert,
        expert,
        expert,
        rows,
        P(),
    )
    out_specs = (
        rows,
        rows,
        P(),
        columns,
        columns,
        columns,
        P(),
        P(),
        P("expert", None),
        P(),
        P(),
        expert,
        expert,
        expert,
    )
    return jax.shard_map(
        on_device, mesh=mesh, in_specs=in_specs, out_specs=out_specs, check_vma=False
    )
```

```python
import functools
import math

import jax
import jax.numpy as jnp
from jax import lax
from jax.experimental import pallas as pl
from jax.experimental.pallas import tpu as pltpu
from jax.sharding import PartitionSpec as P

EPS = 1e-06
THETA = 1000000.0
TILE = 256
VMEM_BYTES = 56 * 1024 * 1024
LOG2E = math.log2(math.e)
LOW = jnp.bfloat16
F32 = jnp.float32
ALL_AXES = ("dp", "context", "expert")
GROUP_AXES = ("dp", "context")


def dot_nn(a, b):
    return lax.dot_general(a, b, (((1,), (0,)), ((), ())), preferred_element_type=F32)


def dot_nt(a, b):
    return lax.dot_general(a, b, (((1,), (1,)), ((), ())), preferred_element_type=F32)


def dot_tn(a, b):
    return lax.dot_general(a, b, (((0,), (0,)), ((), ())), preferred_element_type=F32)


def params(**more):
    return pltpu.CompilerParams(vmem_limit_bytes=VMEM_BYTES, **more)


def cost(flops, nbytes, exps=0):
    return pl.CostEstimate(flops=int(flops), bytes_accessed=int(nbytes), transcendentals=int(exps))


def head_forward(u, gain, cos2, sin2):
    rr = lax.rsqrt(jnp.mean(u * u, axis=-1, keepdims=True) + EPS)
    y = u * rr * gain
    return y * cos2 + pltpu.roll(y, 64, 1) * sin2


def head_backward(gy, u, gain, cos2, sin2):
    g = gy * cos2 - pltpu.roll(gy, 64, 1) * sin2
    rr = lax.rsqrt(jnp.mean(u * u, axis=-1, keepdims=True) + EPS)
    n = u * rr
    gn = g * gain
    grad = rr * (gn - n * jnp.mean(gn * n, axis=-1, keepdims=True))
    return grad, jnp.sum(g * n, axis=0, keepdims=True)


def query_kernel(x_ref, w_ref, gain_ref, cos_ref, sin_ref, rot_ref, proj_ref):
    tiles, heads, rows, size = rot_ref.shape
    acc = dot_nn(x_ref[...], w_ref[...])
    for h in range(heads):
        u = acc[:, h * size : (h + 1) * size]
        rot = head_forward(u, gain_ref[...], cos_ref[...], sin_ref[...])
        proj_ref[:, h] = u.reshape(tiles, rows, size)
        rot_ref[:, h] = rot.astype(LOW).reshape(tiles, rows, size)


def project_queries(normed, weight, gain, cos2, sin2):
    block, width = normed.shape
    size = cos2.shape[1]
    heads = weight.shape[1] // size
    tiles = block // TILE
    whole = lambda i: (0, 0)
    per = lambda i: (0, i, 0, 0)
    shape = (tiles, heads, TILE, size)
    return pl.pallas_call(
        query_kernel,
        grid=(heads // 2,),
        in_specs=[
            pl.BlockSpec((block, width), whole),
            pl.BlockSpec((width, 2 * size), lambda i: (0, i)),
            pl.BlockSpec((1, size), whole),
            pl.BlockSpec((block, size), whole),
            pl.BlockSpec((block, size), whole),
        ],
        out_specs=[pl.BlockSpec((tiles, 2, TILE, size), per)] * 2,
        out_shape=[jax.ShapeDtypeStruct(shape, LOW), jax.ShapeDtypeStruct(shape, F32)],
        compiler_params=params(),
        cost_estimate=cost(2 * block * width * heads * size, 12e6),
    )(normed, weight, gain[None], cos2, sin2)


def key_kernel(factor, x_ref, w_ref, gain_ref, cos_ref, sin_ref, kv_ref, proj_ref):
    size = proj_ref.shape[1]
    acc = dot_nn(x_ref[...], w_ref[...])
    u = acc[:, :size]
    rot = head_forward(u, gain_ref[...], cos_ref[...], sin_ref[...])
    proj_ref[...] = u
    kv_ref[:, :size] = (rot * factor).astype(LOW)
    kv_ref[:, size:] = acc[:, size:].astype(LOW)


def project_keys(normed, weight, gain, cos2, sin2, factor):
    block, width = normed.shape
    size = cos2.shape[1]
    return pl.pallas_call(
        functools.partial(key_kernel, factor),
        out_shape=[
            jax.ShapeDtypeStruct((block, 2 * size), LOW),
            jax.ShapeDtypeStruct((block, size), F32),
        ],
        compiler_params=params(),
        cost_estimate=cost(4 * block * width * size, 4e6),
    )(normed, weight, gain[None], cos2, sin2)


def attend_kernel(qpos_ref, kidx_ref, q_ref, kv_ref, *rest):
    out_ref, inv_ref, acc_ref = rest[-3:]
    heads, rows, size = q_ref.shape[1:]
    last = qpos_ref[pl.program_id(0)]
    acc_ref[...] = jnp.zeros_like(acc_ref)
    ones = jnp.ones((rows, size), LOW)

    def step(place, masked):
        start = pl.multiple_of(kidx_ref[place] * rows, rows)
        keys = kv_ref[pl.ds(start, rows), :size]
        values = jnp.concatenate([kv_ref[pl.ds(start, rows), size:], ones], axis=1)
        for h in range(heads):
            e = jnp.exp2(dot_nt(q_ref[0, h], keys))
            if masked:
                qi = lax.broadcasted_iota(jnp.int32, e.shape, 0)
                ki = lax.broadcasted_iota(jnp.int32, e.shape, 1)
                e = jnp.where(ki <= qi, e, 0.0)
            acc_ref[h] += dot_nn(e.astype(LOW), values)

    lax.fori_loop(0, last, lambda p, c: (step(p, False), c)[1], 0)
    step(last, True)
    for h in range(heads):
        inv = 1.0 / acc_ref[h, :, size:]
        inv_ref[0, h] = inv
        out_ref[:, h * size : (h + 1) * size] = (acc_ref[h, :, :size] * inv).astype(LOW)


def attend(qpos, kidx, queries, kv, others):
    tiles, heads, rows, size = queries.shape
    seq = kv.shape[0]
    return pl.pallas_call(
        attend_kernel,
        grid_spec=pltpu.PrefetchScalarGridSpec(
            num_scalar_prefetch=2,
            grid=(tiles,),
            in_specs=[
                pl.BlockSpec((1, heads, rows, size), lambda i, a, b: (i, 0, 0, 0)),
                pl.BlockSpec((seq, 2 * size), lambda i, a, b: (0, 0)),
            ]
            + [pl.BlockSpec(memory_space=pl.ANY)] * len(others),
            out_specs=[
                pl.BlockSpec((rows, heads * size), lambda i, a, b: (i, 0)),
                pl.BlockSpec((1, heads, rows, size), lambda i, a, b: (i, 0, 0, 0)),
            ],
            scratch_shapes=[pltpu.VMEM((heads, rows, 2 * size), F32)],
        ),
        out_shape=[
            jax.ShapeDtypeStruct((tiles * rows, heads * size), LOW),
            jax.ShapeDtypeStruct((tiles, heads, rows, size), F32),
        ],
        compiler_params=params(),
        cost_estimate=cost(
            6 * tiles * rows * heads * seq * size, 8e6, tiles * rows * heads * seq
        ),
    )(qpos, kidx, queries, kv, *others)


def grad_out_kernel(g_ref, w_ref, o_ref, inv_ref, do_ref, centre_ref):
    tiles, heads, rows, size = do_ref.shape
    acc = dot_nt(g_ref[...], w_ref[...])
    ones = jnp.ones((8, size), F32)
    for t in range(tiles):
        for h in range(heads):
            part = slice(t * rows, (t + 1) * rows), slice(h * size, (h + 1) * size)
            low = (acc[part] * inv_ref[t, h]).astype(LOW)
            do_ref[t, h] = low
            product = low.astype(F32) * o_ref[part].astype(F32)
            centre_ref[t, h] = lax.dot_general(
                ones,
                product,
                (((1,), (1,)), ((), ())),
                precision=lax.Precision.HIGHEST,
                preferred_element_type=F32,
            )


def grad_attended(grad_rows, weight, attended, inverse):
    tiles, heads, rows, size = inverse.shape
    block, width = grad_rows.shape
    return pl.pallas_call(
        grad_out_kernel,
        grid=(heads // 2,),
        in_specs=[
            pl.BlockSpec((block, width), lambda i: (0, 0)),
            pl.BlockSpec((2 * size, width), lambda i: (i, 0)),
            pl.BlockSpec((block, 2 * size), lambda i: (0, i)),
            pl.BlockSpec((tiles, 2, rows, size), lambda i: (0, i, 0, 0)),
        ],
        out_specs=[
            pl.BlockSpec((tiles, 2, rows, size), lambda i: (0, i, 0, 0)),
            pl.BlockSpec((tiles, 2, 8, rows), lambda i: (0, i, 0, 0)),
        ],
        out_shape=[
            jax.ShapeDtypeStruct((tiles, heads, rows, size), LOW),
            jax.ShapeDtypeStruct((tiles, heads, 8, rows), F32),
        ],
        compiler_params=params(),
        cost_estimate=cost(2 * block * width * heads * size, 12e6),
    )(grad_rows, weight, attended, inverse)


def attend_back_kernel(
    qpos_ref,
    kidx_ref,
    q_ref,
    do_ref,
    centre_ref,
    kv_ref,
    proj_ref,
    gain_ref,
    cos_ref,
    sin_ref,
    dkv_ref,
    dq_ref,
    dgain_ref,
    acc_ref,
):
    heads, rows, size = q_ref.shape[1:]
    last = qpos_ref[pl.program_id(0)]

    @pl.when(pl.program_id(0) == 0)
    def _():
        dkv_ref[...] = jnp.zeros_like(dkv_ref)
        dgain_ref[...] = jnp.zeros_like(dgain_ref)

    acc_ref[...] = jnp.zeros_like(acc_ref)

    def step(place, masked):
        start = pl.multiple_of(kidx_ref[place] * rows, rows)
        keys = kv_ref[pl.ds(start, rows), :size]
        values = kv_ref[pl.ds(start, rows), size:]
        dk = dkv_ref[pl.ds(start, rows), :size]
        dv = dkv_ref[pl.ds(start, rows), size:]
        for h in range(heads):
            query, grad = q_ref[0, h], do_ref[0, h]
            e = jnp.exp2(dot_nt(keys, query))
            if masked:
                ki = lax.broadcasted_iota(jnp.int32, e.shape, 0)
                qi = lax.broadcasted_iota(jnp.int32, e.shape, 1)
                e = jnp.where(ki <= qi, e, 0.0)
            ds = (e * (dot_nt(values, grad) - centre_ref[0, h, 0:1])).astype(LOW)
            dv += dot_nn(e.astype(LOW), grad)
            dk += dot_nn(ds, query)
            acc_ref[h] += dot_tn(ds, keys)
        dkv_ref[pl.ds(start, rows), :size] = dk
        dkv_ref[pl.ds(start, rows), size:] = dv

    lax.fori_loop(0, last, lambda p, c: (step(p, False), c)[1], 0)
    step(last, True)
    total = jnp.zeros((1, size), F32)
    for h in range(heads):
        grad, gain_part = head_backward(
            acc_ref[h] * (1.0 / LOG2E), proj_ref[0, h], gain_ref[...], cos_ref[...], sin_ref[...]
        )
        dq_ref[:, h * size : (h + 1) * size] = grad.astype(LOW)
        total += gain_part
    dgain_ref[...] += total


def attend_back(qpos, kidx, queries, grads, centre, kv, proj, gain, cos2, sin2):
    tiles, heads, rows, size = queries.shape
    seq = kv.shape[0]
    per = pl.BlockSpec((1, heads, rows, size), lambda i, a, b: (i, 0, 0, 0))
    flat = lambda i, a, b: (0, 0)
    rowwise = lambda i, a, b: (i, 0)
    return pl.pallas_call(
        attend_back_kernel,
        grid_spec=pltpu.PrefetchScalarGridSpec(
            num_scalar_prefetch=2,
            grid=(tiles,),
            in_specs=[
                per,
                per,
                pl.BlockSpec((1, heads, 8, rows), lambda i, a, b: (i, 0, 0, 0)),
                pl.BlockSpec((seq, 2 * size), flat),
                per,
                pl.BlockSpec((1, size), flat),
                pl.BlockSpec((rows, size), rowwise),
                pl.BlockSpec((rows, size), rowwise),
            ],
            out_specs=[
                pl.BlockSpec((seq, 2 * size), flat),
                pl.BlockSpec((rows, heads * size), rowwise),
                pl.BlockSpec((1, size), flat),
            ],
            scratch_shapes=[pltpu.VMEM((heads, rows, size), F32)],
        ),
        out_shape=[
            jax.ShapeDtypeStruct((seq, 2 * size), F32),
            jax.ShapeDtypeStruct((tiles * rows, heads * size), LOW),
            jax.ShapeDtypeStruct((1, size), F32),
        ],
        compiler_params=params(),
        cost_estimate=cost(
            15 * tiles * rows * heads * seq * size, 12e6, tiles * rows * heads * seq
        ),
    )(qpos, kidx, queries, grads, centre, kv, proj, gain[None], cos2, sin2)


def sum_small(flat):
    n = lax.axis_size(ALL_AXES)
    length = flat.shape[0]
    each = -(-length // (n * 128)) * 128
    parts = jnp.pad(flat, (0, n * each - length)).reshape(n, each)
    parts = lax.all_to_all(parts, ALL_AXES, split_axis=0, concat_axis=0, tiled=True)
    own = jnp.sum(parts, axis=0, keepdims=True)
    whole = lax.all_to_all(
        jnp.broadcast_to(own, (n, each)), ALL_AXES, split_axis=0, concat_axis=0, tiled=True
    )
    return whole.reshape(-1)[:length]


def swap_dp(rows):
    return lax.ppermute(rows, "dp", [(0, 1), (1, 0)])


def sum_groups(grad):
    n_dp, n_context = lax.axis_size("dp"), lax.axis_size("context")
    if (n_dp, n_context) != (2, 4):
        return lax.psum(grad, GROUP_AXES).astype(F32)
    d, c = lax.axis_index("dp"), lax.axis_index("context")
    low_bit, high_bit = c % 2, c // 2
    turns = [
        (
            jnp.where(d == 0, low_bit, high_bit),
            [(i, i ^ 1) for i in range(4)] + [(4 + i, 4 + (i ^ 2)) for i in range(4)],
        ),
        (
            jnp.where(d == 0, high_bit, low_bit),
            [(i, i ^ 2) for i in range(4)] + [(4 + i, 4 + (i ^ 1)) for i in range(4)],
        ),
    ]
    swaps = [(d, swap_dp)] + [
        (bit, functools.partial(lax.ppermute, axis_name=GROUP_AXES, perm=perm))
        for bit, perm in turns
    ]
    part = grad
    for bit, swap in swaps:
        rows = part.shape[0] // 2
        got = swap(lax.dynamic_slice_in_dim(part, (1 - bit) * rows, rows))
        kept = lax.dynamic_slice_in_dim(part, bit * rows, rows)
        part = (kept.astype(F32) + got.astype(F32)).astype(LOW)
    for bit, swap in reversed(swaps):
        got = swap(part)
        part = jnp.concatenate(
            [jnp.where(bit == 0, part, got), jnp.where(bit == 0, got, part)], axis=0
        )
    return part.astype(F32)


def arrival_order(n):
    return [sorted(range(n), key=lambda j: (abs(j - i), j)) for i in range(n)]


def choose(index, options):
    distinct = []
    for option in options:
        if option is not None and not any(option is other for other in distinct):
            distinct.append(option)
    result = distinct[0]
    for option in distinct[1:]:
        mask = functools.reduce(
            jnp.logical_or, [index == i for i, other in enumerate(options) if other is option]
        )
        result = jnp.where(mask, option, result)
    return result


def line_gather(chunk):
    n = lax.axis_size("expert")
    found = {0: chunk}
    for s in range(1, n):
        found[-s] = lax.ppermute(
            found[1 - s], "expert", [(i, i + 1) for i in range(s - 1, n - 1)]
        )
        found[s] = lax.ppermute(found[s - 1], "expert", [(i + 1, i) for i in range(n - s)])
    return found


def by_arrival(found):
    n = lax.axis_size("expert")
    order = arrival_order(n)
    me = lax.axis_index("expert")
    return [choose(me, [found[order[i][r] - i] for i in range(n)]) for r in range(n)]


def in_place(found):
    n = lax.axis_size("expert")
    me = lax.axis_index("expert")
    return jnp.concatenate(
        [choose(me, [found[j - i] for i in range(n)]) for j in range(n)], axis=0
    )


def line_reduce(piece):
    n = lax.axis_size("expert")
    add = lambda a, b: (a.astype(F32) + b.astype(F32)).astype(LOW)
    left = right = None
    for s in range(1, n):
        out_left, out_right = piece(-1, s), piece(1, s)
        if s > 1:
            out_left, out_right = add(out_left, left), add(out_right, right)
        left = lax.ppermute(out_left, "expert", [(i, i - 1) for i in range(n - s, n)])
        right = lax.ppermute(out_right, "expert", [(i, i + 1) for i in range(s)])
    return piece(0, n).astype(F32) + left.astype(F32) + right.astype(F32)


def reduce_in_place(partial):
    n = lax.axis_size("expert")
    me = lax.axis_index("expert")
    rows = partial.shape[0] // n

    def piece(side, s):
        owner = jnp.clip(me + side * (n - s), 0, n - 1)
        return lax.dynamic_slice_in_dim(partial, owner * rows, rows)

    return line_reduce(piece)


def reduce_by_arrival(pieces):
    n = lax.axis_size("expert")
    me = lax.axis_index("expert")
    order = arrival_order(n)

    def piece(side, s):
        options = []
        for i in range(n):
            owner = i + side * (n - s)
            options.append(pieces[order[i].index(owner)] if 0 <= owner < n else None)
        return choose(me, options)

    return line_reduce(piece)


def context_gather(rows):
    n = lax.axis_size("context")
    c = lax.axis_index("context")
    found = {0: rows}
    for s in range(1, n):
        found[s] = lax.ppermute(rows, "context", [(i, i ^ s) for i in range(n)])
    return jnp.concatenate([choose(c, [found[i ^ j] for i in range(n)]) for j in range(n)], axis=0)


def context_reduce(rows):
    n = lax.axis_size("context")
    c = lax.axis_index("context")
    each = rows.shape[0] // n
    take = lambda j: lax.dynamic_slice_in_dim(rows, j * each, each)
    total = take(c).astype(F32)
    for s in range(1, n):
        total += lax.ppermute(
            take(c ^ s).astype(LOW), "context", [(i, i ^ s) for i in range(n)]
        ).astype(F32)
    return total


def zero_of(*others):
    return functools.reduce(
        jnp.add, [other.reshape(-1)[0].astype(F32) * 0.0 for other in others]
    )


def after(value, *others):
    return (value.astype(F32) + zero_of(*others)).astype(value.dtype)


def norm_parts(rows):
    rr = lax.rsqrt(jnp.mean(rows * rows, axis=-1, keepdims=True) + EPS)
    return rows * rr, rr


def norm_back(grad, normal, rr, gain):
    weighted = grad * gain
    return rr * (weighted - normal * jnp.mean(weighted * normal, axis=-1, keepdims=True))


def on_device(
    layer_input,
    grad_output,
    attn_gain,
    query_weight,
    key_weight,
    value_weight,
    q_gain,
    k_gain,
    output_weight,
    mlp_gain,
    router,
    w_gate,
    w_up,
    w_down,
    routes,
    half_order,
):
    n_context = lax.axis_size("context")
    n_expert = lax.axis_size("expert")
    n_groups = lax.axis_size(GROUP_AXES)
    tok_dev, width = layer_input.shape[1:]
    size = q_gain.shape[0]
    kv_total = key_weight.shape[1] * n_expert
    group_dev = n_expert // (kv_total // size)
    kv_index = lax.axis_index("expert") // group_dev
    block = tok_dev * n_expert
    seq = block * n_context
    half = block // 2
    experts = router.shape[1]
    top = routes.shape[2]
    capacity = max(2, (tok_dev * top * 9 + 8 * experts - 1) // (8 * experts))
    scale = size ** (-0.5)

    seq_rows = jnp.arange(seq, dtype=jnp.int32)
    context = lax.axis_index("context")
    own_halves = lax.dynamic_slice_in_dim(half_order, 2 * context, 2)
    own_pos = (own_halves[:, None] * half + jnp.arange(half, dtype=jnp.int32)[None]).reshape(-1)
    per_half = half // TILE
    tile_pos = (half_order[:, None] * per_half + jnp.arange(per_half, dtype=jnp.int32)).reshape(-1)
    kidx = jnp.sum(
        (tile_pos[None, :] == jnp.arange(seq // TILE, dtype=jnp.int32)[:, None])
        * jnp.arange(seq // TILE, dtype=jnp.int32)[None, :],
        axis=1,
    ).astype(jnp.int32)
    qpos = lax.dynamic_slice_in_dim(tile_pos, context * (block // TILE), block // TILE)
    freq = jnp.power(THETA, -jnp.arange(0, size, 2).astype(F32) / size)
    angles = own_pos.astype(F32)[:, None] * freq[None, :]
    cosine, sine = jnp.cos(angles), jnp.sin(angles)
    cos2 = jnp.concatenate([cosine, cosine], axis=1)
    sin2 = jnp.concatenate([-sine, sine], axis=1)

    x_rows = layer_input[0].astype(F32)
    x_normal, x_rr = norm_parts(x_rows)
    normed_found = line_gather((x_normal * attn_gain).astype(LOW))
    normed_rows = in_place(normed_found)
    if group_dev == 1:
        kv_weights = jnp.concatenate([key_weight, value_weight], axis=1)
    else:
        key_whole = lax.all_gather(key_weight, "expert", axis=1, tiled=True)
        value_whole = lax.all_gather(value_weight, "expert", axis=1, tiled=True)
        kv_weights = jnp.concatenate(
            [
                lax.dynamic_slice_in_dim(key_whole, kv_index * size, size, 1),
                lax.dynamic_slice_in_dim(value_whole, kv_index * size, size, 1),
            ],
            axis=1,
        )
    own_kv, key_proj = project_keys(normed_rows, kv_weights, k_gain, cos2, sin2, scale * LOG2E)
    kv_whole = context_gather(own_kv)
    queries, query_proj = project_queries(normed_rows, query_weight, q_gain, cos2, sin2)

    grad_low = grad_output[0]
    last = n_expert - 1
    grad_found = line_gather(after(grad_low, own_kv))
    grad_pieces = by_arrival(grad_found)
    order = arrival_order(n_expert)
    place = lax.axis_index("expert")
    order_here = jnp.asarray(order, jnp.int32)[place]
    back_here = jnp.argsort(order_here).astype(jnp.int32)
    routes_col = jnp.take(lax.all_gather(routes[0], "expert", axis=0), order_here, axis=0)
    group_ids = jnp.arange(n_groups, dtype=jnp.int32) * n_expert + place
    col_hits = jnp.any(routes_col[:, :, :, None] == group_ids, axis=2)
    earlier = jnp.tril(jnp.ones((tok_dev, tok_dev), LOW), -1)
    col_ranks = jnp.einsum(
        "ts,zsd->ztd", earlier, col_hits.astype(LOW), preferred_element_type=F32
    ).astype(jnp.int32)
    n_half = n_expert // 2
    cap_half = n_half * capacity
    token_half = n_half * tok_dev
    spreads = []
    for part in range(2):
        pick = slice(part * n_half, (part + 1) * n_half)
        slots = col_ranks[pick] + (jnp.arange(n_half, dtype=jnp.int32) * capacity)[:, None, None]
        slots = jnp.where(col_hits[pick], slots, -1).reshape(token_half, n_groups)
        spreads.append(
            (slots.T[:, None, :] == jnp.arange(cap_half, dtype=jnp.int32)[None, :, None])
            .astype(LOW)
            .reshape(n_groups * cap_half, token_half)
        )

    def swap_plane(rows):
        rows = lax.all_to_all(
            rows.reshape(n_groups, cap_half, width),
            GROUP_AXES,
            split_axis=0,
            concat_axis=0,
            tiled=True,
        )
        return rows.reshape(n_groups * cap_half, width)

    def to_experts(part, pieces, extra=0.0):
        rows = jnp.concatenate(pieces[part * n_half : (part + 1) * n_half], axis=0)
        return swap_plane((dot_nn(spreads[part], rows) + extra).astype(LOW))

    def from_experts(part, rows):
        rows = dot_tn(spreads[part], swap_plane(rows)).astype(LOW)
        return [rows[z * tok_dev : (z + 1) * tok_dev] for z in range(n_half)]

    attended, inverse = attend(
        qpos, kidx, queries, kv_whole, [grad_found[1], grad_found[-1]]
    )
    attn_part = dot_nn(attended, output_weight) + zero_of(grad_found[last], grad_found[-last])
    attn_rows = reduce_in_place(attn_part.astype(LOW))

    grad_x = [to_experts(part, grad_pieces) for part in range(2)]
    act_pull = [dot_nt(rows, w_down[0]) for rows in grad_x]

    hidden = x_rows + attn_rows + zero_of(grad_x[0])
    h_normal, h_rr = norm_parts(hidden)
    mixed = (h_normal * mlp_gain).astype(LOW)
    mixed_pieces = by_arrival(line_gather(mixed))
    logits = dot_nn(mixed, router)
    own_mask = jnp.any(
        routes[0][:, :, None] == jnp.arange(experts, dtype=jnp.int32)[None, None, :], axis=1
    )
    own_ranks = dot_nn(earlier, own_mask.astype(LOW)).astype(jnp.int32)
    own_slots = jnp.where(own_mask, own_ranks, -1)
    own_spread = own_slots.T[:, None, :] == jnp.arange(capacity, dtype=jnp.int32)[None, :, None]
    probs = jax.nn.softmax(logits, axis=-1)
    chosen = jnp.where(own_mask, probs, 0.0)
    chosen_sum = jnp.sum(chosen, axis=1, keepdims=True)
    gates = chosen / chosen_sum
    gate_slots = jnp.sum(jnp.where(own_spread, gates.T[:, None, :], 0.0), axis=2)
    gate_rows = lax.all_to_all(gate_slots, ALL_AXES, split_axis=0, concat_axis=0, tiled=True)
    gate_rows = jnp.take(gate_rows.reshape(n_groups, n_expert, capacity), order_here, axis=1)

    xs, acts, gate_lows, up_lows, copies, gate_parts, outs, grad_rets = ([] for _ in range(8))
    for part in range(2):
        x = to_experts(part, mixed_pieces, zero_of(grad_x[1]))
        gate_part = gate_rows[:, part * n_half : (part + 1) * n_half].reshape(-1, 1)
        pre_gate = dot_nn(x, w_gate[0])
        pre_up = dot_nn(x, w_up[0])
        sig = jax.nn.sigmoid(pre_gate)
        silu = pre_gate * sig
        act = (silu * pre_up).astype(LOW)
        pull = act_pull[part]
        gate_parts.append(
            jnp.sum(act.astype(F32) * pull, axis=1).reshape(n_groups, n_half, capacity)
        )
        grad_act = gate_part * pull
        gate_low = (grad_act * pre_up * (sig * (1.0 + pre_gate * (1.0 - sig)))).astype(LOW)
        up_low = (grad_act * silu).astype(LOW)
        copies.append((dot_nt(gate_low, w_gate[0]) + dot_nt(up_low, w_up[0])).astype(LOW))
        outs.append((act, gate_part))
        grad_rets.append((grad_x[part].astype(F32) * gate_part).astype(LOW))
        xs.append(x)
        acts.append(act)
        gate_lows.append(gate_low)
        up_lows.append(up_low)
    gate_grads = jnp.take(jnp.concatenate(gate_parts, axis=1), back_here, axis=1)
    gate_back = lax.all_to_all(
        gate_grads.reshape(-1, capacity), ALL_AXES, split_axis=0, concat_axis=0, tiled=True
    )
    copies_far = from_experts(1, copies[1])
    copies_near = from_experts(0, copies[0])
    grad_mixed = reduce_by_arrival(copies_near + copies_far)
    returned = [(dot_nn(act, w_down[0]) * gate_part).astype(LOW) for act, gate_part in outs]
    join = lambda parts: jnp.concatenate(parts, axis=0)
    grad_w_down = dot_tn(join(acts), join(grad_rets))
    x_all = join(xs)
    grad_w_gate = dot_tn(x_all, join(gate_lows))
    grad_w_up = dot_tn(x_all, join(up_lows))

    grad_gates = jnp.sum(jnp.where(own_spread, gate_back[:, :, None], 0.0), axis=1).T
    centred = grad_gates - jnp.sum(grad_gates * gates, axis=1, keepdims=True)
    centred = jnp.where(own_mask, centred / chosen_sum, 0.0)
    grad_logits = probs * (centred - jnp.sum(centred * chosen, axis=1, keepdims=True))
    high = lax.Precision.HIGHEST
    grad_mixed = grad_mixed + jnp.einsum(
        "te,de->td", grad_logits, router.astype(F32), precision=high
    )
    grad_router = jnp.einsum("te,td->ed", grad_logits, mixed.astype(F32), precision=high)
    grad_rows = grad_low.astype(F32)
    grad_hidden = grad_rows + norm_back(grad_mixed, h_normal, h_rr, mlp_gain)
    grad_mlp_gain = jnp.sum(grad_mixed * h_normal, axis=0)

    grad_attn = in_place(line_gather(grad_hidden.astype(LOW)))
    grad_o, centre = grad_attended(grad_attn, output_weight, attended, inverse)
    grad_w_out = sum_groups(dot_tn(attended, grad_attn).astype(LOW))
    grad_kv, grad_q, grad_q_gain = attend_back(
        qpos, kidx, queries, grad_o, centre, kv_whole, query_proj, q_gain, cos2, sin2
    )
    grad_kv = context_reduce(grad_kv)
    grad_w_query = sum_groups(dot_tn(normed_rows, grad_q).astype(LOW))

    returned_far = from_experts(1, after(returned[1], copies_near[0]))
    returned_near = from_experts(0, after(returned[0], copies_near[0]))
    output_rows = hidden + reduce_by_arrival(returned_near + returned_far)

    gk = grad_kv[:, :size] * scale
    roll = lambda v: jnp.concatenate([v[:, size // 2 :], v[:, : size // 2]], axis=1)
    gk = gk * cos2 - roll(gk) * sin2
    k_normal, k_rr = norm_parts(key_proj)
    grad_k_gain = jnp.sum(gk * k_normal, axis=0)
    gk = norm_back(gk, k_normal, k_rr, k_gain)
    kv_grads = jnp.concatenate([gk, grad_kv[:, size:]], axis=1).astype(LOW)

    grad_normed = dot_nt(grad_q, query_weight) + dot_nt(kv_grads, kv_weights)
    grad_attn_gain = jnp.sum(grad_normed * normed_rows.astype(F32), axis=0) / attn_gain
    grad_normed = reduce_in_place(grad_normed.astype(LOW))
    grad_w_kv = dot_tn(normed_rows, kv_grads).astype(LOW)
    if group_dev == 1:
        grad_w_kv = sum_groups(grad_w_kv)
        grad_w_key, grad_w_value = grad_w_kv[:, :size], grad_w_kv[:, size:]
    else:
        blank = jnp.zeros((width, kv_total), LOW)
        pieces = []
        for part in (grad_w_kv[:, :size], grad_w_kv[:, size:]):
            padded = lax.dynamic_update_slice(blank, part, (0, kv_index * size))
            pieces.append(
                lax.psum_scatter(padded, "expert", scatter_dimension=1, tiled=True)
            )
        grad_w_key, grad_w_value = (
            lax.psum(piece, GROUP_AXES).astype(F32) for piece in pieces
        )
    grad_input = grad_hidden + norm_back(grad_normed, x_normal, x_rr, attn_gain)

    small = [grad_attn_gain, grad_mlp_gain, grad_q_gain[0], grad_k_gain, grad_router.reshape(-1)]
    summed = sum_small(jnp.concatenate(small))
    pieces = []
    offset = 0
    for part in small:
        pieces.append(summed[offset : offset + part.shape[0]])
        offset += part.shape[0]
    grad_attn_gain, grad_mlp_gain, grad_q_gain, grad_k_gain, grad_router = pieces
    return (
        output_rows.astype(LOW)[None],
        grad_input[None],
        grad_attn_gain,
        grad_w_query,
        grad_w_key,
        grad_w_value,
        grad_q_gain,
        grad_k_gain,
        grad_w_out,
        grad_mlp_gain,
        grad_router.reshape(experts, width).T,
        grad_w_gate[None],
        grad_w_up[None],
        grad_w_down[None],
    )


def solution(mesh):
    rows = P("dp", ("context", "expert"), None)
    expert = P(ALL_AXES, None, None)
    columns = P(None, "expert")
    in_specs = (
        rows,
        rows,
        P(),
        columns,
        columns,
        columns,
        P(),
        P(),
        P("expert", None),
        P(),
        P(),
        expert,
        expert,
        expert,
        rows,
        P(),
    )
    out_specs = (
        rows,
        rows,
        P(),
        columns,
        columns,
        columns,
        P(),
        P(),
        P("expert", None),
        P(),
        P(),
        expert,
        expert,
        expert,
    )
    return jax.shard_map(
        on_device, mesh=mesh, in_specs=in_specs, out_specs=out_specs, check_vma=False
    )
```

```python
import functools
import math

import jax
import jax.numpy as jnp
from jax import lax
from jax.experimental import pallas as pl
from jax.experimental.pallas import tpu as pltpu
from jax.sharding import PartitionSpec as P

EPS = 1e-06
THETA = 1000000.0
TILE = 256
VMEM_BYTES = 56 * 1024 * 1024
LOG2E = math.log2(math.e)
LOW = jnp.bfloat16
F32 = jnp.float32
ALL_AXES = ("dp", "context", "expert")
GROUP_AXES = ("dp", "context")


def dot_nn(a, b):
    return lax.dot_general(a, b, (((1,), (0,)), ((), ())), preferred_element_type=F32)


def dot_nt(a, b):
    return lax.dot_general(a, b, (((1,), (1,)), ((), ())), preferred_element_type=F32)


def dot_tn(a, b):
    return lax.dot_general(a, b, (((0,), (0,)), ((), ())), preferred_element_type=F32)


def params(**more):
    return pltpu.CompilerParams(vmem_limit_bytes=VMEM_BYTES, **more)


def cost(flops, nbytes, exps=0):
    return pl.CostEstimate(flops=int(flops), bytes_accessed=int(nbytes), transcendentals=int(exps))


def head_forward(u, gain, cos2, sin2):
    rr = lax.rsqrt(jnp.mean(u * u, axis=-1, keepdims=True) + EPS)
    y = u * rr * gain
    return y * cos2 + pltpu.roll(y, 64, 1) * sin2


def head_backward(gy, u, gain, cos2, sin2):
    g = gy * cos2 - pltpu.roll(gy, 64, 1) * sin2
    rr = lax.rsqrt(jnp.mean(u * u, axis=-1, keepdims=True) + EPS)
    n = u * rr
    gn = g * gain
    grad = rr * (gn - n * jnp.mean(gn * n, axis=-1, keepdims=True))
    return grad, jnp.sum(g * n, axis=0, keepdims=True)


def query_kernel(x_ref, w_ref, gain_ref, cos_ref, sin_ref, rot_ref, proj_ref):
    tiles, heads, rows, size = rot_ref.shape
    acc = dot_nn(x_ref[...], w_ref[...])
    for h in range(heads):
        u = acc[:, h * size : (h + 1) * size]
        rot = head_forward(u, gain_ref[...], cos_ref[...], sin_ref[...])
        proj_ref[:, h] = u.reshape(tiles, rows, size)
        rot_ref[:, h] = rot.astype(LOW).reshape(tiles, rows, size)


def project_queries(normed, weight, gain, cos2, sin2):
    block, width = normed.shape
    size = cos2.shape[1]
    heads = weight.shape[1] // size
    tiles = block // TILE
    whole = lambda i: (0, 0)
    per = lambda i: (0, i, 0, 0)
    shape = (tiles, heads, TILE, size)
    return pl.pallas_call(
        query_kernel,
        grid=(heads // 2,),
        in_specs=[
            pl.BlockSpec((block, width), whole),
            pl.BlockSpec((width, 2 * size), lambda i: (0, i)),
            pl.BlockSpec((1, size), whole),
            pl.BlockSpec((block, size), whole),
            pl.BlockSpec((block, size), whole),
        ],
        out_specs=[pl.BlockSpec((tiles, 2, TILE, size), per)] * 2,
        out_shape=[jax.ShapeDtypeStruct(shape, LOW), jax.ShapeDtypeStruct(shape, F32)],
        compiler_params=params(),
        cost_estimate=cost(2 * block * width * heads * size, 12e6),
    )(normed, weight, gain[None], cos2, sin2)


def put_in_order(place, refs, out_ref):
    n = (len(refs) + 1) // 2
    rows = refs[0].shape[0]
    for distance in range(1 - n, n):
        ref = refs[distance + n - 1]
        at = place + distance

        @pl.when(jnp.logical_and(at >= 0, at < n))
        def _():
            out_ref[pl.ds(pl.multiple_of(at * rows, rows), rows), :] = ref[...]


def chunk_list(found):
    n = (len(found) + 1) // 2
    return [found[distance] for distance in range(1 - n, n)]


def key_kernel(factor, place_ref, *refs):
    w_ref, gain_ref, cos_ref, sin_ref, rows_ref, kv_ref, proj_ref = refs[-7:]
    size = proj_ref.shape[1]
    put_in_order(place_ref[0], refs[:-7], rows_ref)
    acc = dot_nn(rows_ref[...], w_ref[...])
    u = acc[:, :size]
    rot = head_forward(u, gain_ref[...], cos_ref[...], sin_ref[...])
    proj_ref[...] = u
    kv_ref[:, :size] = (rot * factor).astype(LOW)
    kv_ref[:, size:] = acc[:, size:].astype(LOW)


def full(shape):
    return pl.BlockSpec(shape, lambda *_: (0,) * len(shape))


def project_keys(place, found, weight, gain, cos2, sin2, factor):
    chunks = chunk_list(found)
    rows, width = chunks[0].shape
    block, size = cos2.shape
    operands = [*chunks, weight, gain[None], cos2, sin2]
    shapes = [
        jax.ShapeDtypeStruct((block, width), LOW),
        jax.ShapeDtypeStruct((block, 2 * size), LOW),
        jax.ShapeDtypeStruct((block, size), F32),
    ]
    return pl.pallas_call(
        functools.partial(key_kernel, factor),
        grid_spec=pltpu.PrefetchScalarGridSpec(
            num_scalar_prefetch=1,
            grid=(1,),
            in_specs=[full(x.shape) for x in operands],
            out_specs=[full(x.shape) for x in shapes],
        ),
        out_shape=shapes,
        compiler_params=params(),
        cost_estimate=cost(4 * block * width * size, 8e6),
    )(place, *operands)


def attend_kernel(qpos_ref, kidx_ref, q_ref, kv_ref, *rest):
    out_ref, inv_ref, acc_ref = rest[-3:]
    heads, rows, size = q_ref.shape[1:]
    last = qpos_ref[pl.program_id(0)]
    acc_ref[...] = jnp.zeros_like(acc_ref)
    ones = jnp.ones((rows, size), LOW)

    def step(place, masked):
        start = pl.multiple_of(kidx_ref[place] * rows, rows)
        keys = kv_ref[pl.ds(start, rows), :size]
        values = jnp.concatenate([kv_ref[pl.ds(start, rows), size:], ones], axis=1)
        for h in range(heads):
            e = jnp.exp2(dot_nt(q_ref[0, h], keys))
            if masked:
                qi = lax.broadcasted_iota(jnp.int32, e.shape, 0)
                ki = lax.broadcasted_iota(jnp.int32, e.shape, 1)
                e = jnp.where(ki <= qi, e, 0.0)
            acc_ref[h] += dot_nn(e.astype(LOW), values)

    lax.fori_loop(0, last, lambda p, c: (step(p, False), c)[1], 0)
    step(last, True)
    for h in range(heads):
        inv = 1.0 / acc_ref[h, :, size:]
        inv_ref[0, h] = inv
        out_ref[:, h * size : (h + 1) * size] = (acc_ref[h, :, :size] * inv).astype(LOW)


def attend(qpos, kidx, queries, kv, others):
    tiles, heads, rows, size = queries.shape
    seq = kv.shape[0]
    return pl.pallas_call(
        attend_kernel,
        grid_spec=pltpu.PrefetchScalarGridSpec(
            num_scalar_prefetch=2,
            grid=(tiles,),
            in_specs=[
                pl.BlockSpec((1, heads, rows, size), lambda i, a, b: (i, 0, 0, 0)),
                pl.BlockSpec((seq, 2 * size), lambda i, a, b: (0, 0)),
            ]
            + [pl.BlockSpec(memory_space=pl.ANY)] * len(others),
            out_specs=[
                pl.BlockSpec((rows, heads * size), lambda i, a, b: (i, 0)),
                pl.BlockSpec((1, heads, rows, size), lambda i, a, b: (i, 0, 0, 0)),
            ],
            scratch_shapes=[pltpu.VMEM((heads, rows, 2 * size), F32)],
        ),
        out_shape=[
            jax.ShapeDtypeStruct((tiles * rows, heads * size), LOW),
            jax.ShapeDtypeStruct((tiles, heads, rows, size), F32),
        ],
        compiler_params=params(),
        cost_estimate=cost(
            6 * tiles * rows * heads * seq * size, 8e6, tiles * rows * heads * seq
        ),
    )(qpos, kidx, queries, kv, *others)


def grad_out_kernel(place_ref, *refs):
    w_ref, o_ref, inv_ref, rows_ref, do_ref, centre_ref = refs[-6:]
    tiles, heads, rows, size = do_ref.shape

    @pl.when(pl.program_id(0) == 0)
    def _():
        put_in_order(place_ref[0], refs[:-6], rows_ref)

    acc = dot_nt(rows_ref[...], w_ref[...])
    ones = jnp.ones((8, size), F32)
    for t in range(tiles):
        for h in range(heads):
            part = slice(t * rows, (t + 1) * rows), slice(h * size, (h + 1) * size)
            low = (acc[part] * inv_ref[t, h]).astype(LOW)
            do_ref[t, h] = low
            product = low.astype(F32) * o_ref[part].astype(F32)
            centre_ref[t, h] = lax.dot_general(
                ones,
                product,
                (((1,), (1,)), ((), ())),
                precision=lax.Precision.HIGHEST,
                preferred_element_type=F32,
            )


def grad_attended(place, found, weight, attended, inverse):
    chunks = chunk_list(found)
    tiles, heads, rows, size = inverse.shape
    width = weight.shape[1]
    block = attended.shape[0]
    return pl.pallas_call(
        grad_out_kernel,
        grid_spec=pltpu.PrefetchScalarGridSpec(
            num_scalar_prefetch=1,
            grid=(heads // 2,),
            in_specs=[full(x.shape) for x in chunks]
            + [
                pl.BlockSpec((2 * size, width), lambda i, p: (i, 0)),
                pl.BlockSpec((block, 2 * size), lambda i, p: (0, i)),
                pl.BlockSpec((tiles, 2, rows, size), lambda i, p: (0, i, 0, 0)),
            ],
            out_specs=[
                full((block, width)),
                pl.BlockSpec((tiles, 2, rows, size), lambda i, p: (0, i, 0, 0)),
                pl.BlockSpec((tiles, 2, 8, rows), lambda i, p: (0, i, 0, 0)),
            ],
        ),
        out_shape=[
            jax.ShapeDtypeStruct((block, width), LOW),
            jax.ShapeDtypeStruct((tiles, heads, rows, size), LOW),
            jax.ShapeDtypeStruct((tiles, heads, 8, rows), F32),
        ],
        compiler_params=params(),
        cost_estimate=cost(2 * block * width * heads * size, 12e6),
    )(place, *chunks, weight, attended, inverse)


def attend_back_kernel(
    qpos_ref,
    kidx_ref,
    q_ref,
    do_ref,
    centre_ref,
    kv_ref,
    proj_ref,
    gain_ref,
    cos_ref,
    sin_ref,
    *rest,
):
    dkv_ref, dq_ref, dgain_ref, acc_ref = rest[-4:]
    heads, rows, size = q_ref.shape[1:]
    last = qpos_ref[pl.program_id(0)]

    @pl.when(pl.program_id(0) == 0)
    def _():
        dkv_ref[...] = jnp.zeros_like(dkv_ref)
        dgain_ref[...] = jnp.zeros_like(dgain_ref)

    acc_ref[...] = jnp.zeros_like(acc_ref)

    def step(place, masked):
        start = pl.multiple_of(kidx_ref[place] * rows, rows)
        keys = kv_ref[pl.ds(start, rows), :size]
        values = kv_ref[pl.ds(start, rows), size:]
        dk = dkv_ref[pl.ds(start, rows), :size]
        dv = dkv_ref[pl.ds(start, rows), size:]
        for h in range(heads):
            query, grad = q_ref[0, h], do_ref[0, h]
            e = jnp.exp2(dot_nt(keys, query))
            if masked:
                ki = lax.broadcasted_iota(jnp.int32, e.shape, 0)
                qi = lax.broadcasted_iota(jnp.int32, e.shape, 1)
                e = jnp.where(ki <= qi, e, 0.0)
            ds = (e * (dot_nt(values, grad) - centre_ref[0, h, 0:1])).astype(LOW)
            dv += dot_nn(e.astype(LOW), grad)
            dk += dot_nn(ds, query)
            acc_ref[h] += dot_tn(ds, keys)
        dkv_ref[pl.ds(start, rows), :size] = dk
        dkv_ref[pl.ds(start, rows), size:] = dv

    lax.fori_loop(0, last, lambda p, c: (step(p, False), c)[1], 0)
    step(last, True)
    total = jnp.zeros((1, size), F32)
    for h in range(heads):
        grad, gain_part = head_backward(
            acc_ref[h] * (1.0 / LOG2E), proj_ref[0, h], gain_ref[...], cos_ref[...], sin_ref[...]
        )
        dq_ref[:, h * size : (h + 1) * size] = grad.astype(LOW)
        total += gain_part
    dgain_ref[...] += total


def attend_back(qpos, kidx, queries, grads, centre, kv, proj, gain, cos2, sin2, others):
    tiles, heads, rows, size = queries.shape
    seq = kv.shape[0]
    per = pl.BlockSpec((1, heads, rows, size), lambda i, a, b: (i, 0, 0, 0))
    flat = lambda i, a, b: (0, 0)
    rowwise = lambda i, a, b: (i, 0)
    return pl.pallas_call(
        attend_back_kernel,
        grid_spec=pltpu.PrefetchScalarGridSpec(
            num_scalar_prefetch=2,
            grid=(tiles,),
            in_specs=[
                per,
                per,
                pl.BlockSpec((1, heads, 8, rows), lambda i, a, b: (i, 0, 0, 0)),
                pl.BlockSpec((seq, 2 * size), flat),
                per,
                pl.BlockSpec((1, size), flat),
                pl.BlockSpec((rows, size), rowwise),
                pl.BlockSpec((rows, size), rowwise),
            ]
            + [pl.BlockSpec(memory_space=pl.ANY)] * len(others),
            out_specs=[
                pl.BlockSpec((seq, 2 * size), flat),
                pl.BlockSpec((rows, heads * size), rowwise),
                pl.BlockSpec((1, size), flat),
            ],
            scratch_shapes=[pltpu.VMEM((heads, rows, size), F32)],
        ),
        out_shape=[
            jax.ShapeDtypeStruct((seq, 2 * size), F32),
            jax.ShapeDtypeStruct((tiles * rows, heads * size), LOW),
            jax.ShapeDtypeStruct((1, size), F32),
        ],
        compiler_params=params(),
        cost_estimate=cost(
            15 * tiles * rows * heads * seq * size, 12e6, tiles * rows * heads * seq
        ),
    )(qpos, kidx, queries, grads, centre, kv, proj, gain[None], cos2, sin2, *others)


def split_low(value):
    high = value.astype(LOW)
    return high, (value - high.astype(F32)).astype(LOW)


def norm_parts(rows):
    rr = lax.rsqrt(jnp.mean(rows * rows, axis=-1, keepdims=True) + EPS)
    return rows * rr, rr


def norm_back(grad, normal, rr, gain):
    weighted = grad * gain
    return rr * (weighted - normal * jnp.mean(weighted * normal, axis=-1, keepdims=True))


def add_all(refs):
    return functools.reduce(jnp.add, [ref[...].astype(F32) for ref in refs])


def router_kernel(experts, place_ref, *refs):
    x_ref, own_ref, left_ref, right_ref, gain_ref, router_ref, mask_ref = refs[:7]
    hidden_ref, mixed_ref, probs_ref = refs[-3:]
    width = x_ref.shape[1]
    lanes = router_ref.shape[1]
    hidden = add_all([x_ref, own_ref, left_ref, right_ref])
    hidden_ref[...] = hidden
    mixed = (norm_parts(hidden)[0] * gain_ref[...]).astype(LOW)
    mixed_ref[:, :width] = mixed
    logits = dot_nn(mixed, router_ref[...])
    lane = lax.broadcasted_iota(jnp.int32, logits.shape, 1)
    logits = jnp.where(lane < experts, logits, -1e30)
    weights = jnp.exp(logits - jnp.max(logits, axis=1, keepdims=True))
    probs = weights / jnp.sum(weights, axis=1, keepdims=True)
    probs_ref[...] = probs
    chosen = probs * mask_ref[...]
    high, low = split_low(chosen / jnp.sum(chosen, axis=1, keepdims=True))
    both = high.astype(F32) + pltpu.roll(low.astype(F32), experts, 1)
    mixed_ref[:, width:] = both.astype(LOW)


def route_rows(place, x, partial, left, right, gain, router, mask, experts, others):
    tokens, width = x.shape
    lanes = router.shape[1]
    shapes = [
        jax.ShapeDtypeStruct((tokens, width), F32),
        jax.ShapeDtypeStruct((tokens, width + lanes), LOW),
        jax.ShapeDtypeStruct((tokens, lanes), F32),
    ]
    return pl.pallas_call(
        functools.partial(router_kernel, experts),
        grid_spec=pltpu.PrefetchScalarGridSpec(
            num_scalar_prefetch=1,
            grid=(1,),
            in_specs=[
                full(x.shape),
                pl.BlockSpec((tokens, width), lambda i, p: (p[0], 0)),
                full(left.shape),
                full(right.shape),
                full((1, width)),
                full(router.shape),
                full(mask.shape),
            ]
            + [pl.BlockSpec(memory_space=pl.ANY)] * len(others),
            out_specs=[full(shape.shape) for shape in shapes],
        ),
        out_shape=shapes,
        compiler_params=params(),
        cost_estimate=cost(2 * tokens * width * lanes, 5e6),
    )(place, x, partial, left, right, gain[None], router, mask, *others)


def router_back_kernel(experts, *refs):
    own_ref, left_ref, right_ref, g_ref, hidden_ref, gain_ref, router_ref, mask_ref, probs_ref = (
        refs[:9]
    )
    grad_ref, low_ref, dgain_ref, drouter_ref = refs[9:]
    width = g_ref.shape[1]
    lanes = router_ref.shape[1]
    total = add_all([own_ref, left_ref, right_ref])
    table = total[:, width:]
    mask, probs = mask_ref[...], probs_ref[...]
    grad_gates = (table + pltpu.roll(table, lanes - experts, 1)) * mask
    chosen = probs * mask
    chosen_sum = jnp.sum(chosen, axis=1, keepdims=True)
    mean = jnp.sum(grad_gates * (chosen / chosen_sum), axis=1, keepdims=True)
    centred = mask * (grad_gates - mean) / chosen_sum
    grad_logits = probs * (centred - jnp.sum(centred * chosen, axis=1, keepdims=True))
    high, low = split_low(grad_logits)
    router = router_ref[...]
    grad = total[:, :width] + dot_nt(high, router) + dot_nt(low, router)
    normal, rr = norm_parts(hidden_ref[...])
    mixed = (normal * gain_ref[...]).astype(LOW)
    drouter_ref[...] = dot_tn(high, mixed) + dot_tn(low, mixed)
    dgain_ref[...] = jnp.sum(grad * normal, axis=0, keepdims=True)
    grad_hidden = g_ref[...].astype(F32) + norm_back(grad, normal, rr, gain_ref[...])
    grad_ref[...] = grad_hidden
    low_ref[...] = grad_hidden.astype(LOW)


def route_back(own, left, right, g, hidden, gain, router, mask, probs, experts):
    tokens, width = g.shape
    lanes = router.shape[1]
    shapes = [
        jax.ShapeDtypeStruct((tokens, width), F32),
        jax.ShapeDtypeStruct((tokens, width), LOW),
        jax.ShapeDtypeStruct((1, width), F32),
        jax.ShapeDtypeStruct((lanes, width), F32),
    ]
    return pl.pallas_call(
        functools.partial(router_back_kernel, experts),
        grid=(1,),
        in_specs=[
            pl.BlockSpec((tokens, width + lanes), lambda i: (0, 0)),
            full(left.shape),
            full(right.shape),
            full(g.shape),
            full(hidden.shape),
            full((1, width)),
            full(router.shape),
            full(mask.shape),
            full(probs.shape),
        ],
        out_specs=[full(shape.shape) for shape in shapes],
        out_shape=shapes,
        compiler_params=params(),
        cost_estimate=cost(8 * tokens * width * lanes, 8e6),
    )(own, left, right, g, hidden, gain[None], router, mask, probs)


def expert_kernel(experts, who_ref, x_ref, gate_ref, up_ref, pull_ref, *outs):
    act_ref, dgate_ref, dup_ref, copy_ref = outs
    width = gate_ref.shape[0]
    x = x_ref[:, :width]
    table = x_ref[:, width:].astype(F32)
    lane = lax.broadcasted_iota(jnp.int32, table.shape, 1)
    mine = who_ref[0]
    gate = jnp.sum(
        jnp.where(jnp.logical_or(lane == mine, lane == mine + experts), table, 0.0),
        axis=1,
        keepdims=True,
    )
    pre_gate = dot_nn(x, gate_ref[...])
    pre_up = dot_nn(x, up_ref[...])
    pull = pull_ref[...]
    sig = 1.0 / (1.0 + jnp.exp(-pre_gate))
    silu = pre_gate * sig
    act = silu * pre_up
    act_ref[...] = (act * gate).astype(LOW)
    high, low = split_low(jnp.sum(act * pull, axis=1, keepdims=True))
    pull = pull * gate
    dup = (pull * silu).astype(LOW)
    dgate = (pull * pre_up * (sig * (1.0 + pre_gate * (1.0 - sig)))).astype(LOW)
    dgate_ref[...] = dgate
    dup_ref[...] = dup
    copy_ref[:, :width] = (dot_nt(dgate, gate_ref[...]) + dot_nt(dup, up_ref[...])).astype(LOW)
    back = jnp.where(lane == mine, high.astype(F32), 0.0)
    back = jnp.where(lane == mine + experts, low.astype(F32), back)
    copy_ref[:, width:] = back.astype(LOW)


def run_expert(who, x, w_gate, w_up, pull, experts):
    rows, wide = x.shape
    width, hidden = w_gate.shape
    tile = rows // 2 if rows % 32 == 0 else rows
    by_rows = lambda columns: pl.BlockSpec((tile, columns), lambda i, p: (i, 0))
    return pl.pallas_call(
        functools.partial(expert_kernel, experts),
        grid_spec=pltpu.PrefetchScalarGridSpec(
            num_scalar_prefetch=1,
            grid=(rows // tile,),
            in_specs=[by_rows(wide), full(w_gate.shape), full(w_up.shape), by_rows(hidden)],
            out_specs=[by_rows(hidden), by_rows(hidden), by_rows(hidden), by_rows(wide)],
        ),
        out_shape=[jax.ShapeDtypeStruct((rows, hidden), LOW)] * 3
        + [jax.ShapeDtypeStruct((rows, wide), LOW)],
        compiler_params=params(),
        cost_estimate=cost(8 * rows * width * hidden, 20e6, rows * hidden),
    )(who, x, w_gate, w_up, pull)


def input_kernel(place_ref, own_ref, left_ref, right_ref, x_ref, gain_ref, more_ref, out_ref):
    normal, rr = norm_parts(x_ref[...].astype(F32))
    grad = add_all([own_ref, left_ref, right_ref])
    out_ref[...] = more_ref[...] + norm_back(grad, normal, rr, gain_ref[...])


def input_back(place, partial, left, right, x, gain, more):
    tokens, width = x.shape
    return pl.pallas_call(
        input_kernel,
        grid_spec=pltpu.PrefetchScalarGridSpec(
            num_scalar_prefetch=1,
            grid=(1,),
            in_specs=[
                pl.BlockSpec((tokens, width), lambda i, p: (p[0], 0)),
                full(left.shape),
                full(right.shape),
                full(x.shape),
                full((1, width)),
                full(more.shape),
            ],
            out_specs=full(more.shape),
        ),
        out_shape=jax.ShapeDtypeStruct((tokens, width), F32),
        compiler_params=params(),
        cost_estimate=cost(20 * tokens * width, 5e6),
    )(place, partial, left, right, x, gain[None], more)


def sum_small(flat):
    n = lax.axis_size(ALL_AXES)
    length = flat.shape[0]
    each = -(-length // (n * 128)) * 128
    parts = jnp.pad(flat, (0, n * each - length)).reshape(n, each)
    parts = lax.all_to_all(parts, ALL_AXES, split_axis=0, concat_axis=0, tiled=True)
    own = jnp.sum(parts, axis=0, keepdims=True)
    whole = lax.all_to_all(
        jnp.broadcast_to(own, (n, each)), ALL_AXES, split_axis=0, concat_axis=0, tiled=True
    )
    return whole.reshape(-1)[:length]


def swap_dp(rows):
    return lax.ppermute(rows, "dp", [(0, 1), (1, 0)])


def share_context(parts):
    return lax.all_to_all(parts, "context", split_axis=0, concat_axis=0, tiled=True)


def half_groups(grad):
    d = lax.axis_index("dp")
    rows = grad.shape[0] // 2
    got = swap_dp(lax.dynamic_slice_in_dim(grad, (1 - d) * rows, rows))
    kept = lax.dynamic_slice_in_dim(grad, d * rows, rows)
    return (kept.astype(F32) + got.astype(F32)).astype(LOW)


def rest_groups(half):
    n = lax.axis_size("context")
    d = lax.axis_index("dp")
    rows, columns = half.shape
    parts = share_context(half.reshape(n, rows // n, columns))
    part = jnp.sum(parts.astype(F32), axis=0, keepdims=True).astype(LOW)
    half = share_context(jnp.broadcast_to(part, parts.shape)).reshape(rows, columns)
    got = swap_dp(half)
    return jnp.concatenate(
        [jnp.where(d == 0, half, got), jnp.where(d == 0, got, half)], axis=0
    ).astype(F32)


def arrival_order(n):
    return [sorted(range(n), key=lambda j: (abs(j - i), j)) for i in range(n)]


def choose(index, options):
    distinct = []
    for option in options:
        if option is not None and not any(option is other for other in distinct):
            distinct.append(option)
    result = distinct[0]
    for option in distinct[1:]:
        mask = functools.reduce(
            jnp.logical_or, [index == i for i, other in enumerate(options) if other is option]
        )
        result = jnp.where(mask, option, result)
    return result


def line_gather(chunk):
    n = lax.axis_size("expert")
    found = {0: chunk}
    for s in range(1, n):
        found[-s] = lax.ppermute(
            found[1 - s], "expert", [(i, i + 1) for i in range(s - 1, n - 1)]
        )
        found[s] = lax.ppermute(found[s - 1], "expert", [(i + 1, i) for i in range(n - s)])
    return found


def by_arrival(found):
    n = lax.axis_size("expert")
    order = arrival_order(n)
    me = lax.axis_index("expert")
    return [choose(me, [found[order[i][r] - i] for i in range(n)]) for r in range(n)]


def line_reduce(piece):
    n = lax.axis_size("expert")
    add = lambda a, b: (a.astype(F32) + b.astype(F32)).astype(LOW)
    left = right = None
    for s in range(1, n):
        out_left, out_right = piece(-1, s), piece(1, s)
        if s > 1:
            out_left, out_right = add(out_left, left), add(out_right, right)
        left = lax.ppermute(out_left, "expert", [(i, i - 1) for i in range(n - s, n)])
        right = lax.ppermute(out_right, "expert", [(i, i + 1) for i in range(s)])
    return left, right


def reduce_in_place(partial):
    n = lax.axis_size("expert")
    me = lax.axis_index("expert")
    rows = partial.shape[0] // n

    def piece(side, s):
        owner = jnp.clip(me + side * (n - s), 0, n - 1)
        return lax.dynamic_slice_in_dim(partial, owner * rows, rows)

    return line_reduce(piece)


def reduce_by_arrival(pieces):
    n = lax.axis_size("expert")
    me = lax.axis_index("expert")
    order = arrival_order(n)

    def piece(side, s):
        options = []
        for i in range(n):
            owner = i + side * (n - s)
            options.append(pieces[order[i].index(owner)] if 0 <= owner < n else None)
        return choose(me, options)

    return line_reduce(piece)


def context_gather(rows):
    n = lax.axis_size("context")
    c = lax.axis_index("context")
    found = {0: rows}
    for s in range(1, n):
        found[s] = lax.ppermute(rows, "context", [(i, i ^ s) for i in range(n)])
    return jnp.concatenate([choose(c, [found[i ^ j] for i in range(n)]) for j in range(n)], axis=0)


def context_reduce(rows):
    n = lax.axis_size("context")
    c = lax.axis_index("context")
    each = rows.shape[0] // n
    take = lambda j: lax.dynamic_slice_in_dim(rows, j * each, each)
    total = take(c).astype(F32)
    for s in range(1, n):
        total += lax.ppermute(
            take(c ^ s).astype(LOW), "context", [(i, i ^ s) for i in range(n)]
        ).astype(F32)
    return total


def zero_of(*others):
    return functools.reduce(
        jnp.add, [other.reshape(-1)[0].astype(F32) * 0.0 for other in others]
    )


def after(value, *others):
    return (value.astype(F32) + zero_of(*others)).astype(value.dtype)


def on_device(
    layer_input,
    grad_output,
    attn_gain,
    query_weight,
    key_weight,
    value_weight,
    q_gain,
    k_gain,
    output_weight,
    mlp_gain,
    router,
    w_gate,
    w_up,
    w_down,
    routes,
    half_order,
):
    n_context = lax.axis_size("context")
    n_expert = lax.axis_size("expert")
    n_groups = lax.axis_size(GROUP_AXES)
    tok_dev, width = layer_input.shape[1:]
    size = q_gain.shape[0]
    kv_total = key_weight.shape[1] * n_expert
    group_dev = n_expert // (kv_total // size)
    kv_index = lax.axis_index("expert") // group_dev
    block = tok_dev * n_expert
    seq = block * n_context
    half = block // 2
    experts = router.shape[1]
    exp_dev = w_gate.shape[0]
    top = routes.shape[2]
    capacity = max(2, (tok_dev * top * 9 + 8 * experts - 1) // (8 * experts))
    scale = size ** (-0.5)

    seq_rows = jnp.arange(seq, dtype=jnp.int32)
    context = lax.axis_index("context")
    own_halves = lax.dynamic_slice_in_dim(half_order, 2 * context, 2)
    own_pos = (own_halves[:, None] * half + jnp.arange(half, dtype=jnp.int32)[None]).reshape(-1)
    per_half = half // TILE
    tile_pos = (half_order[:, None] * per_half + jnp.arange(per_half, dtype=jnp.int32)).reshape(-1)
    kidx = jnp.sum(
        (tile_pos[None, :] == jnp.arange(seq // TILE, dtype=jnp.int32)[:, None])
        * jnp.arange(seq // TILE, dtype=jnp.int32)[None, :],
        axis=1,
    ).astype(jnp.int32)
    qpos = lax.dynamic_slice_in_dim(tile_pos, context * (block // TILE), block // TILE)
    freq = jnp.power(THETA, -jnp.arange(0, size, 2).astype(F32) / size)
    angles = own_pos.astype(F32)[:, None] * freq[None, :]
    cosine, sine = jnp.cos(angles), jnp.sin(angles)
    cos2 = jnp.concatenate([cosine, cosine], axis=1)
    sin2 = jnp.concatenate([-sine, sine], axis=1)

    place = lax.axis_index("expert")
    place_1 = place.astype(jnp.int32)[None]
    lanes = -(-2 * experts // 128) * 128
    mask = jnp.any(
        routes[0][:, :, None] == jnp.arange(lanes, dtype=jnp.int32)[None, None, :], axis=1
    )
    mask_wide = mask.astype(F32)
    router_wide = jnp.pad(router, ((0, 0), (0, lanes - experts)))

    x_low = layer_input[0]
    x_normal, _ = norm_parts(x_low.astype(F32))
    normed_found = line_gather((x_normal * attn_gain).astype(LOW))
    if group_dev == 1:
        kv_weights = jnp.concatenate([key_weight, value_weight], axis=1)
    else:
        key_whole = lax.all_gather(key_weight, "expert", axis=1, tiled=True)
        value_whole = lax.all_gather(value_weight, "expert", axis=1, tiled=True)
        kv_weights = jnp.concatenate(
            [
                lax.dynamic_slice_in_dim(key_whole, kv_index * size, size, 1),
                lax.dynamic_slice_in_dim(value_whole, kv_index * size, size, 1),
            ],
            axis=1,
        )
    normed_rows, own_kv, key_proj = project_keys(
        place_1, normed_found, kv_weights, k_gain, cos2, sin2, scale * LOG2E
    )
    kv_whole = context_gather(own_kv)
    queries, query_proj = project_queries(normed_rows, query_weight, q_gain, cos2, sin2)

    grad_low = grad_output[0]
    last = n_expert - 1
    grad_wide = jnp.concatenate(
        [
            after(grad_low, normed_found[last - 1], normed_found[1 - last]),
            mask.astype(LOW),
        ],
        axis=1,
    )
    grad_col = lax.all_gather(grad_wide, "expert", axis=0, tiled=True)
    order_here = jnp.asarray(arrival_order(n_expert), jnp.int32)[place]
    turn_here = jnp.argsort(order_here).astype(jnp.int32)
    col_mask = grad_col[:, width : width + experts].reshape(n_expert, tok_dev, experts)
    col_hits = lax.dynamic_slice_in_dim(
        col_mask.reshape(n_expert, tok_dev, n_groups, n_expert), place, 1, 3
    )[..., 0]
    earlier = jnp.tril(jnp.ones((tok_dev, tok_dev), LOW), -1)
    col_ranks = jnp.einsum("ts,zsd->ztd", earlier, col_hits, preferred_element_type=F32)
    col_ranks = jnp.where(col_hits > 0, col_ranks.astype(jnp.int32), -1)
    n_half = n_expert // 2
    cap_half = n_half * capacity
    token_half = n_half * tok_dev
    rows_half = n_groups * cap_half

    def spread_of(ranks, turns, first):
        slots = ranks + ((turns - first) * capacity)[:, None, None]
        kept = (ranks >= 0) & (turns >= first)[:, None, None]
        kept = kept & (turns < first + n_half)[:, None, None]
        slots = jnp.where(kept, slots, -1).reshape(-1, n_groups)
        return (
            (slots.T[:, None, :] == jnp.arange(cap_half, dtype=jnp.int32)[None, :, None])
            .astype(LOW)
            .reshape(rows_half, -1)
        )

    ranks_arrived = jnp.take(col_ranks, order_here, axis=0)
    turns = jnp.arange(n_expert, dtype=jnp.int32)
    spreads = [
        spread_of(ranks_arrived[first : first + n_half], turns[first : first + n_half], first)
        for first in (0, n_half)
    ]
    spreads_placed = [spread_of(col_ranks, turn_here, first) for first in (0, n_half)]

    def swap_plane(rows):
        wide = rows.shape[1]
        rows = lax.all_to_all(
            rows.reshape(n_groups, cap_half, wide),
            GROUP_AXES,
            split_axis=0,
            concat_axis=0,
            tiled=True,
        )
        return rows.reshape(rows_half, wide)

    attended, inverse = attend(qpos, kidx, queries, kv_whole, [])
    attn_part = (dot_nn(attended, output_weight) + zero_of(grad_col)).astype(LOW)
    left, right = reduce_in_place(attn_part)

    grad_x = [
        swap_plane(dot_nn(spread, grad_col[:, :width]).astype(LOW)) for spread in spreads_placed
    ]
    act_pull = [dot_nt(rows, w_down[0]) for rows in grad_x]

    hidden, mixed, probs = route_rows(
        place_1,
        x_low,
        attn_part,
        left,
        right,
        mlp_gain,
        router_wide,
        mask_wide,
        experts,
        [grad_x[0]],
    )
    mixed_pieces = by_arrival(line_gather(mixed))

    who = (lax.axis_index(ALL_AXES) * exp_dev).astype(jnp.int32)[None]
    xs, acts, gate_lows, up_lows, copies = ([] for _ in range(5))
    for part in range(2):
        pieces = jnp.concatenate(mixed_pieces[part * n_half : (part + 1) * n_half], axis=0)
        ready = zero_of(grad_x[1]) if part == 0 else zero_of(xs[0])
        x = swap_plane((dot_nn(spreads[part], pieces) + ready).astype(LOW))
        act, gate_low, up_low, copy = run_expert(
            who, x, w_gate[0], w_up[0], act_pull[part], experts
        )
        xs.append(x)
        acts.append(act)
        gate_lows.append(gate_low)
        up_lows.append(up_low)
        copies.append(copy)
    copies_far = dot_tn(spreads[1], swap_plane(copies[1])).astype(LOW)
    copies_near = dot_tn(spreads[0], swap_plane(copies[0])).astype(LOW)
    chunks = lambda rows: [rows[z * tok_dev : (z + 1) * tok_dev] for z in range(n_half)]
    left, right = reduce_by_arrival(chunks(copies_near) + chunks(copies_far))
    returned = [
        (dot_nn(act, w_down[0]) + zero_of(copies_near)).astype(LOW) for act in acts
    ]
    join = lambda parts: jnp.concatenate(parts, axis=0)
    x_all = join([x[:, :width] for x in xs])
    grad_w_down = dot_tn(join(acts), join(grad_x))
    grad_w_gate = dot_tn(x_all, join(gate_lows))
    grad_w_up = dot_tn(x_all, join(up_lows))

    grad_hidden, grad_hidden_low, grad_mlp_gain, grad_router = route_back(
        copies_near,
        left,
        right,
        grad_low,
        hidden,
        mlp_gain,
        router_wide,
        mask_wide,
        probs,
        experts,
    )

    grad_found = line_gather(grad_hidden_low)
    grad_attn, grad_o, centre = grad_attended(
        place_1, grad_found, output_weight, attended, inverse
    )
    half_w_out = half_groups(dot_tn(attended, grad_attn).astype(LOW))
    grad_kv, grad_q, grad_q_gain = attend_back(
        qpos,
        kidx,
        queries,
        grad_o,
        centre,
        kv_whole,
        query_proj,
        q_gain,
        cos2,
        sin2,
        [half_w_out],
    )
    grad_w_out = rest_groups(half_w_out)
    grad_kv = context_reduce(grad_kv)
    grad_w_query = dot_tn(normed_rows, grad_q).astype(LOW)

    combined = functools.reduce(
        jnp.add, [dot_tn(spread, swap_plane(rows)) for spread, rows in zip(spreads_placed, returned)]
    )
    combined = (combined + zero_of(grad_attn)).astype(LOW)
    output_rows = hidden + lax.psum_scatter(
        combined, "expert", scatter_dimension=0, tiled=True
    ).astype(F32)

    gk = grad_kv[:, :size] * scale
    roll = lambda v: jnp.concatenate([v[:, size // 2 :], v[:, : size // 2]], axis=1)
    gk = gk * cos2 - roll(gk) * sin2
    k_normal, k_rr = norm_parts(key_proj)
    grad_k_gain = jnp.sum(gk * k_normal, axis=0)
    gk = norm_back(gk, k_normal, k_rr, k_gain)
    kv_grads = jnp.concatenate([gk, grad_kv[:, size:]], axis=1).astype(LOW)

    grad_normed = dot_nt(grad_q, query_weight) + dot_nt(kv_grads, kv_weights)
    grad_attn_gain = jnp.sum(grad_normed * normed_rows.astype(F32), axis=0) / attn_gain
    grad_normed = grad_normed.astype(LOW)
    left, right = reduce_in_place(grad_normed)
    grad_input = input_back(place_1, grad_normed, left, right, x_low, attn_gain, grad_hidden)

    grad_w_kv = dot_tn(normed_rows, kv_grads).astype(LOW)
    grad_w_query = rest_groups(half_groups(grad_w_query))
    if group_dev == 1:
        grad_w_kv = rest_groups(half_groups(grad_w_kv))
        grad_w_key, grad_w_value = grad_w_kv[:, :size], grad_w_kv[:, size:]
    else:
        blank = jnp.zeros((width, kv_total), LOW)
        pieces = []
        for part in (grad_w_kv[:, :size], grad_w_kv[:, size:]):
            padded = lax.dynamic_update_slice(blank, part, (0, kv_index * size))
            pieces.append(lax.psum_scatter(padded, "expert", scatter_dimension=1, tiled=True))
        grad_w_key, grad_w_value = (lax.psum(piece, GROUP_AXES).astype(F32) for piece in pieces)

    small = [
        grad_attn_gain,
        grad_mlp_gain[0],
        grad_q_gain[0],
        grad_k_gain,
        grad_router[:experts].reshape(-1),
    ]
    summed = sum_small(jnp.concatenate(small))
    pieces = []
    offset = 0
    for part in small:
        pieces.append(summed[offset : offset + part.shape[0]])
        offset += part.shape[0]
    grad_attn_gain, grad_mlp_gain, grad_q_gain, grad_k_gain, grad_router = pieces
    return (
        output_rows.astype(LOW)[None],
        grad_input[None],
        grad_attn_gain,
        grad_w_query,
        grad_w_key,
        grad_w_value,
        grad_q_gain,
        grad_k_gain,
        grad_w_out,
        grad_mlp_gain,
        grad_router.reshape(experts, width).T,
        grad_w_gate[None],
        grad_w_up[None],
        grad_w_down[None],
    )


def solution(mesh):
    rows = P("dp", ("context", "expert"), None)
    expert = P(ALL_AXES, None, None)
    columns = P(None, "expert")
    in_specs = (
        rows,
        rows,
        P(),
        columns,
        columns,
        columns,
        P(),
        P(),
        P("expert", None),
        P(),
        P(),
        expert,
        expert,
        expert,
        rows,
        P(),
    )
    out_specs = (
        rows,
        rows,
        P(),
        columns,
        columns,
        columns,
        P(),
        P(),
        P("expert", None),
        P(),
        P(),
        expert,
        expert,
        expert,
    )
    return jax.shard_map(
        on_device, mesh=mesh, in_specs=in_specs, out_specs=out_specs, check_vma=False
    )
```

```python
import functools
import math

import jax
import jax.numpy as jnp
from jax import lax
from jax.experimental import pallas as pl
from jax.experimental.pallas import tpu as pltpu
from jax.sharding import PartitionSpec as P

EPS = 1e-06
THETA = 1000000.0
TILE = 256
VMEM_BYTES = 56 * 1024 * 1024
LOG2E = math.log2(math.e)
LOW = jnp.bfloat16
F32 = jnp.float32
ALL_AXES = ("dp", "context", "expert")
GROUP_AXES = ("dp", "context")


def dot_nn(a, b):
    return lax.dot_general(a, b, (((1,), (0,)), ((), ())), preferred_element_type=F32)


def dot_nt(a, b):
    return lax.dot_general(a, b, (((1,), (1,)), ((), ())), preferred_element_type=F32)


def dot_tn(a, b):
    return lax.dot_general(a, b, (((0,), (0,)), ((), ())), preferred_element_type=F32)


def params(**more):
    return pltpu.CompilerParams(vmem_limit_bytes=VMEM_BYTES, **more)


def cost(flops, nbytes, exps=0):
    return pl.CostEstimate(flops=int(flops), bytes_accessed=int(nbytes), transcendentals=int(exps))


def head_forward(u, gain, cos2, sin2):
    rr = lax.rsqrt(jnp.mean(u * u, axis=-1, keepdims=True) + EPS)
    y = u * rr * gain
    return y * cos2 + pltpu.roll(y, 64, 1) * sin2


def head_backward(gy, u, gain, cos2, sin2):
    g = gy * cos2 - pltpu.roll(gy, 64, 1) * sin2
    rr = lax.rsqrt(jnp.mean(u * u, axis=-1, keepdims=True) + EPS)
    n = u * rr
    gn = g * gain
    grad = rr * (gn - n * jnp.mean(gn * n, axis=-1, keepdims=True))
    return grad, jnp.sum(g * n, axis=0, keepdims=True)


def query_kernel(x_ref, w_ref, gain_ref, cos_ref, sin_ref, rot_ref, proj_ref):
    tiles, heads, rows, size = rot_ref.shape
    acc = dot_nn(x_ref[...], w_ref[...])
    for h in range(heads):
        u = acc[:, h * size : (h + 1) * size]
        rot = head_forward(u, gain_ref[...], cos_ref[...], sin_ref[...])
        proj_ref[:, h] = u.reshape(tiles, rows, size)
        rot_ref[:, h] = rot.astype(LOW).reshape(tiles, rows, size)


def project_queries(normed, weight, gain, cos2, sin2):
    block, width = normed.shape
    size = cos2.shape[1]
    heads = weight.shape[1] // size
    tiles = block // TILE
    whole = lambda i: (0, 0)
    per = lambda i: (0, i, 0, 0)
    shape = (tiles, heads, TILE, size)
    return pl.pallas_call(
        query_kernel,
        grid=(heads // 2,),
        in_specs=[
            pl.BlockSpec((block, width), whole),
            pl.BlockSpec((width, 2 * size), lambda i: (0, i)),
            pl.BlockSpec((1, size), whole),
            pl.BlockSpec((block, size), whole),
            pl.BlockSpec((block, size), whole),
        ],
        out_specs=[pl.BlockSpec((tiles, 2, TILE, size), per)] * 2,
        out_shape=[jax.ShapeDtypeStruct(shape, LOW), jax.ShapeDtypeStruct(shape, F32)],
        compiler_params=params(),
        cost_estimate=cost(2 * block * width * heads * size, 12e6),
    )(normed, weight, gain[None], cos2, sin2)


def put_in_order(place, refs, out_ref):
    n = (len(refs) + 1) // 2
    rows = refs[0].shape[0]
    for distance in range(1 - n, n):
        ref = refs[distance + n - 1]
        at = place + distance

        @pl.when(jnp.logical_and(at >= 0, at < n))
        def _():
            out_ref[pl.ds(pl.multiple_of(at * rows, rows), rows), :] = ref[...]


def chunk_list(found):
    n = (len(found) + 1) // 2
    return [found[distance] for distance in range(1 - n, n)]


def key_kernel(factor, place_ref, *refs):
    w_ref, gain_ref, cos_ref, sin_ref, rows_ref, kv_ref, proj_ref = refs[-7:]
    size = proj_ref.shape[1]
    put_in_order(place_ref[0], refs[:-7], rows_ref)
    acc = dot_nn(rows_ref[...], w_ref[...])
    u = acc[:, :size]
    rot = head_forward(u, gain_ref[...], cos_ref[...], sin_ref[...])
    proj_ref[...] = u
    kv_ref[:, :size] = (rot * factor).astype(LOW)
    kv_ref[:, size:] = acc[:, size:].astype(LOW)


def full(shape):
    return pl.BlockSpec(shape, lambda *_: (0,) * len(shape))


def project_keys(place, found, weight, gain, cos2, sin2, factor):
    chunks = chunk_list(found)
    rows, width = chunks[0].shape
    block, size = cos2.shape
    operands = [*chunks, weight, gain[None], cos2, sin2]
    shapes = [
        jax.ShapeDtypeStruct((block, width), LOW),
        jax.ShapeDtypeStruct((block, 2 * size), LOW),
        jax.ShapeDtypeStruct((block, size), F32),
    ]
    return pl.pallas_call(
        functools.partial(key_kernel, factor),
        grid_spec=pltpu.PrefetchScalarGridSpec(
            num_scalar_prefetch=1,
            grid=(1,),
            in_specs=[full(x.shape) for x in operands],
            out_specs=[full(x.shape) for x in shapes],
        ),
        out_shape=shapes,
        compiler_params=params(),
        cost_estimate=cost(4 * block * width * size, 8e6),
    )(place, *operands)


def attend_kernel(qpos_ref, kidx_ref, q_ref, kv_ref, *rest):
    out_ref, inv_ref, acc_ref = rest[-3:]
    heads, rows, size = q_ref.shape[1:]
    last = qpos_ref[pl.program_id(0)]
    acc_ref[...] = jnp.zeros_like(acc_ref)
    ones = jnp.ones((rows, size), LOW)

    def step(place, masked):
        start = pl.multiple_of(kidx_ref[place] * rows, rows)
        keys = kv_ref[pl.ds(start, rows), :size]
        values = jnp.concatenate([kv_ref[pl.ds(start, rows), size:], ones], axis=1)
        for h in range(heads):
            e = jnp.exp2(dot_nt(q_ref[0, h], keys))
            if masked:
                qi = lax.broadcasted_iota(jnp.int32, e.shape, 0)
                ki = lax.broadcasted_iota(jnp.int32, e.shape, 1)
                e = jnp.where(ki <= qi, e, 0.0)
            acc_ref[h] += dot_nn(e.astype(LOW), values)

    lax.fori_loop(0, last, lambda p, c: (step(p, False), c)[1], 0)
    step(last, True)
    for h in range(heads):
        inv = 1.0 / acc_ref[h, :, size:]
        inv_ref[0, h] = inv
        out_ref[:, h * size : (h + 1) * size] = (acc_ref[h, :, :size] * inv).astype(LOW)


def attend(qpos, kidx, queries, kv, others):
    tiles, heads, rows, size = queries.shape
    seq = kv.shape[0]
    return pl.pallas_call(
        attend_kernel,
        grid_spec=pltpu.PrefetchScalarGridSpec(
            num_scalar_prefetch=2,
            grid=(tiles,),
            in_specs=[
                pl.BlockSpec((1, heads, rows, size), lambda i, a, b: (i, 0, 0, 0)),
                pl.BlockSpec((seq, 2 * size), lambda i, a, b: (0, 0)),
            ]
            + [pl.BlockSpec(memory_space=pl.ANY)] * len(others),
            out_specs=[
                pl.BlockSpec((rows, heads * size), lambda i, a, b: (i, 0)),
                pl.BlockSpec((1, heads, rows, size), lambda i, a, b: (i, 0, 0, 0)),
            ],
            scratch_shapes=[pltpu.VMEM((heads, rows, 2 * size), F32)],
        ),
        out_shape=[
            jax.ShapeDtypeStruct((tiles * rows, heads * size), LOW),
            jax.ShapeDtypeStruct((tiles, heads, rows, size), F32),
        ],
        compiler_params=params(),
        cost_estimate=cost(
            6 * tiles * rows * heads * seq * size, 8e6, tiles * rows * heads * seq
        ),
    )(qpos, kidx, queries, kv, *others)


def grad_out_kernel(place_ref, *refs):
    w_ref, o_ref, inv_ref, rows_ref, do_ref, centre_ref = refs[-6:]
    tiles, heads, rows, size = do_ref.shape

    @pl.when(pl.program_id(0) == 0)
    def _():
        put_in_order(place_ref[0], refs[:-6], rows_ref)

    acc = dot_nt(rows_ref[...], w_ref[...])
    ones = jnp.ones((8, size), F32)
    for t in range(tiles):
        for h in range(heads):
            part = slice(t * rows, (t + 1) * rows), slice(h * size, (h + 1) * size)
            low = (acc[part] * inv_ref[t, h]).astype(LOW)
            do_ref[t, h] = low
            product = low.astype(F32) * o_ref[part].astype(F32)
            centre_ref[t, h] = lax.dot_general(
                ones,
                product,
                (((1,), (1,)), ((), ())),
                precision=lax.Precision.HIGHEST,
                preferred_element_type=F32,
            )


def grad_attended(place, found, weight, attended, inverse):
    chunks = chunk_list(found)
    tiles, heads, rows, size = inverse.shape
    width = weight.shape[1]
    block = attended.shape[0]
    return pl.pallas_call(
        grad_out_kernel,
        grid_spec=pltpu.PrefetchScalarGridSpec(
            num_scalar_prefetch=1,
            grid=(heads // 2,),
            in_specs=[full(x.shape) for x in chunks]
            + [
                pl.BlockSpec((2 * size, width), lambda i, p: (i, 0)),
                pl.BlockSpec((block, 2 * size), lambda i, p: (0, i)),
                pl.BlockSpec((tiles, 2, rows, size), lambda i, p: (0, i, 0, 0)),
            ],
            out_specs=[
                full((block, width)),
                pl.BlockSpec((tiles, 2, rows, size), lambda i, p: (0, i, 0, 0)),
                pl.BlockSpec((tiles, 2, 8, rows), lambda i, p: (0, i, 0, 0)),
            ],
        ),
        out_shape=[
            jax.ShapeDtypeStruct((block, width), LOW),
            jax.ShapeDtypeStruct((tiles, heads, rows, size), LOW),
            jax.ShapeDtypeStruct((tiles, heads, 8, rows), F32),
        ],
        compiler_params=params(),
        cost_estimate=cost(2 * block * width * heads * size, 12e6),
    )(place, *chunks, weight, attended, inverse)


def attend_back_kernel(
    qpos_ref,
    kidx_ref,
    q_ref,
    do_ref,
    centre_ref,
    kv_ref,
    proj_ref,
    gain_ref,
    cos_ref,
    sin_ref,
    *rest,
):
    dkv_ref, dq_ref, dgain_ref, acc_ref = rest[-4:]
    heads, rows, size = q_ref.shape[1:]
    last = qpos_ref[pl.program_id(0)]

    @pl.when(pl.program_id(0) == 0)
    def _():
        dkv_ref[...] = jnp.zeros_like(dkv_ref)
        dgain_ref[...] = jnp.zeros_like(dgain_ref)

    acc_ref[...] = jnp.zeros_like(acc_ref)

    def step(place, masked):
        start = pl.multiple_of(kidx_ref[place] * rows, rows)
        keys = kv_ref[pl.ds(start, rows), :size]
        values = kv_ref[pl.ds(start, rows), size:]
        dk = dkv_ref[pl.ds(start, rows), :size]
        dv = dkv_ref[pl.ds(start, rows), size:]
        for h in range(heads):
            query, grad = q_ref[0, h], do_ref[0, h]
            e = jnp.exp2(dot_nt(keys, query))
            if masked:
                ki = lax.broadcasted_iota(jnp.int32, e.shape, 0)
                qi = lax.broadcasted_iota(jnp.int32, e.shape, 1)
                e = jnp.where(ki <= qi, e, 0.0)
            ds = (e * (dot_nt(values, grad) - centre_ref[0, h, 0:1])).astype(LOW)
            dv += dot_nn(e.astype(LOW), grad)
            dk += dot_nn(ds, query)
            acc_ref[h] += dot_tn(ds, keys)
        dkv_ref[pl.ds(start, rows), :size] = dk
        dkv_ref[pl.ds(start, rows), size:] = dv

    lax.fori_loop(0, last, lambda p, c: (step(p, False), c)[1], 0)
    step(last, True)
    total = jnp.zeros((1, size), F32)
    for h in range(heads):
        grad, gain_part = head_backward(
            acc_ref[h] * (1.0 / LOG2E), proj_ref[0, h], gain_ref[...], cos_ref[...], sin_ref[...]
        )
        dq_ref[:, h * size : (h + 1) * size] = grad.astype(LOW)
        total += gain_part
    dgain_ref[...] += total


def attend_back(qpos, kidx, queries, grads, centre, kv, proj, gain, cos2, sin2, others):
    tiles, heads, rows, size = queries.shape
    seq = kv.shape[0]
    per = pl.BlockSpec((1, heads, rows, size), lambda i, a, b: (i, 0, 0, 0))
    flat = lambda i, a, b: (0, 0)
    rowwise = lambda i, a, b: (i, 0)
    return pl.pallas_call(
        attend_back_kernel,
        grid_spec=pltpu.PrefetchScalarGridSpec(
            num_scalar_prefetch=2,
            grid=(tiles,),
            in_specs=[
                per,
                per,
                pl.BlockSpec((1, heads, 8, rows), lambda i, a, b: (i, 0, 0, 0)),
                pl.BlockSpec((seq, 2 * size), flat),
                per,
                pl.BlockSpec((1, size), flat),
                pl.BlockSpec((rows, size), rowwise),
                pl.BlockSpec((rows, size), rowwise),
            ]
            + [pl.BlockSpec(memory_space=pl.ANY)] * len(others),
            out_specs=[
                pl.BlockSpec((seq, 2 * size), flat),
                pl.BlockSpec((rows, heads * size), rowwise),
                pl.BlockSpec((1, size), flat),
            ],
            scratch_shapes=[pltpu.VMEM((heads, rows, size), F32)],
        ),
        out_shape=[
            jax.ShapeDtypeStruct((seq, 2 * size), F32),
            jax.ShapeDtypeStruct((tiles * rows, heads * size), LOW),
            jax.ShapeDtypeStruct((1, size), F32),
        ],
        compiler_params=params(),
        cost_estimate=cost(
            15 * tiles * rows * heads * seq * size, 12e6, tiles * rows * heads * seq
        ),
    )(qpos, kidx, queries, grads, centre, kv, proj, gain[None], cos2, sin2, *others)


def split_low(value):
    high = value.astype(LOW)
    return high, (value - high.astype(F32)).astype(LOW)


def norm_parts(rows):
    rr = lax.rsqrt(jnp.mean(rows * rows, axis=-1, keepdims=True) + EPS)
    return rows * rr, rr


def norm_back(grad, normal, rr, gain):
    weighted = grad * gain
    return rr * (weighted - normal * jnp.mean(weighted * normal, axis=-1, keepdims=True))


def add_all(refs):
    return functools.reduce(jnp.add, [ref[...].astype(F32) for ref in refs])


def router_kernel(experts, *refs):
    x_ref, attn_ref, gain_ref, router_ref, mask_ref = refs[:5]
    hidden_ref, mixed_ref, probs_ref = refs[-3:]
    width = x_ref.shape[1]
    lanes = router_ref.shape[1]
    hidden = add_all([x_ref, attn_ref])
    hidden_ref[...] = hidden
    mixed = (norm_parts(hidden)[0] * gain_ref[...]).astype(LOW)
    mixed_ref[:, :width] = mixed
    logits = dot_nn(mixed, router_ref[...])
    lane = lax.broadcasted_iota(jnp.int32, logits.shape, 1)
    logits = jnp.where(lane < experts, logits, -1e30)
    weights = jnp.exp(logits - jnp.max(logits, axis=1, keepdims=True))
    probs = weights / jnp.sum(weights, axis=1, keepdims=True)
    probs_ref[...] = probs
    chosen = probs * mask_ref[...]
    high, low = split_low(chosen / jnp.sum(chosen, axis=1, keepdims=True))
    both = high.astype(F32) + pltpu.roll(low.astype(F32), experts, 1)
    mixed_ref[:, width:] = both.astype(LOW)


def route_rows(x, attn, gain, router, mask, experts, others):
    tokens, width = x.shape
    lanes = router.shape[1]
    operands = [x, attn, gain[None], router, mask]
    shapes = [
        jax.ShapeDtypeStruct((tokens, width), F32),
        jax.ShapeDtypeStruct((tokens, width + lanes), LOW),
        jax.ShapeDtypeStruct((tokens, lanes), F32),
    ]
    return pl.pallas_call(
        functools.partial(router_kernel, experts),
        grid=(1,),
        in_specs=[full(value.shape) for value in operands]
        + [pl.BlockSpec(memory_space=pl.ANY)] * len(others),
        out_specs=[full(shape.shape) for shape in shapes],
        out_shape=shapes,
        compiler_params=params(),
        cost_estimate=cost(2 * tokens * width * lanes, 5e6),
    )(*operands, *others)


def table_kernel(capacity, n_half, meta_ref, col_ref, *outs):
    block = col_ref.shape[0]
    rows, width = outs[0].shape
    n = 2 * n_half
    tokens = block // n
    cap_half = n_half * capacity
    groups = rows // cap_half
    mask = col_ref[:, width:]
    lanes = mask.shape[1]
    padded = -(-groups // 16) * 16
    group = lax.broadcasted_iota(jnp.int32, (padded, lanes), 0)
    lane = lax.broadcasted_iota(jnp.int32, (padded, lanes), 1)
    wanted = jnp.logical_and(lane == group * n + meta_ref[0], group < groups)
    hits = dot_nt(jnp.where(wanted, 1.0, 0.0).astype(LOW), mask)
    before = lax.broadcasted_iota(jnp.int32, (tokens, tokens), 0)
    after_it = lax.broadcasted_iota(jnp.int32, (tokens, tokens), 1)
    earlier = jnp.where(before < after_it, 1.0, 0.0).astype(LOW)
    slots = []
    for z in range(n):
        hit = hits[:, z * tokens : (z + 1) * tokens]
        rank = dot_nn(hit.astype(LOW), earlier)
        turn = (meta_ref[1 + z] * capacity).astype(F32)
        slots.append(jnp.where(hit > 0.5, rank + turn, -1.0))
    slots = jnp.concatenate(slots, axis=1)[:groups]
    slot = lax.broadcasted_iota(jnp.int32, (groups, cap_half, block), 1).astype(F32)
    for part in range(2):
        rows_ref, placed_ref, arrived_ref = outs[part], outs[2 + part], outs[4 + part]
        same = slots[:, None, :] == slot + float(part * cap_half)
        spread = jnp.where(same, 1.0, 0.0).reshape(rows, block).astype(LOW)
        placed_ref[...] = spread
        rows_ref[...] = dot_nn(spread, col_ref[:, :width]).astype(LOW)
        for k in range(n_half):
            start = pl.multiple_of(meta_ref[1 + n + part * n_half + k] * tokens, tokens)
            arrived_ref[:, k * tokens : (k + 1) * tokens] = placed_ref[:, pl.ds(start, tokens)]


def make_tables(meta, col, width, groups, n_half, capacity):
    block = col.shape[0]
    rows = groups * n_half * capacity
    shapes = (
        [jax.ShapeDtypeStruct((rows, width), LOW)] * 2
        + [jax.ShapeDtypeStruct((rows, block), LOW)] * 2
        + [jax.ShapeDtypeStruct((rows, block // 2), LOW)] * 2
    )
    outs = pl.pallas_call(
        functools.partial(table_kernel, capacity, n_half),
        grid_spec=pltpu.PrefetchScalarGridSpec(
            num_scalar_prefetch=1,
            grid=(1,),
            in_specs=[full(col.shape)],
            out_specs=[full(shape.shape) for shape in shapes],
        ),
        out_shape=shapes,
        compiler_params=params(),
        cost_estimate=cost(4 * rows * block * width, 12e6),
    )(meta, col)
    return outs[:2], outs[2:4], outs[4:]


def spread_kernel(choices, place_ref, spread_ref, *refs):
    out_ref, rows_ref = refs[-2:]
    for k, by_place in enumerate(choices):
        for which in sorted(set(by_place)):
            hit = functools.reduce(
                jnp.logical_or,
                [place_ref[0] == i for i, other in enumerate(by_place) if other == which],
            )

            @pl.when(hit)
            def _():
                tokens = refs[which].shape[0]
                rows_ref[k * tokens : (k + 1) * tokens] = refs[which][...]

    out_ref[...] = dot_nn(spread_ref[...], rows_ref[...]).astype(LOW)


def spread_rows(place, spread, found, turns, others):
    n = lax.axis_size("expert")
    order = arrival_order(n)
    distances = sorted({order[i][turn] - i for i in range(n) for turn in turns})
    choices = [[distances.index(order[i][turn] - i) for i in range(n)] for turn in turns]
    chunks = [found[distance] for distance in distances]
    tokens, wide = chunks[0].shape
    rows = spread.shape[0]
    return pl.pallas_call(
        functools.partial(spread_kernel, choices),
        grid_spec=pltpu.PrefetchScalarGridSpec(
            num_scalar_prefetch=1,
            grid=(1,),
            in_specs=[full(spread.shape)]
            + [full(chunk.shape) for chunk in chunks]
            + [pl.BlockSpec(memory_space=pl.ANY)] * len(others),
            out_specs=full((rows, wide)),
            scratch_shapes=[pltpu.VMEM((len(turns) * tokens, wide), LOW)],
        ),
        out_shape=jax.ShapeDtypeStruct((rows, wide), LOW),
        compiler_params=params(),
        cost_estimate=cost(2 * rows * len(turns) * tokens * wide, 5e6),
    )(place, spread, *chunks, *others)


def router_back_kernel(experts, *refs):
    own_ref, left_ref, right_ref, g_ref, hidden_ref, gain_ref, router_ref, mask_ref, probs_ref = (
        refs[:9]
    )
    grad_ref, low_ref, dgain_ref, drouter_ref = refs[9:]
    width = g_ref.shape[1]
    lanes = router_ref.shape[1]
    total = add_all([own_ref, left_ref, right_ref])
    table = total[:, width:]
    mask, probs = mask_ref[...], probs_ref[...]
    grad_gates = (table + pltpu.roll(table, lanes - experts, 1)) * mask
    chosen = probs * mask
    chosen_sum = jnp.sum(chosen, axis=1, keepdims=True)
    mean = jnp.sum(grad_gates * (chosen / chosen_sum), axis=1, keepdims=True)
    centred = mask * (grad_gates - mean) / chosen_sum
    grad_logits = probs * (centred - jnp.sum(centred * chosen, axis=1, keepdims=True))
    high, low = split_low(grad_logits)
    router = router_ref[...]
    grad = total[:, :width] + dot_nt(high, router) + dot_nt(low, router)
    normal, rr = norm_parts(hidden_ref[...])
    mixed = (normal * gain_ref[...]).astype(LOW)
    drouter_ref[...] = dot_tn(high, mixed) + dot_tn(low, mixed)
    dgain_ref[...] = jnp.sum(grad * normal, axis=0, keepdims=True)
    grad_hidden = g_ref[...].astype(F32) + norm_back(grad, normal, rr, gain_ref[...])
    grad_ref[...] = grad_hidden
    low_ref[...] = grad_hidden.astype(LOW)


def route_back(own, left, right, g, hidden, gain, router, mask, probs, experts):
    tokens, width = g.shape
    lanes = router.shape[1]
    shapes = [
        jax.ShapeDtypeStruct((tokens, width), F32),
        jax.ShapeDtypeStruct((tokens, width), LOW),
        jax.ShapeDtypeStruct((1, width), F32),
        jax.ShapeDtypeStruct((lanes, width), F32),
    ]
    return pl.pallas_call(
        functools.partial(router_back_kernel, experts),
        grid=(1,),
        in_specs=[
            pl.BlockSpec((tokens, width + lanes), lambda i: (0, 0)),
            full(left.shape),
            full(right.shape),
            full(g.shape),
            full(hidden.shape),
            full((1, width)),
            full(router.shape),
            full(mask.shape),
            full(probs.shape),
        ],
        out_specs=[full(shape.shape) for shape in shapes],
        out_shape=shapes,
        compiler_params=params(),
        cost_estimate=cost(8 * tokens * width * lanes, 8e6),
    )(own, left, right, g, hidden, gain[None], router, mask, probs)


def expert_kernel(experts, who_ref, x_ref, gate_ref, up_ref, pull_ref, *rest):
    act_ref, dgate_ref, dup_ref, copy_ref = rest[-4:]
    width = gate_ref.shape[0]
    x = x_ref[:, :width]
    table = x_ref[:, width:].astype(F32)
    lane = lax.broadcasted_iota(jnp.int32, table.shape, 1)
    mine = who_ref[0]
    gate = jnp.sum(
        jnp.where(jnp.logical_or(lane == mine, lane == mine + experts), table, 0.0),
        axis=1,
        keepdims=True,
    )
    pre_gate = dot_nn(x, gate_ref[...])
    pre_up = dot_nn(x, up_ref[...])
    pull = pull_ref[...]
    sig = 1.0 / (1.0 + jnp.exp(-pre_gate))
    silu = pre_gate * sig
    act = silu * pre_up
    act_ref[...] = (act * gate).astype(LOW)
    high, low = split_low(jnp.sum(act * pull, axis=1, keepdims=True))
    pull = pull * gate
    dup = (pull * silu).astype(LOW)
    dgate = (pull * pre_up * (sig * (1.0 + pre_gate * (1.0 - sig)))).astype(LOW)
    dgate_ref[...] = dgate
    dup_ref[...] = dup
    copy_ref[:, :width] = (dot_nt(dgate, gate_ref[...]) + dot_nt(dup, up_ref[...])).astype(LOW)
    back = jnp.where(lane == mine, high.astype(F32), 0.0)
    back = jnp.where(lane == mine + experts, low.astype(F32), back)
    copy_ref[:, width:] = back.astype(LOW)


def run_expert(who, x, w_gate, w_up, pull, experts, others):
    rows, wide = x.shape
    width, hidden = w_gate.shape
    tile = rows // 2 if rows % 32 == 0 else rows
    by_rows = lambda columns: pl.BlockSpec((tile, columns), lambda i, p: (i, 0))
    return pl.pallas_call(
        functools.partial(expert_kernel, experts),
        grid_spec=pltpu.PrefetchScalarGridSpec(
            num_scalar_prefetch=1,
            grid=(rows // tile,),
            in_specs=[by_rows(wide), full(w_gate.shape), full(w_up.shape), by_rows(hidden)]
            + [pl.BlockSpec(memory_space=pl.ANY)] * len(others),
            out_specs=[by_rows(hidden), by_rows(hidden), by_rows(hidden), by_rows(wide)],
        ),
        out_shape=[jax.ShapeDtypeStruct((rows, hidden), LOW)] * 3
        + [jax.ShapeDtypeStruct((rows, wide), LOW)],
        compiler_params=params(),
        cost_estimate=cost(8 * rows * width * hidden, 20e6, rows * hidden),
    )(who, x, w_gate, w_up, pull, *others)


def input_kernel(grad_ref, x_ref, gain_ref, more_ref, out_ref):
    normal, rr = norm_parts(x_ref[...].astype(F32))
    grad = grad_ref[...].astype(F32)
    out_ref[...] = more_ref[...] + norm_back(grad, normal, rr, gain_ref[...])


def input_back(grad, x, gain, more):
    tokens, width = x.shape
    operands = [grad, x, gain[None], more]
    return pl.pallas_call(
        input_kernel,
        grid=(1,),
        in_specs=[full(value.shape) for value in operands],
        out_specs=full(more.shape),
        out_shape=jax.ShapeDtypeStruct((tokens, width), F32),
        compiler_params=params(),
        cost_estimate=cost(20 * tokens * width, 5e6),
    )(*operands)


def widen_kernel(d_ref, kept_ref, got_ref, out_ref):
    @pl.when(pl.program_id(0) == 0)
    def _():
        out_ref[...] = kept_ref[...].astype(F32)

    @pl.when(pl.program_id(0) == 1)
    def _():
        out_ref[...] = got_ref[...].astype(F32)


def widen(d, kept, got):
    rows, columns = kept.shape
    tiles = 4 if rows % 64 == 0 else 1
    tile = rows // tiles
    return pl.pallas_call(
        widen_kernel,
        grid_spec=pltpu.PrefetchScalarGridSpec(
            num_scalar_prefetch=1,
            grid=(2, tiles),
            in_specs=[
                pl.BlockSpec((tile, columns), lambda i, j, d: (j * (1 - i) + (tiles - 1) * i, 0)),
                pl.BlockSpec((tile, columns), lambda i, j, d: (j * i, 0)),
            ],
            out_specs=pl.BlockSpec(
                (tile, columns), lambda i, j, d: ((d[0] + i - 2 * d[0] * i) * tiles + j, 0)
            ),
        ),
        out_shape=jax.ShapeDtypeStruct((2 * rows, columns), F32),
        compiler_params=params(),
        cost_estimate=cost(2 * rows * columns, 12 * rows * columns),
    )(d.astype(jnp.int32)[None], kept, got)


def sum_small(flat):
    n = lax.axis_size(ALL_AXES)
    length = flat.shape[0]
    each = -(-length // (n * 128)) * 128
    parts = jnp.pad(flat, (0, n * each - length)).reshape(n, each)
    parts = lax.all_to_all(parts, ALL_AXES, split_axis=0, concat_axis=0, tiled=True)
    own = jnp.sum(parts, axis=0, keepdims=True)
    whole = lax.all_to_all(
        jnp.broadcast_to(own, (n, each)), ALL_AXES, split_axis=0, concat_axis=0, tiled=True
    )
    return whole.reshape(-1)[:length]


def swap_dp(rows):
    return lax.ppermute(rows, "dp", [(0, 1), (1, 0)])


def share_context(parts):
    return lax.all_to_all(parts, "context", split_axis=0, concat_axis=0, tiled=True)


def half_groups(grad):
    d = lax.axis_index("dp")
    rows = grad.shape[0] // 2
    got = swap_dp(lax.dynamic_slice_in_dim(grad, (1 - d) * rows, rows))
    kept = lax.dynamic_slice_in_dim(grad, d * rows, rows)
    return (kept.astype(F32) + got.astype(F32)).astype(LOW)


def rest_groups(half):
    n = lax.axis_size("context")
    d = lax.axis_index("dp")
    rows, columns = half.shape
    parts = share_context(half.reshape(n, rows // n, columns))
    part = jnp.sum(parts.astype(F32), axis=0, keepdims=True).astype(LOW)
    half = share_context(jnp.broadcast_to(part, parts.shape)).reshape(rows, columns)
    return widen(d, half, swap_dp(half))


def arrival_order(n):
    return [sorted(range(n), key=lambda j: (abs(j - i), j)) for i in range(n)]


def choose(index, options):
    distinct = []
    for option in options:
        if option is not None and not any(option is other for other in distinct):
            distinct.append(option)
    result = distinct[0]
    for option in distinct[1:]:
        mask = functools.reduce(
            jnp.logical_or, [index == i for i, other in enumerate(options) if other is option]
        )
        result = jnp.where(mask, option, result)
    return result


def line_gather(chunk):
    return line_steps({0: chunk}, 1, lax.axis_size("expert"))


def line_steps(found, first, stop):
    n = lax.axis_size("expert")
    found = dict(found)
    for s in range(first, stop):
        found[-s] = lax.ppermute(
            found[1 - s], "expert", [(i, i + 1) for i in range(s - 1, n - 1)]
        )
        found[s] = lax.ppermute(found[s - 1], "expert", [(i + 1, i) for i in range(n - s)])
    return found


def line_reduce(piece):
    n = lax.axis_size("expert")
    add = lambda a, b: (a.astype(F32) + b.astype(F32)).astype(LOW)
    left = right = None
    for s in range(1, n):
        out_left, out_right = piece(-1, s), piece(1, s)
        if s > 1:
            out_left = add(out_left.astype(F32) + zero_of(right), left)
            out_right = add(out_right.astype(F32) + zero_of(left), right)
        left = lax.ppermute(out_left, "expert", [(i, i - 1) for i in range(n - s, n)])
        right = lax.ppermute(out_right, "expert", [(i, i + 1) for i in range(s)])
    return left, right


def reduce_by_arrival(pieces):
    n = lax.axis_size("expert")
    me = lax.axis_index("expert")
    order = arrival_order(n)

    def piece(side, s):
        options = []
        for i in range(n):
            owner = i + side * (n - s)
            options.append(pieces[order[i].index(owner)] if 0 <= owner < n else None)
        return choose(me, options)

    return line_reduce(piece)


def context_gather(rows):
    n = lax.axis_size("context")
    c = lax.axis_index("context")
    found = {0: rows}
    for s in range(1, n):
        found[s] = lax.ppermute(rows, "context", [(i, i ^ s) for i in range(n)])
    return jnp.concatenate([choose(c, [found[i ^ j] for i in range(n)]) for j in range(n)], axis=0)


def context_reduce(rows):
    n = lax.axis_size("context")
    c = lax.axis_index("context")
    each = rows.shape[0] // n
    take = lambda j: lax.dynamic_slice_in_dim(rows, j * each, each)
    total = take(c).astype(F32)
    for s in range(1, n):
        total += lax.ppermute(
            take(c ^ s).astype(LOW), "context", [(i, i ^ s) for i in range(n)]
        ).astype(F32)
    return total


def zero_of(*others):
    return functools.reduce(
        jnp.add, [other.reshape(-1)[0].astype(F32) * 0.0 for other in others]
    )


def after(value, *others):
    return (value.astype(F32) + zero_of(*others)).astype(value.dtype)


def on_device(
    layer_input,
    grad_output,
    attn_gain,
    query_weight,
    key_weight,
    value_weight,
    q_gain,
    k_gain,
    output_weight,
    mlp_gain,
    router,
    w_gate,
    w_up,
    w_down,
    routes,
    half_order,
):
    n_context = lax.axis_size("context")
    n_expert = lax.axis_size("expert")
    n_groups = lax.axis_size(GROUP_AXES)
    tok_dev, width = layer_input.shape[1:]
    size = q_gain.shape[0]
    kv_total = key_weight.shape[1] * n_expert
    group_dev = n_expert // (kv_total // size)
    kv_index = lax.axis_index("expert") // group_dev
    block = tok_dev * n_expert
    seq = block * n_context
    half = block // 2
    experts = router.shape[1]
    exp_dev = w_gate.shape[0]
    top = routes.shape[2]
    capacity = max(2, (tok_dev * top * 9 + 8 * experts - 1) // (8 * experts))
    scale = size ** (-0.5)

    seq_rows = jnp.arange(seq, dtype=jnp.int32)
    context = lax.axis_index("context")
    own_halves = lax.dynamic_slice_in_dim(half_order, 2 * context, 2)
    own_pos = (own_halves[:, None] * half + jnp.arange(half, dtype=jnp.int32)[None]).reshape(-1)
    per_half = half // TILE
    tile_pos = (half_order[:, None] * per_half + jnp.arange(per_half, dtype=jnp.int32)).reshape(-1)
    kidx = jnp.sum(
        (tile_pos[None, :] == jnp.arange(seq // TILE, dtype=jnp.int32)[:, None])
        * jnp.arange(seq // TILE, dtype=jnp.int32)[None, :],
        axis=1,
    ).astype(jnp.int32)
    qpos = lax.dynamic_slice_in_dim(tile_pos, context * (block // TILE), block // TILE)
    freq = jnp.power(THETA, -jnp.arange(0, size, 2).astype(F32) / size)
    angles = own_pos.astype(F32)[:, None] * freq[None, :]
    cosine, sine = jnp.cos(angles), jnp.sin(angles)
    cos2 = jnp.concatenate([cosine, cosine], axis=1)
    sin2 = jnp.concatenate([-sine, sine], axis=1)

    place = lax.axis_index("expert")
    place_1 = place.astype(jnp.int32)[None]
    lanes = -(-2 * experts // 128) * 128
    mask = jnp.any(
        routes[0][:, :, None] == jnp.arange(lanes, dtype=jnp.int32)[None, None, :], axis=1
    )
    mask_wide = mask.astype(F32)
    router_wide = jnp.pad(router, ((0, 0), (0, lanes - experts)))

    x_low = layer_input[0]
    x_normal, _ = norm_parts(x_low.astype(F32))
    normed_found = line_gather((x_normal * attn_gain).astype(LOW))
    if group_dev == 1:
        kv_weights = jnp.concatenate([key_weight, value_weight], axis=1)
    else:
        key_whole = lax.all_gather(key_weight, "expert", axis=1, tiled=True)
        value_whole = lax.all_gather(value_weight, "expert", axis=1, tiled=True)
        kv_weights = jnp.concatenate(
            [
                lax.dynamic_slice_in_dim(key_whole, kv_index * size, size, 1),
                lax.dynamic_slice_in_dim(value_whole, kv_index * size, size, 1),
            ],
            axis=1,
        )
    normed_rows, own_kv, key_proj = project_keys(
        place_1, normed_found, kv_weights, k_gain, cos2, sin2, scale * LOG2E
    )
    kv_whole = context_gather(own_kv)
    queries, query_proj = project_queries(normed_rows, query_weight, q_gain, cos2, sin2)

    grad_low = grad_output[0]
    last = n_expert - 1
    n_half = n_expert // 2
    rows_half = n_groups * n_half * capacity
    grad_wide = jnp.concatenate(
        [after(grad_low, normed_found[last], normed_found[-last]), mask.astype(LOW)], axis=1
    )
    grad_col = lax.all_gather(grad_wide, "expert", axis=0, tiled=True)
    order_here = jnp.asarray(arrival_order(n_expert), jnp.int32)[place]
    turn_here = jnp.sum(
        (order_here[:, None] == jnp.arange(n_expert, dtype=jnp.int32)[None, :])
        * jnp.arange(n_expert, dtype=jnp.int32)[:, None],
        axis=0,
    ).astype(jnp.int32)
    meta = jnp.concatenate([place_1, turn_here, order_here])
    grad_sent, spreads_placed, spreads = make_tables(
        meta, grad_col, width, n_groups, n_half, capacity
    )

    def swap_plane(rows):
        wide = rows.shape[1]
        rows = lax.all_to_all(
            rows.reshape(n_groups, n_half * capacity, wide),
            GROUP_AXES,
            split_axis=0,
            concat_axis=0,
            tiled=True,
        )
        return rows.reshape(rows_half, wide)

    attended, inverse = attend(qpos, kidx, queries, kv_whole, [])
    attn_part = (dot_nn(attended, output_weight) + zero_of(grad_col)).astype(LOW)
    attn_rows = lax.psum_scatter(attn_part, "expert", scatter_dimension=0, tiled=True)

    grad_x = [swap_plane(rows) for rows in grad_sent]
    act_pull = [dot_nt(rows, w_down[0]) for rows in grad_x]

    hidden, mixed, probs = route_rows(
        x_low, attn_rows, mlp_gain, router_wide, mask_wide, experts, [grad_x[0]]
    )

    who = (lax.axis_index(ALL_AXES) * exp_dev).astype(jnp.int32)[None]
    mixed_found = line_gather(mixed)
    near = spread_rows(place_1, spreads[0], mixed_found, range(n_half), [grad_x[1]])
    x_near = swap_plane(near)
    worked_near = run_expert(who, x_near, w_gate[0], w_up[0], act_pull[0], experts, [])
    far = spread_rows(
        place_1, spreads[1], mixed_found, range(n_half, n_expert), [worked_near[-1]]
    )
    x_far = swap_plane(far)
    worked_far = run_expert(who, x_far, w_gate[0], w_up[0], act_pull[1], experts, [])
    xs = [x_near, x_far]
    acts, gate_lows, up_lows, copies = (list(pair) for pair in zip(worked_near, worked_far))
    copies_far = dot_tn(spreads[1], swap_plane(copies[1])).astype(LOW)
    copies_near = dot_tn(spreads[0], swap_plane(copies[0])).astype(LOW)
    chunks = lambda rows: [rows[z * tok_dev : (z + 1) * tok_dev] for z in range(n_half)]
    left, right = reduce_by_arrival(chunks(copies_near) + chunks(copies_far))
    returned = [
        (dot_nn(act, w_down[0]) + zero_of(copies_near)).astype(LOW) for act in acts
    ]
    join = lambda parts: jnp.concatenate(parts, axis=0)
    x_all = join([x[:, :width] for x in xs])
    grad_w_down = dot_tn(join(acts), join(grad_x))
    grad_w_gate = dot_tn(x_all, join(gate_lows))
    grad_w_up = dot_tn(x_all, join(up_lows))

    grad_hidden, grad_hidden_low, grad_mlp_gain, grad_router = route_back(
        copies_near,
        left,
        right,
        grad_low,
        hidden,
        mlp_gain,
        router_wide,
        mask_wide,
        probs,
        experts,
    )

    grad_found = line_gather(grad_hidden_low)
    grad_attn, grad_o, centre = grad_attended(
        place_1, grad_found, output_weight, attended, inverse
    )
    half_w_out = half_groups(dot_tn(attended, grad_attn).astype(LOW))
    combined = functools.reduce(
        jnp.add, [dot_tn(spread, swap_plane(rows)) for spread, rows in zip(spreads_placed, returned)]
    )
    combined = (combined + zero_of(grad_attn)).astype(LOW)
    output_rows = hidden + lax.psum_scatter(
        combined, "expert", scatter_dimension=0, tiled=True
    ).astype(F32)
    grad_kv, grad_q, grad_q_gain = attend_back(
        qpos,
        kidx,
        queries,
        grad_o,
        centre,
        kv_whole,
        query_proj,
        q_gain,
        cos2,
        sin2,
        [half_w_out, grad_w_gate, grad_w_up, grad_w_down, combined],
    )
    grad_w_out = rest_groups(half_w_out)
    grad_kv = context_reduce(grad_kv)
    grad_w_query = dot_tn(normed_rows, grad_q).astype(LOW)

    gk = grad_kv[:, :size] * scale
    roll = lambda v: jnp.concatenate([v[:, size // 2 :], v[:, : size // 2]], axis=1)
    gk = gk * cos2 - roll(gk) * sin2
    k_normal, k_rr = norm_parts(key_proj)
    grad_k_gain = jnp.sum(gk * k_normal, axis=0)
    gk = norm_back(gk, k_normal, k_rr, k_gain)
    kv_grads = jnp.concatenate([gk, grad_kv[:, size:]], axis=1).astype(LOW)

    grad_normed = dot_nt(grad_q, query_weight) + dot_nt(kv_grads, kv_weights)
    grad_attn_gain = jnp.sum(grad_normed * normed_rows.astype(F32), axis=0) / attn_gain
    grad_normed = lax.psum_scatter(
        (grad_normed + zero_of(output_rows)).astype(LOW), "expert", scatter_dimension=0, tiled=True
    )
    grad_input = input_back(grad_normed, x_low, attn_gain, grad_hidden)

    grad_w_kv = dot_tn(normed_rows, kv_grads).astype(LOW)
    grad_w_query = rest_groups(half_groups(grad_w_query))
    if group_dev == 1:
        grad_w_kv = rest_groups(half_groups(grad_w_kv))
        grad_w_key, grad_w_value = grad_w_kv[:, :size], grad_w_kv[:, size:]
    else:
        blank = jnp.zeros((width, kv_total), LOW)
        pieces = []
        for part in (grad_w_kv[:, :size], grad_w_kv[:, size:]):
            padded = lax.dynamic_update_slice(blank, part, (0, kv_index * size))
            pieces.append(lax.psum_scatter(padded, "expert", scatter_dimension=1, tiled=True))
        grad_w_key, grad_w_value = (lax.psum(piece, GROUP_AXES).astype(F32) for piece in pieces)

    small = [
        grad_attn_gain,
        grad_mlp_gain[0],
        grad_q_gain[0],
        grad_k_gain,
        grad_router[:experts].reshape(-1),
    ]
    summed = sum_small(jnp.concatenate(small))
    pieces = []
    offset = 0
    for part in small:
        pieces.append(summed[offset : offset + part.shape[0]])
        offset += part.shape[0]
    grad_attn_gain, grad_mlp_gain, grad_q_gain, grad_k_gain, grad_router = pieces
    return (
        output_rows.astype(LOW)[None],
        grad_input[None],
        grad_attn_gain,
        grad_w_query,
        grad_w_key,
        grad_w_value,
        grad_q_gain,
        grad_k_gain,
        grad_w_out,
        grad_mlp_gain,
        grad_router.reshape(experts, width).T,
        grad_w_gate[None],
        grad_w_up[None],
        grad_w_down[None],
    )


def solution(mesh):
    rows = P("dp", ("context", "expert"), None)
    expert = P(ALL_AXES, None, None)
    columns = P(None, "expert")
    in_specs = (
        rows,
        rows,
        P(),
        columns,
        columns,
        columns,
        P(),
        P(),
        P("expert", None),
        P(),
        P(),
        expert,
        expert,
        expert,
        rows,
        P(),
    )
    out_specs = (
        rows,
        rows,
        P(),
        columns,
        columns,
        columns,
        P(),
        P(),
        P("expert", None),
        P(),
        P(),
        expert,
        expert,
        expert,
    )
    return jax.shard_map(
        on_device, mesh=mesh, in_specs=in_specs, out_specs=out_specs, check_vma=False
    )
```

```python
import functools
import math

import jax
import jax.numpy as jnp
from jax import lax
from jax.experimental import pallas as pl
from jax.experimental.pallas import tpu as pltpu
from jax.sharding import PartitionSpec as P

EPS = 1e-06
THETA = 1000000.0
TILE = 256
VMEM_BYTES = 56 * 1024 * 1024
LOG2E = math.log2(math.e)
LOW = jnp.bfloat16
F32 = jnp.float32
ALL_AXES = ("dp", "context", "expert")
GROUP_AXES = ("dp", "context")


def dot_nn(a, b):
    return lax.dot_general(a, b, (((1,), (0,)), ((), ())), preferred_element_type=F32)


def dot_nt(a, b):
    return lax.dot_general(a, b, (((1,), (1,)), ((), ())), preferred_element_type=F32)


def dot_tn(a, b):
    return lax.dot_general(a, b, (((0,), (0,)), ((), ())), preferred_element_type=F32)


def params(**more):
    return pltpu.CompilerParams(vmem_limit_bytes=VMEM_BYTES, **more)


def cost(flops, nbytes, exps=0):
    return pl.CostEstimate(flops=int(flops), bytes_accessed=int(nbytes), transcendentals=int(exps))


def head_forward(u, gain, cos2, sin2):
    rr = lax.rsqrt(jnp.mean(u * u, axis=-1, keepdims=True) + EPS)
    y = u * rr * gain
    return y * cos2 + pltpu.roll(y, 64, 1) * sin2


def head_backward(gy, u, gain, cos2, sin2):
    g = gy * cos2 - pltpu.roll(gy, 64, 1) * sin2
    rr = lax.rsqrt(jnp.mean(u * u, axis=-1, keepdims=True) + EPS)
    n = u * rr
    gn = g * gain
    grad = rr * (gn - n * jnp.mean(gn * n, axis=-1, keepdims=True))
    return grad, jnp.sum(g * n, axis=0, keepdims=True)


def query_kernel(x_ref, w_ref, gain_ref, cos_ref, sin_ref, rot_ref, proj_ref):
    tiles, heads, rows, size = rot_ref.shape
    acc = dot_nn(x_ref[...], w_ref[...])
    for h in range(heads):
        u = acc[:, h * size : (h + 1) * size]
        rot = head_forward(u, gain_ref[...], cos_ref[...], sin_ref[...])
        proj_ref[:, h] = u.reshape(tiles, rows, size)
        rot_ref[:, h] = rot.astype(LOW).reshape(tiles, rows, size)


def project_queries(normed, weight, gain, cos2, sin2):
    block, width = normed.shape
    size = cos2.shape[1]
    heads = weight.shape[1] // size
    tiles = block // TILE
    whole = lambda i: (0, 0)
    per = lambda i: (0, i, 0, 0)
    shape = (tiles, heads, TILE, size)
    return pl.pallas_call(
        query_kernel,
        grid=(heads // 2,),
        in_specs=[
            pl.BlockSpec((block, width), whole),
            pl.BlockSpec((width, 2 * size), lambda i: (0, i)),
            pl.BlockSpec((1, size), whole),
            pl.BlockSpec((block, size), whole),
            pl.BlockSpec((block, size), whole),
        ],
        out_specs=[pl.BlockSpec((tiles, 2, TILE, size), per)] * 2,
        out_shape=[jax.ShapeDtypeStruct(shape, LOW), jax.ShapeDtypeStruct(shape, F32)],
        compiler_params=params(),
        cost_estimate=cost(2 * block * width * heads * size, 12e6),
    )(normed, weight, gain[None], cos2, sin2)


def put_in_order(place, refs, out_ref):
    n = (len(refs) + 1) // 2
    rows = refs[0].shape[0]
    for distance in range(1 - n, n):
        ref = refs[distance + n - 1]
        at = place + distance

        @pl.when(jnp.logical_and(at >= 0, at < n))
        def _():
            out_ref[pl.ds(pl.multiple_of(at * rows, rows), rows), :] = ref[...]


def chunk_list(found):
    n = (len(found) + 1) // 2
    return [found[distance] for distance in range(1 - n, n)]


def key_kernel(factor, n_chunks, place_ref, *refs):
    w_ref, gain_ref, cos_ref, sin_ref = refs[n_chunks : n_chunks + 4]
    rows_ref, kv_ref, proj_ref = refs[-3:]
    size = proj_ref.shape[1]
    put_in_order(place_ref[0], refs[:n_chunks], rows_ref)
    acc = dot_nn(rows_ref[...], w_ref[...])
    u = acc[:, :size]
    rot = head_forward(u, gain_ref[...], cos_ref[...], sin_ref[...])
    proj_ref[...] = u
    kv_ref[:, :size] = (rot * factor).astype(LOW)
    kv_ref[:, size:] = acc[:, size:].astype(LOW)


def full(shape):
    return pl.BlockSpec(shape, lambda *_: (0,) * len(shape))


def project_keys(place, found, weight, gain, cos2, sin2, factor, others):
    chunks = chunk_list(found)
    rows, width = chunks[0].shape
    block, size = cos2.shape
    operands = [*chunks, weight, gain[None], cos2, sin2]
    shapes = [
        jax.ShapeDtypeStruct((block, width), LOW),
        jax.ShapeDtypeStruct((block, 2 * size), LOW),
        jax.ShapeDtypeStruct((block, size), F32),
    ]
    return pl.pallas_call(
        functools.partial(key_kernel, factor, len(chunks)),
        grid_spec=pltpu.PrefetchScalarGridSpec(
            num_scalar_prefetch=1,
            grid=(1,),
            in_specs=[full(x.shape) for x in operands]
            + [pl.BlockSpec(memory_space=pl.ANY)] * len(others),
            out_specs=[full(x.shape) for x in shapes],
        ),
        out_shape=shapes,
        compiler_params=params(),
        cost_estimate=cost(4 * block * width * size, 8e6),
    )(place, *operands, *others)


def attend_kernel(qpos_ref, kidx_ref, q_ref, kv_ref, *rest):
    out_ref, inv_ref, acc_ref = rest[-3:]
    heads, rows, size = q_ref.shape[1:]
    last = qpos_ref[pl.program_id(0)]
    acc_ref[...] = jnp.zeros_like(acc_ref)
    ones = jnp.ones((rows, size), LOW)

    def step(place, masked):
        start = pl.multiple_of(kidx_ref[place] * rows, rows)
        keys = kv_ref[pl.ds(start, rows), :size]
        values = jnp.concatenate([kv_ref[pl.ds(start, rows), size:], ones], axis=1)
        for h in range(heads):
            e = jnp.exp2(dot_nt(q_ref[0, h], keys))
            if masked:
                qi = lax.broadcasted_iota(jnp.int32, e.shape, 0)
                ki = lax.broadcasted_iota(jnp.int32, e.shape, 1)
                e = jnp.where(ki <= qi, e, 0.0)
            acc_ref[h] += dot_nn(e.astype(LOW), values)

    lax.fori_loop(0, last, lambda p, c: (step(p, False), c)[1], 0)
    step(last, True)
    for h in range(heads):
        inv = 1.0 / acc_ref[h, :, size:]
        inv_ref[0, h] = inv
        out_ref[:, h * size : (h + 1) * size] = (acc_ref[h, :, :size] * inv).astype(LOW)


def attend(qpos, kidx, queries, kv, others):
    tiles, heads, rows, size = queries.shape
    seq = kv.shape[0]
    return pl.pallas_call(
        attend_kernel,
        grid_spec=pltpu.PrefetchScalarGridSpec(
            num_scalar_prefetch=2,
            grid=(tiles,),
            in_specs=[
                pl.BlockSpec((1, heads, rows, size), lambda i, a, b: (i, 0, 0, 0)),
                pl.BlockSpec((seq, 2 * size), lambda i, a, b: (0, 0)),
            ]
            + [pl.BlockSpec(memory_space=pl.ANY)] * len(others),
            out_specs=[
                pl.BlockSpec((rows, heads * size), lambda i, a, b: (i, 0)),
                pl.BlockSpec((1, heads, rows, size), lambda i, a, b: (i, 0, 0, 0)),
            ],
            scratch_shapes=[pltpu.VMEM((heads, rows, 2 * size), F32)],
        ),
        out_shape=[
            jax.ShapeDtypeStruct((tiles * rows, heads * size), LOW),
            jax.ShapeDtypeStruct((tiles, heads, rows, size), F32),
        ],
        compiler_params=params(),
        cost_estimate=cost(
            6 * tiles * rows * heads * seq * size, 8e6, tiles * rows * heads * seq
        ),
    )(qpos, kidx, queries, kv, *others)


def grad_out_kernel(rows_ref, w_ref, o_ref, inv_ref, *rest):
    do_ref, centre_ref = rest[-2:]
    tiles, heads, rows, size = do_ref.shape
    acc = dot_nt(rows_ref[...], w_ref[...])
    ones = jnp.ones((8, size), F32)
    for t in range(tiles):
        for h in range(heads):
            part = slice(t * rows, (t + 1) * rows), slice(h * size, (h + 1) * size)
            low = (acc[part] * inv_ref[t, h]).astype(LOW)
            do_ref[t, h] = low
            product = low.astype(F32) * o_ref[part].astype(F32)
            centre_ref[t, h] = lax.dot_general(
                ones,
                product,
                (((1,), (1,)), ((), ())),
                precision=lax.Precision.HIGHEST,
                preferred_element_type=F32,
            )


def grad_attended(grad_rows, weight, attended, inverse, others):
    tiles, heads, rows, size = inverse.shape
    block, width = grad_rows.shape
    return pl.pallas_call(
        grad_out_kernel,
        grid=(heads // 2,),
        in_specs=[
            pl.BlockSpec((block, width), lambda i: (0, 0)),
            pl.BlockSpec((2 * size, width), lambda i: (i, 0)),
            pl.BlockSpec((block, 2 * size), lambda i: (0, i)),
            pl.BlockSpec((tiles, 2, rows, size), lambda i: (0, i, 0, 0)),
        ]
        + [pl.BlockSpec(memory_space=pl.ANY)] * len(others),
        out_specs=[
            pl.BlockSpec((tiles, 2, rows, size), lambda i: (0, i, 0, 0)),
            pl.BlockSpec((tiles, 2, 8, rows), lambda i: (0, i, 0, 0)),
        ],
        out_shape=[
            jax.ShapeDtypeStruct((tiles, heads, rows, size), LOW),
            jax.ShapeDtypeStruct((tiles, heads, 8, rows), F32),
        ],
        compiler_params=params(),
        cost_estimate=cost(2 * block * width * heads * size, 12e6),
    )(grad_rows, weight, attended, inverse, *others)


def attend_back_kernel(
    qpos_ref,
    kidx_ref,
    q_ref,
    do_ref,
    centre_ref,
    kv_ref,
    proj_ref,
    gain_ref,
    cos_ref,
    sin_ref,
    *rest,
):
    dkv_ref, dq_ref, dgain_ref, acc_ref = rest[-4:]
    heads, rows, size = q_ref.shape[1:]
    last = qpos_ref[pl.program_id(0)]

    @pl.when(pl.program_id(0) == 0)
    def _():
        dkv_ref[...] = jnp.zeros_like(dkv_ref)
        dgain_ref[...] = jnp.zeros_like(dgain_ref)

    acc_ref[...] = jnp.zeros_like(acc_ref)

    def step(place, masked):
        start = pl.multiple_of(kidx_ref[place] * rows, rows)
        keys = kv_ref[pl.ds(start, rows), :size]
        values = kv_ref[pl.ds(start, rows), size:]
        dk = dkv_ref[pl.ds(start, rows), :size]
        dv = dkv_ref[pl.ds(start, rows), size:]
        for h in range(heads):
            query, grad = q_ref[0, h], do_ref[0, h]
            e = jnp.exp2(dot_nt(keys, query))
            if masked:
                ki = lax.broadcasted_iota(jnp.int32, e.shape, 0)
                qi = lax.broadcasted_iota(jnp.int32, e.shape, 1)
                e = jnp.where(ki <= qi, e, 0.0)
            ds = (e * (dot_nt(values, grad) - centre_ref[0, h, 0:1])).astype(LOW)
            dv += dot_nn(e.astype(LOW), grad)
            dk += dot_nn(ds, query)
            acc_ref[h] += dot_tn(ds, keys)
        dkv_ref[pl.ds(start, rows), :size] = dk
        dkv_ref[pl.ds(start, rows), size:] = dv

    lax.fori_loop(0, last, lambda p, c: (step(p, False), c)[1], 0)
    step(last, True)
    total = jnp.zeros((1, size), F32)
    for h in range(heads):
        grad, gain_part = head_backward(
            acc_ref[h] * (1.0 / LOG2E), proj_ref[0, h], gain_ref[...], cos_ref[...], sin_ref[...]
        )
        dq_ref[:, h * size : (h + 1) * size] = grad.astype(LOW)
        total += gain_part
    dgain_ref[...] += total


def attend_back(qpos, kidx, queries, grads, centre, kv, proj, gain, cos2, sin2, others):
    tiles, heads, rows, size = queries.shape
    seq = kv.shape[0]
    per = pl.BlockSpec((1, heads, rows, size), lambda i, a, b: (i, 0, 0, 0))
    flat = lambda i, a, b: (0, 0)
    rowwise = lambda i, a, b: (i, 0)
    return pl.pallas_call(
        attend_back_kernel,
        grid_spec=pltpu.PrefetchScalarGridSpec(
            num_scalar_prefetch=2,
            grid=(tiles,),
            in_specs=[
                per,
                per,
                pl.BlockSpec((1, heads, 8, rows), lambda i, a, b: (i, 0, 0, 0)),
                pl.BlockSpec((seq, 2 * size), flat),
                per,
                pl.BlockSpec((1, size), flat),
                pl.BlockSpec((rows, size), rowwise),
                pl.BlockSpec((rows, size), rowwise),
            ]
            + [pl.BlockSpec(memory_space=pl.ANY)] * len(others),
            out_specs=[
                pl.BlockSpec((seq, 2 * size), flat),
                pl.BlockSpec((rows, heads * size), rowwise),
                pl.BlockSpec((1, size), flat),
            ],
            scratch_shapes=[pltpu.VMEM((heads, rows, size), F32)],
        ),
        out_shape=[
            jax.ShapeDtypeStruct((seq, 2 * size), F32),
            jax.ShapeDtypeStruct((tiles * rows, heads * size), LOW),
            jax.ShapeDtypeStruct((1, size), F32),
        ],
        compiler_params=params(),
        cost_estimate=cost(
            15 * tiles * rows * heads * seq * size, 12e6, tiles * rows * heads * seq
        ),
    )(qpos, kidx, queries, grads, centre, kv, proj, gain[None], cos2, sin2, *others)


def split_low(value):
    high = value.astype(LOW)
    return high, (value - high.astype(F32)).astype(LOW)


def norm_parts(rows):
    rr = lax.rsqrt(jnp.mean(rows * rows, axis=-1, keepdims=True) + EPS)
    return rows * rr, rr


def norm_back(grad, normal, rr, gain):
    weighted = grad * gain
    return rr * (weighted - normal * jnp.mean(weighted * normal, axis=-1, keepdims=True))


def add_all(refs):
    return functools.reduce(jnp.add, [ref[...].astype(F32) for ref in refs])


def router_kernel(experts, *refs):
    x_ref, attn_ref, gain_ref, router_ref, mask_ref = refs[:5]
    hidden_ref, mixed_ref, probs_ref = refs[-3:]
    width = x_ref.shape[1]
    lanes = router_ref.shape[1]
    hidden = add_all([x_ref, attn_ref])
    hidden_ref[...] = hidden
    mixed = (norm_parts(hidden)[0] * gain_ref[...]).astype(LOW)
    mixed_ref[:, :width] = mixed
    logits = dot_nn(mixed, router_ref[...])
    lane = lax.broadcasted_iota(jnp.int32, logits.shape, 1)
    logits = jnp.where(lane < experts, logits, -1e30)
    weights = jnp.exp(logits - jnp.max(logits, axis=1, keepdims=True))
    probs = weights / jnp.sum(weights, axis=1, keepdims=True)
    probs_ref[...] = probs
    chosen = probs * mask_ref[...]
    high, low = split_low(chosen / jnp.sum(chosen, axis=1, keepdims=True))
    both = high.astype(F32) + pltpu.roll(low.astype(F32), experts, 1)
    mixed_ref[:, width:] = both.astype(LOW)


def route_rows(x, attn, gain, router, mask, experts, others):
    tokens, width = x.shape
    lanes = router.shape[1]
    operands = [x, attn, gain[None], router, mask]
    shapes = [
        jax.ShapeDtypeStruct((tokens, width), F32),
        jax.ShapeDtypeStruct((tokens, width + lanes), LOW),
        jax.ShapeDtypeStruct((tokens, lanes), F32),
    ]
    return pl.pallas_call(
        functools.partial(router_kernel, experts),
        grid=(1,),
        in_specs=[full(value.shape) for value in operands]
        + [pl.BlockSpec(memory_space=pl.ANY)] * len(others),
        out_specs=[full(shape.shape) for shape in shapes],
        out_shape=shapes,
        compiler_params=params(),
        cost_estimate=cost(2 * tokens * width * lanes, 5e6),
    )(*operands, *others)


def table_kernel(capacity, n_half, meta_ref, col_ref, *rest):
    outs = rest[-6:]
    block = col_ref.shape[0]
    rows, width = outs[0].shape
    n = 2 * n_half
    tokens = block // n
    cap_half = n_half * capacity
    groups = rows // cap_half
    mask = col_ref[:, width:]
    lanes = mask.shape[1]
    padded = -(-groups // 16) * 16
    group = lax.broadcasted_iota(jnp.int32, (padded, lanes), 0)
    lane = lax.broadcasted_iota(jnp.int32, (padded, lanes), 1)
    wanted = jnp.logical_and(lane == group * n + meta_ref[0], group < groups)
    hits = dot_nt(jnp.where(wanted, 1.0, 0.0).astype(LOW), mask)
    before = lax.broadcasted_iota(jnp.int32, (tokens, tokens), 0)
    after_it = lax.broadcasted_iota(jnp.int32, (tokens, tokens), 1)
    earlier = jnp.where(before < after_it, 1.0, 0.0).astype(LOW)
    slots = []
    for z in range(n):
        hit = hits[:, z * tokens : (z + 1) * tokens]
        rank = dot_nn(hit.astype(LOW), earlier)
        turn = (meta_ref[1 + z] * capacity).astype(F32)
        slots.append(jnp.where(hit > 0.5, rank + turn, -1.0))
    slots = jnp.concatenate(slots, axis=1)[:groups]
    slot = lax.broadcasted_iota(jnp.int32, (groups, cap_half, block), 1).astype(F32)
    for part in range(2):
        rows_ref, placed_ref, arrived_ref = outs[part], outs[2 + part], outs[4 + part]
        same = slots[:, None, :] == slot + float(part * cap_half)
        spread = jnp.where(same, 1.0, 0.0).reshape(rows, block).astype(LOW)
        placed_ref[...] = spread
        rows_ref[...] = dot_nn(spread, col_ref[:, :width]).astype(LOW)
        for k in range(n_half):
            start = pl.multiple_of(meta_ref[1 + n + part * n_half + k] * tokens, tokens)
            arrived_ref[:, k * tokens : (k + 1) * tokens] = placed_ref[:, pl.ds(start, tokens)]


def make_tables(meta, col, width, groups, n_half, capacity, others):
    block = col.shape[0]
    rows = groups * n_half * capacity
    shapes = (
        [jax.ShapeDtypeStruct((rows, width), LOW)] * 2
        + [jax.ShapeDtypeStruct((rows, block), LOW)] * 2
        + [jax.ShapeDtypeStruct((rows, block // 2), LOW)] * 2
    )
    outs = pl.pallas_call(
        functools.partial(table_kernel, capacity, n_half),
        grid_spec=pltpu.PrefetchScalarGridSpec(
            num_scalar_prefetch=1,
            grid=(1,),
            in_specs=[full(col.shape)] + [pl.BlockSpec(memory_space=pl.ANY)] * len(others),
            out_specs=[full(shape.shape) for shape in shapes],
        ),
        out_shape=shapes,
        compiler_params=params(),
        cost_estimate=cost(4 * rows * block * width, 12e6),
    )(meta, col, *others)
    return outs[:2], outs[2:4], outs[4:]


def spread_kernel(choices, place_ref, spread_ref, *refs):
    out_ref, rows_ref = refs[-2:]
    for k, by_place in enumerate(choices):
        for which in sorted(set(by_place)):
            hit = functools.reduce(
                jnp.logical_or,
                [place_ref[0] == i for i, other in enumerate(by_place) if other == which],
            )

            @pl.when(hit)
            def _():
                tokens = refs[which].shape[0]
                rows_ref[k * tokens : (k + 1) * tokens] = refs[which][...]

    out_ref[...] = dot_nn(spread_ref[...], rows_ref[...]).astype(LOW)


def spread_rows(place, spread, found, turns, others):
    n = lax.axis_size("expert")
    order = arrival_order(n)
    distances = sorted({order[i][turn] - i for i in range(n) for turn in turns})
    choices = [[distances.index(order[i][turn] - i) for i in range(n)] for turn in turns]
    chunks = [found[distance] for distance in distances]
    tokens, wide = chunks[0].shape
    rows = spread.shape[0]
    return pl.pallas_call(
        functools.partial(spread_kernel, choices),
        grid_spec=pltpu.PrefetchScalarGridSpec(
            num_scalar_prefetch=1,
            grid=(1,),
            in_specs=[full(spread.shape)]
            + [full(chunk.shape) for chunk in chunks]
            + [pl.BlockSpec(memory_space=pl.ANY)] * len(others),
            out_specs=full((rows, wide)),
            scratch_shapes=[pltpu.VMEM((len(turns) * tokens, wide), LOW)],
        ),
        out_shape=jax.ShapeDtypeStruct((rows, wide), LOW),
        compiler_params=params(),
        cost_estimate=cost(2 * rows * len(turns) * tokens * wide, 5e6),
    )(place, spread, *chunks, *others)


def router_back_kernel(experts, *refs):
    sum_ref, g_ref, hidden_ref, gain_ref, router_ref, mask_ref, probs_ref = refs[:7]
    grad_ref, low_ref, dgain_ref, drouter_ref = refs[-4:]
    width = g_ref.shape[1]
    lanes = router_ref.shape[1]
    total = sum_ref[...].astype(F32)
    table = total[:, width:]
    mask, probs = mask_ref[...], probs_ref[...]
    grad_gates = (table + pltpu.roll(table, lanes - experts, 1)) * mask
    chosen = probs * mask
    chosen_sum = jnp.sum(chosen, axis=1, keepdims=True)
    mean = jnp.sum(grad_gates * (chosen / chosen_sum), axis=1, keepdims=True)
    centred = mask * (grad_gates - mean) / chosen_sum
    grad_logits = probs * (centred - jnp.sum(centred * chosen, axis=1, keepdims=True))
    high, low = split_low(grad_logits)
    router = router_ref[...]
    grad = total[:, :width] + dot_nt(high, router) + dot_nt(low, router)
    normal, rr = norm_parts(hidden_ref[...])
    mixed = (normal * gain_ref[...]).astype(LOW)
    drouter_ref[...] = dot_tn(high, mixed) + dot_tn(low, mixed)
    dgain_ref[...] = jnp.sum(grad * normal, axis=0, keepdims=True)
    grad_hidden = g_ref[...].astype(F32) + norm_back(grad, normal, rr, gain_ref[...])
    grad_ref[...] = grad_hidden
    low_ref[...] = grad_hidden.astype(LOW)


def route_back(summed, g, hidden, gain, router, mask, probs, experts, others):
    tokens, width = g.shape
    lanes = router.shape[1]
    operands = [summed, g, hidden, gain[None], router, mask, probs]
    shapes = [
        jax.ShapeDtypeStruct((tokens, width), F32),
        jax.ShapeDtypeStruct((tokens, width), LOW),
        jax.ShapeDtypeStruct((1, width), F32),
        jax.ShapeDtypeStruct((lanes, width), F32),
    ]
    return pl.pallas_call(
        functools.partial(router_back_kernel, experts),
        grid=(1,),
        in_specs=[full(value.shape) for value in operands]
        + [pl.BlockSpec(memory_space=pl.ANY)] * len(others),
        out_specs=[full(shape.shape) for shape in shapes],
        out_shape=shapes,
        compiler_params=params(),
        cost_estimate=cost(8 * tokens * width * lanes, 8e6),
    )(*operands, *others)


def combine_kernel(near_ref, far_ref, near_rows_ref, far_rows_ref, *rest):
    total = dot_tn(near_ref[...], near_rows_ref[...]) + dot_tn(far_ref[...], far_rows_ref[...])
    rest[-1][...] = total.astype(LOW)


def combine_rows(spreads, rows, others):
    slots, block = spreads[0].shape
    wide = rows[0].shape[1]
    tile = 128 * next(k for k in (4, 3, 2, 1) if wide % (128 * k) == 0) if wide % 512 else 512
    return pl.pallas_call(
        combine_kernel,
        grid=(wide // tile,),
        in_specs=[full(spread.shape) for spread in spreads]
        + [pl.BlockSpec((slots, tile), lambda i: (0, i))] * 2
        + [pl.BlockSpec(memory_space=pl.ANY)] * len(others),
        out_specs=pl.BlockSpec((block, tile), lambda i: (0, i)),
        out_shape=jax.ShapeDtypeStruct((block, wide), LOW),
        compiler_params=params(),
        cost_estimate=cost(4 * slots * block * wide, 10e6),
    )(*spreads, *rows, *others)


def expert_kernel(experts, who_ref, x_ref, gate_ref, up_ref, pull_ref, *rest):
    act_ref, dgate_ref, dup_ref, copy_ref = rest[-4:]
    width = gate_ref.shape[0]
    x = x_ref[:, :width]
    table = x_ref[:, width:].astype(F32)
    lane = lax.broadcasted_iota(jnp.int32, table.shape, 1)
    mine = who_ref[0]
    gate = jnp.sum(
        jnp.where(jnp.logical_or(lane == mine, lane == mine + experts), table, 0.0),
        axis=1,
        keepdims=True,
    )
    pre_gate = dot_nn(x, gate_ref[...])
    pre_up = dot_nn(x, up_ref[...])
    pull = pull_ref[...]
    sig = 1.0 / (1.0 + jnp.exp(-pre_gate))
    silu = pre_gate * sig
    act = silu * pre_up
    act_ref[...] = (act * gate).astype(LOW)
    high, low = split_low(jnp.sum(act * pull, axis=1, keepdims=True))
    pull = pull * gate
    dup = (pull * silu).astype(LOW)
    dgate = (pull * pre_up * (sig * (1.0 + pre_gate * (1.0 - sig)))).astype(LOW)
    dgate_ref[...] = dgate
    dup_ref[...] = dup
    copy_ref[:, :width] = (dot_nt(dgate, gate_ref[...]) + dot_nt(dup, up_ref[...])).astype(LOW)
    back = jnp.where(lane == mine, high.astype(F32), 0.0)
    back = jnp.where(lane == mine + experts, low.astype(F32), back)
    copy_ref[:, width:] = back.astype(LOW)


def run_expert(who, x, w_gate, w_up, pull, experts, others):
    rows, wide = x.shape
    width, hidden = w_gate.shape
    tile = rows // 2 if rows % 32 == 0 else rows
    by_rows = lambda columns: pl.BlockSpec((tile, columns), lambda i, p: (i, 0))
    return pl.pallas_call(
        functools.partial(expert_kernel, experts),
        grid_spec=pltpu.PrefetchScalarGridSpec(
            num_scalar_prefetch=1,
            grid=(rows // tile,),
            in_specs=[by_rows(wide), full(w_gate.shape), full(w_up.shape), by_rows(hidden)]
            + [pl.BlockSpec(memory_space=pl.ANY)] * len(others),
            out_specs=[by_rows(hidden), by_rows(hidden), by_rows(hidden), by_rows(wide)],
        ),
        out_shape=[jax.ShapeDtypeStruct((rows, hidden), LOW)] * 3
        + [jax.ShapeDtypeStruct((rows, wide), LOW)],
        compiler_params=params(),
        cost_estimate=cost(8 * rows * width * hidden, 20e6, rows * hidden),
    )(who, x, w_gate, w_up, pull, *others)


def input_kernel(grad_ref, x_ref, gain_ref, more_ref, out_ref):
    normal, rr = norm_parts(x_ref[...].astype(F32))
    grad = grad_ref[...].astype(F32)
    out_ref[...] = more_ref[...] + norm_back(grad, normal, rr, gain_ref[...])


def input_back(grad, x, gain, more):
    tokens, width = x.shape
    operands = [grad, x, gain[None], more]
    return pl.pallas_call(
        input_kernel,
        grid=(1,),
        in_specs=[full(value.shape) for value in operands],
        out_specs=full(more.shape),
        out_shape=jax.ShapeDtypeStruct((tokens, width), F32),
        compiler_params=params(),
        cost_estimate=cost(20 * tokens * width, 5e6),
    )(*operands)


def kv_back_kernel(factor, c_ref, dkv_ref, *refs):
    parts = refs[:-7]
    proj_ref, gain_ref, cos_ref, sin_ref, more_ref, grad_ref, dgain_ref = refs[-7:]
    del more_ref
    size = proj_ref.shape[1]
    total = functools.reduce(jnp.add, [part[...].astype(F32) for part in parts], dkv_ref[...])
    grad, dgain = head_backward(
        total[:, :size] * factor, proj_ref[...], gain_ref[...], cos_ref[...], sin_ref[...]
    )
    grad_ref[:, :size] = grad.astype(LOW)
    grad_ref[:, size:] = total[:, size:].astype(LOW)
    dgain_ref[...] = dgain


def kv_back(context, dkv, parts, proj, gain, cos2, sin2, factor, other):
    block, size = proj.shape
    operands = [proj, gain[None], cos2, sin2]
    shapes = [
        jax.ShapeDtypeStruct((block, 2 * size), LOW),
        jax.ShapeDtypeStruct((1, size), F32),
    ]
    return pl.pallas_call(
        functools.partial(kv_back_kernel, factor),
        grid_spec=pltpu.PrefetchScalarGridSpec(
            num_scalar_prefetch=1,
            grid=(1,),
            in_specs=[pl.BlockSpec((block, 2 * size), lambda i, c: (c[0], 0))]
            + [full(part.shape) for part in parts]
            + [full(value.shape) for value in operands]
            + [pl.BlockSpec(memory_space=pl.ANY)],
            out_specs=[full(shape.shape) for shape in shapes],
        ),
        out_shape=shapes,
        compiler_params=params(),
        cost_estimate=cost(40 * block * size, 5e6),
    )(context.astype(jnp.int32)[None], dkv, *parts, *operands, other)


def widen_kernel(at_ref, *refs):
    out_ref = refs[-1]
    for k, ref in enumerate(refs[:-1]):

        @pl.when(pl.program_id(0) == k)
        def _():
            out_ref[...] = ref[...].astype(F32)


def widen(places, chunks):
    rows, columns = chunks[0].shape
    return pl.pallas_call(
        widen_kernel,
        grid_spec=pltpu.PrefetchScalarGridSpec(
            num_scalar_prefetch=1,
            grid=(len(chunks),),
            in_specs=[full(chunk.shape) for chunk in chunks],
            out_specs=pl.BlockSpec((rows, columns), lambda i, at: (at[i], 0)),
        ),
        out_shape=jax.ShapeDtypeStruct((len(chunks) * rows, columns), F32),
        compiler_params=params(),
        cost_estimate=cost(rows * columns, 6 * len(chunks) * rows * columns),
    )(jnp.stack(places).astype(jnp.int32), *chunks)


def sum_late(values):
    n = lax.axis_size(ALL_AXES)
    parts = lax.all_to_all(
        jnp.broadcast_to(values[None], (n,) + values.shape),
        ALL_AXES,
        split_axis=0,
        concat_axis=0,
        tiled=True,
    )
    return jnp.sum(parts, axis=0)


def sum_small(flat):
    n = lax.axis_size(ALL_AXES)
    length = flat.shape[0]
    each = -(-length // (n * 128)) * 128
    parts = jnp.pad(flat, (0, n * each - length)).reshape(n, each)
    parts = lax.all_to_all(parts, ALL_AXES, split_axis=0, concat_axis=0, tiled=True)
    own = jnp.sum(parts, axis=0, keepdims=True)
    whole = lax.all_to_all(
        jnp.broadcast_to(own, (n, each)), ALL_AXES, split_axis=0, concat_axis=0, tiled=True
    )
    return whole.reshape(-1)[:length]


def swap_dp(rows):
    return lax.ppermute(rows, "dp", [(0, 1), (1, 0)])


def swap_context(rows, s):
    n = lax.axis_size("context")
    return lax.ppermute(rows, "context", [(i, i ^ s) for i in range(n)])


def half_groups(grad):
    d, c = lax.axis_index("dp"), lax.axis_index("context")
    n = lax.axis_size("context")
    rows = grad.shape[0] // 2
    each = rows // n
    got = swap_dp(lax.dynamic_slice_in_dim(grad, (1 - d) * rows, rows))
    chunks = []
    for s in range(n):
        mine = lax.dynamic_slice_in_dim(grad, d * rows + (c ^ s) * each, each)
        other = lax.dynamic_slice_in_dim(got, (c ^ s) * each, each)
        chunks.append((mine.astype(F32) + other.astype(F32)).astype(LOW))
    return chunks


def rest_groups(chunks):
    n = lax.axis_size("context")
    d, c = lax.axis_index("dp"), lax.axis_index("context")
    total = chunks[0].astype(F32)
    for s in range(1, n):
        total += swap_context(chunks[s], s).astype(F32)
    total = total.astype(LOW)
    found = [total] + [swap_context(total, s) for s in range(1, n)]
    places = [d * n + (c ^ s) for s in range(n)] + [(1 - d) * n + (c ^ s) for s in range(n)]
    return widen(places, found + [swap_dp(part) for part in found])


def arrival_order(n):
    return [sorted(range(n), key=lambda j: (abs(j - i), j)) for i in range(n)]


def choose(index, options):
    distinct = []
    for option in options:
        if option is not None and not any(option is other for other in distinct):
            distinct.append(option)
    result = distinct[0]
    for option in distinct[1:]:
        mask = functools.reduce(
            jnp.logical_or, [index == i for i, other in enumerate(options) if other is option]
        )
        result = jnp.where(mask, option, result)
    return result


def line_gather(chunk):
    return line_steps({0: chunk}, 1, lax.axis_size("expert"))


def line_steps(found, first, stop):
    n = lax.axis_size("expert")
    found = dict(found)
    for s in range(first, stop):
        found[-s] = lax.ppermute(
            found[1 - s], "expert", [(i, i + 1) for i in range(s - 1, n - 1)]
        )
        found[s] = lax.ppermute(found[s - 1], "expert", [(i + 1, i) for i in range(n - s)])
    return found


def context_gather(rows):
    n = lax.axis_size("context")
    c = lax.axis_index("context")
    found = {0: rows}
    for s in range(1, n):
        found[s] = lax.ppermute(rows, "context", [(i, i ^ s) for i in range(n)])
    return jnp.concatenate([choose(c, [found[i ^ j] for i in range(n)]) for j in range(n)], axis=0)


def context_parts(rows):
    n = lax.axis_size("context")
    c = lax.axis_index("context")
    each = rows.shape[0] // n
    return [
        swap_context(lax.dynamic_slice_in_dim(rows, (c ^ s) * each, each).astype(LOW), s)
        for s in range(1, n)
    ]


def zero_of(*others):
    return functools.reduce(
        jnp.add,
        [
            lax.slice(other, (0,) * other.ndim, (1,) * other.ndim).reshape(()).astype(F32) * 0.0
            for other in others
        ],
    )


def after(value, *others):
    return (value.astype(F32) + zero_of(*others)).astype(value.dtype)


def on_device(
    layer_input,
    grad_output,
    attn_gain,
    query_weight,
    key_weight,
    value_weight,
    q_gain,
    k_gain,
    output_weight,
    mlp_gain,
    router,
    w_gate,
    w_up,
    w_down,
    routes,
    half_order,
):
    n_context = lax.axis_size("context")
    n_expert = lax.axis_size("expert")
    n_groups = lax.axis_size(GROUP_AXES)
    tok_dev, width = layer_input.shape[1:]
    size = q_gain.shape[0]
    kv_total = key_weight.shape[1] * n_expert
    group_dev = n_expert // (kv_total // size)
    kv_index = lax.axis_index("expert") // group_dev
    block = tok_dev * n_expert
    seq = block * n_context
    half = block // 2
    experts = router.shape[1]
    exp_dev = w_gate.shape[0]
    top = routes.shape[2]
    capacity = max(2, (tok_dev * top * 9 + 8 * experts - 1) // (8 * experts))
    scale = size ** (-0.5)

    seq_rows = jnp.arange(seq, dtype=jnp.int32)
    context = lax.axis_index("context")
    own_halves = lax.dynamic_slice_in_dim(half_order, 2 * context, 2)
    own_pos = (own_halves[:, None] * half + jnp.arange(half, dtype=jnp.int32)[None]).reshape(-1)
    per_half = half // TILE
    tile_pos = (half_order[:, None] * per_half + jnp.arange(per_half, dtype=jnp.int32)).reshape(-1)
    kidx = jnp.sum(
        (tile_pos[None, :] == jnp.arange(seq // TILE, dtype=jnp.int32)[:, None])
        * jnp.arange(seq // TILE, dtype=jnp.int32)[None, :],
        axis=1,
    ).astype(jnp.int32)
    qpos = lax.dynamic_slice_in_dim(tile_pos, context * (block // TILE), block // TILE)
    freq = jnp.power(THETA, -jnp.arange(0, size, 2).astype(F32) / size)
    angles = own_pos.astype(F32)[:, None] * freq[None, :]
    cosine, sine = jnp.cos(angles), jnp.sin(angles)
    cos2 = jnp.concatenate([cosine, cosine], axis=1)
    sin2 = jnp.concatenate([-sine, sine], axis=1)

    place = lax.axis_index("expert")
    place_1 = place.astype(jnp.int32)[None]
    lanes = -(-2 * experts // 128) * 128
    mask = jnp.any(
        routes[0][:, :, None] == jnp.arange(lanes, dtype=jnp.int32)[None, None, :], axis=1
    )
    mask_wide = mask.astype(F32)
    router_wide = jnp.pad(router, ((0, 0), (0, lanes - experts)))

    grad_low = grad_output[0]
    grad_wide = jnp.concatenate([grad_low, mask.astype(LOW)], axis=1)
    grad_col = lax.all_gather(grad_wide, "expert", axis=0, tiled=True)

    x_low = layer_input[0]
    x_normal, _ = norm_parts(x_low.astype(F32))
    normed_found = line_gather((x_normal * attn_gain).astype(LOW))
    if group_dev == 1:
        kv_weights = jnp.concatenate([key_weight, value_weight], axis=1)
    else:
        key_whole = lax.all_gather(key_weight, "expert", axis=1, tiled=True)
        value_whole = lax.all_gather(value_weight, "expert", axis=1, tiled=True)
        kv_weights = jnp.concatenate(
            [
                lax.dynamic_slice_in_dim(key_whole, kv_index * size, size, 1),
                lax.dynamic_slice_in_dim(value_whole, kv_index * size, size, 1),
            ],
            axis=1,
        )
    normed_rows, own_kv, key_proj = project_keys(
        place_1, normed_found, kv_weights, k_gain, cos2, sin2, scale * LOG2E, [grad_col]
    )
    kv_whole = context_gather(own_kv)
    queries, query_proj = project_queries(normed_rows, query_weight, q_gain, cos2, sin2)

    n_half = n_expert // 2
    rows_half = n_groups * n_half * capacity
    order_here = jnp.asarray(arrival_order(n_expert), jnp.int32)[place]
    turn_here = jnp.sum(
        (order_here[:, None] == jnp.arange(n_expert, dtype=jnp.int32)[None, :])
        * jnp.arange(n_expert, dtype=jnp.int32)[:, None],
        axis=0,
    ).astype(jnp.int32)
    meta = jnp.concatenate([place_1, turn_here, order_here])
    grad_sent, spreads_placed, spreads = make_tables(
        meta, grad_col, width, n_groups, n_half, capacity, [router_wide, mask_wide]
    )

    def swap_plane(rows):
        wide = rows.shape[1]
        rows = lax.all_to_all(
            rows.reshape(n_groups, n_half * capacity, wide),
            GROUP_AXES,
            split_axis=0,
            concat_axis=0,
            tiled=True,
        )
        return rows.reshape(rows_half, wide)

    attended, inverse = attend(qpos, kidx, queries, kv_whole, [])
    attn_part = dot_nn(attended, output_weight).astype(LOW)
    attn_rows = lax.psum_scatter(attn_part, "expert", scatter_dimension=0, tiled=True)

    grad_x = [swap_plane(rows) for rows in grad_sent]
    act_pull = [dot_nt(rows, w_down[0]) for rows in grad_x]

    hidden, mixed, probs = route_rows(
        x_low, attn_rows, mlp_gain, router_wide, mask_wide, experts, [grad_x[0]]
    )

    who = (lax.axis_index(ALL_AXES) * exp_dev).astype(jnp.int32)[None]
    mixed_found = line_gather(mixed)
    near = spread_rows(place_1, spreads[0], mixed_found, range(n_half), [grad_x[1]])
    x_near = swap_plane(near)
    worked_near = run_expert(who, x_near, w_gate[0], w_up[0], act_pull[0], experts, [])
    far = spread_rows(
        place_1, spreads[1], mixed_found, range(n_half, n_expert), [worked_near[-1]]
    )
    x_far = swap_plane(far)
    worked_far = run_expert(who, x_far, w_gate[0], w_up[0], act_pull[1], experts, [])
    xs = [x_near, x_far]
    acts, gate_lows, up_lows, copies = (list(pair) for pair in zip(worked_near, worked_far))
    back_far = swap_plane(copies[1])
    back_near = swap_plane(copies[0])
    copies_col = combine_rows(spreads_placed, [back_near, back_far], [])
    copies_sum = lax.psum_scatter(copies_col, "expert", scatter_dimension=0, tiled=True)
    join = lambda parts: jnp.concatenate(parts, axis=0)
    x_all = join([x[:, :width] for x in xs])
    grad_w_gate = dot_tn(x_all, join(gate_lows))
    grad_w_up = dot_tn(x_all, join(up_lows))
    grad_w_down = dot_tn(join(acts), join(grad_x))

    returned = [(dot_nn(act, w_down[0]) + zero_of(back_near)).astype(LOW) for act in acts]
    returned_near = swap_plane(returned[0])

    grad_hidden, grad_hidden_low, grad_mlp_gain, grad_router = route_back(
        copies_sum,
        grad_low,
        hidden,
        mlp_gain,
        router_wide,
        mask_wide,
        probs,
        experts,
        [returned_near, grad_w_gate],
    )
    early = sum_small(jnp.concatenate([grad_mlp_gain[0], grad_router[:experts].reshape(-1)]))

    returned_far = swap_plane(returned[1])
    grad_attn = lax.all_gather(grad_hidden_low, "expert", axis=0, tiled=True)
    grad_o, centre = grad_attended(
        grad_attn, output_weight, attended, inverse, [returned_far, grad_w_up, grad_w_down]
    )
    combined = combine_rows(spreads_placed, [returned_near, returned_far], [grad_attn])
    output_rows = hidden + lax.psum_scatter(
        combined, "expert", scatter_dimension=0, tiled=True
    ).astype(F32)
    half_w_out = half_groups(dot_tn(attended, grad_attn).astype(LOW))
    grad_kv, grad_q, grad_q_gain = attend_back(
        qpos,
        kidx,
        queries,
        grad_o,
        centre,
        kv_whole,
        query_proj,
        q_gain,
        cos2,
        sin2,
        [*half_w_out, combined],
    )
    kv_parts = context_parts(grad_kv)
    half_w_query = half_groups(dot_tn(normed_rows, grad_q).astype(LOW))

    kv_grads, grad_k_gain = kv_back(
        context, grad_kv, kv_parts, key_proj, k_gain, cos2, sin2, scale, output_rows
    )
    grad_normed = dot_nt(grad_q, query_weight) + dot_nt(kv_grads, kv_weights)
    grad_attn_gain = jnp.sum(grad_normed * normed_rows.astype(F32), axis=0) / attn_gain
    grad_normed = lax.psum_scatter(
        grad_normed.astype(LOW), "expert", scatter_dimension=0, tiled=True
    )
    grad_input = input_back(grad_normed, x_low, attn_gain, grad_hidden)

    grad_w_out = rest_groups(half_w_out)
    grad_w_query = rest_groups(half_w_query)
    grad_w_kv = dot_tn(normed_rows, kv_grads).astype(LOW)
    if group_dev == 1:
        grad_w_kv = rest_groups(half_groups(grad_w_kv))
        grad_w_key, grad_w_value = grad_w_kv[:, :size], grad_w_kv[:, size:]
    else:
        blank = jnp.zeros((width, kv_total), LOW)
        pieces = []
        for part in (grad_w_kv[:, :size], grad_w_kv[:, size:]):
            padded = lax.dynamic_update_slice(blank, part, (0, kv_index * size))
            pieces.append(lax.psum_scatter(padded, "expert", scatter_dimension=1, tiled=True))
        grad_w_key, grad_w_value = (lax.psum(piece, GROUP_AXES).astype(F32) for piece in pieces)

    late = sum_late(jnp.concatenate([grad_attn_gain, grad_q_gain[0], grad_k_gain[0]]))
    grad_attn_gain, late_heads = late[:width], late[width:]
    grad_q_gain, grad_k_gain = late_heads[:size], late_heads[size:]
    grad_mlp_gain, grad_router = early[:width], early[width:]
    return (
        output_rows.astype(LOW)[None],
        grad_input[None],
        grad_attn_gain,
        grad_w_query,
        grad_w_key,
        grad_w_value,
        grad_q_gain,
        grad_k_gain,
        grad_w_out,
        grad_mlp_gain,
        grad_router.reshape(experts, width).T,
        grad_w_gate[None],
        grad_w_up[None],
        grad_w_down[None],
    )


def solution(mesh):
    rows = P("dp", ("context", "expert"), None)
    expert = P(ALL_AXES, None, None)
    columns = P(None, "expert")
    in_specs = (
        rows,
        rows,
        P(),
        columns,
        columns,
        columns,
        P(),
        P(),
        P("expert", None),
        P(),
        P(),
        expert,
        expert,
        expert,
        rows,
        P(),
    )
    out_specs = (
        rows,
        rows,
        P(),
        columns,
        columns,
        columns,
        P(),
        P(),
        P("expert", None),
        P(),
        P(),
        expert,
        expert,
        expert,
    )
    return jax.shard_map(
        on_device, mesh=mesh, in_specs=in_specs, out_specs=out_specs, check_vma=False
    )
```

```python
import functools
import math

import jax
import jax.numpy as jnp
from jax import lax
from jax.experimental import pallas as pl
from jax.experimental.pallas import tpu as pltpu
from jax.sharding import PartitionSpec as P

EPS = 1e-06
THETA = 1000000.0
TILE = 256
VMEM_BYTES = 56 * 1024 * 1024
LOG2E = math.log2(math.e)
LOW = jnp.bfloat16
F32 = jnp.float32
ALL_AXES = ("dp", "context", "expert")
GROUP_AXES = ("dp", "context")


def dot_nn(a, b):
    return lax.dot_general(a, b, (((1,), (0,)), ((), ())), preferred_element_type=F32)


def dot_nt(a, b):
    return lax.dot_general(a, b, (((1,), (1,)), ((), ())), preferred_element_type=F32)


def dot_tn(a, b):
    return lax.dot_general(a, b, (((0,), (0,)), ((), ())), preferred_element_type=F32)


def params(**more):
    return pltpu.CompilerParams(vmem_limit_bytes=VMEM_BYTES, **more)


def cost(flops, nbytes, exps=0):
    return pl.CostEstimate(flops=int(flops), bytes_accessed=int(nbytes), transcendentals=int(exps))


def head_forward(u, gain, cos2, sin2):
    rr = lax.rsqrt(jnp.mean(u * u, axis=-1, keepdims=True) + EPS)
    y = u * rr * gain
    return y * cos2 + pltpu.roll(y, 64, 1) * sin2


def head_backward(gy, u, gain, cos2, sin2):
    g = gy * cos2 - pltpu.roll(gy, 64, 1) * sin2
    rr = lax.rsqrt(jnp.mean(u * u, axis=-1, keepdims=True) + EPS)
    n = u * rr
    gn = g * gain
    grad = rr * (gn - n * jnp.mean(gn * n, axis=-1, keepdims=True))
    return grad, jnp.sum(g * n, axis=0, keepdims=True)


def query_kernel(x_ref, w_ref, gain_ref, cos_ref, sin_ref, rot_ref, proj_ref):
    tiles, heads, rows, size = rot_ref.shape
    acc = dot_nn(x_ref[...], w_ref[...])
    for h in range(heads):
        u = acc[:, h * size : (h + 1) * size]
        rot = head_forward(u, gain_ref[...], cos_ref[...], sin_ref[...])
        proj_ref[:, h] = u.reshape(tiles, rows, size)
        rot_ref[:, h] = rot.astype(LOW).reshape(tiles, rows, size)


def project_queries(normed, weight, gain, cos2, sin2):
    block, width = normed.shape
    size = cos2.shape[1]
    heads = weight.shape[1] // size
    tiles = block // TILE
    whole = lambda i: (0, 0)
    per = lambda i: (0, i, 0, 0)
    shape = (tiles, heads, TILE, size)
    return pl.pallas_call(
        query_kernel,
        grid=(heads // 2,),
        in_specs=[
            pl.BlockSpec((block, width), whole),
            pl.BlockSpec((width, 2 * size), lambda i: (0, i)),
            pl.BlockSpec((1, size), whole),
            pl.BlockSpec((block, size), whole),
            pl.BlockSpec((block, size), whole),
        ],
        out_specs=[pl.BlockSpec((tiles, 2, TILE, size), per)] * 2,
        out_shape=[jax.ShapeDtypeStruct(shape, LOW), jax.ShapeDtypeStruct(shape, F32)],
        compiler_params=params(),
        cost_estimate=cost(2 * block * width * heads * size, 12e6),
    )(normed, weight, gain[None], cos2, sin2)


def put_in_order(place, refs, out_ref):
    n = (len(refs) + 1) // 2
    rows = refs[0].shape[0]
    for distance in range(1 - n, n):
        ref = refs[distance + n - 1]
        at = place + distance

        @pl.when(jnp.logical_and(at >= 0, at < n))
        def _():
            out_ref[pl.ds(pl.multiple_of(at * rows, rows), rows), :] = ref[...]


def chunk_list(found):
    n = (len(found) + 1) // 2
    return [found[distance] for distance in range(1 - n, n)]


def key_kernel(factor, n_chunks, place_ref, *refs):
    w_ref, gain_ref, cos_ref, sin_ref = refs[n_chunks : n_chunks + 4]
    rows_ref, kv_ref, proj_ref = refs[-3:]
    size = proj_ref.shape[1]
    put_in_order(place_ref[0], refs[:n_chunks], rows_ref)
    acc = dot_nn(rows_ref[...], w_ref[...])
    u = acc[:, :size]
    rot = head_forward(u, gain_ref[...], cos_ref[...], sin_ref[...])
    proj_ref[...] = u
    kv_ref[:, :size] = (rot * factor).astype(LOW)
    kv_ref[:, size:] = acc[:, size:].astype(LOW)


def full(shape):
    return pl.BlockSpec(shape, lambda *_: (0,) * len(shape))


def project_keys(place, found, weight, gain, cos2, sin2, factor, others):
    chunks = chunk_list(found)
    rows, width = chunks[0].shape
    block, size = cos2.shape
    operands = [*chunks, weight, gain[None], cos2, sin2]
    shapes = [
        jax.ShapeDtypeStruct((block, width), LOW),
        jax.ShapeDtypeStruct((block, 2 * size), LOW),
        jax.ShapeDtypeStruct((block, size), F32),
    ]
    return pl.pallas_call(
        functools.partial(key_kernel, factor, len(chunks)),
        grid_spec=pltpu.PrefetchScalarGridSpec(
            num_scalar_prefetch=1,
            grid=(1,),
            in_specs=[full(x.shape) for x in operands]
            + [pl.BlockSpec(memory_space=pl.ANY)] * len(others),
            out_specs=[full(x.shape) for x in shapes],
        ),
        out_shape=shapes,
        compiler_params=params(),
        cost_estimate=cost(4 * block * width * size, 8e6),
    )(place, *operands, *others)


def attend_kernel(qpos_ref, kidx_ref, q_ref, kv_ref, *rest):
    out_ref, inv_ref, acc_ref = rest[-3:]
    heads, rows, size = q_ref.shape[1:]
    last = qpos_ref[pl.program_id(0)]
    acc_ref[...] = jnp.zeros_like(acc_ref)
    ones = jnp.ones((rows, size), LOW)

    def step(place, masked):
        start = pl.multiple_of(kidx_ref[place] * rows, rows)
        keys = kv_ref[pl.ds(start, rows), :size]
        values = jnp.concatenate([kv_ref[pl.ds(start, rows), size:], ones], axis=1)
        for h in range(heads):
            e = jnp.exp2(dot_nt(q_ref[0, h], keys))
            if masked:
                qi = lax.broadcasted_iota(jnp.int32, e.shape, 0)
                ki = lax.broadcasted_iota(jnp.int32, e.shape, 1)
                e = jnp.where(ki <= qi, e, 0.0)
            acc_ref[h] += dot_nn(e.astype(LOW), values)

    lax.fori_loop(0, last, lambda p, c: (step(p, False), c)[1], 0)
    step(last, True)
    for h in range(heads):
        inv = 1.0 / acc_ref[h, :, size:]
        inv_ref[0, h] = inv
        out_ref[:, h * size : (h + 1) * size] = (acc_ref[h, :, :size] * inv).astype(LOW)


def attend(qpos, kidx, queries, kv, others):
    tiles, heads, rows, size = queries.shape
    seq = kv.shape[0]
    return pl.pallas_call(
        attend_kernel,
        grid_spec=pltpu.PrefetchScalarGridSpec(
            num_scalar_prefetch=2,
            grid=(tiles,),
            in_specs=[
                pl.BlockSpec((1, heads, rows, size), lambda i, a, b: (i, 0, 0, 0)),
                pl.BlockSpec((seq, 2 * size), lambda i, a, b: (0, 0)),
            ]
            + [pl.BlockSpec(memory_space=pl.ANY)] * len(others),
            out_specs=[
                pl.BlockSpec((rows, heads * size), lambda i, a, b: (i, 0)),
                pl.BlockSpec((1, heads, rows, size), lambda i, a, b: (i, 0, 0, 0)),
            ],
            scratch_shapes=[pltpu.VMEM((heads, rows, 2 * size), F32)],
        ),
        out_shape=[
            jax.ShapeDtypeStruct((tiles * rows, heads * size), LOW),
            jax.ShapeDtypeStruct((tiles, heads, rows, size), F32),
        ],
        compiler_params=params(),
        cost_estimate=cost(
            6 * tiles * rows * heads * seq * size, 8e6, tiles * rows * heads * seq
        ),
    )(qpos, kidx, queries, kv, *others)


def grad_out_kernel(rows_ref, w_ref, o_ref, inv_ref, *rest):
    do_ref, centre_ref = rest[-2:]
    tiles, heads, rows, size = do_ref.shape
    acc = dot_nt(rows_ref[...], w_ref[...])
    for t in range(tiles):
        for h in range(heads):
            part = slice(t * rows, (t + 1) * rows), slice(h * size, (h + 1) * size)
            low = (acc[part] * inv_ref[t, h]).astype(LOW)
            do_ref[t, h] = low
            product = low.astype(F32) * o_ref[part].astype(F32)
            centre = jnp.sum(jnp.transpose(product), axis=0, keepdims=True)
            centre_ref[t, h] = jnp.broadcast_to(centre, (8, rows))


def grad_attended(grad_rows, weight, attended, inverse, others):
    tiles, heads, rows, size = inverse.shape
    block, width = grad_rows.shape
    return pl.pallas_call(
        grad_out_kernel,
        grid=(heads // 2,),
        in_specs=[
            pl.BlockSpec((block, width), lambda i: (0, 0)),
            pl.BlockSpec((2 * size, width), lambda i: (i, 0)),
            pl.BlockSpec((block, 2 * size), lambda i: (0, i)),
            pl.BlockSpec((tiles, 2, rows, size), lambda i: (0, i, 0, 0)),
        ]
        + [pl.BlockSpec(memory_space=pl.ANY)] * len(others),
        out_specs=[
            pl.BlockSpec((tiles, 2, rows, size), lambda i: (0, i, 0, 0)),
            pl.BlockSpec((tiles, 2, 8, rows), lambda i: (0, i, 0, 0)),
        ],
        out_shape=[
            jax.ShapeDtypeStruct((tiles, heads, rows, size), LOW),
            jax.ShapeDtypeStruct((tiles, heads, 8, rows), F32),
        ],
        compiler_params=params(),
        cost_estimate=cost(2 * block * width * heads * size, 12e6),
    )(grad_rows, weight, attended, inverse, *others)


def attend_back_kernel(
    qpos_ref,
    kidx_ref,
    q_ref,
    do_ref,
    centre_ref,
    kv_ref,
    proj_ref,
    gain_ref,
    cos_ref,
    sin_ref,
    *rest,
):
    dkv_ref, dq_ref, dgain_ref, acc_ref = rest[-4:]
    heads, rows, size = q_ref.shape[1:]
    last = qpos_ref[pl.program_id(0)]

    @pl.when(pl.program_id(0) == 0)
    def _():
        dkv_ref[...] = jnp.zeros_like(dkv_ref)
        dgain_ref[...] = jnp.zeros_like(dgain_ref)

    acc_ref[...] = jnp.zeros_like(acc_ref)

    def step(place, masked):
        start = pl.multiple_of(kidx_ref[place] * rows, rows)
        keys = kv_ref[pl.ds(start, rows), :size]
        values = kv_ref[pl.ds(start, rows), size:]
        dk = dkv_ref[pl.ds(start, rows), :size]
        dv = dkv_ref[pl.ds(start, rows), size:]
        for h in range(heads):
            query, grad = q_ref[0, h], do_ref[0, h]
            e = jnp.exp2(dot_nt(keys, query))
            if masked:
                ki = lax.broadcasted_iota(jnp.int32, e.shape, 0)
                qi = lax.broadcasted_iota(jnp.int32, e.shape, 1)
                e = jnp.where(ki <= qi, e, 0.0)
            ds = (e * (dot_nt(values, grad) - centre_ref[0, h, 0:1])).astype(LOW)
            dv += dot_nn(e.astype(LOW), grad)
            dk += dot_nn(ds, query)
            acc_ref[h] += dot_tn(ds, keys)
        dkv_ref[pl.ds(start, rows), :size] = dk
        dkv_ref[pl.ds(start, rows), size:] = dv

    lax.fori_loop(0, last, lambda p, c: (step(p, False), c)[1], 0)
    step(last, True)
    total = jnp.zeros((1, size), F32)
    for h in range(heads):
        grad, gain_part = head_backward(
            acc_ref[h] * (1.0 / LOG2E), proj_ref[0, h], gain_ref[...], cos_ref[...], sin_ref[...]
        )
        dq_ref[:, h * size : (h + 1) * size] = grad.astype(LOW)
        total += gain_part
    dgain_ref[...] += total


def attend_back(qpos, kidx, queries, grads, centre, kv, proj, gain, cos2, sin2, others):
    tiles, heads, rows, size = queries.shape
    seq = kv.shape[0]
    per = pl.BlockSpec((1, heads, rows, size), lambda i, a, b: (i, 0, 0, 0))
    flat = lambda i, a, b: (0, 0)
    rowwise = lambda i, a, b: (i, 0)
    return pl.pallas_call(
        attend_back_kernel,
        grid_spec=pltpu.PrefetchScalarGridSpec(
            num_scalar_prefetch=2,
            grid=(tiles,),
            in_specs=[
                per,
                per,
                pl.BlockSpec((1, heads, 8, rows), lambda i, a, b: (i, 0, 0, 0)),
                pl.BlockSpec((seq, 2 * size), flat),
                per,
                pl.BlockSpec((1, size), flat),
                pl.BlockSpec((rows, size), rowwise),
                pl.BlockSpec((rows, size), rowwise),
            ]
            + [pl.BlockSpec(memory_space=pl.ANY)] * len(others),
            out_specs=[
                pl.BlockSpec((seq, 2 * size), flat),
                pl.BlockSpec((rows, heads * size), rowwise),
                pl.BlockSpec((1, size), flat),
            ],
            scratch_shapes=[pltpu.VMEM((heads, rows, size), F32)],
        ),
        out_shape=[
            jax.ShapeDtypeStruct((seq, 2 * size), F32),
            jax.ShapeDtypeStruct((tiles * rows, heads * size), LOW),
            jax.ShapeDtypeStruct((1, size), F32),
        ],
        compiler_params=params(),
        cost_estimate=cost(
            15 * tiles * rows * heads * seq * size, 12e6, tiles * rows * heads * seq
        ),
    )(qpos, kidx, queries, grads, centre, kv, proj, gain[None], cos2, sin2, *others)


def split_low(value):
    high = value.astype(LOW)
    return high, (value - high.astype(F32)).astype(LOW)


def norm_parts(rows):
    rr = lax.rsqrt(jnp.mean(rows * rows, axis=-1, keepdims=True) + EPS)
    return rows * rr, rr


def norm_back(grad, normal, rr, gain):
    weighted = grad * gain
    return rr * (weighted - normal * jnp.mean(weighted * normal, axis=-1, keepdims=True))


def add_all(refs):
    return functools.reduce(jnp.add, [ref[...].astype(F32) for ref in refs])


def router_kernel(experts, *refs):
    x_ref, attn_ref, gain_ref, router_ref, mask_ref = refs[:5]
    hidden_ref, mixed_ref, probs_ref = refs[-3:]
    width = x_ref.shape[1]
    lanes = router_ref.shape[1]
    hidden = add_all([x_ref, attn_ref])
    hidden_ref[...] = hidden
    mixed = (norm_parts(hidden)[0] * gain_ref[...]).astype(LOW)
    mixed_ref[:, :width] = mixed
    logits = dot_nn(mixed, router_ref[...])
    lane = lax.broadcasted_iota(jnp.int32, logits.shape, 1)
    logits = jnp.where(lane < experts, logits, -1e30)
    weights = jnp.exp(logits - jnp.max(logits, axis=1, keepdims=True))
    probs = weights / jnp.sum(weights, axis=1, keepdims=True)
    probs_ref[...] = probs
    chosen = probs * mask_ref[...]
    high, low = split_low(chosen / jnp.sum(chosen, axis=1, keepdims=True))
    both = high.astype(F32) + pltpu.roll(low.astype(F32), experts, 1)
    mixed_ref[:, width:] = both.astype(LOW)


def route_rows(x, attn, gain, router, mask, experts, others):
    tokens, width = x.shape
    lanes = router.shape[1]
    operands = [x, attn, gain[None], router, mask]
    shapes = [
        jax.ShapeDtypeStruct((tokens, width), F32),
        jax.ShapeDtypeStruct((tokens, width + lanes), LOW),
        jax.ShapeDtypeStruct((tokens, lanes), F32),
    ]
    return pl.pallas_call(
        functools.partial(router_kernel, experts),
        grid=(1,),
        in_specs=[full(value.shape) for value in operands]
        + [pl.BlockSpec(memory_space=pl.ANY)] * len(others),
        out_specs=[full(shape.shape) for shape in shapes],
        out_shape=shapes,
        compiler_params=params(),
        cost_estimate=cost(2 * tokens * width * lanes, 5e6),
    )(*operands, *others)


def table_kernel(capacity, n_half, meta_ref, col_ref, *rest):
    outs = rest[-6:-1]
    block = col_ref.shape[0]
    rows, width = outs[0].shape
    n = 2 * n_half
    tokens = block // n
    cap_half = n_half * capacity
    groups = rows // cap_half
    mask = col_ref[:, width:]
    lanes = mask.shape[1]
    padded = -(-groups // 16) * 16
    group = lax.broadcasted_iota(jnp.int32, (padded, lanes), 0)
    lane = lax.broadcasted_iota(jnp.int32, (padded, lanes), 1)
    wanted = jnp.logical_and(lane == group * n + meta_ref[0], group < groups)
    hits = dot_nt(jnp.where(wanted, 1.0, 0.0).astype(LOW), mask)
    before = lax.broadcasted_iota(jnp.int32, (tokens, tokens), 0)
    after_it = lax.broadcasted_iota(jnp.int32, (tokens, tokens), 1)
    earlier = jnp.where(before < after_it, 1.0, 0.0).astype(LOW)
    slots = []
    for z in range(n):
        hit = hits[:, z * tokens : (z + 1) * tokens]
        rank = dot_nn(hit.astype(LOW), earlier)
        turn = (meta_ref[1 + z] * capacity).astype(F32)
        slots.append(jnp.where(hit > 0.5, rank + turn, -1.0))
    slots = jnp.concatenate(slots, axis=1)[:groups]
    slot = lax.broadcasted_iota(jnp.int32, (groups, cap_half, block), 1).astype(F32)
    placed_ref, back_ref = rest[-1], outs[4]
    spreads = []
    for part in range(2):
        rows_ref, arrived_ref = outs[part], outs[2 + part]
        same = slots[:, None, :] == slot + float(part * cap_half)
        spread = jnp.where(same, 1.0, 0.0).reshape(rows, block)
        spreads.append(spread)
        spread = spread.astype(LOW)
        placed_ref[...] = spread
        rows_ref[...] = dot_nn(spread, col_ref[:, :width]).astype(LOW)
        for k in range(n_half):
            start = pl.multiple_of(meta_ref[1 + n + part * n_half + k] * tokens, tokens)
            arrived_ref[:, k * tokens : (k + 1) * tokens] = placed_ref[:, pl.ds(start, tokens)]
    back_ref[...] = jnp.transpose(jnp.concatenate(spreads, axis=0)).astype(LOW)


def make_tables(meta, col, width, groups, n_half, capacity, others):
    block = col.shape[0]
    rows = groups * n_half * capacity
    shapes = (
        [jax.ShapeDtypeStruct((rows, width), LOW)] * 2
        + [jax.ShapeDtypeStruct((rows, block // 2), LOW)] * 2
        + [jax.ShapeDtypeStruct((block, 2 * rows), LOW)]
    )
    outs = pl.pallas_call(
        functools.partial(table_kernel, capacity, n_half),
        grid_spec=pltpu.PrefetchScalarGridSpec(
            num_scalar_prefetch=1,
            grid=(1,),
            in_specs=[full(col.shape)] + [pl.BlockSpec(memory_space=pl.ANY)] * len(others),
            out_specs=[full(shape.shape) for shape in shapes],
            scratch_shapes=[pltpu.VMEM((rows, block), LOW)],
        ),
        out_shape=shapes,
        compiler_params=params(),
        cost_estimate=cost(4 * rows * block * width, 12e6),
    )(meta, col, *others)
    return outs[:2], outs[2:4], outs[4]


def spread_kernel(choices, place_ref, spread_ref, *refs):
    out_ref, rows_ref = refs[-2:]
    for k, by_place in enumerate(choices):
        for which in sorted(set(by_place)):
            hit = functools.reduce(
                jnp.logical_or,
                [place_ref[0] == i for i, other in enumerate(by_place) if other == which],
            )

            @pl.when(hit)
            def _():
                tokens = refs[which].shape[0]
                rows_ref[k * tokens : (k + 1) * tokens] = refs[which][...]

    out_ref[...] = dot_nn(spread_ref[...], rows_ref[...]).astype(LOW)


def spread_rows(place, spread, found, turns, others):
    n = lax.axis_size("expert")
    order = arrival_order(n)
    distances = sorted({order[i][turn] - i for i in range(n) for turn in turns})
    choices = [[distances.index(order[i][turn] - i) for i in range(n)] for turn in turns]
    chunks = [found[distance] for distance in distances]
    tokens, wide = chunks[0].shape
    rows = spread.shape[0]
    return pl.pallas_call(
        functools.partial(spread_kernel, choices),
        grid_spec=pltpu.PrefetchScalarGridSpec(
            num_scalar_prefetch=1,
            grid=(1,),
            in_specs=[full(spread.shape)]
            + [full(chunk.shape) for chunk in chunks]
            + [pl.BlockSpec(memory_space=pl.ANY)] * len(others),
            out_specs=full((rows, wide)),
            scratch_shapes=[pltpu.VMEM((len(turns) * tokens, wide), LOW)],
        ),
        out_shape=jax.ShapeDtypeStruct((rows, wide), LOW),
        compiler_params=params(),
        cost_estimate=cost(2 * rows * len(turns) * tokens * wide, 5e6),
    )(place, spread, *chunks, *others)


def router_back_kernel(experts, *refs):
    sum_ref, g_ref, hidden_ref, gain_ref, router_ref, mask_ref, probs_ref = refs[:7]
    grad_ref, low_ref, dgain_ref, drouter_ref = refs[-4:]
    width = g_ref.shape[1]
    lanes = router_ref.shape[1]
    total = sum_ref[...].astype(F32)
    table = total[:, width:]
    mask, probs = mask_ref[...], probs_ref[...]
    grad_gates = (table + pltpu.roll(table, lanes - experts, 1)) * mask
    chosen = probs * mask
    chosen_sum = jnp.sum(chosen, axis=1, keepdims=True)
    mean = jnp.sum(grad_gates * (chosen / chosen_sum), axis=1, keepdims=True)
    centred = mask * (grad_gates - mean) / chosen_sum
    grad_logits = probs * (centred - jnp.sum(centred * chosen, axis=1, keepdims=True))
    high, low = split_low(grad_logits)
    router = router_ref[...]
    grad = total[:, :width] + dot_nt(high, router) + dot_nt(low, router)
    normal, rr = norm_parts(hidden_ref[...])
    mixed = (normal * gain_ref[...]).astype(LOW)
    drouter_ref[...] = dot_tn(high, mixed) + dot_tn(low, mixed)
    dgain_ref[...] = jnp.sum(grad * normal, axis=0, keepdims=True)
    grad_hidden = g_ref[...].astype(F32) + norm_back(grad, normal, rr, gain_ref[...])
    grad_ref[...] = grad_hidden
    low_ref[...] = grad_hidden.astype(LOW)


def route_back(summed, g, hidden, gain, router, mask, probs, experts, others):
    tokens, width = g.shape
    lanes = router.shape[1]
    operands = [summed, g, hidden, gain[None], router, mask, probs]
    shapes = [
        jax.ShapeDtypeStruct((tokens, width), F32),
        jax.ShapeDtypeStruct((tokens, width), LOW),
        jax.ShapeDtypeStruct((1, width), F32),
        jax.ShapeDtypeStruct((lanes, width), F32),
    ]
    return pl.pallas_call(
        functools.partial(router_back_kernel, experts),
        grid=(1,),
        in_specs=[full(value.shape) for value in operands]
        + [pl.BlockSpec(memory_space=pl.ANY)] * len(others),
        out_specs=[full(shape.shape) for shape in shapes],
        out_shape=shapes,
        compiler_params=params(),
        cost_estimate=cost(8 * tokens * width * lanes, 8e6),
    )(*operands, *others)


def combine_kernel(table_ref, near_ref, far_ref, *rest):
    rows = near_ref.shape[0]
    total = dot_nn(table_ref[:, :rows], near_ref[...]) + dot_nn(table_ref[:, rows:], far_ref[...])
    rest[-1][...] = total.astype(LOW)


def combine_rows(table, rows, others):
    block = table.shape[0]
    slots, wide = rows[0].shape
    tile = min(block, 256)
    return pl.pallas_call(
        combine_kernel,
        grid=(block // tile,),
        in_specs=[pl.BlockSpec((tile, 2 * slots), lambda i: (i, 0))]
        + [full(value.shape) for value in rows]
        + [pl.BlockSpec(memory_space=pl.ANY)] * len(others),
        out_specs=pl.BlockSpec((tile, wide), lambda i: (i, 0)),
        out_shape=jax.ShapeDtypeStruct((block, wide), LOW),
        compiler_params=params(),
        cost_estimate=cost(4 * slots * block * wide, 10e6),
    )(table, *rows, *others)


def expert_kernel(experts, who_ref, x_ref, gate_ref, up_ref, pull_ref, *rest):
    act_ref, dgate_ref, dup_ref, copy_ref = rest[-4:]
    width = gate_ref.shape[0]
    x = x_ref[:, :width]
    table = x_ref[:, width:].astype(F32)
    lane = lax.broadcasted_iota(jnp.int32, table.shape, 1)
    mine = who_ref[0]
    gate = jnp.sum(
        jnp.where(jnp.logical_or(lane == mine, lane == mine + experts), table, 0.0),
        axis=1,
        keepdims=True,
    )
    pre_gate = dot_nn(x, gate_ref[...])
    pre_up = dot_nn(x, up_ref[...])
    pull = pull_ref[...]
    sig = 1.0 / (1.0 + jnp.exp(-pre_gate))
    silu = pre_gate * sig
    act = silu * pre_up
    act_ref[...] = (act * gate).astype(LOW)
    high, low = split_low(jnp.sum(act * pull, axis=1, keepdims=True))
    pull = pull * gate
    dup = (pull * silu).astype(LOW)
    dgate = (pull * pre_up * (sig * (1.0 + pre_gate * (1.0 - sig)))).astype(LOW)
    dgate_ref[...] = dgate
    dup_ref[...] = dup
    copy_ref[:, :width] = (dot_nt(dgate, gate_ref[...]) + dot_nt(dup, up_ref[...])).astype(LOW)
    back = jnp.where(lane == mine, high.astype(F32), 0.0)
    back = jnp.where(lane == mine + experts, low.astype(F32), back)
    copy_ref[:, width:] = back.astype(LOW)


def run_expert(who, x, w_gate, w_up, pull, experts, others):
    rows, wide = x.shape
    width, hidden = w_gate.shape
    tile = rows // 2 if rows % 32 == 0 else rows
    by_rows = lambda columns: pl.BlockSpec((tile, columns), lambda i, p: (i, 0))
    return pl.pallas_call(
        functools.partial(expert_kernel, experts),
        grid_spec=pltpu.PrefetchScalarGridSpec(
            num_scalar_prefetch=1,
            grid=(rows // tile,),
            in_specs=[by_rows(wide), full(w_gate.shape), full(w_up.shape), by_rows(hidden)]
            + [pl.BlockSpec(memory_space=pl.ANY)] * len(others),
            out_specs=[by_rows(hidden), by_rows(hidden), by_rows(hidden), by_rows(wide)],
        ),
        out_shape=[jax.ShapeDtypeStruct((rows, hidden), LOW)] * 3
        + [jax.ShapeDtypeStruct((rows, wide), LOW)],
        compiler_params=params(),
        cost_estimate=cost(8 * rows * width * hidden, 20e6, rows * hidden),
    )(who, x, w_gate, w_up, pull, *others)


def input_kernel(grad_ref, x_ref, gain_ref, more_ref, out_ref):
    normal, rr = norm_parts(x_ref[...].astype(F32))
    grad = grad_ref[...].astype(F32)
    out_ref[...] = more_ref[...] + norm_back(grad, normal, rr, gain_ref[...])


def input_back(grad, x, gain, more):
    tokens, width = x.shape
    operands = [grad, x, gain[None], more]
    return pl.pallas_call(
        input_kernel,
        grid=(1,),
        in_specs=[full(value.shape) for value in operands],
        out_specs=full(more.shape),
        out_shape=jax.ShapeDtypeStruct((tokens, width), F32),
        compiler_params=params(),
        cost_estimate=cost(20 * tokens * width, 5e6),
    )(*operands)


def kv_back_kernel(factor, n_parts, c_ref, dkv_ref, *refs):
    parts = refs[:n_parts]
    proj_ref, gain_ref, cos_ref, sin_ref = refs[n_parts : n_parts + 4]
    grad_ref, dgain_ref = refs[-2:]
    size = proj_ref.shape[1]
    total = functools.reduce(jnp.add, [part[...].astype(F32) for part in parts], dkv_ref[...])
    grad, dgain = head_backward(
        total[:, :size] * factor, proj_ref[...], gain_ref[...], cos_ref[...], sin_ref[...]
    )
    grad_ref[:, :size] = grad.astype(LOW)
    grad_ref[:, size:] = total[:, size:].astype(LOW)
    dgain_ref[...] = dgain


def kv_back(context, dkv, parts, proj, gain, cos2, sin2, factor, others):
    block, size = proj.shape
    operands = [proj, gain[None], cos2, sin2]
    shapes = [
        jax.ShapeDtypeStruct((block, 2 * size), LOW),
        jax.ShapeDtypeStruct((1, size), F32),
    ]
    return pl.pallas_call(
        functools.partial(kv_back_kernel, factor, len(parts)),
        grid_spec=pltpu.PrefetchScalarGridSpec(
            num_scalar_prefetch=1,
            grid=(1,),
            in_specs=[pl.BlockSpec((block, 2 * size), lambda i, c: (c[0], 0))]
            + [full(part.shape) for part in parts]
            + [full(value.shape) for value in operands]
            + [pl.BlockSpec(memory_space=pl.ANY)] * len(others),
            out_specs=[full(shape.shape) for shape in shapes],
        ),
        out_shape=shapes,
        compiler_params=params(),
        cost_estimate=cost(40 * block * size, 5e6),
    )(context.astype(jnp.int32)[None], dkv, *parts, *operands, *others)


def widen_kernel(at_ref, *refs):
    out_ref = refs[-1]
    for k, ref in enumerate(refs[:-1]):

        @pl.when(pl.program_id(0) == k)
        def _():
            out_ref[...] = ref[...].astype(F32)


def widen(places, chunks):
    rows, columns = chunks[0].shape
    tiles = 2 if rows % 32 == 0 else 1
    tile = rows // tiles

    def only_at(k):
        return pl.BlockSpec(
            (tile, columns),
            lambda i, j, at: (jnp.where(i < k, 0, jnp.where(i == k, j, tiles - 1)), 0),
        )

    return pl.pallas_call(
        widen_kernel,
        grid_spec=pltpu.PrefetchScalarGridSpec(
            num_scalar_prefetch=1,
            grid=(len(chunks), tiles),
            in_specs=[only_at(k) for k in range(len(chunks))],
            out_specs=pl.BlockSpec((tile, columns), lambda i, j, at: (at[i] * tiles + j, 0)),
        ),
        out_shape=jax.ShapeDtypeStruct((len(chunks) * rows, columns), F32),
        compiler_params=params(),
        cost_estimate=cost(rows * columns, 6 * len(chunks) * rows * columns),
    )(jnp.stack(places).astype(jnp.int32), *chunks)


def sum_small(flat):
    n = lax.axis_size(ALL_AXES)
    length = flat.shape[0]
    each = -(-length // (n * 128)) * 128
    parts = jnp.pad(flat, (0, n * each - length)).reshape(n, each)
    parts = lax.all_to_all(parts, ALL_AXES, split_axis=0, concat_axis=0, tiled=True)
    own = jnp.sum(parts, axis=0, keepdims=True)
    whole = lax.all_to_all(
        jnp.broadcast_to(own, (n, each)), ALL_AXES, split_axis=0, concat_axis=0, tiled=True
    )
    return whole.reshape(-1)[:length]


def swap_dp(rows):
    return lax.ppermute(rows, "dp", [(0, 1), (1, 0)])


def swap_context(rows, s):
    n = lax.axis_size("context")
    return lax.ppermute(rows, "context", [(i, i ^ s) for i in range(n)])


def half_groups(grad):
    d, c = lax.axis_index("dp"), lax.axis_index("context")
    n = lax.axis_size("context")
    rows = grad.shape[0] // 2
    each = rows // n
    got = swap_dp(lax.dynamic_slice_in_dim(grad, (1 - d) * rows, rows))
    chunks = []
    for s in range(n):
        mine = lax.dynamic_slice_in_dim(grad, d * rows + (c ^ s) * each, each)
        other = lax.dynamic_slice_in_dim(got, (c ^ s) * each, each)
        chunks.append((mine.astype(F32) + other.astype(F32)).astype(LOW))
    return chunks


def rest_groups(chunks):
    n = lax.axis_size("context")
    d, c = lax.axis_index("dp"), lax.axis_index("context")
    total = chunks[0].astype(F32)
    for s in range(1, n):
        total += swap_context(chunks[s], s).astype(F32)
    total = total.astype(LOW)
    found = [total] + [swap_context(total, s) for s in range(1, n)]
    places = [d * n + (c ^ s) for s in range(n)] + [(1 - d) * n + (c ^ s) for s in range(n)]
    return widen(places, found + [swap_dp(part) for part in found])


def arrival_order(n):
    return [sorted(range(n), key=lambda j: (abs(j - i), j)) for i in range(n)]


def choose(index, options):
    distinct = []
    for option in options:
        if option is not None and not any(option is other for other in distinct):
            distinct.append(option)
    result = distinct[0]
    for option in distinct[1:]:
        mask = functools.reduce(
            jnp.logical_or, [index == i for i, other in enumerate(options) if other is option]
        )
        result = jnp.where(mask, option, result)
    return result


def line_gather(chunk):
    return line_steps({0: chunk}, 1, lax.axis_size("expert"))


def line_steps(found, first, stop):
    n = lax.axis_size("expert")
    found = dict(found)
    for s in range(first, stop):
        found[-s] = lax.ppermute(
            found[1 - s], "expert", [(i, i + 1) for i in range(s - 1, n - 1)]
        )
        found[s] = lax.ppermute(found[s - 1], "expert", [(i + 1, i) for i in range(n - s)])
    return found


def context_gather(rows):
    n = lax.axis_size("context")
    c = lax.axis_index("context")
    found = {0: rows}
    for s in range(1, n):
        found[s] = lax.ppermute(rows, "context", [(i, i ^ s) for i in range(n)])
    return jnp.concatenate([choose(c, [found[i ^ j] for i in range(n)]) for j in range(n)], axis=0)


def context_parts(rows):
    n = lax.axis_size("context")
    c = lax.axis_index("context")
    each = rows.shape[0] // n
    return [
        swap_context(lax.dynamic_slice_in_dim(rows, (c ^ s) * each, each).astype(LOW), s)
        for s in range(1, n)
    ]


def zero_of(*others):
    return functools.reduce(
        jnp.add,
        [
            lax.slice(other, (0,) * other.ndim, (1,) * other.ndim).reshape(()).astype(F32) * 0.0
            for other in others
        ],
    )


def after(value, *others):
    return (value.astype(F32) + zero_of(*others)).astype(value.dtype)


def on_device(
    layer_input,
    grad_output,
    attn_gain,
    query_weight,
    key_weight,
    value_weight,
    q_gain,
    k_gain,
    output_weight,
    mlp_gain,
    router,
    w_gate,
    w_up,
    w_down,
    routes,
    half_order,
):
    n_context = lax.axis_size("context")
    n_expert = lax.axis_size("expert")
    n_groups = lax.axis_size(GROUP_AXES)
    tok_dev, width = layer_input.shape[1:]
    size = q_gain.shape[0]
    kv_total = key_weight.shape[1] * n_expert
    group_dev = n_expert // (kv_total // size)
    kv_index = lax.axis_index("expert") // group_dev
    block = tok_dev * n_expert
    seq = block * n_context
    half = block // 2
    experts = router.shape[1]
    exp_dev = w_gate.shape[0]
    top = routes.shape[2]
    capacity = max(2, (tok_dev * top * 9 + 8 * experts - 1) // (8 * experts))
    scale = size ** (-0.5)

    seq_rows = jnp.arange(seq, dtype=jnp.int32)
    context = lax.axis_index("context")
    own_halves = lax.dynamic_slice_in_dim(half_order, 2 * context, 2)
    own_pos = (own_halves[:, None] * half + jnp.arange(half, dtype=jnp.int32)[None]).reshape(-1)
    per_half = half // TILE
    tile_pos = (half_order[:, None] * per_half + jnp.arange(per_half, dtype=jnp.int32)).reshape(-1)
    kidx = jnp.sum(
        (tile_pos[None, :] == jnp.arange(seq // TILE, dtype=jnp.int32)[:, None])
        * jnp.arange(seq // TILE, dtype=jnp.int32)[None, :],
        axis=1,
    ).astype(jnp.int32)
    qpos = lax.dynamic_slice_in_dim(tile_pos, context * (block // TILE), block // TILE)
    entry = jnp.arange(size)
    freq = jnp.power(THETA, -(2 * (entry % (size // 2))).astype(F32) / size)
    angles = own_pos.astype(F32)[:, None] * freq[None, :]
    cos2 = jnp.cos(angles)
    sin2 = jnp.sin(angles) * jnp.where(entry < size // 2, -1.0, 1.0)[None, :]

    place = lax.axis_index("expert")
    place_1 = place.astype(jnp.int32)[None]
    lanes = -(-2 * experts // 128) * 128
    mask = jnp.any(
        routes[0][:, :, None] == jnp.arange(lanes, dtype=jnp.int32)[None, None, :], axis=1
    )
    mask_wide = mask.astype(F32)
    router_wide = jnp.pad(router, ((0, 0), (0, lanes - experts)))

    x_low = layer_input[0]
    x_normal, _ = norm_parts(x_low.astype(F32))
    normed_found = line_gather((x_normal * attn_gain).astype(LOW))
    grad_low = grad_output[0]
    last = n_expert - 1
    grad_wide = after(
        jnp.concatenate([grad_low, mask.astype(LOW)], axis=1),
        normed_found[last],
        normed_found[-last],
    )
    grad_col = lax.all_gather(grad_wide, "expert", axis=0, tiled=True)
    if group_dev == 1:
        kv_weights = jnp.concatenate([key_weight, value_weight], axis=1)
    else:
        key_whole = lax.all_gather(key_weight, "expert", axis=1, tiled=True)
        value_whole = lax.all_gather(value_weight, "expert", axis=1, tiled=True)
        kv_weights = jnp.concatenate(
            [
                lax.dynamic_slice_in_dim(key_whole, kv_index * size, size, 1),
                lax.dynamic_slice_in_dim(value_whole, kv_index * size, size, 1),
            ],
            axis=1,
        )
    normed_rows, own_kv, key_proj = project_keys(
        place_1, normed_found, kv_weights, k_gain, cos2, sin2, scale * LOG2E, []
    )
    kv_whole = context_gather(own_kv)
    queries, query_proj = project_queries(normed_rows, query_weight, q_gain, cos2, sin2)

    n_half = n_expert // 2
    rows_half = n_groups * n_half * capacity
    order_here = jnp.asarray(arrival_order(n_expert), jnp.int32)[place]
    turn_here = jnp.sum(
        (order_here[:, None] == jnp.arange(n_expert, dtype=jnp.int32)[None, :])
        * jnp.arange(n_expert, dtype=jnp.int32)[:, None],
        axis=0,
    ).astype(jnp.int32)
    meta = jnp.concatenate([place_1, turn_here, order_here])
    grad_sent, spreads, back_table = make_tables(
        meta, grad_col, width, n_groups, n_half, capacity, [router_wide, mask_wide]
    )

    def swap_plane(rows):
        wide = rows.shape[1]
        rows = lax.all_to_all(
            rows.reshape(n_groups, n_half * capacity, wide),
            GROUP_AXES,
            split_axis=0,
            concat_axis=0,
            tiled=True,
        )
        return rows.reshape(rows_half, wide)

    attended, inverse = attend(qpos, kidx, queries, kv_whole, [])
    attn_part = (dot_nn(attended, output_weight) + zero_of(grad_col)).astype(LOW)
    attn_rows = lax.psum_scatter(attn_part, "expert", scatter_dimension=0, tiled=True)

    grad_x = [swap_plane(rows) for rows in grad_sent]
    act_pull = [dot_nt(rows, w_down[0]) for rows in grad_x]

    hidden, mixed, probs = route_rows(
        x_low, attn_rows, mlp_gain, router_wide, mask_wide, experts, [grad_x[0]]
    )

    who = (lax.axis_index(ALL_AXES) * exp_dev).astype(jnp.int32)[None]
    mixed_found = line_gather(mixed)
    near = spread_rows(place_1, spreads[0], mixed_found, range(n_half), [grad_x[1]])
    x_near = swap_plane(near)
    worked_near = run_expert(who, x_near, w_gate[0], w_up[0], act_pull[0], experts, [])
    far = spread_rows(
        place_1, spreads[1], mixed_found, range(n_half, n_expert), [x_near]
    )
    x_far = swap_plane(far)
    worked_far = run_expert(who, x_far, w_gate[0], w_up[0], act_pull[1], experts, [])
    xs = [x_near, x_far]
    acts, gate_lows, up_lows, copies = (list(pair) for pair in zip(worked_near, worked_far))
    back_far = swap_plane(copies[1])
    back_near = swap_plane(copies[0])
    join = lambda parts: jnp.concatenate(parts, axis=0)
    x_all = join([x[:, :width] for x in xs])
    grad_w_gate = dot_tn(x_all, join(gate_lows))
    grad_w_up = dot_tn(x_all, join(up_lows))
    grad_w_down = dot_tn(join(acts), join(grad_x))
    copies_col = combine_rows(back_table, [back_near, back_far], [grad_w_gate, grad_w_up])
    copies_sum = lax.psum_scatter(copies_col, "expert", scatter_dimension=0, tiled=True)

    returned = [(dot_nn(act, w_down[0]) + zero_of(back_near)).astype(LOW) for act in acts]
    returned_near = swap_plane(returned[0])

    grad_hidden, grad_hidden_low, grad_mlp_gain, grad_router = route_back(
        copies_sum,
        grad_low,
        hidden,
        mlp_gain,
        router_wide,
        mask_wide,
        probs,
        experts,
        [returned_near, grad_w_down],
    )

    returned_far = swap_plane(returned[1])
    grad_attn = lax.all_gather(grad_hidden_low, "expert", axis=0, tiled=True)
    grad_o, centre = grad_attended(
        grad_attn, output_weight, attended, inverse, [returned_far]
    )
    combined = combine_rows(back_table, [returned_near, returned_far], [grad_attn])
    output_rows = hidden + lax.psum_scatter(
        combined, "expert", scatter_dimension=0, tiled=True
    ).astype(F32)
    grad_w_out = lax.psum(dot_tn(attended, grad_attn).astype(LOW), GROUP_AXES)
    grad_kv, grad_q, grad_q_gain = attend_back(
        qpos,
        kidx,
        queries,
        grad_o,
        centre,
        kv_whole,
        query_proj,
        q_gain,
        cos2,
        sin2,
        [combined],
    )
    kv_parts = context_parts(grad_kv)
    half_w_query = half_groups(dot_tn(normed_rows, grad_q).astype(LOW))

    kv_grads, grad_k_gain = kv_back(
        context, grad_kv, kv_parts, key_proj, k_gain, cos2, sin2, scale, [output_rows, grad_w_out]
    )
    grad_normed = dot_nt(grad_q, query_weight) + dot_nt(kv_grads, kv_weights)
    grad_attn_gain = jnp.sum(grad_normed * normed_rows.astype(F32), axis=0) / attn_gain
    grad_normed = lax.psum_scatter(
        grad_normed.astype(LOW), "expert", scatter_dimension=0, tiled=True
    )
    grad_input = input_back(grad_normed, x_low, attn_gain, grad_hidden)

    grad_w_out = grad_w_out.astype(F32)
    grad_w_query = rest_groups(half_w_query)
    grad_w_kv = dot_tn(normed_rows, kv_grads).astype(LOW)
    if group_dev == 1:
        grad_w_kv = lax.psum(
            (grad_w_kv.astype(F32) + zero_of(grad_normed)).astype(LOW), GROUP_AXES
        ).astype(F32)
        grad_w_key, grad_w_value = grad_w_kv[:, :size], grad_w_kv[:, size:]
    else:
        blank = jnp.zeros((width, kv_total), LOW)
        pieces = []
        for part in (grad_w_kv[:, :size], grad_w_kv[:, size:]):
            padded = lax.dynamic_update_slice(blank, part, (0, kv_index * size))
            pieces.append(lax.psum_scatter(padded, "expert", scatter_dimension=1, tiled=True))
        grad_w_key, grad_w_value = (lax.psum(piece, GROUP_AXES).astype(F32) for piece in pieces)

    small = [
        grad_attn_gain,
        grad_mlp_gain[0],
        grad_q_gain[0],
        grad_k_gain[0],
        grad_router[:experts].reshape(-1),
    ]
    summed = sum_small(jnp.concatenate(small))
    pieces = []
    offset = 0
    for part in small:
        pieces.append(summed[offset : offset + part.shape[0]])
        offset += part.shape[0]
    grad_attn_gain, grad_mlp_gain, grad_q_gain, grad_k_gain, grad_router = pieces
    return (
        output_rows.astype(LOW)[None],
        grad_input[None],
        grad_attn_gain,
        grad_w_query,
        grad_w_key,
        grad_w_value,
        grad_q_gain,
        grad_k_gain,
        grad_w_out,
        grad_mlp_gain,
        grad_router.reshape(experts, width).T,
        grad_w_gate[None],
        grad_w_up[None],
        grad_w_down[None],
    )


def solution(mesh):
    rows = P("dp", ("context", "expert"), None)
    expert = P(ALL_AXES, None, None)
    columns = P(None, "expert")
    in_specs = (
        rows,
        rows,
        P(),
        columns,
        columns,
        columns,
        P(),
        P(),
        P("expert", None),
        P(),
        P(),
        expert,
        expert,
        expert,
        rows,
        P(),
    )
    out_specs = (
        rows,
        rows,
        P(),
        columns,
        columns,
        columns,
        P(),
        P(),
        P("expert", None),
        P(),
        P(),
        expert,
        expert,
        expert,
    )
    return jax.shard_map(
        on_device, mesh=mesh, in_specs=in_specs, out_specs=out_specs, check_vma=False
    )
```

```python
import functools
import math

import jax
import jax.numpy as jnp
from jax import lax
from jax.experimental import pallas as pl
from jax.experimental.pallas import tpu as pltpu
from jax.sharding import PartitionSpec as P

EPS = 1e-06
THETA = 1000000.0
TILE = 256
VMEM_BYTES = 56 * 1024 * 1024
LOG2E = math.log2(math.e)
LOW = jnp.bfloat16
F32 = jnp.float32
ALL_AXES = ("dp", "context", "expert")
GROUP_AXES = ("dp", "context")


def dot_nn(a, b):
    return lax.dot_general(a, b, (((1,), (0,)), ((), ())), preferred_element_type=F32)


def dot_nt(a, b):
    return lax.dot_general(a, b, (((1,), (1,)), ((), ())), preferred_element_type=F32)


def dot_tn(a, b):
    return lax.dot_general(a, b, (((0,), (0,)), ((), ())), preferred_element_type=F32)


def params(**more):
    return pltpu.CompilerParams(vmem_limit_bytes=VMEM_BYTES, **more)


def cost(flops, nbytes, exps=0):
    return pl.CostEstimate(flops=int(flops), bytes_accessed=int(nbytes), transcendentals=int(exps))


def head_forward(u, gain, cos2, sin2):
    rr = lax.rsqrt(jnp.mean(u * u, axis=-1, keepdims=True) + EPS)
    y = u * rr * gain
    return y * cos2 + pltpu.roll(y, 64, 1) * sin2


def head_backward(gy, u, gain, cos2, sin2):
    g = gy * cos2 - pltpu.roll(gy, 64, 1) * sin2
    rr = lax.rsqrt(jnp.mean(u * u, axis=-1, keepdims=True) + EPS)
    n = u * rr
    gn = g * gain
    grad = rr * (gn - n * jnp.mean(gn * n, axis=-1, keepdims=True))
    return grad, jnp.sum(g * n, axis=0, keepdims=True)


def query_kernel(x_ref, w_ref, gain_ref, cos_ref, sin_ref, rot_ref, proj_ref):
    tiles, heads, rows, size = rot_ref.shape
    acc = dot_nn(x_ref[...], w_ref[...])
    for h in range(heads):
        u = acc[:, h * size : (h + 1) * size]
        rot = head_forward(u, gain_ref[...], cos_ref[...], sin_ref[...])
        proj_ref[:, h] = u.reshape(tiles, rows, size)
        rot_ref[:, h] = rot.astype(LOW).reshape(tiles, rows, size)


def project_queries(normed, weight, gain, cos2, sin2):
    block, width = normed.shape
    size = cos2.shape[1]
    heads = weight.shape[1] // size
    tiles = block // TILE
    whole = lambda i: (0, 0)
    per = lambda i: (0, i, 0, 0)
    shape = (tiles, heads, TILE, size)
    return pl.pallas_call(
        query_kernel,
        grid=(heads // 2,),
        in_specs=[
            pl.BlockSpec((block, width), whole),
            pl.BlockSpec((width, 2 * size), lambda i: (0, i)),
            pl.BlockSpec((1, size), whole),
            pl.BlockSpec((block, size), whole),
            pl.BlockSpec((block, size), whole),
        ],
        out_specs=[pl.BlockSpec((tiles, 2, TILE, size), per)] * 2,
        out_shape=[jax.ShapeDtypeStruct(shape, LOW), jax.ShapeDtypeStruct(shape, F32)],
        compiler_params=params(),
        cost_estimate=cost(2 * block * width * heads * size, 12e6),
    )(normed, weight, gain[None], cos2, sin2)


def put_in_order(place, refs, out_ref):
    n = (len(refs) + 1) // 2
    rows = refs[0].shape[0]
    for distance in range(1 - n, n):
        ref = refs[distance + n - 1]
        at = place + distance

        @pl.when(jnp.logical_and(at >= 0, at < n))
        def _():
            out_ref[pl.ds(pl.multiple_of(at * rows, rows), rows), :] = ref[...]


def chunk_list(found):
    n = (len(found) + 1) // 2
    return [found[distance] for distance in range(1 - n, n)]


def key_kernel(factor, n_chunks, place_ref, *refs):
    w_ref, gain_ref, cos_ref, sin_ref, g_ref, mask_ref = refs[n_chunks:-4]
    rows_ref, kv_ref, proj_ref, wide_ref = refs[-4:]
    size = proj_ref.shape[1]
    width = g_ref.shape[1]
    put_in_order(place_ref[0], refs[:n_chunks], rows_ref)
    wide_ref[:, :width] = g_ref[...]
    wide_ref[:, width:] = mask_ref[...].astype(LOW)
    acc = dot_nn(rows_ref[...], w_ref[...])
    u = acc[:, :size]
    rot = head_forward(u, gain_ref[...], cos_ref[...], sin_ref[...])
    proj_ref[...] = u
    kv_ref[:, :size] = (rot * factor).astype(LOW)
    kv_ref[:, size:] = acc[:, size:].astype(LOW)


def full(shape):
    return pl.BlockSpec(shape, lambda *_: (0,) * len(shape))


def project_keys(place, found, weight, gain, cos2, sin2, factor, g, mask):
    chunks = chunk_list(found)
    rows, width = chunks[0].shape
    block, size = cos2.shape
    operands = [*chunks, weight, gain[None], cos2, sin2, g, mask]
    shapes = [
        jax.ShapeDtypeStruct((block, width), LOW),
        jax.ShapeDtypeStruct((block, 2 * size), LOW),
        jax.ShapeDtypeStruct((block, size), F32),
        jax.ShapeDtypeStruct((rows, width + mask.shape[1]), LOW),
    ]
    return pl.pallas_call(
        functools.partial(key_kernel, factor, len(chunks)),
        grid_spec=pltpu.PrefetchScalarGridSpec(
            num_scalar_prefetch=1,
            grid=(1,),
            in_specs=[full(x.shape) for x in operands],
            out_specs=[full(x.shape) for x in shapes],
        ),
        out_shape=shapes,
        compiler_params=params(),
        cost_estimate=cost(4 * block * width * size, 8e6),
    )(place, *operands)


def attend_kernel(qpos_ref, kidx_ref, q_ref, kv_ref, *rest):
    out_ref, inv_ref, acc_ref = rest[-3:]
    heads, rows, size = q_ref.shape[1:]
    last = qpos_ref[pl.program_id(0)]
    acc_ref[...] = jnp.zeros_like(acc_ref)
    ones = jnp.ones((rows, size), LOW)

    def step(place, masked):
        start = pl.multiple_of(kidx_ref[place] * rows, rows)
        keys = kv_ref[pl.ds(start, rows), :size]
        values = jnp.concatenate([kv_ref[pl.ds(start, rows), size:], ones], axis=1)
        for h in range(heads):
            e = jnp.exp2(dot_nt(q_ref[0, h], keys))
            if masked:
                qi = lax.broadcasted_iota(jnp.int32, e.shape, 0)
                ki = lax.broadcasted_iota(jnp.int32, e.shape, 1)
                e = jnp.where(ki <= qi, e, 0.0)
            acc_ref[h] += dot_nn(e.astype(LOW), values)

    lax.fori_loop(0, last, lambda p, c: (step(p, False), c)[1], 0)
    step(last, True)
    for h in range(heads):
        inv = 1.0 / acc_ref[h, :, size:]
        inv_ref[0, h] = inv
        out_ref[:, h * size : (h + 1) * size] = (acc_ref[h, :, :size] * inv).astype(LOW)


def attend(qpos, kidx, queries, kv, others):
    tiles, heads, rows, size = queries.shape
    seq = kv.shape[0]
    return pl.pallas_call(
        attend_kernel,
        grid_spec=pltpu.PrefetchScalarGridSpec(
            num_scalar_prefetch=2,
            grid=(tiles,),
            in_specs=[
                pl.BlockSpec((1, heads, rows, size), lambda i, a, b: (i, 0, 0, 0)),
                pl.BlockSpec((seq, 2 * size), lambda i, a, b: (0, 0)),
            ]
            + [pl.BlockSpec(memory_space=pl.ANY)] * len(others),
            out_specs=[
                pl.BlockSpec((rows, heads * size), lambda i, a, b: (i, 0)),
                pl.BlockSpec((1, heads, rows, size), lambda i, a, b: (i, 0, 0, 0)),
            ],
            scratch_shapes=[pltpu.VMEM((heads, rows, 2 * size), F32)],
        ),
        out_shape=[
            jax.ShapeDtypeStruct((tiles * rows, heads * size), LOW),
            jax.ShapeDtypeStruct((tiles, heads, rows, size), F32),
        ],
        compiler_params=params(),
        cost_estimate=cost(
            6 * tiles * rows * heads * seq * size, 8e6, tiles * rows * heads * seq
        ),
    )(qpos, kidx, queries, kv, *others)


def grad_out_kernel(rows_ref, w_ref, o_ref, inv_ref, *rest):
    do_ref, centre_ref = rest[-2:]
    tiles, heads, rows, size = do_ref.shape
    acc = dot_nt(rows_ref[...], w_ref[...])
    for t in range(tiles):
        for h in range(heads):
            part = slice(t * rows, (t + 1) * rows), slice(h * size, (h + 1) * size)
            low = (acc[part] * inv_ref[t, h]).astype(LOW)
            do_ref[t, h] = low
            product = low.astype(F32) * o_ref[part].astype(F32)
            centre = jnp.sum(jnp.transpose(product), axis=0, keepdims=True)
            centre_ref[t, h] = jnp.broadcast_to(centre, (8, rows))


def grad_attended(grad_rows, weight, attended, inverse, others):
    tiles, heads, rows, size = inverse.shape
    block, width = grad_rows.shape
    return pl.pallas_call(
        grad_out_kernel,
        grid=(heads // 2,),
        in_specs=[
            pl.BlockSpec((block, width), lambda i: (0, 0)),
            pl.BlockSpec((2 * size, width), lambda i: (i, 0)),
            pl.BlockSpec((block, 2 * size), lambda i: (0, i)),
            pl.BlockSpec((tiles, 2, rows, size), lambda i: (0, i, 0, 0)),
        ]
        + [pl.BlockSpec(memory_space=pl.ANY)] * len(others),
        out_specs=[
            pl.BlockSpec((tiles, 2, rows, size), lambda i: (0, i, 0, 0)),
            pl.BlockSpec((tiles, 2, 8, rows), lambda i: (0, i, 0, 0)),
        ],
        out_shape=[
            jax.ShapeDtypeStruct((tiles, heads, rows, size), LOW),
            jax.ShapeDtypeStruct((tiles, heads, 8, rows), F32),
        ],
        compiler_params=params(),
        cost_estimate=cost(2 * block * width * heads * size, 12e6),
    )(grad_rows, weight, attended, inverse, *others)


def attend_back_kernel(
    qpos_ref,
    kidx_ref,
    q_ref,
    do_ref,
    centre_ref,
    kv_ref,
    proj_ref,
    gain_ref,
    cos_ref,
    sin_ref,
    *rest,
):
    dkv_ref, dq_ref, dgain_ref, acc_ref = rest[-4:]
    heads, rows, size = q_ref.shape[1:]
    last = qpos_ref[pl.program_id(0)]

    @pl.when(pl.program_id(0) == 0)
    def _():
        dkv_ref[...] = jnp.zeros_like(dkv_ref)
        dgain_ref[...] = jnp.zeros_like(dgain_ref)

    acc_ref[...] = jnp.zeros_like(acc_ref)

    def step(place, masked):
        start = pl.multiple_of(kidx_ref[place] * rows, rows)
        keys = kv_ref[pl.ds(start, rows), :size]
        values = kv_ref[pl.ds(start, rows), size:]
        dk = dkv_ref[pl.ds(start, rows), :size]
        dv = dkv_ref[pl.ds(start, rows), size:]
        for h in range(heads):
            query, grad = q_ref[0, h], do_ref[0, h]
            e = jnp.exp2(dot_nt(keys, query))
            if masked:
                ki = lax.broadcasted_iota(jnp.int32, e.shape, 0)
                qi = lax.broadcasted_iota(jnp.int32, e.shape, 1)
                e = jnp.where(ki <= qi, e, 0.0)
            ds = (e * (dot_nt(values, grad) - centre_ref[0, h, 0:1])).astype(LOW)
            dv += dot_nn(e.astype(LOW), grad)
            dk += dot_nn(ds, query)
            acc_ref[h] += dot_tn(ds, keys)
        dkv_ref[pl.ds(start, rows), :size] = dk
        dkv_ref[pl.ds(start, rows), size:] = dv

    lax.fori_loop(0, last, lambda p, c: (step(p, False), c)[1], 0)
    step(last, True)
    total = jnp.zeros((1, size), F32)
    for h in range(heads):
        grad, gain_part = head_backward(
            acc_ref[h] * (1.0 / LOG2E), proj_ref[0, h], gain_ref[...], cos_ref[...], sin_ref[...]
        )
        dq_ref[:, h * size : (h + 1) * size] = grad.astype(LOW)
        total += gain_part
    dgain_ref[...] += total


def attend_back(qpos, kidx, queries, grads, centre, kv, proj, gain, cos2, sin2, part, others):
    tiles, heads, rows, size = queries.shape
    heads = heads // 2
    seq = kv.shape[0]
    per = pl.BlockSpec((1, heads, rows, size), lambda i, a, b: (i, part, 0, 0))
    flat = lambda i, a, b: (0, 0)
    rowwise = lambda i, a, b: (i, 0)
    return pl.pallas_call(
        attend_back_kernel,
        grid_spec=pltpu.PrefetchScalarGridSpec(
            num_scalar_prefetch=2,
            grid=(tiles,),
            in_specs=[
                per,
                per,
                pl.BlockSpec((1, heads, 8, rows), lambda i, a, b: (i, part, 0, 0)),
                pl.BlockSpec((seq, 2 * size), flat),
                per,
                pl.BlockSpec((1, size), flat),
                pl.BlockSpec((rows, size), rowwise),
                pl.BlockSpec((rows, size), rowwise),
            ]
            + [pl.BlockSpec(memory_space=pl.ANY)] * len(others),
            out_specs=[
                pl.BlockSpec((seq, 2 * size), flat),
                pl.BlockSpec((rows, heads * size), rowwise),
                pl.BlockSpec((1, size), flat),
            ],
            scratch_shapes=[pltpu.VMEM((heads, rows, size), F32)],
        ),
        out_shape=[
            jax.ShapeDtypeStruct((seq, 2 * size), F32),
            jax.ShapeDtypeStruct((tiles * rows, heads * size), LOW),
            jax.ShapeDtypeStruct((1, size), F32),
        ],
        compiler_params=params(),
        cost_estimate=cost(
            15 * tiles * rows * heads * seq * size, 12e6, tiles * rows * heads * seq
        ),
    )(qpos, kidx, queries, grads, centre, kv, proj, gain[None], cos2, sin2, *others)


def token_kernel(a_ref, b_ref, *rest):
    rest[-1][...] = dot_tn(a_ref[...], b_ref[...]).astype(LOW)


def token_dot(a, b, others):
    block, rows = a.shape
    columns = b.shape[1]
    tile = min(rows, 512)
    return pl.pallas_call(
        token_kernel,
        grid=(rows // tile,),
        in_specs=[
            pl.BlockSpec((block, tile), lambda i: (0, i)),
            pl.BlockSpec((block, columns), lambda i: (0, 0)),
        ]
        + [pl.BlockSpec(memory_space=pl.ANY)] * len(others),
        out_specs=pl.BlockSpec((tile, columns), lambda i: (i, 0)),
        out_shape=jax.ShapeDtypeStruct((rows, columns), LOW),
        compiler_params=params(),
        cost_estimate=cost(2 * block * rows * columns, 6e6),
    )(a, b, *others)


def split_low(value):
    high = value.astype(LOW)
    return high, (value - high.astype(F32)).astype(LOW)


def norm_parts(rows):
    rr = lax.rsqrt(jnp.mean(rows * rows, axis=-1, keepdims=True) + EPS)
    return rows * rr, rr


def norm_back(grad, normal, rr, gain):
    weighted = grad * gain
    return rr * (weighted - normal * jnp.mean(weighted * normal, axis=-1, keepdims=True))


def add_all(refs):
    return functools.reduce(jnp.add, [ref[...].astype(F32) for ref in refs])


def router_kernel(experts, *refs):
    x_ref, attn_ref, gain_ref, router_ref, mask_ref = refs[:5]
    hidden_ref, mixed_ref, probs_ref = refs[-3:]
    width = x_ref.shape[1]
    lanes = router_ref.shape[1]
    hidden = add_all([x_ref, attn_ref])
    hidden_ref[...] = hidden
    mixed = (norm_parts(hidden)[0] * gain_ref[...]).astype(LOW)
    mixed_ref[:, :width] = mixed
    logits = dot_nn(mixed, router_ref[...])
    lane = lax.broadcasted_iota(jnp.int32, logits.shape, 1)
    logits = jnp.where(lane < experts, logits, -1e30)
    weights = jnp.exp(logits - jnp.max(logits, axis=1, keepdims=True))
    probs = weights / jnp.sum(weights, axis=1, keepdims=True)
    probs_ref[...] = probs
    chosen = probs * mask_ref[...]
    high, low = split_low(chosen / jnp.sum(chosen, axis=1, keepdims=True))
    both = high.astype(F32) + pltpu.roll(low.astype(F32), experts, 1)
    mixed_ref[:, width:] = both.astype(LOW)


def route_rows(x, attn, gain, router, mask, experts, others):
    tokens, width = x.shape
    lanes = router.shape[1]
    operands = [x, attn, gain[None], router, mask]
    shapes = [
        jax.ShapeDtypeStruct((tokens, width), F32),
        jax.ShapeDtypeStruct((tokens, width + lanes), LOW),
        jax.ShapeDtypeStruct((tokens, lanes), F32),
    ]
    return pl.pallas_call(
        functools.partial(router_kernel, experts),
        grid=(1,),
        in_specs=[full(value.shape) for value in operands]
        + [pl.BlockSpec(memory_space=pl.ANY)] * len(others),
        out_specs=[full(shape.shape) for shape in shapes],
        out_shape=shapes,
        compiler_params=params(),
        cost_estimate=cost(2 * tokens * width * lanes, 5e6),
    )(*operands, *others)


def table_kernel(capacity, n_half, meta_ref, col_ref, *rest):
    rows_ref, near_ref, far_ref, near_back_ref, far_back_ref, slots_ref = rest[-6:]
    block = col_ref.shape[0]
    rows, width = rows_ref.shape
    n = 2 * n_half
    tokens = block // n
    cap_half = n_half * capacity
    groups = rows // (2 * cap_half)
    mask = col_ref[:, width:]
    lanes = mask.shape[1]
    padded = -(-groups // 16) * 16
    group = lax.broadcasted_iota(jnp.int32, (padded, lanes), 0)
    lane = lax.broadcasted_iota(jnp.int32, (padded, lanes), 1)
    wanted = jnp.logical_and(lane == group * n + meta_ref[0], group < groups)
    hits = dot_nt(jnp.where(wanted, 1.0, 0.0).astype(LOW), mask)
    before = lax.broadcasted_iota(jnp.int32, (tokens, tokens), 0)
    after_it = lax.broadcasted_iota(jnp.int32, (tokens, tokens), 1)
    earlier = jnp.where(before < after_it, 1.0, 0.0).astype(LOW)
    for z in range(n):
        hit = hits[:, z * tokens : (z + 1) * tokens]
        rank = dot_nn(hit.astype(LOW), earlier)
        turn = (meta_ref[1 + z] * capacity).astype(F32)
        slot = jnp.where(hit > 0.5, rank + turn, -1.0)
        slots_ref[:, z * tokens : (z + 1) * tokens] = slot[:groups]

    def one_hot(slots, count, first):
        slot = lax.broadcasted_iota(jnp.int32, (groups, count, slots.shape[1]), 1).astype(F32)
        same = slots[:, None, :] == slot + float(first)
        return jnp.where(same, 1.0, 0.0).reshape(groups * count, slots.shape[1])

    spread = one_hot(slots_ref[...], 2 * cap_half, 0).astype(LOW)
    rows_ref[...] = dot_nn(spread, col_ref[:, :width]).astype(LOW)
    for part, (to_ref, back_ref) in enumerate([(near_ref, near_back_ref), (far_ref, far_back_ref)]):
        pieces = []
        for k in range(n_half):
            start = pl.multiple_of(meta_ref[1 + n + part * n_half + k] * tokens, tokens)
            pieces.append(slots_ref[:, pl.ds(start, tokens)])
        spread = one_hot(jnp.concatenate(pieces, axis=1), cap_half, part * cap_half)
        to_ref[...] = spread.astype(LOW)
        back_ref[...] = jnp.transpose(spread).astype(LOW)


def make_tables(meta, col, width, groups, n_half, capacity, others):
    block = col.shape[0]
    rows = groups * n_half * capacity
    shapes = (
        [jax.ShapeDtypeStruct((2 * rows, width), LOW)]
        + [jax.ShapeDtypeStruct((rows, block // 2), LOW)] * 2
        + [jax.ShapeDtypeStruct((block // 2, rows), LOW)] * 2
    )
    outs = pl.pallas_call(
        functools.partial(table_kernel, capacity, n_half),
        grid_spec=pltpu.PrefetchScalarGridSpec(
            num_scalar_prefetch=1,
            grid=(1,),
            in_specs=[full(col.shape)] + [pl.BlockSpec(memory_space=pl.ANY)] * len(others),
            out_specs=[full(shape.shape) for shape in shapes],
            scratch_shapes=[pltpu.VMEM((groups, block), F32)],
        ),
        out_shape=shapes,
        compiler_params=params(),
        cost_estimate=cost(4 * rows * block * width, 12e6),
    )(meta, col, *others)
    return outs[0], outs[1:3], outs[3:]


def spread_kernel(choices, place_ref, spread_ref, *refs):
    out_ref, rows_ref = refs[-2:]
    for k, by_place in enumerate(choices):
        for which in sorted(set(by_place)):
            hit = functools.reduce(
                jnp.logical_or,
                [place_ref[0] == i for i, other in enumerate(by_place) if other == which],
            )

            @pl.when(hit)
            def _():
                tokens = refs[which].shape[0]
                rows_ref[k * tokens : (k + 1) * tokens] = refs[which][...]

    out_ref[...] = dot_nn(spread_ref[...], rows_ref[...]).astype(LOW)


def spread_rows(place, spread, found, turns, others):
    n = lax.axis_size("expert")
    order = arrival_order(n)
    distances = sorted({order[i][turn] - i for i in range(n) for turn in turns})
    choices = [[distances.index(order[i][turn] - i) for i in range(n)] for turn in turns]
    chunks = [found[distance] for distance in distances]
    tokens, wide = chunks[0].shape
    rows = spread.shape[0]
    return pl.pallas_call(
        functools.partial(spread_kernel, choices),
        grid_spec=pltpu.PrefetchScalarGridSpec(
            num_scalar_prefetch=1,
            grid=(1,),
            in_specs=[full(spread.shape)]
            + [full(chunk.shape) for chunk in chunks]
            + [pl.BlockSpec(memory_space=pl.ANY)] * len(others),
            out_specs=full((rows, wide)),
            scratch_shapes=[pltpu.VMEM((len(turns) * tokens, wide), LOW)],
        ),
        out_shape=jax.ShapeDtypeStruct((rows, wide), LOW),
        compiler_params=params(),
        cost_estimate=cost(2 * rows * len(turns) * tokens * wide, 5e6),
    )(place, spread, *chunks, *others)


def router_back_kernel(experts, *refs):
    sum_ref, g_ref, hidden_ref, gain_ref, router_ref, mask_ref, probs_ref = refs[:7]
    grad_ref, low_ref, dgain_ref, drouter_ref = refs[-4:]
    width = g_ref.shape[1]
    lanes = router_ref.shape[1]
    total = sum_ref[...].astype(F32)
    table = total[:, width:]
    mask, probs = mask_ref[...], probs_ref[...]
    grad_gates = (table + pltpu.roll(table, lanes - experts, 1)) * mask
    chosen = probs * mask
    chosen_sum = jnp.sum(chosen, axis=1, keepdims=True)
    mean = jnp.sum(grad_gates * (chosen / chosen_sum), axis=1, keepdims=True)
    centred = mask * (grad_gates - mean) / chosen_sum
    grad_logits = probs * (centred - jnp.sum(centred * chosen, axis=1, keepdims=True))
    high, low = split_low(grad_logits)
    router = router_ref[...]
    grad = total[:, :width] + dot_nt(high, router) + dot_nt(low, router)
    normal, rr = norm_parts(hidden_ref[...])
    mixed = (normal * gain_ref[...]).astype(LOW)
    drouter_ref[...] = dot_tn(high, mixed) + dot_tn(low, mixed)
    dgain_ref[...] = jnp.sum(grad * normal, axis=0, keepdims=True)
    grad_hidden = g_ref[...].astype(F32) + norm_back(grad, normal, rr, gain_ref[...])
    grad_ref[...] = grad_hidden
    low_ref[...] = grad_hidden.astype(LOW)


def route_back(summed, g, hidden, gain, router, mask, probs, experts, others):
    tokens, width = g.shape
    lanes = router.shape[1]
    operands = [summed, g, hidden, gain[None], router, mask, probs]
    shapes = [
        jax.ShapeDtypeStruct((tokens, width), F32),
        jax.ShapeDtypeStruct((tokens, width), LOW),
        jax.ShapeDtypeStruct((1, width), F32),
        jax.ShapeDtypeStruct((lanes, width), F32),
    ]
    return pl.pallas_call(
        functools.partial(router_back_kernel, experts),
        grid=(1,),
        in_specs=[full(value.shape) for value in operands]
        + [pl.BlockSpec(memory_space=pl.ANY)] * len(others),
        out_specs=[full(shape.shape) for shape in shapes],
        out_shape=shapes,
        compiler_params=params(),
        cost_estimate=cost(8 * tokens * width * lanes, 8e6),
    )(*operands, *others)


def combine_kernel(n_half, meta_ref, near_table_ref, far_table_ref, near_ref, far_ref, *rest):
    del meta_ref
    turn = pl.program_id(0)

    @pl.when(turn < n_half)
    def _():
        rest[-1][...] = dot_nn(near_table_ref[...], near_ref[...]).astype(LOW)

    @pl.when(turn >= n_half)
    def _():
        rest[-1][...] = dot_nn(far_table_ref[...], far_ref[...]).astype(LOW)


def combine_rows(meta, tables, rows, n_half, others):
    tokens = tables[0].shape[0] // n_half
    slots, wide = rows[0].shape
    n = 2 * n_half
    return pl.pallas_call(
        functools.partial(combine_kernel, n_half),
        grid_spec=pltpu.PrefetchScalarGridSpec(
            num_scalar_prefetch=1,
            grid=(n,),
            in_specs=[
                pl.BlockSpec((tokens, slots), lambda i, m: (jnp.minimum(i, n_half - 1), 0)),
                pl.BlockSpec((tokens, slots), lambda i, m: (jnp.maximum(i - n_half, 0), 0)),
            ]
            + [full(value.shape) for value in rows]
            + [pl.BlockSpec(memory_space=pl.ANY)] * len(others),
            out_specs=pl.BlockSpec((tokens, wide), lambda i, m: (m[1 + n + i], 0)),
        ),
        out_shape=jax.ShapeDtypeStruct((n * tokens, wide), LOW),
        compiler_params=params(),
        cost_estimate=cost(2 * slots * n * tokens * wide, 10e6),
    )(meta, *tables, *rows, *others)


def expert_kernel(experts, who_ref, x_ref, gate_ref, up_ref, pull_ref, *rest):
    act_ref, dgate_ref, dup_ref, copy_ref = rest[-4:]
    width = gate_ref.shape[0]
    x = x_ref[:, :width]
    table = x_ref[:, width:].astype(F32)
    lane = lax.broadcasted_iota(jnp.int32, table.shape, 1)
    mine = who_ref[0]
    gate = jnp.sum(
        jnp.where(jnp.logical_or(lane == mine, lane == mine + experts), table, 0.0),
        axis=1,
        keepdims=True,
    )
    pre_gate = dot_nn(x, gate_ref[...])
    pre_up = dot_nn(x, up_ref[...])
    pull = pull_ref[...].reshape(pre_up.shape)
    sig = 1.0 / (1.0 + jnp.exp(-pre_gate))
    silu = pre_gate * sig
    act = silu * pre_up
    act_ref[...] = (act * gate).astype(LOW)
    high, low = split_low(jnp.sum(act * pull, axis=1, keepdims=True))
    pull = pull * gate
    dup = (pull * silu).astype(LOW)
    dgate = (pull * pre_up * (sig * (1.0 + pre_gate * (1.0 - sig)))).astype(LOW)
    dgate_ref[...] = dgate
    dup_ref[...] = dup
    copy_ref[:, :width] = (dot_nt(dgate, gate_ref[...]) + dot_nt(dup, up_ref[...])).astype(LOW)
    back = jnp.where(lane == mine, high.astype(F32), 0.0)
    back = jnp.where(lane == mine + experts, low.astype(F32), back)
    copy_ref[:, width:] = back.astype(LOW)


def run_expert(who, x, w_gate, w_up, pull, part, experts):
    rows, wide = x.shape
    width, hidden = w_gate.shape
    groups, _, slots, _ = pull.shape
    each = groups // 2
    tile = each * slots
    by_rows = lambda columns: pl.BlockSpec((tile, columns), lambda i, p: (i, 0))
    return pl.pallas_call(
        functools.partial(expert_kernel, experts),
        grid_spec=pltpu.PrefetchScalarGridSpec(
            num_scalar_prefetch=1,
            grid=(2,),
            in_specs=[
                by_rows(wide),
                full(w_gate.shape),
                full(w_up.shape),
                pl.BlockSpec((each, 1, slots, hidden), lambda i, p: (i, part, 0, 0)),
            ],
            out_specs=[by_rows(hidden), by_rows(hidden), by_rows(hidden), by_rows(wide)],
        ),
        out_shape=[jax.ShapeDtypeStruct((rows, hidden), LOW)] * 3
        + [jax.ShapeDtypeStruct((rows, wide), LOW)],
        compiler_params=params(),
        cost_estimate=cost(8 * rows * width * hidden, 20e6, rows * hidden),
    )(who, x, w_gate, w_up, pull)


def input_kernel(grad_ref, x_ref, gain_ref, more_ref, out_ref):
    normal, rr = norm_parts(x_ref[...].astype(F32))
    grad = grad_ref[...].astype(F32)
    out_ref[...] = more_ref[...] + norm_back(grad, normal, rr, gain_ref[...])


def input_back(grad, x, gain, more):
    tokens, width = x.shape
    operands = [grad, x, gain[None], more]
    return pl.pallas_call(
        input_kernel,
        grid=(1,),
        in_specs=[full(value.shape) for value in operands],
        out_specs=full(more.shape),
        out_shape=jax.ShapeDtypeStruct((tokens, width), F32),
        compiler_params=params(),
        cost_estimate=cost(20 * tokens * width, 5e6),
    )(*operands)


def kv_back_kernel(factor, n_parts, c_ref, dkv_ref, *refs):
    parts = refs[:n_parts]
    proj_ref, gain_ref, cos_ref, sin_ref = refs[n_parts : n_parts + 4]
    grad_ref, dgain_ref = refs[-2:]
    size = proj_ref.shape[1]
    total = functools.reduce(jnp.add, [part[...].astype(F32) for part in parts], dkv_ref[...])
    grad, dgain = head_backward(
        total[:, :size] * factor, proj_ref[...], gain_ref[...], cos_ref[...], sin_ref[...]
    )
    grad_ref[:, :size] = grad.astype(LOW)
    grad_ref[:, size:] = total[:, size:].astype(LOW)
    dgain_ref[...] = dgain


def kv_back(context, dkv, parts, proj, gain, cos2, sin2, factor, others):
    block, size = proj.shape
    operands = [proj, gain[None], cos2, sin2]
    shapes = [
        jax.ShapeDtypeStruct((block, 2 * size), LOW),
        jax.ShapeDtypeStruct((1, size), F32),
    ]
    return pl.pallas_call(
        functools.partial(kv_back_kernel, factor, len(parts)),
        grid_spec=pltpu.PrefetchScalarGridSpec(
            num_scalar_prefetch=1,
            grid=(1,),
            in_specs=[pl.BlockSpec((block, 2 * size), lambda i, c: (c[0], 0))]
            + [full(part.shape) for part in parts]
            + [full(value.shape) for value in operands]
            + [pl.BlockSpec(memory_space=pl.ANY)] * len(others),
            out_specs=[full(shape.shape) for shape in shapes],
        ),
        out_shape=shapes,
        compiler_params=params(),
        cost_estimate=cost(40 * block * size, 5e6),
    )(context.astype(jnp.int32)[None], dkv, *parts, *operands, *others)


def widen_kernel(at_ref, *refs):
    out_ref = refs[-1]
    for k, ref in enumerate(refs[:-1]):

        @pl.when(pl.program_id(0) == k)
        def _():
            out_ref[...] = ref[...].astype(F32)


def widen(places, groups):
    chunks = [chunk for group in groups for chunk in group]
    count = len(places)
    rows, columns = chunks[0].shape
    tiles = 2 if rows % 32 == 0 else 1
    tile = rows // tiles

    def only_at(k):
        return pl.BlockSpec(
            (tile, columns),
            lambda i, j, at: (jnp.where(i < k, 0, jnp.where(i == k, j, tiles - 1)), 0),
        )

    return pl.pallas_call(
        widen_kernel,
        grid_spec=pltpu.PrefetchScalarGridSpec(
            num_scalar_prefetch=1,
            grid=(len(chunks), tiles),
            in_specs=[only_at(k) for k in range(len(chunks))],
            out_specs=pl.BlockSpec(
                (tile, columns),
                lambda i, j, at: (at[lax.rem(i, count)] * tiles + j, lax.div(i, count)),
            ),
        ),
        out_shape=jax.ShapeDtypeStruct((count * rows, len(groups) * columns), F32),
        compiler_params=params(),
        cost_estimate=cost(rows * columns, 6 * len(chunks) * rows * columns),
    )(jnp.stack(places).astype(jnp.int32), *chunks)


def sum_small(flat):
    n = lax.axis_size(ALL_AXES)
    length = flat.shape[0]
    each = -(-length // (n * 128)) * 128
    parts = jnp.pad(flat, (0, n * each - length)).reshape(n, each)
    parts = lax.all_to_all(parts, ALL_AXES, split_axis=0, concat_axis=0, tiled=True)
    own = jnp.sum(parts, axis=0, keepdims=True)
    whole = lax.all_to_all(
        jnp.broadcast_to(own, (n, each)), ALL_AXES, split_axis=0, concat_axis=0, tiled=True
    )
    return whole.reshape(-1)[:length]


def swap_dp(rows):
    return lax.ppermute(rows, "dp", [(0, 1), (1, 0)])


def swap_context(rows, s):
    n = lax.axis_size("context")
    return lax.ppermute(rows, "context", [(i, i ^ s) for i in range(n)])


def dp_got(grad):
    d = lax.axis_index("dp")
    rows = grad.shape[0] // 2
    return swap_dp(lax.dynamic_slice_in_dim(grad, (1 - d) * rows, rows))


def dp_chunks(grad, got):
    d, c = lax.axis_index("dp"), lax.axis_index("context")
    n = lax.axis_size("context")
    rows = grad.shape[0] // 2
    each = rows // n
    chunks = []
    for s in range(n):
        mine = lax.dynamic_slice_in_dim(grad, d * rows + (c ^ s) * each, each)
        other = lax.dynamic_slice_in_dim(got, (c ^ s) * each, each)
        chunks.append((mine.astype(F32) + other.astype(F32)).astype(LOW))
    return chunks


def context_sum(chunks):
    total = chunks[0].astype(F32)
    for s in range(1, len(chunks)):
        total += swap_context(chunks[s], s).astype(F32)
    return total.astype(LOW)


def context_spread(total):
    return [total] + [swap_context(total, s) for s in range(1, lax.axis_size("context"))]


def dp_spread(groups):
    n = lax.axis_size("context")
    d, c = lax.axis_index("dp"), lax.axis_index("context")
    places = [d * n + (c ^ s) for s in range(n)] + [(1 - d) * n + (c ^ s) for s in range(n)]
    return widen(places, [found + [swap_dp(part) for part in found] for found in groups])


def arrival_order(n):
    return [sorted(range(n), key=lambda j: (abs(j - i), j)) for i in range(n)]


def choose(index, options):
    distinct = []
    for option in options:
        if option is not None and not any(option is other for other in distinct):
            distinct.append(option)
    result = distinct[0]
    for option in distinct[1:]:
        mask = functools.reduce(
            jnp.logical_or, [index == i for i, other in enumerate(options) if other is option]
        )
        result = jnp.where(mask, option, result)
    return result


def line_gather(chunk):
    return line_steps({0: chunk}, 1, lax.axis_size("expert"))


def line_steps(found, first, stop):
    n = lax.axis_size("expert")
    found = dict(found)
    for s in range(first, stop):
        found[-s] = lax.ppermute(
            found[1 - s], "expert", [(i, i + 1) for i in range(s - 1, n - 1)]
        )
        found[s] = lax.ppermute(found[s - 1], "expert", [(i + 1, i) for i in range(n - s)])
    return found


def context_gather(rows):
    n = lax.axis_size("context")
    c = lax.axis_index("context")
    found = {0: rows}
    for s in range(1, n):
        found[s] = lax.ppermute(rows, "context", [(i, i ^ s) for i in range(n)])
    return jnp.concatenate([choose(c, [found[i ^ j] for i in range(n)]) for j in range(n)], axis=0)


def context_parts(rows):
    n = lax.axis_size("context")
    c = lax.axis_index("context")
    each = rows.shape[0] // n
    return [
        swap_context(lax.dynamic_slice_in_dim(rows, (c ^ s) * each, each).astype(LOW), s)
        for s in range(1, n)
    ]


def zero_of(*others):
    return functools.reduce(
        jnp.add,
        [
            lax.slice(other, (0,) * other.ndim, (1,) * other.ndim).reshape(()).astype(F32) * 0.0
            for other in others
        ],
    )


def after(value, *others):
    return (value.astype(F32) + zero_of(*others)).astype(value.dtype)


def on_device(
    layer_input,
    grad_output,
    attn_gain,
    query_weight,
    key_weight,
    value_weight,
    q_gain,
    k_gain,
    output_weight,
    mlp_gain,
    router,
    w_gate,
    w_up,
    w_down,
    routes,
    half_order,
):
    n_context = lax.axis_size("context")
    n_expert = lax.axis_size("expert")
    n_groups = lax.axis_size(GROUP_AXES)
    tok_dev, width = layer_input.shape[1:]
    size = q_gain.shape[0]
    kv_total = key_weight.shape[1] * n_expert
    group_dev = n_expert // (kv_total // size)
    kv_index = lax.axis_index("expert") // group_dev
    block = tok_dev * n_expert
    seq = block * n_context
    half = block // 2
    experts = router.shape[1]
    exp_dev = w_gate.shape[0]
    top = routes.shape[2]
    capacity = max(2, (tok_dev * top * 9 + 8 * experts - 1) // (8 * experts))
    scale = size ** (-0.5)

    seq_rows = jnp.arange(seq, dtype=jnp.int32)
    context = lax.axis_index("context")
    own_halves = lax.dynamic_slice_in_dim(half_order, 2 * context, 2)
    own_pos = (own_halves[:, None] * half + jnp.arange(half, dtype=jnp.int32)[None]).reshape(-1)
    per_half = half // TILE
    tile_pos = (half_order[:, None] * per_half + jnp.arange(per_half, dtype=jnp.int32)).reshape(-1)
    kidx = jnp.sum(
        (tile_pos[None, :] == jnp.arange(seq // TILE, dtype=jnp.int32)[:, None])
        * jnp.arange(seq // TILE, dtype=jnp.int32)[None, :],
        axis=1,
    ).astype(jnp.int32)
    qpos = lax.dynamic_slice_in_dim(tile_pos, context * (block // TILE), block // TILE)
    entry = jnp.arange(size)
    freq = jnp.power(THETA, -(2 * (entry % (size // 2))).astype(F32) / size)
    angles = own_pos.astype(F32)[:, None] * freq[None, :]
    cos2 = jnp.cos(angles)
    sin2 = jnp.sin(angles) * jnp.where(entry < size // 2, -1.0, 1.0)[None, :]

    place = lax.axis_index("expert")
    place_1 = place.astype(jnp.int32)[None]
    lanes = -(-2 * experts // 128) * 128
    mask = jnp.any(
        routes[0][:, :, None] == jnp.arange(lanes, dtype=jnp.int32)[None, None, :], axis=1
    )
    mask_wide = mask.astype(F32)
    router_wide = jnp.pad(router, ((0, 0), (0, lanes - experts)))

    x_low = layer_input[0]
    x_normal, _ = norm_parts(x_low.astype(F32))
    normed_found = line_gather((x_normal * attn_gain).astype(LOW))
    if group_dev == 1:
        kv_weights = jnp.concatenate([key_weight, value_weight], axis=1)
    else:
        key_whole = lax.all_gather(key_weight, "expert", axis=1, tiled=True)
        value_whole = lax.all_gather(value_weight, "expert", axis=1, tiled=True)
        kv_weights = jnp.concatenate(
            [
                lax.dynamic_slice_in_dim(key_whole, kv_index * size, size, 1),
                lax.dynamic_slice_in_dim(value_whole, kv_index * size, size, 1),
            ],
            axis=1,
        )
    grad_low = grad_output[0]
    normed_rows, own_kv, key_proj, grad_wide = project_keys(
        place_1,
        normed_found,
        kv_weights,
        k_gain,
        cos2,
        sin2,
        scale * LOG2E,
        grad_low,
        mask_wide,
    )
    grad_col = lax.all_gather(grad_wide, "expert", axis=0, tiled=True)
    kv_whole = context_gather(own_kv)
    queries, query_proj = project_queries(normed_rows, query_weight, q_gain, cos2, sin2)

    n_half = n_expert // 2
    order_here = jnp.asarray(arrival_order(n_expert), jnp.int32)[place]
    turn_here = jnp.sum(
        (order_here[:, None] == jnp.arange(n_expert, dtype=jnp.int32)[None, :])
        * jnp.arange(n_expert, dtype=jnp.int32)[:, None],
        axis=0,
    ).astype(jnp.int32)
    meta = jnp.concatenate([place_1, turn_here, order_here])
    grad_sent, spreads, back_tables = make_tables(
        meta, grad_col, width, n_groups, n_half, capacity, [router_wide, mask_wide]
    )

    def swap_plane(rows):
        parts = rows.reshape(n_groups, -1, rows.shape[1])
        parts = lax.all_to_all(parts, GROUP_AXES, split_axis=0, concat_axis=0, tiled=True)
        return parts.reshape(rows.shape)

    attended, inverse = attend(qpos, kidx, queries, kv_whole, [])
    attn_part = (dot_nn(attended, output_weight) + zero_of(grad_sent)).astype(LOW)
    attn_rows = lax.psum_scatter(attn_part, "expert", scatter_dimension=0, tiled=True)

    grad_x = swap_plane(grad_sent)
    act_pull = dot_nt(grad_x, w_down[0]).reshape(n_groups, 2, n_half * capacity, -1)

    hidden, mixed, probs = route_rows(
        x_low, attn_rows, mlp_gain, router_wide, mask_wide, experts, []
    )

    who = (lax.axis_index(ALL_AXES) * exp_dev).astype(jnp.int32)[None]
    mixed_found = line_gather(mixed)
    near = spread_rows(place_1, spreads[0], mixed_found, range(n_half), [grad_x])
    x_near = swap_plane(near)
    worked_near = run_expert(who, x_near, w_gate[0], w_up[0], act_pull, 0, experts)
    far = spread_rows(place_1, spreads[1], mixed_found, range(n_half, n_expert), [x_near])
    x_far = swap_plane(far)
    worked_far = run_expert(who, x_far, w_gate[0], w_up[0], act_pull, 1, experts)
    xs = [x_near, x_far]
    acts, gate_lows, up_lows, copies = (list(pair) for pair in zip(worked_near, worked_far))
    back_far = swap_plane(copies[1])
    back_near = swap_plane(copies[0])
    join = lambda parts: jnp.concatenate(parts, axis=0)
    x_all = join([x[:, :width] for x in xs])
    grad_w_gate = dot_tn(x_all, join(gate_lows))
    grad_w_up = dot_tn(x_all, join(up_lows))
    grad_by_round = jnp.swapaxes(
        grad_x.reshape(n_groups, 2, n_half * capacity, width), 0, 1
    ).reshape(-1, width)
    grad_w_down = dot_tn(join(acts), grad_by_round)
    copies_col = combine_rows(
        meta, back_tables, [back_near, back_far], n_half, [grad_w_gate, grad_w_up]
    )
    copies_sum = lax.psum_scatter(copies_col, "expert", scatter_dimension=0, tiled=True)

    returned = [dot_nn(act, w_down[0]).astype(LOW) for act in acts]
    returned_near = swap_plane(returned[0])

    grad_hidden, grad_hidden_low, grad_mlp_gain, grad_router = route_back(
        copies_sum,
        grad_low,
        hidden,
        mlp_gain,
        router_wide,
        mask_wide,
        probs,
        experts,
        [returned_near, grad_w_down],
    )

    returned_far = swap_plane(returned[1])
    grad_attn = lax.all_gather(grad_hidden_low, "expert", axis=0, tiled=True)
    grad_o, centre = grad_attended(
        grad_attn, output_weight, attended, inverse, [returned_far]
    )
    combined = combine_rows(meta, back_tables, [returned_near, returned_far], n_half, [])
    output_rows = hidden + lax.psum_scatter(
        combined, "expert", scatter_dimension=0, tiled=True
    ).astype(F32)
    w_out_part = token_dot(attended, grad_attn, [])
    w_out_chunks = dp_chunks(w_out_part, dp_got(w_out_part))
    back = functools.partial(
        attend_back,
        qpos,
        kidx,
        queries,
        grad_o,
        centre,
        kv_whole,
        query_proj,
        q_gain,
        cos2,
        sin2,
    )
    grad_kv_1, grad_q_1, grad_q_gain_1 = back(0, [combined, *w_out_chunks])
    w_out_total = context_sum(w_out_chunks)
    w_query_1 = token_dot(normed_rows, grad_q_1, [])
    grad_kv_2, grad_q_2, grad_q_gain_2 = back(1, [w_out_total, w_query_1])
    w_out_found = context_spread(w_out_total)
    w_query_got_1 = dp_got(w_query_1)
    w_query_2 = token_dot(normed_rows, grad_q_2, [*w_out_found, w_query_got_1])
    grad_kv = grad_kv_1 + grad_kv_2
    grad_q = jnp.concatenate([grad_q_1, grad_q_2], axis=1)
    grad_q_gain = grad_q_gain_1 + grad_q_gain_2
    kv_parts = context_parts(grad_kv)

    kv_grads, grad_k_gain = kv_back(
        context, grad_kv, kv_parts, key_proj, k_gain, cos2, sin2, scale, [output_rows]
    )
    grad_normed = dot_nt(grad_q, query_weight) + dot_nt(kv_grads, kv_weights)
    grad_attn_gain = jnp.sum(grad_normed * normed_rows.astype(F32), axis=0) / attn_gain
    grad_normed = lax.psum_scatter(
        grad_normed.astype(LOW), "expert", scatter_dimension=0, tiled=True
    )
    grad_input = input_back(grad_normed, x_low, attn_gain, grad_hidden)

    grad_w_out = dp_spread([w_out_found])
    grad_w_query = dp_spread(
        [
            context_spread(context_sum(dp_chunks(w_query_1, w_query_got_1))),
            context_spread(context_sum(dp_chunks(w_query_2, dp_got(w_query_2)))),
        ]
    )
    grad_w_kv = token_dot(normed_rows, kv_grads, [])
    if group_dev == 1:
        grad_w_kv = dp_spread([context_spread(context_sum(dp_chunks(grad_w_kv, dp_got(grad_w_kv))))])
        grad_w_key, grad_w_value = grad_w_kv[:, :size], grad_w_kv[:, size:]
    else:
        blank = jnp.zeros((width, kv_total), LOW)
        pieces = []
        for part in (grad_w_kv[:, :size], grad_w_kv[:, size:]):
            padded = lax.dynamic_update_slice(blank, part, (0, kv_index * size))
            pieces.append(lax.psum_scatter(padded, "expert", scatter_dimension=1, tiled=True))
        grad_w_key, grad_w_value = (lax.psum(piece, GROUP_AXES).astype(F32) for piece in pieces)

    small = [
        grad_attn_gain,
        grad_mlp_gain[0],
        grad_q_gain[0],
        grad_k_gain[0],
        grad_router[:experts].reshape(-1),
    ]
    summed = sum_small(jnp.concatenate(small))
    pieces = []
    offset = 0
    for part in small:
        pieces.append(summed[offset : offset + part.shape[0]])
        offset += part.shape[0]
    grad_attn_gain, grad_mlp_gain, grad_q_gain, grad_k_gain, grad_router = pieces
    return (
        output_rows.astype(LOW)[None],
        grad_input[None],
        grad_attn_gain,
        grad_w_query,
        grad_w_key,
        grad_w_value,
        grad_q_gain,
        grad_k_gain,
        grad_w_out,
        grad_mlp_gain,
        grad_router.reshape(experts, width).T,
        grad_w_gate[None],
        grad_w_up[None],
        grad_w_down[None],
    )


def solution(mesh):
    rows = P("dp", ("context", "expert"), None)
    expert = P(ALL_AXES, None, None)
    columns = P(None, "expert")
    in_specs = (
        rows,
        rows,
        P(),
        columns,
        columns,
        columns,
        P(),
        P(),
        P("expert", None),
        P(),
        P(),
        expert,
        expert,
        expert,
        rows,
        P(),
    )
    out_specs = (
        rows,
        rows,
        P(),
        columns,
        columns,
        columns,
        P(),
        P(),
        P("expert", None),
        P(),
        P(),
        expert,
        expert,
        expert,
    )
    return jax.shard_map(
        on_device, mesh=mesh, in_specs=in_specs, out_specs=out_specs, check_vma=False
    )
```

```python
import functools
import math

import jax
import jax.numpy as jnp
from jax import lax
from jax.experimental import pallas as pl
from jax.experimental.pallas import tpu as pltpu
from jax.sharding import PartitionSpec as P

EPS = 1e-06
THETA = 1000000.0
TILE = 256
VMEM_BYTES = 56 * 1024 * 1024
LOG2E = math.log2(math.e)
LOW = jnp.bfloat16
F32 = jnp.float32
ALL_AXES = ("dp", "context", "expert")
GROUP_AXES = ("dp", "context")


def dot_nn(a, b):
    return lax.dot_general(a, b, (((1,), (0,)), ((), ())), preferred_element_type=F32)


def dot_nt(a, b):
    return lax.dot_general(a, b, (((1,), (1,)), ((), ())), preferred_element_type=F32)


def dot_tn(a, b):
    return lax.dot_general(a, b, (((0,), (0,)), ((), ())), preferred_element_type=F32)


def params(**more):
    return pltpu.CompilerParams(vmem_limit_bytes=VMEM_BYTES, **more)


def cost(flops, nbytes, exps=0):
    return pl.CostEstimate(flops=int(flops), bytes_accessed=int(nbytes), transcendentals=int(exps))


def head_forward(u, gain, cos2, sin2):
    rr = lax.rsqrt(jnp.mean(u * u, axis=-1, keepdims=True) + EPS)
    y = u * rr * gain
    return y * cos2 + pltpu.roll(y, 64, 1) * sin2


def head_backward(gy, u, gain, cos2, sin2):
    g = gy * cos2 - pltpu.roll(gy, 64, 1) * sin2
    rr = lax.rsqrt(jnp.mean(u * u, axis=-1, keepdims=True) + EPS)
    n = u * rr
    gn = g * gain
    grad = rr * (gn - n * jnp.mean(gn * n, axis=-1, keepdims=True))
    return grad, jnp.sum(g * n, axis=0, keepdims=True)


def query_kernel(x_ref, w_ref, gain_ref, cos_ref, sin_ref, rot_ref, proj_ref):
    tiles, heads, rows, size = rot_ref.shape
    acc = dot_nn(x_ref[...], w_ref[...])
    for h in range(heads):
        u = acc[:, h * size : (h + 1) * size]
        rot = head_forward(u, gain_ref[...], cos_ref[...], sin_ref[...])
        proj_ref[:, h] = u.reshape(tiles, rows, size)
        rot_ref[:, h] = rot.astype(LOW).reshape(tiles, rows, size)


def project_queries(normed, weight, gain, cos2, sin2):
    block, width = normed.shape
    size = cos2.shape[1]
    heads = weight.shape[1] // size
    tiles = block // TILE
    whole = lambda i: (0, 0)
    per = lambda i: (0, i, 0, 0)
    shape = (tiles, heads, TILE, size)
    return pl.pallas_call(
        query_kernel,
        grid=(heads // 2,),
        in_specs=[
            pl.BlockSpec((block, width), whole),
            pl.BlockSpec((width, 2 * size), lambda i: (0, i)),
            pl.BlockSpec((1, size), whole),
            pl.BlockSpec((block, size), whole),
            pl.BlockSpec((block, size), whole),
        ],
        out_specs=[pl.BlockSpec((tiles, 2, TILE, size), per)] * 2,
        out_shape=[jax.ShapeDtypeStruct(shape, LOW), jax.ShapeDtypeStruct(shape, F32)],
        compiler_params=params(),
        cost_estimate=cost(2 * block * width * heads * size, 12e6),
    )(normed, weight, gain[None], cos2, sin2)


def put_in_order(place, refs, out_ref):
    n = (len(refs) + 1) // 2
    rows = refs[0].shape[0]
    for distance in range(1 - n, n):
        ref = refs[distance + n - 1]
        at = place + distance

        @pl.when(jnp.logical_and(at >= 0, at < n))
        def _():
            out_ref[pl.ds(pl.multiple_of(at * rows, rows), rows), :] = ref[...]


def chunk_list(found):
    n = (len(found) + 1) // 2
    return [found[distance] for distance in range(1 - n, n)]


def key_kernel(factor, n_chunks, place_ref, *refs):
    w_ref, gain_ref, cos_ref, sin_ref, g_ref, mask_ref = refs[n_chunks:-4]
    rows_ref, kv_ref, proj_ref, wide_ref = refs[-4:]
    size = proj_ref.shape[1]
    width = g_ref.shape[1]
    put_in_order(place_ref[0], refs[:n_chunks], rows_ref)
    wide_ref[:, :width] = g_ref[...]
    wide_ref[:, width:] = mask_ref[...].astype(LOW)
    acc = dot_nn(rows_ref[...], w_ref[...])
    u = acc[:, :size]
    rot = head_forward(u, gain_ref[...], cos_ref[...], sin_ref[...])
    proj_ref[...] = u
    kv_ref[:, :size] = (rot * factor).astype(LOW)
    kv_ref[:, size:] = acc[:, size:].astype(LOW)


def full(shape):
    return pl.BlockSpec(shape, lambda *_: (0,) * len(shape))


def project_keys(place, found, weight, gain, cos2, sin2, factor, g, mask):
    chunks = chunk_list(found)
    rows, width = chunks[0].shape
    block, size = cos2.shape
    operands = [*chunks, weight, gain[None], cos2, sin2, g, mask]
    shapes = [
        jax.ShapeDtypeStruct((block, width), LOW),
        jax.ShapeDtypeStruct((block, 2 * size), LOW),
        jax.ShapeDtypeStruct((block, size), F32),
        jax.ShapeDtypeStruct((rows, width + mask.shape[1]), LOW),
    ]
    return pl.pallas_call(
        functools.partial(key_kernel, factor, len(chunks)),
        grid_spec=pltpu.PrefetchScalarGridSpec(
            num_scalar_prefetch=1,
            grid=(1,),
            in_specs=[full(x.shape) for x in operands],
            out_specs=[full(x.shape) for x in shapes],
        ),
        out_shape=shapes,
        compiler_params=params(),
        cost_estimate=cost(4 * block * width * size, 8e6),
    )(place, *operands)


def in_order(last, step):
    lax.fori_loop(0, lax.div(last, 2), lambda p, c: (step([2 * p, 2 * p + 1], False), c)[1], 0)

    @pl.when(lax.rem(last, 2) == 1)
    def _():
        step([last - 1, last], True)

    @pl.when(lax.rem(last, 2) == 0)
    def _():
        step([last], True)


def attend_kernel(qpos_ref, kidx_ref, q_ref, kv_ref, *rest):
    out_ref, inv_ref, acc_ref = rest[-3:]
    heads, rows, size = q_ref.shape[1:]
    acc_ref[...] = jnp.zeros_like(acc_ref)

    def step(places, masked):
        starts = [pl.multiple_of(kidx_ref[place] * rows, rows) for place in places]
        count = len(places) * rows
        keys = jnp.concatenate([kv_ref[pl.ds(start, rows), :size] for start in starts], axis=0)
        values = jnp.concatenate([kv_ref[pl.ds(start, rows), size:] for start in starts], axis=0)
        values = jnp.concatenate([values, jnp.ones((count, size), LOW)], axis=1)
        for h in range(heads):
            e = jnp.exp2(dot_nt(q_ref[0, h], keys))
            if masked:
                qi = lax.broadcasted_iota(jnp.int32, e.shape, 0)
                ki = lax.broadcasted_iota(jnp.int32, e.shape, 1) - (count - rows)
                e = jnp.where(ki <= qi, e, 0.0)
            acc_ref[h] += dot_nn(e.astype(LOW), values)

    in_order(qpos_ref[pl.program_id(0)], step)
    for h in range(heads):
        inv = 1.0 / acc_ref[h, :, size:]
        inv_ref[0, h] = inv
        out_ref[:, h * size : (h + 1) * size] = (acc_ref[h, :, :size] * inv).astype(LOW)


def attend(qpos, kidx, queries, kv, others):
    tiles, heads, rows, size = queries.shape
    seq = kv.shape[0]
    return pl.pallas_call(
        attend_kernel,
        grid_spec=pltpu.PrefetchScalarGridSpec(
            num_scalar_prefetch=2,
            grid=(tiles,),
            in_specs=[
                pl.BlockSpec((1, heads, rows, size), lambda i, a, b: (i, 0, 0, 0)),
                pl.BlockSpec((seq, 2 * size), lambda i, a, b: (0, 0)),
            ]
            + [pl.BlockSpec(memory_space=pl.ANY)] * len(others),
            out_specs=[
                pl.BlockSpec((rows, heads * size), lambda i, a, b: (i, 0)),
                pl.BlockSpec((1, heads, rows, size), lambda i, a, b: (i, 0, 0, 0)),
            ],
            scratch_shapes=[pltpu.VMEM((heads, rows, 2 * size), F32)],
        ),
        out_shape=[
            jax.ShapeDtypeStruct((tiles * rows, heads * size), LOW),
            jax.ShapeDtypeStruct((tiles, heads, rows, size), F32),
        ],
        compiler_params=params(),
        cost_estimate=cost(
            6 * tiles * rows * heads * seq * size, 8e6, tiles * rows * heads * seq
        ),
    )(qpos, kidx, queries, kv, *others)


def grad_out_kernel(rows_ref, w_ref, o_ref, inv_ref, *rest):
    do_ref, centre_ref = rest[-2:]
    tiles, heads, rows, size = do_ref.shape
    acc = dot_nt(rows_ref[...], w_ref[...])
    for t in range(tiles):
        for h in range(heads):
            part = slice(t * rows, (t + 1) * rows), slice(h * size, (h + 1) * size)
            low = (acc[part] * inv_ref[t, h]).astype(LOW)
            do_ref[t, h] = low
            product = low.astype(F32) * o_ref[part].astype(F32)
            centre = jnp.sum(jnp.transpose(product), axis=0, keepdims=True)
            centre_ref[t, h] = jnp.broadcast_to(centre, (8, rows))


def grad_attended(grad_rows, weight, attended, inverse, others):
    tiles, heads, rows, size = inverse.shape
    block, width = grad_rows.shape
    return pl.pallas_call(
        grad_out_kernel,
        grid=(heads // 2,),
        in_specs=[
            pl.BlockSpec((block, width), lambda i: (0, 0)),
            pl.BlockSpec((2 * size, width), lambda i: (i, 0)),
            pl.BlockSpec((block, 2 * size), lambda i: (0, i)),
            pl.BlockSpec((tiles, 2, rows, size), lambda i: (0, i, 0, 0)),
        ]
        + [pl.BlockSpec(memory_space=pl.ANY)] * len(others),
        out_specs=[
            pl.BlockSpec((tiles, 2, rows, size), lambda i: (0, i, 0, 0)),
            pl.BlockSpec((tiles, 2, 8, rows), lambda i: (0, i, 0, 0)),
        ],
        out_shape=[
            jax.ShapeDtypeStruct((tiles, heads, rows, size), LOW),
            jax.ShapeDtypeStruct((tiles, heads, 8, rows), F32),
        ],
        compiler_params=params(),
        cost_estimate=cost(2 * block * width * heads * size, 12e6),
    )(grad_rows, weight, attended, inverse, *others)


def attend_back_kernel(
    qpos_ref,
    kidx_ref,
    q_ref,
    do_ref,
    centre_ref,
    kv_ref,
    proj_ref,
    gain_ref,
    cos_ref,
    sin_ref,
    *rest,
):
    dkv_ref, dq_ref, dgain_ref, acc_ref, e_ref, ds_ref = rest[-6:]
    heads, rows, size = q_ref.shape[1:]

    @pl.when(pl.program_id(0) == 0)
    def _():
        dkv_ref[...] = jnp.zeros_like(dkv_ref)
        dgain_ref[...] = jnp.zeros_like(dgain_ref)

    acc_ref[...] = jnp.zeros_like(acc_ref)

    def step(places, masked):
        starts = [pl.multiple_of(kidx_ref[place] * rows, rows) for place in places]
        count = len(places) * rows
        keys = jnp.concatenate([kv_ref[pl.ds(start, rows), :size] for start in starts], axis=0)
        values = jnp.concatenate([kv_ref[pl.ds(start, rows), size:] for start in starts], axis=0)
        for h in range(heads):
            query, grad = q_ref[0, h], do_ref[0, h]
            e = jnp.exp2(dot_nt(keys, query))
            if masked:
                ki = lax.broadcasted_iota(jnp.int32, e.shape, 0) - (count - rows)
                qi = lax.broadcasted_iota(jnp.int32, e.shape, 1)
                e = jnp.where(ki <= qi, e, 0.0)
            ds = (e * (dot_nt(values, grad) - centre_ref[0, h, 0:1])).astype(LOW)
            e_ref[:count, h * rows : (h + 1) * rows] = e.astype(LOW)
            ds_ref[:count, h * rows : (h + 1) * rows] = ds
            acc_ref[h] += dot_tn(ds, keys)
        dk = dot_nn(ds_ref[:count], q_ref[0].reshape(heads * rows, size))
        dv = dot_nn(e_ref[:count], do_ref[0].reshape(heads * rows, size))
        for k, start in enumerate(starts):
            dkv_ref[pl.ds(start, rows), :size] += dk[k * rows : (k + 1) * rows]
            dkv_ref[pl.ds(start, rows), size:] += dv[k * rows : (k + 1) * rows]

    in_order(qpos_ref[pl.program_id(0)], step)
    total = jnp.zeros((1, size), F32)
    for h in range(heads):
        grad, gain_part = head_backward(
            acc_ref[h] * (1.0 / LOG2E), proj_ref[0, h], gain_ref[...], cos_ref[...], sin_ref[...]
        )
        dq_ref[:, h * size : (h + 1) * size] = grad.astype(LOW)
        total += gain_part
    dgain_ref[...] += total


def attend_back(qpos, kidx, queries, grads, centre, kv, proj, gain, cos2, sin2):
    tiles, heads, rows, size = queries.shape
    seq = kv.shape[0]
    per = pl.BlockSpec((1, heads, rows, size), lambda i, a, b: (i, 0, 0, 0))
    flat = lambda i, a, b: (0, 0)
    rowwise = lambda i, a, b: (i, 0)
    return pl.pallas_call(
        attend_back_kernel,
        grid_spec=pltpu.PrefetchScalarGridSpec(
            num_scalar_prefetch=2,
            grid=(tiles,),
            in_specs=[
                per,
                per,
                pl.BlockSpec((1, heads, 8, rows), lambda i, a, b: (i, 0, 0, 0)),
                pl.BlockSpec((seq, 2 * size), flat),
                per,
                pl.BlockSpec((1, size), flat),
                pl.BlockSpec((rows, size), rowwise),
                pl.BlockSpec((rows, size), rowwise),
            ],
            out_specs=[
                pl.BlockSpec((seq, 2 * size), flat),
                pl.BlockSpec((rows, heads * size), rowwise),
                pl.BlockSpec((1, size), flat),
            ],
            scratch_shapes=[pltpu.VMEM((heads, rows, size), F32)]
            + [pltpu.VMEM((2 * rows, heads * rows), LOW)] * 2,
        ),
        out_shape=[
            jax.ShapeDtypeStruct((seq, 2 * size), F32),
            jax.ShapeDtypeStruct((tiles * rows, heads * size), LOW),
            jax.ShapeDtypeStruct((1, size), F32),
        ],
        compiler_params=params(),
        cost_estimate=cost(
            15 * tiles * rows * heads * seq * size, 12e6, tiles * rows * heads * seq
        ),
    )(qpos, kidx, queries, grads, centre, kv, proj, gain[None], cos2, sin2)


def token_kernel(a_ref, b_ref, *rest):
    rest[-1][...] = dot_tn(a_ref[...], b_ref[...]).astype(LOW)


def token_dot(a, b, others):
    block, rows = a.shape
    columns = b.shape[1]
    tile = min(rows, 512)
    return pl.pallas_call(
        token_kernel,
        grid=(rows // tile,),
        in_specs=[
            pl.BlockSpec((block, tile), lambda i: (0, i)),
            pl.BlockSpec((block, columns), lambda i: (0, 0)),
        ]
        + [pl.BlockSpec(memory_space=pl.ANY)] * len(others),
        out_specs=pl.BlockSpec((tile, columns), lambda i: (i, 0)),
        out_shape=jax.ShapeDtypeStruct((rows, columns), LOW),
        compiler_params=params(),
        cost_estimate=cost(2 * block * rows * columns, 6e6),
    )(a, b, *others)


def split_low(value):
    high = value.astype(LOW)
    return high, (value - high.astype(F32)).astype(LOW)


def norm_parts(rows):
    rr = lax.rsqrt(jnp.mean(rows * rows, axis=-1, keepdims=True) + EPS)
    return rows * rr, rr


def norm_back(grad, normal, rr, gain):
    weighted = grad * gain
    return rr * (weighted - normal * jnp.mean(weighted * normal, axis=-1, keepdims=True))


def add_all(refs):
    return functools.reduce(jnp.add, [ref[...].astype(F32) for ref in refs])


def pad_rows(rows, count):
    if rows.shape[0] == count:
        return rows
    return jnp.concatenate(
        [rows, jnp.zeros((count - rows.shape[0], rows.shape[1]), rows.dtype)], axis=0
    )


def router_kernel(experts, *refs):
    x_ref, attn_ref, gain_ref, router_ref, mask_ref = refs[:5]
    hidden_ref, mixed_ref, probs_ref = refs[-3:]
    width = x_ref.shape[1]
    lanes = mask_ref.shape[1]
    hidden = add_all([x_ref, attn_ref])
    hidden_ref[...] = hidden
    mixed = (norm_parts(hidden)[0] * gain_ref[...]).astype(LOW)
    mixed_ref[:, :width] = mixed
    logits = dot_nt(mixed, pad_rows(router_ref[...], lanes))
    lane = lax.broadcasted_iota(jnp.int32, logits.shape, 1)
    logits = jnp.where(lane < experts, logits, -1e30)
    weights = jnp.exp(logits - jnp.max(logits, axis=1, keepdims=True))
    probs = weights / jnp.sum(weights, axis=1, keepdims=True)
    probs_ref[...] = probs
    chosen = probs * mask_ref[...]
    high, low = split_low(chosen / jnp.sum(chosen, axis=1, keepdims=True))
    both = high.astype(F32) + pltpu.roll(low.astype(F32), experts, 1)
    mixed_ref[:, width:] = both.astype(LOW)


def route_rows(x, attn, gain, router, mask, experts, others):
    tokens, width = x.shape
    lanes = mask.shape[1]
    operands = [x, attn, gain[None], router, mask]
    shapes = [
        jax.ShapeDtypeStruct((tokens, width), F32),
        jax.ShapeDtypeStruct((tokens, width + lanes), LOW),
        jax.ShapeDtypeStruct((tokens, lanes), F32),
    ]
    return pl.pallas_call(
        functools.partial(router_kernel, experts),
        grid=(1,),
        in_specs=[full(value.shape) for value in operands]
        + [pl.BlockSpec(memory_space=pl.ANY)] * len(others),
        out_specs=[full(shape.shape) for shape in shapes],
        out_shape=shapes,
        compiler_params=params(),
        cost_estimate=cost(2 * tokens * width * lanes, 5e6),
    )(*operands, *others)


def table_kernel(capacity, n_half, meta_ref, col_ref, *rest):
    rows_ref, near_ref, far_ref, near_back_ref, far_back_ref, slots_ref = rest[-6:]
    block = col_ref.shape[0]
    rows, width = rows_ref.shape
    n = 2 * n_half
    tokens = block // n
    cap_half = n_half * capacity
    groups = rows // (2 * cap_half)
    mask = col_ref[:, width:]
    lanes = mask.shape[1]
    padded = -(-groups // 16) * 16
    group = lax.broadcasted_iota(jnp.int32, (padded, lanes), 0)
    lane = lax.broadcasted_iota(jnp.int32, (padded, lanes), 1)
    wanted = jnp.logical_and(lane == group * n + meta_ref[0], group < groups)
    hits = dot_nt(jnp.where(wanted, 1.0, 0.0).astype(LOW), mask)
    before = lax.broadcasted_iota(jnp.int32, (tokens, tokens), 0)
    after_it = lax.broadcasted_iota(jnp.int32, (tokens, tokens), 1)
    earlier = jnp.where(before < after_it, 1.0, 0.0).astype(LOW)
    for z in range(n):
        hit = hits[:, z * tokens : (z + 1) * tokens]
        rank = dot_nn(hit.astype(LOW), earlier)
        turn = (meta_ref[1 + z] * capacity).astype(F32)
        slot = jnp.where(hit > 0.5, rank + turn, -1.0)
        slots_ref[:, z * tokens : (z + 1) * tokens] = slot[:groups]

    def one_hot(slots, count, first):
        slot = lax.broadcasted_iota(jnp.int32, (groups, count, slots.shape[1]), 1).astype(F32)
        same = slots[:, None, :] == slot + float(first)
        return jnp.where(same, 1.0, 0.0).reshape(groups * count, slots.shape[1])

    spread = one_hot(slots_ref[...], 2 * cap_half, 0).astype(LOW)
    rows_ref[...] = dot_nn(spread, col_ref[:, :width]).astype(LOW)
    for part, (to_ref, back_ref) in enumerate([(near_ref, near_back_ref), (far_ref, far_back_ref)]):
        pieces = []
        for k in range(n_half):
            start = pl.multiple_of(meta_ref[1 + n + part * n_half + k] * tokens, tokens)
            pieces.append(slots_ref[:, pl.ds(start, tokens)])
        spread = one_hot(jnp.concatenate(pieces, axis=1), cap_half, part * cap_half)
        to_ref[...] = spread.astype(LOW)
        back_ref[...] = jnp.transpose(spread).astype(LOW)


def make_tables(meta, col, width, groups, n_half, capacity, others):
    block = col.shape[0]
    rows = groups * n_half * capacity
    shapes = (
        [jax.ShapeDtypeStruct((2 * rows, width), LOW)]
        + [jax.ShapeDtypeStruct((rows, block // 2), LOW)] * 2
        + [jax.ShapeDtypeStruct((block // 2, rows), LOW)] * 2
    )
    outs = pl.pallas_call(
        functools.partial(table_kernel, capacity, n_half),
        grid_spec=pltpu.PrefetchScalarGridSpec(
            num_scalar_prefetch=1,
            grid=(1,),
            in_specs=[full(col.shape)] + [pl.BlockSpec(memory_space=pl.ANY)] * len(others),
            out_specs=[full(shape.shape) for shape in shapes],
            scratch_shapes=[pltpu.VMEM((groups, block), F32)],
        ),
        out_shape=shapes,
        compiler_params=params(),
        cost_estimate=cost(4 * rows * block * width, 12e6),
    )(meta, col, *others)
    return outs[0], outs[1:3], outs[3:]


def spread_kernel(choices, place_ref, spread_ref, *refs):
    out_ref, rows_ref = refs[-2:]
    for k, by_place in enumerate(choices):
        for which in sorted(set(by_place)):
            hit = functools.reduce(
                jnp.logical_or,
                [place_ref[0] == i for i, other in enumerate(by_place) if other == which],
            )

            @pl.when(hit)
            def _():
                tokens = refs[which].shape[0]
                rows_ref[k * tokens : (k + 1) * tokens] = refs[which][...]

    out_ref[...] = dot_nn(spread_ref[...], rows_ref[...]).astype(LOW)


def spread_rows(place, spread, found, turns, others):
    n = lax.axis_size("expert")
    order = arrival_order(n)
    distances = sorted({order[i][turn] - i for i in range(n) for turn in turns})
    choices = [[distances.index(order[i][turn] - i) for i in range(n)] for turn in turns]
    chunks = [found[distance] for distance in distances]
    tokens, wide = chunks[0].shape
    rows = spread.shape[0]
    return pl.pallas_call(
        functools.partial(spread_kernel, choices),
        grid_spec=pltpu.PrefetchScalarGridSpec(
            num_scalar_prefetch=1,
            grid=(1,),
            in_specs=[full(spread.shape)]
            + [full(chunk.shape) for chunk in chunks]
            + [pl.BlockSpec(memory_space=pl.ANY)] * len(others),
            out_specs=full((rows, wide)),
            scratch_shapes=[pltpu.VMEM((len(turns) * tokens, wide), LOW)],
        ),
        out_shape=jax.ShapeDtypeStruct((rows, wide), LOW),
        compiler_params=params(),
        cost_estimate=cost(2 * rows * len(turns) * tokens * wide, 5e6),
    )(place, spread, *chunks, *others)


def router_back_kernel(experts, *refs):
    sum_ref, g_ref, hidden_ref, gain_ref, router_ref, mask_ref, probs_ref = refs[:7]
    grad_ref, low_ref, dgain_ref, drouter_ref = refs[-4:]
    width = g_ref.shape[1]
    lanes = mask_ref.shape[1]
    total = sum_ref[...].astype(F32)
    table = total[:, width:]
    mask, probs = mask_ref[...], probs_ref[...]
    grad_gates = (table + pltpu.roll(table, lanes - experts, 1)) * mask
    chosen = probs * mask
    chosen_sum = jnp.sum(chosen, axis=1, keepdims=True)
    mean = jnp.sum(grad_gates * (chosen / chosen_sum), axis=1, keepdims=True)
    centred = mask * (grad_gates - mean) / chosen_sum
    grad_logits = probs * (centred - jnp.sum(centred * chosen, axis=1, keepdims=True))
    high, low = split_low(grad_logits)
    router = pad_rows(router_ref[...], lanes)
    grad = total[:, :width] + dot_nn(high, router) + dot_nn(low, router)
    normal, rr = norm_parts(hidden_ref[...])
    mixed = (normal * gain_ref[...]).astype(LOW)
    drouter_ref[...] = dot_tn(high, mixed) + dot_tn(low, mixed)
    dgain_ref[...] = jnp.sum(grad * normal, axis=0, keepdims=True)
    grad_hidden = g_ref[...].astype(F32) + norm_back(grad, normal, rr, gain_ref[...])
    grad_ref[...] = grad_hidden
    low_ref[...] = grad_hidden.astype(LOW)


def route_back(summed, g, hidden, gain, router, mask, probs, experts, others):
    tokens, width = g.shape
    lanes = mask.shape[1]
    operands = [summed, g, hidden, gain[None], router, mask, probs]
    shapes = [
        jax.ShapeDtypeStruct((tokens, width), F32),
        jax.ShapeDtypeStruct((tokens, width), LOW),
        jax.ShapeDtypeStruct((1, width), F32),
        jax.ShapeDtypeStruct((lanes, width), F32),
    ]
    return pl.pallas_call(
        functools.partial(router_back_kernel, experts),
        grid=(1,),
        in_specs=[full(value.shape) for value in operands]
        + [pl.BlockSpec(memory_space=pl.ANY)] * len(others),
        out_specs=[full(shape.shape) for shape in shapes],
        out_shape=shapes,
        compiler_params=params(),
        cost_estimate=cost(8 * tokens * width * lanes, 8e6),
    )(*operands, *others)


def combine_kernel(n_half, meta_ref, near_table_ref, far_table_ref, near_ref, far_ref, *rest):
    del meta_ref
    turn = pl.program_id(0)

    @pl.when(turn < n_half)
    def _():
        rest[-1][...] = dot_nn(near_table_ref[...], near_ref[...]).astype(LOW)

    @pl.when(turn >= n_half)
    def _():
        rest[-1][...] = dot_nn(far_table_ref[...], far_ref[...]).astype(LOW)


def combine_rows(meta, tables, rows, n_half, others):
    tokens = tables[0].shape[0] // n_half
    slots, wide = rows[0].shape
    n = 2 * n_half
    return pl.pallas_call(
        functools.partial(combine_kernel, n_half),
        grid_spec=pltpu.PrefetchScalarGridSpec(
            num_scalar_prefetch=1,
            grid=(n,),
            in_specs=[
                pl.BlockSpec((tokens, slots), lambda i, m: (jnp.minimum(i, n_half - 1), 0)),
                pl.BlockSpec((tokens, slots), lambda i, m: (jnp.maximum(i - n_half, 0), 0)),
            ]
            + [full(value.shape) for value in rows]
            + [pl.BlockSpec(memory_space=pl.ANY)] * len(others),
            out_specs=pl.BlockSpec((tokens, wide), lambda i, m: (m[1 + n + i], 0)),
        ),
        out_shape=jax.ShapeDtypeStruct((n * tokens, wide), LOW),
        compiler_params=params(),
        cost_estimate=cost(2 * slots * n * tokens * wide, 10e6),
    )(meta, *tables, *rows, *others)


def expert_kernel(experts, who_ref, x_ref, gate_ref, up_ref, pull_ref, *rest):
    act_ref, dgate_ref, dup_ref, copy_ref = rest[-4:]
    width = gate_ref.shape[0]
    x = x_ref[:, :width]
    table = x_ref[:, width:].astype(F32)
    lane = lax.broadcasted_iota(jnp.int32, table.shape, 1)
    mine = who_ref[0]
    gate = jnp.sum(
        jnp.where(jnp.logical_or(lane == mine, lane == mine + experts), table, 0.0),
        axis=1,
        keepdims=True,
    )
    pre_gate = dot_nn(x, gate_ref[...])
    pre_up = dot_nn(x, up_ref[...])
    pull = pull_ref[...].reshape(pre_up.shape)
    sig = 1.0 / (1.0 + jnp.exp(-pre_gate))
    silu = pre_gate * sig
    act = silu * pre_up
    act_ref[...] = (act * gate).astype(LOW)
    high, low = split_low(jnp.sum(act * pull, axis=1, keepdims=True))
    pull = pull * gate
    dup = (pull * silu).astype(LOW)
    dgate = (pull * pre_up * (sig * (1.0 + pre_gate * (1.0 - sig)))).astype(LOW)
    dgate_ref[...] = dgate
    dup_ref[...] = dup
    copy_ref[:, :width] = (dot_nt(dgate, gate_ref[...]) + dot_nt(dup, up_ref[...])).astype(LOW)
    back = jnp.where(lane == mine, high.astype(F32), 0.0)
    back = jnp.where(lane == mine + experts, low.astype(F32), back)
    copy_ref[:, width:] = back.astype(LOW)


def run_expert(who, x, w_gate, w_up, pull, part, experts):
    rows, wide = x.shape
    width, hidden = w_gate.shape
    groups, _, slots, _ = pull.shape
    each = groups // 2
    tile = each * slots
    by_rows = lambda columns: pl.BlockSpec((tile, columns), lambda i, p: (i, 0))
    return pl.pallas_call(
        functools.partial(expert_kernel, experts),
        grid_spec=pltpu.PrefetchScalarGridSpec(
            num_scalar_prefetch=1,
            grid=(2,),
            in_specs=[
                by_rows(wide),
                full(w_gate.shape),
                full(w_up.shape),
                pl.BlockSpec((each, 1, slots, hidden), lambda i, p: (i, part, 0, 0)),
            ],
            out_specs=[by_rows(hidden), by_rows(hidden), by_rows(hidden), by_rows(wide)],
        ),
        out_shape=[jax.ShapeDtypeStruct((rows, hidden), LOW)] * 3
        + [jax.ShapeDtypeStruct((rows, wide), LOW)],
        compiler_params=params(),
        cost_estimate=cost(8 * rows * width * hidden, 20e6, rows * hidden),
    )(who, x, w_gate, w_up, pull)


def input_kernel(grad_ref, x_ref, gain_ref, more_ref, out_ref):
    normal, rr = norm_parts(x_ref[...].astype(F32))
    grad = grad_ref[...].astype(F32)
    out_ref[...] = more_ref[...] + norm_back(grad, normal, rr, gain_ref[...])


def input_back(grad, x, gain, more):
    tokens, width = x.shape
    operands = [grad, x, gain[None], more]
    return pl.pallas_call(
        input_kernel,
        grid=(1,),
        in_specs=[full(value.shape) for value in operands],
        out_specs=full(more.shape),
        out_shape=jax.ShapeDtypeStruct((tokens, width), F32),
        compiler_params=params(),
        cost_estimate=cost(20 * tokens * width, 5e6),
    )(*operands)


def kv_back_kernel(factor, n_parts, c_ref, dkv_ref, *refs):
    parts = refs[:n_parts]
    proj_ref, gain_ref, cos_ref, sin_ref = refs[n_parts : n_parts + 4]
    grad_ref, dgain_ref = refs[-2:]
    size = proj_ref.shape[1]
    total = functools.reduce(jnp.add, [part[...].astype(F32) for part in parts], dkv_ref[...])
    grad, dgain = head_backward(
        total[:, :size] * factor, proj_ref[...], gain_ref[...], cos_ref[...], sin_ref[...]
    )
    grad_ref[:, :size] = grad.astype(LOW)
    grad_ref[:, size:] = total[:, size:].astype(LOW)
    dgain_ref[...] = dgain


def kv_back(context, dkv, parts, proj, gain, cos2, sin2, factor, others):
    block, size = proj.shape
    operands = [proj, gain[None], cos2, sin2]
    shapes = [
        jax.ShapeDtypeStruct((block, 2 * size), LOW),
        jax.ShapeDtypeStruct((1, size), F32),
    ]
    return pl.pallas_call(
        functools.partial(kv_back_kernel, factor, len(parts)),
        grid_spec=pltpu.PrefetchScalarGridSpec(
            num_scalar_prefetch=1,
            grid=(1,),
            in_specs=[pl.BlockSpec((block, 2 * size), lambda i, c: (c[0], 0))]
            + [full(part.shape) for part in parts]
            + [full(value.shape) for value in operands]
            + [pl.BlockSpec(memory_space=pl.ANY)] * len(others),
            out_specs=[full(shape.shape) for shape in shapes],
        ),
        out_shape=shapes,
        compiler_params=params(),
        cost_estimate=cost(40 * block * size, 5e6),
    )(context.astype(jnp.int32)[None], dkv, *parts, *operands, *others)


def dp_sum_kernel(d_ref, *refs):
    out_ref = refs[-1]
    first = 0
    for kept_ref, got_ref in zip(refs[:-1:2], refs[1:-1:2]):
        last = first + kept_ref.shape[1]
        total = kept_ref[...].astype(F32) + got_ref[...].astype(F32)
        out_ref[:, first:last] = total.astype(LOW)
        first = last


def dp_sum(d, pairs):
    rows = pairs[0][1].shape[0]
    columns = sum(got.shape[1] for _, got in pairs)
    tiles = 4
    tile = rows // tiles
    specs = []
    for _, got in pairs:
        wide = got.shape[1]
        specs.append(pl.BlockSpec((tile, wide), lambda i, d: (d[0] * tiles + i, 0)))
        specs.append(pl.BlockSpec((tile, wide), lambda i, d: (i, 0)))
    return pl.pallas_call(
        dp_sum_kernel,
        grid_spec=pltpu.PrefetchScalarGridSpec(
            num_scalar_prefetch=1,
            grid=(tiles,),
            in_specs=specs,
            out_specs=pl.BlockSpec((tile, columns), lambda i, d: (i, 0)),
        ),
        out_shape=jax.ShapeDtypeStruct((rows, columns), LOW),
        compiler_params=params(),
        cost_estimate=cost(rows * columns, 6 * rows * columns),
    )(d, *[value for pair in pairs for value in pair])


def part_sum_kernel(parts_ref, out_ref):
    total = parts_ref[0].astype(F32)
    for k in range(1, parts_ref.shape[0]):
        total += parts_ref[k].astype(F32)
    for k in range(out_ref.shape[0]):
        out_ref[k] = total.astype(LOW)


def part_sum(parts):
    count, rows, columns = parts.shape
    tiles = 4 if rows % 64 == 0 else 1
    spec = pl.BlockSpec((count, rows // tiles, columns), lambda i: (0, i, 0))
    return pl.pallas_call(
        part_sum_kernel,
        grid=(tiles,),
        in_specs=[spec],
        out_specs=spec,
        out_shape=jax.ShapeDtypeStruct(parts.shape, LOW),
        compiler_params=params(),
        cost_estimate=cost(count * rows * columns, 4 * count * rows * columns),
    )(parts)


def widen_kernel(d_ref, kept_ref, got_ref, *outs):
    first = 0
    for out_ref in outs:
        last = first + out_ref.shape[1]

        @pl.when(pl.program_id(0) == 0)
        def _():
            out_ref[...] = kept_ref[:, first:last].astype(F32)

        @pl.when(pl.program_id(0) == 1)
        def _():
            out_ref[...] = got_ref[:, first:last].astype(F32)

        first = last


def widen(d, kept, got, widths):
    rows, columns = kept.shape
    tiles = 4
    tile = rows // tiles
    return pl.pallas_call(
        widen_kernel,
        grid_spec=pltpu.PrefetchScalarGridSpec(
            num_scalar_prefetch=1,
            grid=(2, tiles),
            in_specs=[
                pl.BlockSpec((tile, columns), lambda i, j, d: (j * (1 - i) + (tiles - 1) * i, 0)),
                pl.BlockSpec((tile, columns), lambda i, j, d: (j * i, 0)),
            ],
            out_specs=[
                pl.BlockSpec(
                    (tile, wide), lambda i, j, d: ((d[0] + i - 2 * d[0] * i) * tiles + j, 0)
                )
                for wide in widths
            ],
        ),
        out_shape=[jax.ShapeDtypeStruct((2 * rows, wide), F32) for wide in widths],
        compiler_params=params(),
        cost_estimate=cost(2 * rows * columns, 12 * rows * columns),
    )(d, kept, got)


def sum_small(flat):
    n = lax.axis_size(ALL_AXES)
    length = flat.shape[0]
    each = -(-length // (n * 128)) * 128
    parts = jnp.pad(flat, (0, n * each - length)).reshape(n, each)
    parts = lax.all_to_all(parts, ALL_AXES, split_axis=0, concat_axis=0, tiled=True)
    own = jnp.sum(parts, axis=0, keepdims=True)
    whole = lax.all_to_all(
        jnp.broadcast_to(own, (n, each)), ALL_AXES, split_axis=0, concat_axis=0, tiled=True
    )
    return whole.reshape(-1)[:length]


def swap_dp(rows):
    return lax.ppermute(rows, "dp", [(0, 1), (1, 0)])


def swap_context(rows, s):
    n = lax.axis_size("context")
    return lax.ppermute(rows, "context", [(i, i ^ s) for i in range(n)])


def dp_got(grad):
    d = lax.axis_index("dp")
    rows = grad.shape[0] // 2
    return swap_dp(lax.dynamic_slice_in_dim(grad, (1 - d) * rows, rows))


def share_context(parts):
    return lax.all_to_all(parts, "context", split_axis=0, concat_axis=0, tiled=True)


def sum_groups(grads, gots, widths):
    n = lax.axis_size("context")
    d = lax.axis_index("dp").astype(jnp.int32)[None]
    half = dp_sum(d, list(zip(grads, gots)))
    rows, columns = half.shape
    parts = part_sum(share_context(half.reshape(n, rows // n, columns)))
    half = share_context(parts).reshape(rows, columns)
    return widen(d, half, swap_dp(half), widths)


def arrival_order(n):
    return [sorted(range(n), key=lambda j: (abs(j - i), j)) for i in range(n)]


def choose(index, options):
    distinct = []
    for option in options:
        if option is not None and not any(option is other for other in distinct):
            distinct.append(option)
    result = distinct[0]
    for option in distinct[1:]:
        mask = functools.reduce(
            jnp.logical_or, [index == i for i, other in enumerate(options) if other is option]
        )
        result = jnp.where(mask, option, result)
    return result


def line_gather(chunk):
    return line_steps({0: chunk}, 1, lax.axis_size("expert"))


def line_steps(found, first, stop):
    n = lax.axis_size("expert")
    found = dict(found)
    for s in range(first, stop):
        found[-s] = lax.ppermute(
            found[1 - s], "expert", [(i, i + 1) for i in range(s - 1, n - 1)]
        )
        found[s] = lax.ppermute(found[s - 1], "expert", [(i + 1, i) for i in range(n - s)])
    return found


def context_gather(rows):
    n = lax.axis_size("context")
    c = lax.axis_index("context")
    found = {0: rows}
    for s in range(1, n):
        found[s] = lax.ppermute(rows, "context", [(i, i ^ s) for i in range(n)])
    return jnp.concatenate([choose(c, [found[i ^ j] for i in range(n)]) for j in range(n)], axis=0)


def context_parts(rows):
    n = lax.axis_size("context")
    c = lax.axis_index("context")
    each = rows.shape[0] // n
    return [
        swap_context(lax.dynamic_slice_in_dim(rows, (c ^ s) * each, each).astype(LOW), s)
        for s in range(1, n)
    ]


def zero_of(*others):
    return functools.reduce(
        jnp.add,
        [
            lax.slice(other, (0,) * other.ndim, (1,) * other.ndim).reshape(()).astype(F32) * 0.0
            for other in others
        ],
    )


def after(value, *others):
    return (value.astype(F32) + zero_of(*others)).astype(value.dtype)


def on_device(
    layer_input,
    grad_output,
    attn_gain,
    query_weight,
    key_weight,
    value_weight,
    q_gain,
    k_gain,
    output_weight,
    mlp_gain,
    router,
    w_gate,
    w_up,
    w_down,
    routes,
    half_order,
):
    n_context = lax.axis_size("context")
    n_expert = lax.axis_size("expert")
    n_groups = lax.axis_size(GROUP_AXES)
    tok_dev, width = layer_input.shape[1:]
    size = q_gain.shape[0]
    kv_total = key_weight.shape[1] * n_expert
    group_dev = n_expert // (kv_total // size)
    kv_index = lax.axis_index("expert") // group_dev
    block = tok_dev * n_expert
    seq = block * n_context
    half = block // 2
    experts = router.shape[1]
    exp_dev = w_gate.shape[0]
    top = routes.shape[2]
    capacity = max(2, (tok_dev * top * 9 + 8 * experts - 1) // (8 * experts))
    scale = size ** (-0.5)

    seq_rows = jnp.arange(seq, dtype=jnp.int32)
    context = lax.axis_index("context")
    own_halves = lax.dynamic_slice_in_dim(half_order, 2 * context, 2)
    own_pos = (own_halves[:, None] * half + jnp.arange(half, dtype=jnp.int32)[None]).reshape(-1)
    per_half = half // TILE
    tile_pos = (half_order[:, None] * per_half + jnp.arange(per_half, dtype=jnp.int32)).reshape(-1)
    kidx = jnp.sum(
        (tile_pos[None, :] == jnp.arange(seq // TILE, dtype=jnp.int32)[:, None])
        * jnp.arange(seq // TILE, dtype=jnp.int32)[None, :],
        axis=1,
    ).astype(jnp.int32)
    qpos = lax.dynamic_slice_in_dim(tile_pos, context * (block // TILE), block // TILE)
    entry = jnp.arange(size)
    freq = jnp.power(THETA, -(2 * (entry % (size // 2))).astype(F32) / size)
    angles = own_pos.astype(F32)[:, None] * freq[None, :]
    cos2 = jnp.cos(angles)
    sin2 = jnp.sin(angles) * jnp.where(entry < size // 2, -1.0, 1.0)[None, :]

    place = lax.axis_index("expert")
    place_1 = place.astype(jnp.int32)[None]
    lanes = -(-2 * experts // 128) * 128
    mask = jnp.any(
        routes[0][:, :, None] == jnp.arange(lanes, dtype=jnp.int32)[None, None, :], axis=1
    )
    mask_wide = mask.astype(F32)
    router_rows = router.T

    x_low = layer_input[0]
    x_normal, _ = norm_parts(x_low.astype(F32))
    normed_found = line_gather((x_normal * attn_gain).astype(LOW))
    if group_dev == 1:
        kv_weights = jnp.concatenate([key_weight, value_weight], axis=1)
    else:
        key_whole = lax.all_gather(key_weight, "expert", axis=1, tiled=True)
        value_whole = lax.all_gather(value_weight, "expert", axis=1, tiled=True)
        kv_weights = jnp.concatenate(
            [
                lax.dynamic_slice_in_dim(key_whole, kv_index * size, size, 1),
                lax.dynamic_slice_in_dim(value_whole, kv_index * size, size, 1),
            ],
            axis=1,
        )
    grad_low = grad_output[0]
    normed_rows, own_kv, key_proj, grad_wide = project_keys(
        place_1,
        normed_found,
        kv_weights,
        k_gain,
        cos2,
        sin2,
        scale * LOG2E,
        grad_low,
        mask_wide,
    )
    grad_col = lax.all_gather(grad_wide, "expert", axis=0, tiled=True)
    kv_whole = context_gather(own_kv)
    queries, query_proj = project_queries(normed_rows, query_weight, q_gain, cos2, sin2)

    n_half = n_expert // 2
    order_here = jnp.asarray(arrival_order(n_expert), jnp.int32)[place]
    turn_here = jnp.sum(
        (order_here[:, None] == jnp.arange(n_expert, dtype=jnp.int32)[None, :])
        * jnp.arange(n_expert, dtype=jnp.int32)[:, None],
        axis=0,
    ).astype(jnp.int32)
    meta = jnp.concatenate([place_1, turn_here, order_here])
    grad_sent, spreads, back_tables = make_tables(
        meta, grad_col, width, n_groups, n_half, capacity, []
    )

    def swap_plane(rows):
        parts = rows.reshape(n_groups, -1, rows.shape[1])
        parts = lax.all_to_all(parts, GROUP_AXES, split_axis=0, concat_axis=0, tiled=True)
        return parts.reshape(rows.shape)

    attended, inverse = attend(qpos, kidx, queries, kv_whole, [])
    attn_part = (dot_nn(attended, output_weight) + zero_of(grad_sent)).astype(LOW)
    attn_rows = lax.psum_scatter(attn_part, "expert", scatter_dimension=0, tiled=True)

    grad_x = swap_plane(grad_sent)
    act_pull = dot_nt(grad_x, w_down[0]).reshape(n_groups, 2, n_half * capacity, -1)

    hidden, mixed, probs = route_rows(
        x_low, attn_rows, mlp_gain, router_rows, mask_wide, experts, []
    )

    who = (lax.axis_index(ALL_AXES) * exp_dev).astype(jnp.int32)[None]
    mixed_found = line_gather(mixed)
    near = spread_rows(place_1, spreads[0], mixed_found, range(n_half), [grad_x])
    x_near = swap_plane(near)
    worked_near = run_expert(who, x_near, w_gate[0], w_up[0], act_pull, 0, experts)
    far = spread_rows(place_1, spreads[1], mixed_found, range(n_half, n_expert), [x_near])
    x_far = swap_plane(far)
    worked_far = run_expert(who, x_far, w_gate[0], w_up[0], act_pull, 1, experts)
    xs = [x_near, x_far]
    acts, gate_lows, up_lows, copies = (list(pair) for pair in zip(worked_near, worked_far))
    back_far = swap_plane(copies[1])
    back_near = swap_plane(copies[0])
    join = lambda parts: jnp.concatenate(parts, axis=0)
    x_all = join([x[:, :width] for x in xs])
    grad_w_gate = dot_tn(x_all, join(gate_lows))
    grad_w_up = dot_tn(x_all, join(up_lows))
    grad_by_round = jnp.swapaxes(
        grad_x.reshape(n_groups, 2, n_half * capacity, width), 0, 1
    ).reshape(-1, width)
    grad_w_down = dot_tn(join(acts), grad_by_round)
    copies_col = combine_rows(
        meta, back_tables, [back_near, back_far], n_half, [grad_w_gate, grad_w_up]
    )
    copies_sum = lax.psum_scatter(copies_col, "expert", scatter_dimension=0, tiled=True)

    returned = [dot_nn(act, w_down[0]).astype(LOW) for act in acts]
    returned_near = swap_plane(returned[0])

    grad_hidden, grad_hidden_low, grad_mlp_gain, grad_router = route_back(
        copies_sum,
        grad_low,
        hidden,
        mlp_gain,
        router_rows,
        mask_wide,
        probs,
        experts,
        [returned_near, grad_w_down],
    )

    returned_far = swap_plane(returned[1])
    grad_attn = lax.all_gather(grad_hidden_low, "expert", axis=0, tiled=True)
    grad_o, centre = grad_attended(
        grad_attn, output_weight, attended, inverse, [returned_far]
    )
    grad_w_out = lax.psum(token_dot(attended, grad_attn, []), GROUP_AXES)
    grad_kv, grad_q, grad_q_gain = attend_back(
        qpos, kidx, queries, grad_o, centre, kv_whole, query_proj, q_gain, cos2, sin2
    )
    kv_parts = context_parts(grad_kv)
    w_query = token_dot(normed_rows, grad_q, [])
    w_query_got = dp_got(w_query)

    kv_grads, grad_k_gain = kv_back(
        context, grad_kv, kv_parts, key_proj, k_gain, cos2, sin2, scale, []
    )
    grad_normed = dot_nt(grad_q, query_weight) + dot_nt(kv_grads, kv_weights)
    grad_attn_gain = jnp.sum(grad_normed * normed_rows.astype(F32), axis=0) / attn_gain
    grad_normed = lax.psum_scatter(
        grad_normed.astype(LOW), "expert", scatter_dimension=0, tiled=True
    )
    grad_input = input_back(grad_normed, x_low, attn_gain, grad_hidden)

    combined = combine_rows(
        meta, back_tables, [returned_near, returned_far], n_half, [grad_normed]
    )
    output_rows = hidden + lax.psum_scatter(
        combined, "expert", scatter_dimension=0, tiled=True
    ).astype(F32)

    grad_w_out = grad_w_out.astype(F32)
    w_kv = token_dot(normed_rows, kv_grads, [])
    if group_dev == 1:
        half_width = key_weight.shape[1]
        grad_w_query, grad_w_key, grad_w_value = sum_groups(
            [w_query, w_kv],
            [w_query_got, dp_got(w_kv)],
            [query_weight.shape[1], half_width, half_width],
        )
    else:
        (grad_w_query,) = sum_groups([w_query], [w_query_got], [query_weight.shape[1]])
        blank = jnp.zeros((width, kv_total), LOW)
        pieces = []
        for part in (w_kv[:, :size], w_kv[:, size:]):
            padded = lax.dynamic_update_slice(blank, part, (0, kv_index * size))
            pieces.append(lax.psum_scatter(padded, "expert", scatter_dimension=1, tiled=True))
        grad_w_key, grad_w_value = (lax.psum(piece, GROUP_AXES).astype(F32) for piece in pieces)

    small = [
        grad_attn_gain,
        grad_mlp_gain[0],
        grad_q_gain[0],
        grad_k_gain[0],
        grad_router[:experts].reshape(-1),
    ]
    summed = sum_small(jnp.concatenate(small))
    pieces = []
    offset = 0
    for part in small:
        pieces.append(summed[offset : offset + part.shape[0]])
        offset += part.shape[0]
    grad_attn_gain, grad_mlp_gain, grad_q_gain, grad_k_gain, grad_router = pieces
    return (
        output_rows.astype(LOW)[None],
        grad_input[None],
        grad_attn_gain,
        grad_w_query,
        grad_w_key,
        grad_w_value,
        grad_q_gain,
        grad_k_gain,
        grad_w_out,
        grad_mlp_gain,
        grad_router.reshape(experts, width).T,
        grad_w_gate[None],
        grad_w_up[None],
        grad_w_down[None],
    )


def solution(mesh):
    rows = P("dp", ("context", "expert"), None)
    expert = P(ALL_AXES, None, None)
    columns = P(None, "expert")
    in_specs = (
        rows,
        rows,
        P(),
        columns,
        columns,
        columns,
        P(),
        P(),
        P("expert", None),
        P(),
        P(),
        expert,
        expert,
        expert,
        rows,
        P(),
    )
    out_specs = (
        rows,
        rows,
        P(),
        columns,
        columns,
        columns,
        P(),
        P(),
        P("expert", None),
        P(),
        P(),
        expert,
        expert,
        expert,
    )
    return jax.shard_map(
        on_device, mesh=mesh, in_specs=in_specs, out_specs=out_specs, check_vma=False
    )
```

```python
import functools
import math

import jax
import jax.numpy as jnp
from jax import lax
from jax.experimental import pallas as pl
from jax.experimental.pallas import tpu as pltpu
from jax.sharding import PartitionSpec as P

EPS = 1e-06
THETA = 1000000.0
TILE = 256
VMEM_BYTES = 56 * 1024 * 1024
LOG2E = math.log2(math.e)
LOW = jnp.bfloat16
F32 = jnp.float32
ALL_AXES = ("dp", "context", "expert")
GROUP_AXES = ("dp", "context")


def dot_nn(a, b):
    return lax.dot_general(a, b, (((1,), (0,)), ((), ())), preferred_element_type=F32)


def dot_nt(a, b):
    return lax.dot_general(a, b, (((1,), (1,)), ((), ())), preferred_element_type=F32)


def dot_tn(a, b):
    return lax.dot_general(a, b, (((0,), (0,)), ((), ())), preferred_element_type=F32)


def params(**more):
    return pltpu.CompilerParams(vmem_limit_bytes=VMEM_BYTES, **more)


def cost(flops, nbytes, exps=0):
    return pl.CostEstimate(flops=int(flops), bytes_accessed=int(nbytes), transcendentals=int(exps))


def head_forward(u, gain, cos2, sin2):
    rr = lax.rsqrt(jnp.mean(u * u, axis=-1, keepdims=True) + EPS)
    y = u * rr * gain
    return y * cos2 + pltpu.roll(y, 64, 1) * sin2


def head_backward(gy, u, gain, cos2, sin2):
    g = gy * cos2 - pltpu.roll(gy, 64, 1) * sin2
    rr = lax.rsqrt(jnp.mean(u * u, axis=-1, keepdims=True) + EPS)
    n = u * rr
    gn = g * gain
    grad = rr * (gn - n * jnp.mean(gn * n, axis=-1, keepdims=True))
    return grad, jnp.sum(g * n, axis=0, keepdims=True)


def query_kernel(x_ref, w_ref, gain_ref, cos_ref, sin_ref, rot_ref, proj_ref):
    tiles, heads, rows, size = rot_ref.shape
    acc = dot_nn(x_ref[...], w_ref[...])
    for h in range(heads):
        u = acc[:, h * size : (h + 1) * size]
        rot = head_forward(u, gain_ref[...], cos_ref[...], sin_ref[...])
        proj_ref[:, h] = u.reshape(tiles, rows, size)
        rot_ref[:, h] = rot.astype(LOW).reshape(tiles, rows, size)


def project_queries(normed, weight, gain, cos2, sin2):
    block, width = normed.shape
    size = cos2.shape[1]
    heads = weight.shape[1] // size
    tiles = block // TILE
    whole = lambda i: (0, 0)
    per = lambda i: (0, i, 0, 0)
    shape = (tiles, heads, TILE, size)
    return pl.pallas_call(
        query_kernel,
        grid=(heads // 2,),
        in_specs=[
            pl.BlockSpec((block, width), whole),
            pl.BlockSpec((width, 2 * size), lambda i: (0, i)),
            pl.BlockSpec((1, size), whole),
            pl.BlockSpec((block, size), whole),
            pl.BlockSpec((block, size), whole),
        ],
        out_specs=[pl.BlockSpec((tiles, 2, TILE, size), per)] * 2,
        out_shape=[jax.ShapeDtypeStruct(shape, LOW), jax.ShapeDtypeStruct(shape, F32)],
        compiler_params=params(),
        cost_estimate=cost(2 * block * width * heads * size, 12e6),
    )(normed, weight, gain[None], cos2, sin2)


def put_in_order(place, refs, out_ref):
    n = (len(refs) + 1) // 2
    rows = refs[0].shape[0]
    for distance in range(1 - n, n):
        ref = refs[distance + n - 1]
        at = place + distance

        @pl.when(jnp.logical_and(at >= 0, at < n))
        def _():
            out_ref[pl.ds(pl.multiple_of(at * rows, rows), rows), :] = ref[...]


def chunk_list(found):
    n = (len(found) + 1) // 2
    return [found[distance] for distance in range(1 - n, n)]


def key_kernel(factor, n_chunks, place_ref, *refs):
    w_ref, gain_ref, cos_ref, sin_ref, g_ref, mask_ref = refs[n_chunks:-4]
    rows_ref, kv_ref, proj_ref, wide_ref = refs[-4:]
    size = proj_ref.shape[1]
    width = g_ref.shape[1]
    put_in_order(place_ref[0], refs[:n_chunks], rows_ref)
    wide_ref[:, :width] = g_ref[...]
    wide_ref[:, width:] = mask_ref[...].astype(LOW)
    acc = dot_nn(rows_ref[...], w_ref[...])
    u = acc[:, :size]
    rot = head_forward(u, gain_ref[...], cos_ref[...], sin_ref[...])
    proj_ref[...] = u
    kv_ref[:, :size] = (rot * factor).astype(LOW)
    kv_ref[:, size:] = acc[:, size:].astype(LOW)


def full(shape):
    return pl.BlockSpec(shape, lambda *_: (0,) * len(shape))


def project_keys(place, found, weight, gain, cos2, sin2, factor, g, mask):
    chunks = chunk_list(found)
    rows, width = chunks[0].shape
    block, size = cos2.shape
    operands = [*chunks, weight, gain[None], cos2, sin2, g, mask]
    shapes = [
        jax.ShapeDtypeStruct((block, width), LOW),
        jax.ShapeDtypeStruct((block, 2 * size), LOW),
        jax.ShapeDtypeStruct((block, size), F32),
        jax.ShapeDtypeStruct((rows, width + mask.shape[1]), LOW),
    ]
    return pl.pallas_call(
        functools.partial(key_kernel, factor, len(chunks)),
        grid_spec=pltpu.PrefetchScalarGridSpec(
            num_scalar_prefetch=1,
            grid=(1,),
            in_specs=[full(x.shape) for x in operands],
            out_specs=[full(x.shape) for x in shapes],
        ),
        out_shape=shapes,
        compiler_params=params(),
        cost_estimate=cost(4 * block * width * size, 8e6),
    )(place, *operands)


def in_order(last, step):
    lax.fori_loop(0, lax.div(last, 2), lambda p, c: (step([2 * p, 2 * p + 1], False), c)[1], 0)

    @pl.when(lax.rem(last, 2) == 1)
    def _():
        step([last - 1, last], True)

    @pl.when(lax.rem(last, 2) == 0)
    def _():
        step([last], True)


def attend_kernel(qpos_ref, kidx_ref, q_ref, kv_ref, *rest):
    out_ref, inv_ref, acc_ref = rest[-3:]
    heads, rows, size = q_ref.shape[1:]
    acc_ref[...] = jnp.zeros_like(acc_ref)

    def step(places, masked):
        starts = [pl.multiple_of(kidx_ref[place] * rows, rows) for place in places]
        count = len(places) * rows
        keys = jnp.concatenate([kv_ref[pl.ds(start, rows), :size] for start in starts], axis=0)
        values = jnp.concatenate([kv_ref[pl.ds(start, rows), size:] for start in starts], axis=0)
        values = jnp.concatenate([values, jnp.ones((count, size), LOW)], axis=1)
        for h in range(heads):
            e = jnp.exp2(dot_nt(q_ref[0, h], keys))
            if masked:
                qi = lax.broadcasted_iota(jnp.int32, e.shape, 0)
                ki = lax.broadcasted_iota(jnp.int32, e.shape, 1) - (count - rows)
                e = jnp.where(ki <= qi, e, 0.0)
            acc_ref[h] += dot_nn(e.astype(LOW), values)

    in_order(qpos_ref[pl.program_id(0)], step)
    for h in range(heads):
        inv = 1.0 / acc_ref[h, :, size:]
        inv_ref[0, h] = inv
        out_ref[:, h * size : (h + 1) * size] = (acc_ref[h, :, :size] * inv).astype(LOW)


def attend(qpos, kidx, queries, kv, others):
    tiles, heads, rows, size = queries.shape
    seq = kv.shape[0]
    return pl.pallas_call(
        attend_kernel,
        grid_spec=pltpu.PrefetchScalarGridSpec(
            num_scalar_prefetch=2,
            grid=(tiles,),
            in_specs=[
                pl.BlockSpec((1, heads, rows, size), lambda i, a, b: (i, 0, 0, 0)),
                pl.BlockSpec((seq, 2 * size), lambda i, a, b: (0, 0)),
            ]
            + [pl.BlockSpec(memory_space=pl.ANY)] * len(others),
            out_specs=[
                pl.BlockSpec((rows, heads * size), lambda i, a, b: (i, 0)),
                pl.BlockSpec((1, heads, rows, size), lambda i, a, b: (i, 0, 0, 0)),
            ],
            scratch_shapes=[pltpu.VMEM((heads, rows, 2 * size), F32)],
        ),
        out_shape=[
            jax.ShapeDtypeStruct((tiles * rows, heads * size), LOW),
            jax.ShapeDtypeStruct((tiles, heads, rows, size), F32),
        ],
        compiler_params=params(),
        cost_estimate=cost(
            6 * tiles * rows * heads * seq * size, 8e6, tiles * rows * heads * seq
        ),
    )(qpos, kidx, queries, kv, *others)


def grad_out_kernel(rows_ref, w_ref, o_ref, inv_ref, *rest):
    do_ref, centre_ref = rest[-2:]
    tiles, heads, rows, size = do_ref.shape
    acc = dot_nt(rows_ref[...], w_ref[...])
    for t in range(tiles):
        for h in range(heads):
            part = slice(t * rows, (t + 1) * rows), slice(h * size, (h + 1) * size)
            low = (acc[part] * inv_ref[t, h]).astype(LOW)
            do_ref[t, h] = low
            product = low.astype(F32) * o_ref[part].astype(F32)
            centre = jnp.sum(jnp.transpose(product), axis=0, keepdims=True)
            centre_ref[t, h] = jnp.broadcast_to(centre, (8, rows))


def grad_attended(grad_rows, weight, attended, inverse, others):
    tiles, heads, rows, size = inverse.shape
    block, width = grad_rows.shape
    return pl.pallas_call(
        grad_out_kernel,
        grid=(heads // 2,),
        in_specs=[
            pl.BlockSpec((block, width), lambda i: (0, 0)),
            pl.BlockSpec((2 * size, width), lambda i: (i, 0)),
            pl.BlockSpec((block, 2 * size), lambda i: (0, i)),
            pl.BlockSpec((tiles, 2, rows, size), lambda i: (0, i, 0, 0)),
        ]
        + [pl.BlockSpec(memory_space=pl.ANY)] * len(others),
        out_specs=[
            pl.BlockSpec((tiles, 2, rows, size), lambda i: (0, i, 0, 0)),
            pl.BlockSpec((tiles, 2, 8, rows), lambda i: (0, i, 0, 0)),
        ],
        out_shape=[
            jax.ShapeDtypeStruct((tiles, heads, rows, size), LOW),
            jax.ShapeDtypeStruct((tiles, heads, 8, rows), F32),
        ],
        compiler_params=params(),
        cost_estimate=cost(2 * block * width * heads * size, 12e6),
    )(grad_rows, weight, attended, inverse, *others)


def attend_back_kernel(
    qpos_ref,
    kidx_ref,
    q_ref,
    do_ref,
    centre_ref,
    kv_ref,
    proj_ref,
    gain_ref,
    cos_ref,
    sin_ref,
    *rest,
):
    dkv_ref, dq_ref, dgain_ref, acc_ref, e_ref, ds_ref = rest[-6:]
    heads, rows, size = q_ref.shape[1:]

    @pl.when(pl.program_id(0) == 0)
    def _():
        dkv_ref[...] = jnp.zeros_like(dkv_ref)
        dgain_ref[...] = jnp.zeros_like(dgain_ref)

    acc_ref[...] = jnp.zeros_like(acc_ref)

    def step(places, masked):
        starts = [pl.multiple_of(kidx_ref[place] * rows, rows) for place in places]
        count = len(places) * rows
        keys = jnp.concatenate([kv_ref[pl.ds(start, rows), :size] for start in starts], axis=0)
        values = jnp.concatenate([kv_ref[pl.ds(start, rows), size:] for start in starts], axis=0)
        for h in range(heads):
            query, grad = q_ref[0, h], do_ref[0, h]
            e = jnp.exp2(dot_nt(keys, query))
            if masked:
                ki = lax.broadcasted_iota(jnp.int32, e.shape, 0) - (count - rows)
                qi = lax.broadcasted_iota(jnp.int32, e.shape, 1)
                e = jnp.where(ki <= qi, e, 0.0)
            ds = (e * (dot_nt(values, grad) - centre_ref[0, h, 0:1])).astype(LOW)
            e_ref[:count, h * rows : (h + 1) * rows] = e.astype(LOW)
            ds_ref[:count, h * rows : (h + 1) * rows] = ds
            acc_ref[h] += dot_tn(ds, keys)
        dk = dot_nn(ds_ref[:count], q_ref[0].reshape(heads * rows, size))
        dv = dot_nn(e_ref[:count], do_ref[0].reshape(heads * rows, size))
        for k, start in enumerate(starts):
            dkv_ref[pl.ds(start, rows), :size] += dk[k * rows : (k + 1) * rows]
            dkv_ref[pl.ds(start, rows), size:] += dv[k * rows : (k + 1) * rows]

    in_order(qpos_ref[pl.program_id(0)], step)
    total = jnp.zeros((1, size), F32)
    for h in range(heads):
        grad, gain_part = head_backward(
            acc_ref[h] * (1.0 / LOG2E), proj_ref[0, h], gain_ref[...], cos_ref[...], sin_ref[...]
        )
        dq_ref[:, h * size : (h + 1) * size] = grad.astype(LOW)
        total += gain_part
    dgain_ref[...] += total


def attend_back(qpos, kidx, queries, grads, centre, kv, proj, gain, cos2, sin2, others):
    tiles, heads, rows, size = queries.shape
    seq = kv.shape[0]
    per = pl.BlockSpec((1, heads, rows, size), lambda i, a, b: (i, 0, 0, 0))
    flat = lambda i, a, b: (0, 0)
    rowwise = lambda i, a, b: (i, 0)
    return pl.pallas_call(
        attend_back_kernel,
        grid_spec=pltpu.PrefetchScalarGridSpec(
            num_scalar_prefetch=2,
            grid=(tiles,),
            in_specs=[
                per,
                per,
                pl.BlockSpec((1, heads, 8, rows), lambda i, a, b: (i, 0, 0, 0)),
                pl.BlockSpec((seq, 2 * size), flat),
                per,
                pl.BlockSpec((1, size), flat),
                pl.BlockSpec((rows, size), rowwise),
                pl.BlockSpec((rows, size), rowwise),
            ]
            + [pl.BlockSpec(memory_space=pl.ANY)] * len(others),
            out_specs=[
                pl.BlockSpec((seq, 2 * size), flat),
                pl.BlockSpec((rows, heads * size), rowwise),
                pl.BlockSpec((1, size), flat),
            ],
            scratch_shapes=[pltpu.VMEM((heads, rows, size), F32)]
            + [pltpu.VMEM((2 * rows, heads * rows), LOW)] * 2,
        ),
        out_shape=[
            jax.ShapeDtypeStruct((seq, 2 * size), F32),
            jax.ShapeDtypeStruct((tiles * rows, heads * size), LOW),
            jax.ShapeDtypeStruct((1, size), F32),
        ],
        compiler_params=params(),
        cost_estimate=cost(
            15 * tiles * rows * heads * seq * size, 12e6, tiles * rows * heads * seq
        ),
    )(qpos, kidx, queries, grads, centre, kv, proj, gain[None], cos2, sin2, *others)


def token_kernel(a_ref, b_ref, *rest):
    rest[-1][...] = dot_tn(a_ref[...], b_ref[...]).astype(LOW)


def token_dot(a, b, others):
    block, rows = a.shape
    columns = b.shape[1]
    tile = min(rows, 512)
    return pl.pallas_call(
        token_kernel,
        grid=(rows // tile,),
        in_specs=[
            pl.BlockSpec((block, tile), lambda i: (0, i)),
            pl.BlockSpec((block, columns), lambda i: (0, 0)),
        ]
        + [pl.BlockSpec(memory_space=pl.ANY)] * len(others),
        out_specs=pl.BlockSpec((tile, columns), lambda i: (i, 0)),
        out_shape=jax.ShapeDtypeStruct((rows, columns), LOW),
        compiler_params=params(),
        cost_estimate=cost(2 * block * rows * columns, 6e6),
    )(a, b, *others)


def split_low(value):
    high = value.astype(LOW)
    return high, (value - high.astype(F32)).astype(LOW)


def norm_parts(rows):
    rr = lax.rsqrt(jnp.mean(rows * rows, axis=-1, keepdims=True) + EPS)
    return rows * rr, rr


def norm_back(grad, normal, rr, gain):
    weighted = grad * gain
    return rr * (weighted - normal * jnp.mean(weighted * normal, axis=-1, keepdims=True))


def add_all(refs):
    return functools.reduce(jnp.add, [ref[...].astype(F32) for ref in refs])


def pad_rows(rows, count):
    if rows.shape[0] == count:
        return rows
    return jnp.concatenate(
        [rows, jnp.zeros((count - rows.shape[0], rows.shape[1]), rows.dtype)], axis=0
    )


def router_kernel(experts, *refs):
    x_ref, attn_ref, gain_ref, router_ref, mask_ref = refs[:5]
    hidden_ref, mixed_ref, probs_ref = refs[-3:]
    width = x_ref.shape[1]
    lanes = mask_ref.shape[1]
    hidden = add_all([x_ref, attn_ref])
    hidden_ref[...] = hidden
    mixed = (norm_parts(hidden)[0] * gain_ref[...]).astype(LOW)
    mixed_ref[:, :width] = mixed
    logits = dot_nt(mixed, pad_rows(router_ref[...], lanes))
    lane = lax.broadcasted_iota(jnp.int32, logits.shape, 1)
    logits = jnp.where(lane < experts, logits, -1e30)
    weights = jnp.exp(logits - jnp.max(logits, axis=1, keepdims=True))
    probs = weights / jnp.sum(weights, axis=1, keepdims=True)
    probs_ref[...] = probs
    chosen = probs * mask_ref[...]
    high, low = split_low(chosen / jnp.sum(chosen, axis=1, keepdims=True))
    both = high.astype(F32) + pltpu.roll(low.astype(F32), experts, 1)
    mixed_ref[:, width:] = both.astype(LOW)


def route_rows(x, attn, gain, router, mask, experts, others):
    tokens, width = x.shape
    lanes = mask.shape[1]
    operands = [x, attn, gain[None], router, mask]
    shapes = [
        jax.ShapeDtypeStruct((tokens, width), F32),
        jax.ShapeDtypeStruct((tokens, width + lanes), LOW),
        jax.ShapeDtypeStruct((tokens, lanes), F32),
    ]
    return pl.pallas_call(
        functools.partial(router_kernel, experts),
        grid=(1,),
        in_specs=[full(value.shape) for value in operands]
        + [pl.BlockSpec(memory_space=pl.ANY)] * len(others),
        out_specs=[full(shape.shape) for shape in shapes],
        out_shape=shapes,
        compiler_params=params(),
        cost_estimate=cost(2 * tokens * width * lanes, 5e6),
    )(*operands, *others)


def table_kernel(capacity, n_half, meta_ref, col_ref, *rest):
    rows_ref, near_ref, far_ref, near_back_ref, far_back_ref, slots_ref = rest[-6:]
    block = col_ref.shape[0]
    rows, width = rows_ref.shape
    n = 2 * n_half
    tokens = block // n
    cap_half = n_half * capacity
    groups = rows // (2 * cap_half)
    mask = col_ref[:, width:]
    lanes = mask.shape[1]
    padded = -(-groups // 16) * 16
    group = lax.broadcasted_iota(jnp.int32, (padded, lanes), 0)
    lane = lax.broadcasted_iota(jnp.int32, (padded, lanes), 1)
    wanted = jnp.logical_and(lane == group * n + meta_ref[0], group < groups)
    hits = dot_nt(jnp.where(wanted, 1.0, 0.0).astype(LOW), mask)
    before = lax.broadcasted_iota(jnp.int32, (tokens, tokens), 0)
    after_it = lax.broadcasted_iota(jnp.int32, (tokens, tokens), 1)
    earlier = jnp.where(before < after_it, 1.0, 0.0).astype(LOW)
    for z in range(n):
        hit = hits[:, z * tokens : (z + 1) * tokens]
        rank = dot_nn(hit.astype(LOW), earlier)
        turn = (meta_ref[1 + z] * capacity).astype(F32)
        slot = jnp.where(hit > 0.5, rank + turn, -1.0)
        slots_ref[:, z * tokens : (z + 1) * tokens] = slot[:groups]

    def one_hot(slots, count, first):
        slot = lax.broadcasted_iota(jnp.int32, (groups, count, slots.shape[1]), 1).astype(F32)
        same = slots[:, None, :] == slot + float(first)
        return jnp.where(same, 1.0, 0.0).reshape(groups * count, slots.shape[1])

    spread = one_hot(slots_ref[...], 2 * cap_half, 0).astype(LOW)
    rows_ref[...] = dot_nn(spread, col_ref[:, :width]).astype(LOW)
    for part, (to_ref, back_ref) in enumerate([(near_ref, near_back_ref), (far_ref, far_back_ref)]):
        pieces = []
        for k in range(n_half):
            start = pl.multiple_of(meta_ref[1 + n + part * n_half + k] * tokens, tokens)
            pieces.append(slots_ref[:, pl.ds(start, tokens)])
        spread = one_hot(jnp.concatenate(pieces, axis=1), cap_half, part * cap_half)
        to_ref[...] = spread.astype(LOW)
        back_ref[...] = jnp.transpose(spread).astype(LOW)


def make_tables(meta, col, width, groups, n_half, capacity, others):
    block = col.shape[0]
    rows = groups * n_half * capacity
    shapes = (
        [jax.ShapeDtypeStruct((2 * rows, width), LOW)]
        + [jax.ShapeDtypeStruct((rows, block // 2), LOW)] * 2
        + [jax.ShapeDtypeStruct((block // 2, rows), LOW)] * 2
    )
    outs = pl.pallas_call(
        functools.partial(table_kernel, capacity, n_half),
        grid_spec=pltpu.PrefetchScalarGridSpec(
            num_scalar_prefetch=1,
            grid=(1,),
            in_specs=[full(col.shape)] + [pl.BlockSpec(memory_space=pl.ANY)] * len(others),
            out_specs=[full(shape.shape) for shape in shapes],
            scratch_shapes=[pltpu.VMEM((groups, block), F32)],
        ),
        out_shape=shapes,
        compiler_params=params(),
        cost_estimate=cost(4 * rows * block * width, 12e6),
    )(meta, col, *others)
    return outs[0], outs[1:3], outs[3:]


def spread_kernel(choices, place_ref, spread_ref, *refs):
    out_ref, rows_ref = refs[-2:]
    for k, by_place in enumerate(choices):
        for which in sorted(set(by_place)):
            hit = functools.reduce(
                jnp.logical_or,
                [place_ref[0] == i for i, other in enumerate(by_place) if other == which],
            )

            @pl.when(hit)
            def _():
                tokens = refs[which].shape[0]
                rows_ref[k * tokens : (k + 1) * tokens] = refs[which][...]

    out_ref[...] = dot_nn(spread_ref[...], rows_ref[...]).astype(LOW)


def spread_rows(place, spread, found, turns, others):
    n = lax.axis_size("expert")
    order = arrival_order(n)
    distances = sorted({order[i][turn] - i for i in range(n) for turn in turns})
    choices = [[distances.index(order[i][turn] - i) for i in range(n)] for turn in turns]
    chunks = [found[distance] for distance in distances]
    tokens, wide = chunks[0].shape
    rows = spread.shape[0]
    return pl.pallas_call(
        functools.partial(spread_kernel, choices),
        grid_spec=pltpu.PrefetchScalarGridSpec(
            num_scalar_prefetch=1,
            grid=(1,),
            in_specs=[full(spread.shape)]
            + [full(chunk.shape) for chunk in chunks]
            + [pl.BlockSpec(memory_space=pl.ANY)] * len(others),
            out_specs=full((rows, wide)),
            scratch_shapes=[pltpu.VMEM((len(turns) * tokens, wide), LOW)],
        ),
        out_shape=jax.ShapeDtypeStruct((rows, wide), LOW),
        compiler_params=params(),
        cost_estimate=cost(2 * rows * len(turns) * tokens * wide, 5e6),
    )(place, spread, *chunks, *others)


def router_back_kernel(experts, *refs):
    sum_ref, g_ref, hidden_ref, gain_ref, router_ref, mask_ref, probs_ref = refs[:7]
    grad_ref, low_ref, dgain_ref, drouter_ref = refs[-4:]
    width = g_ref.shape[1]
    lanes = mask_ref.shape[1]
    total = sum_ref[...].astype(F32)
    table = total[:, width:]
    mask, probs = mask_ref[...], probs_ref[...]
    grad_gates = (table + pltpu.roll(table, lanes - experts, 1)) * mask
    chosen = probs * mask
    chosen_sum = jnp.sum(chosen, axis=1, keepdims=True)
    mean = jnp.sum(grad_gates * (chosen / chosen_sum), axis=1, keepdims=True)
    centred = mask * (grad_gates - mean) / chosen_sum
    grad_logits = probs * (centred - jnp.sum(centred * chosen, axis=1, keepdims=True))
    high, low = split_low(grad_logits)
    router = pad_rows(router_ref[...], lanes)
    grad = total[:, :width] + dot_nn(high, router) + dot_nn(low, router)
    normal, rr = norm_parts(hidden_ref[...])
    mixed = (normal * gain_ref[...]).astype(LOW)
    drouter_ref[...] = dot_tn(high, mixed) + dot_tn(low, mixed)
    dgain_ref[...] = jnp.sum(grad * normal, axis=0, keepdims=True)
    grad_hidden = g_ref[...].astype(F32) + norm_back(grad, normal, rr, gain_ref[...])
    grad_ref[...] = grad_hidden
    low_ref[...] = grad_hidden.astype(LOW)


def route_back(summed, g, hidden, gain, router, mask, probs, experts, others):
    tokens, width = g.shape
    lanes = mask.shape[1]
    operands = [summed, g, hidden, gain[None], router, mask, probs]
    shapes = [
        jax.ShapeDtypeStruct((tokens, width), F32),
        jax.ShapeDtypeStruct((tokens, width), LOW),
        jax.ShapeDtypeStruct((1, width), F32),
        jax.ShapeDtypeStruct((lanes, width), F32),
    ]
    return pl.pallas_call(
        functools.partial(router_back_kernel, experts),
        grid=(1,),
        in_specs=[full(value.shape) for value in operands]
        + [pl.BlockSpec(memory_space=pl.ANY)] * len(others),
        out_specs=[full(shape.shape) for shape in shapes],
        out_shape=shapes,
        compiler_params=params(),
        cost_estimate=cost(8 * tokens * width * lanes, 8e6),
    )(*operands, *others)


def combine_kernel(n_half, meta_ref, near_table_ref, far_table_ref, near_ref, far_ref, *rest):
    del meta_ref
    turn = pl.program_id(0)

    @pl.when(turn < n_half)
    def _():
        rest[-1][...] = dot_nn(near_table_ref[...], near_ref[...]).astype(LOW)

    @pl.when(turn >= n_half)
    def _():
        rest[-1][...] = dot_nn(far_table_ref[...], far_ref[...]).astype(LOW)


def combine_rows(meta, tables, rows, n_half, others):
    tokens = tables[0].shape[0] // n_half
    slots, wide = rows[0].shape
    n = 2 * n_half
    return pl.pallas_call(
        functools.partial(combine_kernel, n_half),
        grid_spec=pltpu.PrefetchScalarGridSpec(
            num_scalar_prefetch=1,
            grid=(n,),
            in_specs=[
                pl.BlockSpec((tokens, slots), lambda i, m: (jnp.minimum(i, n_half - 1), 0)),
                pl.BlockSpec((tokens, slots), lambda i, m: (jnp.maximum(i - n_half, 0), 0)),
            ]
            + [full(value.shape) for value in rows]
            + [pl.BlockSpec(memory_space=pl.ANY)] * len(others),
            out_specs=pl.BlockSpec((tokens, wide), lambda i, m: (m[1 + n + i], 0)),
        ),
        out_shape=jax.ShapeDtypeStruct((n * tokens, wide), LOW),
        compiler_params=params(),
        cost_estimate=cost(2 * slots * n * tokens * wide, 10e6),
    )(meta, *tables, *rows, *others)


def expert_kernel(experts, who_ref, x_ref, gate_ref, up_ref, pull_ref, *rest):
    act_ref, dgate_ref, dup_ref, copy_ref = rest[-4:]
    width = gate_ref.shape[0]
    x = x_ref[:, :width]
    table = x_ref[:, width:].astype(F32)
    lane = lax.broadcasted_iota(jnp.int32, table.shape, 1)
    mine = who_ref[0]
    gate = jnp.sum(
        jnp.where(jnp.logical_or(lane == mine, lane == mine + experts), table, 0.0),
        axis=1,
        keepdims=True,
    )
    pre_gate = dot_nn(x, gate_ref[...])
    pre_up = dot_nn(x, up_ref[...])
    pull = pull_ref[...].reshape(pre_up.shape)
    sig = 1.0 / (1.0 + jnp.exp(-pre_gate))
    silu = pre_gate * sig
    act = silu * pre_up
    act_ref[...] = (act * gate).astype(LOW)
    high, low = split_low(jnp.sum(act * pull, axis=1, keepdims=True))
    pull = pull * gate
    dup = (pull * silu).astype(LOW)
    dgate = (pull * pre_up * (sig * (1.0 + pre_gate * (1.0 - sig)))).astype(LOW)
    dgate_ref[...] = dgate
    dup_ref[...] = dup
    copy_ref[:, :width] = (dot_nt(dgate, gate_ref[...]) + dot_nt(dup, up_ref[...])).astype(LOW)
    back = jnp.where(lane == mine, high.astype(F32), 0.0)
    back = jnp.where(lane == mine + experts, low.astype(F32), back)
    copy_ref[:, width:] = back.astype(LOW)


def run_expert(who, x, w_gate, w_up, pull, part, experts):
    rows, wide = x.shape
    width, hidden = w_gate.shape
    groups, _, slots, _ = pull.shape
    each = groups // 2
    tile = each * slots
    by_rows = lambda columns: pl.BlockSpec((tile, columns), lambda i, p: (i, 0))
    return pl.pallas_call(
        functools.partial(expert_kernel, experts),
        grid_spec=pltpu.PrefetchScalarGridSpec(
            num_scalar_prefetch=1,
            grid=(2,),
            in_specs=[
                by_rows(wide),
                full(w_gate.shape),
                full(w_up.shape),
                pl.BlockSpec((each, 1, slots, hidden), lambda i, p: (i, part, 0, 0)),
            ],
            out_specs=[by_rows(hidden), by_rows(hidden), by_rows(hidden), by_rows(wide)],
        ),
        out_shape=[jax.ShapeDtypeStruct((rows, hidden), LOW)] * 3
        + [jax.ShapeDtypeStruct((rows, wide), LOW)],
        compiler_params=params(),
        cost_estimate=cost(8 * rows * width * hidden, 20e6, rows * hidden),
    )(who, x, w_gate, w_up, pull)


def input_kernel(grad_ref, x_ref, gain_ref, more_ref, out_ref):
    normal, rr = norm_parts(x_ref[...].astype(F32))
    grad = grad_ref[...].astype(F32)
    out_ref[...] = more_ref[...] + norm_back(grad, normal, rr, gain_ref[...])


def input_back(grad, x, gain, more):
    tokens, width = x.shape
    operands = [grad, x, gain[None], more]
    return pl.pallas_call(
        input_kernel,
        grid=(1,),
        in_specs=[full(value.shape) for value in operands],
        out_specs=full(more.shape),
        out_shape=jax.ShapeDtypeStruct((tokens, width), F32),
        compiler_params=params(),
        cost_estimate=cost(20 * tokens * width, 5e6),
    )(*operands)


def kv_back_kernel(factor, n_parts, c_ref, dkv_ref, *refs):
    parts = refs[:n_parts]
    proj_ref, gain_ref, cos_ref, sin_ref = refs[n_parts : n_parts + 4]
    grad_ref, dgain_ref = refs[-2:]
    size = proj_ref.shape[1]
    total = functools.reduce(jnp.add, [part[...].astype(F32) for part in parts], dkv_ref[...])
    grad, dgain = head_backward(
        total[:, :size] * factor, proj_ref[...], gain_ref[...], cos_ref[...], sin_ref[...]
    )
    grad_ref[:, :size] = grad.astype(LOW)
    grad_ref[:, size:] = total[:, size:].astype(LOW)
    dgain_ref[...] = dgain


def kv_back(context, dkv, parts, proj, gain, cos2, sin2, factor, others):
    block, size = proj.shape
    operands = [proj, gain[None], cos2, sin2]
    shapes = [
        jax.ShapeDtypeStruct((block, 2 * size), LOW),
        jax.ShapeDtypeStruct((1, size), F32),
    ]
    return pl.pallas_call(
        functools.partial(kv_back_kernel, factor, len(parts)),
        grid_spec=pltpu.PrefetchScalarGridSpec(
            num_scalar_prefetch=1,
            grid=(1,),
            in_specs=[pl.BlockSpec((block, 2 * size), lambda i, c: (c[0], 0))]
            + [full(part.shape) for part in parts]
            + [full(value.shape) for value in operands]
            + [pl.BlockSpec(memory_space=pl.ANY)] * len(others),
            out_specs=[full(shape.shape) for shape in shapes],
        ),
        out_shape=shapes,
        compiler_params=params(),
        cost_estimate=cost(40 * block * size, 5e6),
    )(context.astype(jnp.int32)[None], dkv, *parts, *operands, *others)


def dp_sum_kernel(d_ref, *refs):
    out_ref = refs[-1]
    first = 0
    for kept_ref, got_ref in zip(refs[:-1:2], refs[1:-1:2]):
        last = first + kept_ref.shape[1]
        total = kept_ref[...].astype(F32) + got_ref[...].astype(F32)
        out_ref[:, first:last] = total.astype(LOW)
        first = last


def dp_sum(d, pairs):
    rows = pairs[0][1].shape[0]
    columns = sum(got.shape[1] for _, got in pairs)
    tiles = 4
    tile = rows // tiles
    specs = []
    for _, got in pairs:
        wide = got.shape[1]
        specs.append(pl.BlockSpec((tile, wide), lambda i, d: (d[0] * tiles + i, 0)))
        specs.append(pl.BlockSpec((tile, wide), lambda i, d: (i, 0)))
    return pl.pallas_call(
        dp_sum_kernel,
        grid_spec=pltpu.PrefetchScalarGridSpec(
            num_scalar_prefetch=1,
            grid=(tiles,),
            in_specs=specs,
            out_specs=pl.BlockSpec((tile, columns), lambda i, d: (i, 0)),
        ),
        out_shape=jax.ShapeDtypeStruct((rows, columns), LOW),
        compiler_params=params(),
        cost_estimate=cost(rows * columns, 6 * rows * columns),
    )(d, *[value for pair in pairs for value in pair])


def normed_kernel(q_ref, kv_ref, wq_ref, wkv_ref, rows_ref, out_ref, dgain_ref):
    grad = dot_nt(q_ref[...], wq_ref[...]) + dot_nt(kv_ref[...], wkv_ref[...])
    out_ref[...] = grad.astype(LOW)
    dgain_ref[...] = jnp.sum(grad * rows_ref[...].astype(F32), axis=0, keepdims=True)


def normed_back(grad_q, grad_kv, w_q, w_kv, rows):
    block, width = rows.shape
    tile = 512
    column = lambda i: (0, i)
    return pl.pallas_call(
        normed_kernel,
        grid=(width // tile,),
        in_specs=[
            full(grad_q.shape),
            full(grad_kv.shape),
            pl.BlockSpec((tile, w_q.shape[1]), lambda i: (i, 0)),
            pl.BlockSpec((tile, w_kv.shape[1]), lambda i: (i, 0)),
            pl.BlockSpec((block, tile), column),
        ],
        out_specs=[pl.BlockSpec((block, tile), column), pl.BlockSpec((1, tile), column)],
        out_shape=[
            jax.ShapeDtypeStruct((block, width), LOW),
            jax.ShapeDtypeStruct((1, width), F32),
        ],
        compiler_params=params(),
        cost_estimate=cost(2 * block * width * (w_q.shape[1] + w_kv.shape[1]), 12e6),
    )(grad_q, grad_kv, w_q, w_kv, rows)


def pack_kernel(experts, router_ref, attn_ref, mlp_ref, q_ref, k_ref, out_ref, rows_ref):
    size = q_ref.shape[1]
    rows_ref[:experts] = router_ref[:experts]
    rows_ref[experts:] = jnp.zeros_like(rows_ref[experts:])
    rows_ref[experts : experts + 1] = attn_ref[...]
    rows_ref[experts + 1 : experts + 2] = mlp_ref[...]
    rows_ref[experts + 2 : experts + 3, :size] = q_ref[...]
    rows_ref[experts + 2 : experts + 3, size : 2 * size] = k_ref[...]
    out_ref[...] = rows_ref[...].astype(LOW)


def pack_small(experts, router, attn, mlp, q, k):
    width = attn.shape[1]
    shape = (-(-(experts + 3) // 16) * 16, width)
    operands = [router, attn, mlp, q, k]
    return pl.pallas_call(
        functools.partial(pack_kernel, experts),
        grid=(1,),
        in_specs=[full(value.shape) for value in operands],
        out_specs=full(shape),
        out_shape=jax.ShapeDtypeStruct(shape, LOW),
        scratch_shapes=[pltpu.VMEM(shape, F32)],
        compiler_params=params(),
        cost_estimate=cost(shape[0] * width, 6 * shape[0] * width),
    )(*operands)


def part_sum_kernel(parts_ref, out_ref):
    total = parts_ref[0].astype(F32)
    for k in range(1, parts_ref.shape[0]):
        total += parts_ref[k].astype(F32)
    for k in range(out_ref.shape[0]):
        out_ref[k] = total.astype(LOW)


def part_sum(parts, copies):
    count, rows, columns = parts.shape
    tiles = 4 if rows % 64 == 0 else 1
    spec = lambda n: pl.BlockSpec((n, rows // tiles, columns), lambda i: (0, i, 0))
    return pl.pallas_call(
        part_sum_kernel,
        grid=(tiles,),
        in_specs=[spec(count)],
        out_specs=spec(copies),
        out_shape=jax.ShapeDtypeStruct((copies, rows, columns), LOW),
        compiler_params=params(),
        cost_estimate=cost(count * rows * columns, 4 * count * rows * columns),
    )(parts)


def widen_kernel(d_ref, kept_ref, got_ref, *outs):
    first = 0
    for out_ref in outs:
        last = first + out_ref.shape[1]

        @pl.when(pl.program_id(0) == 0)
        def _():
            out_ref[...] = kept_ref[:, first:last].astype(F32)

        @pl.when(pl.program_id(0) == 1)
        def _():
            out_ref[...] = got_ref[:, first:last].astype(F32)

        first = last


def widen(d, kept, got, widths):
    rows, columns = kept.shape
    tiles = 4
    tile = rows // tiles
    return pl.pallas_call(
        widen_kernel,
        grid_spec=pltpu.PrefetchScalarGridSpec(
            num_scalar_prefetch=1,
            grid=(2, tiles),
            in_specs=[
                pl.BlockSpec((tile, columns), lambda i, j, d: (j * (1 - i) + (tiles - 1) * i, 0)),
                pl.BlockSpec((tile, columns), lambda i, j, d: (j * i, 0)),
            ],
            out_specs=[
                pl.BlockSpec(
                    (tile, wide), lambda i, j, d: ((d[0] + i - 2 * d[0] * i) * tiles + j, 0)
                )
                for wide in widths
            ],
        ),
        out_shape=[jax.ShapeDtypeStruct((2 * rows, wide), F32) for wide in widths],
        compiler_params=params(),
        cost_estimate=cost(2 * rows * columns, 12 * rows * columns),
    )(d, kept, got)


def sum_all(rows):
    total = rows.astype(F32)
    for axis in ("dp", "context", "expert"):
        n = lax.axis_size(axis)
        sent = total.astype(LOW)
        for s in range(1, n):
            total += lax.ppermute(sent, axis, [(i, (i + s) % n) for i in range(n)]).astype(F32)
    return total


def swap_dp(rows):
    return lax.ppermute(rows, "dp", [(0, 1), (1, 0)])


def swap_context(rows, s):
    n = lax.axis_size("context")
    return lax.ppermute(rows, "context", [(i, i ^ s) for i in range(n)])


def dp_got(grad):
    d = lax.axis_index("dp")
    rows = grad.shape[0] // 2
    return swap_dp(lax.dynamic_slice_in_dim(grad, (1 - d) * rows, rows))


def share_context(parts):
    return lax.all_to_all(parts, "context", split_axis=0, concat_axis=0, tiled=True)


def sum_groups(grads, gots, widths):
    n = lax.axis_size("context")
    d = lax.axis_index("dp").astype(jnp.int32)[None]
    half = dp_sum(d, list(zip(grads, gots)))
    rows, columns = half.shape
    parts = part_sum(share_context(half.reshape(n, rows // n, columns)), n)
    half = share_context(parts).reshape(rows, columns)
    return widen(d, half, swap_dp(half), widths)


def arrival_order(n):
    return [sorted(range(n), key=lambda j: (abs(j - i), j)) for i in range(n)]


def choose(index, options):
    distinct = []
    for option in options:
        if option is not None and not any(option is other for other in distinct):
            distinct.append(option)
    result = distinct[0]
    for option in distinct[1:]:
        mask = functools.reduce(
            jnp.logical_or, [index == i for i, other in enumerate(options) if other is option]
        )
        result = jnp.where(mask, option, result)
    return result


def line_gather(chunk):
    return line_steps({0: chunk}, 1, lax.axis_size("expert"))


def line_steps(found, first, stop):
    n = lax.axis_size("expert")
    found = dict(found)
    for s in range(first, stop):
        found[-s] = lax.ppermute(
            found[1 - s], "expert", [(i, i + 1) for i in range(s - 1, n - 1)]
        )
        found[s] = lax.ppermute(found[s - 1], "expert", [(i + 1, i) for i in range(n - s)])
    return found


def context_gather(rows):
    n = lax.axis_size("context")
    c = lax.axis_index("context")
    found = {0: rows}
    for s in range(1, n):
        found[s] = lax.ppermute(rows, "context", [(i, i ^ s) for i in range(n)])
    return jnp.concatenate([choose(c, [found[i ^ j] for i in range(n)]) for j in range(n)], axis=0)


def context_parts(rows, extra):
    n = lax.axis_size("context")
    c = lax.axis_index("context")
    each = rows.shape[0] // n
    return [
        swap_context((lax.dynamic_slice_in_dim(rows, (c ^ s) * each, each) + extra).astype(LOW), s)
        for s in range(1, n)
    ]


def zero_of(*others):
    return functools.reduce(
        jnp.add,
        [
            lax.slice(other, (0,) * other.ndim, (1,) * other.ndim).reshape(()).astype(F32) * 0.0
            for other in others
        ],
    )


def after(value, *others):
    return (value.astype(F32) + zero_of(*others)).astype(value.dtype)


def on_device(
    layer_input,
    grad_output,
    attn_gain,
    query_weight,
    key_weight,
    value_weight,
    q_gain,
    k_gain,
    output_weight,
    mlp_gain,
    router,
    w_gate,
    w_up,
    w_down,
    routes,
    half_order,
):
    n_context = lax.axis_size("context")
    n_expert = lax.axis_size("expert")
    n_groups = lax.axis_size(GROUP_AXES)
    tok_dev, width = layer_input.shape[1:]
    size = q_gain.shape[0]
    kv_total = key_weight.shape[1] * n_expert
    group_dev = n_expert // (kv_total // size)
    kv_index = lax.axis_index("expert") // group_dev
    block = tok_dev * n_expert
    seq = block * n_context
    half = block // 2
    experts = router.shape[1]
    exp_dev = w_gate.shape[0]
    top = routes.shape[2]
    capacity = max(2, (tok_dev * top * 9 + 8 * experts - 1) // (8 * experts))
    scale = size ** (-0.5)

    seq_rows = jnp.arange(seq, dtype=jnp.int32)
    context = lax.axis_index("context")
    own_halves = lax.dynamic_slice_in_dim(half_order, 2 * context, 2)
    own_pos = (own_halves[:, None] * half + jnp.arange(half, dtype=jnp.int32)[None]).reshape(-1)
    per_half = half // TILE
    tile_pos = (half_order[:, None] * per_half + jnp.arange(per_half, dtype=jnp.int32)).reshape(-1)
    kidx = jnp.sum(
        (tile_pos[None, :] == jnp.arange(seq // TILE, dtype=jnp.int32)[:, None])
        * jnp.arange(seq // TILE, dtype=jnp.int32)[None, :],
        axis=1,
    ).astype(jnp.int32)
    qpos = lax.dynamic_slice_in_dim(tile_pos, context * (block // TILE), block // TILE)
    entry = jnp.arange(size)
    freq = jnp.power(THETA, -(2 * (entry % (size // 2))).astype(F32) / size)
    angles = own_pos.astype(F32)[:, None] * freq[None, :]
    cos2 = jnp.cos(angles)
    sin2 = jnp.sin(angles) * jnp.where(entry < size // 2, -1.0, 1.0)[None, :]

    place = lax.axis_index("expert")
    place_1 = place.astype(jnp.int32)[None]
    lanes = -(-2 * experts // 128) * 128
    mask = jnp.any(
        routes[0][:, :, None] == jnp.arange(lanes, dtype=jnp.int32)[None, None, :], axis=1
    )
    mask_wide = mask.astype(F32)
    router_rows = router.T

    x_low = layer_input[0]
    x_normal, _ = norm_parts(x_low.astype(F32))
    normed_found = line_gather((x_normal * attn_gain).astype(LOW))
    if group_dev == 1:
        kv_weights = jnp.concatenate([key_weight, value_weight], axis=1)
    else:
        key_whole = lax.all_gather(key_weight, "expert", axis=1, tiled=True)
        value_whole = lax.all_gather(value_weight, "expert", axis=1, tiled=True)
        kv_weights = jnp.concatenate(
            [
                lax.dynamic_slice_in_dim(key_whole, kv_index * size, size, 1),
                lax.dynamic_slice_in_dim(value_whole, kv_index * size, size, 1),
            ],
            axis=1,
        )
    grad_low = grad_output[0]
    normed_rows, own_kv, key_proj, grad_wide = project_keys(
        place_1,
        normed_found,
        kv_weights,
        k_gain,
        cos2,
        sin2,
        scale * LOG2E,
        grad_low,
        mask_wide,
    )
    grad_col = lax.all_gather(grad_wide, "expert", axis=0, tiled=True)
    kv_whole = context_gather(own_kv)
    queries, query_proj = project_queries(normed_rows, query_weight, q_gain, cos2, sin2)

    n_half = n_expert // 2
    order_here = jnp.asarray(arrival_order(n_expert), jnp.int32)[place]
    turn_here = jnp.sum(
        (order_here[:, None] == jnp.arange(n_expert, dtype=jnp.int32)[None, :])
        * jnp.arange(n_expert, dtype=jnp.int32)[:, None],
        axis=0,
    ).astype(jnp.int32)
    meta = jnp.concatenate([place_1, turn_here, order_here])
    grad_sent, spreads, back_tables = make_tables(
        meta, grad_col, width, n_groups, n_half, capacity, []
    )

    def swap_plane(rows):
        parts = rows.reshape(n_groups, -1, rows.shape[1])
        parts = lax.all_to_all(parts, GROUP_AXES, split_axis=0, concat_axis=0, tiled=True)
        return parts.reshape(rows.shape)

    attended, inverse = attend(qpos, kidx, queries, kv_whole, [])
    attn_part = (dot_nn(attended, output_weight) + zero_of(grad_sent)).astype(LOW)
    attn_rows = lax.psum_scatter(attn_part, "expert", scatter_dimension=0, tiled=True)

    grad_x = swap_plane(grad_sent)
    act_pull = dot_nt(grad_x, w_down[0]).reshape(n_groups, 2, n_half * capacity, -1)

    hidden, mixed, probs = route_rows(
        x_low, attn_rows, mlp_gain, router_rows, mask_wide, experts, []
    )

    who = (lax.axis_index(ALL_AXES) * exp_dev).astype(jnp.int32)[None]
    mixed_found = line_gather(mixed)
    near = spread_rows(place_1, spreads[0], mixed_found, range(n_half), [grad_x])
    x_near = swap_plane(near)
    worked_near = run_expert(who, x_near, w_gate[0], w_up[0], act_pull, 0, experts)
    far = spread_rows(place_1, spreads[1], mixed_found, range(n_half, n_expert), [x_near])
    x_far = swap_plane(far)
    worked_far = run_expert(who, x_far, w_gate[0], w_up[0], act_pull, 1, experts)
    xs = [x_near, x_far]
    acts, gate_lows, up_lows, copies = (list(pair) for pair in zip(worked_near, worked_far))
    back_far = swap_plane(copies[1])
    back_near = swap_plane(copies[0])
    join = lambda parts: jnp.concatenate(parts, axis=0)
    x_all = join([x[:, :width] for x in xs])
    grad_w_gate = dot_tn(x_all, join(gate_lows))
    grad_w_up = dot_tn(x_all, join(up_lows))
    grad_by_round = jnp.swapaxes(
        grad_x.reshape(n_groups, 2, n_half * capacity, width), 0, 1
    ).reshape(-1, width)
    grad_w_down = dot_tn(join(acts), grad_by_round)
    copies_col = combine_rows(
        meta, back_tables, [back_near, back_far], n_half, [grad_w_gate, grad_w_up]
    )
    copies_sum = lax.psum_scatter(copies_col, "expert", scatter_dimension=0, tiled=True)

    returned = [dot_nn(act, w_down[0]).astype(LOW) for act in acts]
    returned_near = swap_plane(returned[0])

    grad_hidden, grad_hidden_low, grad_mlp_gain, grad_router = route_back(
        copies_sum,
        grad_low,
        hidden,
        mlp_gain,
        router_rows,
        mask_wide,
        probs,
        experts,
        [returned_near, grad_w_down],
    )

    returned_far = swap_plane(returned[1])
    grad_attn = lax.all_gather(grad_hidden_low, "expert", axis=0, tiled=True)
    grad_o, centre = grad_attended(
        grad_attn, output_weight, attended, inverse, [returned_far]
    )
    w_out = token_dot(attended, grad_attn, [])
    w_out_parts = swap_plane(w_out)
    grad_kv, grad_q, grad_q_gain = attend_back(
        qpos, kidx, queries, grad_o, centre, kv_whole, query_proj, q_gain, cos2, sin2, [w_out]
    )
    kv_parts = context_parts(grad_kv, zero_of(w_out_parts))
    w_query = token_dot(normed_rows, grad_q, [])
    w_query_got = dp_got(w_query)

    kv_grads, grad_k_gain = kv_back(
        context, grad_kv, kv_parts, key_proj, k_gain, cos2, sin2, scale, [w_query_got]
    )
    grad_normed, gain_rows = normed_back(grad_q, kv_grads, query_weight, kv_weights, normed_rows)
    grad_attn_gain = gain_rows / attn_gain[None]
    grad_normed = lax.psum_scatter(grad_normed, "expert", scatter_dimension=0, tiled=True)
    grad_input = input_back(grad_normed, x_low, attn_gain, grad_hidden)

    combined = combine_rows(
        meta, back_tables, [returned_near, returned_far], n_half, [grad_normed]
    )
    output_rows = hidden + lax.psum_scatter(
        combined, "expert", scatter_dimension=0, tiled=True
    ).astype(F32)

    w_out_half = context_gather(
        part_sum(w_out_parts.reshape(n_groups, -1, width), 1)[0]
    )
    dp_place = lax.axis_index("dp").astype(jnp.int32)[None]
    (grad_w_out,) = widen(dp_place, w_out_half, swap_dp(w_out_half), [width])
    w_kv = token_dot(normed_rows, kv_grads, [])
    if group_dev == 1:
        half_width = key_weight.shape[1]
        grad_w_query, grad_w_key, grad_w_value = sum_groups(
            [w_query, w_kv],
            [w_query_got, dp_got(w_kv)],
            [query_weight.shape[1], half_width, half_width],
        )
    else:
        (grad_w_query,) = sum_groups([w_query], [w_query_got], [query_weight.shape[1]])
        blank = jnp.zeros((width, kv_total), LOW)
        pieces = []
        for part in (w_kv[:, :size], w_kv[:, size:]):
            padded = lax.dynamic_update_slice(blank, part, (0, kv_index * size))
            pieces.append(lax.psum_scatter(padded, "expert", scatter_dimension=1, tiled=True))
        grad_w_key, grad_w_value = (lax.psum(piece, GROUP_AXES).astype(F32) for piece in pieces)

    small = sum_all(
        pack_small(
            experts, grad_router, grad_attn_gain, grad_mlp_gain, grad_q_gain, grad_k_gain
        )
    )
    grad_attn_gain, grad_mlp_gain = small[experts], small[experts + 1]
    grad_q_gain = small[experts + 2, :size]
    grad_k_gain = small[experts + 2, size : 2 * size]
    return (
        output_rows.astype(LOW)[None],
        grad_input[None],
        grad_attn_gain,
        grad_w_query,
        grad_w_key,
        grad_w_value,
        grad_q_gain,
        grad_k_gain,
        grad_w_out,
        grad_mlp_gain,
        small[:experts].T,
        grad_w_gate[None],
        grad_w_up[None],
        grad_w_down[None],
    )


def solution(mesh):
    rows = P("dp", ("context", "expert"), None)
    expert = P(ALL_AXES, None, None)
    columns = P(None, "expert")
    in_specs = (
        rows,
        rows,
        P(),
        columns,
        columns,
        columns,
        P(),
        P(),
        P("expert", None),
        P(),
        P(),
        expert,
        expert,
        expert,
        rows,
        P(),
    )
    out_specs = (
        rows,
        rows,
        P(),
        columns,
        columns,
        columns,
        P(),
        P(),
        P("expert", None),
        P(),
        P(),
        expert,
        expert,
        expert,
    )
    return jax.shard_map(
        on_device, mesh=mesh, in_specs=in_specs, out_specs=out_specs, check_vma=False
    )
```

```python
import functools
import math

import jax
import jax.numpy as jnp
from jax import lax
from jax.experimental import pallas as pl
from jax.experimental.pallas import tpu as pltpu
from jax.sharding import PartitionSpec as P

EPS = 1e-06
THETA = 1000000.0
TILE = 256
VMEM_BYTES = 56 * 1024 * 1024
LOG2E = math.log2(math.e)
LOW = jnp.bfloat16
F32 = jnp.float32
ALL_AXES = ("dp", "context", "expert")
GROUP_AXES = ("dp", "context")


def dot_nn(a, b):
    return lax.dot_general(a, b, (((1,), (0,)), ((), ())), preferred_element_type=F32)


def dot_nt(a, b):
    return lax.dot_general(a, b, (((1,), (1,)), ((), ())), preferred_element_type=F32)


def dot_tn(a, b):
    return lax.dot_general(a, b, (((0,), (0,)), ((), ())), preferred_element_type=F32)


def params(**more):
    return pltpu.CompilerParams(vmem_limit_bytes=VMEM_BYTES, **more)


def cost(flops, nbytes, exps=0):
    return pl.CostEstimate(flops=int(flops), bytes_accessed=int(nbytes), transcendentals=int(exps))


def head_forward(u, gain, cos2, sin2):
    rr = lax.rsqrt(jnp.mean(u * u, axis=-1, keepdims=True) + EPS)
    y = u * rr * gain
    return y * cos2 + pltpu.roll(y, 64, 1) * sin2


def head_backward(gy, u, gain, cos2, sin2):
    g = gy * cos2 - pltpu.roll(gy, 64, 1) * sin2
    rr = lax.rsqrt(jnp.mean(u * u, axis=-1, keepdims=True) + EPS)
    n = u * rr
    gn = g * gain
    grad = rr * (gn - n * jnp.mean(gn * n, axis=-1, keepdims=True))
    return grad, jnp.sum(g * n, axis=0, keepdims=True)


def query_kernel(x_ref, w_ref, gain_ref, cos_ref, sin_ref, rot_ref, proj_ref):
    tiles, heads, rows, size = rot_ref.shape
    acc = dot_nn(x_ref[...], w_ref[...])
    for h in range(heads):
        u = acc[:, h * size : (h + 1) * size]
        rot = head_forward(u, gain_ref[...], cos_ref[...], sin_ref[...])
        proj_ref[:, h] = u.reshape(tiles, rows, size)
        rot_ref[:, h] = rot.astype(LOW).reshape(tiles, rows, size)


def project_queries(normed, weight, gain, cos2, sin2):
    block, width = normed.shape
    size = cos2.shape[1]
    heads = weight.shape[1] // size
    tiles = block // TILE
    whole = lambda i: (0, 0)
    per = lambda i: (0, i, 0, 0)
    shape = (tiles, heads, TILE, size)
    return pl.pallas_call(
        query_kernel,
        grid=(heads // 2,),
        in_specs=[
            pl.BlockSpec((block, width), whole),
            pl.BlockSpec((width, 2 * size), lambda i: (0, i)),
            pl.BlockSpec((1, size), whole),
            pl.BlockSpec((block, size), whole),
            pl.BlockSpec((block, size), whole),
        ],
        out_specs=[pl.BlockSpec((tiles, 2, TILE, size), per)] * 2,
        out_shape=[jax.ShapeDtypeStruct(shape, LOW), jax.ShapeDtypeStruct(shape, F32)],
        compiler_params=params(),
        cost_estimate=cost(2 * block * width * heads * size, 12e6),
    )(normed, weight, gain[None], cos2, sin2)


def put_in_order(place, refs, out_ref):
    n = (len(refs) + 1) // 2
    rows = refs[0].shape[0]
    for distance in range(1 - n, n):
        ref = refs[distance + n - 1]
        at = place + distance

        @pl.when(jnp.logical_and(at >= 0, at < n))
        def _():
            out_ref[pl.ds(pl.multiple_of(at * rows, rows), rows), :] = ref[...]


def chunk_list(found):
    n = (len(found) + 1) // 2
    return [found[distance] for distance in range(1 - n, n)]


def key_kernel(factor, n_chunks, place_ref, *refs):
    w_ref, gain_ref, cos_ref, sin_ref, g_ref, mask_ref = refs[n_chunks:-4]
    rows_ref, kv_ref, proj_ref, wide_ref = refs[-4:]
    size = proj_ref.shape[1]
    width = g_ref.shape[1]
    put_in_order(place_ref[0], refs[:n_chunks], rows_ref)
    wide_ref[:, :width] = g_ref[...]
    wide_ref[:, width:] = mask_ref[...].astype(LOW)
    acc = dot_nn(rows_ref[...], w_ref[...])
    u = acc[:, :size]
    rot = head_forward(u, gain_ref[...], cos_ref[...], sin_ref[...])
    proj_ref[...] = u
    kv_ref[:, :size] = (rot * factor).astype(LOW)
    kv_ref[:, size:] = acc[:, size:].astype(LOW)


def full(shape):
    return pl.BlockSpec(shape, lambda *_: (0,) * len(shape))


def project_keys(place, found, weight, gain, cos2, sin2, factor, g, mask):
    chunks = chunk_list(found)
    rows, width = chunks[0].shape
    block, size = cos2.shape
    operands = [*chunks, weight, gain[None], cos2, sin2, g, mask]
    shapes = [
        jax.ShapeDtypeStruct((block, width), LOW),
        jax.ShapeDtypeStruct((block, 2 * size), LOW),
        jax.ShapeDtypeStruct((block, size), F32),
        jax.ShapeDtypeStruct((rows, width + mask.shape[1]), LOW),
    ]
    return pl.pallas_call(
        functools.partial(key_kernel, factor, len(chunks)),
        grid_spec=pltpu.PrefetchScalarGridSpec(
            num_scalar_prefetch=1,
            grid=(1,),
            in_specs=[full(x.shape) for x in operands],
            out_specs=[full(x.shape) for x in shapes],
        ),
        out_shape=shapes,
        compiler_params=params(),
        cost_estimate=cost(4 * block * width * size, 8e6),
    )(place, *operands)


def in_order(last, step):
    lax.fori_loop(0, lax.div(last, 2), lambda p, c: (step([2 * p, 2 * p + 1], False), c)[1], 0)

    @pl.when(lax.rem(last, 2) == 1)
    def _():
        step([last - 1, last], True)

    @pl.when(lax.rem(last, 2) == 0)
    def _():
        step([last], True)


def attend_kernel(qpos_ref, kidx_ref, q_ref, kv_ref, *rest):
    out_ref, inv_ref, acc_ref = rest[-3:]
    heads, rows, size = q_ref.shape[1:]
    acc_ref[...] = jnp.zeros_like(acc_ref)

    def step(places, masked):
        starts = [pl.multiple_of(kidx_ref[place] * rows, rows) for place in places]
        count = len(places) * rows
        keys = jnp.concatenate([kv_ref[pl.ds(start, rows), :size] for start in starts], axis=0)
        values = jnp.concatenate([kv_ref[pl.ds(start, rows), size:] for start in starts], axis=0)
        values = jnp.concatenate([values, jnp.ones((count, size), LOW)], axis=1)
        for h in range(heads):
            e = jnp.exp2(dot_nt(q_ref[0, h], keys))
            if masked:
                qi = lax.broadcasted_iota(jnp.int32, e.shape, 0)
                ki = lax.broadcasted_iota(jnp.int32, e.shape, 1) - (count - rows)
                e = jnp.where(ki <= qi, e, 0.0)
            acc_ref[h] += dot_nn(e.astype(LOW), values)

    in_order(qpos_ref[pl.program_id(0)], step)
    for h in range(heads):
        inv = 1.0 / acc_ref[h, :, size:]
        inv_ref[0, h] = inv
        out_ref[:, h * size : (h + 1) * size] = (acc_ref[h, :, :size] * inv).astype(LOW)


def attend(qpos, kidx, queries, kv, others):
    tiles, heads, rows, size = queries.shape
    seq = kv.shape[0]
    return pl.pallas_call(
        attend_kernel,
        grid_spec=pltpu.PrefetchScalarGridSpec(
            num_scalar_prefetch=2,
            grid=(tiles,),
            in_specs=[
                pl.BlockSpec((1, heads, rows, size), lambda i, a, b: (i, 0, 0, 0)),
                pl.BlockSpec((seq, 2 * size), lambda i, a, b: (0, 0)),
            ]
            + [pl.BlockSpec(memory_space=pl.ANY)] * len(others),
            out_specs=[
                pl.BlockSpec((rows, heads * size), lambda i, a, b: (i, 0)),
                pl.BlockSpec((1, heads, rows, size), lambda i, a, b: (i, 0, 0, 0)),
            ],
            scratch_shapes=[pltpu.VMEM((heads, rows, 2 * size), F32)],
        ),
        out_shape=[
            jax.ShapeDtypeStruct((tiles * rows, heads * size), LOW),
            jax.ShapeDtypeStruct((tiles, heads, rows, size), F32),
        ],
        compiler_params=params(),
        cost_estimate=cost(
            6 * tiles * rows * heads * seq * size, 8e6, tiles * rows * heads * seq
        ),
    )(qpos, kidx, queries, kv, *others)


def grad_out_kernel(rows_ref, w_ref, o_ref, inv_ref, *rest):
    do_ref, centre_ref = rest[-2:]
    tiles, heads, rows, size = do_ref.shape
    acc = dot_nt(rows_ref[...], w_ref[...])
    for t in range(tiles):
        for h in range(heads):
            part = slice(t * rows, (t + 1) * rows), slice(h * size, (h + 1) * size)
            low = (acc[part] * inv_ref[t, h]).astype(LOW)
            do_ref[t, h] = low
            product = low.astype(F32) * o_ref[part].astype(F32)
            centre = jnp.sum(jnp.transpose(product), axis=0, keepdims=True)
            centre_ref[t, h] = jnp.broadcast_to(centre, (8, rows))


def grad_attended(grad_rows, weight, attended, inverse, others):
    tiles, heads, rows, size = inverse.shape
    block, width = grad_rows.shape
    return pl.pallas_call(
        grad_out_kernel,
        grid=(heads // 2,),
        in_specs=[
            pl.BlockSpec((block, width), lambda i: (0, 0)),
            pl.BlockSpec((2 * size, width), lambda i: (i, 0)),
            pl.BlockSpec((block, 2 * size), lambda i: (0, i)),
            pl.BlockSpec((tiles, 2, rows, size), lambda i: (0, i, 0, 0)),
        ]
        + [pl.BlockSpec(memory_space=pl.ANY)] * len(others),
        out_specs=[
            pl.BlockSpec((tiles, 2, rows, size), lambda i: (0, i, 0, 0)),
            pl.BlockSpec((tiles, 2, 8, rows), lambda i: (0, i, 0, 0)),
        ],
        out_shape=[
            jax.ShapeDtypeStruct((tiles, heads, rows, size), LOW),
            jax.ShapeDtypeStruct((tiles, heads, 8, rows), F32),
        ],
        compiler_params=params(),
        cost_estimate=cost(2 * block * width * heads * size, 12e6),
    )(grad_rows, weight, attended, inverse, *others)


def attend_back_kernel(
    qpos_ref,
    kidx_ref,
    q_ref,
    do_ref,
    centre_ref,
    kv_ref,
    proj_ref,
    gain_ref,
    cos_ref,
    sin_ref,
    *rest,
):
    dkv_ref, dq_ref, dgain_ref, acc_ref, e_ref, ds_ref = rest[-6:]
    heads, rows, size = q_ref.shape[1:]

    @pl.when(pl.program_id(0) == 0)
    def _():
        dkv_ref[...] = jnp.zeros_like(dkv_ref)
        dgain_ref[...] = jnp.zeros_like(dgain_ref)

    acc_ref[...] = jnp.zeros_like(acc_ref)

    def step(places, masked):
        starts = [pl.multiple_of(kidx_ref[place] * rows, rows) for place in places]
        count = len(places) * rows
        keys = jnp.concatenate([kv_ref[pl.ds(start, rows), :size] for start in starts], axis=0)
        values = jnp.concatenate([kv_ref[pl.ds(start, rows), size:] for start in starts], axis=0)
        for h in range(heads):
            query, grad = q_ref[0, h], do_ref[0, h]
            e = jnp.exp2(dot_nt(keys, query))
            if masked:
                ki = lax.broadcasted_iota(jnp.int32, e.shape, 0) - (count - rows)
                qi = lax.broadcasted_iota(jnp.int32, e.shape, 1)
                e = jnp.where(ki <= qi, e, 0.0)
            ds = (e * (dot_nt(values, grad) - centre_ref[0, h, 0:1])).astype(LOW)
            e_ref[:count, h * rows : (h + 1) * rows] = e.astype(LOW)
            ds_ref[:count, h * rows : (h + 1) * rows] = ds
            acc_ref[h] += dot_tn(ds, keys)
        dk = dot_nn(ds_ref[:count], q_ref[0].reshape(heads * rows, size))
        dv = dot_nn(e_ref[:count], do_ref[0].reshape(heads * rows, size))
        for k, start in enumerate(starts):
            dkv_ref[pl.ds(start, rows), :size] += dk[k * rows : (k + 1) * rows]
            dkv_ref[pl.ds(start, rows), size:] += dv[k * rows : (k + 1) * rows]

    in_order(qpos_ref[pl.program_id(0)], step)
    total = jnp.zeros((1, size), F32)
    for h in range(heads):
        grad, gain_part = head_backward(
            acc_ref[h] * (1.0 / LOG2E), proj_ref[0, h], gain_ref[...], cos_ref[...], sin_ref[...]
        )
        dq_ref[:, h * size : (h + 1) * size] = grad.astype(LOW)
        total += gain_part
    dgain_ref[...] += total


def attend_back(qpos, kidx, queries, grads, centre, kv, proj, gain, cos2, sin2, others):
    tiles, heads, rows, size = queries.shape
    seq = kv.shape[0]
    per = pl.BlockSpec((1, heads, rows, size), lambda i, a, b: (i, 0, 0, 0))
    flat = lambda i, a, b: (0, 0)
    rowwise = lambda i, a, b: (i, 0)
    return pl.pallas_call(
        attend_back_kernel,
        grid_spec=pltpu.PrefetchScalarGridSpec(
            num_scalar_prefetch=2,
            grid=(tiles,),
            in_specs=[
                per,
                per,
                pl.BlockSpec((1, heads, 8, rows), lambda i, a, b: (i, 0, 0, 0)),
                pl.BlockSpec((seq, 2 * size), flat),
                per,
                pl.BlockSpec((1, size), flat),
                pl.BlockSpec((rows, size), rowwise),
                pl.BlockSpec((rows, size), rowwise),
            ]
            + [pl.BlockSpec(memory_space=pl.ANY)] * len(others),
            out_specs=[
                pl.BlockSpec((seq, 2 * size), flat),
                pl.BlockSpec((rows, heads * size), rowwise),
                pl.BlockSpec((1, size), flat),
            ],
            scratch_shapes=[pltpu.VMEM((heads, rows, size), F32)]
            + [pltpu.VMEM((2 * rows, heads * rows), LOW)] * 2,
        ),
        out_shape=[
            jax.ShapeDtypeStruct((seq, 2 * size), F32),
            jax.ShapeDtypeStruct((tiles * rows, heads * size), LOW),
            jax.ShapeDtypeStruct((1, size), F32),
        ],
        compiler_params=params(),
        cost_estimate=cost(
            15 * tiles * rows * heads * seq * size, 12e6, tiles * rows * heads * seq
        ),
    )(qpos, kidx, queries, grads, centre, kv, proj, gain[None], cos2, sin2, *others)


def token_kernel(a_ref, b_ref, *rest):
    rest[-1][...] = dot_tn(a_ref[...], b_ref[...]).astype(LOW)


def token_dot(a, b, others):
    block, rows = a.shape
    columns = b.shape[1]
    tile = min(rows, 512)
    return pl.pallas_call(
        token_kernel,
        grid=(rows // tile,),
        in_specs=[
            pl.BlockSpec((block, tile), lambda i: (0, i)),
            pl.BlockSpec((block, columns), lambda i: (0, 0)),
        ]
        + [pl.BlockSpec(memory_space=pl.ANY)] * len(others),
        out_specs=pl.BlockSpec((tile, columns), lambda i: (i, 0)),
        out_shape=jax.ShapeDtypeStruct((rows, columns), LOW),
        compiler_params=params(),
        cost_estimate=cost(2 * block * rows * columns, 6e6),
    )(a, b, *others)


def split_low(value):
    high = value.astype(LOW)
    return high, (value - high.astype(F32)).astype(LOW)


def norm_parts(rows):
    rr = lax.rsqrt(jnp.mean(rows * rows, axis=-1, keepdims=True) + EPS)
    return rows * rr, rr


def norm_back(grad, normal, rr, gain):
    weighted = grad * gain
    return rr * (weighted - normal * jnp.mean(weighted * normal, axis=-1, keepdims=True))


def add_all(refs):
    return functools.reduce(jnp.add, [ref[...].astype(F32) for ref in refs])


def pad_rows(rows, count):
    if rows.shape[0] == count:
        return rows
    return jnp.concatenate(
        [rows, jnp.zeros((count - rows.shape[0], rows.shape[1]), rows.dtype)], axis=0
    )


def router_kernel(experts, *refs):
    x_ref, attn_ref, gain_ref, router_ref, mask_ref = refs[:5]
    hidden_ref, mixed_ref, probs_ref = refs[-3:]
    width = x_ref.shape[1]
    lanes = mask_ref.shape[1]
    hidden = add_all([x_ref, attn_ref])
    hidden_ref[...] = hidden
    mixed = (norm_parts(hidden)[0] * gain_ref[...]).astype(LOW)
    mixed_ref[:, :width] = mixed
    logits = dot_nt(mixed, pad_rows(router_ref[...], lanes))
    lane = lax.broadcasted_iota(jnp.int32, logits.shape, 1)
    logits = jnp.where(lane < experts, logits, -1e30)
    weights = jnp.exp(logits - jnp.max(logits, axis=1, keepdims=True))
    probs = weights / jnp.sum(weights, axis=1, keepdims=True)
    probs_ref[...] = probs
    chosen = probs * mask_ref[...]
    high, low = split_low(chosen / jnp.sum(chosen, axis=1, keepdims=True))
    both = high.astype(F32) + pltpu.roll(low.astype(F32), experts, 1)
    mixed_ref[:, width:] = both.astype(LOW)


def route_rows(x, attn, gain, router, mask, experts, others):
    tokens, width = x.shape
    lanes = mask.shape[1]
    operands = [x, attn, gain[None], router, mask]
    shapes = [
        jax.ShapeDtypeStruct((tokens, width), F32),
        jax.ShapeDtypeStruct((tokens, width + lanes), LOW),
        jax.ShapeDtypeStruct((tokens, lanes), F32),
    ]
    return pl.pallas_call(
        functools.partial(router_kernel, experts),
        grid=(1,),
        in_specs=[full(value.shape) for value in operands]
        + [pl.BlockSpec(memory_space=pl.ANY)] * len(others),
        out_specs=[full(shape.shape) for shape in shapes],
        out_shape=shapes,
        compiler_params=params(),
        cost_estimate=cost(2 * tokens * width * lanes, 5e6),
    )(*operands, *others)


def table_kernel(capacity, n_half, meta_ref, col_ref, *rest):
    rows_ref, near_ref, far_ref, near_back_ref, far_back_ref, slots_ref = rest[-6:]
    block = col_ref.shape[0]
    rows, width = rows_ref.shape
    n = 2 * n_half
    tokens = block // n
    cap_half = n_half * capacity
    groups = rows // (2 * cap_half)
    mask = col_ref[:, width:]
    lanes = mask.shape[1]
    padded = -(-groups // 16) * 16
    group = lax.broadcasted_iota(jnp.int32, (padded, lanes), 0)
    lane = lax.broadcasted_iota(jnp.int32, (padded, lanes), 1)
    wanted = jnp.logical_and(lane == group * n + meta_ref[0], group < groups)
    hits = dot_nt(jnp.where(wanted, 1.0, 0.0).astype(LOW), mask)
    before = lax.broadcasted_iota(jnp.int32, (tokens, tokens), 0)
    after_it = lax.broadcasted_iota(jnp.int32, (tokens, tokens), 1)
    earlier = jnp.where(before < after_it, 1.0, 0.0).astype(LOW)
    for z in range(n):
        hit = hits[:, z * tokens : (z + 1) * tokens]
        rank = dot_nn(hit.astype(LOW), earlier)
        turn = (meta_ref[1 + z] * capacity).astype(F32)
        slot = jnp.where(hit > 0.5, rank + turn, -1.0)
        slots_ref[:, z * tokens : (z + 1) * tokens] = slot[:groups]

    def one_hot(slots, count, first):
        slot = lax.broadcasted_iota(jnp.int32, (groups, count, slots.shape[1]), 1).astype(F32)
        same = slots[:, None, :] == slot + float(first)
        return jnp.where(same, 1.0, 0.0).reshape(groups * count, slots.shape[1])

    spread = one_hot(slots_ref[...], 2 * cap_half, 0).astype(LOW)
    rows_ref[...] = dot_nn(spread, col_ref[:, :width]).astype(LOW)
    for part, (to_ref, back_ref) in enumerate([(near_ref, near_back_ref), (far_ref, far_back_ref)]):
        pieces = []
        for k in range(n_half):
            start = pl.multiple_of(meta_ref[1 + n + part * n_half + k] * tokens, tokens)
            pieces.append(slots_ref[:, pl.ds(start, tokens)])
        spread = one_hot(jnp.concatenate(pieces, axis=1), cap_half, part * cap_half)
        to_ref[...] = spread.astype(LOW)
        back_ref[...] = jnp.transpose(spread).astype(LOW)


def make_tables(meta, col, width, groups, n_half, capacity, others):
    block = col.shape[0]
    rows = groups * n_half * capacity
    shapes = (
        [jax.ShapeDtypeStruct((2 * rows, width), LOW)]
        + [jax.ShapeDtypeStruct((rows, block // 2), LOW)] * 2
        + [jax.ShapeDtypeStruct((block // 2, rows), LOW)] * 2
    )
    outs = pl.pallas_call(
        functools.partial(table_kernel, capacity, n_half),
        grid_spec=pltpu.PrefetchScalarGridSpec(
            num_scalar_prefetch=1,
            grid=(1,),
            in_specs=[full(col.shape)] + [pl.BlockSpec(memory_space=pl.ANY)] * len(others),
            out_specs=[full(shape.shape) for shape in shapes],
            scratch_shapes=[pltpu.VMEM((groups, block), F32)],
        ),
        out_shape=shapes,
        compiler_params=params(),
        cost_estimate=cost(4 * rows * block * width, 12e6),
    )(meta, col, *others)
    return outs[0], outs[1:3], outs[3:]


def spread_kernel(choices, place_ref, spread_ref, *refs):
    out_ref, rows_ref = refs[-2:]
    for k, by_place in enumerate(choices):
        for which in sorted(set(by_place)):
            hit = functools.reduce(
                jnp.logical_or,
                [place_ref[0] == i for i, other in enumerate(by_place) if other == which],
            )

            @pl.when(hit)
            def _():
                tokens = refs[which].shape[0]
                rows_ref[k * tokens : (k + 1) * tokens] = refs[which][...]

    out_ref[...] = dot_nn(spread_ref[...], rows_ref[...]).astype(LOW)


def spread_rows(place, spread, found, turns, others):
    n = lax.axis_size("expert")
    order = arrival_order(n)
    distances = sorted({order[i][turn] - i for i in range(n) for turn in turns})
    choices = [[distances.index(order[i][turn] - i) for i in range(n)] for turn in turns]
    chunks = [found[distance] for distance in distances]
    tokens, wide = chunks[0].shape
    rows = spread.shape[0]
    return pl.pallas_call(
        functools.partial(spread_kernel, choices),
        grid_spec=pltpu.PrefetchScalarGridSpec(
            num_scalar_prefetch=1,
            grid=(1,),
            in_specs=[full(spread.shape)]
            + [full(chunk.shape) for chunk in chunks]
            + [pl.BlockSpec(memory_space=pl.ANY)] * len(others),
            out_specs=full((rows, wide)),
            scratch_shapes=[pltpu.VMEM((len(turns) * tokens, wide), LOW)],
        ),
        out_shape=jax.ShapeDtypeStruct((rows, wide), LOW),
        compiler_params=params(),
        cost_estimate=cost(2 * rows * len(turns) * tokens * wide, 5e6),
    )(place, spread, *chunks, *others)


def router_back_kernel(experts, *refs):
    sum_ref, g_ref, hidden_ref, gain_ref, router_ref, mask_ref, probs_ref = refs[:7]
    grad_ref, low_ref, dgain_ref, drouter_ref = refs[-4:]
    width = g_ref.shape[1]
    lanes = mask_ref.shape[1]
    total = sum_ref[...].astype(F32)
    table = total[:, width:]
    mask, probs = mask_ref[...], probs_ref[...]
    grad_gates = (table + pltpu.roll(table, lanes - experts, 1)) * mask
    chosen = probs * mask
    chosen_sum = jnp.sum(chosen, axis=1, keepdims=True)
    mean = jnp.sum(grad_gates * (chosen / chosen_sum), axis=1, keepdims=True)
    centred = mask * (grad_gates - mean) / chosen_sum
    grad_logits = probs * (centred - jnp.sum(centred * chosen, axis=1, keepdims=True))
    high, low = split_low(grad_logits)
    router = pad_rows(router_ref[...], lanes)
    grad = total[:, :width] + dot_nn(high, router) + dot_nn(low, router)
    normal, rr = norm_parts(hidden_ref[...])
    mixed = (normal * gain_ref[...]).astype(LOW)
    drouter_ref[...] = dot_tn(high, mixed) + dot_tn(low, mixed)
    dgain_ref[...] = jnp.sum(grad * normal, axis=0, keepdims=True)
    grad_hidden = g_ref[...].astype(F32) + norm_back(grad, normal, rr, gain_ref[...])
    grad_ref[...] = grad_hidden
    low_ref[...] = grad_hidden.astype(LOW)


def route_back(summed, g, hidden, gain, router, mask, probs, experts, others):
    tokens, width = g.shape
    lanes = mask.shape[1]
    operands = [summed, g, hidden, gain[None], router, mask, probs]
    shapes = [
        jax.ShapeDtypeStruct((tokens, width), F32),
        jax.ShapeDtypeStruct((tokens, width), LOW),
        jax.ShapeDtypeStruct((1, width), F32),
        jax.ShapeDtypeStruct((lanes, width), F32),
    ]
    return pl.pallas_call(
        functools.partial(router_back_kernel, experts),
        grid=(1,),
        in_specs=[full(value.shape) for value in operands]
        + [pl.BlockSpec(memory_space=pl.ANY)] * len(others),
        out_specs=[full(shape.shape) for shape in shapes],
        out_shape=shapes,
        compiler_params=params(),
        cost_estimate=cost(8 * tokens * width * lanes, 8e6),
    )(*operands, *others)


def combine_kernel(n_half, meta_ref, near_table_ref, far_table_ref, near_ref, far_ref, *rest):
    del meta_ref
    turn = pl.program_id(0)

    @pl.when(turn < n_half)
    def _():
        rest[-1][...] = dot_nn(near_table_ref[...], near_ref[...]).astype(LOW)

    @pl.when(turn >= n_half)
    def _():
        rest[-1][...] = dot_nn(far_table_ref[...], far_ref[...]).astype(LOW)


def combine_rows(meta, tables, rows, n_half, others):
    tokens = tables[0].shape[0] // n_half
    slots, wide = rows[0].shape
    n = 2 * n_half
    return pl.pallas_call(
        functools.partial(combine_kernel, n_half),
        grid_spec=pltpu.PrefetchScalarGridSpec(
            num_scalar_prefetch=1,
            grid=(n,),
            in_specs=[
                pl.BlockSpec((tokens, slots), lambda i, m: (jnp.minimum(i, n_half - 1), 0)),
                pl.BlockSpec((tokens, slots), lambda i, m: (jnp.maximum(i - n_half, 0), 0)),
            ]
            + [full(value.shape) for value in rows]
            + [pl.BlockSpec(memory_space=pl.ANY)] * len(others),
            out_specs=pl.BlockSpec((tokens, wide), lambda i, m: (m[1 + n + i], 0)),
        ),
        out_shape=jax.ShapeDtypeStruct((n * tokens, wide), LOW),
        compiler_params=params(),
        cost_estimate=cost(2 * slots * n * tokens * wide, 10e6),
    )(meta, *tables, *rows, *others)


def expert_kernel(experts, who_ref, x_ref, gate_ref, up_ref, pull_ref, *rest):
    act_ref, dgate_ref, dup_ref, copy_ref = rest[-4:]
    width = gate_ref.shape[0]
    x = x_ref[:, :width]
    table = x_ref[:, width:].astype(F32)
    lane = lax.broadcasted_iota(jnp.int32, table.shape, 1)
    mine = who_ref[0]
    gate = jnp.sum(
        jnp.where(jnp.logical_or(lane == mine, lane == mine + experts), table, 0.0),
        axis=1,
        keepdims=True,
    )
    pre_gate = dot_nn(x, gate_ref[...])
    pre_up = dot_nn(x, up_ref[...])
    pull = pull_ref[...].reshape(pre_up.shape)
    sig = 1.0 / (1.0 + jnp.exp(-pre_gate))
    silu = pre_gate * sig
    act = silu * pre_up
    act_ref[...] = (act * gate).astype(LOW)
    high, low = split_low(jnp.sum(act * pull, axis=1, keepdims=True))
    pull = pull * gate
    dup = (pull * silu).astype(LOW)
    dgate = (pull * pre_up * (sig * (1.0 + pre_gate * (1.0 - sig)))).astype(LOW)
    dgate_ref[...] = dgate
    dup_ref[...] = dup
    copy_ref[:, :width] = (dot_nt(dgate, gate_ref[...]) + dot_nt(dup, up_ref[...])).astype(LOW)
    back = jnp.where(lane == mine, high.astype(F32), 0.0)
    back = jnp.where(lane == mine + experts, low.astype(F32), back)
    copy_ref[:, width:] = back.astype(LOW)


def run_expert(who, x, w_gate, w_up, pull, part, experts):
    rows, wide = x.shape
    width, hidden = w_gate.shape
    groups, _, slots, _ = pull.shape
    each = groups // 2
    tile = each * slots
    by_rows = lambda columns: pl.BlockSpec((tile, columns), lambda i, p: (i, 0))
    return pl.pallas_call(
        functools.partial(expert_kernel, experts),
        grid_spec=pltpu.PrefetchScalarGridSpec(
            num_scalar_prefetch=1,
            grid=(2,),
            in_specs=[
                by_rows(wide),
                full(w_gate.shape),
                full(w_up.shape),
                pl.BlockSpec((each, 1, slots, hidden), lambda i, p: (i, part, 0, 0)),
            ],
            out_specs=[by_rows(hidden), by_rows(hidden), by_rows(hidden), by_rows(wide)],
        ),
        out_shape=[jax.ShapeDtypeStruct((rows, hidden), LOW)] * 3
        + [jax.ShapeDtypeStruct((rows, wide), LOW)],
        compiler_params=params(),
        cost_estimate=cost(8 * rows * width * hidden, 20e6, rows * hidden),
    )(who, x, w_gate, w_up, pull)


def input_kernel(grad_ref, x_ref, gain_ref, more_ref, out_ref):
    normal, rr = norm_parts(x_ref[...].astype(F32))
    grad = grad_ref[...].astype(F32)
    out_ref[...] = more_ref[...] + norm_back(grad, normal, rr, gain_ref[...])


def input_back(grad, x, gain, more):
    tokens, width = x.shape
    operands = [grad, x, gain[None], more]
    return pl.pallas_call(
        input_kernel,
        grid=(1,),
        in_specs=[full(value.shape) for value in operands],
        out_specs=full(more.shape),
        out_shape=jax.ShapeDtypeStruct((tokens, width), F32),
        compiler_params=params(),
        cost_estimate=cost(20 * tokens * width, 5e6),
    )(*operands)


def kv_back_kernel(factor, n_parts, c_ref, dkv_ref, *refs):
    parts = refs[:n_parts]
    proj_ref, gain_ref, cos_ref, sin_ref = refs[n_parts : n_parts + 4]
    grad_ref, dgain_ref = refs[-2:]
    size = proj_ref.shape[1]
    total = functools.reduce(jnp.add, [part[...].astype(F32) for part in parts], dkv_ref[...])
    grad, dgain = head_backward(
        total[:, :size] * factor, proj_ref[...], gain_ref[...], cos_ref[...], sin_ref[...]
    )
    grad_ref[:, :size] = grad.astype(LOW)
    grad_ref[:, size:] = total[:, size:].astype(LOW)
    dgain_ref[...] = dgain


def kv_back(context, dkv, parts, proj, gain, cos2, sin2, factor, others):
    block, size = proj.shape
    operands = [proj, gain[None], cos2, sin2]
    shapes = [
        jax.ShapeDtypeStruct((block, 2 * size), LOW),
        jax.ShapeDtypeStruct((1, size), F32),
    ]
    return pl.pallas_call(
        functools.partial(kv_back_kernel, factor, len(parts)),
        grid_spec=pltpu.PrefetchScalarGridSpec(
            num_scalar_prefetch=1,
            grid=(1,),
            in_specs=[pl.BlockSpec((block, 2 * size), lambda i, c: (c[0], 0))]
            + [full(part.shape) for part in parts]
            + [full(value.shape) for value in operands]
            + [pl.BlockSpec(memory_space=pl.ANY)] * len(others),
            out_specs=[full(shape.shape) for shape in shapes],
        ),
        out_shape=shapes,
        compiler_params=params(),
        cost_estimate=cost(40 * block * size, 5e6),
    )(context.astype(jnp.int32)[None], dkv, *parts, *operands, *others)


def dp_sum_kernel(d_ref, kept_ref, got_ref, *rest):
    total = kept_ref[...].astype(F32) + got_ref[...].astype(F32)
    rest[-1][...] = total.astype(LOW)


def dp_sum(grad, got, others):
    d = lax.axis_index("dp").astype(jnp.int32)[None]
    rows, columns = got.shape
    tiles = 2
    tile = rows // tiles
    return pl.pallas_call(
        dp_sum_kernel,
        grid_spec=pltpu.PrefetchScalarGridSpec(
            num_scalar_prefetch=1,
            grid=(tiles,),
            in_specs=[
                pl.BlockSpec((tile, columns), lambda i, d: (d[0] * tiles + i, 0)),
                pl.BlockSpec((tile, columns), lambda i, d: (i, 0)),
            ]
            + [pl.BlockSpec(memory_space=pl.ANY)] * len(others),
            out_specs=pl.BlockSpec((tile, columns), lambda i, d: (i, 0)),
        ),
        out_shape=jax.ShapeDtypeStruct((rows, columns), LOW),
        compiler_params=params(),
        cost_estimate=cost(rows * columns, 6 * rows * columns),
    )(d, grad, got, *others)


def normed_kernel(q_ref, kv_ref, wq_ref, wkv_ref, rows_ref, out_ref, dgain_ref):
    grad = dot_nt(q_ref[...], wq_ref[...]) + dot_nt(kv_ref[...], wkv_ref[...])
    out_ref[...] = grad.astype(LOW)
    dgain_ref[...] = jnp.sum(grad * rows_ref[...].astype(F32), axis=0, keepdims=True)


def normed_back(grad_q, grad_kv, w_q, w_kv, rows):
    block, width = rows.shape
    tile = 512
    column = lambda i: (0, i)
    return pl.pallas_call(
        normed_kernel,
        grid=(width // tile,),
        in_specs=[
            full(grad_q.shape),
            full(grad_kv.shape),
            pl.BlockSpec((tile, w_q.shape[1]), lambda i: (i, 0)),
            pl.BlockSpec((tile, w_kv.shape[1]), lambda i: (i, 0)),
            pl.BlockSpec((block, tile), column),
        ],
        out_specs=[pl.BlockSpec((block, tile), column), pl.BlockSpec((1, tile), column)],
        out_shape=[
            jax.ShapeDtypeStruct((block, width), LOW),
            jax.ShapeDtypeStruct((1, width), F32),
        ],
        compiler_params=params(),
        cost_estimate=cost(2 * block * width * (w_q.shape[1] + w_kv.shape[1]), 12e6),
    )(grad_q, grad_kv, w_q, w_kv, rows)


def pack_kernel(experts, router_ref, attn_ref, mlp_ref, q_ref, k_ref, out_ref, rows_ref):
    size = q_ref.shape[1]
    rows_ref[:experts] = router_ref[:experts]
    rows_ref[experts:] = jnp.zeros_like(rows_ref[experts:])
    rows_ref[experts : experts + 1] = attn_ref[...]
    rows_ref[experts + 1 : experts + 2] = mlp_ref[...]
    rows_ref[experts + 2 : experts + 3, :size] = q_ref[...]
    rows_ref[experts + 2 : experts + 3, size : 2 * size] = k_ref[...]
    out_ref[...] = rows_ref[...].astype(LOW)


def pack_small(experts, router, attn, mlp, q, k):
    width = attn.shape[1]
    shape = (-(-(experts + 3) // 16) * 16, width)
    operands = [router, attn, mlp, q, k]
    return pl.pallas_call(
        functools.partial(pack_kernel, experts),
        grid=(1,),
        in_specs=[full(value.shape) for value in operands],
        out_specs=full(shape),
        out_shape=jax.ShapeDtypeStruct(shape, LOW),
        scratch_shapes=[pltpu.VMEM(shape, F32)],
        compiler_params=params(),
        cost_estimate=cost(shape[0] * width, 6 * shape[0] * width),
    )(*operands)


def part_sum_kernel(parts_ref, out_ref):
    total = parts_ref[0].astype(F32)
    for k in range(1, parts_ref.shape[0]):
        total += parts_ref[k].astype(F32)
    out_ref[...] = total.astype(LOW)


def part_sum(parts):
    count, rows, columns = parts.shape
    tiles = 2
    return pl.pallas_call(
        part_sum_kernel,
        grid=(tiles,),
        in_specs=[pl.BlockSpec((count, rows // tiles, columns), lambda i: (0, i, 0))],
        out_specs=pl.BlockSpec((rows // tiles, columns), lambda i: (i, 0)),
        out_shape=jax.ShapeDtypeStruct((rows, columns), LOW),
        compiler_params=params(),
        cost_estimate=cost(count * rows * columns, 4 * count * rows * columns),
    )(parts)


def join_kernel(n_more, c_ref, parts_ref, *refs):
    del c_ref
    out_ref = refs[-1]
    count, _, columns = parts_ref.shape
    total = parts_ref[0].astype(F32)
    for k in range(1, count):
        total += parts_ref[k].astype(F32)
    total = total.astype(LOW)
    more = add_all(refs[:n_more]).astype(LOW) if n_more else None
    for k in range(count):
        out_ref[k, :, :columns] = total
        if n_more:
            out_ref[k, :, columns:] = more


def join_sums(parts, own, more, others):
    count, rows, columns = parts.shape
    c = lax.axis_index("context").astype(jnp.int32)[None]
    extra = [own, *more] if more else []
    wide = columns + (own.shape[1] if more else 0)
    tiles = 2
    tile = rows // tiles
    specs = []
    if more:
        specs = [pl.BlockSpec((tile, own.shape[1]), lambda i, c: (c[0] * tiles + i, 0))]
        specs += [pl.BlockSpec((tile, own.shape[1]), lambda i, c: (i, 0))] * len(more)
    return pl.pallas_call(
        functools.partial(join_kernel, len(extra)),
        grid_spec=pltpu.PrefetchScalarGridSpec(
            num_scalar_prefetch=1,
            grid=(tiles,),
            in_specs=[pl.BlockSpec((count, tile, columns), lambda i, c: (0, i, 0))]
            + specs
            + [pl.BlockSpec(memory_space=pl.ANY)] * len(others),
            out_specs=pl.BlockSpec((count, tile, wide), lambda i, c: (0, i, 0)),
        ),
        out_shape=jax.ShapeDtypeStruct((count, rows, wide), LOW),
        compiler_params=params(),
        cost_estimate=cost(count * rows * wide, 4 * count * rows * wide),
    )(c, parts, *extra, *others)


def widen_kernel(n_others, d_ref, kept_ref, got_ref, *outs):
    outs = outs[n_others:]
    first = 0
    for out_ref in outs:
        last = first + out_ref.shape[1]

        @pl.when(pl.program_id(0) == 0)
        def _():
            out_ref[...] = kept_ref[:, first:last].astype(F32)

        @pl.when(pl.program_id(0) == 1)
        def _():
            out_ref[...] = got_ref[:, first:last].astype(F32)

        first = last


def widen(kept, got, widths, others):
    d = lax.axis_index("dp").astype(jnp.int32)[None]
    rows, columns = kept.shape
    tiles = 4
    tile = rows // tiles
    return pl.pallas_call(
        functools.partial(widen_kernel, len(others)),
        grid_spec=pltpu.PrefetchScalarGridSpec(
            num_scalar_prefetch=1,
            grid=(2, tiles),
            in_specs=[
                pl.BlockSpec((tile, columns), lambda i, j, d: (j * (1 - i) + (tiles - 1) * i, 0)),
                pl.BlockSpec((tile, columns), lambda i, j, d: (j * i, 0)),
            ]
            + [pl.BlockSpec(memory_space=pl.ANY)] * len(others),
            out_specs=[
                pl.BlockSpec(
                    (tile, wide), lambda i, j, d: ((d[0] + i - 2 * d[0] * i) * tiles + j, 0)
                )
                for wide in widths
            ],
        ),
        out_shape=[jax.ShapeDtypeStruct((2 * rows, wide), F32) for wide in widths],
        compiler_params=params(),
        cost_estimate=cost(2 * rows * columns, 12 * rows * columns),
    )(d, kept, got, *others)


def sum_axis(total, axis):
    n = lax.axis_size(axis)
    sent = total.astype(LOW)
    total = total.astype(F32)
    for s in range(1, n):
        total += lax.ppermute(sent, axis, [(i, (i + s) % n) for i in range(n)]).astype(F32)
    return total


def swap_dp(rows):
    return lax.ppermute(rows, "dp", [(0, 1), (1, 0)])


def swap_context(rows, s):
    n = lax.axis_size("context")
    return lax.ppermute(rows, "context", [(i, i ^ s) for i in range(n)])


def dp_got(grad):
    d = lax.axis_index("dp")
    rows = grad.shape[0] // 2
    return swap_dp(lax.dynamic_slice_in_dim(grad, (1 - d) * rows, rows))


def share_context(parts):
    return lax.all_to_all(parts, "context", split_axis=0, concat_axis=0, tiled=True)


def arrival_order(n):
    return [sorted(range(n), key=lambda j: (abs(j - i), j)) for i in range(n)]


def choose(index, options):
    distinct = []
    for option in options:
        if option is not None and not any(option is other for other in distinct):
            distinct.append(option)
    result = distinct[0]
    for option in distinct[1:]:
        mask = functools.reduce(
            jnp.logical_or, [index == i for i, other in enumerate(options) if other is option]
        )
        result = jnp.where(mask, option, result)
    return result


def line_gather(chunk):
    return line_steps({0: chunk}, 1, lax.axis_size("expert"))


def line_steps(found, first, stop):
    n = lax.axis_size("expert")
    found = dict(found)
    for s in range(first, stop):
        found[-s] = lax.ppermute(
            found[1 - s], "expert", [(i, i + 1) for i in range(s - 1, n - 1)]
        )
        found[s] = lax.ppermute(found[s - 1], "expert", [(i + 1, i) for i in range(n - s)])
    return found


def context_gather(rows):
    n = lax.axis_size("context")
    c = lax.axis_index("context")
    found = {0: rows}
    for s in range(1, n):
        found[s] = lax.ppermute(rows, "context", [(i, i ^ s) for i in range(n)])
    return jnp.concatenate([choose(c, [found[i ^ j] for i in range(n)]) for j in range(n)], axis=0)


def context_parts(rows, extra):
    n = lax.axis_size("context")
    c = lax.axis_index("context")
    each = rows.shape[0] // n
    return [
        swap_context((lax.dynamic_slice_in_dim(rows, (c ^ s) * each, each) + extra).astype(LOW), s)
        for s in range(1, n)
    ]


def zero_of(*others):
    return functools.reduce(
        jnp.add,
        [
            lax.slice(other, (0,) * other.ndim, (1,) * other.ndim).reshape(()).astype(F32) * 0.0
            for other in others
        ],
    )


def after(value, *others):
    return (value.astype(F32) + zero_of(*others)).astype(value.dtype)


def on_device(
    layer_input,
    grad_output,
    attn_gain,
    query_weight,
    key_weight,
    value_weight,
    q_gain,
    k_gain,
    output_weight,
    mlp_gain,
    router,
    w_gate,
    w_up,
    w_down,
    routes,
    half_order,
):
    n_context = lax.axis_size("context")
    n_expert = lax.axis_size("expert")
    n_groups = lax.axis_size(GROUP_AXES)
    tok_dev, width = layer_input.shape[1:]
    size = q_gain.shape[0]
    kv_total = key_weight.shape[1] * n_expert
    group_dev = n_expert // (kv_total // size)
    kv_index = lax.axis_index("expert") // group_dev
    block = tok_dev * n_expert
    seq = block * n_context
    half = block // 2
    experts = router.shape[1]
    exp_dev = w_gate.shape[0]
    top = routes.shape[2]
    capacity = max(2, (tok_dev * top * 9 + 8 * experts - 1) // (8 * experts))
    scale = size ** (-0.5)

    seq_rows = jnp.arange(seq, dtype=jnp.int32)
    context = lax.axis_index("context")
    own_halves = lax.dynamic_slice_in_dim(half_order, 2 * context, 2)
    own_pos = (own_halves[:, None] * half + jnp.arange(half, dtype=jnp.int32)[None]).reshape(-1)
    per_half = half // TILE
    tile_pos = (half_order[:, None] * per_half + jnp.arange(per_half, dtype=jnp.int32)).reshape(-1)
    kidx = jnp.sum(
        (tile_pos[None, :] == jnp.arange(seq // TILE, dtype=jnp.int32)[:, None])
        * jnp.arange(seq // TILE, dtype=jnp.int32)[None, :],
        axis=1,
    ).astype(jnp.int32)
    qpos = lax.dynamic_slice_in_dim(tile_pos, context * (block // TILE), block // TILE)
    entry = jnp.arange(size)
    freq = jnp.power(THETA, -(2 * (entry % (size // 2))).astype(F32) / size)
    angles = own_pos.astype(F32)[:, None] * freq[None, :]
    cos2 = jnp.cos(angles)
    sin2 = jnp.sin(angles) * jnp.where(entry < size // 2, -1.0, 1.0)[None, :]

    place = lax.axis_index("expert")
    place_1 = place.astype(jnp.int32)[None]
    lanes = -(-2 * experts // 128) * 128
    mask = jnp.any(
        routes[0][:, :, None] == jnp.arange(lanes, dtype=jnp.int32)[None, None, :], axis=1
    )
    mask_wide = mask.astype(F32)
    router_rows = router.T

    x_low = layer_input[0]
    x_normal, _ = norm_parts(x_low.astype(F32))
    normed_found = line_gather((x_normal * attn_gain).astype(LOW))
    if group_dev == 1:
        kv_weights = jnp.concatenate([key_weight, value_weight], axis=1)
    else:
        key_whole = lax.all_gather(key_weight, "expert", axis=1, tiled=True)
        value_whole = lax.all_gather(value_weight, "expert", axis=1, tiled=True)
        kv_weights = jnp.concatenate(
            [
                lax.dynamic_slice_in_dim(key_whole, kv_index * size, size, 1),
                lax.dynamic_slice_in_dim(value_whole, kv_index * size, size, 1),
            ],
            axis=1,
        )
    grad_low = grad_output[0]
    normed_rows, own_kv, key_proj, grad_wide = project_keys(
        place_1,
        normed_found,
        kv_weights,
        k_gain,
        cos2,
        sin2,
        scale * LOG2E,
        grad_low,
        mask_wide,
    )
    grad_col = lax.all_gather(grad_wide, "expert", axis=0, tiled=True)
    kv_whole = context_gather(own_kv)
    queries, query_proj = project_queries(normed_rows, query_weight, q_gain, cos2, sin2)

    n_half = n_expert // 2
    order_here = jnp.asarray(arrival_order(n_expert), jnp.int32)[place]
    turn_here = jnp.sum(
        (order_here[:, None] == jnp.arange(n_expert, dtype=jnp.int32)[None, :])
        * jnp.arange(n_expert, dtype=jnp.int32)[:, None],
        axis=0,
    ).astype(jnp.int32)
    meta = jnp.concatenate([place_1, turn_here, order_here])
    grad_sent, spreads, back_tables = make_tables(
        meta, grad_col, width, n_groups, n_half, capacity, []
    )

    def swap_plane(rows):
        parts = rows.reshape(n_groups, -1, rows.shape[1])
        parts = lax.all_to_all(parts, GROUP_AXES, split_axis=0, concat_axis=0, tiled=True)
        return parts.reshape(rows.shape)

    attended, inverse = attend(qpos, kidx, queries, kv_whole, [])
    attn_part = (dot_nn(attended, output_weight) + zero_of(grad_sent)).astype(LOW)
    attn_rows = lax.psum_scatter(attn_part, "expert", scatter_dimension=0, tiled=True)

    grad_x = swap_plane(grad_sent)
    act_pull = dot_nt(grad_x, w_down[0]).reshape(n_groups, 2, n_half * capacity, -1)

    hidden, mixed, probs = route_rows(
        x_low, attn_rows, mlp_gain, router_rows, mask_wide, experts, []
    )

    who = (lax.axis_index(ALL_AXES) * exp_dev).astype(jnp.int32)[None]
    mixed_found = line_gather(mixed)
    near = spread_rows(place_1, spreads[0], mixed_found, range(n_half), [grad_x])
    x_near = swap_plane(near)
    worked_near = run_expert(who, x_near, w_gate[0], w_up[0], act_pull, 0, experts)
    far = spread_rows(place_1, spreads[1], mixed_found, range(n_half, n_expert), [x_near])
    x_far = swap_plane(far)
    worked_far = run_expert(who, x_far, w_gate[0], w_up[0], act_pull, 1, experts)
    xs = [x_near, x_far]
    acts, gate_lows, up_lows, copies = (list(pair) for pair in zip(worked_near, worked_far))
    back_far = swap_plane(copies[1])
    back_near = swap_plane(copies[0])
    join = lambda parts: jnp.concatenate(parts, axis=0)
    x_all = join([x[:, :width] for x in xs])
    grad_w_gate = dot_tn(x_all, join(gate_lows))
    grad_w_up = dot_tn(x_all, join(up_lows))
    grad_by_round = jnp.swapaxes(
        grad_x.reshape(n_groups, 2, n_half * capacity, width), 0, 1
    ).reshape(-1, width)
    grad_w_down = dot_tn(join(acts), grad_by_round)
    copies_col = combine_rows(
        meta, back_tables, [back_near, back_far], n_half, [grad_w_gate, grad_w_up]
    )
    copies_sum = lax.psum_scatter(copies_col, "expert", scatter_dimension=0, tiled=True)

    returned = [dot_nn(act, w_down[0]).astype(LOW) for act in acts]
    returned_near = swap_plane(returned[0])

    grad_hidden, grad_hidden_low, grad_mlp_gain, grad_router = route_back(
        copies_sum,
        grad_low,
        hidden,
        mlp_gain,
        router_rows,
        mask_wide,
        probs,
        experts,
        [returned_near, grad_w_down],
    )

    returned_far = swap_plane(returned[1])
    grad_attn = lax.all_gather(grad_hidden_low, "expert", axis=0, tiled=True)
    grad_o, centre = grad_attended(
        grad_attn, output_weight, attended, inverse, [returned_far]
    )
    w_out = token_dot(attended, grad_attn, [])
    w_out_parts = swap_plane(w_out)
    grad_kv, grad_q, grad_q_gain = attend_back(
        qpos, kidx, queries, grad_o, centre, kv_whole, query_proj, q_gain, cos2, sin2, [w_out]
    )
    kv_parts = context_parts(grad_kv, zero_of(w_out_parts))
    w_query = token_dot(normed_rows, grad_q, [])
    w_query_got = dp_got(w_query)

    kv_grads, grad_k_gain = kv_back(
        context, grad_kv, kv_parts, key_proj, k_gain, cos2, sin2, scale, [w_query_got]
    )
    grad_normed, gain_rows = normed_back(grad_q, kv_grads, query_weight, kv_weights, normed_rows)
    grad_attn_gain = gain_rows / attn_gain[None]
    grad_normed = lax.psum_scatter(grad_normed, "expert", scatter_dimension=0, tiled=True)
    grad_input = input_back(grad_normed, x_low, attn_gain, grad_hidden)
    small = pack_small(
        experts, grad_router, grad_attn_gain, grad_mlp_gain, grad_q_gain, grad_k_gain
    )
    small_dp = sum_axis(small, "dp")
    small_context = sum_axis(small_dp, "context")
    small_sum = sum_axis(small_context, "expert")

    combined = combine_rows(meta, back_tables, [returned_near, returned_far], n_half, [])
    output_rows = lax.psum_scatter(combined, "expert", scatter_dimension=0, tiled=True)
    output_rows = hidden + output_rows.astype(F32) + zero_of(grad_normed)

    w_out_half = context_gather(part_sum(w_out_parts.reshape(n_groups, -1, width)))
    w_query_half = dp_sum(w_query, w_query_got, [*kv_parts, w_out_half])
    w_query_parts = share_context(w_query_half.reshape(n_context, -1, w_query_half.shape[1]))
    w_kv = token_dot(normed_rows, kv_grads, [])
    if group_dev == 1:
        w_kv_half = dp_sum(w_kv, dp_got(w_kv), [])
        w_kv_parts = context_parts(w_kv_half, 0.0)
        widths = [query_weight.shape[1], key_weight.shape[1], value_weight.shape[1]]
    else:
        w_kv_half, w_kv_parts = None, []
        widths = [query_weight.shape[1]]
    joined = join_sums(w_query_parts, w_kv_half, w_kv_parts, [small_dp])
    joined = share_context(joined).reshape(w_query_half.shape[0], -1)
    (grad_w_out,) = widen(w_out_half, swap_dp(w_out_half), [width], [])
    grad_w_query, *more = widen(joined, swap_dp(joined), widths, [small_context])
    if group_dev == 1:
        grad_w_key, grad_w_value = more
    else:
        blank = jnp.zeros((width, kv_total), LOW)
        pieces = []
        for part in (w_kv[:, :size], w_kv[:, size:]):
            padded = lax.dynamic_update_slice(blank, part, (0, kv_index * size))
            pieces.append(lax.psum_scatter(padded, "expert", scatter_dimension=1, tiled=True))
        grad_w_key, grad_w_value = (lax.psum(piece, GROUP_AXES).astype(F32) for piece in pieces)
    grad_attn_gain, grad_mlp_gain = small_sum[experts], small_sum[experts + 1]
    grad_q_gain = small_sum[experts + 2, :size]
    grad_k_gain = small_sum[experts + 2, size : 2 * size]
    return (
        output_rows.astype(LOW)[None],
        grad_input[None],
        grad_attn_gain,
        grad_w_query,
        grad_w_key,
        grad_w_value,
        grad_q_gain,
        grad_k_gain,
        grad_w_out,
        grad_mlp_gain,
        small_sum[:experts].T,
        grad_w_gate[None],
        grad_w_up[None],
        grad_w_down[None],
    )


def solution(mesh):
    rows = P("dp", ("context", "expert"), None)
    expert = P(ALL_AXES, None, None)
    columns = P(None, "expert")
    in_specs = (
        rows,
        rows,
        P(),
        columns,
        columns,
        columns,
        P(),
        P(),
        P("expert", None),
        P(),
        P(),
        expert,
        expert,
        expert,
        rows,
        P(),
    )
    out_specs = (
        rows,
        rows,
        P(),
        columns,
        columns,
        columns,
        P(),
        P(),
        P("expert", None),
        P(),
        P(),
        expert,
        expert,
        expert,
    )
    return jax.shard_map(
        on_device, mesh=mesh, in_specs=in_specs, out_specs=out_specs, check_vma=False
    )
```

```python
import functools
import math

import jax
import jax.numpy as jnp
from jax import lax
from jax.experimental import pallas as pl
from jax.experimental.pallas import tpu as pltpu
from jax.sharding import PartitionSpec as P

EPS = 1e-06
THETA = 1000000.0
TILE = 256
VMEM_BYTES = 56 * 1024 * 1024
LOG2E = math.log2(math.e)
LOW = jnp.bfloat16
F32 = jnp.float32
ALL_AXES = ("dp", "context", "expert")
GROUP_AXES = ("dp", "context")


def dot_nn(a, b):
    return lax.dot_general(a, b, (((1,), (0,)), ((), ())), preferred_element_type=F32)


def dot_nt(a, b):
    return lax.dot_general(a, b, (((1,), (1,)), ((), ())), preferred_element_type=F32)


def dot_tn(a, b):
    return lax.dot_general(a, b, (((0,), (0,)), ((), ())), preferred_element_type=F32)


def params(**more):
    return pltpu.CompilerParams(vmem_limit_bytes=VMEM_BYTES, **more)


def cost(flops, nbytes, exps=0):
    return pl.CostEstimate(flops=int(flops), bytes_accessed=int(nbytes), transcendentals=int(exps))


def head_forward(u, gain, cos2, sin2):
    rr = lax.rsqrt(jnp.mean(u * u, axis=-1, keepdims=True) + EPS)
    y = u * rr * gain
    return y * cos2 + pltpu.roll(y, 64, 1) * sin2


def head_backward(gy, u, gain, cos2, sin2):
    g = gy * cos2 - pltpu.roll(gy, 64, 1) * sin2
    rr = lax.rsqrt(jnp.mean(u * u, axis=-1, keepdims=True) + EPS)
    n = u * rr
    gn = g * gain
    grad = rr * (gn - n * jnp.mean(gn * n, axis=-1, keepdims=True))
    return grad, jnp.sum(g * n, axis=0, keepdims=True)


def query_kernel(x_ref, w_ref, gain_ref, cos_ref, sin_ref, rot_ref, proj_ref):
    tiles, heads, rows, size = rot_ref.shape
    acc = dot_nn(x_ref[...], w_ref[...])
    for h in range(heads):
        u = acc[:, h * size : (h + 1) * size]
        rot = head_forward(u, gain_ref[...], cos_ref[...], sin_ref[...])
        proj_ref[:, h] = u.reshape(tiles, rows, size)
        rot_ref[:, h] = rot.astype(LOW).reshape(tiles, rows, size)


def project_queries(normed, weight, gain, cos2, sin2):
    block, width = normed.shape
    size = cos2.shape[1]
    heads = weight.shape[1] // size
    tiles = block // TILE
    whole = lambda i: (0, 0)
    per = lambda i: (0, i, 0, 0)
    shape = (tiles, heads, TILE, size)
    return pl.pallas_call(
        query_kernel,
        grid=(heads // 2,),
        in_specs=[
            pl.BlockSpec((block, width), whole),
            pl.BlockSpec((width, 2 * size), lambda i: (0, i)),
            pl.BlockSpec((1, size), whole),
            pl.BlockSpec((block, size), whole),
            pl.BlockSpec((block, size), whole),
        ],
        out_specs=[pl.BlockSpec((tiles, 2, TILE, size), per)] * 2,
        out_shape=[jax.ShapeDtypeStruct(shape, LOW), jax.ShapeDtypeStruct(shape, F32)],
        compiler_params=params(),
        cost_estimate=cost(2 * block * width * heads * size, 12e6),
    )(normed, weight, gain[None], cos2, sin2)


def put_in_order(place, refs, out_ref):
    n = (len(refs) + 1) // 2
    rows = refs[0].shape[0]
    for distance in range(1 - n, n):
        ref = refs[distance + n - 1]
        at = place + distance

        @pl.when(jnp.logical_and(at >= 0, at < n))
        def _():
            out_ref[pl.ds(pl.multiple_of(at * rows, rows), rows), :] = ref[...]


def chunk_list(found):
    n = (len(found) + 1) // 2
    return [found[distance] for distance in range(1 - n, n)]


def key_kernel(factor, n_chunks, place_ref, *refs):
    w_ref, gain_ref, cos_ref, sin_ref, g_ref, mask_ref = refs[n_chunks:-4]
    rows_ref, kv_ref, proj_ref, wide_ref = refs[-4:]
    size = proj_ref.shape[1]
    width = g_ref.shape[1]
    put_in_order(place_ref[0], refs[:n_chunks], rows_ref)
    wide_ref[:, :width] = g_ref[...]
    wide_ref[:, width:] = mask_ref[...].astype(LOW)
    acc = dot_nn(rows_ref[...], w_ref[...])
    u = acc[:, :size]
    rot = head_forward(u, gain_ref[...], cos_ref[...], sin_ref[...])
    proj_ref[...] = u
    kv_ref[:, :size] = (rot * factor).astype(LOW)
    kv_ref[:, size:] = acc[:, size:].astype(LOW)


def full(shape):
    return pl.BlockSpec(shape, lambda *_: (0,) * len(shape))


def project_keys(place, found, weight, gain, cos2, sin2, factor, g, mask):
    chunks = chunk_list(found)
    rows, width = chunks[0].shape
    block, size = cos2.shape
    operands = [*chunks, weight, gain[None], cos2, sin2, g, mask]
    shapes = [
        jax.ShapeDtypeStruct((block, width), LOW),
        jax.ShapeDtypeStruct((block, 2 * size), LOW),
        jax.ShapeDtypeStruct((block, size), F32),
        jax.ShapeDtypeStruct((rows, width + mask.shape[1]), LOW),
    ]
    return pl.pallas_call(
        functools.partial(key_kernel, factor, len(chunks)),
        grid_spec=pltpu.PrefetchScalarGridSpec(
            num_scalar_prefetch=1,
            grid=(1,),
            in_specs=[full(x.shape) for x in operands],
            out_specs=[full(x.shape) for x in shapes],
        ),
        out_shape=shapes,
        compiler_params=params(),
        cost_estimate=cost(4 * block * width * size, 8e6),
    )(place, *operands)


def in_order(last, step):
    lax.fori_loop(0, lax.div(last, 2), lambda p, c: (step([2 * p, 2 * p + 1], False), c)[1], 0)

    @pl.when(lax.rem(last, 2) == 1)
    def _():
        step([last - 1, last], True)

    @pl.when(lax.rem(last, 2) == 0)
    def _():
        step([last], True)


def attend_kernel(qpos_ref, kidx_ref, q_ref, kv_ref, *rest):
    out_ref, inv_ref, acc_ref = rest[-3:]
    heads, rows, size = q_ref.shape[1:]
    acc_ref[...] = jnp.zeros_like(acc_ref)

    def step(places, masked):
        starts = [pl.multiple_of(kidx_ref[place] * rows, rows) for place in places]
        count = len(places) * rows
        keys = jnp.concatenate([kv_ref[pl.ds(start, rows), :size] for start in starts], axis=0)
        values = jnp.concatenate([kv_ref[pl.ds(start, rows), size:] for start in starts], axis=0)
        values = jnp.concatenate([values, jnp.ones((count, size), LOW)], axis=1)
        for h in range(heads):
            e = jnp.exp2(dot_nt(q_ref[0, h], keys))
            if masked:
                qi = lax.broadcasted_iota(jnp.int32, e.shape, 0)
                ki = lax.broadcasted_iota(jnp.int32, e.shape, 1) - (count - rows)
                e = jnp.where(ki <= qi, e, 0.0)
            acc_ref[h] += dot_nn(e.astype(LOW), values)

    in_order(qpos_ref[pl.program_id(0)], step)
    for h in range(heads):
        inv = 1.0 / acc_ref[h, :, size:]
        inv_ref[0, h] = inv
        out_ref[:, h * size : (h + 1) * size] = (acc_ref[h, :, :size] * inv).astype(LOW)


def attend(qpos, kidx, queries, kv, others):
    tiles, heads, rows, size = queries.shape
    seq = kv.shape[0]
    return pl.pallas_call(
        attend_kernel,
        grid_spec=pltpu.PrefetchScalarGridSpec(
            num_scalar_prefetch=2,
            grid=(tiles,),
            in_specs=[
                pl.BlockSpec((1, heads, rows, size), lambda i, a, b: (i, 0, 0, 0)),
                pl.BlockSpec((seq, 2 * size), lambda i, a, b: (0, 0)),
            ]
            + [pl.BlockSpec(memory_space=pl.ANY)] * len(others),
            out_specs=[
                pl.BlockSpec((rows, heads * size), lambda i, a, b: (i, 0)),
                pl.BlockSpec((1, heads, rows, size), lambda i, a, b: (i, 0, 0, 0)),
            ],
            scratch_shapes=[pltpu.VMEM((heads, rows, 2 * size), F32)],
        ),
        out_shape=[
            jax.ShapeDtypeStruct((tiles * rows, heads * size), LOW),
            jax.ShapeDtypeStruct((tiles, heads, rows, size), F32),
        ],
        compiler_params=params(),
        cost_estimate=cost(
            6 * tiles * rows * heads * seq * size, 8e6, tiles * rows * heads * seq
        ),
    )(qpos, kidx, queries, kv, *others)


def grad_out_kernel(rows_ref, w_ref, o_ref, inv_ref, *rest):
    do_ref, centre_ref = rest[-2:]
    tiles, heads, rows, size = do_ref.shape
    acc = dot_nt(rows_ref[...], w_ref[...])
    for t in range(tiles):
        for h in range(heads):
            part = slice(t * rows, (t + 1) * rows), slice(h * size, (h + 1) * size)
            low = (acc[part] * inv_ref[t, h]).astype(LOW)
            do_ref[t, h] = low
            product = low.astype(F32) * o_ref[part].astype(F32)
            centre = jnp.sum(jnp.transpose(product), axis=0, keepdims=True)
            centre_ref[t, h] = jnp.broadcast_to(centre, (8, rows))


def grad_attended(grad_rows, weight, attended, inverse, others):
    tiles, heads, rows, size = inverse.shape
    block, width = grad_rows.shape
    return pl.pallas_call(
        grad_out_kernel,
        grid=(heads // 2,),
        in_specs=[
            pl.BlockSpec((block, width), lambda i: (0, 0)),
            pl.BlockSpec((2 * size, width), lambda i: (i, 0)),
            pl.BlockSpec((block, 2 * size), lambda i: (0, i)),
            pl.BlockSpec((tiles, 2, rows, size), lambda i: (0, i, 0, 0)),
        ]
        + [pl.BlockSpec(memory_space=pl.ANY)] * len(others),
        out_specs=[
            pl.BlockSpec((tiles, 2, rows, size), lambda i: (0, i, 0, 0)),
            pl.BlockSpec((tiles, 2, 8, rows), lambda i: (0, i, 0, 0)),
        ],
        out_shape=[
            jax.ShapeDtypeStruct((tiles, heads, rows, size), LOW),
            jax.ShapeDtypeStruct((tiles, heads, 8, rows), F32),
        ],
        compiler_params=params(),
        cost_estimate=cost(2 * block * width * heads * size, 12e6),
    )(grad_rows, weight, attended, inverse, *others)


def attend_back_kernel(
    qpos_ref,
    kidx_ref,
    q_ref,
    do_ref,
    centre_ref,
    kv_ref,
    proj_ref,
    gain_ref,
    cos_ref,
    sin_ref,
    *rest,
):
    dkv_ref, dq_ref, dgain_ref, acc_ref, e_ref, ds_ref = rest[-6:]
    heads, rows, size = q_ref.shape[1:]

    @pl.when(pl.program_id(0) == 0)
    def _():
        dkv_ref[...] = jnp.zeros_like(dkv_ref)
        dgain_ref[...] = jnp.zeros_like(dgain_ref)

    acc_ref[...] = jnp.zeros_like(acc_ref)

    def step(places, masked):
        starts = [pl.multiple_of(kidx_ref[place] * rows, rows) for place in places]
        count = len(places) * rows
        keys = jnp.concatenate([kv_ref[pl.ds(start, rows), :size] for start in starts], axis=0)
        values = jnp.concatenate([kv_ref[pl.ds(start, rows), size:] for start in starts], axis=0)
        for h in range(heads):
            query, grad = q_ref[0, h], do_ref[0, h]
            e = jnp.exp2(dot_nt(keys, query))
            if masked:
                ki = lax.broadcasted_iota(jnp.int32, e.shape, 0) - (count - rows)
                qi = lax.broadcasted_iota(jnp.int32, e.shape, 1)
                e = jnp.where(ki <= qi, e, 0.0)
            ds = (e * (dot_nt(values, grad) - centre_ref[0, h, 0:1])).astype(LOW)
            e_ref[:count, h * rows : (h + 1) * rows] = e.astype(LOW)
            ds_ref[:count, h * rows : (h + 1) * rows] = ds
            acc_ref[h] += dot_tn(ds, keys)
        dk = dot_nn(ds_ref[:count], q_ref[0].reshape(heads * rows, size))
        dv = dot_nn(e_ref[:count], do_ref[0].reshape(heads * rows, size))
        for k, start in enumerate(starts):
            dkv_ref[pl.ds(start, rows), :size] += dk[k * rows : (k + 1) * rows]
            dkv_ref[pl.ds(start, rows), size:] += dv[k * rows : (k + 1) * rows]

    in_order(qpos_ref[pl.program_id(0)], step)
    total = jnp.zeros((1, size), F32)
    for h in range(heads):
        grad, gain_part = head_backward(
            acc_ref[h] * (1.0 / LOG2E), proj_ref[0, h], gain_ref[...], cos_ref[...], sin_ref[...]
        )
        dq_ref[:, h * size : (h + 1) * size] = grad.astype(LOW)
        total += gain_part
    dgain_ref[...] += total


def attend_back(qpos, kidx, queries, grads, centre, kv, proj, gain, cos2, sin2, others):
    tiles, heads, rows, size = queries.shape
    seq = kv.shape[0]
    per = pl.BlockSpec((1, heads, rows, size), lambda i, a, b: (i, 0, 0, 0))
    flat = lambda i, a, b: (0, 0)
    rowwise = lambda i, a, b: (i, 0)
    return pl.pallas_call(
        attend_back_kernel,
        grid_spec=pltpu.PrefetchScalarGridSpec(
            num_scalar_prefetch=2,
            grid=(tiles,),
            in_specs=[
                per,
                per,
                pl.BlockSpec((1, heads, 8, rows), lambda i, a, b: (i, 0, 0, 0)),
                pl.BlockSpec((seq, 2 * size), flat),
                per,
                pl.BlockSpec((1, size), flat),
                pl.BlockSpec((rows, size), rowwise),
                pl.BlockSpec((rows, size), rowwise),
            ]
            + [pl.BlockSpec(memory_space=pl.ANY)] * len(others),
            out_specs=[
                pl.BlockSpec((seq, 2 * size), flat),
                pl.BlockSpec((rows, heads * size), rowwise),
                pl.BlockSpec((1, size), flat),
            ],
            scratch_shapes=[pltpu.VMEM((heads, rows, size), F32)]
            + [pltpu.VMEM((2 * rows, heads * rows), LOW)] * 2,
        ),
        out_shape=[
            jax.ShapeDtypeStruct((seq, 2 * size), F32),
            jax.ShapeDtypeStruct((tiles * rows, heads * size), LOW),
            jax.ShapeDtypeStruct((1, size), F32),
        ],
        compiler_params=params(),
        cost_estimate=cost(
            15 * tiles * rows * heads * seq * size, 12e6, tiles * rows * heads * seq
        ),
    )(qpos, kidx, queries, grads, centre, kv, proj, gain[None], cos2, sin2, *others)


def token_kernel(a_ref, b_ref, *rest):
    rest[-1][...] = dot_tn(a_ref[...], b_ref[...]).astype(LOW)


def token_dot(a, b, others):
    block, rows = a.shape
    columns = b.shape[1]
    tile = min(rows, 512)
    return pl.pallas_call(
        token_kernel,
        grid=(rows // tile,),
        in_specs=[
            pl.BlockSpec((block, tile), lambda i: (0, i)),
            pl.BlockSpec((block, columns), lambda i: (0, 0)),
        ]
        + [pl.BlockSpec(memory_space=pl.ANY)] * len(others),
        out_specs=pl.BlockSpec((tile, columns), lambda i: (i, 0)),
        out_shape=jax.ShapeDtypeStruct((rows, columns), LOW),
        compiler_params=params(),
        cost_estimate=cost(2 * block * rows * columns, 6e6),
    )(a, b, *others)


def split_low(value):
    high = value.astype(LOW)
    return high, (value - high.astype(F32)).astype(LOW)


def norm_parts(rows):
    rr = lax.rsqrt(jnp.mean(rows * rows, axis=-1, keepdims=True) + EPS)
    return rows * rr, rr


def norm_back(grad, normal, rr, gain):
    weighted = grad * gain
    return rr * (weighted - normal * jnp.mean(weighted * normal, axis=-1, keepdims=True))


def add_all(refs):
    return functools.reduce(jnp.add, [ref[...].astype(F32) for ref in refs])


def pad_rows(rows, count):
    if rows.shape[0] == count:
        return rows
    return jnp.concatenate(
        [rows, jnp.zeros((count - rows.shape[0], rows.shape[1]), rows.dtype)], axis=0
    )


def router_kernel(experts, *refs):
    x_ref, attn_ref, gain_ref, router_ref, mask_ref = refs[:5]
    hidden_ref, mixed_ref, probs_ref = refs[-3:]
    width = x_ref.shape[1]
    lanes = mask_ref.shape[1]
    hidden = add_all([x_ref, attn_ref])
    hidden_ref[...] = hidden
    mixed = (norm_parts(hidden)[0] * gain_ref[...]).astype(LOW)
    mixed_ref[:, :width] = mixed
    logits = dot_nt(mixed, pad_rows(router_ref[...], lanes))
    lane = lax.broadcasted_iota(jnp.int32, logits.shape, 1)
    logits = jnp.where(lane < experts, logits, -1e30)
    weights = jnp.exp(logits - jnp.max(logits, axis=1, keepdims=True))
    probs = weights / jnp.sum(weights, axis=1, keepdims=True)
    probs_ref[...] = probs
    chosen = probs * mask_ref[...]
    high, low = split_low(chosen / jnp.sum(chosen, axis=1, keepdims=True))
    both = high.astype(F32) + pltpu.roll(low.astype(F32), experts, 1)
    mixed_ref[:, width:] = both.astype(LOW)


def route_rows(x, attn, gain, router, mask, experts, others):
    tokens, width = x.shape
    lanes = mask.shape[1]
    operands = [x, attn, gain[None], router, mask]
    shapes = [
        jax.ShapeDtypeStruct((tokens, width), F32),
        jax.ShapeDtypeStruct((tokens, width + lanes), LOW),
        jax.ShapeDtypeStruct((tokens, lanes), F32),
    ]
    return pl.pallas_call(
        functools.partial(router_kernel, experts),
        grid=(1,),
        in_specs=[full(value.shape) for value in operands]
        + [pl.BlockSpec(memory_space=pl.ANY)] * len(others),
        out_specs=[full(shape.shape) for shape in shapes],
        out_shape=shapes,
        compiler_params=params(),
        cost_estimate=cost(2 * tokens * width * lanes, 5e6),
    )(*operands, *others)


def table_kernel(capacity, n_half, meta_ref, col_ref, *rest):
    rows_ref, near_ref, far_ref, near_back_ref, far_back_ref, slots_ref = rest[-6:]
    block = col_ref.shape[0]
    rows, width = rows_ref.shape
    n = 2 * n_half
    tokens = block // n
    cap_half = n_half * capacity
    groups = rows // (2 * cap_half)
    mask = col_ref[:, width:]
    lanes = mask.shape[1]
    padded = -(-groups // 16) * 16
    group = lax.broadcasted_iota(jnp.int32, (padded, lanes), 0)
    lane = lax.broadcasted_iota(jnp.int32, (padded, lanes), 1)
    wanted = jnp.logical_and(lane == group * n + meta_ref[0], group < groups)
    hits = dot_nt(jnp.where(wanted, 1.0, 0.0).astype(LOW), mask)
    before = lax.broadcasted_iota(jnp.int32, (tokens, tokens), 0)
    after_it = lax.broadcasted_iota(jnp.int32, (tokens, tokens), 1)
    earlier = jnp.where(before < after_it, 1.0, 0.0).astype(LOW)
    for z in range(n):
        hit = hits[:, z * tokens : (z + 1) * tokens]
        rank = dot_nn(hit.astype(LOW), earlier)
        turn = (meta_ref[1 + z] * capacity).astype(F32)
        slot = jnp.where(hit > 0.5, rank + turn, -1.0)
        slots_ref[:, z * tokens : (z + 1) * tokens] = slot[:groups]

    def one_hot(slots, count, first):
        slot = lax.broadcasted_iota(jnp.int32, (groups, count, slots.shape[1]), 1).astype(F32)
        same = slots[:, None, :] == slot + float(first)
        return jnp.where(same, 1.0, 0.0).reshape(groups * count, slots.shape[1])

    spread = one_hot(slots_ref[...], 2 * cap_half, 0).astype(LOW)
    rows_ref[...] = dot_nn(spread, col_ref[:, :width]).astype(LOW)
    for part, (to_ref, back_ref) in enumerate([(near_ref, near_back_ref), (far_ref, far_back_ref)]):
        pieces = []
        for k in range(n_half):
            start = pl.multiple_of(meta_ref[1 + n + part * n_half + k] * tokens, tokens)
            pieces.append(slots_ref[:, pl.ds(start, tokens)])
        spread = one_hot(jnp.concatenate(pieces, axis=1), cap_half, part * cap_half)
        to_ref[...] = spread.astype(LOW)
        back_ref[...] = jnp.transpose(spread).astype(LOW)


def make_tables(meta, col, width, groups, n_half, capacity, others):
    block = col.shape[0]
    rows = groups * n_half * capacity
    shapes = (
        [jax.ShapeDtypeStruct((2 * rows, width), LOW)]
        + [jax.ShapeDtypeStruct((rows, block // 2), LOW)] * 2
        + [jax.ShapeDtypeStruct((block // 2, rows), LOW)] * 2
    )
    outs = pl.pallas_call(
        functools.partial(table_kernel, capacity, n_half),
        grid_spec=pltpu.PrefetchScalarGridSpec(
            num_scalar_prefetch=1,
            grid=(1,),
            in_specs=[full(col.shape)] + [pl.BlockSpec(memory_space=pl.ANY)] * len(others),
            out_specs=[full(shape.shape) for shape in shapes],
            scratch_shapes=[pltpu.VMEM((groups, block), F32)],
        ),
        out_shape=shapes,
        compiler_params=params(),
        cost_estimate=cost(4 * rows * block * width, 12e6),
    )(meta, col, *others)
    return outs[0], outs[1:3], outs[3:]


def spread_kernel(choices, place_ref, spread_ref, *refs):
    out_ref, rows_ref = refs[-2:]
    for k, by_place in enumerate(choices):
        for which in sorted(set(by_place)):
            hit = functools.reduce(
                jnp.logical_or,
                [place_ref[0] == i for i, other in enumerate(by_place) if other == which],
            )

            @pl.when(hit)
            def _():
                tokens = refs[which].shape[0]
                rows_ref[k * tokens : (k + 1) * tokens] = refs[which][...]

    out_ref[...] = dot_nn(spread_ref[...], rows_ref[...]).astype(LOW)


def spread_rows(place, spread, found, turns, others):
    n = lax.axis_size("expert")
    order = arrival_order(n)
    distances = sorted({order[i][turn] - i for i in range(n) for turn in turns})
    choices = [[distances.index(order[i][turn] - i) for i in range(n)] for turn in turns]
    chunks = [found[distance] for distance in distances]
    tokens, wide = chunks[0].shape
    rows = spread.shape[0]
    return pl.pallas_call(
        functools.partial(spread_kernel, choices),
        grid_spec=pltpu.PrefetchScalarGridSpec(
            num_scalar_prefetch=1,
            grid=(1,),
            in_specs=[full(spread.shape)]
            + [full(chunk.shape) for chunk in chunks]
            + [pl.BlockSpec(memory_space=pl.ANY)] * len(others),
            out_specs=full((rows, wide)),
            scratch_shapes=[pltpu.VMEM((len(turns) * tokens, wide), LOW)],
        ),
        out_shape=jax.ShapeDtypeStruct((rows, wide), LOW),
        compiler_params=params(),
        cost_estimate=cost(2 * rows * len(turns) * tokens * wide, 5e6),
    )(place, spread, *chunks, *others)


def router_back_kernel(experts, *refs):
    sum_ref, g_ref, hidden_ref, gain_ref, router_ref, mask_ref, probs_ref = refs[:7]
    grad_ref, low_ref, dgain_ref, drouter_ref = refs[-4:]
    width = g_ref.shape[1]
    lanes = mask_ref.shape[1]
    total = sum_ref[...].astype(F32)
    table = total[:, width:]
    mask, probs = mask_ref[...], probs_ref[...]
    grad_gates = (table + pltpu.roll(table, lanes - experts, 1)) * mask
    chosen = probs * mask
    chosen_sum = jnp.sum(chosen, axis=1, keepdims=True)
    mean = jnp.sum(grad_gates * (chosen / chosen_sum), axis=1, keepdims=True)
    centred = mask * (grad_gates - mean) / chosen_sum
    grad_logits = probs * (centred - jnp.sum(centred * chosen, axis=1, keepdims=True))
    high, low = split_low(grad_logits)
    router = pad_rows(router_ref[...], lanes)
    grad = total[:, :width] + dot_nn(high, router) + dot_nn(low, router)
    normal, rr = norm_parts(hidden_ref[...])
    mixed = (normal * gain_ref[...]).astype(LOW)
    drouter_ref[...] = dot_tn(high, mixed) + dot_tn(low, mixed)
    dgain_ref[...] = jnp.sum(grad * normal, axis=0, keepdims=True)
    grad_hidden = g_ref[...].astype(F32) + norm_back(grad, normal, rr, gain_ref[...])
    grad_ref[...] = grad_hidden
    low_ref[...] = grad_hidden.astype(LOW)


def route_back(summed, g, hidden, gain, router, mask, probs, experts, others):
    tokens, width = g.shape
    lanes = mask.shape[1]
    operands = [summed, g, hidden, gain[None], router, mask, probs]
    shapes = [
        jax.ShapeDtypeStruct((tokens, width), F32),
        jax.ShapeDtypeStruct((tokens, width), LOW),
        jax.ShapeDtypeStruct((1, width), F32),
        jax.ShapeDtypeStruct((lanes, width), F32),
    ]
    return pl.pallas_call(
        functools.partial(router_back_kernel, experts),
        grid=(1,),
        in_specs=[full(value.shape) for value in operands]
        + [pl.BlockSpec(memory_space=pl.ANY)] * len(others),
        out_specs=[full(shape.shape) for shape in shapes],
        out_shape=shapes,
        compiler_params=params(),
        cost_estimate=cost(8 * tokens * width * lanes, 8e6),
    )(*operands, *others)


def combine_kernel(n_half, meta_ref, near_table_ref, far_table_ref, near_ref, far_ref, *rest):
    del meta_ref
    turn = pl.program_id(0)

    @pl.when(turn < n_half)
    def _():
        rest[-1][...] = dot_nn(near_table_ref[...], near_ref[...]).astype(LOW)

    @pl.when(turn >= n_half)
    def _():
        rest[-1][...] = dot_nn(far_table_ref[...], far_ref[...]).astype(LOW)


def combine_rows(meta, tables, rows, n_half, others):
    tokens = tables[0].shape[0] // n_half
    slots, wide = rows[0].shape
    n = 2 * n_half
    return pl.pallas_call(
        functools.partial(combine_kernel, n_half),
        grid_spec=pltpu.PrefetchScalarGridSpec(
            num_scalar_prefetch=1,
            grid=(n,),
            in_specs=[
                pl.BlockSpec((tokens, slots), lambda i, m: (jnp.minimum(i, n_half - 1), 0)),
                pl.BlockSpec((tokens, slots), lambda i, m: (jnp.maximum(i - n_half, 0), 0)),
            ]
            + [full(value.shape) for value in rows]
            + [pl.BlockSpec(memory_space=pl.ANY)] * len(others),
            out_specs=pl.BlockSpec((tokens, wide), lambda i, m: (m[1 + n + i], 0)),
        ),
        out_shape=jax.ShapeDtypeStruct((n * tokens, wide), LOW),
        compiler_params=params(),
        cost_estimate=cost(2 * slots * n * tokens * wide, 10e6),
    )(meta, *tables, *rows, *others)


def expert_kernel(experts, who_ref, x_ref, gate_ref, up_ref, pull_ref, *rest):
    act_ref, dgate_ref, dup_ref, copy_ref = rest[-4:]
    width = gate_ref.shape[0]
    x = x_ref[:, :width]
    table = x_ref[:, width:].astype(F32)
    lane = lax.broadcasted_iota(jnp.int32, table.shape, 1)
    mine = who_ref[0]
    gate = jnp.sum(
        jnp.where(jnp.logical_or(lane == mine, lane == mine + experts), table, 0.0),
        axis=1,
        keepdims=True,
    )
    pre_gate = dot_nn(x, gate_ref[...])
    pre_up = dot_nn(x, up_ref[...])
    pull = pull_ref[...].reshape(pre_up.shape)
    sig = 1.0 / (1.0 + jnp.exp(-pre_gate))
    silu = pre_gate * sig
    act = silu * pre_up
    act_ref[...] = (act * gate).astype(LOW)
    high, low = split_low(jnp.sum(act * pull, axis=1, keepdims=True))
    pull = pull * gate
    dup = (pull * silu).astype(LOW)
    dgate = (pull * pre_up * (sig * (1.0 + pre_gate * (1.0 - sig)))).astype(LOW)
    dgate_ref[...] = dgate
    dup_ref[...] = dup
    copy_ref[:, :width] = (dot_nt(dgate, gate_ref[...]) + dot_nt(dup, up_ref[...])).astype(LOW)
    back = jnp.where(lane == mine, high.astype(F32), 0.0)
    back = jnp.where(lane == mine + experts, low.astype(F32), back)
    copy_ref[:, width:] = back.astype(LOW)


def run_expert(who, x, w_gate, w_up, pull, part, experts):
    rows, wide = x.shape
    width, hidden = w_gate.shape
    groups, _, slots, _ = pull.shape
    each = groups // 2
    tile = each * slots
    by_rows = lambda columns: pl.BlockSpec((tile, columns), lambda i, p: (i, 0))
    return pl.pallas_call(
        functools.partial(expert_kernel, experts),
        grid_spec=pltpu.PrefetchScalarGridSpec(
            num_scalar_prefetch=1,
            grid=(2,),
            in_specs=[
                by_rows(wide),
                full(w_gate.shape),
                full(w_up.shape),
                pl.BlockSpec((each, 1, slots, hidden), lambda i, p: (i, part, 0, 0)),
            ],
            out_specs=[by_rows(hidden), by_rows(hidden), by_rows(hidden), by_rows(wide)],
        ),
        out_shape=[jax.ShapeDtypeStruct((rows, hidden), LOW)] * 3
        + [jax.ShapeDtypeStruct((rows, wide), LOW)],
        compiler_params=params(),
        cost_estimate=cost(8 * rows * width * hidden, 20e6, rows * hidden),
    )(who, x, w_gate, w_up, pull)


def input_kernel(grad_ref, x_ref, gain_ref, more_ref, out_ref):
    normal, rr = norm_parts(x_ref[...].astype(F32))
    grad = grad_ref[...].astype(F32)
    out_ref[...] = more_ref[...] + norm_back(grad, normal, rr, gain_ref[...])


def input_back(grad, x, gain, more):
    tokens, width = x.shape
    operands = [grad, x, gain[None], more]
    return pl.pallas_call(
        input_kernel,
        grid=(1,),
        in_specs=[full(value.shape) for value in operands],
        out_specs=full(more.shape),
        out_shape=jax.ShapeDtypeStruct((tokens, width), F32),
        compiler_params=params(),
        cost_estimate=cost(20 * tokens * width, 5e6),
    )(*operands)


def kv_back_kernel(factor, n_parts, c_ref, dkv_ref, *refs):
    parts = refs[:n_parts]
    proj_ref, gain_ref, cos_ref, sin_ref = refs[n_parts : n_parts + 4]
    grad_ref, dgain_ref = refs[-2:]
    size = proj_ref.shape[1]
    total = functools.reduce(jnp.add, [part[...].astype(F32) for part in parts], dkv_ref[...])
    grad, dgain = head_backward(
        total[:, :size] * factor, proj_ref[...], gain_ref[...], cos_ref[...], sin_ref[...]
    )
    grad_ref[:, :size] = grad.astype(LOW)
    grad_ref[:, size:] = total[:, size:].astype(LOW)
    dgain_ref[...] = dgain


def kv_back(context, dkv, parts, proj, gain, cos2, sin2, factor, others):
    block, size = proj.shape
    operands = [proj, gain[None], cos2, sin2]
    shapes = [
        jax.ShapeDtypeStruct((block, 2 * size), LOW),
        jax.ShapeDtypeStruct((1, size), F32),
    ]
    return pl.pallas_call(
        functools.partial(kv_back_kernel, factor, len(parts)),
        grid_spec=pltpu.PrefetchScalarGridSpec(
            num_scalar_prefetch=1,
            grid=(1,),
            in_specs=[pl.BlockSpec((block, 2 * size), lambda i, c: (c[0], 0))]
            + [full(part.shape) for part in parts]
            + [full(value.shape) for value in operands]
            + [pl.BlockSpec(memory_space=pl.ANY)] * len(others),
            out_specs=[full(shape.shape) for shape in shapes],
        ),
        out_shape=shapes,
        compiler_params=params(),
        cost_estimate=cost(40 * block * size, 5e6),
    )(context.astype(jnp.int32)[None], dkv, *parts, *operands, *others)


def fold_kernel(n_pairs, s_ref, *refs):
    del s_ref
    send_ref, keep_ref = refs[-2:]
    totals = [
        (refs[2 * k][...].astype(F32) + refs[2 * k + 1][...].astype(F32)).astype(LOW)
        for k in range(n_pairs)
    ]
    for half, out_ref in enumerate((send_ref, keep_ref)):

        @pl.when(pl.program_id(0) == half)
        def _():
            first = 0
            for total in totals:
                last = first + total.shape[1]
                out_ref[:, first:last] = total
                first = last


def fold(pairs, base, bit, others):
    rows = pairs[0][1].shape[0]
    columns = sum(got.shape[1] for _, got in pairs)
    tiles = 2
    tile = rows // (2 * tiles)
    side = lambda h, m: (1 - m[1]) * (1 - h) + m[1] * h
    specs = []
    for _, got in pairs:
        wide = got.shape[1]
        specs.append(
            pl.BlockSpec(
                (tile, wide), lambda h, j, m: (m[0] * 2 * tiles + side(h, m) * tiles + j, 0)
            )
        )
        specs.append(pl.BlockSpec((tile, wide), lambda h, j, m: (side(h, m) * tiles + j, 0)))
    shape = jax.ShapeDtypeStruct((rows // 2, columns), LOW)
    return pl.pallas_call(
        functools.partial(fold_kernel, len(pairs)),
        grid_spec=pltpu.PrefetchScalarGridSpec(
            num_scalar_prefetch=1,
            grid=(2, tiles),
            in_specs=specs + [pl.BlockSpec(memory_space=pl.ANY)] * len(others),
            out_specs=[
                pl.BlockSpec((tile, columns), lambda h, j, m: (j * (1 - h) + (tiles - 1) * h, 0)),
                pl.BlockSpec((tile, columns), lambda h, j, m: (j * h, 0)),
            ],
        ),
        out_shape=[shape, shape],
        compiler_params=params(),
        cost_estimate=cost(rows * columns, 6 * rows * columns),
    )(
        jnp.stack([base, bit]).astype(jnp.int32),
        *[value for pair in pairs for value in pair],
        *others,
    )


def normed_kernel(q_ref, kv_ref, wq_ref, wkv_ref, rows_ref, out_ref, dgain_ref):
    grad = dot_nt(q_ref[...], wq_ref[...]) + dot_nt(kv_ref[...], wkv_ref[...])
    out_ref[...] = grad.astype(LOW)
    dgain_ref[...] = jnp.sum(grad * rows_ref[...].astype(F32), axis=0, keepdims=True)


def normed_back(grad_q, grad_kv, w_q, w_kv, rows):
    block, width = rows.shape
    tile = 512
    column = lambda i: (0, i)
    return pl.pallas_call(
        normed_kernel,
        grid=(width // tile,),
        in_specs=[
            full(grad_q.shape),
            full(grad_kv.shape),
            pl.BlockSpec((tile, w_q.shape[1]), lambda i: (i, 0)),
            pl.BlockSpec((tile, w_kv.shape[1]), lambda i: (i, 0)),
            pl.BlockSpec((block, tile), column),
        ],
        out_specs=[pl.BlockSpec((block, tile), column), pl.BlockSpec((1, tile), column)],
        out_shape=[
            jax.ShapeDtypeStruct((block, width), LOW),
            jax.ShapeDtypeStruct((1, width), F32),
        ],
        compiler_params=params(),
        cost_estimate=cost(2 * block * width * (w_q.shape[1] + w_kv.shape[1]), 12e6),
    )(grad_q, grad_kv, w_q, w_kv, rows)


def pack_kernel(experts, router_ref, attn_ref, mlp_ref, q_ref, k_ref, out_ref, rows_ref):
    size = q_ref.shape[1]
    rows_ref[:experts] = router_ref[:experts]
    rows_ref[experts:] = jnp.zeros_like(rows_ref[experts:])
    rows_ref[experts : experts + 1] = attn_ref[...]
    rows_ref[experts + 1 : experts + 2] = mlp_ref[...]
    rows_ref[experts + 2 : experts + 3, :size] = q_ref[...]
    rows_ref[experts + 2 : experts + 3, size : 2 * size] = k_ref[...]
    out_ref[...] = rows_ref[...].astype(LOW)


def pack_small(experts, router, attn, mlp, q, k):
    width = attn.shape[1]
    shape = (-(-(experts + 3) // 16) * 16, width)
    operands = [router, attn, mlp, q, k]
    return pl.pallas_call(
        functools.partial(pack_kernel, experts),
        grid=(1,),
        in_specs=[full(value.shape) for value in operands],
        out_specs=full(shape),
        out_shape=jax.ShapeDtypeStruct(shape, LOW),
        scratch_shapes=[pltpu.VMEM(shape, F32)],
        compiler_params=params(),
        cost_estimate=cost(shape[0] * width, 6 * shape[0] * width),
    )(*operands)


def part_sum_kernel(parts_ref, out_ref):
    total = parts_ref[0].astype(F32)
    for k in range(1, parts_ref.shape[0]):
        total += parts_ref[k].astype(F32)
    out_ref[...] = total.astype(LOW)


def part_sum(parts):
    count, rows, columns = parts.shape
    tiles = 2
    return pl.pallas_call(
        part_sum_kernel,
        grid=(tiles,),
        in_specs=[pl.BlockSpec((count, rows // tiles, columns), lambda i: (0, i, 0))],
        out_specs=pl.BlockSpec((rows // tiles, columns), lambda i: (i, 0)),
        out_shape=jax.ShapeDtypeStruct((rows, columns), LOW),
        compiler_params=params(),
        cost_estimate=cost(count * rows * columns, 4 * count * rows * columns),
    )(parts)


def widen_kernel(n_chunks, at_ref, *refs):
    del at_ref
    widths = [ref.shape[1] for ref in refs[n_chunks:]]
    for k in range(n_chunks):

        @pl.when(pl.program_id(0) == k)
        def _():
            first = 0
            for wide, out_ref in zip(widths, refs[n_chunks:]):
                out_ref[...] = refs[k][:, first : first + wide].astype(F32)
                first += wide


def widen(places, chunks, widths):
    rows, columns = chunks[0].shape
    count = len(chunks)
    return pl.pallas_call(
        functools.partial(widen_kernel, count),
        grid_spec=pltpu.PrefetchScalarGridSpec(
            num_scalar_prefetch=1,
            grid=(count,),
            in_specs=[full(chunk.shape) for chunk in chunks],
            out_specs=[pl.BlockSpec((rows, wide), lambda i, at: (at[i], 0)) for wide in widths],
        ),
        out_shape=[jax.ShapeDtypeStruct((count * rows, wide), F32) for wide in widths],
        compiler_params=params(),
        cost_estimate=cost(rows * columns, 6 * count * rows * columns),
    )(jnp.stack(places).astype(jnp.int32), *chunks)


def sum_axis(total, axis):
    n = lax.axis_size(axis)
    s = 1
    while s < n:
        got = lax.ppermute(total.astype(LOW), axis, [(i, i ^ s) for i in range(n)])
        total = total.astype(F32) + got.astype(F32)
        s *= 2
    return total


def swap_dp(rows):
    return lax.ppermute(rows, "dp", [(0, 1), (1, 0)])


def swap_context(rows, s):
    n = lax.axis_size("context")
    return lax.ppermute(rows, "context", [(i, i ^ s) for i in range(n)])


def dp_got(grad):
    d = lax.axis_index("dp")
    rows = grad.shape[0] // 2
    return swap_dp(lax.dynamic_slice_in_dim(grad, (1 - d) * rows, rows))


def plane_turns():
    d, c = lax.axis_index("dp"), lax.axis_index("context")
    low, high = lax.rem(c, 2), lax.div(c, 2)

    def swap(first, second):
        perm = [(i, i ^ first) for i in range(4)] + [(4 + i, 4 + (i ^ second)) for i in range(4)]
        return lambda rows: lax.ppermute(rows, GROUP_AXES, perm)

    return [
        (jnp.where(d == 0, low, high), swap(1, 2)),
        (jnp.where(d == 0, high, low), swap(2, 1)),
    ]


def plane_sum(pairs, others):
    (bit_1, swap_1), (bit_2, swap_2) = plane_turns()
    zero = jnp.int32(0)
    send, keep = fold(pairs, lax.axis_index("dp"), bit_1, others)
    send, keep = fold([(keep, swap_1(send))], zero, bit_2, [])
    return (keep.astype(F32) + swap_2(send).astype(F32)).astype(LOW)


def plane_spread(own):
    (_, swap_1), (_, swap_2) = plane_turns()
    second = swap_2(own)
    return [own, second, swap_1(own), swap_1(second)]


def quarter_places(rank):
    d = lax.axis_index("dp")
    c = lax.axis_index("context")
    low, high = lax.rem(c, 2), lax.div(c, 2)
    places = []
    for core in (d, 1 - d):
        bit_1 = jnp.where(core == 0, low, high)
        bit_2 = jnp.where(core == 0, high, low)
        for flip_1, flip_2 in ((0, 0), (0, 1), (1, 0), (1, 1)):
            places.append(4 * core + rank(core, bit_1 ^ flip_1, bit_2 ^ flip_2))
    return places


def widen_all(quarters, rank, widths):
    return widen(quarter_places(rank), quarters + [swap_dp(part) for part in quarters], widths)


def arrival_order(n):
    return [sorted(range(n), key=lambda j: (abs(j - i), j)) for i in range(n)]


def choose(index, options):
    distinct = []
    for option in options:
        if option is not None and not any(option is other for other in distinct):
            distinct.append(option)
    result = distinct[0]
    for option in distinct[1:]:
        mask = functools.reduce(
            jnp.logical_or, [index == i for i, other in enumerate(options) if other is option]
        )
        result = jnp.where(mask, option, result)
    return result


def line_gather(chunk):
    return line_steps({0: chunk}, 1, lax.axis_size("expert"))


def line_steps(found, first, stop):
    n = lax.axis_size("expert")
    found = dict(found)
    for s in range(first, stop):
        found[-s] = lax.ppermute(
            found[1 - s], "expert", [(i, i + 1) for i in range(s - 1, n - 1)]
        )
        found[s] = lax.ppermute(found[s - 1], "expert", [(i + 1, i) for i in range(n - s)])
    return found


def context_gather(rows):
    n = lax.axis_size("context")
    c = lax.axis_index("context")
    found = {0: rows}
    for s in range(1, n):
        found[s] = lax.ppermute(rows, "context", [(i, i ^ s) for i in range(n)])
    return jnp.concatenate([choose(c, [found[i ^ j] for i in range(n)]) for j in range(n)], axis=0)


def context_parts(rows, extra):
    n = lax.axis_size("context")
    c = lax.axis_index("context")
    each = rows.shape[0] // n
    return [
        swap_context((lax.dynamic_slice_in_dim(rows, (c ^ s) * each, each) + extra).astype(LOW), s)
        for s in range(1, n)
    ]


def zero_of(*others):
    return functools.reduce(
        jnp.add,
        [
            lax.slice(other, (0,) * other.ndim, (1,) * other.ndim).reshape(()).astype(F32) * 0.0
            for other in others
        ],
    )


def after(value, *others):
    return (value.astype(F32) + zero_of(*others)).astype(value.dtype)


def on_device(
    layer_input,
    grad_output,
    attn_gain,
    query_weight,
    key_weight,
    value_weight,
    q_gain,
    k_gain,
    output_weight,
    mlp_gain,
    router,
    w_gate,
    w_up,
    w_down,
    routes,
    half_order,
):
    n_context = lax.axis_size("context")
    n_expert = lax.axis_size("expert")
    n_groups = lax.axis_size(GROUP_AXES)
    tok_dev, width = layer_input.shape[1:]
    size = q_gain.shape[0]
    kv_total = key_weight.shape[1] * n_expert
    group_dev = n_expert // (kv_total // size)
    kv_index = lax.axis_index("expert") // group_dev
    block = tok_dev * n_expert
    seq = block * n_context
    half = block // 2
    experts = router.shape[1]
    exp_dev = w_gate.shape[0]
    top = routes.shape[2]
    capacity = max(2, (tok_dev * top * 9 + 8 * experts - 1) // (8 * experts))
    scale = size ** (-0.5)

    seq_rows = jnp.arange(seq, dtype=jnp.int32)
    context = lax.axis_index("context")
    own_halves = lax.dynamic_slice_in_dim(half_order, 2 * context, 2)
    own_pos = (own_halves[:, None] * half + jnp.arange(half, dtype=jnp.int32)[None]).reshape(-1)
    per_half = half // TILE
    tile_pos = (half_order[:, None] * per_half + jnp.arange(per_half, dtype=jnp.int32)).reshape(-1)
    kidx = jnp.sum(
        (tile_pos[None, :] == jnp.arange(seq // TILE, dtype=jnp.int32)[:, None])
        * jnp.arange(seq // TILE, dtype=jnp.int32)[None, :],
        axis=1,
    ).astype(jnp.int32)
    qpos = lax.dynamic_slice_in_dim(tile_pos, context * (block // TILE), block // TILE)
    entry = jnp.arange(size)
    freq = jnp.power(THETA, -(2 * (entry % (size // 2))).astype(F32) / size)
    angles = own_pos.astype(F32)[:, None] * freq[None, :]
    cos2 = jnp.cos(angles)
    sin2 = jnp.sin(angles) * jnp.where(entry < size // 2, -1.0, 1.0)[None, :]

    place = lax.axis_index("expert")
    place_1 = place.astype(jnp.int32)[None]
    lanes = -(-2 * experts // 128) * 128
    mask = jnp.any(
        routes[0][:, :, None] == jnp.arange(lanes, dtype=jnp.int32)[None, None, :], axis=1
    )
    mask_wide = mask.astype(F32)
    router_rows = router.T

    x_low = layer_input[0]
    x_normal, _ = norm_parts(x_low.astype(F32))
    normed_found = line_gather((x_normal * attn_gain).astype(LOW))
    if group_dev == 1:
        kv_weights = jnp.concatenate([key_weight, value_weight], axis=1)
    else:
        key_whole = lax.all_gather(key_weight, "expert", axis=1, tiled=True)
        value_whole = lax.all_gather(value_weight, "expert", axis=1, tiled=True)
        kv_weights = jnp.concatenate(
            [
                lax.dynamic_slice_in_dim(key_whole, kv_index * size, size, 1),
                lax.dynamic_slice_in_dim(value_whole, kv_index * size, size, 1),
            ],
            axis=1,
        )
    grad_low = grad_output[0]
    normed_rows, own_kv, key_proj, grad_wide = project_keys(
        place_1,
        normed_found,
        kv_weights,
        k_gain,
        cos2,
        sin2,
        scale * LOG2E,
        grad_low,
        mask_wide,
    )
    grad_col = lax.all_gather(grad_wide, "expert", axis=0, tiled=True)
    kv_whole = context_gather(own_kv)
    queries, query_proj = project_queries(normed_rows, query_weight, q_gain, cos2, sin2)

    n_half = n_expert // 2
    order_here = jnp.asarray(arrival_order(n_expert), jnp.int32)[place]
    turn_here = jnp.sum(
        (order_here[:, None] == jnp.arange(n_expert, dtype=jnp.int32)[None, :])
        * jnp.arange(n_expert, dtype=jnp.int32)[:, None],
        axis=0,
    ).astype(jnp.int32)
    meta = jnp.concatenate([place_1, turn_here, order_here])
    grad_sent, spreads, back_tables = make_tables(
        meta, grad_col, width, n_groups, n_half, capacity, []
    )

    def swap_plane(rows):
        parts = rows.reshape(n_groups, -1, rows.shape[1])
        parts = lax.all_to_all(parts, GROUP_AXES, split_axis=0, concat_axis=0, tiled=True)
        return parts.reshape(rows.shape)

    attended, inverse = attend(qpos, kidx, queries, kv_whole, [])
    attn_part = (dot_nn(attended, output_weight) + zero_of(grad_sent)).astype(LOW)
    attn_rows = lax.psum_scatter(attn_part, "expert", scatter_dimension=0, tiled=True)

    grad_x = swap_plane(grad_sent)
    act_pull = dot_nt(grad_x, w_down[0]).reshape(n_groups, 2, n_half * capacity, -1)

    hidden, mixed, probs = route_rows(
        x_low, attn_rows, mlp_gain, router_rows, mask_wide, experts, []
    )

    who = (lax.axis_index(ALL_AXES) * exp_dev).astype(jnp.int32)[None]
    mixed_found = line_gather(mixed)
    near = spread_rows(place_1, spreads[0], mixed_found, range(n_half), [grad_x])
    x_near = swap_plane(near)
    worked_near = run_expert(who, x_near, w_gate[0], w_up[0], act_pull, 0, experts)
    far = spread_rows(place_1, spreads[1], mixed_found, range(n_half, n_expert), [x_near])
    x_far = swap_plane(far)
    worked_far = run_expert(who, x_far, w_gate[0], w_up[0], act_pull, 1, experts)
    xs = [x_near, x_far]
    acts, gate_lows, up_lows, copies = (list(pair) for pair in zip(worked_near, worked_far))
    back_far = swap_plane(copies[1])
    back_near = swap_plane(copies[0])
    join = lambda parts: jnp.concatenate(parts, axis=0)
    x_all = join([x[:, :width] for x in xs])
    grad_w_gate = dot_tn(x_all, join(gate_lows))
    grad_w_up = dot_tn(x_all, join(up_lows))
    grad_by_round = jnp.swapaxes(
        grad_x.reshape(n_groups, 2, n_half * capacity, width), 0, 1
    ).reshape(-1, width)
    grad_w_down = dot_tn(join(acts), grad_by_round)
    copies_col = combine_rows(
        meta, back_tables, [back_near, back_far], n_half, [grad_w_gate, grad_w_up]
    )
    copies_sum = lax.psum_scatter(copies_col, "expert", scatter_dimension=0, tiled=True)

    returned = [dot_nn(act, w_down[0]).astype(LOW) for act in acts]
    returned_near = swap_plane(returned[0])

    grad_hidden, grad_hidden_low, grad_mlp_gain, grad_router = route_back(
        copies_sum,
        grad_low,
        hidden,
        mlp_gain,
        router_rows,
        mask_wide,
        probs,
        experts,
        [returned_near, grad_w_down],
    )

    returned_far = swap_plane(returned[1])
    grad_attn = lax.all_gather(grad_hidden_low, "expert", axis=0, tiled=True)
    grad_o, centre = grad_attended(
        grad_attn, output_weight, attended, inverse, [returned_far]
    )
    combined = combine_rows(meta, back_tables, [returned_near, returned_far], n_half, [])
    output_rows = lax.psum_scatter(combined, "expert", scatter_dimension=0, tiled=True)
    w_out = token_dot(attended, grad_attn, [])
    w_out_parts = swap_plane(w_out)
    grad_kv, grad_q, grad_q_gain = attend_back(
        qpos,
        kidx,
        queries,
        grad_o,
        centre,
        kv_whole,
        query_proj,
        q_gain,
        cos2,
        sin2,
        [w_out, combined],
    )
    output_rows = hidden + output_rows.astype(F32) + zero_of(grad_q)
    kv_parts = context_parts(grad_kv, zero_of(w_out_parts))
    w_query = token_dot(normed_rows, grad_q, [])
    w_query_got = dp_got(w_query)

    kv_grads, grad_k_gain = kv_back(
        context, grad_kv, kv_parts, key_proj, k_gain, cos2, sin2, scale, [w_query_got, output_rows]
    )
    grad_normed, gain_rows = normed_back(grad_q, kv_grads, query_weight, kv_weights, normed_rows)
    grad_attn_gain = gain_rows / attn_gain[None]
    grad_normed = lax.psum_scatter(grad_normed, "expert", scatter_dimension=0, tiled=True)
    grad_input = input_back(grad_normed, x_low, attn_gain, grad_hidden)
    small = pack_small(
        experts, grad_router, grad_attn_gain, grad_mlp_gain, grad_q_gain, grad_k_gain
    )
    small_dp = sum_axis(small, "dp")
    small_context = sum_axis(small_dp, "context")
    small_sum = sum_axis(small_context, "expert")

    w_out_quarters = plane_spread(part_sum(w_out_parts.reshape(n_groups, -1, width)))
    (grad_w_out,) = widen_all(
        w_out_quarters,
        lambda core, b1, b2: jnp.where(core == 0, b1 + 2 * b2, 2 * b1 + b2),
        [width],
    )
    w_kv = token_dot(normed_rows, kv_grads, [])
    by_turns = lambda core, b1, b2: 2 * b1 + b2
    if group_dev == 1:
        quarter = plane_sum(
            [(w_query, w_query_got), (w_kv, dp_got(w_kv))], [*kv_parts, *w_out_quarters]
        )
        grad_w_query, grad_w_key, grad_w_value = widen_all(
            plane_spread(quarter),
            by_turns,
            [query_weight.shape[1], key_weight.shape[1], value_weight.shape[1]],
        )
    else:
        quarter = plane_sum([(w_query, w_query_got)], [*kv_parts, *w_out_quarters])
        (grad_w_query,) = widen_all(plane_spread(quarter), by_turns, [query_weight.shape[1]])
        blank = jnp.zeros((width, kv_total), LOW)
        pieces = []
        for part in (w_kv[:, :size], w_kv[:, size:]):
            padded = lax.dynamic_update_slice(blank, part, (0, kv_index * size))
            pieces.append(lax.psum_scatter(padded, "expert", scatter_dimension=1, tiled=True))
        grad_w_key, grad_w_value = (lax.psum(piece, GROUP_AXES).astype(F32) for piece in pieces)
    grad_attn_gain, grad_mlp_gain = small_sum[experts], small_sum[experts + 1]
    grad_q_gain = small_sum[experts + 2, :size]
    grad_k_gain = small_sum[experts + 2, size : 2 * size]
    return (
        output_rows.astype(LOW)[None],
        grad_input[None],
        grad_attn_gain,
        grad_w_query,
        grad_w_key,
        grad_w_value,
        grad_q_gain,
        grad_k_gain,
        grad_w_out,
        grad_mlp_gain,
        small_sum[:experts].T,
        grad_w_gate[None],
        grad_w_up[None],
        grad_w_down[None],
    )


def solution(mesh):
    rows = P("dp", ("context", "expert"), None)
    expert = P(ALL_AXES, None, None)
    columns = P(None, "expert")
    in_specs = (
        rows,
        rows,
        P(),
        columns,
        columns,
        columns,
        P(),
        P(),
        P("expert", None),
        P(),
        P(),
        expert,
        expert,
        expert,
        rows,
        P(),
    )
    out_specs = (
        rows,
        rows,
        P(),
        columns,
        columns,
        columns,
        P(),
        P(),
        P("expert", None),
        P(),
        P(),
        expert,
        expert,
        expert,
    )
    return jax.shard_map(
        on_device, mesh=mesh, in_specs=in_specs, out_specs=out_specs, check_vma=False
    )
```

```python
import functools
import math

import jax
import jax.numpy as jnp
from jax import lax
from jax.experimental import pallas as pl
from jax.experimental.pallas import tpu as pltpu
from jax.sharding import PartitionSpec as P

EPS = 1e-06
THETA = 1000000.0
TILE = 256
PIECE = 128
VMEM_BYTES = 56 * 1024 * 1024
LOG2E = math.log2(math.e)
LOW = jnp.bfloat16
F32 = jnp.float32
ALL_AXES = ("dp", "context", "expert")
GROUP_AXES = ("dp", "context")


def dot_nn(a, b):
    return lax.dot_general(a, b, (((1,), (0,)), ((), ())), preferred_element_type=F32)


def dot_nt(a, b):
    return lax.dot_general(a, b, (((1,), (1,)), ((), ())), preferred_element_type=F32)


def dot_tn(a, b):
    return lax.dot_general(a, b, (((0,), (0,)), ((), ())), preferred_element_type=F32)


def params(**more):
    return pltpu.CompilerParams(vmem_limit_bytes=VMEM_BYTES, **more)


def cost(flops, nbytes, exps=0):
    return pl.CostEstimate(flops=int(flops), bytes_accessed=int(nbytes), transcendentals=int(exps))


def head_forward(u, gain, cos2, sin2):
    rr = lax.rsqrt(jnp.mean(u * u, axis=-1, keepdims=True) + EPS)
    y = u * rr * gain
    return y * cos2 + pltpu.roll(y, 64, 1) * sin2


def head_backward(gy, u, gain, cos2, sin2):
    g = gy * cos2 - pltpu.roll(gy, 64, 1) * sin2
    rr = lax.rsqrt(jnp.mean(u * u, axis=-1, keepdims=True) + EPS)
    n = u * rr
    gn = g * gain
    grad = rr * (gn - n * jnp.mean(gn * n, axis=-1, keepdims=True))
    return grad, jnp.sum(g * n, axis=0, keepdims=True)


def query_kernel(x_ref, w_ref, gain_ref, cos_ref, sin_ref, rot_ref, proj_ref):
    tiles, heads, rows, size = rot_ref.shape
    acc = dot_nn(x_ref[...], w_ref[...])
    for h in range(heads):
        u = acc[:, h * size : (h + 1) * size]
        rot = head_forward(u, gain_ref[...], cos_ref[...], sin_ref[...])
        proj_ref[:, h] = u.reshape(tiles, rows, size)
        rot_ref[:, h] = rot.astype(LOW).reshape(tiles, rows, size)


def project_queries(normed, weight, gain, cos2, sin2):
    block, width = normed.shape
    size = cos2.shape[1]
    heads = weight.shape[1] // size
    tiles = block // TILE
    whole = lambda i: (0, 0)
    per = lambda i: (0, i, 0, 0)
    shape = (tiles, heads, TILE, size)
    return pl.pallas_call(
        query_kernel,
        grid=(heads // 2,),
        in_specs=[
            pl.BlockSpec((block, width), whole),
            pl.BlockSpec((width, 2 * size), lambda i: (0, i)),
            pl.BlockSpec((1, size), whole),
            pl.BlockSpec((block, size), whole),
            pl.BlockSpec((block, size), whole),
        ],
        out_specs=[pl.BlockSpec((tiles, 2, TILE, size), per)] * 2,
        out_shape=[jax.ShapeDtypeStruct(shape, LOW), jax.ShapeDtypeStruct(shape, F32)],
        compiler_params=params(),
        cost_estimate=cost(2 * block * width * heads * size, 12e6),
    )(normed, weight, gain[None], cos2, sin2)


def put_in_order(place, refs, out_ref):
    n = (len(refs) + 1) // 2
    rows = refs[0].shape[0]
    for distance in range(1 - n, n):
        ref = refs[distance + n - 1]
        at = place + distance

        @pl.when(jnp.logical_and(at >= 0, at < n))
        def _():
            out_ref[pl.ds(pl.multiple_of(at * rows, rows), rows), :] = ref[...]


def chunk_list(found):
    n = (len(found) + 1) // 2
    return [found[distance] for distance in range(1 - n, n)]


def key_kernel(factor, n_chunks, place_ref, *refs):
    w_ref, gain_ref, cos_ref, sin_ref, g_ref, mask_ref = refs[n_chunks:-4]
    rows_ref, kv_ref, proj_ref, wide_ref = refs[-4:]
    size = proj_ref.shape[1]
    width = g_ref.shape[1]
    put_in_order(place_ref[0], refs[:n_chunks], rows_ref)
    wide_ref[:, :width] = g_ref[...]
    wide_ref[:, width:] = mask_ref[...].astype(LOW)
    acc = dot_nn(rows_ref[...], w_ref[...])
    u = acc[:, :size]
    rot = head_forward(u, gain_ref[...], cos_ref[...], sin_ref[...])
    proj_ref[...] = u
    kv_ref[:, :size] = (rot * factor).astype(LOW)
    kv_ref[:, size:] = acc[:, size:].astype(LOW)


def full(shape):
    return pl.BlockSpec(shape, lambda *_: (0,) * len(shape))


def project_keys(place, found, weight, gain, cos2, sin2, factor, g, mask):
    chunks = chunk_list(found)
    rows, width = chunks[0].shape
    block, size = cos2.shape
    operands = [*chunks, weight, gain[None], cos2, sin2, g, mask]
    shapes = [
        jax.ShapeDtypeStruct((block, width), LOW),
        jax.ShapeDtypeStruct((block, 2 * size), LOW),
        jax.ShapeDtypeStruct((block, size), F32),
        jax.ShapeDtypeStruct((rows, width + mask.shape[1]), LOW),
    ]
    return pl.pallas_call(
        functools.partial(key_kernel, factor, len(chunks)),
        grid_spec=pltpu.PrefetchScalarGridSpec(
            num_scalar_prefetch=1,
            grid=(1,),
            in_specs=[full(x.shape) for x in operands],
            out_specs=[full(x.shape) for x in shapes],
        ),
        out_shape=shapes,
        compiler_params=params(),
        cost_estimate=cost(4 * block * width * size, 8e6),
    )(place, *operands)


def in_order(last, step):
    lax.fori_loop(0, lax.div(last, 2), lambda p, c: (step([2 * p, 2 * p + 1], False), c)[1], 0)

    @pl.when(lax.rem(last, 2) == 1)
    def _():
        step([last - 1, last], True)

    @pl.when(lax.rem(last, 2) == 0)
    def _():
        step([last], True)


def attend_kernel(qpos_ref, kidx_ref, q_ref, kv_ref, *rest):
    out_ref, inv_ref, acc_ref = rest[-3:]
    heads, rows, size = q_ref.shape[1:]
    acc_ref[...] = jnp.zeros_like(acc_ref)

    def step(places, masked):
        starts = [pl.multiple_of(kidx_ref[place] * rows, rows) for place in places]
        count = len(places) * rows
        keys = jnp.concatenate([kv_ref[pl.ds(start, rows), :size] for start in starts], axis=0)
        values = jnp.concatenate([kv_ref[pl.ds(start, rows), size:] for start in starts], axis=0)
        values = jnp.concatenate([values, jnp.ones((count, size), LOW)], axis=1)
        for h in range(heads):
            for first in range(0, rows, PIECE):
                part = slice(first, first + PIECE)
                e = jnp.exp2(dot_nt(q_ref[0, h, part], keys))
                if masked:
                    qi = lax.broadcasted_iota(jnp.int32, e.shape, 0) + first
                    ki = lax.broadcasted_iota(jnp.int32, e.shape, 1) - (count - rows)
                    e = jnp.where(ki <= qi, e, 0.0)
                acc_ref[h, part] += dot_nn(e.astype(LOW), values)

    in_order(qpos_ref[pl.program_id(0)], step)
    for h in range(heads):
        inv = 1.0 / acc_ref[h, :, size:]
        inv_ref[0, h] = inv
        out_ref[:, h * size : (h + 1) * size] = (acc_ref[h, :, :size] * inv).astype(LOW)


def attend(qpos, kidx, queries, kv, others):
    tiles, heads, rows, size = queries.shape
    seq = kv.shape[0]
    return pl.pallas_call(
        attend_kernel,
        grid_spec=pltpu.PrefetchScalarGridSpec(
            num_scalar_prefetch=2,
            grid=(tiles,),
            in_specs=[
                pl.BlockSpec((1, heads, rows, size), lambda i, a, b: (i, 0, 0, 0)),
                pl.BlockSpec((seq, 2 * size), lambda i, a, b: (0, 0)),
            ]
            + [pl.BlockSpec(memory_space=pl.ANY)] * len(others),
            out_specs=[
                pl.BlockSpec((rows, heads * size), lambda i, a, b: (i, 0)),
                pl.BlockSpec((1, heads, rows, size), lambda i, a, b: (i, 0, 0, 0)),
            ],
            scratch_shapes=[pltpu.VMEM((heads, rows, 2 * size), F32)],
        ),
        out_shape=[
            jax.ShapeDtypeStruct((tiles * rows, heads * size), LOW),
            jax.ShapeDtypeStruct((tiles, heads, rows, size), F32),
        ],
        compiler_params=params(),
        cost_estimate=cost(
            6 * tiles * rows * heads * seq * size, 8e6, tiles * rows * heads * seq
        ),
    )(qpos, kidx, queries, kv, *others)


def grad_out_kernel(rows_ref, w_ref, o_ref, inv_ref, *rest):
    do_ref, centre_ref = rest[-2:]
    tiles, heads, rows, size = do_ref.shape
    acc = dot_nt(rows_ref[...], w_ref[...])
    for t in range(tiles):
        for h in range(heads):
            part = slice(t * rows, (t + 1) * rows), slice(h * size, (h + 1) * size)
            low = (acc[part] * inv_ref[t, h]).astype(LOW)
            do_ref[t, h] = low
            product = low.astype(F32) * o_ref[part].astype(F32)
            centre = jnp.sum(jnp.transpose(product), axis=0, keepdims=True)
            centre_ref[t, h] = jnp.broadcast_to(centre, (8, rows))


def grad_attended(grad_rows, weight, attended, inverse, others):
    tiles, heads, rows, size = inverse.shape
    block, width = grad_rows.shape
    return pl.pallas_call(
        grad_out_kernel,
        grid=(heads // 2,),
        in_specs=[
            pl.BlockSpec((block, width), lambda i: (0, 0)),
            pl.BlockSpec((2 * size, width), lambda i: (i, 0)),
            pl.BlockSpec((block, 2 * size), lambda i: (0, i)),
            pl.BlockSpec((tiles, 2, rows, size), lambda i: (0, i, 0, 0)),
        ]
        + [pl.BlockSpec(memory_space=pl.ANY)] * len(others),
        out_specs=[
            pl.BlockSpec((tiles, 2, rows, size), lambda i: (0, i, 0, 0)),
            pl.BlockSpec((tiles, 2, 8, rows), lambda i: (0, i, 0, 0)),
        ],
        out_shape=[
            jax.ShapeDtypeStruct((tiles, heads, rows, size), LOW),
            jax.ShapeDtypeStruct((tiles, heads, 8, rows), F32),
        ],
        compiler_params=params(),
        cost_estimate=cost(2 * block * width * heads * size, 12e6),
    )(grad_rows, weight, attended, inverse, *others)


def attend_back_kernel(
    qpos_ref,
    kidx_ref,
    q_ref,
    do_ref,
    centre_ref,
    kv_ref,
    proj_ref,
    gain_ref,
    cos_ref,
    sin_ref,
    *rest,
):
    dkv_ref, dq_ref, dgain_ref, acc_ref, e_ref, ds_ref = rest[-6:]
    heads, rows, size = q_ref.shape[1:]

    @pl.when(pl.program_id(0) == 0)
    def _():
        dkv_ref[...] = jnp.zeros_like(dkv_ref)
        dgain_ref[...] = jnp.zeros_like(dgain_ref)

    acc_ref[...] = jnp.zeros_like(acc_ref)

    def step(places, masked):
        starts = [pl.multiple_of(kidx_ref[place] * rows, rows) for place in places]
        count = len(places) * rows
        keys = jnp.concatenate([kv_ref[pl.ds(start, rows), :size] for start in starts], axis=0)
        values = jnp.concatenate([kv_ref[pl.ds(start, rows), size:] for start in starts], axis=0)
        for h in range(heads):
            query, grad = q_ref[0, h], do_ref[0, h]
            centre = centre_ref[0, h, 0:1]
            columns = slice(h * rows, (h + 1) * rows)
            for first in range(0, count, PIECE):
                part = slice(first, first + PIECE)
                e = jnp.exp2(dot_nt(keys[part], query))
                if masked and first >= count - rows:
                    ki = lax.broadcasted_iota(jnp.int32, e.shape, 0) + (first - (count - rows))
                    qi = lax.broadcasted_iota(jnp.int32, e.shape, 1)
                    e = jnp.where(ki <= qi, e, 0.0)
                ds = e * (dot_nt(values[part], grad) - centre)
                e_ref[part, columns] = e.astype(LOW)
                ds_ref[part, columns] = ds.astype(LOW)
            acc_ref[h] += dot_tn(ds_ref[:count, columns], keys)
        dk = dot_nn(ds_ref[:count], q_ref[0].reshape(heads * rows, size))
        dv = dot_nn(e_ref[:count], do_ref[0].reshape(heads * rows, size))
        for k, start in enumerate(starts):
            dkv_ref[pl.ds(start, rows), :size] += dk[k * rows : (k + 1) * rows]
            dkv_ref[pl.ds(start, rows), size:] += dv[k * rows : (k + 1) * rows]

    in_order(qpos_ref[pl.program_id(0)], step)
    total = jnp.zeros((1, size), F32)
    for h in range(heads):
        grad, gain_part = head_backward(
            acc_ref[h] * (1.0 / LOG2E), proj_ref[0, h], gain_ref[...], cos_ref[...], sin_ref[...]
        )
        dq_ref[:, h * size : (h + 1) * size] = grad.astype(LOW)
        total += gain_part
    dgain_ref[...] += total


def attend_back(qpos, kidx, queries, grads, centre, kv, proj, gain, cos2, sin2, others):
    tiles, heads, rows, size = queries.shape
    seq = kv.shape[0]
    per = pl.BlockSpec((1, heads, rows, size), lambda i, a, b: (i, 0, 0, 0))
    flat = lambda i, a, b: (0, 0)
    rowwise = lambda i, a, b: (i, 0)
    return pl.pallas_call(
        attend_back_kernel,
        grid_spec=pltpu.PrefetchScalarGridSpec(
            num_scalar_prefetch=2,
            grid=(tiles,),
            in_specs=[
                per,
                per,
                pl.BlockSpec((1, heads, 8, rows), lambda i, a, b: (i, 0, 0, 0)),
                pl.BlockSpec((seq, 2 * size), flat),
                per,
                pl.BlockSpec((1, size), flat),
                pl.BlockSpec((rows, size), rowwise),
                pl.BlockSpec((rows, size), rowwise),
            ]
            + [pl.BlockSpec(memory_space=pl.ANY)] * len(others),
            out_specs=[
                pl.BlockSpec((seq, 2 * size), flat),
                pl.BlockSpec((rows, heads * size), rowwise),
                pl.BlockSpec((1, size), flat),
            ],
            scratch_shapes=[pltpu.VMEM((heads, rows, size), F32)]
            + [pltpu.VMEM((2 * rows, heads * rows), LOW)] * 2,
        ),
        out_shape=[
            jax.ShapeDtypeStruct((seq, 2 * size), F32),
            jax.ShapeDtypeStruct((tiles * rows, heads * size), LOW),
            jax.ShapeDtypeStruct((1, size), F32),
        ],
        compiler_params=params(),
        cost_estimate=cost(
            15 * tiles * rows * heads * seq * size, 12e6, tiles * rows * heads * seq
        ),
    )(qpos, kidx, queries, grads, centre, kv, proj, gain[None], cos2, sin2, *others)


def token_kernel(a_ref, b_ref, *rest):
    rest[-1][...] = dot_tn(a_ref[...], b_ref[...]).astype(LOW)


def token_dot(a, b, others):
    block, rows = a.shape
    columns = b.shape[1]
    tile = min(rows, 512)
    return pl.pallas_call(
        token_kernel,
        grid=(rows // tile,),
        in_specs=[
            pl.BlockSpec((block, tile), lambda i: (0, i)),
            pl.BlockSpec((block, columns), lambda i: (0, 0)),
        ]
        + [pl.BlockSpec(memory_space=pl.ANY)] * len(others),
        out_specs=pl.BlockSpec((tile, columns), lambda i: (i, 0)),
        out_shape=jax.ShapeDtypeStruct((rows, columns), LOW),
        compiler_params=params(),
        cost_estimate=cost(2 * block * rows * columns, 6e6),
    )(a, b, *others)


def split_low(value):
    high = value.astype(LOW)
    return high, (value - high.astype(F32)).astype(LOW)


def norm_parts(rows):
    rr = lax.rsqrt(jnp.mean(rows * rows, axis=-1, keepdims=True) + EPS)
    return rows * rr, rr


def norm_back(grad, normal, rr, gain):
    weighted = grad * gain
    return rr * (weighted - normal * jnp.mean(weighted * normal, axis=-1, keepdims=True))


def add_all(refs):
    return functools.reduce(jnp.add, [ref[...].astype(F32) for ref in refs])


def pad_rows(rows, count):
    if rows.shape[0] == count:
        return rows
    return jnp.concatenate(
        [rows, jnp.zeros((count - rows.shape[0], rows.shape[1]), rows.dtype)], axis=0
    )


def router_kernel(experts, *refs):
    x_ref, attn_ref, gain_ref, router_ref, mask_ref = refs[:5]
    hidden_ref, mixed_ref, probs_ref = refs[-3:]
    width = x_ref.shape[1]
    lanes = mask_ref.shape[1]
    hidden = add_all([x_ref, attn_ref])
    hidden_ref[...] = hidden
    mixed = (norm_parts(hidden)[0] * gain_ref[...]).astype(LOW)
    mixed_ref[:, :width] = mixed
    logits = dot_nt(mixed, pad_rows(router_ref[...], lanes))
    lane = lax.broadcasted_iota(jnp.int32, logits.shape, 1)
    logits = jnp.where(lane < experts, logits, -1e30)
    weights = jnp.exp(logits - jnp.max(logits, axis=1, keepdims=True))
    probs = weights / jnp.sum(weights, axis=1, keepdims=True)
    probs_ref[...] = probs
    chosen = probs * mask_ref[...]
    high, low = split_low(chosen / jnp.sum(chosen, axis=1, keepdims=True))
    both = high.astype(F32) + pltpu.roll(low.astype(F32), experts, 1)
    mixed_ref[:, width:] = both.astype(LOW)


def route_rows(x, attn, gain, router, mask, experts, others):
    tokens, width = x.shape
    lanes = mask.shape[1]
    operands = [x, attn, gain[None], router, mask]
    shapes = [
        jax.ShapeDtypeStruct((tokens, width), F32),
        jax.ShapeDtypeStruct((tokens, width + lanes), LOW),
        jax.ShapeDtypeStruct((tokens, lanes), F32),
    ]
    return pl.pallas_call(
        functools.partial(router_kernel, experts),
        grid=(1,),
        in_specs=[full(value.shape) for value in operands]
        + [pl.BlockSpec(memory_space=pl.ANY)] * len(others),
        out_specs=[full(shape.shape) for shape in shapes],
        out_shape=shapes,
        compiler_params=params(),
        cost_estimate=cost(2 * tokens * width * lanes, 5e6),
    )(*operands, *others)


def table_kernel(capacity, n_half, meta_ref, col_ref, *rest):
    rows_ref, near_ref, far_ref, near_back_ref, far_back_ref, slots_ref = rest[-6:]
    block = col_ref.shape[0]
    rows, width = rows_ref.shape
    n = 2 * n_half
    tokens = block // n
    cap_half = n_half * capacity
    groups = rows // (2 * cap_half)
    mask = col_ref[:, width:]
    lanes = mask.shape[1]
    padded = -(-groups // 16) * 16
    group = lax.broadcasted_iota(jnp.int32, (padded, lanes), 0)
    lane = lax.broadcasted_iota(jnp.int32, (padded, lanes), 1)
    wanted = jnp.logical_and(lane == group * n + meta_ref[0], group < groups)
    hits = dot_nt(jnp.where(wanted, 1.0, 0.0).astype(LOW), mask)
    before = lax.broadcasted_iota(jnp.int32, (tokens, tokens), 0)
    after_it = lax.broadcasted_iota(jnp.int32, (tokens, tokens), 1)
    earlier = jnp.where(before < after_it, 1.0, 0.0).astype(LOW)
    for z in range(n):
        hit = hits[:, z * tokens : (z + 1) * tokens]
        rank = dot_nn(hit.astype(LOW), earlier)
        turn = (meta_ref[1 + z] * capacity).astype(F32)
        slot = jnp.where(hit > 0.5, rank + turn, -1.0)
        slots_ref[:, z * tokens : (z + 1) * tokens] = slot[:groups]

    def one_hot(slots, count, first):
        slot = lax.broadcasted_iota(jnp.int32, (groups, count, slots.shape[1]), 1).astype(F32)
        same = slots[:, None, :] == slot + float(first)
        return jnp.where(same, 1.0, 0.0).reshape(groups * count, slots.shape[1])

    spread = one_hot(slots_ref[...], 2 * cap_half, 0).astype(LOW)
    rows_ref[...] = dot_nn(spread, col_ref[:, :width]).astype(LOW)
    for part, (to_ref, back_ref) in enumerate([(near_ref, near_back_ref), (far_ref, far_back_ref)]):
        pieces = []
        for k in range(n_half):
            start = pl.multiple_of(meta_ref[1 + n + part * n_half + k] * tokens, tokens)
            pieces.append(slots_ref[:, pl.ds(start, tokens)])
        spread = one_hot(jnp.concatenate(pieces, axis=1), cap_half, part * cap_half)
        to_ref[...] = spread.astype(LOW)
        back_ref[...] = jnp.transpose(spread).astype(LOW)


def make_tables(meta, col, width, groups, n_half, capacity, others):
    block = col.shape[0]
    rows = groups * n_half * capacity
    shapes = (
        [jax.ShapeDtypeStruct((2 * rows, width), LOW)]
        + [jax.ShapeDtypeStruct((rows, block // 2), LOW)] * 2
        + [jax.ShapeDtypeStruct((block // 2, rows), LOW)] * 2
    )
    outs = pl.pallas_call(
        functools.partial(table_kernel, capacity, n_half),
        grid_spec=pltpu.PrefetchScalarGridSpec(
            num_scalar_prefetch=1,
            grid=(1,),
            in_specs=[full(col.shape)] + [pl.BlockSpec(memory_space=pl.ANY)] * len(others),
            out_specs=[full(shape.shape) for shape in shapes],
            scratch_shapes=[pltpu.VMEM((groups, block), F32)],
        ),
        out_shape=shapes,
        compiler_params=params(),
        cost_estimate=cost(4 * rows * block * width, 12e6),
    )(meta, col, *others)
    return outs[0], outs[1:3], outs[3:]


def spread_kernel(choices, place_ref, spread_ref, *refs):
    out_ref, rows_ref = refs[-2:]
    for k, by_place in enumerate(choices):
        for which in sorted(set(by_place)):
            hit = functools.reduce(
                jnp.logical_or,
                [place_ref[0] == i for i, other in enumerate(by_place) if other == which],
            )

            @pl.when(hit)
            def _():
                tokens = refs[which].shape[0]
                rows_ref[k * tokens : (k + 1) * tokens] = refs[which][...]

    out_ref[...] = dot_nn(spread_ref[...], rows_ref[...]).astype(LOW)


def spread_rows(place, spread, found, turns, others):
    n = lax.axis_size("expert")
    order = arrival_order(n)
    distances = sorted({order[i][turn] - i for i in range(n) for turn in turns})
    choices = [[distances.index(order[i][turn] - i) for i in range(n)] for turn in turns]
    chunks = [found[distance] for distance in distances]
    tokens, wide = chunks[0].shape
    rows = spread.shape[0]
    return pl.pallas_call(
        functools.partial(spread_kernel, choices),
        grid_spec=pltpu.PrefetchScalarGridSpec(
            num_scalar_prefetch=1,
            grid=(1,),
            in_specs=[full(spread.shape)]
            + [full(chunk.shape) for chunk in chunks]
            + [pl.BlockSpec(memory_space=pl.ANY)] * len(others),
            out_specs=full((rows, wide)),
            scratch_shapes=[pltpu.VMEM((len(turns) * tokens, wide), LOW)],
        ),
        out_shape=jax.ShapeDtypeStruct((rows, wide), LOW),
        compiler_params=params(),
        cost_estimate=cost(2 * rows * len(turns) * tokens * wide, 5e6),
    )(place, spread, *chunks, *others)


def router_back_kernel(experts, *refs):
    sum_ref, g_ref, hidden_ref, gain_ref, router_ref, mask_ref, probs_ref = refs[:7]
    grad_ref, low_ref, dgain_ref, drouter_ref = refs[-4:]
    width = g_ref.shape[1]
    lanes = mask_ref.shape[1]
    total = sum_ref[...].astype(F32)
    table = total[:, width:]
    mask, probs = mask_ref[...], probs_ref[...]
    grad_gates = (table + pltpu.roll(table, lanes - experts, 1)) * mask
    chosen = probs * mask
    chosen_sum = jnp.sum(chosen, axis=1, keepdims=True)
    mean = jnp.sum(grad_gates * (chosen / chosen_sum), axis=1, keepdims=True)
    centred = mask * (grad_gates - mean) / chosen_sum
    grad_logits = probs * (centred - jnp.sum(centred * chosen, axis=1, keepdims=True))
    high, low = split_low(grad_logits)
    router = pad_rows(router_ref[...], lanes)
    grad = total[:, :width] + dot_nn(high, router) + dot_nn(low, router)
    normal, rr = norm_parts(hidden_ref[...])
    mixed = (normal * gain_ref[...]).astype(LOW)
    drouter_ref[...] = dot_tn(high, mixed) + dot_tn(low, mixed)
    dgain_ref[...] = jnp.sum(grad * normal, axis=0, keepdims=True)
    grad_hidden = g_ref[...].astype(F32) + norm_back(grad, normal, rr, gain_ref[...])
    grad_ref[...] = grad_hidden
    low_ref[...] = grad_hidden.astype(LOW)


def route_back(summed, g, hidden, gain, router, mask, probs, experts, others):
    tokens, width = g.shape
    lanes = mask.shape[1]
    operands = [summed, g, hidden, gain[None], router, mask, probs]
    shapes = [
        jax.ShapeDtypeStruct((tokens, width), F32),
        jax.ShapeDtypeStruct((tokens, width), LOW),
        jax.ShapeDtypeStruct((1, width), F32),
        jax.ShapeDtypeStruct((lanes, width), F32),
    ]
    return pl.pallas_call(
        functools.partial(router_back_kernel, experts),
        grid=(1,),
        in_specs=[full(value.shape) for value in operands]
        + [pl.BlockSpec(memory_space=pl.ANY)] * len(others),
        out_specs=[full(shape.shape) for shape in shapes],
        out_shape=shapes,
        compiler_params=params(),
        cost_estimate=cost(8 * tokens * width * lanes, 8e6),
    )(*operands, *others)


def combine_kernel(n_half, meta_ref, near_table_ref, far_table_ref, near_ref, far_ref, *rest):
    del meta_ref
    turn = pl.program_id(0)

    @pl.when(turn < n_half)
    def _():
        rest[-1][...] = dot_nn(near_table_ref[...], near_ref[...]).astype(LOW)

    @pl.when(turn >= n_half)
    def _():
        rest[-1][...] = dot_nn(far_table_ref[...], far_ref[...]).astype(LOW)


def combine_rows(meta, tables, rows, n_half, others):
    tokens = tables[0].shape[0] // n_half
    slots, wide = rows[0].shape
    n = 2 * n_half
    return pl.pallas_call(
        functools.partial(combine_kernel, n_half),
        grid_spec=pltpu.PrefetchScalarGridSpec(
            num_scalar_prefetch=1,
            grid=(n,),
            in_specs=[
                pl.BlockSpec((tokens, slots), lambda i, m: (jnp.minimum(i, n_half - 1), 0)),
                pl.BlockSpec((tokens, slots), lambda i, m: (jnp.maximum(i - n_half, 0), 0)),
            ]
            + [full(value.shape) for value in rows]
            + [pl.BlockSpec(memory_space=pl.ANY)] * len(others),
            out_specs=pl.BlockSpec((tokens, wide), lambda i, m: (m[1 + n + i], 0)),
        ),
        out_shape=jax.ShapeDtypeStruct((n * tokens, wide), LOW),
        compiler_params=params(),
        cost_estimate=cost(2 * slots * n * tokens * wide, 10e6),
    )(meta, *tables, *rows, *others)


def expert_kernel(experts, who_ref, x_ref, gate_ref, up_ref, pull_ref, *rest):
    act_ref, dgate_ref, dup_ref, copy_ref = rest[-4:]
    width = gate_ref.shape[0]
    x = x_ref[:, :width]
    table = x_ref[:, width:].astype(F32)
    lane = lax.broadcasted_iota(jnp.int32, table.shape, 1)
    mine = who_ref[0]
    gate = jnp.sum(
        jnp.where(jnp.logical_or(lane == mine, lane == mine + experts), table, 0.0),
        axis=1,
        keepdims=True,
    )
    pre_gate = dot_nn(x, gate_ref[...])
    pre_up = dot_nn(x, up_ref[...])
    pull = pull_ref[...].reshape(pre_up.shape)
    sig = 1.0 / (1.0 + jnp.exp(-pre_gate))
    silu = pre_gate * sig
    act = silu * pre_up
    act_ref[...] = (act * gate).astype(LOW)
    high, low = split_low(jnp.sum(act * pull, axis=1, keepdims=True))
    pull = pull * gate
    dup = (pull * silu).astype(LOW)
    dgate = (pull * pre_up * (sig * (1.0 + pre_gate * (1.0 - sig)))).astype(LOW)
    dgate_ref[...] = dgate
    dup_ref[...] = dup
    copy_ref[:, :width] = (dot_nt(dgate, gate_ref[...]) + dot_nt(dup, up_ref[...])).astype(LOW)
    back = jnp.where(lane == mine, high.astype(F32), 0.0)
    back = jnp.where(lane == mine + experts, low.astype(F32), back)
    copy_ref[:, width:] = back.astype(LOW)


def run_expert(who, x, w_gate, w_up, pull, part, experts):
    rows, wide = x.shape
    width, hidden = w_gate.shape
    groups, _, slots, _ = pull.shape
    each = groups // 2
    tile = each * slots
    by_rows = lambda columns: pl.BlockSpec((tile, columns), lambda i, p: (i, 0))
    return pl.pallas_call(
        functools.partial(expert_kernel, experts),
        grid_spec=pltpu.PrefetchScalarGridSpec(
            num_scalar_prefetch=1,
            grid=(2,),
            in_specs=[
                by_rows(wide),
                full(w_gate.shape),
                full(w_up.shape),
                pl.BlockSpec((each, 1, slots, hidden), lambda i, p: (i, part, 0, 0)),
            ],
            out_specs=[by_rows(hidden), by_rows(hidden), by_rows(hidden), by_rows(wide)],
        ),
        out_shape=[jax.ShapeDtypeStruct((rows, hidden), LOW)] * 3
        + [jax.ShapeDtypeStruct((rows, wide), LOW)],
        compiler_params=params(),
        cost_estimate=cost(8 * rows * width * hidden, 20e6, rows * hidden),
    )(who, x, w_gate, w_up, pull)


def input_kernel(grad_ref, x_ref, gain_ref, more_ref, out_ref):
    normal, rr = norm_parts(x_ref[...].astype(F32))
    grad = grad_ref[...].astype(F32)
    out_ref[...] = more_ref[...] + norm_back(grad, normal, rr, gain_ref[...])


def input_back(grad, x, gain, more):
    tokens, width = x.shape
    operands = [grad, x, gain[None], more]
    return pl.pallas_call(
        input_kernel,
        grid=(1,),
        in_specs=[full(value.shape) for value in operands],
        out_specs=full(more.shape),
        out_shape=jax.ShapeDtypeStruct((tokens, width), F32),
        compiler_params=params(),
        cost_estimate=cost(20 * tokens * width, 5e6),
    )(*operands)


def kv_back_kernel(factor, n_parts, c_ref, dkv_ref, *refs):
    parts = refs[:n_parts]
    proj_ref, gain_ref, cos_ref, sin_ref = refs[n_parts : n_parts + 4]
    grad_ref, dgain_ref = refs[-2:]
    size = proj_ref.shape[1]
    total = functools.reduce(jnp.add, [part[...].astype(F32) for part in parts], dkv_ref[...])
    grad, dgain = head_backward(
        total[:, :size] * factor, proj_ref[...], gain_ref[...], cos_ref[...], sin_ref[...]
    )
    grad_ref[:, :size] = grad.astype(LOW)
    grad_ref[:, size:] = total[:, size:].astype(LOW)
    dgain_ref[...] = dgain


def kv_back(context, dkv, parts, proj, gain, cos2, sin2, factor, others):
    block, size = proj.shape
    operands = [proj, gain[None], cos2, sin2]
    shapes = [
        jax.ShapeDtypeStruct((block, 2 * size), LOW),
        jax.ShapeDtypeStruct((1, size), F32),
    ]
    return pl.pallas_call(
        functools.partial(kv_back_kernel, factor, len(parts)),
        grid_spec=pltpu.PrefetchScalarGridSpec(
            num_scalar_prefetch=1,
            grid=(1,),
            in_specs=[pl.BlockSpec((block, 2 * size), lambda i, c: (c[0], 0))]
            + [full(part.shape) for part in parts]
            + [full(value.shape) for value in operands]
            + [pl.BlockSpec(memory_space=pl.ANY)] * len(others),
            out_specs=[full(shape.shape) for shape in shapes],
        ),
        out_shape=shapes,
        compiler_params=params(),
        cost_estimate=cost(40 * block * size, 5e6),
    )(context.astype(jnp.int32)[None], dkv, *parts, *operands, *others)


def fold_kernel(n_pairs, s_ref, *refs):
    del s_ref
    send_ref, keep_ref = refs[-2:]
    totals = [
        (refs[2 * k][...].astype(F32) + refs[2 * k + 1][...].astype(F32)).astype(LOW)
        for k in range(n_pairs)
    ]
    for half, out_ref in enumerate((send_ref, keep_ref)):

        @pl.when(pl.program_id(0) == half)
        def _():
            first = 0
            for total in totals:
                last = first + total.shape[1]
                out_ref[:, first:last] = total
                first = last


def fold(pairs, base, bit, others):
    rows = pairs[0][1].shape[0]
    columns = sum(got.shape[1] for _, got in pairs)
    tiles = 2
    tile = rows // (2 * tiles)
    side = lambda h, m: (1 - m[1]) * (1 - h) + m[1] * h
    specs = []
    for _, got in pairs:
        wide = got.shape[1]
        specs.append(
            pl.BlockSpec(
                (tile, wide), lambda h, j, m: (m[0] * 2 * tiles + side(h, m) * tiles + j, 0)
            )
        )
        specs.append(pl.BlockSpec((tile, wide), lambda h, j, m: (side(h, m) * tiles + j, 0)))
    shape = jax.ShapeDtypeStruct((rows // 2, columns), LOW)
    return pl.pallas_call(
        functools.partial(fold_kernel, len(pairs)),
        grid_spec=pltpu.PrefetchScalarGridSpec(
            num_scalar_prefetch=1,
            grid=(2, tiles),
            in_specs=specs + [pl.BlockSpec(memory_space=pl.ANY)] * len(others),
            out_specs=[
                pl.BlockSpec((tile, columns), lambda h, j, m: (j * (1 - h) + (tiles - 1) * h, 0)),
                pl.BlockSpec((tile, columns), lambda h, j, m: (j * h, 0)),
            ],
        ),
        out_shape=[shape, shape],
        compiler_params=params(),
        cost_estimate=cost(rows * columns, 6 * rows * columns),
    )(
        jnp.stack([base, bit]).astype(jnp.int32),
        *[value for pair in pairs for value in pair],
        *others,
    )


def normed_kernel(q_ref, kv_ref, wq_ref, wkv_ref, rows_ref, *rest):
    out_ref, dgain_ref = rest[-2:]
    grad = dot_nt(q_ref[...], wq_ref[...]) + dot_nt(kv_ref[...], wkv_ref[...])
    out_ref[...] = grad.astype(LOW)
    dgain_ref[...] = jnp.sum(grad * rows_ref[...].astype(F32), axis=0, keepdims=True)


def normed_back(grad_q, grad_kv, w_q, w_kv, rows, others):
    block, width = rows.shape
    tile = 512
    column = lambda i: (0, i)
    return pl.pallas_call(
        normed_kernel,
        grid=(width // tile,),
        in_specs=[
            full(grad_q.shape),
            full(grad_kv.shape),
            pl.BlockSpec((tile, w_q.shape[1]), lambda i: (i, 0)),
            pl.BlockSpec((tile, w_kv.shape[1]), lambda i: (i, 0)),
            pl.BlockSpec((block, tile), column),
        ]
        + [pl.BlockSpec(memory_space=pl.ANY)] * len(others),
        out_specs=[pl.BlockSpec((block, tile), column), pl.BlockSpec((1, tile), column)],
        out_shape=[
            jax.ShapeDtypeStruct((block, width), LOW),
            jax.ShapeDtypeStruct((1, width), F32),
        ],
        compiler_params=params(),
        cost_estimate=cost(2 * block * width * (w_q.shape[1] + w_kv.shape[1]), 12e6),
    )(grad_q, grad_kv, w_q, w_kv, rows, *others)


def pack_kernel(
    experts, router_ref, attn_ref, gain_ref, mlp_ref, q_ref, k_ref, out_ref, rows_ref
):
    size = q_ref.shape[1]
    rows_ref[:experts] = router_ref[:experts]
    rows_ref[experts:] = jnp.zeros_like(rows_ref[experts:])
    rows_ref[experts : experts + 1] = attn_ref[...] / gain_ref[...]
    rows_ref[experts + 1 : experts + 2] = mlp_ref[...]
    rows_ref[experts + 2 : experts + 3, :size] = q_ref[...]
    rows_ref[experts + 2 : experts + 3, size : 2 * size] = k_ref[...]
    out_ref[...] = rows_ref[...].astype(LOW)


def pack_small(experts, router, attn, gain, mlp, q, k):
    width = attn.shape[1]
    shape = (-(-(experts + 3) // 16) * 16, width)
    operands = [router, attn, gain[None], mlp, q, k]
    return pl.pallas_call(
        functools.partial(pack_kernel, experts),
        grid=(1,),
        in_specs=[full(value.shape) for value in operands],
        out_specs=full(shape),
        out_shape=jax.ShapeDtypeStruct(shape, LOW),
        scratch_shapes=[pltpu.VMEM(shape, F32)],
        compiler_params=params(),
        cost_estimate=cost(shape[0] * width, 6 * shape[0] * width),
    )(*operands)


def part_sum_kernel(parts_ref, out_ref):
    total = parts_ref[0].astype(F32)
    for k in range(1, parts_ref.shape[0]):
        total += parts_ref[k].astype(F32)
    out_ref[...] = total.astype(LOW)


def part_sum(parts):
    count, rows, columns = parts.shape
    tiles = 2
    return pl.pallas_call(
        part_sum_kernel,
        grid=(tiles,),
        in_specs=[pl.BlockSpec((count, rows // tiles, columns), lambda i: (0, i, 0))],
        out_specs=pl.BlockSpec((rows // tiles, columns), lambda i: (i, 0)),
        out_shape=jax.ShapeDtypeStruct((rows, columns), LOW),
        compiler_params=params(),
        cost_estimate=cost(count * rows * columns, 4 * count * rows * columns),
    )(parts)


def widen_kernel(n_chunks, n_outs, at_ref, *refs):
    del at_ref
    outs = refs[-n_outs:]
    widths = [ref.shape[1] for ref in outs]
    for k in range(n_chunks):

        @pl.when(pl.program_id(0) == k)
        def _():
            first = 0
            for wide, out_ref in zip(widths, outs):
                out_ref[...] = refs[k][:, first : first + wide].astype(F32)
                first += wide


def widen(places, chunks, widths, others):
    rows, columns = chunks[0].shape
    count = len(chunks)
    return pl.pallas_call(
        functools.partial(widen_kernel, count, len(widths)),
        grid_spec=pltpu.PrefetchScalarGridSpec(
            num_scalar_prefetch=1,
            grid=(count,),
            in_specs=[full(chunk.shape) for chunk in chunks]
            + [pl.BlockSpec(memory_space=pl.ANY)] * len(others),
            out_specs=[pl.BlockSpec((rows, wide), lambda i, at: (at[i], 0)) for wide in widths],
        ),
        out_shape=[jax.ShapeDtypeStruct((count * rows, wide), F32) for wide in widths],
        compiler_params=params(),
        cost_estimate=cost(rows * columns, 6 * count * rows * columns),
    )(jnp.stack(places).astype(jnp.int32), *chunks, *others)


def sum_axis(total, axis):
    n = lax.axis_size(axis)
    s = 1
    while s < n:
        got = lax.ppermute(total.astype(LOW), axis, [(i, i ^ s) for i in range(n)])
        total = total.astype(F32) + got.astype(F32)
        s *= 2
    return total


def swap_dp(rows):
    return lax.ppermute(rows, "dp", [(0, 1), (1, 0)])


def swap_context(rows, s):
    n = lax.axis_size("context")
    return lax.ppermute(rows, "context", [(i, i ^ s) for i in range(n)])


def dp_got(grad):
    d = lax.axis_index("dp")
    rows = grad.shape[0] // 2
    return swap_dp(lax.dynamic_slice_in_dim(grad, (1 - d) * rows, rows))


def plane_turns():
    d, c = lax.axis_index("dp"), lax.axis_index("context")
    low, high = lax.rem(c, 2), lax.div(c, 2)

    def swap(first, second):
        perm = [(i, i ^ first) for i in range(4)] + [(4 + i, 4 + (i ^ second)) for i in range(4)]
        return lambda rows: lax.ppermute(rows, GROUP_AXES, perm)

    return [
        (jnp.where(d == 0, low, high), swap(1, 2)),
        (jnp.where(d == 0, high, low), swap(2, 1)),
    ]


def plane_first(pairs, others):
    (bit_1, _), _ = plane_turns()
    return fold(pairs, lax.axis_index("dp"), bit_1, others)


def plane_rest(send, keep, others):
    (_, swap_1), (bit_2, swap_2) = plane_turns()
    send, keep = fold([(keep, swap_1(send))], jnp.int32(0), bit_2, others)
    return (keep.astype(F32) + swap_2(send).astype(F32)).astype(LOW)


def plane_spread(own):
    (_, swap_1), (_, swap_2) = plane_turns()
    second = swap_2(own)
    return [own, second, swap_1(own), swap_1(second)]


def quarter_places(rank):
    d = lax.axis_index("dp")
    c = lax.axis_index("context")
    low, high = lax.rem(c, 2), lax.div(c, 2)
    places = []
    for core in (d, 1 - d):
        bit_1 = jnp.where(core == 0, low, high)
        bit_2 = jnp.where(core == 0, high, low)
        for flip_1, flip_2 in ((0, 0), (0, 1), (1, 0), (1, 1)):
            places.append(4 * core + rank(core, bit_1 ^ flip_1, bit_2 ^ flip_2))
    return places


def widen_all(quarters, rank, widths, others):
    chunks = quarters + [swap_dp(part) for part in quarters]
    return widen(quarter_places(rank), chunks, widths, others)


def arrival_order(n):
    return [sorted(range(n), key=lambda j: (abs(j - i), j)) for i in range(n)]


def choose(index, options):
    distinct = []
    for option in options:
        if option is not None and not any(option is other for other in distinct):
            distinct.append(option)
    result = distinct[0]
    for option in distinct[1:]:
        mask = functools.reduce(
            jnp.logical_or, [index == i for i, other in enumerate(options) if other is option]
        )
        result = jnp.where(mask, option, result)
    return result


def line_gather(chunk):
    return line_steps({0: chunk}, 1, lax.axis_size("expert"))


def line_steps(found, first, stop):
    n = lax.axis_size("expert")
    found = dict(found)
    for s in range(first, stop):
        found[-s] = lax.ppermute(
            found[1 - s], "expert", [(i, i + 1) for i in range(s - 1, n - 1)]
        )
        found[s] = lax.ppermute(found[s - 1], "expert", [(i + 1, i) for i in range(n - s)])
    return found


def context_gather(rows):
    n = lax.axis_size("context")
    c = lax.axis_index("context")
    found = {0: rows}
    for s in range(1, n):
        found[s] = lax.ppermute(rows, "context", [(i, i ^ s) for i in range(n)])
    return jnp.concatenate([choose(c, [found[i ^ j] for i in range(n)]) for j in range(n)], axis=0)


def context_parts(rows, extra):
    n = lax.axis_size("context")
    c = lax.axis_index("context")
    each = rows.shape[0] // n
    return [
        swap_context((lax.dynamic_slice_in_dim(rows, (c ^ s) * each, each) + extra).astype(LOW), s)
        for s in range(1, n)
    ]


def zero_of(*others):
    return functools.reduce(
        jnp.add,
        [
            lax.slice(other, (0,) * other.ndim, (1,) * other.ndim).reshape(()).astype(F32) * 0.0
            for other in others
        ],
    )


def after(value, *others):
    return (value.astype(F32) + zero_of(*others)).astype(value.dtype)


def on_device(
    layer_input,
    grad_output,
    attn_gain,
    query_weight,
    key_weight,
    value_weight,
    q_gain,
    k_gain,
    output_weight,
    mlp_gain,
    router,
    w_gate,
    w_up,
    w_down,
    routes,
    half_order,
):
    n_context = lax.axis_size("context")
    n_expert = lax.axis_size("expert")
    n_groups = lax.axis_size(GROUP_AXES)
    tok_dev, width = layer_input.shape[1:]
    size = q_gain.shape[0]
    kv_total = key_weight.shape[1] * n_expert
    group_dev = n_expert // (kv_total // size)
    kv_index = lax.axis_index("expert") // group_dev
    block = tok_dev * n_expert
    seq = block * n_context
    half = block // 2
    experts = router.shape[1]
    exp_dev = w_gate.shape[0]
    top = routes.shape[2]
    capacity = max(2, (tok_dev * top * 9 + 8 * experts - 1) // (8 * experts))
    scale = size ** (-0.5)

    seq_rows = jnp.arange(seq, dtype=jnp.int32)
    context = lax.axis_index("context")
    own_halves = lax.dynamic_slice_in_dim(half_order, 2 * context, 2)
    own_pos = (own_halves[:, None] * half + jnp.arange(half, dtype=jnp.int32)[None]).reshape(-1)
    per_half = half // TILE
    tile_pos = (half_order[:, None] * per_half + jnp.arange(per_half, dtype=jnp.int32)).reshape(-1)
    kidx = jnp.sum(
        (tile_pos[None, :] == jnp.arange(seq // TILE, dtype=jnp.int32)[:, None])
        * jnp.arange(seq // TILE, dtype=jnp.int32)[None, :],
        axis=1,
    ).astype(jnp.int32)
    qpos = lax.dynamic_slice_in_dim(tile_pos, context * (block // TILE), block // TILE)
    entry = jnp.arange(size)
    freq = jnp.power(THETA, -(2 * (entry % (size // 2))).astype(F32) / size)
    angles = own_pos.astype(F32)[:, None] * freq[None, :]
    cos2 = jnp.cos(angles)
    sin2 = jnp.sin(angles) * jnp.where(entry < size // 2, -1.0, 1.0)[None, :]

    place = lax.axis_index("expert")
    place_1 = place.astype(jnp.int32)[None]
    lanes = -(-2 * experts // 128) * 128
    mask = jnp.any(
        routes[0][:, :, None] == jnp.arange(lanes, dtype=jnp.int32)[None, None, :], axis=1
    )
    mask_wide = mask.astype(F32)
    router_rows = router.T

    x_low = layer_input[0]
    x_normal, _ = norm_parts(x_low.astype(F32))
    normed_found = line_gather((x_normal * attn_gain).astype(LOW))
    if group_dev == 1:
        kv_weights = jnp.concatenate([key_weight, value_weight], axis=1)
    else:
        key_whole = lax.all_gather(key_weight, "expert", axis=1, tiled=True)
        value_whole = lax.all_gather(value_weight, "expert", axis=1, tiled=True)
        kv_weights = jnp.concatenate(
            [
                lax.dynamic_slice_in_dim(key_whole, kv_index * size, size, 1),
                lax.dynamic_slice_in_dim(value_whole, kv_index * size, size, 1),
            ],
            axis=1,
        )
    grad_low = grad_output[0]
    normed_rows, own_kv, key_proj, grad_wide = project_keys(
        place_1,
        normed_found,
        kv_weights,
        k_gain,
        cos2,
        sin2,
        scale * LOG2E,
        grad_low,
        mask_wide,
    )
    grad_col = lax.all_gather(grad_wide, "expert", axis=0, tiled=True)
    kv_whole = context_gather(own_kv)
    queries, query_proj = project_queries(normed_rows, query_weight, q_gain, cos2, sin2)

    n_half = n_expert // 2
    order_here = jnp.asarray(arrival_order(n_expert), jnp.int32)[place]
    turn_here = jnp.sum(
        (order_here[:, None] == jnp.arange(n_expert, dtype=jnp.int32)[None, :])
        * jnp.arange(n_expert, dtype=jnp.int32)[:, None],
        axis=0,
    ).astype(jnp.int32)
    meta = jnp.concatenate([place_1, turn_here, order_here])
    grad_sent, spreads, back_tables = make_tables(
        meta, grad_col, width, n_groups, n_half, capacity, []
    )

    def swap_plane(rows):
        parts = rows.reshape(n_groups, -1, rows.shape[1])
        parts = lax.all_to_all(parts, GROUP_AXES, split_axis=0, concat_axis=0, tiled=True)
        return parts.reshape(rows.shape)

    attended, inverse = attend(qpos, kidx, queries, kv_whole, [])
    attn_part = (dot_nn(attended, output_weight) + zero_of(grad_col)).astype(LOW)
    attn_rows = lax.psum_scatter(attn_part, "expert", scatter_dimension=0, tiled=True)

    grad_x = swap_plane(grad_sent)
    act_pull = dot_nt(grad_x, w_down[0]).reshape(n_groups, 2, n_half * capacity, -1)

    hidden, mixed, probs = route_rows(
        x_low, attn_rows, mlp_gain, router_rows, mask_wide, experts, []
    )

    who = (lax.axis_index(ALL_AXES) * exp_dev).astype(jnp.int32)[None]
    mixed_found = line_gather(mixed)
    near = spread_rows(place_1, spreads[0], mixed_found, range(n_half), [grad_x])
    x_near = swap_plane(near)
    worked_near = run_expert(who, x_near, w_gate[0], w_up[0], act_pull, 0, experts)
    far = spread_rows(place_1, spreads[1], mixed_found, range(n_half, n_expert), [x_near])
    x_far = swap_plane(far)
    worked_far = run_expert(who, x_far, w_gate[0], w_up[0], act_pull, 1, experts)
    xs = [x_near, x_far]
    acts, gate_lows, up_lows, copies = (list(pair) for pair in zip(worked_near, worked_far))
    back_far = swap_plane(copies[1])
    back_near = swap_plane(copies[0])
    join = lambda parts: jnp.concatenate(parts, axis=0)
    x_all = join([x[:, :width] for x in xs])
    grad_w_gate = dot_tn(x_all, join(gate_lows))
    grad_w_up = dot_tn(x_all, join(up_lows))
    grad_by_round = jnp.swapaxes(
        grad_x.reshape(n_groups, 2, n_half * capacity, width), 0, 1
    ).reshape(-1, width)
    grad_w_down = dot_tn(join(acts), grad_by_round)
    copies_col = combine_rows(
        meta, back_tables, [back_near, back_far], n_half, [grad_w_gate, grad_w_up]
    )
    copies_sum = lax.psum_scatter(copies_col, "expert", scatter_dimension=0, tiled=True)

    returned = [dot_nn(act, w_down[0]).astype(LOW) for act in acts]
    returned_near = swap_plane(returned[0])

    grad_hidden, grad_hidden_low, grad_mlp_gain, grad_router = route_back(
        copies_sum,
        grad_low,
        hidden,
        mlp_gain,
        router_rows,
        mask_wide,
        probs,
        experts,
        [returned_near, grad_w_down],
    )

    returned_far = swap_plane(returned[1])
    grad_attn = lax.all_gather(grad_hidden_low, "expert", axis=0, tiled=True)
    grad_o, centre = grad_attended(
        grad_attn, output_weight, attended, inverse, [returned_far]
    )
    combined = combine_rows(meta, back_tables, [returned_near, returned_far], n_half, [])
    output_rows = lax.psum_scatter(combined, "expert", scatter_dimension=0, tiled=True)
    w_out = token_dot(attended, grad_attn, [])
    w_out_parts = swap_plane(w_out)
    grad_kv, grad_q, grad_q_gain = attend_back(
        qpos,
        kidx,
        queries,
        grad_o,
        centre,
        kv_whole,
        query_proj,
        q_gain,
        cos2,
        sin2,
        [w_out, combined],
    )
    kv_parts = context_parts(grad_kv, zero_of(w_out_parts))
    w_query = token_dot(normed_rows, grad_q, [])
    w_query_got = dp_got(w_query)
    output_rows = hidden + output_rows.astype(F32) + zero_of(w_query)

    kv_grads, grad_k_gain = kv_back(
        context, grad_kv, kv_parts, key_proj, k_gain, cos2, sin2, scale, [w_query_got]
    )
    w_out_quarters = plane_spread(part_sum(w_out_parts.reshape(n_groups, -1, width)))
    w_kv = token_dot(normed_rows, kv_grads, [])
    pairs = [(w_query, w_query_got)]
    widths = [query_weight.shape[1]]
    if group_dev == 1:
        pairs.append((w_kv, dp_got(w_kv)))
        widths += [key_weight.shape[1], value_weight.shape[1]]
    send, keep = plane_first(pairs, [*kv_parts, *w_out_quarters])

    grad_normed, gain_rows = normed_back(
        grad_q, kv_grads, query_weight, kv_weights, normed_rows, [keep]
    )
    grad_normed = lax.psum_scatter(grad_normed, "expert", scatter_dimension=0, tiled=True)
    grad_input = input_back(grad_normed, x_low, attn_gain, grad_hidden)
    small = pack_small(
        experts, grad_router, gain_rows, attn_gain, grad_mlp_gain, grad_q_gain, grad_k_gain
    )
    small_dp = sum_axis(small, "dp")
    small_context = sum_axis(small_dp, "context")
    small_sum = sum_axis(small_context, "expert")

    (grad_w_out,) = widen_all(
        w_out_quarters,
        lambda core, b1, b2: jnp.where(core == 0, b1 + 2 * b2, 2 * b1 + b2),
        [width],
        [],
    )
    quarter = plane_rest(send, keep, [grad_w_out, output_rows])
    grad_w_query, *more = widen_all(
        plane_spread(quarter), lambda core, b1, b2: 2 * b1 + b2, widths, [grad_input]
    )
    if group_dev == 1:
        grad_w_key, grad_w_value = more
    else:
        blank = jnp.zeros((width, kv_total), LOW)
        pieces = []
        for part in (w_kv[:, :size], w_kv[:, size:]):
            padded = lax.dynamic_update_slice(blank, part, (0, kv_index * size))
            pieces.append(lax.psum_scatter(padded, "expert", scatter_dimension=1, tiled=True))
        grad_w_key, grad_w_value = (lax.psum(piece, GROUP_AXES).astype(F32) for piece in pieces)
    grad_attn_gain, grad_mlp_gain = small_sum[experts], small_sum[experts + 1]
    grad_q_gain = small_sum[experts + 2, :size]
    grad_k_gain = small_sum[experts + 2, size : 2 * size]
    return (
        output_rows.astype(LOW)[None],
        grad_input[None],
        grad_attn_gain,
        grad_w_query,
        grad_w_key,
        grad_w_value,
        grad_q_gain,
        grad_k_gain,
        grad_w_out,
        grad_mlp_gain,
        small_sum[:experts].T,
        grad_w_gate[None],
        grad_w_up[None],
        grad_w_down[None],
    )


def solution(mesh):
    rows = P("dp", ("context", "expert"), None)
    expert = P(ALL_AXES, None, None)
    columns = P(None, "expert")
    in_specs = (
        rows,
        rows,
        P(),
        columns,
        columns,
        columns,
        P(),
        P(),
        P("expert", None),
        P(),
        P(),
        expert,
        expert,
        expert,
        rows,
        P(),
    )
    out_specs = (
        rows,
        rows,
        P(),
        columns,
        columns,
        columns,
        P(),
        P(),
        P("expert", None),
        P(),
        P(),
        expert,
        expert,
        expert,
    )
    return jax.shard_map(
        on_device, mesh=mesh, in_specs=in_specs, out_specs=out_specs, check_vma=False
    )
```

```python
import functools
import math

import jax
import jax.numpy as jnp
from jax import lax
from jax.experimental import pallas as pl
from jax.experimental.pallas import tpu as pltpu
from jax.sharding import PartitionSpec as P

EPS = 1e-06
THETA = 1000000.0
TILE = 256
PIECE = 128
VMEM_BYTES = 56 * 1024 * 1024
LOG2E = math.log2(math.e)
LOW = jnp.bfloat16
F32 = jnp.float32
ALL_AXES = ("dp", "context", "expert")
GROUP_AXES = ("dp", "context")


def dot_nn(a, b):
    return lax.dot_general(a, b, (((1,), (0,)), ((), ())), preferred_element_type=F32)


def dot_nt(a, b):
    return lax.dot_general(a, b, (((1,), (1,)), ((), ())), preferred_element_type=F32)


def dot_tn(a, b):
    return lax.dot_general(a, b, (((0,), (0,)), ((), ())), preferred_element_type=F32)


def params(**more):
    return pltpu.CompilerParams(vmem_limit_bytes=VMEM_BYTES, **more)


def cost(flops, nbytes, exps=0):
    return pl.CostEstimate(flops=int(flops), bytes_accessed=int(nbytes), transcendentals=int(exps))


def head_forward(u, gain, cos2, sin2):
    rr = lax.rsqrt(jnp.mean(u * u, axis=-1, keepdims=True) + EPS)
    y = u * rr * gain
    return y * cos2 + pltpu.roll(y, 64, 1) * sin2


def head_backward(gy, u, gain, cos2, sin2):
    g = gy * cos2 - pltpu.roll(gy, 64, 1) * sin2
    rr = lax.rsqrt(jnp.mean(u * u, axis=-1, keepdims=True) + EPS)
    n = u * rr
    gn = g * gain
    grad = rr * (gn - n * jnp.mean(gn * n, axis=-1, keepdims=True))
    return grad, jnp.sum(g * n, axis=0, keepdims=True)


def query_kernel(x_ref, w_ref, gain_ref, cos_ref, sin_ref, rot_ref, proj_ref):
    tiles, heads, rows, size = rot_ref.shape
    acc = dot_nn(x_ref[...], w_ref[...])
    for h in range(heads):
        u = acc[:, h * size : (h + 1) * size]
        rot = head_forward(u, gain_ref[...], cos_ref[...], sin_ref[...])
        proj_ref[:, h] = u.reshape(tiles, rows, size)
        rot_ref[:, h] = rot.astype(LOW).reshape(tiles, rows, size)


def project_queries(normed, weight, gain, cos2, sin2):
    block, width = normed.shape
    size = cos2.shape[1]
    heads = weight.shape[1] // size
    tiles = block // TILE
    whole = lambda i: (0, 0)
    per = lambda i: (0, i, 0, 0)
    shape = (tiles, heads, TILE, size)
    return pl.pallas_call(
        query_kernel,
        grid=(heads // 2,),
        in_specs=[
            pl.BlockSpec((block, width), whole),
            pl.BlockSpec((width, 2 * size), lambda i: (0, i)),
            pl.BlockSpec((1, size), whole),
            pl.BlockSpec((block, size), whole),
            pl.BlockSpec((block, size), whole),
        ],
        out_specs=[pl.BlockSpec((tiles, 2, TILE, size), per)] * 2,
        out_shape=[jax.ShapeDtypeStruct(shape, LOW), jax.ShapeDtypeStruct(shape, F32)],
        compiler_params=params(),
        cost_estimate=cost(2 * block * width * heads * size, 12e6),
    )(normed, weight, gain[None], cos2, sin2)


def put_in_order(place, refs, out_ref):
    n = (len(refs) + 1) // 2
    rows = refs[0].shape[0]
    for distance in range(1 - n, n):
        ref = refs[distance + n - 1]
        at = place + distance

        @pl.when(jnp.logical_and(at >= 0, at < n))
        def _():
            out_ref[pl.ds(pl.multiple_of(at * rows, rows), rows), :] = ref[...]


def chunk_list(found):
    n = (len(found) + 1) // 2
    return [found[distance] for distance in range(1 - n, n)]


def key_kernel(factor, n_chunks, place_ref, *refs):
    w_ref, gain_ref, cos_ref, sin_ref, g_ref, mask_ref = refs[n_chunks:-4]
    rows_ref, kv_ref, proj_ref, wide_ref = refs[-4:]
    size = proj_ref.shape[1]
    width = g_ref.shape[1]
    put_in_order(place_ref[0], refs[:n_chunks], rows_ref)
    wide_ref[:, :width] = g_ref[...]
    wide_ref[:, width:] = mask_ref[...].astype(LOW)
    acc = dot_nn(rows_ref[...], w_ref[...])
    u = acc[:, :size]
    rot = head_forward(u, gain_ref[...], cos_ref[...], sin_ref[...])
    proj_ref[...] = u
    kv_ref[:, :size] = (rot * factor).astype(LOW)
    kv_ref[:, size:] = acc[:, size:].astype(LOW)


def full(shape):
    return pl.BlockSpec(shape, lambda *_: (0,) * len(shape))


def project_keys(place, found, weight, gain, cos2, sin2, factor, g, mask):
    chunks = chunk_list(found)
    rows, width = chunks[0].shape
    block, size = cos2.shape
    operands = [*chunks, weight, gain[None], cos2, sin2, g, mask]
    shapes = [
        jax.ShapeDtypeStruct((block, width), LOW),
        jax.ShapeDtypeStruct((block, 2 * size), LOW),
        jax.ShapeDtypeStruct((block, size), F32),
        jax.ShapeDtypeStruct((rows, width + mask.shape[1]), LOW),
    ]
    return pl.pallas_call(
        functools.partial(key_kernel, factor, len(chunks)),
        grid_spec=pltpu.PrefetchScalarGridSpec(
            num_scalar_prefetch=1,
            grid=(1,),
            in_specs=[full(x.shape) for x in operands],
            out_specs=[full(x.shape) for x in shapes],
        ),
        out_shape=shapes,
        compiler_params=params(),
        cost_estimate=cost(4 * block * width * size, 8e6),
    )(place, *operands)


def in_order(last, step):
    lax.fori_loop(0, lax.div(last, 2), lambda p, c: (step([2 * p, 2 * p + 1], False), c)[1], 0)

    @pl.when(lax.rem(last, 2) == 1)
    def _():
        step([last - 1, last], True)

    @pl.when(lax.rem(last, 2) == 0)
    def _():
        step([last], True)


def attend_kernel(qpos_ref, kidx_ref, q_ref, kv_ref, *rest):
    out_ref, inv_ref, acc_ref = rest[-3:]
    heads, rows, size = q_ref.shape[1:]
    acc_ref[...] = jnp.zeros_like(acc_ref)

    def step(places, masked):
        starts = [pl.multiple_of(kidx_ref[place] * rows, rows) for place in places]
        count = len(places) * rows
        keys = jnp.concatenate([kv_ref[pl.ds(start, rows), :size] for start in starts], axis=0)
        values = jnp.concatenate([kv_ref[pl.ds(start, rows), size:] for start in starts], axis=0)
        values = jnp.concatenate([values, jnp.ones((count, size), LOW)], axis=1)
        for h in range(heads):
            for first in range(0, rows, PIECE):
                part = slice(first, first + PIECE)
                e = jnp.exp2(dot_nt(q_ref[0, h, part], keys))
                if masked:
                    qi = lax.broadcasted_iota(jnp.int32, e.shape, 0) + first
                    ki = lax.broadcasted_iota(jnp.int32, e.shape, 1) - (count - rows)
                    e = jnp.where(ki <= qi, e, 0.0)
                acc_ref[h, part] += dot_nn(e.astype(LOW), values)

    in_order(qpos_ref[pl.program_id(0)], step)
    for h in range(heads):
        inv = 1.0 / acc_ref[h, :, size:]
        inv_ref[0, h] = inv
        out_ref[:, h * size : (h + 1) * size] = (acc_ref[h, :, :size] * inv).astype(LOW)


def attend(qpos, kidx, queries, kv, others):
    tiles, heads, rows, size = queries.shape
    seq = kv.shape[0]
    return pl.pallas_call(
        attend_kernel,
        grid_spec=pltpu.PrefetchScalarGridSpec(
            num_scalar_prefetch=2,
            grid=(tiles,),
            in_specs=[
                pl.BlockSpec((1, heads, rows, size), lambda i, a, b: (i, 0, 0, 0)),
                pl.BlockSpec((seq, 2 * size), lambda i, a, b: (0, 0)),
            ]
            + [pl.BlockSpec(memory_space=pl.ANY)] * len(others),
            out_specs=[
                pl.BlockSpec((rows, heads * size), lambda i, a, b: (i, 0)),
                pl.BlockSpec((1, heads, rows, size), lambda i, a, b: (i, 0, 0, 0)),
            ],
            scratch_shapes=[pltpu.VMEM((heads, rows, 2 * size), F32)],
        ),
        out_shape=[
            jax.ShapeDtypeStruct((tiles * rows, heads * size), LOW),
            jax.ShapeDtypeStruct((tiles, heads, rows, size), F32),
        ],
        compiler_params=params(),
        cost_estimate=cost(
            6 * tiles * rows * heads * seq * size, 8e6, tiles * rows * heads * seq
        ),
    )(qpos, kidx, queries, kv, *others)


def grad_out_kernel(rows_ref, w_ref, o_ref, inv_ref, *rest):
    do_ref, centre_ref = rest[-2:]
    tiles, heads, rows, size = do_ref.shape
    acc = dot_nt(rows_ref[...], w_ref[...])
    for t in range(tiles):
        for h in range(heads):
            part = slice(t * rows, (t + 1) * rows), slice(h * size, (h + 1) * size)
            low = (acc[part] * inv_ref[t, h]).astype(LOW)
            do_ref[t, h] = low
            product = low.astype(F32) * o_ref[part].astype(F32)
            centre = jnp.sum(jnp.transpose(product), axis=0, keepdims=True)
            centre_ref[t, h] = jnp.broadcast_to(centre, (8, rows))


def grad_attended(grad_rows, weight, attended, inverse, others):
    tiles, heads, rows, size = inverse.shape
    block, width = grad_rows.shape
    return pl.pallas_call(
        grad_out_kernel,
        grid=(heads // 2,),
        in_specs=[
            pl.BlockSpec((block, width), lambda i: (0, 0)),
            pl.BlockSpec((2 * size, width), lambda i: (i, 0)),
            pl.BlockSpec((block, 2 * size), lambda i: (0, i)),
            pl.BlockSpec((tiles, 2, rows, size), lambda i: (0, i, 0, 0)),
        ]
        + [pl.BlockSpec(memory_space=pl.ANY)] * len(others),
        out_specs=[
            pl.BlockSpec((tiles, 2, rows, size), lambda i: (0, i, 0, 0)),
            pl.BlockSpec((tiles, 2, 8, rows), lambda i: (0, i, 0, 0)),
        ],
        out_shape=[
            jax.ShapeDtypeStruct((tiles, heads, rows, size), LOW),
            jax.ShapeDtypeStruct((tiles, heads, 8, rows), F32),
        ],
        compiler_params=params(),
        cost_estimate=cost(2 * block * width * heads * size, 12e6),
    )(grad_rows, weight, attended, inverse, *others)


def attend_back_kernel(
    qpos_ref,
    kidx_ref,
    q_ref,
    do_ref,
    centre_ref,
    kv_ref,
    proj_ref,
    gain_ref,
    cos_ref,
    sin_ref,
    *rest,
):
    dkv_ref, dq_ref, dgain_ref, acc_ref, e_ref, ds_ref = rest[-6:]
    heads, rows, size = q_ref.shape[1:]

    @pl.when(pl.program_id(0) == 0)
    def _():
        dkv_ref[...] = jnp.zeros_like(dkv_ref)
        dgain_ref[...] = jnp.zeros_like(dgain_ref)

    acc_ref[...] = jnp.zeros_like(acc_ref)

    def step(places, masked):
        starts = [pl.multiple_of(kidx_ref[place] * rows, rows) for place in places]
        count = len(places) * rows
        keys = jnp.concatenate([kv_ref[pl.ds(start, rows), :size] for start in starts], axis=0)
        values = jnp.concatenate([kv_ref[pl.ds(start, rows), size:] for start in starts], axis=0)
        for h in range(heads):
            query, grad = q_ref[0, h], do_ref[0, h]
            centre = centre_ref[0, h, 0:1]
            columns = slice(h * rows, (h + 1) * rows)
            for first in range(0, count, PIECE):
                part = slice(first, first + PIECE)
                e = jnp.exp2(dot_nt(keys[part], query))
                if masked and first >= count - rows:
                    ki = lax.broadcasted_iota(jnp.int32, e.shape, 0) + (first - (count - rows))
                    qi = lax.broadcasted_iota(jnp.int32, e.shape, 1)
                    e = jnp.where(ki <= qi, e, 0.0)
                ds = e * (dot_nt(values[part], grad) - centre)
                e_ref[part, columns] = e.astype(LOW)
                ds_ref[part, columns] = ds.astype(LOW)
            acc_ref[h] += dot_tn(ds_ref[:count, columns], keys)
        dk = dot_nn(ds_ref[:count], q_ref[0].reshape(heads * rows, size))
        dv = dot_nn(e_ref[:count], do_ref[0].reshape(heads * rows, size))
        for k, start in enumerate(starts):
            dkv_ref[pl.ds(start, rows), :size] += dk[k * rows : (k + 1) * rows]
            dkv_ref[pl.ds(start, rows), size:] += dv[k * rows : (k + 1) * rows]

    in_order(qpos_ref[pl.program_id(0)], step)
    total = jnp.zeros((1, size), F32)
    for h in range(heads):
        grad, gain_part = head_backward(
            acc_ref[h] * (1.0 / LOG2E), proj_ref[0, h], gain_ref[...], cos_ref[...], sin_ref[...]
        )
        dq_ref[:, h * size : (h + 1) * size] = grad.astype(LOW)
        total += gain_part
    dgain_ref[...] += total


def attend_back(qpos, kidx, queries, grads, centre, kv, proj, gain, cos2, sin2, others):
    tiles, heads, rows, size = queries.shape
    seq = kv.shape[0]
    per = pl.BlockSpec((1, heads, rows, size), lambda i, a, b: (i, 0, 0, 0))
    flat = lambda i, a, b: (0, 0)
    rowwise = lambda i, a, b: (i, 0)
    return pl.pallas_call(
        attend_back_kernel,
        grid_spec=pltpu.PrefetchScalarGridSpec(
            num_scalar_prefetch=2,
            grid=(tiles,),
            in_specs=[
                per,
                per,
                pl.BlockSpec((1, heads, 8, rows), lambda i, a, b: (i, 0, 0, 0)),
                pl.BlockSpec((seq, 2 * size), flat),
                per,
                pl.BlockSpec((1, size), flat),
                pl.BlockSpec((rows, size), rowwise),
                pl.BlockSpec((rows, size), rowwise),
            ]
            + [pl.BlockSpec(memory_space=pl.ANY)] * len(others),
            out_specs=[
                pl.BlockSpec((seq, 2 * size), flat),
                pl.BlockSpec((rows, heads * size), rowwise),
                pl.BlockSpec((1, size), flat),
            ],
            scratch_shapes=[pltpu.VMEM((heads, rows, size), F32)]
            + [pltpu.VMEM((2 * rows, heads * rows), LOW)] * 2,
        ),
        out_shape=[
            jax.ShapeDtypeStruct((seq, 2 * size), F32),
            jax.ShapeDtypeStruct((tiles * rows, heads * size), LOW),
            jax.ShapeDtypeStruct((1, size), F32),
        ],
        compiler_params=params(),
        cost_estimate=cost(
            15 * tiles * rows * heads * seq * size, 12e6, tiles * rows * heads * seq
        ),
    )(qpos, kidx, queries, grads, centre, kv, proj, gain[None], cos2, sin2, *others)


def out_kernel(a_ref, b_ref, *rest):
    rest[-1][...] = dot_nn(a_ref[...], b_ref[...]).astype(LOW)


def out_dot(a, b, others):
    block, inner = a.shape
    columns = b.shape[1]
    tile = min(columns, 512)
    return pl.pallas_call(
        out_kernel,
        grid=(columns // tile,),
        in_specs=[
            pl.BlockSpec((block, inner), lambda i: (0, 0)),
            pl.BlockSpec((inner, tile), lambda i: (0, i)),
        ]
        + [pl.BlockSpec(memory_space=pl.ANY)] * len(others),
        out_specs=pl.BlockSpec((block, tile), lambda i: (0, i)),
        out_shape=jax.ShapeDtypeStruct((block, columns), LOW),
        compiler_params=params(),
        cost_estimate=cost(2 * block * inner * columns, 8e6),
    )(a, b, *others)


def token_kernel(a_ref, b_ref, *rest):
    rest[-1][...] = dot_tn(a_ref[...], b_ref[...]).astype(LOW)


def token_dot(a, b, others):
    block, rows = a.shape
    columns = b.shape[1]
    tile = min(rows, 512)
    return pl.pallas_call(
        token_kernel,
        grid=(rows // tile,),
        in_specs=[
            pl.BlockSpec((block, tile), lambda i: (0, i)),
            pl.BlockSpec((block, columns), lambda i: (0, 0)),
        ]
        + [pl.BlockSpec(memory_space=pl.ANY)] * len(others),
        out_specs=pl.BlockSpec((tile, columns), lambda i: (i, 0)),
        out_shape=jax.ShapeDtypeStruct((rows, columns), LOW),
        compiler_params=params(),
        cost_estimate=cost(2 * block * rows * columns, 6e6),
    )(a, b, *others)


def split_low(value):
    high = value.astype(LOW)
    return high, (value - high.astype(F32)).astype(LOW)


def norm_parts(rows):
    rr = lax.rsqrt(jnp.mean(rows * rows, axis=-1, keepdims=True) + EPS)
    return rows * rr, rr


def norm_back(grad, normal, rr, gain):
    weighted = grad * gain
    return rr * (weighted - normal * jnp.mean(weighted * normal, axis=-1, keepdims=True))


def add_all(refs):
    return functools.reduce(jnp.add, [ref[...].astype(F32) for ref in refs])


def pad_rows(rows, count):
    if rows.shape[0] == count:
        return rows
    return jnp.concatenate(
        [rows, jnp.zeros((count - rows.shape[0], rows.shape[1]), rows.dtype)], axis=0
    )


def router_kernel(experts, *refs):
    x_ref, attn_ref, gain_ref, router_ref, mask_ref = refs[:5]
    hidden_ref, mixed_ref, probs_ref = refs[-3:]
    width = x_ref.shape[1]
    lanes = mask_ref.shape[1]
    hidden = add_all([x_ref, attn_ref])
    hidden_ref[...] = hidden
    mixed = (norm_parts(hidden)[0] * gain_ref[...]).astype(LOW)
    mixed_ref[:, :width] = mixed
    logits = dot_nt(mixed, pad_rows(router_ref[...], lanes))
    lane = lax.broadcasted_iota(jnp.int32, logits.shape, 1)
    logits = jnp.where(lane < experts, logits, -1e30)
    weights = jnp.exp(logits - jnp.max(logits, axis=1, keepdims=True))
    probs = weights / jnp.sum(weights, axis=1, keepdims=True)
    probs_ref[...] = probs
    chosen = probs * mask_ref[...]
    high, low = split_low(chosen / jnp.sum(chosen, axis=1, keepdims=True))
    both = high.astype(F32) + pltpu.roll(low.astype(F32), experts, 1)
    mixed_ref[:, width:] = both.astype(LOW)


def route_rows(x, attn, gain, router, mask, experts, others):
    tokens, width = x.shape
    lanes = mask.shape[1]
    operands = [x, attn, gain[None], router, mask]
    shapes = [
        jax.ShapeDtypeStruct((tokens, width), F32),
        jax.ShapeDtypeStruct((tokens, width + lanes), LOW),
        jax.ShapeDtypeStruct((tokens, lanes), F32),
    ]
    return pl.pallas_call(
        functools.partial(router_kernel, experts),
        grid=(1,),
        in_specs=[full(value.shape) for value in operands]
        + [pl.BlockSpec(memory_space=pl.ANY)] * len(others),
        out_specs=[full(shape.shape) for shape in shapes],
        out_shape=shapes,
        compiler_params=params(),
        cost_estimate=cost(2 * tokens * width * lanes, 5e6),
    )(*operands, *others)


def table_kernel(capacity, n_half, meta_ref, col_ref, *rest):
    rows_ref, near_ref, far_ref, near_back_ref, far_back_ref, slots_ref = rest[-6:]
    block = col_ref.shape[0]
    rows, width = rows_ref.shape
    n = 2 * n_half
    tokens = block // n
    cap_half = n_half * capacity
    groups = rows // (2 * cap_half)
    mask = col_ref[:, width:]
    lanes = mask.shape[1]
    padded = -(-groups // 16) * 16
    group = lax.broadcasted_iota(jnp.int32, (padded, lanes), 0)
    lane = lax.broadcasted_iota(jnp.int32, (padded, lanes), 1)
    wanted = jnp.logical_and(lane == group * n + meta_ref[0], group < groups)
    hits = dot_nt(jnp.where(wanted, 1.0, 0.0).astype(LOW), mask)
    before = lax.broadcasted_iota(jnp.int32, (tokens, tokens), 0)
    after_it = lax.broadcasted_iota(jnp.int32, (tokens, tokens), 1)
    earlier = jnp.where(before < after_it, 1.0, 0.0).astype(LOW)
    for z in range(n):
        hit = hits[:, z * tokens : (z + 1) * tokens]
        rank = dot_nn(hit.astype(LOW), earlier)
        turn = (meta_ref[1 + z] * capacity).astype(F32)
        slot = jnp.where(hit > 0.5, rank + turn, -1.0)
        slots_ref[:, z * tokens : (z + 1) * tokens] = slot[:groups]

    def one_hot(slots, count, first):
        slot = lax.broadcasted_iota(jnp.int32, (groups, count, slots.shape[1]), 1).astype(F32)
        same = slots[:, None, :] == slot + float(first)
        return jnp.where(same, 1.0, 0.0).reshape(groups * count, slots.shape[1])

    spread = one_hot(slots_ref[...], 2 * cap_half, 0).astype(LOW)
    rows_ref[...] = dot_nn(spread, col_ref[:, :width]).astype(LOW)
    for part, (to_ref, back_ref) in enumerate([(near_ref, near_back_ref), (far_ref, far_back_ref)]):
        pieces = []
        for k in range(n_half):
            start = pl.multiple_of(meta_ref[1 + n + part * n_half + k] * tokens, tokens)
            pieces.append(slots_ref[:, pl.ds(start, tokens)])
        spread = one_hot(jnp.concatenate(pieces, axis=1), cap_half, part * cap_half)
        to_ref[...] = spread.astype(LOW)
        back_ref[...] = jnp.transpose(spread).astype(LOW)


def make_tables(meta, col, width, groups, n_half, capacity, others):
    block = col.shape[0]
    rows = groups * n_half * capacity
    shapes = (
        [jax.ShapeDtypeStruct((2 * rows, width), LOW)]
        + [jax.ShapeDtypeStruct((rows, block // 2), LOW)] * 2
        + [jax.ShapeDtypeStruct((block // 2, rows), LOW)] * 2
    )
    outs = pl.pallas_call(
        functools.partial(table_kernel, capacity, n_half),
        grid_spec=pltpu.PrefetchScalarGridSpec(
            num_scalar_prefetch=1,
            grid=(1,),
            in_specs=[full(col.shape)] + [pl.BlockSpec(memory_space=pl.ANY)] * len(others),
            out_specs=[full(shape.shape) for shape in shapes],
            scratch_shapes=[pltpu.VMEM((groups, block), F32)],
        ),
        out_shape=shapes,
        compiler_params=params(),
        cost_estimate=cost(4 * rows * block * width, 12e6),
    )(meta, col, *others)
    return outs[0], outs[1:3], outs[3:]


def spread_kernel(choices, place_ref, spread_ref, *refs):
    out_ref, rows_ref = refs[-2:]
    for k, by_place in enumerate(choices):
        for which in sorted(set(by_place)):
            hit = functools.reduce(
                jnp.logical_or,
                [place_ref[0] == i for i, other in enumerate(by_place) if other == which],
            )

            @pl.when(hit)
            def _():
                tokens = refs[which].shape[0]
                rows_ref[k * tokens : (k + 1) * tokens] = refs[which][...]

    out_ref[...] = dot_nn(spread_ref[...], rows_ref[...]).astype(LOW)


def spread_rows(place, spread, found, turns, others):
    n = lax.axis_size("expert")
    order = arrival_order(n)
    distances = sorted({order[i][turn] - i for i in range(n) for turn in turns})
    choices = [[distances.index(order[i][turn] - i) for i in range(n)] for turn in turns]
    chunks = [found[distance] for distance in distances]
    tokens, wide = chunks[0].shape
    rows = spread.shape[0]
    return pl.pallas_call(
        functools.partial(spread_kernel, choices),
        grid_spec=pltpu.PrefetchScalarGridSpec(
            num_scalar_prefetch=1,
            grid=(1,),
            in_specs=[full(spread.shape)]
            + [full(chunk.shape) for chunk in chunks]
            + [pl.BlockSpec(memory_space=pl.ANY)] * len(others),
            out_specs=full((rows, wide)),
            scratch_shapes=[pltpu.VMEM((len(turns) * tokens, wide), LOW)],
        ),
        out_shape=jax.ShapeDtypeStruct((rows, wide), LOW),
        compiler_params=params(),
        cost_estimate=cost(2 * rows * len(turns) * tokens * wide, 5e6),
    )(place, spread, *chunks, *others)


def router_back_kernel(experts, *refs):
    sum_ref, g_ref, hidden_ref, gain_ref, router_ref, mask_ref, probs_ref = refs[:7]
    grad_ref, low_ref, dgain_ref, drouter_ref = refs[-4:]
    width = g_ref.shape[1]
    lanes = mask_ref.shape[1]
    total = sum_ref[...].astype(F32)
    table = total[:, width:]
    mask, probs = mask_ref[...], probs_ref[...]
    grad_gates = (table + pltpu.roll(table, lanes - experts, 1)) * mask
    chosen = probs * mask
    chosen_sum = jnp.sum(chosen, axis=1, keepdims=True)
    mean = jnp.sum(grad_gates * (chosen / chosen_sum), axis=1, keepdims=True)
    centred = mask * (grad_gates - mean) / chosen_sum
    grad_logits = probs * (centred - jnp.sum(centred * chosen, axis=1, keepdims=True))
    high, low = split_low(grad_logits)
    router = pad_rows(router_ref[...], lanes)
    grad = total[:, :width] + dot_nn(high, router) + dot_nn(low, router)
    normal, rr = norm_parts(hidden_ref[...])
    mixed = (normal * gain_ref[...]).astype(LOW)
    drouter_ref[...] = dot_tn(high, mixed) + dot_tn(low, mixed)
    dgain_ref[...] = jnp.sum(grad * normal, axis=0, keepdims=True)
    grad_hidden = g_ref[...].astype(F32) + norm_back(grad, normal, rr, gain_ref[...])
    grad_ref[...] = grad_hidden
    low_ref[...] = grad_hidden.astype(LOW)


def route_back(summed, g, hidden, gain, router, mask, probs, experts, others):
    tokens, width = g.shape
    lanes = mask.shape[1]
    operands = [summed, g, hidden, gain[None], router, mask, probs]
    shapes = [
        jax.ShapeDtypeStruct((tokens, width), F32),
        jax.ShapeDtypeStruct((tokens, width), LOW),
        jax.ShapeDtypeStruct((1, width), F32),
        jax.ShapeDtypeStruct((lanes, width), F32),
    ]
    return pl.pallas_call(
        functools.partial(router_back_kernel, experts),
        grid=(1,),
        in_specs=[full(value.shape) for value in operands]
        + [pl.BlockSpec(memory_space=pl.ANY)] * len(others),
        out_specs=[full(shape.shape) for shape in shapes],
        out_shape=shapes,
        compiler_params=params(),
        cost_estimate=cost(8 * tokens * width * lanes, 8e6),
    )(*operands, *others)


def combine_kernel(n_half, meta_ref, near_table_ref, far_table_ref, near_ref, far_ref, *rest):
    del meta_ref
    turn = pl.program_id(0)

    @pl.when(turn < n_half)
    def _():
        rest[-1][...] = dot_nn(near_table_ref[...], near_ref[...]).astype(LOW)

    @pl.when(turn >= n_half)
    def _():
        rest[-1][...] = dot_nn(far_table_ref[...], far_ref[...]).astype(LOW)


def combine_rows(meta, tables, rows, n_half, others):
    tokens = tables[0].shape[0] // n_half
    slots, wide = rows[0].shape
    n = 2 * n_half
    return pl.pallas_call(
        functools.partial(combine_kernel, n_half),
        grid_spec=pltpu.PrefetchScalarGridSpec(
            num_scalar_prefetch=1,
            grid=(n,),
            in_specs=[
                pl.BlockSpec((tokens, slots), lambda i, m: (jnp.minimum(i, n_half - 1), 0)),
                pl.BlockSpec((tokens, slots), lambda i, m: (jnp.maximum(i - n_half, 0), 0)),
            ]
            + [full(value.shape) for value in rows]
            + [pl.BlockSpec(memory_space=pl.ANY)] * len(others),
            out_specs=pl.BlockSpec((tokens, wide), lambda i, m: (m[1 + n + i], 0)),
        ),
        out_shape=jax.ShapeDtypeStruct((n * tokens, wide), LOW),
        compiler_params=params(),
        cost_estimate=cost(2 * slots * n * tokens * wide, 10e6),
    )(meta, *tables, *rows, *others)


def expert_kernel(experts, who_ref, x_ref, gate_ref, up_ref, pull_ref, *rest):
    act_ref, dgate_ref, dup_ref, copy_ref = rest[-4:]
    width = gate_ref.shape[0]
    x = x_ref[:, :width]
    table = x_ref[:, width:].astype(F32)
    lane = lax.broadcasted_iota(jnp.int32, table.shape, 1)
    mine = who_ref[0]
    gate = jnp.sum(
        jnp.where(jnp.logical_or(lane == mine, lane == mine + experts), table, 0.0),
        axis=1,
        keepdims=True,
    )
    pre_gate = dot_nn(x, gate_ref[...])
    pre_up = dot_nn(x, up_ref[...])
    pull = pull_ref[...].reshape(pre_up.shape)
    sig = 1.0 / (1.0 + jnp.exp(-pre_gate))
    silu = pre_gate * sig
    act = silu * pre_up
    act_ref[...] = (act * gate).astype(LOW)
    high, low = split_low(jnp.sum(act * pull, axis=1, keepdims=True))
    pull = pull * gate
    dup = (pull * silu).astype(LOW)
    dgate = (pull * pre_up * (sig * (1.0 + pre_gate * (1.0 - sig)))).astype(LOW)
    dgate_ref[...] = dgate
    dup_ref[...] = dup
    copy_ref[:, :width] = (dot_nt(dgate, gate_ref[...]) + dot_nt(dup, up_ref[...])).astype(LOW)
    back = jnp.where(lane == mine, high.astype(F32), 0.0)
    back = jnp.where(lane == mine + experts, low.astype(F32), back)
    copy_ref[:, width:] = back.astype(LOW)


def run_expert(who, x, w_gate, w_up, pull, part, experts):
    rows, wide = x.shape
    width, hidden = w_gate.shape
    groups, _, slots, _ = pull.shape
    each = groups // 2
    tile = each * slots
    by_rows = lambda columns: pl.BlockSpec((tile, columns), lambda i, p: (i, 0))
    return pl.pallas_call(
        functools.partial(expert_kernel, experts),
        grid_spec=pltpu.PrefetchScalarGridSpec(
            num_scalar_prefetch=1,
            grid=(2,),
            in_specs=[
                by_rows(wide),
                full(w_gate.shape),
                full(w_up.shape),
                pl.BlockSpec((each, 1, slots, hidden), lambda i, p: (i, part, 0, 0)),
            ],
            out_specs=[by_rows(hidden), by_rows(hidden), by_rows(hidden), by_rows(wide)],
        ),
        out_shape=[jax.ShapeDtypeStruct((rows, hidden), LOW)] * 3
        + [jax.ShapeDtypeStruct((rows, wide), LOW)],
        compiler_params=params(),
        cost_estimate=cost(8 * rows * width * hidden, 20e6, rows * hidden),
    )(who, x, w_gate, w_up, pull)


def input_kernel(grad_ref, x_ref, gain_ref, more_ref, out_ref):
    normal, rr = norm_parts(x_ref[...].astype(F32))
    grad = grad_ref[...].astype(F32)
    out_ref[...] = more_ref[...] + norm_back(grad, normal, rr, gain_ref[...])


def input_back(grad, x, gain, more):
    tokens, width = x.shape
    operands = [grad, x, gain[None], more]
    return pl.pallas_call(
        input_kernel,
        grid=(1,),
        in_specs=[full(value.shape) for value in operands],
        out_specs=full(more.shape),
        out_shape=jax.ShapeDtypeStruct((tokens, width), F32),
        compiler_params=params(),
        cost_estimate=cost(20 * tokens * width, 5e6),
    )(*operands)


def kv_back_kernel(factor, n_parts, c_ref, dkv_ref, *refs):
    parts = refs[:n_parts]
    proj_ref, gain_ref, cos_ref, sin_ref = refs[n_parts : n_parts + 4]
    grad_ref, dgain_ref = refs[-2:]
    size = proj_ref.shape[1]
    total = functools.reduce(jnp.add, [part[...].astype(F32) for part in parts], dkv_ref[...])
    grad, dgain = head_backward(
        total[:, :size] * factor, proj_ref[...], gain_ref[...], cos_ref[...], sin_ref[...]
    )
    grad_ref[:, :size] = grad.astype(LOW)
    grad_ref[:, size:] = total[:, size:].astype(LOW)
    dgain_ref[...] = dgain


def kv_back(context, dkv, parts, proj, gain, cos2, sin2, factor, others):
    block, size = proj.shape
    operands = [proj, gain[None], cos2, sin2]
    shapes = [
        jax.ShapeDtypeStruct((block, 2 * size), LOW),
        jax.ShapeDtypeStruct((1, size), F32),
    ]
    return pl.pallas_call(
        functools.partial(kv_back_kernel, factor, len(parts)),
        grid_spec=pltpu.PrefetchScalarGridSpec(
            num_scalar_prefetch=1,
            grid=(1,),
            in_specs=[pl.BlockSpec((block, 2 * size), lambda i, c: (c[0], 0))]
            + [full(part.shape) for part in parts]
            + [full(value.shape) for value in operands]
            + [pl.BlockSpec(memory_space=pl.ANY)] * len(others),
            out_specs=[full(shape.shape) for shape in shapes],
        ),
        out_shape=shapes,
        compiler_params=params(),
        cost_estimate=cost(40 * block * size, 5e6),
    )(context.astype(jnp.int32)[None], dkv, *parts, *operands, *others)


def pair_kernel(a_ref, b_ref, *rest):
    rest[-1][...] = (a_ref[...].astype(F32) + b_ref[...].astype(F32)).astype(LOW)


def pair_sum(a, b, others):
    rows, columns = a.shape
    tiles = 2
    spec = pl.BlockSpec((rows // tiles, columns), lambda i: (i, 0))
    return pl.pallas_call(
        pair_kernel,
        grid=(tiles,),
        in_specs=[spec, spec] + [pl.BlockSpec(memory_space=pl.ANY)] * len(others),
        out_specs=spec,
        out_shape=jax.ShapeDtypeStruct((rows, columns), LOW),
        compiler_params=params(),
        cost_estimate=cost(rows * columns, 6 * rows * columns),
    )(a, b, *others)


def fold_kernel(n_pairs, s_ref, *refs):
    del s_ref
    send_ref, keep_ref = refs[-2:]
    totals = [
        (refs[2 * k][...].astype(F32) + refs[2 * k + 1][...].astype(F32)).astype(LOW)
        for k in range(n_pairs)
    ]
    for half, out_ref in enumerate((send_ref, keep_ref)):

        @pl.when(pl.program_id(0) == half)
        def _():
            first = 0
            for total in totals:
                last = first + total.shape[1]
                out_ref[:, first:last] = total
                first = last


def fold(pairs, base, bit, others):
    rows = pairs[0][1].shape[0]
    columns = sum(got.shape[1] for _, got in pairs)
    tiles = 2
    tile = rows // (2 * tiles)
    side = lambda h, m: (1 - m[1]) * (1 - h) + m[1] * h
    specs = []
    for _, got in pairs:
        wide = got.shape[1]
        specs.append(
            pl.BlockSpec(
                (tile, wide), lambda h, j, m: (m[0] * 2 * tiles + side(h, m) * tiles + j, 0)
            )
        )
        specs.append(pl.BlockSpec((tile, wide), lambda h, j, m: (side(h, m) * tiles + j, 0)))
    shape = jax.ShapeDtypeStruct((rows // 2, columns), LOW)
    return pl.pallas_call(
        functools.partial(fold_kernel, len(pairs)),
        grid_spec=pltpu.PrefetchScalarGridSpec(
            num_scalar_prefetch=1,
            grid=(2, tiles),
            in_specs=specs + [pl.BlockSpec(memory_space=pl.ANY)] * len(others),
            out_specs=[
                pl.BlockSpec((tile, columns), lambda h, j, m: (j * (1 - h) + (tiles - 1) * h, 0)),
                pl.BlockSpec((tile, columns), lambda h, j, m: (j * h, 0)),
            ],
        ),
        out_shape=[shape, shape],
        compiler_params=params(),
        cost_estimate=cost(rows * columns, 6 * rows * columns),
    )(
        jnp.stack([base, bit]).astype(jnp.int32),
        *[value for pair in pairs for value in pair],
        *others,
    )


def normed_kernel(q_ref, kv_ref, wq_ref, wkv_ref, rows_ref, *rest):
    out_ref, dgain_ref = rest[-2:]
    grad = dot_nt(q_ref[...], wq_ref[...]) + dot_nt(kv_ref[...], wkv_ref[...])
    out_ref[...] = grad.astype(LOW)
    dgain_ref[...] = jnp.sum(grad * rows_ref[...].astype(F32), axis=0, keepdims=True)


def normed_back(grad_q, grad_kv, w_q, w_kv, rows, others):
    block, width = rows.shape
    tile = 512
    column = lambda i: (0, i)
    return pl.pallas_call(
        normed_kernel,
        grid=(width // tile,),
        in_specs=[
            full(grad_q.shape),
            full(grad_kv.shape),
            pl.BlockSpec((tile, w_q.shape[1]), lambda i: (i, 0)),
            pl.BlockSpec((tile, w_kv.shape[1]), lambda i: (i, 0)),
            pl.BlockSpec((block, tile), column),
        ]
        + [pl.BlockSpec(memory_space=pl.ANY)] * len(others),
        out_specs=[pl.BlockSpec((block, tile), column), pl.BlockSpec((1, tile), column)],
        out_shape=[
            jax.ShapeDtypeStruct((block, width), LOW),
            jax.ShapeDtypeStruct((1, width), F32),
        ],
        compiler_params=params(),
        cost_estimate=cost(2 * block * width * (w_q.shape[1] + w_kv.shape[1]), 12e6),
    )(grad_q, grad_kv, w_q, w_kv, rows, *others)


def pack_kernel(
    experts, router_ref, attn_ref, gain_ref, mlp_ref, q_ref, k_ref, out_ref, rows_ref
):
    size = q_ref.shape[1]
    rows_ref[:experts] = router_ref[:experts]
    rows_ref[experts:] = jnp.zeros_like(rows_ref[experts:])
    rows_ref[experts : experts + 1] = attn_ref[...] / gain_ref[...]
    rows_ref[experts + 1 : experts + 2] = mlp_ref[...]
    rows_ref[experts + 2 : experts + 3, :size] = q_ref[...]
    rows_ref[experts + 2 : experts + 3, size : 2 * size] = k_ref[...]
    out_ref[...] = rows_ref[...].astype(LOW)


def pack_small(experts, router, attn, gain, mlp, q, k):
    width = attn.shape[1]
    shape = (-(-(experts + 3) // 16) * 16, width)
    operands = [router, attn, gain[None], mlp, q, k]
    return pl.pallas_call(
        functools.partial(pack_kernel, experts),
        grid=(1,),
        in_specs=[full(value.shape) for value in operands],
        out_specs=full(shape),
        out_shape=jax.ShapeDtypeStruct(shape, LOW),
        scratch_shapes=[pltpu.VMEM(shape, F32)],
        compiler_params=params(),
        cost_estimate=cost(shape[0] * width, 6 * shape[0] * width),
    )(*operands)


def part_sum_kernel(parts_ref, *rest):
    total = parts_ref[0].astype(F32)
    for k in range(1, parts_ref.shape[0]):
        total += parts_ref[k].astype(F32)
    rest[-1][...] = total.astype(LOW)


def part_sum(parts, others):
    count, rows, columns = parts.shape
    tiles = 2
    return pl.pallas_call(
        part_sum_kernel,
        grid=(tiles,),
        in_specs=[pl.BlockSpec((count, rows // tiles, columns), lambda i: (0, i, 0))]
        + [pl.BlockSpec(memory_space=pl.ANY)] * len(others),
        out_specs=pl.BlockSpec((rows // tiles, columns), lambda i: (i, 0)),
        out_shape=jax.ShapeDtypeStruct((rows, columns), LOW),
        compiler_params=params(),
        cost_estimate=cost(count * rows * columns, 4 * count * rows * columns),
    )(parts, *others)


def widen_kernel(n_chunks, n_outs, at_ref, *refs):
    del at_ref
    outs = refs[-n_outs:]
    widths = [ref.shape[1] for ref in outs]
    for k in range(n_chunks):

        @pl.when(pl.program_id(0) == k)
        def _():
            first = 0
            for wide, out_ref in zip(widths, outs):
                out_ref[...] = refs[k][:, first : first + wide].astype(F32)
                first += wide


def widen(places, chunks, widths, others):
    rows, columns = chunks[0].shape
    count = len(chunks)
    return pl.pallas_call(
        functools.partial(widen_kernel, count, len(widths)),
        grid_spec=pltpu.PrefetchScalarGridSpec(
            num_scalar_prefetch=1,
            grid=(count,),
            in_specs=[full(chunk.shape) for chunk in chunks]
            + [pl.BlockSpec(memory_space=pl.ANY)] * len(others),
            out_specs=[pl.BlockSpec((rows, wide), lambda i, at: (at[i], 0)) for wide in widths],
        ),
        out_shape=[jax.ShapeDtypeStruct((count * rows, wide), F32) for wide in widths],
        compiler_params=params(),
        cost_estimate=cost(rows * columns, 6 * count * rows * columns),
    )(jnp.stack(places).astype(jnp.int32), *chunks, *others)


def sum_axis(total, axis):
    n = lax.axis_size(axis)
    s = 1
    while s < n:
        got = lax.ppermute(total.astype(LOW), axis, [(i, i ^ s) for i in range(n)])
        total = total.astype(F32) + got.astype(F32)
        s *= 2
    return total


def swap_dp(rows):
    return lax.ppermute(rows, "dp", [(0, 1), (1, 0)])


def swap_context(rows, s):
    n = lax.axis_size("context")
    return lax.ppermute(rows, "context", [(i, i ^ s) for i in range(n)])


def dp_got(grad):
    d = lax.axis_index("dp")
    rows = grad.shape[0] // 2
    return swap_dp(lax.dynamic_slice_in_dim(grad, (1 - d) * rows, rows))


def plane_turns():
    d, c = lax.axis_index("dp"), lax.axis_index("context")
    low, high = lax.rem(c, 2), lax.div(c, 2)

    def swap(first, second):
        perm = [(i, i ^ first) for i in range(4)] + [(4 + i, 4 + (i ^ second)) for i in range(4)]
        return lambda rows: lax.ppermute(rows, GROUP_AXES, perm)

    return [
        (jnp.where(d == 0, low, high), swap(1, 2)),
        (jnp.where(d == 0, high, low), swap(2, 1)),
    ]


def plane_first(pairs, others):
    (bit_1, _), _ = plane_turns()
    return fold(pairs, lax.axis_index("dp"), bit_1, others)


def plane_rest(send, keep, others):
    (_, swap_1), (bit_2, swap_2) = plane_turns()
    send, keep = fold([(keep, swap_1(send))], jnp.int32(0), bit_2, [])
    return pair_sum(keep, swap_2(send), others)


def plane_spread(own):
    (_, swap_1), (_, swap_2) = plane_turns()
    second = swap_2(own)
    return [own, second, swap_1(own), swap_1(second)]


def quarter_places(rank):
    d = lax.axis_index("dp")
    c = lax.axis_index("context")
    low, high = lax.rem(c, 2), lax.div(c, 2)
    places = []
    for core in (d, 1 - d):
        bit_1 = jnp.where(core == 0, low, high)
        bit_2 = jnp.where(core == 0, high, low)
        for flip_1, flip_2 in ((0, 0), (0, 1), (1, 0), (1, 1)):
            places.append(4 * core + rank(core, bit_1 ^ flip_1, bit_2 ^ flip_2))
    return places


def widen_all(quarters, rank, widths, others):
    chunks = quarters + [swap_dp(part) for part in quarters]
    return widen(quarter_places(rank), chunks, widths, others)


def arrival_order(n):
    return [sorted(range(n), key=lambda j: (abs(j - i), j)) for i in range(n)]


def choose(index, options):
    distinct = []
    for option in options:
        if option is not None and not any(option is other for other in distinct):
            distinct.append(option)
    result = distinct[0]
    for option in distinct[1:]:
        mask = functools.reduce(
            jnp.logical_or, [index == i for i, other in enumerate(options) if other is option]
        )
        result = jnp.where(mask, option, result)
    return result


def line_gather(chunk):
    return line_steps({0: chunk}, 1, lax.axis_size("expert"))


def line_steps(found, first, stop):
    n = lax.axis_size("expert")
    found = dict(found)
    for s in range(first, stop):
        found[-s] = lax.ppermute(
            found[1 - s], "expert", [(i, i + 1) for i in range(s - 1, n - 1)]
        )
        found[s] = lax.ppermute(found[s - 1], "expert", [(i + 1, i) for i in range(n - s)])
    return found


def context_gather(rows):
    n = lax.axis_size("context")
    c = lax.axis_index("context")
    found = {0: rows}
    for s in range(1, n):
        found[s] = lax.ppermute(rows, "context", [(i, i ^ s) for i in range(n)])
    return jnp.concatenate([choose(c, [found[i ^ j] for i in range(n)]) for j in range(n)], axis=0)


def context_parts(rows):
    n = lax.axis_size("context")
    c = lax.axis_index("context")
    each = rows.shape[0] // n
    return [
        swap_context(lax.dynamic_slice_in_dim(rows, (c ^ s) * each, each).astype(LOW), s)
        for s in range(1, n)
    ]


def zero_of(*others):
    return functools.reduce(
        jnp.add,
        [
            lax.slice(other, (0,) * other.ndim, (1,) * other.ndim).reshape(()).astype(F32) * 0.0
            for other in others
        ],
    )


def after(value, *others):
    return (value.astype(F32) + zero_of(*others)).astype(value.dtype)


def on_device(
    layer_input,
    grad_output,
    attn_gain,
    query_weight,
    key_weight,
    value_weight,
    q_gain,
    k_gain,
    output_weight,
    mlp_gain,
    router,
    w_gate,
    w_up,
    w_down,
    routes,
    half_order,
):
    n_context = lax.axis_size("context")
    n_expert = lax.axis_size("expert")
    n_groups = lax.axis_size(GROUP_AXES)
    tok_dev, width = layer_input.shape[1:]
    size = q_gain.shape[0]
    kv_total = key_weight.shape[1] * n_expert
    group_dev = n_expert // (kv_total // size)
    kv_index = lax.axis_index("expert") // group_dev
    block = tok_dev * n_expert
    seq = block * n_context
    half = block // 2
    experts = router.shape[1]
    exp_dev = w_gate.shape[0]
    top = routes.shape[2]
    capacity = max(2, (tok_dev * top * 9 + 8 * experts - 1) // (8 * experts))
    scale = size ** (-0.5)

    seq_rows = jnp.arange(seq, dtype=jnp.int32)
    context = lax.axis_index("context")
    own_halves = lax.dynamic_slice_in_dim(half_order, 2 * context, 2)
    own_pos = (own_halves[:, None] * half + jnp.arange(half, dtype=jnp.int32)[None]).reshape(-1)
    per_half = half // TILE
    tile_pos = (half_order[:, None] * per_half + jnp.arange(per_half, dtype=jnp.int32)).reshape(-1)
    kidx = jnp.sum(
        (tile_pos[None, :] == jnp.arange(seq // TILE, dtype=jnp.int32)[:, None])
        * jnp.arange(seq // TILE, dtype=jnp.int32)[None, :],
        axis=1,
    ).astype(jnp.int32)
    qpos = lax.dynamic_slice_in_dim(tile_pos, context * (block // TILE), block // TILE)
    entry = jnp.arange(size)
    freq = jnp.power(THETA, -(2 * (entry % (size // 2))).astype(F32) / size)
    angles = own_pos.astype(F32)[:, None] * freq[None, :]
    cos2 = jnp.cos(angles)
    sin2 = jnp.sin(angles) * jnp.where(entry < size // 2, -1.0, 1.0)[None, :]

    place = lax.axis_index("expert")
    place_1 = place.astype(jnp.int32)[None]
    lanes = -(-2 * experts // 128) * 128
    mask = jnp.any(
        routes[0][:, :, None] == jnp.arange(lanes, dtype=jnp.int32)[None, None, :], axis=1
    )
    mask_wide = mask.astype(F32)
    router_rows = router.T

    x_low = layer_input[0]
    x_normal, _ = norm_parts(x_low.astype(F32))
    normed_found = line_gather((x_normal * attn_gain).astype(LOW))
    if group_dev == 1:
        kv_weights = jnp.concatenate([key_weight, value_weight], axis=1)
    else:
        key_whole = lax.all_gather(key_weight, "expert", axis=1, tiled=True)
        value_whole = lax.all_gather(value_weight, "expert", axis=1, tiled=True)
        kv_weights = jnp.concatenate(
            [
                lax.dynamic_slice_in_dim(key_whole, kv_index * size, size, 1),
                lax.dynamic_slice_in_dim(value_whole, kv_index * size, size, 1),
            ],
            axis=1,
        )
    grad_low = grad_output[0]
    normed_rows, own_kv, key_proj, grad_wide = project_keys(
        place_1,
        normed_found,
        kv_weights,
        k_gain,
        cos2,
        sin2,
        scale * LOG2E,
        grad_low,
        mask_wide,
    )
    grad_col = lax.all_gather(grad_wide, "expert", axis=0, tiled=True)
    kv_whole = context_gather(own_kv)
    queries, query_proj = project_queries(normed_rows, query_weight, q_gain, cos2, sin2)

    n_half = n_expert // 2
    order_here = jnp.asarray(arrival_order(n_expert), jnp.int32)[place]
    turn_here = jnp.sum(
        (order_here[:, None] == jnp.arange(n_expert, dtype=jnp.int32)[None, :])
        * jnp.arange(n_expert, dtype=jnp.int32)[:, None],
        axis=0,
    ).astype(jnp.int32)
    meta = jnp.concatenate([place_1, turn_here, order_here])
    grad_sent, spreads, back_tables = make_tables(
        meta, grad_col, width, n_groups, n_half, capacity, []
    )

    def swap_plane(rows):
        parts = rows.reshape(n_groups, -1, rows.shape[1])
        parts = lax.all_to_all(parts, GROUP_AXES, split_axis=0, concat_axis=0, tiled=True)
        return parts.reshape(rows.shape)

    attended, inverse = attend(qpos, kidx, queries, kv_whole, [])
    attn_part = out_dot(attended, output_weight, [grad_col])
    attn_rows = lax.psum_scatter(attn_part, "expert", scatter_dimension=0, tiled=True)

    grad_x = swap_plane(grad_sent)
    act_pull = dot_nt(grad_x, w_down[0]).reshape(n_groups, 2, n_half * capacity, -1)

    hidden, mixed, probs = route_rows(
        x_low, attn_rows, mlp_gain, router_rows, mask_wide, experts, []
    )

    who = (lax.axis_index(ALL_AXES) * exp_dev).astype(jnp.int32)[None]
    mixed_found = line_gather(mixed)
    near = spread_rows(place_1, spreads[0], mixed_found, range(n_half), [grad_x])
    x_near = swap_plane(near)
    worked_near = run_expert(who, x_near, w_gate[0], w_up[0], act_pull, 0, experts)
    far = spread_rows(place_1, spreads[1], mixed_found, range(n_half, n_expert), [x_near])
    x_far = swap_plane(far)
    worked_far = run_expert(who, x_far, w_gate[0], w_up[0], act_pull, 1, experts)
    xs = [x_near, x_far]
    acts, gate_lows, up_lows, copies = (list(pair) for pair in zip(worked_near, worked_far))
    back_far = swap_plane(copies[1])
    back_near = swap_plane(copies[0])
    join = lambda parts: jnp.concatenate(parts, axis=0)
    x_all = join([x[:, :width] for x in xs])
    grad_w_gate = dot_tn(x_all, join(gate_lows))
    grad_w_up = dot_tn(x_all, join(up_lows))
    grad_by_round = jnp.swapaxes(
        grad_x.reshape(n_groups, 2, n_half * capacity, width), 0, 1
    ).reshape(-1, width)
    grad_w_down = dot_tn(join(acts), grad_by_round)
    copies_col = combine_rows(
        meta, back_tables, [back_near, back_far], n_half, [grad_w_gate, grad_w_up]
    )
    copies_sum = lax.psum_scatter(copies_col, "expert", scatter_dimension=0, tiled=True)

    returned = [dot_nn(act, w_down[0]).astype(LOW) for act in acts]
    returned_near = swap_plane(returned[0])

    grad_hidden, grad_hidden_low, grad_mlp_gain, grad_router = route_back(
        copies_sum,
        grad_low,
        hidden,
        mlp_gain,
        router_rows,
        mask_wide,
        probs,
        experts,
        [returned_near, grad_w_down],
    )

    returned_far = swap_plane(returned[1])
    grad_attn = lax.all_gather(grad_hidden_low, "expert", axis=0, tiled=True)
    grad_o, centre = grad_attended(
        grad_attn, output_weight, attended, inverse, [returned_far]
    )
    combined = combine_rows(meta, back_tables, [returned_near, returned_far], n_half, [])
    output_rows = lax.psum_scatter(combined, "expert", scatter_dimension=0, tiled=True)
    w_out = token_dot(attended, grad_attn, [])
    w_out_parts = swap_plane(w_out)
    grad_kv, grad_q, grad_q_gain = attend_back(
        qpos,
        kidx,
        queries,
        grad_o,
        centre,
        kv_whole,
        query_proj,
        q_gain,
        cos2,
        sin2,
        [w_out, combined],
    )
    kv_parts = context_parts(grad_kv)
    w_query = token_dot(normed_rows, grad_q, [w_out_parts])
    w_query_got = dp_got(w_query)
    output_rows = hidden + output_rows.astype(F32) + zero_of(w_query)

    kv_grads, grad_k_gain = kv_back(
        context, grad_kv, kv_parts, key_proj, k_gain, cos2, sin2, scale, [w_query_got]
    )
    w_out_quarters = plane_spread(part_sum(w_out_parts.reshape(n_groups, -1, width), kv_parts))
    w_kv = token_dot(normed_rows, kv_grads, [])
    pairs = [(w_query, w_query_got)]
    widths = [query_weight.shape[1]]
    if group_dev == 1:
        pairs.append((w_kv, dp_got(w_kv)))
        widths += [key_weight.shape[1], value_weight.shape[1]]
    send, keep = plane_first(pairs, [*kv_parts, *w_out_quarters])

    grad_normed, gain_rows = normed_back(
        grad_q, kv_grads, query_weight, kv_weights, normed_rows, [keep]
    )
    grad_normed = lax.psum_scatter(grad_normed, "expert", scatter_dimension=0, tiled=True)
    grad_input = input_back(grad_normed, x_low, attn_gain, grad_hidden)
    small = pack_small(
        experts, grad_router, gain_rows, attn_gain, grad_mlp_gain, grad_q_gain, grad_k_gain
    )
    small_dp = sum_axis(small, "dp")
    small_context = sum_axis(small_dp, "context")
    small_sum = sum_axis(small_context, "expert")

    (grad_w_out,) = widen_all(
        w_out_quarters,
        lambda core, b1, b2: jnp.where(core == 0, b1 + 2 * b2, 2 * b1 + b2),
        [width],
        [],
    )
    quarter = plane_rest(send, keep, [grad_w_out, output_rows])
    grad_w_query, *more = widen_all(
        plane_spread(quarter), lambda core, b1, b2: 2 * b1 + b2, widths, [grad_input]
    )
    if group_dev == 1:
        grad_w_key, grad_w_value = more
    else:
        blank = jnp.zeros((width, kv_total), LOW)
        pieces = []
        for part in (w_kv[:, :size], w_kv[:, size:]):
            padded = lax.dynamic_update_slice(blank, part, (0, kv_index * size))
            pieces.append(lax.psum_scatter(padded, "expert", scatter_dimension=1, tiled=True))
        grad_w_key, grad_w_value = (lax.psum(piece, GROUP_AXES).astype(F32) for piece in pieces)
    grad_attn_gain, grad_mlp_gain = small_sum[experts], small_sum[experts + 1]
    grad_q_gain = small_sum[experts + 2, :size]
    grad_k_gain = small_sum[experts + 2, size : 2 * size]
    return (
        output_rows.astype(LOW)[None],
        grad_input[None],
        grad_attn_gain,
        grad_w_query,
        grad_w_key,
        grad_w_value,
        grad_q_gain,
        grad_k_gain,
        grad_w_out,
        grad_mlp_gain,
        small_sum[:experts].T,
        grad_w_gate[None],
        grad_w_up[None],
        grad_w_down[None],
    )


def solution(mesh):
    rows = P("dp", ("context", "expert"), None)
    expert = P(ALL_AXES, None, None)
    columns = P(None, "expert")
    in_specs = (
        rows,
        rows,
        P(),
        columns,
        columns,
        columns,
        P(),
        P(),
        P("expert", None),
        P(),
        P(),
        expert,
        expert,
        expert,
        rows,
        P(),
    )
    out_specs = (
        rows,
        rows,
        P(),
        columns,
        columns,
        columns,
        P(),
        P(),
        P("expert", None),
        P(),
        P(),
        expert,
        expert,
        expert,
    )
    return jax.shard_map(
        on_device, mesh=mesh, in_specs=in_specs, out_specs=out_specs, check_vma=False
    )
```

```python
import functools
import math

import jax
import jax.numpy as jnp
from jax import lax
from jax.experimental import pallas as pl
from jax.experimental.pallas import tpu as pltpu
from jax.sharding import PartitionSpec as P

EPS = 1e-06
THETA = 1000000.0
TILE = 256
PIECE = 128
VMEM_BYTES = 56 * 1024 * 1024
LOG2E = math.log2(math.e)
LOW = jnp.bfloat16
F32 = jnp.float32
ALL_AXES = ("dp", "context", "expert")
GROUP_AXES = ("dp", "context")


def dot_nn(a, b):
    return lax.dot_general(a, b, (((1,), (0,)), ((), ())), preferred_element_type=F32)


def dot_nt(a, b):
    return lax.dot_general(a, b, (((1,), (1,)), ((), ())), preferred_element_type=F32)


def dot_tn(a, b):
    return lax.dot_general(a, b, (((0,), (0,)), ((), ())), preferred_element_type=F32)


def params(**more):
    return pltpu.CompilerParams(vmem_limit_bytes=VMEM_BYTES, **more)


def cost(flops, nbytes, exps=0):
    return pl.CostEstimate(flops=int(flops), bytes_accessed=int(nbytes), transcendentals=int(exps))


def head_forward(u, gain, cos2, sin2):
    rr = lax.rsqrt(jnp.mean(u * u, axis=-1, keepdims=True) + EPS)
    y = u * rr * gain
    return y * cos2 + pltpu.roll(y, 64, 1) * sin2


def head_backward(gy, u, gain, cos2, sin2):
    g = gy * cos2 - pltpu.roll(gy, 64, 1) * sin2
    rr = lax.rsqrt(jnp.mean(u * u, axis=-1, keepdims=True) + EPS)
    n = u * rr
    gn = g * gain
    grad = rr * (gn - n * jnp.mean(gn * n, axis=-1, keepdims=True))
    return grad, jnp.sum(g * n, axis=0, keepdims=True)


def query_kernel(x_ref, w_ref, gain_ref, cos_ref, sin_ref, rot_ref, proj_ref):
    tiles, heads, rows, size = rot_ref.shape
    acc = dot_nn(x_ref[...], w_ref[...])
    for h in range(heads):
        u = acc[:, h * size : (h + 1) * size]
        rot = head_forward(u, gain_ref[...], cos_ref[...], sin_ref[...])
        proj_ref[:, h] = u.reshape(tiles, rows, size)
        rot_ref[:, h] = rot.astype(LOW).reshape(tiles, rows, size)


def project_queries(normed, weight, gain, cos2, sin2):
    block, width = normed.shape
    size = cos2.shape[1]
    heads = weight.shape[1] // size
    tiles = block // TILE
    whole = lambda i: (0, 0)
    per = lambda i: (0, i, 0, 0)
    shape = (tiles, heads, TILE, size)
    return pl.pallas_call(
        query_kernel,
        grid=(heads // 2,),
        in_specs=[
            pl.BlockSpec((block, width), whole),
            pl.BlockSpec((width, 2 * size), lambda i: (0, i)),
            pl.BlockSpec((1, size), whole),
            pl.BlockSpec((block, size), whole),
            pl.BlockSpec((block, size), whole),
        ],
        out_specs=[pl.BlockSpec((tiles, 2, TILE, size), per)] * 2,
        out_shape=[jax.ShapeDtypeStruct(shape, LOW), jax.ShapeDtypeStruct(shape, F32)],
        compiler_params=params(),
        cost_estimate=cost(2 * block * width * heads * size, 12e6),
    )(normed, weight, gain[None], cos2, sin2)


def put_in_order(place, refs, out_ref):
    n = (len(refs) + 1) // 2
    rows = refs[0].shape[0]
    for distance in range(1 - n, n):
        ref = refs[distance + n - 1]
        at = place + distance

        @pl.when(jnp.logical_and(at >= 0, at < n))
        def _():
            out_ref[pl.ds(pl.multiple_of(at * rows, rows), rows), :] = ref[...]


def chunk_list(found):
    n = (len(found) + 1) // 2
    return [found[distance] for distance in range(1 - n, n)]


def key_kernel(factor, n_chunks, place_ref, *refs):
    w_ref, gain_ref, cos_ref, sin_ref, g_ref, mask_ref = refs[n_chunks:-4]
    rows_ref, kv_ref, proj_ref, wide_ref = refs[-4:]
    size = proj_ref.shape[1]
    width = g_ref.shape[1]
    put_in_order(place_ref[0], refs[:n_chunks], rows_ref)
    wide_ref[:, :width] = g_ref[...]
    wide_ref[:, width:] = mask_ref[...].astype(LOW)
    acc = dot_nn(rows_ref[...], w_ref[...])
    u = acc[:, :size]
    rot = head_forward(u, gain_ref[...], cos_ref[...], sin_ref[...])
    proj_ref[...] = u
    kv_ref[:, :size] = (rot * factor).astype(LOW)
    kv_ref[:, size:] = acc[:, size:].astype(LOW)


def full(shape):
    return pl.BlockSpec(shape, lambda *_: (0,) * len(shape))


def project_keys(place, found, weight, gain, cos2, sin2, factor, g, mask):
    chunks = chunk_list(found)
    rows, width = chunks[0].shape
    block, size = cos2.shape
    operands = [*chunks, weight, gain[None], cos2, sin2, g, mask]
    shapes = [
        jax.ShapeDtypeStruct((block, width), LOW),
        jax.ShapeDtypeStruct((block, 2 * size), LOW),
        jax.ShapeDtypeStruct((block, size), F32),
        jax.ShapeDtypeStruct((rows, width + mask.shape[1]), LOW),
    ]
    return pl.pallas_call(
        functools.partial(key_kernel, factor, len(chunks)),
        grid_spec=pltpu.PrefetchScalarGridSpec(
            num_scalar_prefetch=1,
            grid=(1,),
            in_specs=[full(x.shape) for x in operands],
            out_specs=[full(x.shape) for x in shapes],
        ),
        out_shape=shapes,
        compiler_params=params(),
        cost_estimate=cost(4 * block * width * size, 8e6),
    )(place, *operands)


def in_order(last, step):
    lax.fori_loop(0, lax.div(last, 2), lambda p, c: (step([2 * p, 2 * p + 1], False), c)[1], 0)

    @pl.when(lax.rem(last, 2) == 1)
    def _():
        step([last - 1, last], True)

    @pl.when(lax.rem(last, 2) == 0)
    def _():
        step([last], True)


def attend_kernel(qpos_ref, kidx_ref, q_ref, kv_ref, *rest):
    out_ref, inv_ref, acc_ref = rest[-3:]
    heads, rows, size = q_ref.shape[1:]
    acc_ref[...] = jnp.zeros_like(acc_ref)

    def step(places, masked):
        starts = [pl.multiple_of(kidx_ref[place] * rows, rows) for place in places]
        count = len(places) * rows
        keys = jnp.concatenate([kv_ref[pl.ds(start, rows), :size] for start in starts], axis=0)
        values = jnp.concatenate([kv_ref[pl.ds(start, rows), size:] for start in starts], axis=0)
        values = jnp.concatenate([values, jnp.ones((count, size), LOW)], axis=1)
        for h in range(heads):
            for first in range(0, rows, PIECE):
                part = slice(first, first + PIECE)
                e = jnp.exp2(dot_nt(q_ref[0, h, part], keys))
                if masked:
                    qi = lax.broadcasted_iota(jnp.int32, e.shape, 0) + first
                    ki = lax.broadcasted_iota(jnp.int32, e.shape, 1) - (count - rows)
                    e = jnp.where(ki <= qi, e, 0.0)
                acc_ref[h, part] += dot_nn(e.astype(LOW), values)

    in_order(qpos_ref[pl.program_id(0)], step)
    for h in range(heads):
        inv = 1.0 / acc_ref[h, :, size:]
        inv_ref[0, h] = inv
        out_ref[:, h * size : (h + 1) * size] = (acc_ref[h, :, :size] * inv).astype(LOW)


def attend(qpos, kidx, queries, kv, others):
    tiles, heads, rows, size = queries.shape
    seq = kv.shape[0]
    return pl.pallas_call(
        attend_kernel,
        grid_spec=pltpu.PrefetchScalarGridSpec(
            num_scalar_prefetch=2,
            grid=(tiles,),
            in_specs=[
                pl.BlockSpec((1, heads, rows, size), lambda i, a, b: (i, 0, 0, 0)),
                pl.BlockSpec((seq, 2 * size), lambda i, a, b: (0, 0)),
            ]
            + [pl.BlockSpec(memory_space=pl.ANY)] * len(others),
            out_specs=[
                pl.BlockSpec((rows, heads * size), lambda i, a, b: (i, 0)),
                pl.BlockSpec((1, heads, rows, size), lambda i, a, b: (i, 0, 0, 0)),
            ],
            scratch_shapes=[pltpu.VMEM((heads, rows, 2 * size), F32)],
        ),
        out_shape=[
            jax.ShapeDtypeStruct((tiles * rows, heads * size), LOW),
            jax.ShapeDtypeStruct((tiles, heads, rows, size), F32),
        ],
        compiler_params=params(),
        cost_estimate=cost(
            6 * tiles * rows * heads * seq * size, 8e6, tiles * rows * heads * seq
        ),
    )(qpos, kidx, queries, kv, *others)


def grad_out_kernel(rows_ref, w_ref, o_ref, inv_ref, *rest):
    do_ref, centre_ref = rest[-2:]
    tiles, heads, rows, size = do_ref.shape
    acc = dot_nt(rows_ref[...], w_ref[...])
    for t in range(tiles):
        for h in range(heads):
            part = slice(t * rows, (t + 1) * rows), slice(h * size, (h + 1) * size)
            low = (acc[part] * inv_ref[t, h]).astype(LOW)
            do_ref[t, h] = low
            product = low.astype(F32) * o_ref[part].astype(F32)
            centre = jnp.sum(jnp.transpose(product), axis=0, keepdims=True)
            centre_ref[t, h] = jnp.broadcast_to(centre, (8, rows))


def grad_attended(grad_rows, weight, attended, inverse, others):
    tiles, heads, rows, size = inverse.shape
    block, width = grad_rows.shape
    return pl.pallas_call(
        grad_out_kernel,
        grid=(heads // 2,),
        in_specs=[
            pl.BlockSpec((block, width), lambda i: (0, 0)),
            pl.BlockSpec((2 * size, width), lambda i: (i, 0)),
            pl.BlockSpec((block, 2 * size), lambda i: (0, i)),
            pl.BlockSpec((tiles, 2, rows, size), lambda i: (0, i, 0, 0)),
        ]
        + [pl.BlockSpec(memory_space=pl.ANY)] * len(others),
        out_specs=[
            pl.BlockSpec((tiles, 2, rows, size), lambda i: (0, i, 0, 0)),
            pl.BlockSpec((tiles, 2, 8, rows), lambda i: (0, i, 0, 0)),
        ],
        out_shape=[
            jax.ShapeDtypeStruct((tiles, heads, rows, size), LOW),
            jax.ShapeDtypeStruct((tiles, heads, 8, rows), F32),
        ],
        compiler_params=params(),
        cost_estimate=cost(2 * block * width * heads * size, 12e6),
    )(grad_rows, weight, attended, inverse, *others)


def attend_back_kernel(
    qpos_ref,
    kidx_ref,
    q_ref,
    do_ref,
    centre_ref,
    kv_ref,
    proj_ref,
    gain_ref,
    cos_ref,
    sin_ref,
    *rest,
):
    dkv_ref, dq_ref, dgain_ref, acc_ref, e_ref, ds_ref = rest[-6:]
    heads, rows, size = q_ref.shape[1:]

    @pl.when(pl.program_id(0) == 0)
    def _():
        dkv_ref[...] = jnp.zeros_like(dkv_ref)
        dgain_ref[...] = jnp.zeros_like(dgain_ref)

    acc_ref[...] = jnp.zeros_like(acc_ref)

    def step(places, masked):
        starts = [pl.multiple_of(kidx_ref[place] * rows, rows) for place in places]
        count = len(places) * rows
        keys = jnp.concatenate([kv_ref[pl.ds(start, rows), :size] for start in starts], axis=0)
        values = jnp.concatenate([kv_ref[pl.ds(start, rows), size:] for start in starts], axis=0)
        for h in range(heads):
            query, grad = q_ref[0, h], do_ref[0, h]
            centre = centre_ref[0, h, 0:1]
            columns = slice(h * rows, (h + 1) * rows)
            for first in range(0, count, PIECE):
                part = slice(first, first + PIECE)
                e = jnp.exp2(dot_nt(keys[part], query))
                if masked and first >= count - rows:
                    ki = lax.broadcasted_iota(jnp.int32, e.shape, 0) + (first - (count - rows))
                    qi = lax.broadcasted_iota(jnp.int32, e.shape, 1)
                    e = jnp.where(ki <= qi, e, 0.0)
                ds = e * (dot_nt(values[part], grad) - centre)
                e_ref[part, columns] = e.astype(LOW)
                ds_ref[part, columns] = ds.astype(LOW)
            acc_ref[h] += dot_tn(ds_ref[:count, columns], keys)
        dk = dot_nn(ds_ref[:count], q_ref[0].reshape(heads * rows, size))
        dv = dot_nn(e_ref[:count], do_ref[0].reshape(heads * rows, size))
        for k, start in enumerate(starts):
            dkv_ref[pl.ds(start, rows), :size] += dk[k * rows : (k + 1) * rows]
            dkv_ref[pl.ds(start, rows), size:] += dv[k * rows : (k + 1) * rows]

    in_order(qpos_ref[pl.program_id(0)], step)
    total = jnp.zeros((1, size), F32)
    for h in range(heads):
        grad, gain_part = head_backward(
            acc_ref[h] * (1.0 / LOG2E), proj_ref[0, h], gain_ref[...], cos_ref[...], sin_ref[...]
        )
        dq_ref[:, h * size : (h + 1) * size] = grad.astype(LOW)
        total += gain_part
    dgain_ref[...] += total


def attend_back(qpos, kidx, queries, grads, centre, kv, proj, gain, cos2, sin2, others):
    tiles, heads, rows, size = queries.shape
    seq = kv.shape[0]
    per = pl.BlockSpec((1, heads, rows, size), lambda i, a, b: (i, 0, 0, 0))
    flat = lambda i, a, b: (0, 0)
    rowwise = lambda i, a, b: (i, 0)
    return pl.pallas_call(
        attend_back_kernel,
        grid_spec=pltpu.PrefetchScalarGridSpec(
            num_scalar_prefetch=2,
            grid=(tiles,),
            in_specs=[
                per,
                per,
                pl.BlockSpec((1, heads, 8, rows), lambda i, a, b: (i, 0, 0, 0)),
                pl.BlockSpec((seq, 2 * size), flat),
                per,
                pl.BlockSpec((1, size), flat),
                pl.BlockSpec((rows, size), rowwise),
                pl.BlockSpec((rows, size), rowwise),
            ]
            + [pl.BlockSpec(memory_space=pl.ANY)] * len(others),
            out_specs=[
                pl.BlockSpec((seq, 2 * size), flat),
                pl.BlockSpec((rows, heads * size), rowwise),
                pl.BlockSpec((1, size), flat),
            ],
            scratch_shapes=[pltpu.VMEM((heads, rows, size), F32)]
            + [pltpu.VMEM((2 * rows, heads * rows), LOW)] * 2,
        ),
        out_shape=[
            jax.ShapeDtypeStruct((seq, 2 * size), F32),
            jax.ShapeDtypeStruct((tiles * rows, heads * size), LOW),
            jax.ShapeDtypeStruct((1, size), F32),
        ],
        compiler_params=params(),
        cost_estimate=cost(
            15 * tiles * rows * heads * seq * size, 12e6, tiles * rows * heads * seq
        ),
    )(qpos, kidx, queries, grads, centre, kv, proj, gain[None], cos2, sin2, *others)


def out_kernel(a_ref, b_ref, *rest):
    rest[-1][...] = dot_nn(a_ref[...], b_ref[...]).astype(LOW)


def out_dot(a, b, others):
    block, inner = a.shape
    columns = b.shape[1]
    tile = min(columns, 512)
    return pl.pallas_call(
        out_kernel,
        grid=(columns // tile,),
        in_specs=[
            pl.BlockSpec((block, inner), lambda i: (0, 0)),
            pl.BlockSpec((inner, tile), lambda i: (0, i)),
        ]
        + [pl.BlockSpec(memory_space=pl.ANY)] * len(others),
        out_specs=pl.BlockSpec((block, tile), lambda i: (0, i)),
        out_shape=jax.ShapeDtypeStruct((block, columns), LOW),
        compiler_params=params(),
        cost_estimate=cost(2 * block * inner * columns, 8e6),
    )(a, b, *others)


def token_kernel(a_ref, b_ref, *rest):
    rest[-1][...] = dot_tn(a_ref[...], b_ref[...]).astype(LOW)


def token_dot(a, b, others):
    block, rows = a.shape
    columns = b.shape[1]
    tile = min(rows, 512)
    return pl.pallas_call(
        token_kernel,
        grid=(rows // tile,),
        in_specs=[
            pl.BlockSpec((block, tile), lambda i: (0, i)),
            pl.BlockSpec((block, columns), lambda i: (0, 0)),
        ]
        + [pl.BlockSpec(memory_space=pl.ANY)] * len(others),
        out_specs=pl.BlockSpec((tile, columns), lambda i: (i, 0)),
        out_shape=jax.ShapeDtypeStruct((rows, columns), LOW),
        compiler_params=params(),
        cost_estimate=cost(2 * block * rows * columns, 6e6),
    )(a, b, *others)


def split_low(value):
    high = value.astype(LOW)
    return high, (value - high.astype(F32)).astype(LOW)


def norm_parts(rows):
    rr = lax.rsqrt(jnp.mean(rows * rows, axis=-1, keepdims=True) + EPS)
    return rows * rr, rr


def norm_back(grad, normal, rr, gain):
    weighted = grad * gain
    return rr * (weighted - normal * jnp.mean(weighted * normal, axis=-1, keepdims=True))


def add_all(refs):
    return functools.reduce(jnp.add, [ref[...].astype(F32) for ref in refs])


def pad_rows(rows, count):
    if rows.shape[0] == count:
        return rows
    return jnp.concatenate(
        [rows, jnp.zeros((count - rows.shape[0], rows.shape[1]), rows.dtype)], axis=0
    )


def router_kernel(experts, *refs):
    x_ref, attn_ref, gain_ref, router_ref, mask_ref = refs[:5]
    hidden_ref, mixed_ref, probs_ref = refs[-3:]
    width = x_ref.shape[1]
    lanes = mask_ref.shape[1]
    hidden = add_all([x_ref, attn_ref])
    hidden_ref[...] = hidden
    mixed = (norm_parts(hidden)[0] * gain_ref[...]).astype(LOW)
    mixed_ref[:, :width] = mixed
    logits = dot_nt(mixed, pad_rows(router_ref[...], lanes))
    lane = lax.broadcasted_iota(jnp.int32, logits.shape, 1)
    logits = jnp.where(lane < experts, logits, -1e30)
    weights = jnp.exp(logits - jnp.max(logits, axis=1, keepdims=True))
    probs = weights / jnp.sum(weights, axis=1, keepdims=True)
    probs_ref[...] = probs
    chosen = probs * mask_ref[...]
    high, low = split_low(chosen / jnp.sum(chosen, axis=1, keepdims=True))
    both = high.astype(F32) + pltpu.roll(low.astype(F32), experts, 1)
    mixed_ref[:, width:] = both.astype(LOW)


def route_rows(x, attn, gain, router, mask, experts, others):
    tokens, width = x.shape
    lanes = mask.shape[1]
    operands = [x, attn, gain[None], router, mask]
    shapes = [
        jax.ShapeDtypeStruct((tokens, width), F32),
        jax.ShapeDtypeStruct((tokens, width + lanes), LOW),
        jax.ShapeDtypeStruct((tokens, lanes), F32),
    ]
    return pl.pallas_call(
        functools.partial(router_kernel, experts),
        grid=(1,),
        in_specs=[full(value.shape) for value in operands]
        + [pl.BlockSpec(memory_space=pl.ANY)] * len(others),
        out_specs=[full(shape.shape) for shape in shapes],
        out_shape=shapes,
        compiler_params=params(),
        cost_estimate=cost(2 * tokens * width * lanes, 5e6),
    )(*operands, *others)


def table_kernel(capacity, n_half, meta_ref, col_ref, *rest):
    rows_ref, near_ref, far_ref, near_back_ref, far_back_ref, slots_ref = rest[-6:]
    block = col_ref.shape[0]
    rows, width = rows_ref.shape
    n = 2 * n_half
    tokens = block // n
    cap_half = n_half * capacity
    groups = rows // (2 * cap_half)
    mask = col_ref[:, width:]
    lanes = mask.shape[1]
    padded = -(-groups // 16) * 16
    group = lax.broadcasted_iota(jnp.int32, (padded, lanes), 0)
    lane = lax.broadcasted_iota(jnp.int32, (padded, lanes), 1)
    wanted = jnp.logical_and(lane == group * n + meta_ref[0], group < groups)
    hits = dot_nt(jnp.where(wanted, 1.0, 0.0).astype(LOW), mask)
    before = lax.broadcasted_iota(jnp.int32, (tokens, tokens), 0)
    after_it = lax.broadcasted_iota(jnp.int32, (tokens, tokens), 1)
    earlier = jnp.where(before < after_it, 1.0, 0.0).astype(LOW)
    for z in range(n):
        hit = hits[:, z * tokens : (z + 1) * tokens]
        rank = dot_nn(hit.astype(LOW), earlier)
        turn = (meta_ref[1 + z] * capacity).astype(F32)
        slot = jnp.where(hit > 0.5, rank + turn, -1.0)
        slots_ref[:, z * tokens : (z + 1) * tokens] = slot[:groups]

    def one_hot(slots, count, first):
        slot = lax.broadcasted_iota(jnp.int32, (groups, count, slots.shape[1]), 1).astype(F32)
        same = slots[:, None, :] == slot + float(first)
        return jnp.where(same, 1.0, 0.0).reshape(groups * count, slots.shape[1])

    spread = one_hot(slots_ref[...], 2 * cap_half, 0).astype(LOW)
    rows_ref[...] = dot_nn(spread, col_ref[:, :width]).astype(LOW)
    for part, (to_ref, back_ref) in enumerate([(near_ref, near_back_ref), (far_ref, far_back_ref)]):
        pieces = []
        for k in range(n_half):
            start = pl.multiple_of(meta_ref[1 + n + part * n_half + k] * tokens, tokens)
            pieces.append(slots_ref[:, pl.ds(start, tokens)])
        spread = one_hot(jnp.concatenate(pieces, axis=1), cap_half, part * cap_half)
        to_ref[...] = spread.astype(LOW)
        back_ref[...] = jnp.transpose(spread).astype(LOW)


def make_tables(meta, col, width, groups, n_half, capacity, others):
    block = col.shape[0]
    rows = groups * n_half * capacity
    shapes = (
        [jax.ShapeDtypeStruct((2 * rows, width), LOW)]
        + [jax.ShapeDtypeStruct((rows, block // 2), LOW)] * 2
        + [jax.ShapeDtypeStruct((block // 2, rows), LOW)] * 2
    )
    outs = pl.pallas_call(
        functools.partial(table_kernel, capacity, n_half),
        grid_spec=pltpu.PrefetchScalarGridSpec(
            num_scalar_prefetch=1,
            grid=(1,),
            in_specs=[full(col.shape)] + [pl.BlockSpec(memory_space=pl.ANY)] * len(others),
            out_specs=[full(shape.shape) for shape in shapes],
            scratch_shapes=[pltpu.VMEM((groups, block), F32)],
        ),
        out_shape=shapes,
        compiler_params=params(),
        cost_estimate=cost(4 * rows * block * width, 12e6),
    )(meta, col, *others)
    return outs[0], outs[1:3], outs[3:]


def spread_kernel(choices, place_ref, spread_ref, *refs):
    out_ref, rows_ref = refs[-2:]
    for k, by_place in enumerate(choices):
        for which in sorted(set(by_place)):
            hit = functools.reduce(
                jnp.logical_or,
                [place_ref[0] == i for i, other in enumerate(by_place) if other == which],
            )

            @pl.when(hit)
            def _():
                tokens = refs[which].shape[0]
                rows_ref[k * tokens : (k + 1) * tokens] = refs[which][...]

    out_ref[...] = dot_nn(spread_ref[...], rows_ref[...]).astype(LOW)


def spread_rows(place, spread, found, turns, others):
    n = lax.axis_size("expert")
    order = arrival_order(n)
    distances = sorted({order[i][turn] - i for i in range(n) for turn in turns})
    choices = [[distances.index(order[i][turn] - i) for i in range(n)] for turn in turns]
    chunks = [found[distance] for distance in distances]
    tokens, wide = chunks[0].shape
    rows = spread.shape[0]
    return pl.pallas_call(
        functools.partial(spread_kernel, choices),
        grid_spec=pltpu.PrefetchScalarGridSpec(
            num_scalar_prefetch=1,
            grid=(1,),
            in_specs=[full(spread.shape)]
            + [full(chunk.shape) for chunk in chunks]
            + [pl.BlockSpec(memory_space=pl.ANY)] * len(others),
            out_specs=full((rows, wide)),
            scratch_shapes=[pltpu.VMEM((len(turns) * tokens, wide), LOW)],
        ),
        out_shape=jax.ShapeDtypeStruct((rows, wide), LOW),
        compiler_params=params(),
        cost_estimate=cost(2 * rows * len(turns) * tokens * wide, 5e6),
    )(place, spread, *chunks, *others)


def router_back_kernel(experts, *refs):
    sum_ref, g_ref, hidden_ref, gain_ref, router_ref, mask_ref, probs_ref = refs[:7]
    grad_ref, low_ref, dgain_ref, drouter_ref = refs[-4:]
    width = g_ref.shape[1]
    lanes = mask_ref.shape[1]
    total = sum_ref[...].astype(F32)
    table = total[:, width:]
    mask, probs = mask_ref[...], probs_ref[...]
    grad_gates = (table + pltpu.roll(table, lanes - experts, 1)) * mask
    chosen = probs * mask
    chosen_sum = jnp.sum(chosen, axis=1, keepdims=True)
    mean = jnp.sum(grad_gates * (chosen / chosen_sum), axis=1, keepdims=True)
    centred = mask * (grad_gates - mean) / chosen_sum
    grad_logits = probs * (centred - jnp.sum(centred * chosen, axis=1, keepdims=True))
    high, low = split_low(grad_logits)
    router = pad_rows(router_ref[...], lanes)
    grad = total[:, :width] + dot_nn(high, router) + dot_nn(low, router)
    normal, rr = norm_parts(hidden_ref[...])
    mixed = (normal * gain_ref[...]).astype(LOW)
    drouter_ref[...] = dot_tn(high, mixed) + dot_tn(low, mixed)
    dgain_ref[...] = jnp.sum(grad * normal, axis=0, keepdims=True)
    grad_hidden = g_ref[...].astype(F32) + norm_back(grad, normal, rr, gain_ref[...])
    grad_ref[...] = grad_hidden
    low_ref[...] = grad_hidden.astype(LOW)


def route_back(summed, g, hidden, gain, router, mask, probs, experts, others):
    tokens, width = g.shape
    lanes = mask.shape[1]
    operands = [summed, g, hidden, gain[None], router, mask, probs]
    shapes = [
        jax.ShapeDtypeStruct((tokens, width), F32),
        jax.ShapeDtypeStruct((tokens, width), LOW),
        jax.ShapeDtypeStruct((1, width), F32),
        jax.ShapeDtypeStruct((lanes, width), F32),
    ]
    return pl.pallas_call(
        functools.partial(router_back_kernel, experts),
        grid=(1,),
        in_specs=[full(value.shape) for value in operands]
        + [pl.BlockSpec(memory_space=pl.ANY)] * len(others),
        out_specs=[full(shape.shape) for shape in shapes],
        out_shape=shapes,
        compiler_params=params(),
        cost_estimate=cost(8 * tokens * width * lanes, 8e6),
    )(*operands, *others)


def combine_kernel(n_half, meta_ref, near_table_ref, far_table_ref, near_ref, far_ref, *rest):
    del meta_ref
    turn = pl.program_id(0)

    @pl.when(turn < n_half)
    def _():
        rest[-1][...] = dot_nn(near_table_ref[...], near_ref[...]).astype(LOW)

    @pl.when(turn >= n_half)
    def _():
        rest[-1][...] = dot_nn(far_table_ref[...], far_ref[...]).astype(LOW)


def combine_rows(meta, tables, rows, n_half, others):
    tokens = tables[0].shape[0] // n_half
    slots, wide = rows[0].shape
    n = 2 * n_half
    return pl.pallas_call(
        functools.partial(combine_kernel, n_half),
        grid_spec=pltpu.PrefetchScalarGridSpec(
            num_scalar_prefetch=1,
            grid=(n,),
            in_specs=[
                pl.BlockSpec((tokens, slots), lambda i, m: (jnp.minimum(i, n_half - 1), 0)),
                pl.BlockSpec((tokens, slots), lambda i, m: (jnp.maximum(i - n_half, 0), 0)),
            ]
            + [full(value.shape) for value in rows]
            + [pl.BlockSpec(memory_space=pl.ANY)] * len(others),
            out_specs=pl.BlockSpec((tokens, wide), lambda i, m: (m[1 + n + i], 0)),
        ),
        out_shape=jax.ShapeDtypeStruct((n * tokens, wide), LOW),
        compiler_params=params(),
        cost_estimate=cost(2 * slots * n * tokens * wide, 10e6),
    )(meta, *tables, *rows, *others)


def expert_kernel(experts, who_ref, x_ref, gate_ref, up_ref, pull_ref, *rest):
    act_ref, dgate_ref, dup_ref, copy_ref = rest[-4:]
    width = gate_ref.shape[0]
    x = x_ref[:, :width]
    table = x_ref[:, width:].astype(F32)
    lane = lax.broadcasted_iota(jnp.int32, table.shape, 1)
    mine = who_ref[0]
    gate = jnp.sum(
        jnp.where(jnp.logical_or(lane == mine, lane == mine + experts), table, 0.0),
        axis=1,
        keepdims=True,
    )
    pre_gate = dot_nn(x, gate_ref[...])
    pre_up = dot_nn(x, up_ref[...])
    pull = pull_ref[...].reshape(pre_up.shape)
    sig = 1.0 / (1.0 + jnp.exp(-pre_gate))
    silu = pre_gate * sig
    act = silu * pre_up
    act_ref[...] = (act * gate).astype(LOW)
    high, low = split_low(jnp.sum(act * pull, axis=1, keepdims=True))
    pull = pull * gate
    dup = (pull * silu).astype(LOW)
    dgate = (pull * pre_up * (sig * (1.0 + pre_gate * (1.0 - sig)))).astype(LOW)
    dgate_ref[...] = dgate
    dup_ref[...] = dup
    copy_ref[:, :width] = (dot_nt(dgate, gate_ref[...]) + dot_nt(dup, up_ref[...])).astype(LOW)
    back = jnp.where(lane == mine, high.astype(F32), 0.0)
    back = jnp.where(lane == mine + experts, low.astype(F32), back)
    copy_ref[:, width:] = back.astype(LOW)


def run_expert(who, x, w_gate, w_up, pull, part, experts):
    rows, wide = x.shape
    width, hidden = w_gate.shape
    groups, _, slots, _ = pull.shape
    each = groups // 2
    tile = each * slots
    by_rows = lambda columns: pl.BlockSpec((tile, columns), lambda i, p: (i, 0))
    return pl.pallas_call(
        functools.partial(expert_kernel, experts),
        grid_spec=pltpu.PrefetchScalarGridSpec(
            num_scalar_prefetch=1,
            grid=(2,),
            in_specs=[
                by_rows(wide),
                full(w_gate.shape),
                full(w_up.shape),
                pl.BlockSpec((each, 1, slots, hidden), lambda i, p: (i, part, 0, 0)),
            ],
            out_specs=[by_rows(hidden), by_rows(hidden), by_rows(hidden), by_rows(wide)],
        ),
        out_shape=[jax.ShapeDtypeStruct((rows, hidden), LOW)] * 3
        + [jax.ShapeDtypeStruct((rows, wide), LOW)],
        compiler_params=params(),
        cost_estimate=cost(8 * rows * width * hidden, 20e6, rows * hidden),
    )(who, x, w_gate, w_up, pull)


def input_kernel(grad_ref, x_ref, gain_ref, more_ref, out_ref):
    normal, rr = norm_parts(x_ref[...].astype(F32))
    grad = grad_ref[...].astype(F32)
    out_ref[...] = more_ref[...] + norm_back(grad, normal, rr, gain_ref[...])


def input_back(grad, x, gain, more):
    tokens, width = x.shape
    operands = [grad, x, gain[None], more]
    return pl.pallas_call(
        input_kernel,
        grid=(1,),
        in_specs=[full(value.shape) for value in operands],
        out_specs=full(more.shape),
        out_shape=jax.ShapeDtypeStruct((tokens, width), F32),
        compiler_params=params(),
        cost_estimate=cost(20 * tokens * width, 5e6),
    )(*operands)


def kv_back_kernel(factor, n_parts, c_ref, dkv_ref, *refs):
    parts = refs[:n_parts]
    proj_ref, gain_ref, cos_ref, sin_ref = refs[n_parts : n_parts + 4]
    grad_ref, dgain_ref = refs[-2:]
    size = proj_ref.shape[1]
    total = functools.reduce(jnp.add, [part[...].astype(F32) for part in parts], dkv_ref[...])
    grad, dgain = head_backward(
        total[:, :size] * factor, proj_ref[...], gain_ref[...], cos_ref[...], sin_ref[...]
    )
    grad_ref[:, :size] = grad.astype(LOW)
    grad_ref[:, size:] = total[:, size:].astype(LOW)
    dgain_ref[...] = dgain


def kv_back(context, dkv, parts, proj, gain, cos2, sin2, factor, others):
    block, size = proj.shape
    operands = [proj, gain[None], cos2, sin2]
    shapes = [
        jax.ShapeDtypeStruct((block, 2 * size), LOW),
        jax.ShapeDtypeStruct((1, size), F32),
    ]
    return pl.pallas_call(
        functools.partial(kv_back_kernel, factor, len(parts)),
        grid_spec=pltpu.PrefetchScalarGridSpec(
            num_scalar_prefetch=1,
            grid=(1,),
            in_specs=[pl.BlockSpec((block, 2 * size), lambda i, c: (c[0], 0))]
            + [full(part.shape) for part in parts]
            + [full(value.shape) for value in operands]
            + [pl.BlockSpec(memory_space=pl.ANY)] * len(others),
            out_specs=[full(shape.shape) for shape in shapes],
        ),
        out_shape=shapes,
        compiler_params=params(),
        cost_estimate=cost(40 * block * size, 5e6),
    )(context.astype(jnp.int32)[None], dkv, *parts, *operands, *others)


def pair_kernel(a_ref, b_ref, *rest):
    rest[-1][...] = (a_ref[...].astype(F32) + b_ref[...].astype(F32)).astype(LOW)


def pair_sum(a, b, others):
    rows, columns = a.shape
    tiles = 2
    spec = pl.BlockSpec((rows // tiles, columns), lambda i: (i, 0))
    return pl.pallas_call(
        pair_kernel,
        grid=(tiles,),
        in_specs=[spec, spec] + [pl.BlockSpec(memory_space=pl.ANY)] * len(others),
        out_specs=spec,
        out_shape=jax.ShapeDtypeStruct((rows, columns), LOW),
        compiler_params=params(),
        cost_estimate=cost(rows * columns, 6 * rows * columns),
    )(a, b, *others)


def fold_kernel(n_pairs, s_ref, *refs):
    del s_ref
    send_ref, keep_ref = refs[-2:]
    totals = [
        (refs[2 * k][...].astype(F32) + refs[2 * k + 1][...].astype(F32)).astype(LOW)
        for k in range(n_pairs)
    ]
    for half, out_ref in enumerate((send_ref, keep_ref)):

        @pl.when(pl.program_id(0) == half)
        def _():
            first = 0
            for total in totals:
                last = first + total.shape[1]
                out_ref[:, first:last] = total
                first = last


def fold(pairs, base, bit, others):
    rows = pairs[0][1].shape[0]
    columns = sum(got.shape[1] for _, got in pairs)
    tiles = 2
    tile = rows // (2 * tiles)
    side = lambda h, m: (1 - m[1]) * (1 - h) + m[1] * h
    specs = []
    for _, got in pairs:
        wide = got.shape[1]
        specs.append(
            pl.BlockSpec(
                (tile, wide), lambda h, j, m: (m[0] * 2 * tiles + side(h, m) * tiles + j, 0)
            )
        )
        specs.append(pl.BlockSpec((tile, wide), lambda h, j, m: (side(h, m) * tiles + j, 0)))
    shape = jax.ShapeDtypeStruct((rows // 2, columns), LOW)
    return pl.pallas_call(
        functools.partial(fold_kernel, len(pairs)),
        grid_spec=pltpu.PrefetchScalarGridSpec(
            num_scalar_prefetch=1,
            grid=(2, tiles),
            in_specs=specs + [pl.BlockSpec(memory_space=pl.ANY)] * len(others),
            out_specs=[
                pl.BlockSpec((tile, columns), lambda h, j, m: (j * (1 - h) + (tiles - 1) * h, 0)),
                pl.BlockSpec((tile, columns), lambda h, j, m: (j * h, 0)),
            ],
        ),
        out_shape=[shape, shape],
        compiler_params=params(),
        cost_estimate=cost(rows * columns, 6 * rows * columns),
    )(
        jnp.stack([base, bit]).astype(jnp.int32),
        *[value for pair in pairs for value in pair],
        *others,
    )


def normed_kernel(q_ref, kv_ref, wq_ref, wkv_ref, rows_ref, *rest):
    out_ref, dgain_ref = rest[-2:]
    grad = dot_nt(q_ref[...], wq_ref[...]) + dot_nt(kv_ref[...], wkv_ref[...])
    out_ref[...] = grad.astype(LOW)
    dgain_ref[...] = jnp.sum(grad * rows_ref[...].astype(F32), axis=0, keepdims=True)


def normed_back(grad_q, grad_kv, w_q, w_kv, rows, others):
    block, width = rows.shape
    tile = 512
    column = lambda i: (0, i)
    return pl.pallas_call(
        normed_kernel,
        grid=(width // tile,),
        in_specs=[
            full(grad_q.shape),
            full(grad_kv.shape),
            pl.BlockSpec((tile, w_q.shape[1]), lambda i: (i, 0)),
            pl.BlockSpec((tile, w_kv.shape[1]), lambda i: (i, 0)),
            pl.BlockSpec((block, tile), column),
        ]
        + [pl.BlockSpec(memory_space=pl.ANY)] * len(others),
        out_specs=[pl.BlockSpec((block, tile), column), pl.BlockSpec((1, tile), column)],
        out_shape=[
            jax.ShapeDtypeStruct((block, width), LOW),
            jax.ShapeDtypeStruct((1, width), F32),
        ],
        compiler_params=params(),
        cost_estimate=cost(2 * block * width * (w_q.shape[1] + w_kv.shape[1]), 12e6),
    )(grad_q, grad_kv, w_q, w_kv, rows, *others)


def pack_kernel(experts, router_ref, attn_ref, gain_ref, mlp_ref, q_ref, k_ref, *rest):
    out_ref, rows_ref = rest[-2:]
    size = q_ref.shape[1]
    rows_ref[:experts] = router_ref[:experts]
    rows_ref[experts:] = jnp.zeros_like(rows_ref[experts:])
    rows_ref[experts : experts + 1] = attn_ref[...] / gain_ref[...]
    rows_ref[experts + 1 : experts + 2] = mlp_ref[...]
    rows_ref[experts + 2 : experts + 3, :size] = q_ref[...]
    rows_ref[experts + 2 : experts + 3, size : 2 * size] = k_ref[...]
    out_ref[...] = rows_ref[...].astype(LOW)


def pack_small(experts, router, attn, gain, mlp, q, k, others):
    width = attn.shape[1]
    shape = (-(-(experts + 3) // 16) * 16, width)
    operands = [router, attn, gain[None], mlp, q, k]
    return pl.pallas_call(
        functools.partial(pack_kernel, experts),
        grid=(1,),
        in_specs=[full(value.shape) for value in operands]
        + [pl.BlockSpec(memory_space=pl.ANY)] * len(others),
        out_specs=full(shape),
        out_shape=jax.ShapeDtypeStruct(shape, LOW),
        scratch_shapes=[pltpu.VMEM(shape, F32)],
        compiler_params=params(),
        cost_estimate=cost(shape[0] * width, 6 * shape[0] * width),
    )(*operands, *others)


def part_sum_kernel(parts_ref, *rest):
    total = parts_ref[0].astype(F32)
    for k in range(1, parts_ref.shape[0]):
        total += parts_ref[k].astype(F32)
    rest[-1][...] = total.astype(LOW)


def part_sum(parts, others):
    count, rows, columns = parts.shape
    tiles = 2
    return pl.pallas_call(
        part_sum_kernel,
        grid=(tiles,),
        in_specs=[pl.BlockSpec((count, rows // tiles, columns), lambda i: (0, i, 0))]
        + [pl.BlockSpec(memory_space=pl.ANY)] * len(others),
        out_specs=pl.BlockSpec((rows // tiles, columns), lambda i: (i, 0)),
        out_shape=jax.ShapeDtypeStruct((rows, columns), LOW),
        compiler_params=params(),
        cost_estimate=cost(count * rows * columns, 4 * count * rows * columns),
    )(parts, *others)


def widen_kernel(n_chunks, n_outs, at_ref, *refs):
    del at_ref
    outs = refs[-n_outs:]
    widths = [ref.shape[1] for ref in outs]
    for k in range(n_chunks):

        @pl.when(pl.program_id(0) == k)
        def _():
            first = 0
            for wide, out_ref in zip(widths, outs):
                out_ref[...] = refs[k][:, first : first + wide].astype(F32)
                first += wide


def widen(places, chunks, widths, others):
    rows, columns = chunks[0].shape
    count = len(chunks)
    return pl.pallas_call(
        functools.partial(widen_kernel, count, len(widths)),
        grid_spec=pltpu.PrefetchScalarGridSpec(
            num_scalar_prefetch=1,
            grid=(count,),
            in_specs=[full(chunk.shape) for chunk in chunks]
            + [pl.BlockSpec(memory_space=pl.ANY)] * len(others),
            out_specs=[pl.BlockSpec((rows, wide), lambda i, at: (at[i], 0)) for wide in widths],
        ),
        out_shape=[jax.ShapeDtypeStruct((count * rows, wide), F32) for wide in widths],
        compiler_params=params(),
        cost_estimate=cost(rows * columns, 6 * count * rows * columns),
    )(jnp.stack(places).astype(jnp.int32), *chunks, *others)


def sum_axis(total, axis):
    n = lax.axis_size(axis)
    s = 1
    while s < n:
        got = lax.ppermute(total.astype(LOW), axis, [(i, i ^ s) for i in range(n)])
        total = total.astype(F32) + got.astype(F32)
        s *= 2
    return total


def swap_dp(rows):
    return lax.ppermute(rows, "dp", [(0, 1), (1, 0)])


def swap_context(rows, s):
    n = lax.axis_size("context")
    return lax.ppermute(rows, "context", [(i, i ^ s) for i in range(n)])


def dp_got(grad):
    d = lax.axis_index("dp")
    rows = grad.shape[0] // 2
    return swap_dp(lax.dynamic_slice_in_dim(grad, (1 - d) * rows, rows))


def plane_turns():
    d, c = lax.axis_index("dp"), lax.axis_index("context")
    low, high = lax.rem(c, 2), lax.div(c, 2)

    def swap(first, second):
        perm = [(i, i ^ first) for i in range(4)] + [(4 + i, 4 + (i ^ second)) for i in range(4)]
        return lambda rows: lax.ppermute(rows, GROUP_AXES, perm)

    return [
        (jnp.where(d == 0, low, high), swap(1, 2)),
        (jnp.where(d == 0, high, low), swap(2, 1)),
    ]


def plane_first(pairs, others):
    (bit_1, _), _ = plane_turns()
    return fold(pairs, lax.axis_index("dp"), bit_1, others)


def plane_rest(send, keep, first, second):
    (_, swap_1), (bit_2, swap_2) = plane_turns()
    send, keep = fold([(keep, swap_1(send))], jnp.int32(0), bit_2, first)
    return pair_sum(keep, swap_2(send), second)


def plane_spread(own):
    (_, swap_1), (_, swap_2) = plane_turns()
    second = swap_2(own)
    return [own, second, swap_1(own), swap_1(second)]


def quarter_places():
    d = lax.axis_index("dp")
    c = lax.axis_index("context")
    low, high = lax.rem(c, 2), lax.div(c, 2)
    places = []
    for core in (d, 1 - d):
        bit_1 = jnp.where(core == 0, low, high)
        bit_2 = jnp.where(core == 0, high, low)
        for flip_1, flip_2 in ((0, 0), (0, 1), (1, 0), (1, 1)):
            places.append(4 * core + 2 * (bit_1 ^ flip_1) + (bit_2 ^ flip_2))
    return places


def widen_all(quarters, places, widths, others):
    return widen(places, quarters + [swap_dp(part) for part in quarters], widths, others)


def arrival_order(n):
    return [sorted(range(n), key=lambda j: (abs(j - i), j)) for i in range(n)]


def choose(index, options):
    distinct = []
    for option in options:
        if option is not None and not any(option is other for other in distinct):
            distinct.append(option)
    result = distinct[0]
    for option in distinct[1:]:
        mask = functools.reduce(
            jnp.logical_or, [index == i for i, other in enumerate(options) if other is option]
        )
        result = jnp.where(mask, option, result)
    return result


def line_gather(chunk):
    return line_steps({0: chunk}, 1, lax.axis_size("expert"))


def line_steps(found, first, stop):
    n = lax.axis_size("expert")
    found = dict(found)
    for s in range(first, stop):
        found[-s] = lax.ppermute(
            found[1 - s], "expert", [(i, i + 1) for i in range(s - 1, n - 1)]
        )
        found[s] = lax.ppermute(found[s - 1], "expert", [(i + 1, i) for i in range(n - s)])
    return found


def context_gather(rows):
    n = lax.axis_size("context")
    c = lax.axis_index("context")
    found = {0: rows}
    for s in range(1, n):
        found[s] = lax.ppermute(rows, "context", [(i, i ^ s) for i in range(n)])
    return jnp.concatenate([choose(c, [found[i ^ j] for i in range(n)]) for j in range(n)], axis=0)


def context_parts(rows):
    n = lax.axis_size("context")
    c = lax.axis_index("context")
    each = rows.shape[0] // n
    return [
        swap_context(lax.dynamic_slice_in_dim(rows, (c ^ s) * each, each).astype(LOW), s)
        for s in range(1, n)
    ]


def zero_of(*others):
    return functools.reduce(
        jnp.add,
        [
            lax.slice(other, (0,) * other.ndim, (1,) * other.ndim).reshape(()).astype(F32) * 0.0
            for other in others
        ],
    )


def after(value, *others):
    return (value.astype(F32) + zero_of(*others)).astype(value.dtype)


def on_device(
    layer_input,
    grad_output,
    attn_gain,
    query_weight,
    key_weight,
    value_weight,
    q_gain,
    k_gain,
    output_weight,
    mlp_gain,
    router,
    w_gate,
    w_up,
    w_down,
    routes,
    half_order,
):
    n_context = lax.axis_size("context")
    n_expert = lax.axis_size("expert")
    n_groups = lax.axis_size(GROUP_AXES)
    tok_dev, width = layer_input.shape[1:]
    size = q_gain.shape[0]
    kv_total = key_weight.shape[1] * n_expert
    group_dev = n_expert // (kv_total // size)
    kv_index = lax.axis_index("expert") // group_dev
    block = tok_dev * n_expert
    seq = block * n_context
    half = block // 2
    experts = router.shape[1]
    exp_dev = w_gate.shape[0]
    top = routes.shape[2]
    capacity = max(2, (tok_dev * top * 9 + 8 * experts - 1) // (8 * experts))
    scale = size ** (-0.5)

    seq_rows = jnp.arange(seq, dtype=jnp.int32)
    context = lax.axis_index("context")
    own_halves = lax.dynamic_slice_in_dim(half_order, 2 * context, 2)
    own_pos = (own_halves[:, None] * half + jnp.arange(half, dtype=jnp.int32)[None]).reshape(-1)
    per_half = half // TILE
    tile_pos = (half_order[:, None] * per_half + jnp.arange(per_half, dtype=jnp.int32)).reshape(-1)
    kidx = jnp.sum(
        (tile_pos[None, :] == jnp.arange(seq // TILE, dtype=jnp.int32)[:, None])
        * jnp.arange(seq // TILE, dtype=jnp.int32)[None, :],
        axis=1,
    ).astype(jnp.int32)
    qpos = lax.dynamic_slice_in_dim(tile_pos, context * (block // TILE), block // TILE)
    entry = jnp.arange(size)
    freq = jnp.power(THETA, -(2 * (entry % (size // 2))).astype(F32) / size)
    angles = own_pos.astype(F32)[:, None] * freq[None, :]
    cos2 = jnp.cos(angles)
    sin2 = jnp.sin(angles) * jnp.where(entry < size // 2, -1.0, 1.0)[None, :]

    place = lax.axis_index("expert")
    place_1 = place.astype(jnp.int32)[None]
    lanes = -(-2 * experts // 128) * 128
    mask = jnp.any(
        routes[0][:, :, None] == jnp.arange(lanes, dtype=jnp.int32)[None, None, :], axis=1
    )
    mask_wide = mask.astype(F32)
    router_rows = router.T

    x_low = layer_input[0]
    x_normal, _ = norm_parts(x_low.astype(F32))
    normed_found = line_gather((x_normal * attn_gain).astype(LOW))
    if group_dev == 1:
        kv_weights = jnp.concatenate([key_weight, value_weight], axis=1)
    else:
        key_whole = lax.all_gather(key_weight, "expert", axis=1, tiled=True)
        value_whole = lax.all_gather(value_weight, "expert", axis=1, tiled=True)
        kv_weights = jnp.concatenate(
            [
                lax.dynamic_slice_in_dim(key_whole, kv_index * size, size, 1),
                lax.dynamic_slice_in_dim(value_whole, kv_index * size, size, 1),
            ],
            axis=1,
        )
    grad_low = grad_output[0]
    normed_rows, own_kv, key_proj, grad_wide = project_keys(
        place_1,
        normed_found,
        kv_weights,
        k_gain,
        cos2,
        sin2,
        scale * LOG2E,
        grad_low,
        mask_wide,
    )
    grad_col = lax.all_gather(grad_wide, "expert", axis=0, tiled=True)
    kv_whole = context_gather(own_kv)
    queries, query_proj = project_queries(normed_rows, query_weight, q_gain, cos2, sin2)

    n_half = n_expert // 2
    order_here = jnp.asarray(arrival_order(n_expert), jnp.int32)[place]
    turn_here = jnp.sum(
        (order_here[:, None] == jnp.arange(n_expert, dtype=jnp.int32)[None, :])
        * jnp.arange(n_expert, dtype=jnp.int32)[:, None],
        axis=0,
    ).astype(jnp.int32)
    meta = jnp.concatenate([place_1, turn_here, order_here])
    grad_sent, spreads, back_tables = make_tables(
        meta, grad_col, width, n_groups, n_half, capacity, []
    )

    def swap_plane(rows):
        parts = rows.reshape(n_groups, -1, rows.shape[1])
        parts = lax.all_to_all(parts, GROUP_AXES, split_axis=0, concat_axis=0, tiled=True)
        return parts.reshape(rows.shape)

    attended, inverse = attend(qpos, kidx, queries, kv_whole, [])
    attn_part = out_dot(attended, output_weight, [grad_col])
    attn_rows = lax.psum_scatter(attn_part, "expert", scatter_dimension=0, tiled=True)

    grad_x = swap_plane(grad_sent)
    act_pull = dot_nt(grad_x, w_down[0]).reshape(n_groups, 2, n_half * capacity, -1)

    hidden, mixed, probs = route_rows(
        x_low, attn_rows, mlp_gain, router_rows, mask_wide, experts, []
    )

    who = (lax.axis_index(ALL_AXES) * exp_dev).astype(jnp.int32)[None]
    mixed_found = line_gather(mixed)
    near = spread_rows(place_1, spreads[0], mixed_found, range(n_half), [grad_x])
    x_near = swap_plane(near)
    worked_near = run_expert(who, x_near, w_gate[0], w_up[0], act_pull, 0, experts)
    far = spread_rows(place_1, spreads[1], mixed_found, range(n_half, n_expert), [x_near])
    x_far = swap_plane(far)
    worked_far = run_expert(who, x_far, w_gate[0], w_up[0], act_pull, 1, experts)
    xs = [x_near, x_far]
    acts, gate_lows, up_lows, copies = (list(pair) for pair in zip(worked_near, worked_far))
    back_far = swap_plane(copies[1])
    back_near = swap_plane(copies[0])
    join = lambda parts: jnp.concatenate(parts, axis=0)
    x_all = join([x[:, :width] for x in xs])
    grad_w_gate = dot_tn(x_all, join(gate_lows))
    grad_w_up = dot_tn(x_all, join(up_lows))
    grad_by_round = jnp.swapaxes(
        grad_x.reshape(n_groups, 2, n_half * capacity, width), 0, 1
    ).reshape(-1, width)
    grad_w_down = dot_tn(join(acts), grad_by_round)
    copies_col = combine_rows(
        meta, back_tables, [back_near, back_far], n_half, [grad_w_gate, grad_w_up]
    )
    copies_sum = lax.psum_scatter(copies_col, "expert", scatter_dimension=0, tiled=True)

    returned = [dot_nn(act, w_down[0]).astype(LOW) for act in acts]
    returned_near = swap_plane(returned[0])

    grad_hidden, grad_hidden_low, grad_mlp_gain, grad_router = route_back(
        copies_sum,
        grad_low,
        hidden,
        mlp_gain,
        router_rows,
        mask_wide,
        probs,
        experts,
        [returned_near, grad_w_down],
    )

    returned_far = swap_plane(returned[1])
    grad_attn = lax.all_gather(grad_hidden_low, "expert", axis=0, tiled=True)
    grad_o, centre = grad_attended(
        grad_attn, output_weight, attended, inverse, [returned_far]
    )
    combined = combine_rows(meta, back_tables, [returned_near, returned_far], n_half, [])
    output_rows = lax.psum_scatter(combined, "expert", scatter_dimension=0, tiled=True)
    w_out = token_dot(attended, grad_attn, [combined])
    w_out_parts = swap_plane(w_out)
    grad_kv, grad_q, grad_q_gain = attend_back(
        qpos,
        kidx,
        queries,
        grad_o,
        centre,
        kv_whole,
        query_proj,
        q_gain,
        cos2,
        sin2,
        [w_out],
    )
    kv_parts = context_parts(grad_kv)
    w_query = token_dot(normed_rows, grad_q, [w_out_parts])
    w_query_got = dp_got(w_query)
    output_rows = hidden + output_rows.astype(F32) + zero_of(w_query)

    kv_grads, grad_k_gain = kv_back(
        context, grad_kv, kv_parts, key_proj, k_gain, cos2, sin2, scale, [w_query]
    )
    w_out_own = part_sum(w_out_parts.reshape(n_groups, -1, width), kv_parts)
    w_out_quarters = [w_out_own] + [swap_context(w_out_own, s) for s in range(1, n_context)]
    w_kv = token_dot(normed_rows, kv_grads, [])
    pairs = [(w_query, w_query_got)]
    widths = [query_weight.shape[1]]
    if group_dev == 1:
        pairs.append((w_kv, dp_got(w_kv)))
        widths += [key_weight.shape[1], value_weight.shape[1]]
    send, keep = plane_first(pairs, [*kv_parts, *w_out_quarters])

    grad_normed, gain_rows = normed_back(
        grad_q, kv_grads, query_weight, kv_weights, normed_rows, [keep]
    )
    grad_normed = lax.psum_scatter(grad_normed, "expert", scatter_dimension=0, tiled=True)
    grad_input = input_back(grad_normed, x_low, attn_gain, grad_hidden)
    dp_place = lax.axis_index("dp")
    (grad_w_out,) = widen_all(
        w_out_quarters,
        [core * n_context + (context ^ s) for core in (dp_place, 1 - dp_place) for s in range(n_context)],
        [width],
        [],
    )
    quarter = plane_rest(send, keep, [grad_w_out], [output_rows])
    small = pack_small(
        experts,
        grad_router,
        gain_rows,
        attn_gain,
        grad_mlp_gain,
        grad_q_gain,
        grad_k_gain,
        [quarter],
    )
    small_dp = sum_axis(small, "dp")
    small_context = sum_axis(small_dp, "context")
    small_sum = sum_axis(small_context, "expert")
    grad_w_query, *more = widen_all(plane_spread(quarter), quarter_places(), widths, [grad_input])
    if group_dev == 1:
        grad_w_key, grad_w_value = more
    else:
        blank = jnp.zeros((width, kv_total), LOW)
        pieces = []
        for part in (w_kv[:, :size], w_kv[:, size:]):
            padded = lax.dynamic_update_slice(blank, part, (0, kv_index * size))
            pieces.append(lax.psum_scatter(padded, "expert", scatter_dimension=1, tiled=True))
        grad_w_key, grad_w_value = (lax.psum(piece, GROUP_AXES).astype(F32) for piece in pieces)
    grad_attn_gain, grad_mlp_gain = small_sum[experts], small_sum[experts + 1]
    grad_q_gain = small_sum[experts + 2, :size]
    grad_k_gain = small_sum[experts + 2, size : 2 * size]
    return (
        output_rows.astype(LOW)[None],
        grad_input[None],
        grad_attn_gain,
        grad_w_query,
        grad_w_key,
        grad_w_value,
        grad_q_gain,
        grad_k_gain,
        grad_w_out,
        grad_mlp_gain,
        small_sum[:experts].T,
        grad_w_gate[None],
        grad_w_up[None],
        grad_w_down[None],
    )


def solution(mesh):
    rows = P("dp", ("context", "expert"), None)
    expert = P(ALL_AXES, None, None)
    columns = P(None, "expert")
    in_specs = (
        rows,
        rows,
        P(),
        columns,
        columns,
        columns,
        P(),
        P(),
        P("expert", None),
        P(),
        P(),
        expert,
        expert,
        expert,
        rows,
        P(),
    )
    out_specs = (
        rows,
        rows,
        P(),
        columns,
        columns,
        columns,
        P(),
        P(),
        P("expert", None),
        P(),
        P(),
        expert,
        expert,
        expert,
    )
    return jax.shard_map(
        on_device, mesh=mesh, in_specs=in_specs, out_specs=out_specs, check_vma=False
    )
```

```python
import functools
import math

import jax
import jax.numpy as jnp
from jax import lax
from jax.experimental import pallas as pl
from jax.experimental.pallas import tpu as pltpu
from jax.sharding import PartitionSpec as P

EPS = 1e-06
THETA = 1000000.0
TILE = 256
PIECE = 128
VMEM_BYTES = 56 * 1024 * 1024
LOG2E = math.log2(math.e)
LOW = jnp.bfloat16
F32 = jnp.float32
ALL_AXES = ("dp", "context", "expert")
GROUP_AXES = ("dp", "context")


def dot_nn(a, b):
    return lax.dot_general(a, b, (((1,), (0,)), ((), ())), preferred_element_type=F32)


def dot_nt(a, b):
    return lax.dot_general(a, b, (((1,), (1,)), ((), ())), preferred_element_type=F32)


def dot_tn(a, b):
    return lax.dot_general(a, b, (((0,), (0,)), ((), ())), preferred_element_type=F32)


def params(**more):
    return pltpu.CompilerParams(vmem_limit_bytes=VMEM_BYTES, **more)


def cost(flops, nbytes, exps=0):
    return pl.CostEstimate(flops=int(flops), bytes_accessed=int(nbytes), transcendentals=int(exps))


def head_forward(u, gain, cos2, sin2):
    rr = lax.rsqrt(jnp.mean(u * u, axis=-1, keepdims=True) + EPS)
    y = u * rr * gain
    return y * cos2 + pltpu.roll(y, 64, 1) * sin2


def head_backward(gy, u, gain, cos2, sin2):
    g = gy * cos2 - pltpu.roll(gy, 64, 1) * sin2
    rr = lax.rsqrt(jnp.mean(u * u, axis=-1, keepdims=True) + EPS)
    n = u * rr
    gn = g * gain
    grad = rr * (gn - n * jnp.mean(gn * n, axis=-1, keepdims=True))
    return grad, jnp.sum(g * n, axis=0, keepdims=True)


def query_kernel(x_ref, w_ref, gain_ref, cos_ref, sin_ref, rot_ref, proj_ref):
    tiles, heads, rows, size = rot_ref.shape
    acc = dot_nn(x_ref[...], w_ref[...])
    for h in range(heads):
        u = acc[:, h * size : (h + 1) * size]
        rot = head_forward(u, gain_ref[...], cos_ref[...], sin_ref[...])
        proj_ref[:, h] = u.reshape(tiles, rows, size)
        rot_ref[:, h] = rot.astype(LOW).reshape(tiles, rows, size)


def project_queries(normed, weight, gain, cos2, sin2):
    block, width = normed.shape
    size = cos2.shape[1]
    heads = weight.shape[1] // size
    tiles = block // TILE
    whole = lambda i: (0, 0)
    per = lambda i: (0, i, 0, 0)
    shape = (tiles, heads, TILE, size)
    return pl.pallas_call(
        query_kernel,
        grid=(heads // 2,),
        in_specs=[
            pl.BlockSpec((block, width), whole),
            pl.BlockSpec((width, 2 * size), lambda i: (0, i)),
            pl.BlockSpec((1, size), whole),
            pl.BlockSpec((block, size), whole),
            pl.BlockSpec((block, size), whole),
        ],
        out_specs=[pl.BlockSpec((tiles, 2, TILE, size), per)] * 2,
        out_shape=[jax.ShapeDtypeStruct(shape, LOW), jax.ShapeDtypeStruct(shape, F32)],
        compiler_params=params(),
        cost_estimate=cost(2 * block * width * heads * size, 12e6),
    )(normed, weight, gain[None], cos2, sin2)


def put_in_order(place, refs, out_ref):
    n = (len(refs) + 1) // 2
    rows = refs[0].shape[0]
    for distance in range(1 - n, n):
        ref = refs[distance + n - 1]
        at = place + distance

        @pl.when(jnp.logical_and(at >= 0, at < n))
        def _():
            out_ref[pl.ds(pl.multiple_of(at * rows, rows), rows), :] = ref[...]


def chunk_list(found):
    n = (len(found) + 1) // 2
    return [found[distance] for distance in range(1 - n, n)]


def key_kernel(factor, n_chunks, place_ref, *refs):
    w_ref, gain_ref, cos_ref, sin_ref, g_ref, mask_ref = refs[n_chunks:-4]
    rows_ref, kv_ref, proj_ref, wide_ref = refs[-4:]
    size = proj_ref.shape[1]
    width = g_ref.shape[1]
    put_in_order(place_ref[0], refs[:n_chunks], rows_ref)
    wide_ref[:, :width] = g_ref[...]
    wide_ref[:, width:] = mask_ref[...].astype(LOW)
    acc = dot_nn(rows_ref[...], w_ref[...])
    u = acc[:, :size]
    rot = head_forward(u, gain_ref[...], cos_ref[...], sin_ref[...])
    proj_ref[...] = u
    kv_ref[:, :size] = (rot * factor).astype(LOW)
    kv_ref[:, size:] = acc[:, size:].astype(LOW)


def full(shape):
    return pl.BlockSpec(shape, lambda *_: (0,) * len(shape))


def project_keys(place, found, weight, gain, cos2, sin2, factor, g, mask):
    chunks = chunk_list(found)
    rows, width = chunks[0].shape
    block, size = cos2.shape
    operands = [*chunks, weight, gain[None], cos2, sin2, g, mask]
    shapes = [
        jax.ShapeDtypeStruct((block, width), LOW),
        jax.ShapeDtypeStruct((block, 2 * size), LOW),
        jax.ShapeDtypeStruct((block, size), F32),
        jax.ShapeDtypeStruct((rows, width + mask.shape[1]), LOW),
    ]
    return pl.pallas_call(
        functools.partial(key_kernel, factor, len(chunks)),
        grid_spec=pltpu.PrefetchScalarGridSpec(
            num_scalar_prefetch=1,
            grid=(1,),
            in_specs=[full(x.shape) for x in operands],
            out_specs=[full(x.shape) for x in shapes],
        ),
        out_shape=shapes,
        compiler_params=params(),
        cost_estimate=cost(4 * block * width * size, 8e6),
    )(place, *operands)


def in_order(last, step):
    lax.fori_loop(0, lax.div(last, 2), lambda p, c: (step([2 * p, 2 * p + 1], False), c)[1], 0)

    @pl.when(lax.rem(last, 2) == 1)
    def _():
        step([last - 1, last], True)

    @pl.when(lax.rem(last, 2) == 0)
    def _():
        step([last], True)


def attend_kernel(qpos_ref, kidx_ref, q_ref, kv_ref, *rest):
    out_ref, inv_ref, acc_ref = rest[-3:]
    heads, rows, size = q_ref.shape[1:]
    acc_ref[...] = jnp.zeros_like(acc_ref)

    def step(places, masked):
        starts = [pl.multiple_of(kidx_ref[place] * rows, rows) for place in places]
        count = len(places) * rows
        keys = jnp.concatenate([kv_ref[pl.ds(start, rows), :size] for start in starts], axis=0)
        values = jnp.concatenate([kv_ref[pl.ds(start, rows), size:] for start in starts], axis=0)
        values = jnp.concatenate([values, jnp.ones((count, size), LOW)], axis=1)
        for h in range(heads):
            for first in range(0, rows, PIECE):
                part = slice(first, first + PIECE)
                e = jnp.exp2(dot_nt(q_ref[0, h, part], keys))
                if masked:
                    qi = lax.broadcasted_iota(jnp.int32, e.shape, 0) + first
                    ki = lax.broadcasted_iota(jnp.int32, e.shape, 1) - (count - rows)
                    e = jnp.where(ki <= qi, e, 0.0)
                acc_ref[h, part] += dot_nn(e.astype(LOW), values)

    in_order(qpos_ref[pl.program_id(0)], step)
    for h in range(heads):
        inv = 1.0 / acc_ref[h, :, size:]
        inv_ref[0, h] = inv
        out_ref[:, h * size : (h + 1) * size] = (acc_ref[h, :, :size] * inv).astype(LOW)


def attend(qpos, kidx, queries, kv, others):
    tiles, heads, rows, size = queries.shape
    seq = kv.shape[0]
    return pl.pallas_call(
        attend_kernel,
        grid_spec=pltpu.PrefetchScalarGridSpec(
            num_scalar_prefetch=2,
            grid=(tiles,),
            in_specs=[
                pl.BlockSpec((1, heads, rows, size), lambda i, a, b: (i, 0, 0, 0)),
                pl.BlockSpec((seq, 2 * size), lambda i, a, b: (0, 0)),
            ]
            + [pl.BlockSpec(memory_space=pl.ANY)] * len(others),
            out_specs=[
                pl.BlockSpec((rows, heads * size), lambda i, a, b: (i, 0)),
                pl.BlockSpec((1, heads, rows, size), lambda i, a, b: (i, 0, 0, 0)),
            ],
            scratch_shapes=[pltpu.VMEM((heads, rows, 2 * size), F32)],
        ),
        out_shape=[
            jax.ShapeDtypeStruct((tiles * rows, heads * size), LOW),
            jax.ShapeDtypeStruct((tiles, heads, rows, size), F32),
        ],
        compiler_params=params(),
        cost_estimate=cost(
            6 * tiles * rows * heads * seq * size, 8e6, tiles * rows * heads * seq
        ),
    )(qpos, kidx, queries, kv, *others)


def grad_out_kernel(rows_ref, w_ref, o_ref, inv_ref, *rest):
    do_ref, centre_ref = rest[-2:]
    tiles, heads, rows, size = do_ref.shape
    acc = dot_nt(rows_ref[...], w_ref[...])
    for t in range(tiles):
        for h in range(heads):
            part = slice(t * rows, (t + 1) * rows), slice(h * size, (h + 1) * size)
            low = (acc[part] * inv_ref[t, h]).astype(LOW)
            do_ref[t, h] = low
            product = low.astype(F32) * o_ref[part].astype(F32)
            centre = jnp.sum(jnp.transpose(product), axis=0, keepdims=True)
            centre_ref[t, h] = jnp.broadcast_to(centre, (8, rows))


def grad_attended(grad_rows, weight, attended, inverse, others):
    tiles, heads, rows, size = inverse.shape
    block, width = grad_rows.shape
    return pl.pallas_call(
        grad_out_kernel,
        grid=(heads // 2,),
        in_specs=[
            pl.BlockSpec((block, width), lambda i: (0, 0)),
            pl.BlockSpec((2 * size, width), lambda i: (i, 0)),
            pl.BlockSpec((block, 2 * size), lambda i: (0, i)),
            pl.BlockSpec((tiles, 2, rows, size), lambda i: (0, i, 0, 0)),
        ]
        + [pl.BlockSpec(memory_space=pl.ANY)] * len(others),
        out_specs=[
            pl.BlockSpec((tiles, 2, rows, size), lambda i: (0, i, 0, 0)),
            pl.BlockSpec((tiles, 2, 8, rows), lambda i: (0, i, 0, 0)),
        ],
        out_shape=[
            jax.ShapeDtypeStruct((tiles, heads, rows, size), LOW),
            jax.ShapeDtypeStruct((tiles, heads, 8, rows), F32),
        ],
        compiler_params=params(),
        cost_estimate=cost(2 * block * width * heads * size, 12e6),
    )(grad_rows, weight, attended, inverse, *others)


def attend_back_kernel(
    qpos_ref,
    kidx_ref,
    q_ref,
    do_ref,
    centre_ref,
    kv_ref,
    proj_ref,
    gain_ref,
    cos_ref,
    sin_ref,
    *rest,
):
    dkv_ref, dq_ref, dgain_ref, acc_ref, e_ref, ds_ref = rest[-6:]
    heads, rows, size = q_ref.shape[1:]

    @pl.when(pl.program_id(0) == 0)
    def _():
        dkv_ref[...] = jnp.zeros_like(dkv_ref)
        dgain_ref[...] = jnp.zeros_like(dgain_ref)

    acc_ref[...] = jnp.zeros_like(acc_ref)

    def step(places, masked):
        starts = [pl.multiple_of(kidx_ref[place] * rows, rows) for place in places]
        count = len(places) * rows
        keys = jnp.concatenate([kv_ref[pl.ds(start, rows), :size] for start in starts], axis=0)
        values = jnp.concatenate([kv_ref[pl.ds(start, rows), size:] for start in starts], axis=0)
        for h in range(heads):
            query, grad = q_ref[0, h], do_ref[0, h]
            centre = centre_ref[0, h, 0:1]
            columns = slice(h * rows, (h + 1) * rows)
            for first in range(0, count, PIECE):
                part = slice(first, first + PIECE)
                e = jnp.exp2(dot_nt(keys[part], query))
                if masked and first >= count - rows:
                    ki = lax.broadcasted_iota(jnp.int32, e.shape, 0) + (first - (count - rows))
                    qi = lax.broadcasted_iota(jnp.int32, e.shape, 1)
                    e = jnp.where(ki <= qi, e, 0.0)
                ds = e * (dot_nt(values[part], grad) - centre)
                e_ref[part, columns] = e.astype(LOW)
                ds_ref[part, columns] = ds.astype(LOW)
            acc_ref[h] += dot_tn(ds_ref[:count, columns], keys)
        dk = dot_nn(ds_ref[:count], q_ref[0].reshape(heads * rows, size))
        dv = dot_nn(e_ref[:count], do_ref[0].reshape(heads * rows, size))
        for k, start in enumerate(starts):
            dkv_ref[pl.ds(start, rows), :size] += dk[k * rows : (k + 1) * rows]
            dkv_ref[pl.ds(start, rows), size:] += dv[k * rows : (k + 1) * rows]

    in_order(qpos_ref[pl.program_id(0)], step)
    total = jnp.zeros((1, size), F32)
    for h in range(heads):
        grad, gain_part = head_backward(
            acc_ref[h] * (1.0 / LOG2E), proj_ref[0, h], gain_ref[...], cos_ref[...], sin_ref[...]
        )
        dq_ref[:, h * size : (h + 1) * size] = grad.astype(LOW)
        total += gain_part
    dgain_ref[...] += total


def attend_back(qpos, kidx, queries, grads, centre, kv, proj, gain, cos2, sin2, others):
    tiles, heads, rows, size = queries.shape
    seq = kv.shape[0]
    per = pl.BlockSpec((1, heads, rows, size), lambda i, a, b: (i, 0, 0, 0))
    flat = lambda i, a, b: (0, 0)
    rowwise = lambda i, a, b: (i, 0)
    return pl.pallas_call(
        attend_back_kernel,
        grid_spec=pltpu.PrefetchScalarGridSpec(
            num_scalar_prefetch=2,
            grid=(tiles,),
            in_specs=[
                per,
                per,
                pl.BlockSpec((1, heads, 8, rows), lambda i, a, b: (i, 0, 0, 0)),
                pl.BlockSpec((seq, 2 * size), flat),
                per,
                pl.BlockSpec((1, size), flat),
                pl.BlockSpec((rows, size), rowwise),
                pl.BlockSpec((rows, size), rowwise),
            ]
            + [pl.BlockSpec(memory_space=pl.ANY)] * len(others),
            out_specs=[
                pl.BlockSpec((seq, 2 * size), flat),
                pl.BlockSpec((rows, heads * size), rowwise),
                pl.BlockSpec((1, size), flat),
            ],
            scratch_shapes=[pltpu.VMEM((heads, rows, size), F32)]
            + [pltpu.VMEM((2 * rows, heads * rows), LOW)] * 2,
        ),
        out_shape=[
            jax.ShapeDtypeStruct((seq, 2 * size), F32),
            jax.ShapeDtypeStruct((tiles * rows, heads * size), LOW),
            jax.ShapeDtypeStruct((1, size), F32),
        ],
        compiler_params=params(),
        cost_estimate=cost(
            15 * tiles * rows * heads * seq * size, 12e6, tiles * rows * heads * seq
        ),
    )(qpos, kidx, queries, grads, centre, kv, proj, gain[None], cos2, sin2, *others)


def out_kernel(a_ref, b_ref, *rest):
    rest[-1][...] = dot_nn(a_ref[...], b_ref[...]).astype(LOW)


def out_dot(a, b, others):
    block, inner = a.shape
    columns = b.shape[1]
    tile = min(columns, 512)
    return pl.pallas_call(
        out_kernel,
        grid=(columns // tile,),
        in_specs=[
            pl.BlockSpec((block, inner), lambda i: (0, 0)),
            pl.BlockSpec((inner, tile), lambda i: (0, i)),
        ]
        + [pl.BlockSpec(memory_space=pl.ANY)] * len(others),
        out_specs=pl.BlockSpec((block, tile), lambda i: (0, i)),
        out_shape=jax.ShapeDtypeStruct((block, columns), LOW),
        compiler_params=params(),
        cost_estimate=cost(2 * block * inner * columns, 8e6),
    )(a, b, *others)


def token_kernel(a_ref, b_ref, *rest):
    rest[-1][...] = dot_tn(a_ref[...], b_ref[...]).astype(LOW)


def token_dot(a, b, others):
    block, rows = a.shape
    columns = b.shape[1]
    tile = min(rows, 512)
    return pl.pallas_call(
        token_kernel,
        grid=(rows // tile,),
        in_specs=[
            pl.BlockSpec((block, tile), lambda i: (0, i)),
            pl.BlockSpec((block, columns), lambda i: (0, 0)),
        ]
        + [pl.BlockSpec(memory_space=pl.ANY)] * len(others),
        out_specs=pl.BlockSpec((tile, columns), lambda i: (i, 0)),
        out_shape=jax.ShapeDtypeStruct((rows, columns), LOW),
        compiler_params=params(),
        cost_estimate=cost(2 * block * rows * columns, 6e6),
    )(a, b, *others)


def split_low(value):
    high = value.astype(LOW)
    return high, (value - high.astype(F32)).astype(LOW)


def norm_parts(rows):
    rr = lax.rsqrt(jnp.mean(rows * rows, axis=-1, keepdims=True) + EPS)
    return rows * rr, rr


def norm_back(grad, normal, rr, gain):
    weighted = grad * gain
    return rr * (weighted - normal * jnp.mean(weighted * normal, axis=-1, keepdims=True))


def add_all(refs):
    return functools.reduce(jnp.add, [ref[...].astype(F32) for ref in refs])


def pad_rows(rows, count):
    if rows.shape[0] == count:
        return rows
    return jnp.concatenate(
        [rows, jnp.zeros((count - rows.shape[0], rows.shape[1]), rows.dtype)], axis=0
    )


def router_kernel(experts, *refs):
    x_ref, attn_ref, gain_ref, router_ref, mask_ref = refs[:5]
    hidden_ref, mixed_ref, probs_ref = refs[-3:]
    width = x_ref.shape[1]
    lanes = mask_ref.shape[1]
    hidden = add_all([x_ref, attn_ref])
    hidden_ref[...] = hidden
    mixed = (norm_parts(hidden)[0] * gain_ref[...]).astype(LOW)
    mixed_ref[:, :width] = mixed
    logits = dot_nt(mixed, pad_rows(router_ref[...], lanes))
    lane = lax.broadcasted_iota(jnp.int32, logits.shape, 1)
    logits = jnp.where(lane < experts, logits, -1e30)
    weights = jnp.exp(logits - jnp.max(logits, axis=1, keepdims=True))
    probs = weights / jnp.sum(weights, axis=1, keepdims=True)
    probs_ref[...] = probs
    chosen = probs * mask_ref[...]
    high, low = split_low(chosen / jnp.sum(chosen, axis=1, keepdims=True))
    both = high.astype(F32) + pltpu.roll(low.astype(F32), experts, 1)
    mixed_ref[:, width:] = both.astype(LOW)


def route_rows(x, attn, gain, router, mask, experts, others):
    tokens, width = x.shape
    lanes = mask.shape[1]
    operands = [x, attn, gain[None], router, mask]
    shapes = [
        jax.ShapeDtypeStruct((tokens, width), F32),
        jax.ShapeDtypeStruct((tokens, width + lanes), LOW),
        jax.ShapeDtypeStruct((tokens, lanes), F32),
    ]
    return pl.pallas_call(
        functools.partial(router_kernel, experts),
        grid=(1,),
        in_specs=[full(value.shape) for value in operands]
        + [pl.BlockSpec(memory_space=pl.ANY)] * len(others),
        out_specs=[full(shape.shape) for shape in shapes],
        out_shape=shapes,
        compiler_params=params(),
        cost_estimate=cost(2 * tokens * width * lanes, 5e6),
    )(*operands, *others)


def table_kernel(capacity, n_half, meta_ref, col_ref, *rest):
    rows_ref, near_ref, far_ref, near_back_ref, far_back_ref, slots_ref = rest[-6:]
    block = col_ref.shape[0]
    rows, width = rows_ref.shape
    n = 2 * n_half
    tokens = block // n
    cap_half = n_half * capacity
    groups = rows // (2 * cap_half)
    mask = col_ref[:, width:]
    lanes = mask.shape[1]
    padded = -(-groups // 16) * 16
    group = lax.broadcasted_iota(jnp.int32, (padded, lanes), 0)
    lane = lax.broadcasted_iota(jnp.int32, (padded, lanes), 1)
    wanted = jnp.logical_and(lane == group * n + meta_ref[0], group < groups)
    hits = dot_nt(jnp.where(wanted, 1.0, 0.0).astype(LOW), mask)
    before = lax.broadcasted_iota(jnp.int32, (tokens, tokens), 0)
    after_it = lax.broadcasted_iota(jnp.int32, (tokens, tokens), 1)
    earlier = jnp.where(before < after_it, 1.0, 0.0).astype(LOW)
    for z in range(n):
        hit = hits[:, z * tokens : (z + 1) * tokens]
        rank = dot_nn(hit.astype(LOW), earlier)
        turn = (meta_ref[1 + z] * capacity).astype(F32)
        slot = jnp.where(hit > 0.5, rank + turn, -1.0)
        slots_ref[:, z * tokens : (z + 1) * tokens] = slot[:groups]

    def one_hot(slots, count, first):
        slot = lax.broadcasted_iota(jnp.int32, (groups, count, slots.shape[1]), 1).astype(F32)
        same = slots[:, None, :] == slot + float(first)
        return jnp.where(same, 1.0, 0.0).reshape(groups * count, slots.shape[1])

    spread = one_hot(slots_ref[...], 2 * cap_half, 0).astype(LOW)
    rows_ref[...] = dot_nn(spread, col_ref[:, :width]).astype(LOW)
    for part, (to_ref, back_ref) in enumerate([(near_ref, near_back_ref), (far_ref, far_back_ref)]):
        pieces = []
        for k in range(n_half):
            start = pl.multiple_of(meta_ref[1 + n + part * n_half + k] * tokens, tokens)
            pieces.append(slots_ref[:, pl.ds(start, tokens)])
        spread = one_hot(jnp.concatenate(pieces, axis=1), cap_half, part * cap_half)
        to_ref[...] = spread.astype(LOW)
        back_ref[...] = jnp.transpose(spread).astype(LOW)


def make_tables(meta, col, width, groups, n_half, capacity, others):
    block = col.shape[0]
    rows = groups * n_half * capacity
    shapes = (
        [jax.ShapeDtypeStruct((2 * rows, width), LOW)]
        + [jax.ShapeDtypeStruct((rows, block // 2), LOW)] * 2
        + [jax.ShapeDtypeStruct((block // 2, rows), LOW)] * 2
    )
    outs = pl.pallas_call(
        functools.partial(table_kernel, capacity, n_half),
        grid_spec=pltpu.PrefetchScalarGridSpec(
            num_scalar_prefetch=1,
            grid=(1,),
            in_specs=[full(col.shape)] + [pl.BlockSpec(memory_space=pl.ANY)] * len(others),
            out_specs=[full(shape.shape) for shape in shapes],
            scratch_shapes=[pltpu.VMEM((groups, block), F32)],
        ),
        out_shape=shapes,
        compiler_params=params(),
        cost_estimate=cost(4 * rows * block * width, 12e6),
    )(meta, col, *others)
    return outs[0], outs[1:3], outs[3:]


def spread_kernel(choices, place_ref, spread_ref, *refs):
    out_ref, rows_ref = refs[-2:]
    for k, by_place in enumerate(choices):
        for which in sorted(set(by_place)):
            hit = functools.reduce(
                jnp.logical_or,
                [place_ref[0] == i for i, other in enumerate(by_place) if other == which],
            )

            @pl.when(hit)
            def _():
                tokens = refs[which].shape[0]
                rows_ref[k * tokens : (k + 1) * tokens] = refs[which][...]

    out_ref[...] = dot_nn(spread_ref[...], rows_ref[...]).astype(LOW)


def spread_rows(place, spread, found, turns, others):
    n = lax.axis_size("expert")
    order = arrival_order(n)
    distances = sorted({order[i][turn] - i for i in range(n) for turn in turns})
    choices = [[distances.index(order[i][turn] - i) for i in range(n)] for turn in turns]
    chunks = [found[distance] for distance in distances]
    tokens, wide = chunks[0].shape
    rows = spread.shape[0]
    return pl.pallas_call(
        functools.partial(spread_kernel, choices),
        grid_spec=pltpu.PrefetchScalarGridSpec(
            num_scalar_prefetch=1,
            grid=(1,),
            in_specs=[full(spread.shape)]
            + [full(chunk.shape) for chunk in chunks]
            + [pl.BlockSpec(memory_space=pl.ANY)] * len(others),
            out_specs=full((rows, wide)),
            scratch_shapes=[pltpu.VMEM((len(turns) * tokens, wide), LOW)],
        ),
        out_shape=jax.ShapeDtypeStruct((rows, wide), LOW),
        compiler_params=params(),
        cost_estimate=cost(2 * rows * len(turns) * tokens * wide, 5e6),
    )(place, spread, *chunks, *others)


def router_back_kernel(experts, *refs):
    sum_ref, g_ref, hidden_ref, gain_ref, router_ref, mask_ref, probs_ref = refs[:7]
    grad_ref, low_ref, dgain_ref, drouter_ref = refs[-4:]
    width = g_ref.shape[1]
    lanes = mask_ref.shape[1]
    total = sum_ref[...].astype(F32)
    table = total[:, width:]
    mask, probs = mask_ref[...], probs_ref[...]
    grad_gates = (table + pltpu.roll(table, lanes - experts, 1)) * mask
    chosen = probs * mask
    chosen_sum = jnp.sum(chosen, axis=1, keepdims=True)
    mean = jnp.sum(grad_gates * (chosen / chosen_sum), axis=1, keepdims=True)
    centred = mask * (grad_gates - mean) / chosen_sum
    grad_logits = probs * (centred - jnp.sum(centred * chosen, axis=1, keepdims=True))
    high, low = split_low(grad_logits)
    router = pad_rows(router_ref[...], lanes)
    grad = total[:, :width] + dot_nn(high, router) + dot_nn(low, router)
    normal, rr = norm_parts(hidden_ref[...])
    mixed = (normal * gain_ref[...]).astype(LOW)
    drouter_ref[...] = dot_tn(high, mixed) + dot_tn(low, mixed)
    dgain_ref[...] = jnp.sum(grad * normal, axis=0, keepdims=True)
    grad_hidden = g_ref[...].astype(F32) + norm_back(grad, normal, rr, gain_ref[...])
    grad_ref[...] = grad_hidden
    low_ref[...] = grad_hidden.astype(LOW)


def route_back(summed, g, hidden, gain, router, mask, probs, experts, others):
    tokens, width = g.shape
    lanes = mask.shape[1]
    operands = [summed, g, hidden, gain[None], router, mask, probs]
    shapes = [
        jax.ShapeDtypeStruct((tokens, width), F32),
        jax.ShapeDtypeStruct((tokens, width), LOW),
        jax.ShapeDtypeStruct((1, width), F32),
        jax.ShapeDtypeStruct((lanes, width), F32),
    ]
    return pl.pallas_call(
        functools.partial(router_back_kernel, experts),
        grid=(1,),
        in_specs=[full(value.shape) for value in operands]
        + [pl.BlockSpec(memory_space=pl.ANY)] * len(others),
        out_specs=[full(shape.shape) for shape in shapes],
        out_shape=shapes,
        compiler_params=params(),
        cost_estimate=cost(8 * tokens * width * lanes, 8e6),
    )(*operands, *others)


def combine_kernel(n_half, meta_ref, near_table_ref, far_table_ref, near_ref, far_ref, *rest):
    del meta_ref
    turn = pl.program_id(0)

    @pl.when(turn < n_half)
    def _():
        rest[-1][...] = dot_nn(near_table_ref[...], near_ref[...]).astype(LOW)

    @pl.when(turn >= n_half)
    def _():
        rest[-1][...] = dot_nn(far_table_ref[...], far_ref[...]).astype(LOW)


def combine_rows(meta, tables, rows, n_half, others):
    tokens = tables[0].shape[0] // n_half
    slots, wide = rows[0].shape
    n = 2 * n_half
    return pl.pallas_call(
        functools.partial(combine_kernel, n_half),
        grid_spec=pltpu.PrefetchScalarGridSpec(
            num_scalar_prefetch=1,
            grid=(n,),
            in_specs=[
                pl.BlockSpec((tokens, slots), lambda i, m: (jnp.minimum(i, n_half - 1), 0)),
                pl.BlockSpec((tokens, slots), lambda i, m: (jnp.maximum(i - n_half, 0), 0)),
            ]
            + [full(value.shape) for value in rows]
            + [pl.BlockSpec(memory_space=pl.ANY)] * len(others),
            out_specs=pl.BlockSpec((tokens, wide), lambda i, m: (m[1 + n + i], 0)),
        ),
        out_shape=jax.ShapeDtypeStruct((n * tokens, wide), LOW),
        compiler_params=params(),
        cost_estimate=cost(2 * slots * n * tokens * wide, 10e6),
    )(meta, *tables, *rows, *others)


def expert_kernel(experts, who_ref, x_ref, gate_ref, up_ref, pull_ref, *rest):
    act_ref, dgate_ref, dup_ref, copy_ref = rest[-4:]
    width = gate_ref.shape[0]
    x = x_ref[:, :width]
    table = x_ref[:, width:].astype(F32)
    lane = lax.broadcasted_iota(jnp.int32, table.shape, 1)
    mine = who_ref[0]
    gate = jnp.sum(
        jnp.where(jnp.logical_or(lane == mine, lane == mine + experts), table, 0.0),
        axis=1,
        keepdims=True,
    )
    pre_gate = dot_nn(x, gate_ref[...])
    pre_up = dot_nn(x, up_ref[...])
    pull = pull_ref[...].reshape(pre_up.shape)
    sig = 1.0 / (1.0 + jnp.exp(-pre_gate))
    silu = pre_gate * sig
    act = silu * pre_up
    act_ref[...] = (act * gate).astype(LOW)
    high, low = split_low(jnp.sum(act * pull, axis=1, keepdims=True))
    pull = pull * gate
    dup = (pull * silu).astype(LOW)
    dgate = (pull * pre_up * (sig * (1.0 + pre_gate * (1.0 - sig)))).astype(LOW)
    dgate_ref[...] = dgate
    dup_ref[...] = dup
    copy_ref[:, :width] = (dot_nt(dgate, gate_ref[...]) + dot_nt(dup, up_ref[...])).astype(LOW)
    back = jnp.where(lane == mine, high.astype(F32), 0.0)
    back = jnp.where(lane == mine + experts, low.astype(F32), back)
    copy_ref[:, width:] = back.astype(LOW)


def run_expert(who, x, w_gate, w_up, pull, part, experts):
    rows, wide = x.shape
    width, hidden = w_gate.shape
    groups, _, slots, _ = pull.shape
    each = groups // 2
    tile = each * slots
    by_rows = lambda columns: pl.BlockSpec((tile, columns), lambda i, p: (i, 0))
    return pl.pallas_call(
        functools.partial(expert_kernel, experts),
        grid_spec=pltpu.PrefetchScalarGridSpec(
            num_scalar_prefetch=1,
            grid=(2,),
            in_specs=[
                by_rows(wide),
                full(w_gate.shape),
                full(w_up.shape),
                pl.BlockSpec((each, 1, slots, hidden), lambda i, p: (i, part, 0, 0)),
            ],
            out_specs=[by_rows(hidden), by_rows(hidden), by_rows(hidden), by_rows(wide)],
        ),
        out_shape=[jax.ShapeDtypeStruct((rows, hidden), LOW)] * 3
        + [jax.ShapeDtypeStruct((rows, wide), LOW)],
        compiler_params=params(),
        cost_estimate=cost(8 * rows * width * hidden, 20e6, rows * hidden),
    )(who, x, w_gate, w_up, pull)


def input_kernel(grad_ref, x_ref, gain_ref, more_ref, out_ref):
    normal, rr = norm_parts(x_ref[...].astype(F32))
    grad = grad_ref[...].astype(F32)
    out_ref[...] = more_ref[...] + norm_back(grad, normal, rr, gain_ref[...])


def input_back(grad, x, gain, more):
    tokens, width = x.shape
    operands = [grad, x, gain[None], more]
    return pl.pallas_call(
        input_kernel,
        grid=(1,),
        in_specs=[full(value.shape) for value in operands],
        out_specs=full(more.shape),
        out_shape=jax.ShapeDtypeStruct((tokens, width), F32),
        compiler_params=params(),
        cost_estimate=cost(20 * tokens * width, 5e6),
    )(*operands)


def kv_back_kernel(factor, parts_ref, proj_ref, gain_ref, cos_ref, sin_ref, *rest):
    grad_ref, dgain_ref = rest[-2:]
    size = proj_ref.shape[1]
    total = parts_ref[0].astype(F32)
    for k in range(1, parts_ref.shape[0]):
        total += parts_ref[k].astype(F32)
    grad, dgain = head_backward(
        total[:, :size] * factor, proj_ref[...], gain_ref[...], cos_ref[...], sin_ref[...]
    )
    grad_ref[:, :size] = grad.astype(LOW)
    grad_ref[:, size:] = total[:, size:].astype(LOW)
    dgain_ref[...] = dgain


def kv_back(parts, proj, gain, cos2, sin2, factor, others):
    block, size = proj.shape
    operands = [parts, proj, gain[None], cos2, sin2]
    shapes = [
        jax.ShapeDtypeStruct((block, 2 * size), LOW),
        jax.ShapeDtypeStruct((1, size), F32),
    ]
    return pl.pallas_call(
        functools.partial(kv_back_kernel, factor),
        grid=(1,),
        in_specs=[full(value.shape) for value in operands]
        + [pl.BlockSpec(memory_space=pl.ANY)] * len(others),
        out_specs=[full(shape.shape) for shape in shapes],
        out_shape=shapes,
        compiler_params=params(),
        cost_estimate=cost(40 * block * size, 5e6),
    )(*operands, *others)


def pair_kernel(a_ref, b_ref, *rest):
    rest[-1][...] = (a_ref[...].astype(F32) + b_ref[...].astype(F32)).astype(LOW)


def pair_sum(a, b, others):
    rows, columns = a.shape
    tiles = 2 if rows % 32 == 0 else 1
    spec = pl.BlockSpec((rows // tiles, columns), lambda i: (i, 0))
    return pl.pallas_call(
        pair_kernel,
        grid=(tiles,),
        in_specs=[spec, spec] + [pl.BlockSpec(memory_space=pl.ANY)] * len(others),
        out_specs=spec,
        out_shape=jax.ShapeDtypeStruct((rows, columns), LOW),
        compiler_params=params(),
        cost_estimate=cost(rows * columns, 6 * rows * columns),
    )(a, b, *others)


def fold_kernel(n_pairs, s_ref, *refs):
    del s_ref
    send_ref, keep_ref = refs[-2:]
    totals = [
        (refs[2 * k][...].astype(F32) + refs[2 * k + 1][...].astype(F32)).astype(LOW)
        for k in range(n_pairs)
    ]
    for half, out_ref in enumerate((send_ref, keep_ref)):

        @pl.when(pl.program_id(0) == half)
        def _():
            first = 0
            for total in totals:
                last = first + total.shape[1]
                out_ref[:, first:last] = total
                first = last


def fold(pairs, base, bit, others):
    rows = pairs[0][1].shape[0]
    columns = sum(got.shape[1] for _, got in pairs)
    tiles = 2
    tile = rows // (2 * tiles)
    side = lambda h, m: (1 - m[1]) * (1 - h) + m[1] * h
    specs = []
    for _, got in pairs:
        wide = got.shape[1]
        specs.append(
            pl.BlockSpec(
                (tile, wide), lambda h, j, m: (m[0] * 2 * tiles + side(h, m) * tiles + j, 0)
            )
        )
        specs.append(pl.BlockSpec((tile, wide), lambda h, j, m: (side(h, m) * tiles + j, 0)))
    shape = jax.ShapeDtypeStruct((rows // 2, columns), LOW)
    return pl.pallas_call(
        functools.partial(fold_kernel, len(pairs)),
        grid_spec=pltpu.PrefetchScalarGridSpec(
            num_scalar_prefetch=1,
            grid=(2, tiles),
            in_specs=specs + [pl.BlockSpec(memory_space=pl.ANY)] * len(others),
            out_specs=[
                pl.BlockSpec((tile, columns), lambda h, j, m: (j * (1 - h) + (tiles - 1) * h, 0)),
                pl.BlockSpec((tile, columns), lambda h, j, m: (j * h, 0)),
            ],
        ),
        out_shape=[shape, shape],
        compiler_params=params(),
        cost_estimate=cost(rows * columns, 6 * rows * columns),
    )(
        jnp.stack([base, bit]).astype(jnp.int32),
        *[value for pair in pairs for value in pair],
        *others,
    )


def normed_kernel(q_ref, kv_ref, wq_ref, wkv_ref, rows_ref, *rest):
    out_ref, dgain_ref = rest[-2:]
    grad = dot_nt(q_ref[...], wq_ref[...]) + dot_nt(kv_ref[...], wkv_ref[...])
    out_ref[...] = grad.astype(LOW)
    dgain_ref[...] = jnp.sum(grad * rows_ref[...].astype(F32), axis=0, keepdims=True)


def normed_back(grad_q, grad_kv, w_q, w_kv, rows, others):
    block, width = rows.shape
    tile = 512
    column = lambda i: (0, i)
    return pl.pallas_call(
        normed_kernel,
        grid=(width // tile,),
        in_specs=[
            full(grad_q.shape),
            full(grad_kv.shape),
            pl.BlockSpec((tile, w_q.shape[1]), lambda i: (i, 0)),
            pl.BlockSpec((tile, w_kv.shape[1]), lambda i: (i, 0)),
            pl.BlockSpec((block, tile), column),
        ]
        + [pl.BlockSpec(memory_space=pl.ANY)] * len(others),
        out_specs=[pl.BlockSpec((block, tile), column), pl.BlockSpec((1, tile), column)],
        out_shape=[
            jax.ShapeDtypeStruct((block, width), LOW),
            jax.ShapeDtypeStruct((1, width), F32),
        ],
        compiler_params=params(),
        cost_estimate=cost(2 * block * width * (w_q.shape[1] + w_kv.shape[1]), 12e6),
    )(grad_q, grad_kv, w_q, w_kv, rows, *others)


def pack_kernel(experts, router_ref, attn_ref, gain_ref, mlp_ref, q_ref, k_ref, *rest):
    out_ref, rows_ref = rest[-2:]
    size = q_ref.shape[1]
    rows_ref[:experts] = router_ref[:experts]
    rows_ref[experts:] = jnp.zeros_like(rows_ref[experts:])
    rows_ref[experts : experts + 1] = attn_ref[...] / gain_ref[...]
    rows_ref[experts + 1 : experts + 2] = mlp_ref[...]
    rows_ref[experts + 2 : experts + 3, :size] = q_ref[...]
    rows_ref[experts + 2 : experts + 3, size : 2 * size] = k_ref[...]
    out_ref[...] = rows_ref[...].astype(LOW)


def pack_small(experts, router, attn, gain, mlp, q, k, others):
    width = attn.shape[1]
    shape = (-(-(experts + 3) // 16) * 16, width)
    operands = [router, attn, gain[None], mlp, q, k]
    return pl.pallas_call(
        functools.partial(pack_kernel, experts),
        grid=(1,),
        in_specs=[full(value.shape) for value in operands]
        + [pl.BlockSpec(memory_space=pl.ANY)] * len(others),
        out_specs=full(shape),
        out_shape=jax.ShapeDtypeStruct(shape, LOW),
        scratch_shapes=[pltpu.VMEM(shape, F32)],
        compiler_params=params(),
        cost_estimate=cost(shape[0] * width, 6 * shape[0] * width),
    )(*operands, *others)


def part_sum_kernel(parts_ref, *rest):
    total = parts_ref[0].astype(F32)
    for k in range(1, parts_ref.shape[0]):
        total += parts_ref[k].astype(F32)
    rest[-1][...] = total.astype(LOW)


def part_sum(parts, others):
    count, rows, columns = parts.shape
    tiles = 2
    return pl.pallas_call(
        part_sum_kernel,
        grid=(tiles,),
        in_specs=[pl.BlockSpec((count, rows // tiles, columns), lambda i: (0, i, 0))]
        + [pl.BlockSpec(memory_space=pl.ANY)] * len(others),
        out_specs=pl.BlockSpec((rows // tiles, columns), lambda i: (i, 0)),
        out_shape=jax.ShapeDtypeStruct((rows, columns), LOW),
        compiler_params=params(),
        cost_estimate=cost(count * rows * columns, 4 * count * rows * columns),
    )(parts, *others)


def widen_kernel(n_chunks, n_outs, at_ref, *refs):
    del at_ref
    outs = refs[-n_outs:]
    widths = [ref.shape[1] for ref in outs]
    for k in range(n_chunks):

        @pl.when(pl.program_id(0) == k)
        def _():
            first = 0
            for wide, out_ref in zip(widths, outs):
                out_ref[...] = refs[k][:, first : first + wide].astype(F32)
                first += wide


def widen(places, chunks, widths, others):
    rows, columns = chunks[0].shape
    count = len(chunks)
    return pl.pallas_call(
        functools.partial(widen_kernel, count, len(widths)),
        grid_spec=pltpu.PrefetchScalarGridSpec(
            num_scalar_prefetch=1,
            grid=(count,),
            in_specs=[full(chunk.shape) for chunk in chunks]
            + [pl.BlockSpec(memory_space=pl.ANY)] * len(others),
            out_specs=[pl.BlockSpec((rows, wide), lambda i, at: (at[i], 0)) for wide in widths],
        ),
        out_shape=[jax.ShapeDtypeStruct((count * rows, wide), F32) for wide in widths],
        compiler_params=params(),
        cost_estimate=cost(rows * columns, 6 * count * rows * columns),
    )(jnp.stack(places).astype(jnp.int32), *chunks, *others)


def swap_dp(rows):
    return lax.ppermute(rows, "dp", [(0, 1), (1, 0)])


def swap_context(rows, s):
    n = lax.axis_size("context")
    return lax.ppermute(rows, "context", [(i, i ^ s) for i in range(n)])


def dp_got(grad):
    d = lax.axis_index("dp")
    rows = grad.shape[0] // 2
    return swap_dp(lax.dynamic_slice_in_dim(grad, (1 - d) * rows, rows))


def plane_turns():
    d, c = lax.axis_index("dp"), lax.axis_index("context")
    low, high = lax.rem(c, 2), lax.div(c, 2)

    def swap(first, second):
        perm = [(i, i ^ first) for i in range(4)] + [(4 + i, 4 + (i ^ second)) for i in range(4)]
        return lambda rows: lax.ppermute(rows, GROUP_AXES, perm)

    return [
        (jnp.where(d == 0, low, high), swap(1, 2)),
        (jnp.where(d == 0, high, low), swap(2, 1)),
    ]


def plane_first(pairs, others):
    (bit_1, _), _ = plane_turns()
    return fold(pairs, lax.axis_index("dp"), bit_1, others)


def plane_second(send, keep, others):
    (_, swap_1), (bit_2, _) = plane_turns()
    return fold([(keep, swap_1(send))], jnp.int32(0), bit_2, others)


def plane_last(send, keep, others):
    _, (_, swap_2) = plane_turns()
    return pair_sum(keep, swap_2(send), others)


def plane_spread(own):
    (_, swap_1), (_, swap_2) = plane_turns()
    second = swap_2(own)
    return [own, second, swap_1(own), swap_1(second)]


def quarter_places(rank):
    d = lax.axis_index("dp")
    c = lax.axis_index("context")
    low, high = lax.rem(c, 2), lax.div(c, 2)
    places = []
    for core in (d, 1 - d):
        bit_1 = jnp.where(core == 0, low, high)
        bit_2 = jnp.where(core == 0, high, low)
        for flip_1, flip_2 in ((0, 0), (0, 1), (1, 0), (1, 1)):
            places.append(4 * core + rank(core, bit_1 ^ flip_1, bit_2 ^ flip_2))
    return places


def widen_all(quarters, places, widths, others):
    return widen(places, quarters + [swap_dp(part) for part in quarters], widths, others)


def arrival_order(n):
    return [sorted(range(n), key=lambda j: (abs(j - i), j)) for i in range(n)]


def choose(index, options):
    distinct = []
    for option in options:
        if option is not None and not any(option is other for other in distinct):
            distinct.append(option)
    result = distinct[0]
    for option in distinct[1:]:
        mask = functools.reduce(
            jnp.logical_or, [index == i for i, other in enumerate(options) if other is option]
        )
        result = jnp.where(mask, option, result)
    return result


def line_gather(chunk):
    return line_steps({0: chunk}, 1, lax.axis_size("expert"))


def line_steps(found, first, stop):
    n = lax.axis_size("expert")
    found = dict(found)
    for s in range(first, stop):
        found[-s] = lax.ppermute(
            found[1 - s], "expert", [(i, i + 1) for i in range(s - 1, n - 1)]
        )
        found[s] = lax.ppermute(found[s - 1], "expert", [(i + 1, i) for i in range(n - s)])
    return found


def context_gather(rows):
    n = lax.axis_size("context")
    c = lax.axis_index("context")
    found = {0: rows}
    for s in range(1, n):
        found[s] = lax.ppermute(rows, "context", [(i, i ^ s) for i in range(n)])
    return jnp.concatenate([choose(c, [found[i ^ j] for i in range(n)]) for j in range(n)], axis=0)


def zero_of(*others):
    return functools.reduce(
        jnp.add,
        [
            lax.slice(other, (0,) * other.ndim, (1,) * other.ndim).reshape(()).astype(F32) * 0.0
            for other in others
        ],
    )


def after(value, *others):
    return (value.astype(F32) + zero_of(*others)).astype(value.dtype)


def on_device(
    layer_input,
    grad_output,
    attn_gain,
    query_weight,
    key_weight,
    value_weight,
    q_gain,
    k_gain,
    output_weight,
    mlp_gain,
    router,
    w_gate,
    w_up,
    w_down,
    routes,
    half_order,
):
    n_context = lax.axis_size("context")
    n_expert = lax.axis_size("expert")
    n_groups = lax.axis_size(GROUP_AXES)
    tok_dev, width = layer_input.shape[1:]
    size = q_gain.shape[0]
    kv_total = key_weight.shape[1] * n_expert
    group_dev = n_expert // (kv_total // size)
    kv_index = lax.axis_index("expert") // group_dev
    block = tok_dev * n_expert
    seq = block * n_context
    half = block // 2
    experts = router.shape[1]
    exp_dev = w_gate.shape[0]
    top = routes.shape[2]
    capacity = max(2, (tok_dev * top * 9 + 8 * experts - 1) // (8 * experts))
    scale = size ** (-0.5)

    seq_rows = jnp.arange(seq, dtype=jnp.int32)
    context = lax.axis_index("context")
    own_halves = lax.dynamic_slice_in_dim(half_order, 2 * context, 2)
    own_pos = (own_halves[:, None] * half + jnp.arange(half, dtype=jnp.int32)[None]).reshape(-1)
    per_half = half // TILE
    tile_pos = (half_order[:, None] * per_half + jnp.arange(per_half, dtype=jnp.int32)).reshape(-1)
    kidx = jnp.sum(
        (tile_pos[None, :] == jnp.arange(seq // TILE, dtype=jnp.int32)[:, None])
        * jnp.arange(seq // TILE, dtype=jnp.int32)[None, :],
        axis=1,
    ).astype(jnp.int32)
    qpos = lax.dynamic_slice_in_dim(tile_pos, context * (block // TILE), block // TILE)
    entry = jnp.arange(size)
    freq = jnp.power(THETA, -(2 * (entry % (size // 2))).astype(F32) / size)
    angles = own_pos.astype(F32)[:, None] * freq[None, :]
    cos2 = jnp.cos(angles)
    sin2 = jnp.sin(angles) * jnp.where(entry < size // 2, -1.0, 1.0)[None, :]

    place = lax.axis_index("expert")
    place_1 = place.astype(jnp.int32)[None]
    lanes = -(-2 * experts // 128) * 128
    mask = jnp.any(
        routes[0][:, :, None] == jnp.arange(lanes, dtype=jnp.int32)[None, None, :], axis=1
    )
    mask_wide = mask.astype(F32)
    router_rows = router.T

    x_low = layer_input[0]
    x_normal, _ = norm_parts(x_low.astype(F32))
    normed_found = line_gather((x_normal * attn_gain).astype(LOW))
    if group_dev == 1:
        kv_weights = jnp.concatenate([key_weight, value_weight], axis=1)
    else:
        key_whole = lax.all_gather(key_weight, "expert", axis=1, tiled=True)
        value_whole = lax.all_gather(value_weight, "expert", axis=1, tiled=True)
        kv_weights = jnp.concatenate(
            [
                lax.dynamic_slice_in_dim(key_whole, kv_index * size, size, 1),
                lax.dynamic_slice_in_dim(value_whole, kv_index * size, size, 1),
            ],
            axis=1,
        )
    grad_low = grad_output[0]
    normed_rows, own_kv, key_proj, grad_wide = project_keys(
        place_1,
        normed_found,
        kv_weights,
        k_gain,
        cos2,
        sin2,
        scale * LOG2E,
        grad_low,
        mask_wide,
    )
    grad_col = lax.all_gather(grad_wide, "expert", axis=0, tiled=True)
    kv_whole = context_gather(own_kv)
    queries, query_proj = project_queries(normed_rows, query_weight, q_gain, cos2, sin2)

    n_half = n_expert // 2
    order_here = jnp.asarray(arrival_order(n_expert), jnp.int32)[place]
    turn_here = jnp.sum(
        (order_here[:, None] == jnp.arange(n_expert, dtype=jnp.int32)[None, :])
        * jnp.arange(n_expert, dtype=jnp.int32)[:, None],
        axis=0,
    ).astype(jnp.int32)
    meta = jnp.concatenate([place_1, turn_here, order_here])
    grad_sent, spreads, back_tables = make_tables(
        meta, grad_col, width, n_groups, n_half, capacity, []
    )

    def swap_plane(rows):
        parts = rows.reshape(n_groups, -1, rows.shape[1])
        parts = lax.all_to_all(parts, GROUP_AXES, split_axis=0, concat_axis=0, tiled=True)
        return parts.reshape(rows.shape)

    attended, inverse = attend(qpos, kidx, queries, kv_whole, [])
    attn_part = out_dot(attended, output_weight, [grad_col])
    attn_rows = lax.psum_scatter(attn_part, "expert", scatter_dimension=0, tiled=True)

    grad_x = swap_plane(grad_sent)
    act_pull = dot_nt(grad_x, w_down[0]).reshape(n_groups, 2, n_half * capacity, -1)

    hidden, mixed, probs = route_rows(
        x_low, attn_rows, mlp_gain, router_rows, mask_wide, experts, []
    )

    who = (lax.axis_index(ALL_AXES) * exp_dev).astype(jnp.int32)[None]
    mixed_found = line_gather(mixed)
    near = spread_rows(place_1, spreads[0], mixed_found, range(n_half), [grad_x])
    x_near = swap_plane(near)
    worked_near = run_expert(who, x_near, w_gate[0], w_up[0], act_pull, 0, experts)
    far = spread_rows(place_1, spreads[1], mixed_found, range(n_half, n_expert), [x_near])
    x_far = swap_plane(far)
    worked_far = run_expert(who, x_far, w_gate[0], w_up[0], act_pull, 1, experts)
    xs = [x_near, x_far]
    acts, gate_lows, up_lows, copies = (list(pair) for pair in zip(worked_near, worked_far))
    back_far = swap_plane(copies[1])
    back_near = swap_plane(copies[0])
    join = lambda parts: jnp.concatenate(parts, axis=0)
    x_all = join([x[:, :width] for x in xs])
    grad_w_gate = dot_tn(x_all, join(gate_lows))
    grad_w_up = dot_tn(x_all, join(up_lows))
    grad_by_round = jnp.swapaxes(
        grad_x.reshape(n_groups, 2, n_half * capacity, width), 0, 1
    ).reshape(-1, width)
    grad_w_down = dot_tn(join(acts), grad_by_round)
    copies_col = combine_rows(
        meta, back_tables, [back_near, back_far], n_half, [grad_w_gate, grad_w_up]
    )
    copies_sum = lax.psum_scatter(copies_col, "expert", scatter_dimension=0, tiled=True)

    returned = [dot_nn(act, w_down[0]).astype(LOW) for act in acts]
    returned_near = swap_plane(returned[0])

    grad_hidden, grad_hidden_low, grad_mlp_gain, grad_router = route_back(
        copies_sum,
        grad_low,
        hidden,
        mlp_gain,
        router_rows,
        mask_wide,
        probs,
        experts,
        [returned_near, grad_w_down],
    )

    returned_far = swap_plane(returned[1])
    grad_attn = lax.all_gather(grad_hidden_low, "expert", axis=0, tiled=True)
    grad_o, centre = grad_attended(
        grad_attn, output_weight, attended, inverse, [returned_far]
    )
    combined = combine_rows(meta, back_tables, [returned_near, returned_far], n_half, [])
    output_rows = lax.psum_scatter(combined, "expert", scatter_dimension=0, tiled=True)
    w_out = token_dot(attended, grad_attn, [combined])
    w_out_parts = swap_plane(w_out)
    grad_kv, grad_q, grad_q_gain = attend_back(
        qpos,
        kidx,
        queries,
        grad_o,
        centre,
        kv_whole,
        query_proj,
        q_gain,
        cos2,
        sin2,
        [w_out],
    )
    kv_parts = lax.all_to_all(
        grad_kv.astype(LOW).reshape(n_context, block, 2 * size),
        "context",
        split_axis=0,
        concat_axis=0,
        tiled=True,
    )
    w_query = token_dot(normed_rows, grad_q, [w_out_parts])
    w_query_got = dp_got(w_query)
    output_rows = hidden + output_rows.astype(F32) + zero_of(w_query)

    kv_grads, grad_k_gain = kv_back(
        kv_parts, key_proj, k_gain, cos2, sin2, scale, [w_query]
    )
    w_out_quarters = plane_spread(part_sum(w_out_parts.reshape(n_groups, -1, width), [kv_parts]))
    w_kv = token_dot(normed_rows, kv_grads, [])
    pairs = [(w_query, w_query_got)]
    widths = [query_weight.shape[1]]
    if group_dev == 1:
        pairs.append((w_kv, dp_got(w_kv)))
        widths += [key_weight.shape[1], value_weight.shape[1]]
    send, keep = plane_first(pairs, w_out_quarters)

    grad_normed, gain_rows = normed_back(
        grad_q, kv_grads, query_weight, kv_weights, normed_rows, [keep]
    )
    (grad_w_out,) = widen_all(
        w_out_quarters,
        quarter_places(lambda core, b1, b2: jnp.where(core == 0, b1 + 2 * b2, 2 * b1 + b2)),
        [width],
        [],
    )
    second_send, second_keep = plane_second(send, keep, [grad_w_out, grad_normed])
    quarter = plane_last(second_send, second_keep, [output_rows])
    quarters = plane_spread(quarter)
    grad_normed = lax.psum_scatter(grad_normed, "expert", scatter_dimension=0, tiled=True)
    grad_input = input_back(grad_normed, x_low, attn_gain, grad_hidden)
    small = pack_small(
        experts,
        grad_router,
        gain_rows,
        attn_gain,
        grad_mlp_gain,
        grad_q_gain,
        grad_k_gain,
        [],
    )
    steps = [second_send, quarter, quarters[1], quarters[3]]
    doublings = [(axis, 2**k) for axis in ("dp", "context", "expert") for k in range(5)]
    doublings = [(axis, s) for axis, s in doublings if s < lax.axis_size(axis)]
    for k, (axis, s) in enumerate(doublings):
        n = lax.axis_size(axis)
        got = lax.ppermute(small, axis, [(i, i ^ s) for i in range(n)])
        small = pair_sum(small, got, steps[k : k + 1])
    small_sum = small.astype(F32)
    grad_w_query, *more = widen_all(
        quarters, quarter_places(lambda core, b1, b2: 2 * b1 + b2), widths, [grad_input]
    )
    if group_dev == 1:
        grad_w_key, grad_w_value = more
    else:
        blank = jnp.zeros((width, kv_total), LOW)
        pieces = []
        for part in (w_kv[:, :size], w_kv[:, size:]):
            padded = lax.dynamic_update_slice(blank, part, (0, kv_index * size))
            pieces.append(lax.psum_scatter(padded, "expert", scatter_dimension=1, tiled=True))
        grad_w_key, grad_w_value = (lax.psum(piece, GROUP_AXES).astype(F32) for piece in pieces)
    grad_attn_gain, grad_mlp_gain = small_sum[experts], small_sum[experts + 1]
    grad_q_gain = small_sum[experts + 2, :size]
    grad_k_gain = small_sum[experts + 2, size : 2 * size]
    return (
        output_rows.astype(LOW)[None],
        grad_input[None],
        grad_attn_gain,
        grad_w_query,
        grad_w_key,
        grad_w_value,
        grad_q_gain,
        grad_k_gain,
        grad_w_out,
        grad_mlp_gain,
        small_sum[:experts].T,
        grad_w_gate[None],
        grad_w_up[None],
        grad_w_down[None],
    )


def solution(mesh):
    rows = P("dp", ("context", "expert"), None)
    expert = P(ALL_AXES, None, None)
    columns = P(None, "expert")
    in_specs = (
        rows,
        rows,
        P(),
        columns,
        columns,
        columns,
        P(),
        P(),
        P("expert", None),
        P(),
        P(),
        expert,
        expert,
        expert,
        rows,
        P(),
    )
    out_specs = (
        rows,
        rows,
        P(),
        columns,
        columns,
        columns,
        P(),
        P(),
        P("expert", None),
        P(),
        P(),
        expert,
        expert,
        expert,
    )
    return jax.shard_map(
        on_device, mesh=mesh, in_specs=in_specs, out_specs=out_specs, check_vma=False
    )
```

```python
import functools
import math

import jax
import jax.numpy as jnp
from jax import lax
from jax.experimental import pallas as pl
from jax.experimental.pallas import tpu as pltpu
from jax.sharding import PartitionSpec as P

EPS = 1e-06
THETA = 1000000.0
TILE = 256
PIECE = 128
VMEM_BYTES = 56 * 1024 * 1024
LOG2E = math.log2(math.e)
LOW = jnp.bfloat16
F32 = jnp.float32
ALL_AXES = ("dp", "context", "expert")
GROUP_AXES = ("dp", "context")


def dot_nn(a, b):
    return lax.dot_general(a, b, (((1,), (0,)), ((), ())), preferred_element_type=F32)


def dot_nt(a, b):
    return lax.dot_general(a, b, (((1,), (1,)), ((), ())), preferred_element_type=F32)


def dot_tn(a, b):
    return lax.dot_general(a, b, (((0,), (0,)), ((), ())), preferred_element_type=F32)


def params(**more):
    return pltpu.CompilerParams(vmem_limit_bytes=VMEM_BYTES, **more)


def cost(flops, nbytes, exps=0):
    return pl.CostEstimate(flops=int(flops), bytes_accessed=int(nbytes), transcendentals=int(exps))


def head_forward(u, gain, cos2, sin2):
    rr = lax.rsqrt(jnp.mean(u * u, axis=-1, keepdims=True) + EPS)
    y = u * rr * gain
    return y * cos2 + pltpu.roll(y, 64, 1) * sin2


def head_backward(gy, u, gain, cos2, sin2):
    g = gy * cos2 - pltpu.roll(gy, 64, 1) * sin2
    rr = lax.rsqrt(jnp.mean(u * u, axis=-1, keepdims=True) + EPS)
    n = u * rr
    gn = g * gain
    grad = rr * (gn - n * jnp.mean(gn * n, axis=-1, keepdims=True))
    return grad, jnp.sum(g * n, axis=0, keepdims=True)


def query_kernel(x_ref, w_ref, gain_ref, cos_ref, sin_ref, rot_ref, proj_ref):
    tiles, heads, rows, size = rot_ref.shape
    acc = dot_nn(x_ref[...], w_ref[...])
    for h in range(heads):
        u = acc[:, h * size : (h + 1) * size]
        rot = head_forward(u, gain_ref[...], cos_ref[...], sin_ref[...])
        proj_ref[:, h] = u.reshape(tiles, rows, size)
        rot_ref[:, h] = rot.astype(LOW).reshape(tiles, rows, size)


def project_queries(normed, weight, gain, cos2, sin2):
    block, width = normed.shape
    size = cos2.shape[1]
    heads = weight.shape[1] // size
    tiles = block // TILE
    whole = lambda i: (0, 0)
    per = lambda i: (0, i, 0, 0)
    shape = (tiles, heads, TILE, size)
    return pl.pallas_call(
        query_kernel,
        grid=(heads // 2,),
        in_specs=[
            pl.BlockSpec((block, width), whole),
            pl.BlockSpec((width, 2 * size), lambda i: (0, i)),
            pl.BlockSpec((1, size), whole),
            pl.BlockSpec((block, size), whole),
            pl.BlockSpec((block, size), whole),
        ],
        out_specs=[pl.BlockSpec((tiles, 2, TILE, size), per)] * 2,
        out_shape=[jax.ShapeDtypeStruct(shape, LOW), jax.ShapeDtypeStruct(shape, F32)],
        compiler_params=params(),
        cost_estimate=cost(2 * block * width * heads * size, 12e6),
    )(normed, weight, gain[None], cos2, sin2)


def put_in_order(place, refs, out_ref):
    n = (len(refs) + 1) // 2
    rows = refs[0].shape[0]
    for distance in range(1 - n, n):
        ref = refs[distance + n - 1]
        at = place + distance

        @pl.when(jnp.logical_and(at >= 0, at < n))
        def _():
            out_ref[pl.ds(pl.multiple_of(at * rows, rows), rows), :] = ref[...]


def chunk_list(found):
    n = (len(found) + 1) // 2
    return [found[distance] for distance in range(1 - n, n)]


def key_kernel(factor, n_chunks, place_ref, *refs):
    w_ref, gain_ref, cos_ref, sin_ref, g_ref, mask_ref = refs[n_chunks:-4]
    rows_ref, kv_ref, proj_ref, wide_ref = refs[-4:]
    size = proj_ref.shape[1]
    width = g_ref.shape[1]
    put_in_order(place_ref[0], refs[:n_chunks], rows_ref)
    wide_ref[:, :width] = g_ref[...]
    wide_ref[:, width:] = mask_ref[...].astype(LOW)
    acc = dot_nn(rows_ref[...], w_ref[...])
    u = acc[:, :size]
    rot = head_forward(u, gain_ref[...], cos_ref[...], sin_ref[...])
    proj_ref[...] = u
    kv_ref[:, :size] = (rot * factor).astype(LOW)
    kv_ref[:, size:] = acc[:, size:].astype(LOW)


def full(shape):
    return pl.BlockSpec(shape, lambda *_: (0,) * len(shape))


def project_keys(place, found, weight, gain, cos2, sin2, factor, g, mask):
    chunks = chunk_list(found)
    rows, width = chunks[0].shape
    block, size = cos2.shape
    operands = [*chunks, weight, gain[None], cos2, sin2, g, mask]
    shapes = [
        jax.ShapeDtypeStruct((block, width), LOW),
        jax.ShapeDtypeStruct((block, 2 * size), LOW),
        jax.ShapeDtypeStruct((block, size), F32),
        jax.ShapeDtypeStruct((rows, width + mask.shape[1]), LOW),
    ]
    return pl.pallas_call(
        functools.partial(key_kernel, factor, len(chunks)),
        grid_spec=pltpu.PrefetchScalarGridSpec(
            num_scalar_prefetch=1,
            grid=(1,),
            in_specs=[full(x.shape) for x in operands],
            out_specs=[full(x.shape) for x in shapes],
        ),
        out_shape=shapes,
        compiler_params=params(),
        cost_estimate=cost(4 * block * width * size, 8e6),
    )(place, *operands)


def in_order(last, step):
    lax.fori_loop(0, lax.div(last, 2), lambda p, c: (step([2 * p, 2 * p + 1], False), c)[1], 0)

    @pl.when(lax.rem(last, 2) == 1)
    def _():
        step([last - 1, last], True)

    @pl.when(lax.rem(last, 2) == 0)
    def _():
        step([last], True)


def attend_kernel(qpos_ref, kidx_ref, q_ref, kv_ref, *rest):
    out_ref, inv_ref, acc_ref = rest[-3:]
    heads, rows, size = q_ref.shape[1:]
    acc_ref[...] = jnp.zeros_like(acc_ref)

    def step(places, masked):
        starts = [pl.multiple_of(kidx_ref[place] * rows, rows) for place in places]
        count = len(places) * rows
        keys = jnp.concatenate([kv_ref[pl.ds(start, rows), :size] for start in starts], axis=0)
        values = jnp.concatenate([kv_ref[pl.ds(start, rows), size:] for start in starts], axis=0)
        values = jnp.concatenate([values, jnp.ones((count, size), LOW)], axis=1)
        for h in range(heads):
            for first in range(0, rows, PIECE):
                part = slice(first, first + PIECE)
                e = jnp.exp2(dot_nt(q_ref[0, h, part], keys))
                if masked:
                    qi = lax.broadcasted_iota(jnp.int32, e.shape, 0) + first
                    ki = lax.broadcasted_iota(jnp.int32, e.shape, 1) - (count - rows)
                    e = jnp.where(ki <= qi, e, 0.0)
                acc_ref[h, part] += dot_nn(e.astype(LOW), values)

    in_order(qpos_ref[pl.program_id(0)], step)
    for h in range(heads):
        inv = 1.0 / acc_ref[h, :, size:]
        inv_ref[0, h] = inv
        out_ref[:, h * size : (h + 1) * size] = (acc_ref[h, :, :size] * inv).astype(LOW)


def attend(qpos, kidx, queries, kv, others):
    tiles, heads, rows, size = queries.shape
    seq = kv.shape[0]
    return pl.pallas_call(
        attend_kernel,
        grid_spec=pltpu.PrefetchScalarGridSpec(
            num_scalar_prefetch=2,
            grid=(tiles,),
            in_specs=[
                pl.BlockSpec((1, heads, rows, size), lambda i, a, b: (i, 0, 0, 0)),
                pl.BlockSpec((seq, 2 * size), lambda i, a, b: (0, 0)),
            ]
            + [pl.BlockSpec(memory_space=pl.ANY)] * len(others),
            out_specs=[
                pl.BlockSpec((rows, heads * size), lambda i, a, b: (i, 0)),
                pl.BlockSpec((1, heads, rows, size), lambda i, a, b: (i, 0, 0, 0)),
            ],
            scratch_shapes=[pltpu.VMEM((heads, rows, 2 * size), F32)],
        ),
        out_shape=[
            jax.ShapeDtypeStruct((tiles * rows, heads * size), LOW),
            jax.ShapeDtypeStruct((tiles, heads, rows, size), F32),
        ],
        compiler_params=params(),
        cost_estimate=cost(
            6 * tiles * rows * heads * seq * size, 8e6, tiles * rows * heads * seq
        ),
    )(qpos, kidx, queries, kv, *others)


def grad_out_kernel(rows_ref, w_ref, o_ref, inv_ref, *rest):
    do_ref, centre_ref = rest[-2:]
    tiles, heads, rows, size = do_ref.shape
    acc = dot_nt(rows_ref[...], w_ref[...])
    for t in range(tiles):
        for h in range(heads):
            part = slice(t * rows, (t + 1) * rows), slice(h * size, (h + 1) * size)
            low = (acc[part] * inv_ref[t, h]).astype(LOW)
            do_ref[t, h] = low
            product = low.astype(F32) * o_ref[part].astype(F32)
            centre = jnp.sum(jnp.transpose(product), axis=0, keepdims=True)
            centre_ref[t, h] = jnp.broadcast_to(centre, (8, rows))


def grad_attended(grad_rows, weight, attended, inverse, others):
    tiles, heads, rows, size = inverse.shape
    block, width = grad_rows.shape
    return pl.pallas_call(
        grad_out_kernel,
        grid=(heads // 2,),
        in_specs=[
            pl.BlockSpec((block, width), lambda i: (0, 0)),
            pl.BlockSpec((2 * size, width), lambda i: (i, 0)),
            pl.BlockSpec((block, 2 * size), lambda i: (0, i)),
            pl.BlockSpec((tiles, 2, rows, size), lambda i: (0, i, 0, 0)),
        ]
        + [pl.BlockSpec(memory_space=pl.ANY)] * len(others),
        out_specs=[
            pl.BlockSpec((tiles, 2, rows, size), lambda i: (0, i, 0, 0)),
            pl.BlockSpec((tiles, 2, 8, rows), lambda i: (0, i, 0, 0)),
        ],
        out_shape=[
            jax.ShapeDtypeStruct((tiles, heads, rows, size), LOW),
            jax.ShapeDtypeStruct((tiles, heads, 8, rows), F32),
        ],
        compiler_params=params(),
        cost_estimate=cost(2 * block * width * heads * size, 12e6),
    )(grad_rows, weight, attended, inverse, *others)


def attend_back_kernel(
    qpos_ref,
    kidx_ref,
    q_ref,
    do_ref,
    centre_ref,
    kv_ref,
    proj_ref,
    gain_ref,
    cos_ref,
    sin_ref,
    *rest,
):
    dkv_ref, dq_ref, dgain_ref, acc_ref, e_ref, ds_ref = rest[-6:]
    heads, rows, size = q_ref.shape[1:]

    @pl.when(pl.program_id(0) == 0)
    def _():
        dkv_ref[...] = jnp.zeros_like(dkv_ref)
        dgain_ref[...] = jnp.zeros_like(dgain_ref)

    acc_ref[...] = jnp.zeros_like(acc_ref)

    def step(places, masked):
        starts = [pl.multiple_of(kidx_ref[place] * rows, rows) for place in places]
        count = len(places) * rows
        keys = jnp.concatenate([kv_ref[pl.ds(start, rows), :size] for start in starts], axis=0)
        values = jnp.concatenate([kv_ref[pl.ds(start, rows), size:] for start in starts], axis=0)
        for h in range(heads):
            query, grad = q_ref[0, h], do_ref[0, h]
            centre = centre_ref[0, h, 0:1]
            columns = slice(h * rows, (h + 1) * rows)
            for first in range(0, count, PIECE):
                part = slice(first, first + PIECE)
                e = jnp.exp2(dot_nt(keys[part], query))
                if masked and first >= count - rows:
                    ki = lax.broadcasted_iota(jnp.int32, e.shape, 0) + (first - (count - rows))
                    qi = lax.broadcasted_iota(jnp.int32, e.shape, 1)
                    e = jnp.where(ki <= qi, e, 0.0)
                ds = e * (dot_nt(values[part], grad) - centre)
                e_ref[part, columns] = e.astype(LOW)
                ds_ref[part, columns] = ds.astype(LOW)
            acc_ref[h] += dot_tn(ds_ref[:count, columns], keys)
        dk = dot_nn(ds_ref[:count], q_ref[0].reshape(heads * rows, size))
        dv = dot_nn(e_ref[:count], do_ref[0].reshape(heads * rows, size))
        for k, start in enumerate(starts):
            dkv_ref[pl.ds(start, rows), :size] += dk[k * rows : (k + 1) * rows]
            dkv_ref[pl.ds(start, rows), size:] += dv[k * rows : (k + 1) * rows]

    in_order(qpos_ref[pl.program_id(0)], step)
    total = jnp.zeros((1, size), F32)
    for h in range(heads):
        grad, gain_part = head_backward(
            acc_ref[h] * (1.0 / LOG2E), proj_ref[0, h], gain_ref[...], cos_ref[...], sin_ref[...]
        )
        dq_ref[:, h * size : (h + 1) * size] = grad.astype(LOW)
        total += gain_part
    dgain_ref[...] += total


def attend_back(qpos, kidx, queries, grads, centre, kv, proj, gain, cos2, sin2, others):
    tiles, heads, rows, size = queries.shape
    seq = kv.shape[0]
    per = pl.BlockSpec((1, heads, rows, size), lambda i, a, b: (i, 0, 0, 0))
    flat = lambda i, a, b: (0, 0)
    rowwise = lambda i, a, b: (i, 0)
    return pl.pallas_call(
        attend_back_kernel,
        grid_spec=pltpu.PrefetchScalarGridSpec(
            num_scalar_prefetch=2,
            grid=(tiles,),
            in_specs=[
                per,
                per,
                pl.BlockSpec((1, heads, 8, rows), lambda i, a, b: (i, 0, 0, 0)),
                pl.BlockSpec((seq, 2 * size), flat),
                per,
                pl.BlockSpec((1, size), flat),
                pl.BlockSpec((rows, size), rowwise),
                pl.BlockSpec((rows, size), rowwise),
            ]
            + [pl.BlockSpec(memory_space=pl.ANY)] * len(others),
            out_specs=[
                pl.BlockSpec((seq, 2 * size), flat),
                pl.BlockSpec((rows, heads * size), rowwise),
                pl.BlockSpec((1, size), flat),
            ],
            scratch_shapes=[pltpu.VMEM((heads, rows, size), F32)]
            + [pltpu.VMEM((2 * rows, heads * rows), LOW)] * 2,
        ),
        out_shape=[
            jax.ShapeDtypeStruct((seq, 2 * size), F32),
            jax.ShapeDtypeStruct((tiles * rows, heads * size), LOW),
            jax.ShapeDtypeStruct((1, size), F32),
        ],
        compiler_params=params(),
        cost_estimate=cost(
            15 * tiles * rows * heads * seq * size, 12e6, tiles * rows * heads * seq
        ),
    )(qpos, kidx, queries, grads, centre, kv, proj, gain[None], cos2, sin2, *others)


def out_kernel(a_ref, b_ref, *rest):
    rest[-1][...] = dot_nn(a_ref[...], b_ref[...]).astype(LOW)


def out_dot(a, b, others):
    block, inner = a.shape
    columns = b.shape[1]
    tile = min(columns, 512)
    return pl.pallas_call(
        out_kernel,
        grid=(columns // tile,),
        in_specs=[
            pl.BlockSpec((block, inner), lambda i: (0, 0)),
            pl.BlockSpec((inner, tile), lambda i: (0, i)),
        ]
        + [pl.BlockSpec(memory_space=pl.ANY)] * len(others),
        out_specs=pl.BlockSpec((block, tile), lambda i: (0, i)),
        out_shape=jax.ShapeDtypeStruct((block, columns), LOW),
        compiler_params=params(),
        cost_estimate=cost(2 * block * inner * columns, 8e6),
    )(a, b, *others)


def token_kernel(a_ref, b_ref, *rest):
    rest[-1][...] = dot_tn(a_ref[...], b_ref[...]).astype(LOW)


def token_dot(a, b, others):
    block, rows = a.shape
    columns = b.shape[1]
    tile = min(rows, 512)
    return pl.pallas_call(
        token_kernel,
        grid=(rows // tile,),
        in_specs=[
            pl.BlockSpec((block, tile), lambda i: (0, i)),
            pl.BlockSpec((block, columns), lambda i: (0, 0)),
        ]
        + [pl.BlockSpec(memory_space=pl.ANY)] * len(others),
        out_specs=pl.BlockSpec((tile, columns), lambda i: (i, 0)),
        out_shape=jax.ShapeDtypeStruct((rows, columns), LOW),
        compiler_params=params(),
        cost_estimate=cost(2 * block * rows * columns, 6e6),
    )(a, b, *others)


def halves_kernel(d_ref, a_ref, b_ref, *rest):
    send_ref, keep_ref = rest[-2:]
    product = dot_tn(a_ref[...], b_ref[...]).astype(LOW)

    @pl.when(pl.program_id(0) == 0)
    def _():
        send_ref[...] = product

    @pl.when(pl.program_id(0) == 1)
    def _():
        keep_ref[...] = product


def token_halves(a, b, others):
    block, rows = a.shape
    columns = b.shape[1]
    tiles = 2
    tile = rows // (2 * tiles)
    d = lax.axis_index("dp").astype(jnp.int32)[None]
    half = jax.ShapeDtypeStruct((rows // 2, columns), LOW)
    return pl.pallas_call(
        halves_kernel,
        grid_spec=pltpu.PrefetchScalarGridSpec(
            num_scalar_prefetch=1,
            grid=(2, tiles),
            in_specs=[
                pl.BlockSpec(
                    (block, tile),
                    lambda h, j, d: (0, ((1 - d[0]) * (1 - h) + d[0] * h) * tiles + j),
                ),
                pl.BlockSpec((block, columns), lambda h, j, d: (0, 0)),
            ]
            + [pl.BlockSpec(memory_space=pl.ANY)] * len(others),
            out_specs=[
                pl.BlockSpec((tile, columns), lambda h, j, d: (j * (1 - h) + (tiles - 1) * h, 0)),
                pl.BlockSpec((tile, columns), lambda h, j, d: (j * h, 0)),
            ],
        ),
        out_shape=[half, half],
        compiler_params=params(),
        cost_estimate=cost(2 * block * rows * columns, 6e6),
    )(d, a, b, *others)


def split_low(value):
    high = value.astype(LOW)
    return high, (value - high.astype(F32)).astype(LOW)


def norm_parts(rows):
    rr = lax.rsqrt(jnp.mean(rows * rows, axis=-1, keepdims=True) + EPS)
    return rows * rr, rr


def norm_back(grad, normal, rr, gain):
    weighted = grad * gain
    return rr * (weighted - normal * jnp.mean(weighted * normal, axis=-1, keepdims=True))


def add_all(refs):
    return functools.reduce(jnp.add, [ref[...].astype(F32) for ref in refs])


def pad_rows(rows, count):
    if rows.shape[0] == count:
        return rows
    return jnp.concatenate(
        [rows, jnp.zeros((count - rows.shape[0], rows.shape[1]), rows.dtype)], axis=0
    )


def router_kernel(experts, *refs):
    x_ref, attn_ref, gain_ref, router_ref, mask_ref = refs[:5]
    hidden_ref, mixed_ref, probs_ref = refs[-3:]
    width = x_ref.shape[1]
    lanes = mask_ref.shape[1]
    hidden = add_all([x_ref, attn_ref])
    hidden_ref[...] = hidden
    mixed = (norm_parts(hidden)[0] * gain_ref[...]).astype(LOW)
    mixed_ref[:, :width] = mixed
    logits = dot_nt(mixed, pad_rows(router_ref[...], lanes))
    lane = lax.broadcasted_iota(jnp.int32, logits.shape, 1)
    logits = jnp.where(lane < experts, logits, -1e30)
    weights = jnp.exp(logits - jnp.max(logits, axis=1, keepdims=True))
    probs = weights / jnp.sum(weights, axis=1, keepdims=True)
    probs_ref[...] = probs
    chosen = probs * mask_ref[...]
    high, low = split_low(chosen / jnp.sum(chosen, axis=1, keepdims=True))
    both = high.astype(F32) + pltpu.roll(low.astype(F32), experts, 1)
    mixed_ref[:, width:] = both.astype(LOW)


def route_rows(x, attn, gain, router, mask, experts, others):
    tokens, width = x.shape
    lanes = mask.shape[1]
    operands = [x, attn, gain[None], router, mask]
    shapes = [
        jax.ShapeDtypeStruct((tokens, width), F32),
        jax.ShapeDtypeStruct((tokens, width + lanes), LOW),
        jax.ShapeDtypeStruct((tokens, lanes), F32),
    ]
    return pl.pallas_call(
        functools.partial(router_kernel, experts),
        grid=(1,),
        in_specs=[full(value.shape) for value in operands]
        + [pl.BlockSpec(memory_space=pl.ANY)] * len(others),
        out_specs=[full(shape.shape) for shape in shapes],
        out_shape=shapes,
        compiler_params=params(),
        cost_estimate=cost(2 * tokens * width * lanes, 5e6),
    )(*operands, *others)


def one_hot(slots, count, first):
    groups, tokens = slots.shape
    slot = lax.broadcasted_iota(jnp.int32, (groups, count, tokens), 1).astype(F32)
    same = slots[:, None, :] == slot + float(first)
    return jnp.where(same, 1.0, 0.0).reshape(groups * count, tokens)


def slot_kernel(capacity, meta_ref, col_ref, rows_ref, slots_ref):
    groups, block = slots_ref.shape
    rows, width = rows_ref.shape
    n = rows // groups // capacity
    tokens = block // n
    mask = col_ref[:, width:]
    lanes = mask.shape[1]
    padded = -(-groups // 16) * 16
    group = lax.broadcasted_iota(jnp.int32, (padded, lanes), 0)
    lane = lax.broadcasted_iota(jnp.int32, (padded, lanes), 1)
    wanted = jnp.logical_and(lane == group * n + meta_ref[0], group < groups)
    hits = dot_nt(jnp.where(wanted, 1.0, 0.0).astype(LOW), mask)
    before = lax.broadcasted_iota(jnp.int32, (tokens, tokens), 0)
    after_it = lax.broadcasted_iota(jnp.int32, (tokens, tokens), 1)
    earlier = jnp.where(before < after_it, 1.0, 0.0).astype(LOW)
    for z in range(n):
        hit = hits[:, z * tokens : (z + 1) * tokens]
        rank = dot_nn(hit.astype(LOW), earlier)
        turn = (meta_ref[1 + z] * capacity).astype(F32)
        slot = jnp.where(hit > 0.5, rank + turn, -1.0)
        slots_ref[:, z * tokens : (z + 1) * tokens] = slot[:groups]
    spread = one_hot(slots_ref[...], n * capacity, 0).astype(LOW)
    rows_ref[...] = dot_nn(spread, col_ref[:, :width]).astype(LOW)


def make_slots(meta, col, width, groups, capacity):
    block = col.shape[0]
    n = lax.axis_size("expert")
    shapes = [
        jax.ShapeDtypeStruct((groups * n * capacity, width), LOW),
        jax.ShapeDtypeStruct((groups, block), F32),
    ]
    return pl.pallas_call(
        functools.partial(slot_kernel, capacity),
        grid_spec=pltpu.PrefetchScalarGridSpec(
            num_scalar_prefetch=1,
            grid=(1,),
            in_specs=[full(col.shape)],
            out_specs=[full(shape.shape) for shape in shapes],
        ),
        out_shape=shapes,
        compiler_params=params(),
        cost_estimate=cost(2 * groups * n * capacity * block * width, 8e6),
    )(meta, col)


def table_kernel(capacity, n_half, meta_ref, slots_ref, near_ref, far_ref, near_back_ref, far_back_ref):
    n = 2 * n_half
    tokens = slots_ref.shape[1] // n
    cap_half = n_half * capacity
    for part, (to_ref, back_ref) in enumerate([(near_ref, near_back_ref), (far_ref, far_back_ref)]):
        pieces = []
        for k in range(n_half):
            start = pl.multiple_of(meta_ref[1 + n + part * n_half + k] * tokens, tokens)
            pieces.append(slots_ref[:, pl.ds(start, tokens)])
        spread = one_hot(jnp.concatenate(pieces, axis=1), cap_half, part * cap_half)
        to_ref[...] = spread.astype(LOW)
        back_ref[...] = jnp.transpose(spread).astype(LOW)


def make_tables(meta, slots, n_half, capacity):
    groups, block = slots.shape
    rows = groups * n_half * capacity
    shapes = [jax.ShapeDtypeStruct((rows, block // 2), LOW)] * 2
    shapes += [jax.ShapeDtypeStruct((block // 2, rows), LOW)] * 2
    outs = pl.pallas_call(
        functools.partial(table_kernel, capacity, n_half),
        grid_spec=pltpu.PrefetchScalarGridSpec(
            num_scalar_prefetch=1,
            grid=(1,),
            in_specs=[full(slots.shape)],
            out_specs=[full(shape.shape) for shape in shapes],
        ),
        out_shape=shapes,
        compiler_params=params(),
        cost_estimate=cost(8 * rows * block, 3e6),
    )(meta, slots)
    return outs[:2], outs[2:]


def spread_kernel(choices, place_ref, spread_ref, *refs):
    out_ref, rows_ref = refs[-2:]
    for k, by_place in enumerate(choices):
        for which in sorted(set(by_place)):
            hit = functools.reduce(
                jnp.logical_or,
                [place_ref[0] == i for i, other in enumerate(by_place) if other == which],
            )

            @pl.when(hit)
            def _():
                tokens = refs[which].shape[0]
                rows_ref[k * tokens : (k + 1) * tokens] = refs[which][...]

    out_ref[...] = dot_nn(spread_ref[...], rows_ref[...]).astype(LOW)


def spread_rows(place, spread, found, turns, others):
    n = lax.axis_size("expert")
    order = arrival_order(n)
    distances = sorted({order[i][turn] - i for i in range(n) for turn in turns})
    choices = [[distances.index(order[i][turn] - i) for i in range(n)] for turn in turns]
    chunks = [found[distance] for distance in distances]
    tokens, wide = chunks[0].shape
    rows = spread.shape[0]
    return pl.pallas_call(
        functools.partial(spread_kernel, choices),
        grid_spec=pltpu.PrefetchScalarGridSpec(
            num_scalar_prefetch=1,
            grid=(1,),
            in_specs=[full(spread.shape)]
            + [full(chunk.shape) for chunk in chunks]
            + [pl.BlockSpec(memory_space=pl.ANY)] * len(others),
            out_specs=full((rows, wide)),
            scratch_shapes=[pltpu.VMEM((len(turns) * tokens, wide), LOW)],
        ),
        out_shape=jax.ShapeDtypeStruct((rows, wide), LOW),
        compiler_params=params(),
        cost_estimate=cost(2 * rows * len(turns) * tokens * wide, 5e6),
    )(place, spread, *chunks, *others)


def router_back_kernel(experts, *refs):
    sum_ref, g_ref, hidden_ref, gain_ref, router_ref, mask_ref, probs_ref = refs[:7]
    grad_ref, low_ref, dgain_ref, drouter_ref = refs[-4:]
    width = g_ref.shape[1]
    lanes = mask_ref.shape[1]
    total = sum_ref[...].astype(F32)
    table = total[:, width:]
    mask, probs = mask_ref[...], probs_ref[...]
    grad_gates = (table + pltpu.roll(table, lanes - experts, 1)) * mask
    chosen = probs * mask
    chosen_sum = jnp.sum(chosen, axis=1, keepdims=True)
    mean = jnp.sum(grad_gates * (chosen / chosen_sum), axis=1, keepdims=True)
    centred = mask * (grad_gates - mean) / chosen_sum
    grad_logits = probs * (centred - jnp.sum(centred * chosen, axis=1, keepdims=True))
    high, low = split_low(grad_logits)
    router = pad_rows(router_ref[...], lanes)
    grad = total[:, :width] + dot_nn(high, router) + dot_nn(low, router)
    normal, rr = norm_parts(hidden_ref[...])
    mixed = (normal * gain_ref[...]).astype(LOW)
    drouter_ref[...] = dot_tn(high, mixed) + dot_tn(low, mixed)
    dgain_ref[...] = jnp.sum(grad * normal, axis=0, keepdims=True)
    grad_hidden = g_ref[...].astype(F32) + norm_back(grad, normal, rr, gain_ref[...])
    grad_ref[...] = grad_hidden
    low_ref[...] = grad_hidden.astype(LOW)


def route_back(summed, g, hidden, gain, router, mask, probs, experts, others):
    tokens, width = g.shape
    lanes = mask.shape[1]
    operands = [summed, g, hidden, gain[None], router, mask, probs]
    shapes = [
        jax.ShapeDtypeStruct((tokens, width), F32),
        jax.ShapeDtypeStruct((tokens, width), LOW),
        jax.ShapeDtypeStruct((1, width), F32),
        jax.ShapeDtypeStruct((lanes, width), F32),
    ]
    return pl.pallas_call(
        functools.partial(router_back_kernel, experts),
        grid=(1,),
        in_specs=[full(value.shape) for value in operands]
        + [pl.BlockSpec(memory_space=pl.ANY)] * len(others),
        out_specs=[full(shape.shape) for shape in shapes],
        out_shape=shapes,
        compiler_params=params(),
        cost_estimate=cost(8 * tokens * width * lanes, 8e6),
    )(*operands, *others)


def combine_kernel(n_half, meta_ref, near_table_ref, far_table_ref, near_ref, far_ref, *rest):
    del meta_ref
    turn = pl.program_id(0)

    @pl.when(turn < n_half)
    def _():
        rest[-1][...] = dot_nn(near_table_ref[...], near_ref[...]).astype(LOW)

    @pl.when(turn >= n_half)
    def _():
        rest[-1][...] = dot_nn(far_table_ref[...], far_ref[...]).astype(LOW)


def combine_rows(meta, tables, rows, n_half, others):
    tokens = tables[0].shape[0] // n_half
    slots, wide = rows[0].shape
    n = 2 * n_half
    return pl.pallas_call(
        functools.partial(combine_kernel, n_half),
        grid_spec=pltpu.PrefetchScalarGridSpec(
            num_scalar_prefetch=1,
            grid=(n,),
            in_specs=[
                pl.BlockSpec((tokens, slots), lambda i, m: (jnp.minimum(i, n_half - 1), 0)),
                pl.BlockSpec((tokens, slots), lambda i, m: (jnp.maximum(i - n_half, 0), 0)),
            ]
            + [full(value.shape) for value in rows]
            + [pl.BlockSpec(memory_space=pl.ANY)] * len(others),
            out_specs=pl.BlockSpec((tokens, wide), lambda i, m: (m[1 + n + i], 0)),
        ),
        out_shape=jax.ShapeDtypeStruct((n * tokens, wide), LOW),
        compiler_params=params(),
        cost_estimate=cost(2 * slots * n * tokens * wide, 10e6),
    )(meta, *tables, *rows, *others)


def expert_kernel(experts, who_ref, x_ref, gate_ref, up_ref, pull_ref, *rest):
    act_ref, dgate_ref, dup_ref, copy_ref = rest[-4:]
    width = gate_ref.shape[0]
    x = x_ref[:, :width]
    table = x_ref[:, width:].astype(F32)
    lane = lax.broadcasted_iota(jnp.int32, table.shape, 1)
    mine = who_ref[0]
    gate = jnp.sum(
        jnp.where(jnp.logical_or(lane == mine, lane == mine + experts), table, 0.0),
        axis=1,
        keepdims=True,
    )
    pre_gate = dot_nn(x, gate_ref[...])
    pre_up = dot_nn(x, up_ref[...])
    pull = pull_ref[...].reshape(pre_up.shape)
    sig = 1.0 / (1.0 + jnp.exp(-pre_gate))
    silu = pre_gate * sig
    act = silu * pre_up
    act_ref[...] = (act * gate).astype(LOW)
    high, low = split_low(jnp.sum(act * pull, axis=1, keepdims=True))
    pull = pull * gate
    dup = (pull * silu).astype(LOW)
    dgate = (pull * pre_up * (sig * (1.0 + pre_gate * (1.0 - sig)))).astype(LOW)
    dgate_ref[...] = dgate
    dup_ref[...] = dup
    copy_ref[:, :width] = (dot_nt(dgate, gate_ref[...]) + dot_nt(dup, up_ref[...])).astype(LOW)
    back = jnp.where(lane == mine, high.astype(F32), 0.0)
    back = jnp.where(lane == mine + experts, low.astype(F32), back)
    copy_ref[:, width:] = back.astype(LOW)


def run_expert(who, x, w_gate, w_up, pull, part, experts):
    rows, wide = x.shape
    width, hidden = w_gate.shape
    groups, _, slots, _ = pull.shape
    each = groups // 2
    tile = each * slots
    by_rows = lambda columns: pl.BlockSpec((tile, columns), lambda i, p: (i, 0))
    return pl.pallas_call(
        functools.partial(expert_kernel, experts),
        grid_spec=pltpu.PrefetchScalarGridSpec(
            num_scalar_prefetch=1,
            grid=(2,),
            in_specs=[
                by_rows(wide),
                full(w_gate.shape),
                full(w_up.shape),
                pl.BlockSpec((each, 1, slots, hidden), lambda i, p: (i, part, 0, 0)),
            ],
            out_specs=[by_rows(hidden), by_rows(hidden), by_rows(hidden), by_rows(wide)],
        ),
        out_shape=[jax.ShapeDtypeStruct((rows, hidden), LOW)] * 3
        + [jax.ShapeDtypeStruct((rows, wide), LOW)],
        compiler_params=params(),
        cost_estimate=cost(8 * rows * width * hidden, 20e6, rows * hidden),
    )(who, x, w_gate, w_up, pull)


def input_kernel(grad_ref, x_ref, gain_ref, more_ref, out_ref):
    normal, rr = norm_parts(x_ref[...].astype(F32))
    grad = grad_ref[...].astype(F32)
    out_ref[...] = more_ref[...] + norm_back(grad, normal, rr, gain_ref[...])


def input_back(grad, x, gain, more):
    tokens, width = x.shape
    operands = [grad, x, gain[None], more]
    return pl.pallas_call(
        input_kernel,
        grid=(1,),
        in_specs=[full(value.shape) for value in operands],
        out_specs=full(more.shape),
        out_shape=jax.ShapeDtypeStruct((tokens, width), F32),
        compiler_params=params(),
        cost_estimate=cost(20 * tokens * width, 5e6),
    )(*operands)


def kv_back_kernel(factor, parts_ref, proj_ref, gain_ref, cos_ref, sin_ref, *rest):
    grad_ref, dgain_ref = rest[-2:]
    size = proj_ref.shape[1]
    total = parts_ref[0].astype(F32)
    for k in range(1, parts_ref.shape[0]):
        total += parts_ref[k].astype(F32)
    grad, dgain = head_backward(
        total[:, :size] * factor, proj_ref[...], gain_ref[...], cos_ref[...], sin_ref[...]
    )
    grad_ref[:, :size] = grad.astype(LOW)
    grad_ref[:, size:] = total[:, size:].astype(LOW)
    dgain_ref[...] = dgain


def kv_back(parts, proj, gain, cos2, sin2, factor, others):
    block, size = proj.shape
    operands = [parts, proj, gain[None], cos2, sin2]
    shapes = [
        jax.ShapeDtypeStruct((block, 2 * size), LOW),
        jax.ShapeDtypeStruct((1, size), F32),
    ]
    return pl.pallas_call(
        functools.partial(kv_back_kernel, factor),
        grid=(1,),
        in_specs=[full(value.shape) for value in operands]
        + [pl.BlockSpec(memory_space=pl.ANY)] * len(others),
        out_specs=[full(shape.shape) for shape in shapes],
        out_shape=shapes,
        compiler_params=params(),
        cost_estimate=cost(40 * block * size, 5e6),
    )(*operands, *others)


def pair_kernel(a_ref, b_ref, *rest):
    rest[-1][...] = (a_ref[...].astype(F32) + b_ref[...].astype(F32)).astype(LOW)


def pair_sum(a, b, others):
    rows, columns = a.shape
    tiles = 2 if rows % 32 == 0 else 1
    spec = pl.BlockSpec((rows // tiles, columns), lambda i: (i, 0))
    return pl.pallas_call(
        pair_kernel,
        grid=(tiles,),
        in_specs=[spec, spec] + [pl.BlockSpec(memory_space=pl.ANY)] * len(others),
        out_specs=spec,
        out_shape=jax.ShapeDtypeStruct((rows, columns), LOW),
        compiler_params=params(),
        cost_estimate=cost(rows * columns, 6 * rows * columns),
    )(a, b, *others)


def fold_kernel(n_pairs, s_ref, *refs):
    del s_ref
    send_ref, keep_ref = refs[-2:]
    totals = [
        (refs[2 * k][...].astype(F32) + refs[2 * k + 1][...].astype(F32)).astype(LOW)
        for k in range(n_pairs)
    ]
    for half, out_ref in enumerate((send_ref, keep_ref)):

        @pl.when(pl.program_id(0) == half)
        def _():
            first = 0
            for total in totals:
                last = first + total.shape[1]
                out_ref[:, first:last] = total
                first = last


def fold(pairs, bit, others):
    rows = pairs[0][1].shape[0]
    columns = sum(got.shape[1] for _, got in pairs)
    tiles = 2
    tile = rows // (2 * tiles)
    side = lambda h, m: (1 - m[0]) * (1 - h) + m[0] * h
    specs = []
    for _, got in pairs:
        wide = got.shape[1]
        specs += [pl.BlockSpec((tile, wide), lambda h, j, m: (side(h, m) * tiles + j, 0))] * 2
    shape = jax.ShapeDtypeStruct((rows // 2, columns), LOW)
    return pl.pallas_call(
        functools.partial(fold_kernel, len(pairs)),
        grid_spec=pltpu.PrefetchScalarGridSpec(
            num_scalar_prefetch=1,
            grid=(2, tiles),
            in_specs=specs + [pl.BlockSpec(memory_space=pl.ANY)] * len(others),
            out_specs=[
                pl.BlockSpec((tile, columns), lambda h, j, m: (j * (1 - h) + (tiles - 1) * h, 0)),
                pl.BlockSpec((tile, columns), lambda h, j, m: (j * h, 0)),
            ],
        ),
        out_shape=[shape, shape],
        compiler_params=params(),
        cost_estimate=cost(rows * columns, 6 * rows * columns),
    )(
        bit.astype(jnp.int32)[None],
        *[value for pair in pairs for value in pair],
        *others,
    )


def normed_kernel(q_ref, kv_ref, wq_ref, wkv_ref, rows_ref, *rest):
    out_ref, dgain_ref = rest[-2:]
    grad = dot_nt(q_ref[...], wq_ref[...]) + dot_nt(kv_ref[...], wkv_ref[...])
    out_ref[...] = grad.astype(LOW)
    dgain_ref[...] = jnp.sum(grad * rows_ref[...].astype(F32), axis=0, keepdims=True)


def normed_back(grad_q, grad_kv, w_q, w_kv, rows, others):
    block, width = rows.shape
    tile = 512
    column = lambda i: (0, i)
    return pl.pallas_call(
        normed_kernel,
        grid=(width // tile,),
        in_specs=[
            full(grad_q.shape),
            full(grad_kv.shape),
            pl.BlockSpec((tile, w_q.shape[1]), lambda i: (i, 0)),
            pl.BlockSpec((tile, w_kv.shape[1]), lambda i: (i, 0)),
            pl.BlockSpec((block, tile), column),
        ]
        + [pl.BlockSpec(memory_space=pl.ANY)] * len(others),
        out_specs=[pl.BlockSpec((block, tile), column), pl.BlockSpec((1, tile), column)],
        out_shape=[
            jax.ShapeDtypeStruct((block, width), LOW),
            jax.ShapeDtypeStruct((1, width), F32),
        ],
        compiler_params=params(),
        cost_estimate=cost(2 * block * width * (w_q.shape[1] + w_kv.shape[1]), 12e6),
    )(grad_q, grad_kv, w_q, w_kv, rows, *others)


def pack_kernel(experts, router_ref, attn_ref, gain_ref, mlp_ref, q_ref, k_ref, *rest):
    out_ref, rows_ref = rest[-2:]
    size = q_ref.shape[1]
    rows_ref[:experts] = router_ref[:experts]
    rows_ref[experts:] = jnp.zeros_like(rows_ref[experts:])
    rows_ref[experts : experts + 1] = attn_ref[...] / gain_ref[...]
    rows_ref[experts + 1 : experts + 2] = mlp_ref[...]
    rows_ref[experts + 2 : experts + 3, :size] = q_ref[...]
    rows_ref[experts + 2 : experts + 3, size : 2 * size] = k_ref[...]
    out_ref[...] = rows_ref[...].astype(LOW)


def pack_small(experts, router, attn, gain, mlp, q, k, others):
    width = attn.shape[1]
    shape = (-(-(experts + 3) // 16) * 16, width)
    operands = [router, attn, gain[None], mlp, q, k]
    return pl.pallas_call(
        functools.partial(pack_kernel, experts),
        grid=(1,),
        in_specs=[full(value.shape) for value in operands]
        + [pl.BlockSpec(memory_space=pl.ANY)] * len(others),
        out_specs=full(shape),
        out_shape=jax.ShapeDtypeStruct(shape, LOW),
        scratch_shapes=[pltpu.VMEM(shape, F32)],
        compiler_params=params(),
        cost_estimate=cost(shape[0] * width, 6 * shape[0] * width),
    )(*operands, *others)


def part_sum_kernel(parts_ref, *rest):
    total = parts_ref[0].astype(F32)
    for k in range(1, parts_ref.shape[0]):
        total += parts_ref[k].astype(F32)
    rest[-1][...] = total.astype(LOW)


def part_sum(parts, others):
    count, rows, columns = parts.shape
    tiles = 2
    return pl.pallas_call(
        part_sum_kernel,
        grid=(tiles,),
        in_specs=[pl.BlockSpec((count, rows // tiles, columns), lambda i: (0, i, 0))]
        + [pl.BlockSpec(memory_space=pl.ANY)] * len(others),
        out_specs=pl.BlockSpec((rows // tiles, columns), lambda i: (i, 0)),
        out_shape=jax.ShapeDtypeStruct((rows, columns), LOW),
        compiler_params=params(),
        cost_estimate=cost(count * rows * columns, 4 * count * rows * columns),
    )(parts, *others)


def widen_kernel(n_chunks, n_outs, at_ref, *refs):
    del at_ref
    outs = refs[-n_outs:]
    widths = [ref.shape[1] for ref in outs]
    for k in range(n_chunks):

        @pl.when(pl.program_id(0) == k)
        def _():
            first = 0
            for wide, out_ref in zip(widths, outs):
                out_ref[...] = refs[k][:, first : first + wide].astype(F32)
                first += wide


def widen(places, chunks, widths, others):
    rows, columns = chunks[0].shape
    count = len(chunks)
    return pl.pallas_call(
        functools.partial(widen_kernel, count, len(widths)),
        grid_spec=pltpu.PrefetchScalarGridSpec(
            num_scalar_prefetch=1,
            grid=(count,),
            in_specs=[full(chunk.shape) for chunk in chunks]
            + [pl.BlockSpec(memory_space=pl.ANY)] * len(others),
            out_specs=[pl.BlockSpec((rows, wide), lambda i, at: (at[i], 0)) for wide in widths],
        ),
        out_shape=[jax.ShapeDtypeStruct((count * rows, wide), F32) for wide in widths],
        compiler_params=params(),
        cost_estimate=cost(rows * columns, 6 * count * rows * columns),
    )(jnp.stack(places).astype(jnp.int32), *chunks, *others)


def swap_dp(rows):
    return lax.ppermute(rows, "dp", [(0, 1), (1, 0)])


def swap_context(rows, s):
    n = lax.axis_size("context")
    return lax.ppermute(rows, "context", [(i, i ^ s) for i in range(n)])


def plane_turns():
    d, c = lax.axis_index("dp"), lax.axis_index("context")
    low, high = lax.rem(c, 2), lax.div(c, 2)

    def swap(first, second):
        perm = [(i, i ^ first) for i in range(4)] + [(4 + i, 4 + (i ^ second)) for i in range(4)]
        return lambda rows: lax.ppermute(rows, GROUP_AXES, perm)

    return [
        (jnp.where(d == 0, low, high), swap(1, 2)),
        (jnp.where(d == 0, high, low), swap(2, 1)),
    ]


def plane_first(pairs, others):
    (bit_1, _), _ = plane_turns()
    return fold(pairs, bit_1, others)


def plane_second(send, keep, others):
    (_, swap_1), (bit_2, _) = plane_turns()
    return fold([(keep, swap_1(send))], bit_2, others)


def plane_last(send, keep, others):
    _, (_, swap_2) = plane_turns()
    return pair_sum(keep, swap_2(send), others)


def plane_spread(own):
    (_, swap_1), (_, swap_2) = plane_turns()
    second = swap_2(own)
    return [own, second, swap_1(own), swap_1(second)]


def quarter_places(rank):
    d = lax.axis_index("dp")
    c = lax.axis_index("context")
    low, high = lax.rem(c, 2), lax.div(c, 2)
    places = []
    for core in (d, 1 - d):
        bit_1 = jnp.where(core == 0, low, high)
        bit_2 = jnp.where(core == 0, high, low)
        for flip_1, flip_2 in ((0, 0), (0, 1), (1, 0), (1, 1)):
            places.append(4 * core + rank(core, bit_1 ^ flip_1, bit_2 ^ flip_2))
    return places


def widen_all(quarters, places, widths, others):
    return widen(places, quarters + [swap_dp(part) for part in quarters], widths, others)


def arrival_order(n):
    return [sorted(range(n), key=lambda j: (abs(j - i), j)) for i in range(n)]


def choose(index, options):
    distinct = []
    for option in options:
        if option is not None and not any(option is other for other in distinct):
            distinct.append(option)
    result = distinct[0]
    for option in distinct[1:]:
        mask = functools.reduce(
            jnp.logical_or, [index == i for i, other in enumerate(options) if other is option]
        )
        result = jnp.where(mask, option, result)
    return result


def line_gather(chunk):
    return line_steps({0: chunk}, 1, lax.axis_size("expert"))


def line_steps(found, first, stop):
    n = lax.axis_size("expert")
    found = dict(found)
    for s in range(first, stop):
        found[-s] = lax.ppermute(
            found[1 - s], "expert", [(i, i + 1) for i in range(s - 1, n - 1)]
        )
        found[s] = lax.ppermute(found[s - 1], "expert", [(i + 1, i) for i in range(n - s)])
    return found


def context_gather(rows):
    n = lax.axis_size("context")
    c = lax.axis_index("context")
    found = {0: rows}
    for s in range(1, n):
        found[s] = lax.ppermute(rows, "context", [(i, i ^ s) for i in range(n)])
    return jnp.concatenate([choose(c, [found[i ^ j] for i in range(n)]) for j in range(n)], axis=0)


def zero_of(*others):
    return functools.reduce(
        jnp.add,
        [
            lax.slice(other, (0,) * other.ndim, (1,) * other.ndim).reshape(()).astype(F32) * 0.0
            for other in others
        ],
    )


def after(value, *others):
    return (value.astype(F32) + zero_of(*others)).astype(value.dtype)


def on_device(
    layer_input,
    grad_output,
    attn_gain,
    query_weight,
    key_weight,
    value_weight,
    q_gain,
    k_gain,
    output_weight,
    mlp_gain,
    router,
    w_gate,
    w_up,
    w_down,
    routes,
    half_order,
):
    n_context = lax.axis_size("context")
    n_expert = lax.axis_size("expert")
    n_groups = lax.axis_size(GROUP_AXES)
    tok_dev, width = layer_input.shape[1:]
    size = q_gain.shape[0]
    kv_total = key_weight.shape[1] * n_expert
    group_dev = n_expert // (kv_total // size)
    kv_index = lax.axis_index("expert") // group_dev
    block = tok_dev * n_expert
    seq = block * n_context
    half = block // 2
    experts = router.shape[1]
    exp_dev = w_gate.shape[0]
    top = routes.shape[2]
    capacity = max(2, (tok_dev * top * 9 + 8 * experts - 1) // (8 * experts))
    scale = size ** (-0.5)

    seq_rows = jnp.arange(seq, dtype=jnp.int32)
    context = lax.axis_index("context")
    own_halves = lax.dynamic_slice_in_dim(half_order, 2 * context, 2)
    own_pos = (own_halves[:, None] * half + jnp.arange(half, dtype=jnp.int32)[None]).reshape(-1)
    per_half = half // TILE
    tile_pos = (half_order[:, None] * per_half + jnp.arange(per_half, dtype=jnp.int32)).reshape(-1)
    kidx = jnp.sum(
        (tile_pos[None, :] == jnp.arange(seq // TILE, dtype=jnp.int32)[:, None])
        * jnp.arange(seq // TILE, dtype=jnp.int32)[None, :],
        axis=1,
    ).astype(jnp.int32)
    qpos = lax.dynamic_slice_in_dim(tile_pos, context * (block // TILE), block // TILE)
    entry = jnp.arange(size)
    freq = jnp.power(THETA, -(2 * (entry % (size // 2))).astype(F32) / size)
    angles = own_pos.astype(F32)[:, None] * freq[None, :]
    cos2 = jnp.cos(angles)
    sin2 = jnp.sin(angles) * jnp.where(entry < size // 2, -1.0, 1.0)[None, :]

    place = lax.axis_index("expert")
    place_1 = place.astype(jnp.int32)[None]
    lanes = -(-2 * experts // 128) * 128
    mask = jnp.any(
        routes[0][:, :, None] == jnp.arange(lanes, dtype=jnp.int32)[None, None, :], axis=1
    )
    mask_wide = mask.astype(F32)
    router_rows = router.T

    x_low = layer_input[0]
    x_normal, _ = norm_parts(x_low.astype(F32))
    normed_found = line_gather((x_normal * attn_gain).astype(LOW))
    if group_dev == 1:
        kv_weights = jnp.concatenate([key_weight, value_weight], axis=1)
    else:
        key_whole = lax.all_gather(key_weight, "expert", axis=1, tiled=True)
        value_whole = lax.all_gather(value_weight, "expert", axis=1, tiled=True)
        kv_weights = jnp.concatenate(
            [
                lax.dynamic_slice_in_dim(key_whole, kv_index * size, size, 1),
                lax.dynamic_slice_in_dim(value_whole, kv_index * size, size, 1),
            ],
            axis=1,
        )
    grad_low = grad_output[0]
    normed_rows, own_kv, key_proj, grad_wide = project_keys(
        place_1,
        normed_found,
        kv_weights,
        k_gain,
        cos2,
        sin2,
        scale * LOG2E,
        grad_low,
        mask_wide,
    )
    grad_col = lax.all_gather(grad_wide, "expert", axis=0, tiled=True)
    kv_whole = context_gather(own_kv)
    queries, query_proj = project_queries(normed_rows, query_weight, q_gain, cos2, sin2)

    n_half = n_expert // 2
    order_here = jnp.asarray(arrival_order(n_expert), jnp.int32)[place]
    turn_here = jnp.sum(
        (order_here[:, None] == jnp.arange(n_expert, dtype=jnp.int32)[None, :])
        * jnp.arange(n_expert, dtype=jnp.int32)[:, None],
        axis=0,
    ).astype(jnp.int32)
    meta = jnp.concatenate([place_1, turn_here, order_here])
    grad_sent, slots = make_slots(meta, grad_col, width, n_groups, capacity)
    spreads, back_tables = make_tables(meta, slots, n_half, capacity)

    def swap_plane(rows):
        parts = rows.reshape(n_groups, -1, rows.shape[1])
        parts = lax.all_to_all(parts, GROUP_AXES, split_axis=0, concat_axis=0, tiled=True)
        return parts.reshape(rows.shape)

    attended, inverse = attend(qpos, kidx, queries, kv_whole, [])
    attn_part = out_dot(attended, output_weight, [grad_col])
    attn_rows = lax.psum_scatter(attn_part, "expert", scatter_dimension=0, tiled=True)

    grad_x = swap_plane(grad_sent)
    act_pull = dot_nt(grad_x, w_down[0]).reshape(n_groups, 2, n_half * capacity, -1)

    hidden, mixed, probs = route_rows(
        x_low, attn_rows, mlp_gain, router_rows, mask_wide, experts, []
    )

    who = (lax.axis_index(ALL_AXES) * exp_dev).astype(jnp.int32)[None]
    mixed_found = line_gather(mixed)
    near = spread_rows(place_1, spreads[0], mixed_found, range(n_half), [grad_x])
    x_near = swap_plane(near)
    worked_near = run_expert(who, x_near, w_gate[0], w_up[0], act_pull, 0, experts)
    far = spread_rows(place_1, spreads[1], mixed_found, range(n_half, n_expert), [x_near])
    x_far = swap_plane(far)
    worked_far = run_expert(who, x_far, w_gate[0], w_up[0], act_pull, 1, experts)
    xs = [x_near, x_far]
    acts, gate_lows, up_lows, copies = (list(pair) for pair in zip(worked_near, worked_far))
    back_far = swap_plane(copies[1])
    back_near = swap_plane(copies[0])
    join = lambda parts: jnp.concatenate(parts, axis=0)
    x_all = join([x[:, :width] for x in xs])
    grad_w_gate = dot_tn(x_all, join(gate_lows))
    grad_w_up = dot_tn(x_all, join(up_lows))
    grad_by_round = jnp.swapaxes(
        grad_x.reshape(n_groups, 2, n_half * capacity, width), 0, 1
    ).reshape(-1, width)
    grad_w_down = dot_tn(join(acts), grad_by_round)
    copies_col = combine_rows(
        meta, back_tables, [back_near, back_far], n_half, [grad_w_gate, grad_w_up]
    )
    copies_sum = lax.psum_scatter(copies_col, "expert", scatter_dimension=0, tiled=True)

    returned = [dot_nn(act, w_down[0]).astype(LOW) for act in acts]
    returned_near = swap_plane(returned[0])

    grad_hidden, grad_hidden_low, grad_mlp_gain, grad_router = route_back(
        copies_sum,
        grad_low,
        hidden,
        mlp_gain,
        router_rows,
        mask_wide,
        probs,
        experts,
        [returned_near, grad_w_down],
    )

    returned_far = swap_plane(returned[1])
    grad_attn = lax.all_gather(grad_hidden_low, "expert", axis=0, tiled=True)
    grad_o, centre = grad_attended(
        grad_attn, output_weight, attended, inverse, [returned_far]
    )
    combined = combine_rows(meta, back_tables, [returned_near, returned_far], n_half, [])
    output_rows = lax.psum_scatter(combined, "expert", scatter_dimension=0, tiled=True)
    w_out = token_dot(attended, grad_attn, [combined])
    w_out_parts = swap_plane(w_out)
    grad_kv, grad_q, grad_q_gain = attend_back(
        qpos,
        kidx,
        queries,
        grad_o,
        centre,
        kv_whole,
        query_proj,
        q_gain,
        cos2,
        sin2,
        [w_out],
    )
    kv_parts = lax.all_to_all(
        grad_kv.astype(LOW).reshape(n_context, block, 2 * size),
        "context",
        split_axis=0,
        concat_axis=0,
        tiled=True,
    )
    w_query_send, w_query_keep = token_halves(normed_rows, grad_q, [w_out_parts])
    w_query_got = swap_dp(w_query_send)
    output_rows = hidden + output_rows.astype(F32) + zero_of(w_query_keep)

    kv_grads, grad_k_gain = kv_back(
        kv_parts, key_proj, k_gain, cos2, sin2, scale, [w_query_keep]
    )
    w_out_quarters = plane_spread(part_sum(w_out_parts.reshape(n_groups, -1, width), [kv_parts]))
    pairs = [(w_query_keep, w_query_got)]
    widths = [query_weight.shape[1]]
    if group_dev == 1:
        w_kv_send, w_kv_keep = token_halves(normed_rows, kv_grads, [])
        pairs.append((w_kv_keep, swap_dp(w_kv_send)))
        widths += [key_weight.shape[1], value_weight.shape[1]]
    send, keep = plane_first(pairs, w_out_quarters)

    grad_normed, gain_rows = normed_back(
        grad_q, kv_grads, query_weight, kv_weights, normed_rows, [keep]
    )
    (grad_w_out,) = widen_all(
        w_out_quarters,
        quarter_places(lambda core, b1, b2: jnp.where(core == 0, b1 + 2 * b2, 2 * b1 + b2)),
        [width],
        [],
    )
    small = pack_small(
        experts,
        grad_router,
        gain_rows,
        attn_gain,
        grad_mlp_gain,
        grad_q_gain,
        grad_k_gain,
        [],
    )
    second_send, second_keep = plane_second(send, keep, [grad_normed, small])
    quarter = plane_last(second_send, second_keep, [output_rows])
    quarters = plane_spread(quarter)
    grad_normed = lax.psum_scatter(grad_normed, "expert", scatter_dimension=0, tiled=True)
    grad_input = input_back(grad_normed, x_low, attn_gain, grad_hidden)
    steps = [[second_send], [quarter], [quarters[1], grad_w_out], [quarters[3]], [grad_input]]
    doublings = [(axis, 2**k) for axis in ("dp", "context", "expert") for k in range(5)]
    doublings = [(axis, s) for axis, s in doublings if s < lax.axis_size(axis)]
    for k, (axis, s) in enumerate(doublings):
        n = lax.axis_size(axis)
        got = lax.ppermute(small, axis, [(i, i ^ s) for i in range(n)])
        small = pair_sum(small, got, steps[k] if k < len(steps) else [])
    small_sum = small.astype(F32)
    grad_w_query, *more = widen_all(
        quarters, quarter_places(lambda core, b1, b2: 2 * b1 + b2), widths, []
    )
    if group_dev == 1:
        grad_w_key, grad_w_value = more
    else:
        w_kv = token_dot(normed_rows, kv_grads, [])
        blank = jnp.zeros((width, kv_total), LOW)
        pieces = []
        for part in (w_kv[:, :size], w_kv[:, size:]):
            padded = lax.dynamic_update_slice(blank, part, (0, kv_index * size))
            pieces.append(lax.psum_scatter(padded, "expert", scatter_dimension=1, tiled=True))
        grad_w_key, grad_w_value = (lax.psum(piece, GROUP_AXES).astype(F32) for piece in pieces)
    grad_attn_gain, grad_mlp_gain = small_sum[experts], small_sum[experts + 1]
    grad_q_gain = small_sum[experts + 2, :size]
    grad_k_gain = small_sum[experts + 2, size : 2 * size]
    return (
        output_rows.astype(LOW)[None],
        grad_input[None],
        grad_attn_gain,
        grad_w_query,
        grad_w_key,
        grad_w_value,
        grad_q_gain,
        grad_k_gain,
        grad_w_out,
        grad_mlp_gain,
        small_sum[:experts].T,
        grad_w_gate[None],
        grad_w_up[None],
        grad_w_down[None],
    )


def solution(mesh):
    rows = P("dp", ("context", "expert"), None)
    expert = P(ALL_AXES, None, None)
    columns = P(None, "expert")
    in_specs = (
        rows,
        rows,
        P(),
        columns,
        columns,
        columns,
        P(),
        P(),
        P("expert", None),
        P(),
        P(),
        expert,
        expert,
        expert,
        rows,
        P(),
    )
    out_specs = (
        rows,
        rows,
        P(),
        columns,
        columns,
        columns,
        P(),
        P(),
        P("expert", None),
        P(),
        P(),
        expert,
        expert,
        expert,
    )
    return jax.shard_map(
        on_device, mesh=mesh, in_specs=in_specs, out_specs=out_specs, check_vma=False
    )
```

```python
import functools
import math

import jax
import jax.numpy as jnp
from jax import lax
from jax.experimental import pallas as pl
from jax.experimental.pallas import tpu as pltpu
from jax.sharding import PartitionSpec as P

EPS = 1e-06
THETA = 1000000.0
TILE = 256
PIECE = 128
VMEM_BYTES = 56 * 1024 * 1024
LOG2E = math.log2(math.e)
LOW = jnp.bfloat16
F32 = jnp.float32
ALL_AXES = ("dp", "context", "expert")
GROUP_AXES = ("dp", "context")


def dot_nn(a, b):
    return lax.dot_general(a, b, (((1,), (0,)), ((), ())), preferred_element_type=F32)


def dot_nt(a, b):
    return lax.dot_general(a, b, (((1,), (1,)), ((), ())), preferred_element_type=F32)


def dot_tn(a, b):
    return lax.dot_general(a, b, (((0,), (0,)), ((), ())), preferred_element_type=F32)


def params(**more):
    return pltpu.CompilerParams(vmem_limit_bytes=VMEM_BYTES, **more)


def cost(flops, nbytes, exps=0):
    return pl.CostEstimate(flops=int(flops), bytes_accessed=int(nbytes), transcendentals=int(exps))


def head_forward(u, gain, cos2, sin2):
    rr = lax.rsqrt(jnp.mean(u * u, axis=-1, keepdims=True) + EPS)
    y = u * rr * gain
    return y * cos2 + pltpu.roll(y, 64, 1) * sin2


def head_backward(gy, u, gain, cos2, sin2):
    g = gy * cos2 - pltpu.roll(gy, 64, 1) * sin2
    rr = lax.rsqrt(jnp.mean(u * u, axis=-1, keepdims=True) + EPS)
    n = u * rr
    gn = g * gain
    grad = rr * (gn - n * jnp.mean(gn * n, axis=-1, keepdims=True))
    return grad, jnp.sum(g * n, axis=0, keepdims=True)


def query_kernel(x_ref, w_ref, gain_ref, cos_ref, sin_ref, rot_ref, proj_ref):
    tiles, heads, rows, size = rot_ref.shape
    acc = dot_nn(x_ref[...], w_ref[...])
    for h in range(heads):
        u = acc[:, h * size : (h + 1) * size]
        rot = head_forward(u, gain_ref[...], cos_ref[...], sin_ref[...])
        proj_ref[:, h] = u.reshape(tiles, rows, size)
        rot_ref[:, h] = rot.astype(LOW).reshape(tiles, rows, size)


def project_queries(normed, weight, gain, cos2, sin2):
    block, width = normed.shape
    size = cos2.shape[1]
    heads = weight.shape[1] // size
    tiles = block // TILE
    whole = lambda i: (0, 0)
    per = lambda i: (0, i, 0, 0)
    shape = (tiles, heads, TILE, size)
    return pl.pallas_call(
        query_kernel,
        grid=(heads // 2,),
        in_specs=[
            pl.BlockSpec((block, width), whole),
            pl.BlockSpec((width, 2 * size), lambda i: (0, i)),
            pl.BlockSpec((1, size), whole),
            pl.BlockSpec((block, size), whole),
            pl.BlockSpec((block, size), whole),
        ],
        out_specs=[pl.BlockSpec((tiles, 2, TILE, size), per)] * 2,
        out_shape=[jax.ShapeDtypeStruct(shape, LOW), jax.ShapeDtypeStruct(shape, F32)],
        compiler_params=params(),
        cost_estimate=cost(2 * block * width * heads * size, 12e6),
    )(normed, weight, gain[None], cos2, sin2)


def put_in_order(place, refs, out_ref):
    n = (len(refs) + 1) // 2
    rows = refs[0].shape[0]
    for distance in range(1 - n, n):
        ref = refs[distance + n - 1]
        at = place + distance

        @pl.when(jnp.logical_and(at >= 0, at < n))
        def _():
            out_ref[pl.ds(pl.multiple_of(at * rows, rows), rows), :] = ref[...]


def chunk_list(found):
    n = (len(found) + 1) // 2
    return [found[distance] for distance in range(1 - n, n)]


def key_kernel(factor, n_chunks, place_ref, *refs):
    w_ref, gain_ref, cos_ref, sin_ref, g_ref, mask_ref = refs[n_chunks:-4]
    rows_ref, kv_ref, proj_ref, wide_ref = refs[-4:]
    size = proj_ref.shape[1]
    width = g_ref.shape[1]
    put_in_order(place_ref[0], refs[:n_chunks], rows_ref)
    wide_ref[:, :width] = g_ref[...]
    wide_ref[:, width:] = mask_ref[...].astype(LOW)
    acc = dot_nn(rows_ref[...], w_ref[...])
    u = acc[:, :size]
    rot = head_forward(u, gain_ref[...], cos_ref[...], sin_ref[...])
    proj_ref[...] = u
    kv_ref[:, :size] = (rot * factor).astype(LOW)
    kv_ref[:, size:] = acc[:, size:].astype(LOW)


def full(shape):
    return pl.BlockSpec(shape, lambda *_: (0,) * len(shape))


def project_keys(place, found, weight, gain, cos2, sin2, factor, g, mask):
    chunks = chunk_list(found)
    rows, width = chunks[0].shape
    block, size = cos2.shape
    operands = [*chunks, weight, gain[None], cos2, sin2, g, mask]
    shapes = [
        jax.ShapeDtypeStruct((block, width), LOW),
        jax.ShapeDtypeStruct((block, 2 * size), LOW),
        jax.ShapeDtypeStruct((block, size), F32),
        jax.ShapeDtypeStruct((rows, width + mask.shape[1]), LOW),
    ]
    return pl.pallas_call(
        functools.partial(key_kernel, factor, len(chunks)),
        grid_spec=pltpu.PrefetchScalarGridSpec(
            num_scalar_prefetch=1,
            grid=(1,),
            in_specs=[full(x.shape) for x in operands],
            out_specs=[full(x.shape) for x in shapes],
        ),
        out_shape=shapes,
        compiler_params=params(),
        cost_estimate=cost(4 * block * width * size, 8e6),
    )(place, *operands)


def in_order(last, step):
    lax.fori_loop(0, lax.div(last, 2), lambda p, c: (step([2 * p, 2 * p + 1], False), c)[1], 0)

    @pl.when(lax.rem(last, 2) == 1)
    def _():
        step([last - 1, last], True)

    @pl.when(lax.rem(last, 2) == 0)
    def _():
        step([last], True)


def attend_kernel(qpos_ref, kidx_ref, q_ref, kv_ref, *rest):
    out_ref, inv_ref, acc_ref = rest[-3:]
    heads, rows, size = q_ref.shape[1:]
    acc_ref[...] = jnp.zeros_like(acc_ref)

    def step(places, masked):
        starts = [pl.multiple_of(kidx_ref[place] * rows, rows) for place in places]
        count = len(places) * rows
        keys = jnp.concatenate([kv_ref[pl.ds(start, rows), :size] for start in starts], axis=0)
        values = jnp.concatenate([kv_ref[pl.ds(start, rows), size:] for start in starts], axis=0)
        values = jnp.concatenate([values, jnp.ones((count, size), LOW)], axis=1)
        for h in range(heads):
            for first in range(0, rows, PIECE):
                part = slice(first, first + PIECE)
                e = jnp.exp2(dot_nt(q_ref[0, h, part], keys))
                if masked:
                    qi = lax.broadcasted_iota(jnp.int32, e.shape, 0) + first
                    ki = lax.broadcasted_iota(jnp.int32, e.shape, 1) - (count - rows)
                    e = jnp.where(ki <= qi, e, 0.0)
                acc_ref[h, part] += dot_nn(e.astype(LOW), values)

    in_order(qpos_ref[pl.program_id(0)], step)
    for h in range(heads):
        inv = 1.0 / acc_ref[h, :, size:]
        inv_ref[0, h] = inv
        out_ref[:, h * size : (h + 1) * size] = (acc_ref[h, :, :size] * inv).astype(LOW)


def attend(qpos, kidx, queries, kv, others):
    tiles, heads, rows, size = queries.shape
    seq = kv.shape[0]
    return pl.pallas_call(
        attend_kernel,
        grid_spec=pltpu.PrefetchScalarGridSpec(
            num_scalar_prefetch=2,
            grid=(tiles,),
            in_specs=[
                pl.BlockSpec((1, heads, rows, size), lambda i, a, b: (i, 0, 0, 0)),
                pl.BlockSpec((seq, 2 * size), lambda i, a, b: (0, 0)),
            ]
            + [pl.BlockSpec(memory_space=pl.ANY)] * len(others),
            out_specs=[
                pl.BlockSpec((rows, heads * size), lambda i, a, b: (i, 0)),
                pl.BlockSpec((1, heads, rows, size), lambda i, a, b: (i, 0, 0, 0)),
            ],
            scratch_shapes=[pltpu.VMEM((heads, rows, 2 * size), F32)],
        ),
        out_shape=[
            jax.ShapeDtypeStruct((tiles * rows, heads * size), LOW),
            jax.ShapeDtypeStruct((tiles, heads, rows, size), F32),
        ],
        compiler_params=params(),
        cost_estimate=cost(
            6 * tiles * rows * heads * seq * size, 8e6, tiles * rows * heads * seq
        ),
    )(qpos, kidx, queries, kv, *others)


def grad_out_kernel(rows_ref, w_ref, o_ref, inv_ref, *rest):
    do_ref, centre_ref = rest[-2:]
    tiles, heads, rows, size = do_ref.shape
    acc = dot_nt(rows_ref[...], w_ref[...])
    for t in range(tiles):
        for h in range(heads):
            part = slice(t * rows, (t + 1) * rows), slice(h * size, (h + 1) * size)
            low = (acc[part] * inv_ref[t, h]).astype(LOW)
            do_ref[t, h] = low
            product = low.astype(F32) * o_ref[part].astype(F32)
            centre = jnp.sum(jnp.transpose(product), axis=0, keepdims=True)
            centre_ref[t, h] = jnp.broadcast_to(centre, (8, rows))


def grad_attended(grad_rows, weight, attended, inverse, others):
    tiles, heads, rows, size = inverse.shape
    block, width = grad_rows.shape
    return pl.pallas_call(
        grad_out_kernel,
        grid=(heads // 2,),
        in_specs=[
            pl.BlockSpec((block, width), lambda i: (0, 0)),
            pl.BlockSpec((2 * size, width), lambda i: (i, 0)),
            pl.BlockSpec((block, 2 * size), lambda i: (0, i)),
            pl.BlockSpec((tiles, 2, rows, size), lambda i: (0, i, 0, 0)),
        ]
        + [pl.BlockSpec(memory_space=pl.ANY)] * len(others),
        out_specs=[
            pl.BlockSpec((tiles, 2, rows, size), lambda i: (0, i, 0, 0)),
            pl.BlockSpec((tiles, 2, 8, rows), lambda i: (0, i, 0, 0)),
        ],
        out_shape=[
            jax.ShapeDtypeStruct((tiles, heads, rows, size), LOW),
            jax.ShapeDtypeStruct((tiles, heads, 8, rows), F32),
        ],
        compiler_params=params(),
        cost_estimate=cost(2 * block * width * heads * size, 12e6),
    )(grad_rows, weight, attended, inverse, *others)


def attend_back_kernel(
    qpos_ref,
    kidx_ref,
    q_ref,
    do_ref,
    centre_ref,
    kv_ref,
    proj_ref,
    gain_ref,
    cos_ref,
    sin_ref,
    *rest,
):
    dkv_ref, dq_ref, dgain_ref, acc_ref, e_ref, ds_ref = rest[-6:]
    heads, rows, size = q_ref.shape[1:]

    @pl.when(pl.program_id(0) == 0)
    def _():
        dkv_ref[...] = jnp.zeros_like(dkv_ref)
        dgain_ref[...] = jnp.zeros_like(dgain_ref)

    acc_ref[...] = jnp.zeros_like(acc_ref)

    def step(places, masked):
        starts = [pl.multiple_of(kidx_ref[place] * rows, rows) for place in places]
        count = len(places) * rows
        keys = jnp.concatenate([kv_ref[pl.ds(start, rows), :size] for start in starts], axis=0)
        values = jnp.concatenate([kv_ref[pl.ds(start, rows), size:] for start in starts], axis=0)
        for h in range(heads):
            query, grad = q_ref[0, h], do_ref[0, h]
            centre = centre_ref[0, h, 0:1]
            columns = slice(h * rows, (h + 1) * rows)
            for first in range(0, count, PIECE):
                part = slice(first, first + PIECE)
                e = jnp.exp2(dot_nt(keys[part], query))
                if masked and first >= count - rows:
                    ki = lax.broadcasted_iota(jnp.int32, e.shape, 0) + (first - (count - rows))
                    qi = lax.broadcasted_iota(jnp.int32, e.shape, 1)
                    e = jnp.where(ki <= qi, e, 0.0)
                ds = e * (dot_nt(values[part], grad) - centre)
                e_ref[part, columns] = e.astype(LOW)
                ds_ref[part, columns] = ds.astype(LOW)
            acc_ref[h] += dot_tn(ds_ref[:count, columns], keys)
        dk = dot_nn(ds_ref[:count], q_ref[0].reshape(heads * rows, size))
        dv = dot_nn(e_ref[:count], do_ref[0].reshape(heads * rows, size))
        for k, start in enumerate(starts):
            dkv_ref[pl.ds(start, rows), :size] += dk[k * rows : (k + 1) * rows]
            dkv_ref[pl.ds(start, rows), size:] += dv[k * rows : (k + 1) * rows]

    in_order(qpos_ref[pl.program_id(0)], step)
    total = jnp.zeros((1, size), F32)
    for h in range(heads):
        grad, gain_part = head_backward(
            acc_ref[h] * (1.0 / LOG2E), proj_ref[0, h], gain_ref[...], cos_ref[...], sin_ref[...]
        )
        dq_ref[:, h * size : (h + 1) * size] = grad.astype(LOW)
        total += gain_part
    dgain_ref[...] += total


def attend_back(qpos, kidx, queries, grads, centre, kv, proj, gain, cos2, sin2, others):
    tiles, heads, rows, size = queries.shape
    seq = kv.shape[0]
    per = pl.BlockSpec((1, heads, rows, size), lambda i, a, b: (i, 0, 0, 0))
    flat = lambda i, a, b: (0, 0)
    rowwise = lambda i, a, b: (i, 0)
    return pl.pallas_call(
        attend_back_kernel,
        grid_spec=pltpu.PrefetchScalarGridSpec(
            num_scalar_prefetch=2,
            grid=(tiles,),
            in_specs=[
                per,
                per,
                pl.BlockSpec((1, heads, 8, rows), lambda i, a, b: (i, 0, 0, 0)),
                pl.BlockSpec((seq, 2 * size), flat),
                per,
                pl.BlockSpec((1, size), flat),
                pl.BlockSpec((rows, size), rowwise),
                pl.BlockSpec((rows, size), rowwise),
            ]
            + [pl.BlockSpec(memory_space=pl.ANY)] * len(others),
            out_specs=[
                pl.BlockSpec((seq, 2 * size), flat),
                pl.BlockSpec((rows, heads * size), rowwise),
                pl.BlockSpec((1, size), flat),
            ],
            scratch_shapes=[pltpu.VMEM((heads, rows, size), F32)]
            + [pltpu.VMEM((2 * rows, heads * rows), LOW)] * 2,
        ),
        out_shape=[
            jax.ShapeDtypeStruct((seq, 2 * size), F32),
            jax.ShapeDtypeStruct((tiles * rows, heads * size), LOW),
            jax.ShapeDtypeStruct((1, size), F32),
        ],
        compiler_params=params(),
        cost_estimate=cost(
            15 * tiles * rows * heads * seq * size, 12e6, tiles * rows * heads * seq
        ),
    )(qpos, kidx, queries, grads, centre, kv, proj, gain[None], cos2, sin2, *others)


def out_kernel(a_ref, b_ref, *rest):
    rest[-1][...] = dot_nn(a_ref[...], b_ref[...]).astype(LOW)


def out_dot(a, b, others):
    block, inner = a.shape
    columns = b.shape[1]
    tile = min(columns, 512)
    return pl.pallas_call(
        out_kernel,
        grid=(columns // tile,),
        in_specs=[
            pl.BlockSpec((block, inner), lambda i: (0, 0)),
            pl.BlockSpec((inner, tile), lambda i: (0, i)),
        ]
        + [pl.BlockSpec(memory_space=pl.ANY)] * len(others),
        out_specs=pl.BlockSpec((block, tile), lambda i: (0, i)),
        out_shape=jax.ShapeDtypeStruct((block, columns), LOW),
        compiler_params=params(),
        cost_estimate=cost(2 * block * inner * columns, 8e6),
    )(a, b, *others)


def token_kernel(a_ref, b_ref, *rest):
    rest[-1][...] = dot_tn(a_ref[...], b_ref[...]).astype(LOW)


def token_dot(a, b, others):
    block, rows = a.shape
    columns = b.shape[1]
    tile = min(rows, 512)
    return pl.pallas_call(
        token_kernel,
        grid=(rows // tile,),
        in_specs=[
            pl.BlockSpec((block, tile), lambda i: (0, i)),
            pl.BlockSpec((block, columns), lambda i: (0, 0)),
        ]
        + [pl.BlockSpec(memory_space=pl.ANY)] * len(others),
        out_specs=pl.BlockSpec((tile, columns), lambda i: (i, 0)),
        out_shape=jax.ShapeDtypeStruct((rows, columns), LOW),
        compiler_params=params(),
        cost_estimate=cost(2 * block * rows * columns, 6e6),
    )(a, b, *others)


def halves_kernel(d_ref, a_ref, b_ref, *rest):
    send_ref, keep_ref = rest[-2:]
    product = dot_tn(a_ref[...], b_ref[...]).astype(LOW)

    @pl.when(pl.program_id(0) == 0)
    def _():
        send_ref[...] = product

    @pl.when(pl.program_id(0) == 1)
    def _():
        keep_ref[...] = product


def token_halves(a, b, others):
    block, rows = a.shape
    columns = b.shape[1]
    tiles = 2
    tile = rows // (2 * tiles)
    d = lax.axis_index("dp").astype(jnp.int32)[None]
    half = jax.ShapeDtypeStruct((rows // 2, columns), LOW)
    return pl.pallas_call(
        halves_kernel,
        grid_spec=pltpu.PrefetchScalarGridSpec(
            num_scalar_prefetch=1,
            grid=(2, tiles),
            in_specs=[
                pl.BlockSpec(
                    (block, tile),
                    lambda h, j, d: (0, ((1 - d[0]) * (1 - h) + d[0] * h) * tiles + j),
                ),
                pl.BlockSpec((block, columns), lambda h, j, d: (0, 0)),
            ]
            + [pl.BlockSpec(memory_space=pl.ANY)] * len(others),
            out_specs=[
                pl.BlockSpec((tile, columns), lambda h, j, d: (j * (1 - h) + (tiles - 1) * h, 0)),
                pl.BlockSpec((tile, columns), lambda h, j, d: (j * h, 0)),
            ],
        ),
        out_shape=[half, half],
        compiler_params=params(),
        cost_estimate=cost(2 * block * rows * columns, 6e6),
    )(d, a, b, *others)


def split_low(value):
    high = value.astype(LOW)
    return high, (value - high.astype(F32)).astype(LOW)


def norm_parts(rows):
    rr = lax.rsqrt(jnp.mean(rows * rows, axis=-1, keepdims=True) + EPS)
    return rows * rr, rr


def norm_back(grad, normal, rr, gain):
    weighted = grad * gain
    return rr * (weighted - normal * jnp.mean(weighted * normal, axis=-1, keepdims=True))


def add_all(refs):
    return functools.reduce(jnp.add, [ref[...].astype(F32) for ref in refs])


def pad_rows(rows, count):
    if rows.shape[0] == count:
        return rows
    return jnp.concatenate(
        [rows, jnp.zeros((count - rows.shape[0], rows.shape[1]), rows.dtype)], axis=0
    )


def router_kernel(experts, *refs):
    x_ref, attn_ref, gain_ref, router_ref, mask_ref = refs[:5]
    hidden_ref, mixed_ref, probs_ref = refs[-3:]
    width = x_ref.shape[1]
    lanes = mask_ref.shape[1]
    hidden = add_all([x_ref, attn_ref])
    hidden_ref[...] = hidden
    mixed = (norm_parts(hidden)[0] * gain_ref[...]).astype(LOW)
    mixed_ref[:, :width] = mixed
    logits = dot_nt(mixed, pad_rows(router_ref[...], lanes))
    lane = lax.broadcasted_iota(jnp.int32, logits.shape, 1)
    logits = jnp.where(lane < experts, logits, -1e30)
    weights = jnp.exp(logits - jnp.max(logits, axis=1, keepdims=True))
    probs = weights / jnp.sum(weights, axis=1, keepdims=True)
    probs_ref[...] = probs
    chosen = probs * mask_ref[...]
    high, low = split_low(chosen / jnp.sum(chosen, axis=1, keepdims=True))
    both = high.astype(F32) + pltpu.roll(low.astype(F32), experts, 1)
    mixed_ref[:, width:] = both.astype(LOW)


def route_rows(x, attn, gain, router, mask, experts, others):
    tokens, width = x.shape
    lanes = mask.shape[1]
    operands = [x, attn, gain[None], router, mask]
    shapes = [
        jax.ShapeDtypeStruct((tokens, width), F32),
        jax.ShapeDtypeStruct((tokens, width + lanes), LOW),
        jax.ShapeDtypeStruct((tokens, lanes), F32),
    ]
    return pl.pallas_call(
        functools.partial(router_kernel, experts),
        grid=(1,),
        in_specs=[full(value.shape) for value in operands]
        + [pl.BlockSpec(memory_space=pl.ANY)] * len(others),
        out_specs=[full(shape.shape) for shape in shapes],
        out_shape=shapes,
        compiler_params=params(),
        cost_estimate=cost(2 * tokens * width * lanes, 5e6),
    )(*operands, *others)


def one_hot(slots, count, first):
    groups, tokens = slots.shape
    slot = lax.broadcasted_iota(jnp.int32, (groups, count, tokens), 1).astype(F32)
    same = slots[:, None, :] == slot + float(first)
    return jnp.where(same, 1.0, 0.0).reshape(groups * count, tokens)


def slot_kernel(capacity, meta_ref, col_ref, rows_ref, slots_ref):
    groups, block = slots_ref.shape
    rows, width = rows_ref.shape
    n = rows // groups // capacity
    tokens = block // n
    mask = col_ref[:, width:]
    lanes = mask.shape[1]
    padded = -(-groups // 16) * 16
    group = lax.broadcasted_iota(jnp.int32, (padded, lanes), 0)
    lane = lax.broadcasted_iota(jnp.int32, (padded, lanes), 1)
    wanted = jnp.logical_and(lane == group * n + meta_ref[0], group < groups)
    hits = dot_nt(jnp.where(wanted, 1.0, 0.0).astype(LOW), mask)
    before = lax.broadcasted_iota(jnp.int32, (tokens, tokens), 0)
    after_it = lax.broadcasted_iota(jnp.int32, (tokens, tokens), 1)
    earlier = jnp.where(before < after_it, 1.0, 0.0).astype(LOW)
    for z in range(n):
        hit = hits[:, z * tokens : (z + 1) * tokens]
        rank = dot_nn(hit.astype(LOW), earlier)
        turn = (meta_ref[1 + z] * capacity).astype(F32)
        slot = jnp.where(hit > 0.5, rank + turn, -1.0)
        slots_ref[:, z * tokens : (z + 1) * tokens] = slot[:groups]
    spread = one_hot(slots_ref[...], n * capacity, 0).astype(LOW)
    rows_ref[...] = dot_nn(spread, col_ref[:, :width]).astype(LOW)


def make_slots(meta, col, width, groups, capacity):
    block = col.shape[0]
    n = lax.axis_size("expert")
    shapes = [
        jax.ShapeDtypeStruct((groups * n * capacity, width), LOW),
        jax.ShapeDtypeStruct((groups, block), F32),
    ]
    return pl.pallas_call(
        functools.partial(slot_kernel, capacity),
        grid_spec=pltpu.PrefetchScalarGridSpec(
            num_scalar_prefetch=1,
            grid=(1,),
            in_specs=[full(col.shape)],
            out_specs=[full(shape.shape) for shape in shapes],
        ),
        out_shape=shapes,
        compiler_params=params(),
        cost_estimate=cost(2 * groups * n * capacity * block * width, 8e6),
    )(meta, col)


def table_kernel(capacity, n_half, meta_ref, slots_ref, near_ref, far_ref, near_back_ref, far_back_ref):
    n = 2 * n_half
    tokens = slots_ref.shape[1] // n
    cap_half = n_half * capacity
    for part, (to_ref, back_ref) in enumerate([(near_ref, near_back_ref), (far_ref, far_back_ref)]):
        pieces = []
        for k in range(n_half):
            start = pl.multiple_of(meta_ref[1 + n + part * n_half + k] * tokens, tokens)
            pieces.append(slots_ref[:, pl.ds(start, tokens)])
        spread = one_hot(jnp.concatenate(pieces, axis=1), cap_half, part * cap_half)
        to_ref[...] = spread.astype(LOW)
        back_ref[...] = jnp.transpose(spread).astype(LOW)


def make_tables(meta, slots, n_half, capacity):
    groups, block = slots.shape
    rows = groups * n_half * capacity
    shapes = [jax.ShapeDtypeStruct((rows, block // 2), LOW)] * 2
    shapes += [jax.ShapeDtypeStruct((block // 2, rows), LOW)] * 2
    outs = pl.pallas_call(
        functools.partial(table_kernel, capacity, n_half),
        grid_spec=pltpu.PrefetchScalarGridSpec(
            num_scalar_prefetch=1,
            grid=(1,),
            in_specs=[full(slots.shape)],
            out_specs=[full(shape.shape) for shape in shapes],
        ),
        out_shape=shapes,
        compiler_params=params(),
        cost_estimate=cost(8 * rows * block, 3e6),
    )(meta, slots)
    return outs[:2], outs[2:]


def spread_kernel(choices, place_ref, spread_ref, *refs):
    out_ref, rows_ref = refs[-2:]
    for k, by_place in enumerate(choices):
        for which in sorted(set(by_place)):
            hit = functools.reduce(
                jnp.logical_or,
                [place_ref[0] == i for i, other in enumerate(by_place) if other == which],
            )

            @pl.when(hit)
            def _():
                tokens = refs[which].shape[0]
                rows_ref[k * tokens : (k + 1) * tokens] = refs[which][...]

    out_ref[...] = dot_nn(spread_ref[...], rows_ref[...]).astype(LOW)


def spread_rows(place, spread, found, turns, others):
    n = lax.axis_size("expert")
    order = arrival_order(n)
    distances = sorted({order[i][turn] - i for i in range(n) for turn in turns})
    choices = [[distances.index(order[i][turn] - i) for i in range(n)] for turn in turns]
    chunks = [found[distance] for distance in distances]
    tokens, wide = chunks[0].shape
    rows = spread.shape[0]
    return pl.pallas_call(
        functools.partial(spread_kernel, choices),
        grid_spec=pltpu.PrefetchScalarGridSpec(
            num_scalar_prefetch=1,
            grid=(1,),
            in_specs=[full(spread.shape)]
            + [full(chunk.shape) for chunk in chunks]
            + [pl.BlockSpec(memory_space=pl.ANY)] * len(others),
            out_specs=full((rows, wide)),
            scratch_shapes=[pltpu.VMEM((len(turns) * tokens, wide), LOW)],
        ),
        out_shape=jax.ShapeDtypeStruct((rows, wide), LOW),
        compiler_params=params(),
        cost_estimate=cost(2 * rows * len(turns) * tokens * wide, 5e6),
    )(place, spread, *chunks, *others)


def router_back_kernel(experts, *refs):
    sum_ref, g_ref, hidden_ref, gain_ref, router_ref, mask_ref, probs_ref = refs[:7]
    grad_ref, low_ref, dgain_ref, drouter_ref = refs[-4:]
    width = g_ref.shape[1]
    lanes = mask_ref.shape[1]
    total = sum_ref[...].astype(F32)
    table = total[:, width:]
    mask, probs = mask_ref[...], probs_ref[...]
    grad_gates = (table + pltpu.roll(table, lanes - experts, 1)) * mask
    chosen = probs * mask
    chosen_sum = jnp.sum(chosen, axis=1, keepdims=True)
    mean = jnp.sum(grad_gates * (chosen / chosen_sum), axis=1, keepdims=True)
    centred = mask * (grad_gates - mean) / chosen_sum
    grad_logits = probs * (centred - jnp.sum(centred * chosen, axis=1, keepdims=True))
    high, low = split_low(grad_logits)
    router = pad_rows(router_ref[...], lanes)
    grad = total[:, :width] + dot_nn(high, router) + dot_nn(low, router)
    normal, rr = norm_parts(hidden_ref[...])
    mixed = (normal * gain_ref[...]).astype(LOW)
    drouter_ref[...] = dot_tn(high, mixed) + dot_tn(low, mixed)
    dgain_ref[...] = jnp.sum(grad * normal, axis=0, keepdims=True)
    grad_hidden = g_ref[...].astype(F32) + norm_back(grad, normal, rr, gain_ref[...])
    grad_ref[...] = grad_hidden
    low_ref[...] = grad_hidden.astype(LOW)


def route_back(summed, g, hidden, gain, router, mask, probs, experts, others):
    tokens, width = g.shape
    lanes = mask.shape[1]
    operands = [summed, g, hidden, gain[None], router, mask, probs]
    shapes = [
        jax.ShapeDtypeStruct((tokens, width), F32),
        jax.ShapeDtypeStruct((tokens, width), LOW),
        jax.ShapeDtypeStruct((1, width), F32),
        jax.ShapeDtypeStruct((lanes, width), F32),
    ]
    return pl.pallas_call(
        functools.partial(router_back_kernel, experts),
        grid=(1,),
        in_specs=[full(value.shape) for value in operands]
        + [pl.BlockSpec(memory_space=pl.ANY)] * len(others),
        out_specs=[full(shape.shape) for shape in shapes],
        out_shape=shapes,
        compiler_params=params(),
        cost_estimate=cost(8 * tokens * width * lanes, 8e6),
    )(*operands, *others)


def combine_kernel(n_half, meta_ref, near_table_ref, far_table_ref, near_ref, far_ref, *rest):
    del meta_ref
    turn = pl.program_id(0)

    @pl.when(turn < n_half)
    def _():
        rest[-1][...] = dot_nn(near_table_ref[...], near_ref[...]).astype(LOW)

    @pl.when(turn >= n_half)
    def _():
        rest[-1][...] = dot_nn(far_table_ref[...], far_ref[...]).astype(LOW)


def combine_rows(meta, tables, rows, n_half, others):
    tokens = tables[0].shape[0] // n_half
    slots, wide = rows[0].shape
    n = 2 * n_half
    return pl.pallas_call(
        functools.partial(combine_kernel, n_half),
        grid_spec=pltpu.PrefetchScalarGridSpec(
            num_scalar_prefetch=1,
            grid=(n,),
            in_specs=[
                pl.BlockSpec((tokens, slots), lambda i, m: (jnp.minimum(i, n_half - 1), 0)),
                pl.BlockSpec((tokens, slots), lambda i, m: (jnp.maximum(i - n_half, 0), 0)),
            ]
            + [full(value.shape) for value in rows]
            + [pl.BlockSpec(memory_space=pl.ANY)] * len(others),
            out_specs=pl.BlockSpec((tokens, wide), lambda i, m: (m[1 + n + i], 0)),
        ),
        out_shape=jax.ShapeDtypeStruct((n * tokens, wide), LOW),
        compiler_params=params(),
        cost_estimate=cost(2 * slots * n * tokens * wide, 10e6),
    )(meta, *tables, *rows, *others)


def expert_kernel(experts, who_ref, x_ref, gate_ref, up_ref, pull_ref, *rest):
    act_ref, dgate_ref, dup_ref, copy_ref = rest[-4:]
    width = gate_ref.shape[0]
    x = x_ref[:, :width]
    table = x_ref[:, width:].astype(F32)
    lane = lax.broadcasted_iota(jnp.int32, table.shape, 1)
    mine = who_ref[0]
    gate = jnp.sum(
        jnp.where(jnp.logical_or(lane == mine, lane == mine + experts), table, 0.0),
        axis=1,
        keepdims=True,
    )
    pre_gate = dot_nn(x, gate_ref[...])
    pre_up = dot_nn(x, up_ref[...])
    pull = pull_ref[...].reshape(pre_up.shape)
    sig = 1.0 / (1.0 + jnp.exp(-pre_gate))
    silu = pre_gate * sig
    act = silu * pre_up
    act_ref[...] = (act * gate).astype(LOW)
    high, low = split_low(jnp.sum(act * pull, axis=1, keepdims=True))
    pull = pull * gate
    dup = (pull * silu).astype(LOW)
    dgate = (pull * pre_up * (sig * (1.0 + pre_gate * (1.0 - sig)))).astype(LOW)
    dgate_ref[...] = dgate
    dup_ref[...] = dup
    copy_ref[:, :width] = (dot_nt(dgate, gate_ref[...]) + dot_nt(dup, up_ref[...])).astype(LOW)
    back = jnp.where(lane == mine, high.astype(F32), 0.0)
    back = jnp.where(lane == mine + experts, low.astype(F32), back)
    copy_ref[:, width:] = back.astype(LOW)


def run_expert(who, x, w_gate, w_up, pull, part, experts):
    rows, wide = x.shape
    width, hidden = w_gate.shape
    groups, _, slots, _ = pull.shape
    each = groups // 2
    tile = each * slots
    by_rows = lambda columns: pl.BlockSpec((tile, columns), lambda i, p: (i, 0))
    return pl.pallas_call(
        functools.partial(expert_kernel, experts),
        grid_spec=pltpu.PrefetchScalarGridSpec(
            num_scalar_prefetch=1,
            grid=(2,),
            in_specs=[
                by_rows(wide),
                full(w_gate.shape),
                full(w_up.shape),
                pl.BlockSpec((each, 1, slots, hidden), lambda i, p: (i, part, 0, 0)),
            ],
            out_specs=[by_rows(hidden), by_rows(hidden), by_rows(hidden), by_rows(wide)],
        ),
        out_shape=[jax.ShapeDtypeStruct((rows, hidden), LOW)] * 3
        + [jax.ShapeDtypeStruct((rows, wide), LOW)],
        compiler_params=params(),
        cost_estimate=cost(8 * rows * width * hidden, 20e6, rows * hidden),
    )(who, x, w_gate, w_up, pull)


def input_kernel(grad_ref, x_ref, gain_ref, more_ref, out_ref):
    normal, rr = norm_parts(x_ref[...].astype(F32))
    grad = grad_ref[...].astype(F32)
    out_ref[...] = more_ref[...] + norm_back(grad, normal, rr, gain_ref[...])


def input_back(grad, x, gain, more):
    tokens, width = x.shape
    operands = [grad, x, gain[None], more]
    return pl.pallas_call(
        input_kernel,
        grid=(1,),
        in_specs=[full(value.shape) for value in operands],
        out_specs=full(more.shape),
        out_shape=jax.ShapeDtypeStruct((tokens, width), F32),
        compiler_params=params(),
        cost_estimate=cost(20 * tokens * width, 5e6),
    )(*operands)


def kv_back_kernel(factor, parts_ref, proj_ref, gain_ref, cos_ref, sin_ref, *rest):
    grad_ref, dgain_ref = rest[-2:]
    size = proj_ref.shape[1]
    total = parts_ref[0].astype(F32)
    for k in range(1, parts_ref.shape[0]):
        total += parts_ref[k].astype(F32)
    grad, dgain = head_backward(
        total[:, :size] * factor, proj_ref[...], gain_ref[...], cos_ref[...], sin_ref[...]
    )
    grad_ref[:, :size] = grad.astype(LOW)
    grad_ref[:, size:] = total[:, size:].astype(LOW)
    dgain_ref[...] = dgain


def kv_back(parts, proj, gain, cos2, sin2, factor, others):
    block, size = proj.shape
    operands = [parts, proj, gain[None], cos2, sin2]
    shapes = [
        jax.ShapeDtypeStruct((block, 2 * size), LOW),
        jax.ShapeDtypeStruct((1, size), F32),
    ]
    return pl.pallas_call(
        functools.partial(kv_back_kernel, factor),
        grid=(1,),
        in_specs=[full(value.shape) for value in operands]
        + [pl.BlockSpec(memory_space=pl.ANY)] * len(others),
        out_specs=[full(shape.shape) for shape in shapes],
        out_shape=shapes,
        compiler_params=params(),
        cost_estimate=cost(40 * block * size, 5e6),
    )(*operands, *others)


def pair_kernel(a_ref, b_ref, *rest):
    rest[-1][...] = (a_ref[...].astype(F32) + b_ref[...].astype(F32)).astype(LOW)


def pair_sum(a, b, others):
    rows, columns = a.shape
    tiles = 2 if rows % 32 == 0 else 1
    spec = pl.BlockSpec((rows // tiles, columns), lambda i: (i, 0))
    return pl.pallas_call(
        pair_kernel,
        grid=(tiles,),
        in_specs=[spec, spec] + [pl.BlockSpec(memory_space=pl.ANY)] * len(others),
        out_specs=spec,
        out_shape=jax.ShapeDtypeStruct((rows, columns), LOW),
        compiler_params=params(),
        cost_estimate=cost(rows * columns, 6 * rows * columns),
    )(a, b, *others)


def fold_kernel(n_pairs, s_ref, *refs):
    del s_ref
    send_ref, keep_ref = refs[-2:]
    totals = [
        (refs[2 * k][...].astype(F32) + refs[2 * k + 1][...].astype(F32)).astype(LOW)
        for k in range(n_pairs)
    ]
    for half, out_ref in enumerate((send_ref, keep_ref)):

        @pl.when(pl.program_id(0) == half)
        def _():
            first = 0
            for total in totals:
                last = first + total.shape[1]
                out_ref[:, first:last] = total
                first = last


def fold(pairs, bit, others):
    rows = pairs[0][1].shape[0]
    columns = sum(got.shape[1] for _, got in pairs)
    tiles = 2
    tile = rows // (2 * tiles)
    side = lambda h, m: (1 - m[0]) * (1 - h) + m[0] * h
    specs = []
    for _, got in pairs:
        wide = got.shape[1]
        specs += [pl.BlockSpec((tile, wide), lambda h, j, m: (side(h, m) * tiles + j, 0))] * 2
    shape = jax.ShapeDtypeStruct((rows // 2, columns), LOW)
    return pl.pallas_call(
        functools.partial(fold_kernel, len(pairs)),
        grid_spec=pltpu.PrefetchScalarGridSpec(
            num_scalar_prefetch=1,
            grid=(2, tiles),
            in_specs=specs + [pl.BlockSpec(memory_space=pl.ANY)] * len(others),
            out_specs=[
                pl.BlockSpec((tile, columns), lambda h, j, m: (j * (1 - h) + (tiles - 1) * h, 0)),
                pl.BlockSpec((tile, columns), lambda h, j, m: (j * h, 0)),
            ],
        ),
        out_shape=[shape, shape],
        compiler_params=params(),
        cost_estimate=cost(rows * columns, 6 * rows * columns),
    )(
        bit.astype(jnp.int32)[None],
        *[value for pair in pairs for value in pair],
        *others,
    )


def normed_kernel(q_ref, kv_ref, wq_ref, wkv_ref, rows_ref, *rest):
    out_ref, dgain_ref = rest[-2:]
    grad = dot_nt(q_ref[...], wq_ref[...]) + dot_nt(kv_ref[...], wkv_ref[...])
    out_ref[...] = grad.astype(LOW)
    dgain_ref[...] = jnp.sum(grad * rows_ref[...].astype(F32), axis=0, keepdims=True)


def normed_back(grad_q, grad_kv, w_q, w_kv, rows, others):
    block, width = rows.shape
    tile = 512
    column = lambda i: (0, i)
    return pl.pallas_call(
        normed_kernel,
        grid=(width // tile,),
        in_specs=[
            full(grad_q.shape),
            full(grad_kv.shape),
            pl.BlockSpec((tile, w_q.shape[1]), lambda i: (i, 0)),
            pl.BlockSpec((tile, w_kv.shape[1]), lambda i: (i, 0)),
            pl.BlockSpec((block, tile), column),
        ]
        + [pl.BlockSpec(memory_space=pl.ANY)] * len(others),
        out_specs=[pl.BlockSpec((block, tile), column), pl.BlockSpec((1, tile), column)],
        out_shape=[
            jax.ShapeDtypeStruct((block, width), LOW),
            jax.ShapeDtypeStruct((1, width), F32),
        ],
        compiler_params=params(),
        cost_estimate=cost(2 * block * width * (w_q.shape[1] + w_kv.shape[1]), 12e6),
    )(grad_q, grad_kv, w_q, w_kv, rows, *others)


def pack_kernel(experts, router_ref, attn_ref, gain_ref, mlp_ref, q_ref, k_ref, *rest):
    out_ref, rows_ref = rest[-2:]
    size = q_ref.shape[1]
    rows_ref[:experts] = router_ref[:experts]
    rows_ref[experts:] = jnp.zeros_like(rows_ref[experts:])
    rows_ref[experts : experts + 1] = attn_ref[...] / gain_ref[...]
    rows_ref[experts + 1 : experts + 2] = mlp_ref[...]
    rows_ref[experts + 2 : experts + 3, :size] = q_ref[...]
    rows_ref[experts + 2 : experts + 3, size : 2 * size] = k_ref[...]
    out_ref[...] = rows_ref[...].astype(LOW)


def pack_small(experts, router, attn, gain, mlp, q, k, others):
    width = attn.shape[1]
    n = lax.axis_size(ALL_AXES)
    shape = (-(-(experts + 3) // n) * n, width)
    operands = [router, attn, gain[None], mlp, q, k]
    return pl.pallas_call(
        functools.partial(pack_kernel, experts),
        grid=(1,),
        in_specs=[full(value.shape) for value in operands]
        + [pl.BlockSpec(memory_space=pl.ANY)] * len(others),
        out_specs=full(shape),
        out_shape=jax.ShapeDtypeStruct(shape, LOW),
        scratch_shapes=[pltpu.VMEM(shape, F32)],
        compiler_params=params(),
        cost_estimate=cost(shape[0] * width, 6 * shape[0] * width),
    )(*operands, *others)


def part_sum_kernel(parts_ref, *rest):
    total = parts_ref[0].astype(F32)
    for k in range(1, parts_ref.shape[0]):
        total += parts_ref[k].astype(F32)
    rest[-1][...] = total.astype(LOW)


def part_sum(parts, others):
    count, rows, columns = parts.shape
    tiles = 2
    return pl.pallas_call(
        part_sum_kernel,
        grid=(tiles,),
        in_specs=[pl.BlockSpec((count, rows // tiles, columns), lambda i: (0, i, 0))]
        + [pl.BlockSpec(memory_space=pl.ANY)] * len(others),
        out_specs=pl.BlockSpec((rows // tiles, columns), lambda i: (i, 0)),
        out_shape=jax.ShapeDtypeStruct((rows, columns), LOW),
        compiler_params=params(),
        cost_estimate=cost(count * rows * columns, 4 * count * rows * columns),
    )(parts, *others)


def widen_kernel(n_chunks, n_outs, at_ref, *refs):
    del at_ref
    outs = refs[-n_outs:]
    widths = [ref.shape[1] for ref in outs]
    for k in range(n_chunks):

        @pl.when(pl.program_id(0) == k)
        def _():
            first = 0
            for wide, out_ref in zip(widths, outs):
                out_ref[...] = refs[k][:, first : first + wide].astype(F32)
                first += wide


def widen(places, chunks, widths, others):
    rows, columns = chunks[0].shape
    count = len(chunks)
    return pl.pallas_call(
        functools.partial(widen_kernel, count, len(widths)),
        grid_spec=pltpu.PrefetchScalarGridSpec(
            num_scalar_prefetch=1,
            grid=(count,),
            in_specs=[full(chunk.shape) for chunk in chunks]
            + [pl.BlockSpec(memory_space=pl.ANY)] * len(others),
            out_specs=[pl.BlockSpec((rows, wide), lambda i, at: (at[i], 0)) for wide in widths],
        ),
        out_shape=[jax.ShapeDtypeStruct((count * rows, wide), F32) for wide in widths],
        compiler_params=params(),
        cost_estimate=cost(rows * columns, 6 * count * rows * columns),
    )(jnp.stack(places).astype(jnp.int32), *chunks, *others)


def swap_dp(rows):
    return lax.ppermute(rows, "dp", [(0, 1), (1, 0)])


def swap_context(rows, s):
    n = lax.axis_size("context")
    return lax.ppermute(rows, "context", [(i, i ^ s) for i in range(n)])


def plane_turns():
    d, c = lax.axis_index("dp"), lax.axis_index("context")
    low, high = lax.rem(c, 2), lax.div(c, 2)

    def swap(first, second):
        perm = [(i, i ^ first) for i in range(4)] + [(4 + i, 4 + (i ^ second)) for i in range(4)]
        return lambda rows: lax.ppermute(rows, GROUP_AXES, perm)

    return [
        (jnp.where(d == 0, low, high), swap(1, 2)),
        (jnp.where(d == 0, high, low), swap(2, 1)),
    ]


def plane_first(pairs, others):
    (bit_1, _), _ = plane_turns()
    return fold(pairs, bit_1, others)


def plane_second(send, keep, others):
    (_, swap_1), (bit_2, _) = plane_turns()
    return fold([(keep, swap_1(send))], bit_2, others)


def plane_last(send, keep, others):
    _, (_, swap_2) = plane_turns()
    return pair_sum(keep, swap_2(send), others)


def plane_spread(own):
    (_, swap_1), (_, swap_2) = plane_turns()
    second = swap_2(own)
    return [own, second, swap_1(own), swap_1(second)]


def quarter_places(rank):
    d = lax.axis_index("dp")
    c = lax.axis_index("context")
    low, high = lax.rem(c, 2), lax.div(c, 2)
    places = []
    for core in (d, 1 - d):
        bit_1 = jnp.where(core == 0, low, high)
        bit_2 = jnp.where(core == 0, high, low)
        for flip_1, flip_2 in ((0, 0), (0, 1), (1, 0), (1, 1)):
            places.append(4 * core + rank(core, bit_1 ^ flip_1, bit_2 ^ flip_2))
    return places


def widen_all(quarters, places, widths, others):
    return widen(places, quarters + [swap_dp(part) for part in quarters], widths, others)


def arrival_order(n):
    return [sorted(range(n), key=lambda j: (abs(j - i), j)) for i in range(n)]


def choose(index, options):
    distinct = []
    for option in options:
        if option is not None and not any(option is other for other in distinct):
            distinct.append(option)
    result = distinct[0]
    for option in distinct[1:]:
        mask = functools.reduce(
            jnp.logical_or, [index == i for i, other in enumerate(options) if other is option]
        )
        result = jnp.where(mask, option, result)
    return result


def line_gather(chunk):
    return line_steps({0: chunk}, 1, lax.axis_size("expert"))


def line_steps(found, first, stop):
    n = lax.axis_size("expert")
    found = dict(found)
    for s in range(first, stop):
        found[-s] = lax.ppermute(
            found[1 - s], "expert", [(i, i + 1) for i in range(s - 1, n - 1)]
        )
        found[s] = lax.ppermute(found[s - 1], "expert", [(i + 1, i) for i in range(n - s)])
    return found


def context_gather(rows):
    n = lax.axis_size("context")
    c = lax.axis_index("context")
    found = {0: rows}
    for s in range(1, n):
        found[s] = lax.ppermute(rows, "context", [(i, i ^ s) for i in range(n)])
    return jnp.concatenate([choose(c, [found[i ^ j] for i in range(n)]) for j in range(n)], axis=0)


def zero_of(*others):
    return functools.reduce(
        jnp.add,
        [
            lax.slice(other, (0,) * other.ndim, (1,) * other.ndim).reshape(()).astype(F32) * 0.0
            for other in others
        ],
    )


def after(value, *others):
    return (value.astype(F32) + zero_of(*others)).astype(value.dtype)


def on_device(
    layer_input,
    grad_output,
    attn_gain,
    query_weight,
    key_weight,
    value_weight,
    q_gain,
    k_gain,
    output_weight,
    mlp_gain,
    router,
    w_gate,
    w_up,
    w_down,
    routes,
    half_order,
):
    n_context = lax.axis_size("context")
    n_expert = lax.axis_size("expert")
    n_groups = lax.axis_size(GROUP_AXES)
    tok_dev, width = layer_input.shape[1:]
    size = q_gain.shape[0]
    kv_total = key_weight.shape[1] * n_expert
    group_dev = n_expert // (kv_total // size)
    kv_index = lax.axis_index("expert") // group_dev
    block = tok_dev * n_expert
    seq = block * n_context
    half = block // 2
    experts = router.shape[1]
    exp_dev = w_gate.shape[0]
    top = routes.shape[2]
    capacity = max(2, (tok_dev * top * 9 + 8 * experts - 1) // (8 * experts))
    scale = size ** (-0.5)

    seq_rows = jnp.arange(seq, dtype=jnp.int32)
    context = lax.axis_index("context")
    own_halves = lax.dynamic_slice_in_dim(half_order, 2 * context, 2)
    own_pos = (own_halves[:, None] * half + jnp.arange(half, dtype=jnp.int32)[None]).reshape(-1)
    per_half = half // TILE
    tile_pos = (half_order[:, None] * per_half + jnp.arange(per_half, dtype=jnp.int32)).reshape(-1)
    kidx = jnp.sum(
        (tile_pos[None, :] == jnp.arange(seq // TILE, dtype=jnp.int32)[:, None])
        * jnp.arange(seq // TILE, dtype=jnp.int32)[None, :],
        axis=1,
    ).astype(jnp.int32)
    qpos = lax.dynamic_slice_in_dim(tile_pos, context * (block // TILE), block // TILE)
    entry = jnp.arange(size)
    freq = jnp.power(THETA, -(2 * (entry % (size // 2))).astype(F32) / size)
    angles = own_pos.astype(F32)[:, None] * freq[None, :]
    cos2 = jnp.cos(angles)
    sin2 = jnp.sin(angles) * jnp.where(entry < size // 2, -1.0, 1.0)[None, :]

    place = lax.axis_index("expert")
    place_1 = place.astype(jnp.int32)[None]
    lanes = -(-2 * experts // 128) * 128
    mask = jnp.any(
        routes[0][:, :, None] == jnp.arange(lanes, dtype=jnp.int32)[None, None, :], axis=1
    )
    mask_wide = mask.astype(F32)
    router_rows = router.T

    x_low = layer_input[0]
    x_normal, _ = norm_parts(x_low.astype(F32))
    normed_found = line_gather((x_normal * attn_gain).astype(LOW))
    if group_dev == 1:
        kv_weights = jnp.concatenate([key_weight, value_weight], axis=1)
    else:
        key_whole = lax.all_gather(key_weight, "expert", axis=1, tiled=True)
        value_whole = lax.all_gather(value_weight, "expert", axis=1, tiled=True)
        kv_weights = jnp.concatenate(
            [
                lax.dynamic_slice_in_dim(key_whole, kv_index * size, size, 1),
                lax.dynamic_slice_in_dim(value_whole, kv_index * size, size, 1),
            ],
            axis=1,
        )
    grad_low = grad_output[0]
    normed_rows, own_kv, key_proj, grad_wide = project_keys(
        place_1,
        normed_found,
        kv_weights,
        k_gain,
        cos2,
        sin2,
        scale * LOG2E,
        grad_low,
        mask_wide,
    )
    grad_col = lax.all_gather(grad_wide, "expert", axis=0, tiled=True)
    kv_whole = context_gather(own_kv)
    queries, query_proj = project_queries(normed_rows, query_weight, q_gain, cos2, sin2)

    n_half = n_expert // 2
    order_here = jnp.asarray(arrival_order(n_expert), jnp.int32)[place]
    turn_here = jnp.sum(
        (order_here[:, None] == jnp.arange(n_expert, dtype=jnp.int32)[None, :])
        * jnp.arange(n_expert, dtype=jnp.int32)[:, None],
        axis=0,
    ).astype(jnp.int32)
    meta = jnp.concatenate([place_1, turn_here, order_here])
    grad_sent, slots = make_slots(meta, grad_col, width, n_groups, capacity)
    spreads, back_tables = make_tables(meta, slots, n_half, capacity)

    def swap_plane(rows):
        parts = rows.reshape(n_groups, -1, rows.shape[1])
        parts = lax.all_to_all(parts, GROUP_AXES, split_axis=0, concat_axis=0, tiled=True)
        return parts.reshape(rows.shape)

    attended, inverse = attend(qpos, kidx, queries, kv_whole, [])
    attn_part = out_dot(attended, output_weight, [grad_col])
    attn_rows = lax.psum_scatter(attn_part, "expert", scatter_dimension=0, tiled=True)

    grad_x = swap_plane(grad_sent)
    act_pull = dot_nt(grad_x, w_down[0]).reshape(n_groups, 2, n_half * capacity, -1)

    hidden, mixed, probs = route_rows(
        x_low, attn_rows, mlp_gain, router_rows, mask_wide, experts, []
    )

    who = (lax.axis_index(ALL_AXES) * exp_dev).astype(jnp.int32)[None]
    mixed_found = line_gather(mixed)
    near = spread_rows(place_1, spreads[0], mixed_found, range(n_half), [grad_x])
    x_near = swap_plane(near)
    worked_near = run_expert(who, x_near, w_gate[0], w_up[0], act_pull, 0, experts)
    far = spread_rows(place_1, spreads[1], mixed_found, range(n_half, n_expert), [x_near])
    x_far = swap_plane(far)
    worked_far = run_expert(who, x_far, w_gate[0], w_up[0], act_pull, 1, experts)
    xs = [x_near, x_far]
    acts, gate_lows, up_lows, copies = (list(pair) for pair in zip(worked_near, worked_far))
    back_far = swap_plane(copies[1])
    back_near = swap_plane(copies[0])
    join = lambda parts: jnp.concatenate(parts, axis=0)
    x_all = join([x[:, :width] for x in xs])
    grad_w_gate = dot_tn(x_all, join(gate_lows))
    grad_w_up = dot_tn(x_all, join(up_lows))
    grad_by_round = jnp.swapaxes(
        grad_x.reshape(n_groups, 2, n_half * capacity, width), 0, 1
    ).reshape(-1, width)
    grad_w_down = dot_tn(join(acts), grad_by_round)
    copies_col = combine_rows(
        meta, back_tables, [back_near, back_far], n_half, [grad_w_gate, grad_w_up]
    )
    copies_sum = lax.psum_scatter(copies_col, "expert", scatter_dimension=0, tiled=True)

    returned = [dot_nn(act, w_down[0]).astype(LOW) for act in acts]
    returned_near = swap_plane(returned[0])

    grad_hidden, grad_hidden_low, grad_mlp_gain, grad_router = route_back(
        copies_sum,
        grad_low,
        hidden,
        mlp_gain,
        router_rows,
        mask_wide,
        probs,
        experts,
        [returned_near, grad_w_down],
    )

    returned_far = swap_plane(returned[1])
    grad_attn = lax.all_gather(grad_hidden_low, "expert", axis=0, tiled=True)
    grad_o, centre = grad_attended(
        grad_attn, output_weight, attended, inverse, [returned_far]
    )
    combined = combine_rows(meta, back_tables, [returned_near, returned_far], n_half, [])
    output_rows = lax.psum_scatter(combined, "expert", scatter_dimension=0, tiled=True)
    w_out = token_dot(attended, grad_attn, [combined])
    w_out_parts = swap_plane(w_out)
    grad_kv, grad_q, grad_q_gain = attend_back(
        qpos,
        kidx,
        queries,
        grad_o,
        centre,
        kv_whole,
        query_proj,
        q_gain,
        cos2,
        sin2,
        [w_out],
    )
    kv_parts = lax.all_to_all(
        grad_kv.astype(LOW).reshape(n_context, block, 2 * size),
        "context",
        split_axis=0,
        concat_axis=0,
        tiled=True,
    )
    w_query_send, w_query_keep = token_halves(normed_rows, grad_q, [w_out_parts])
    w_query_got = swap_dp(w_query_send)
    output_rows = hidden + output_rows.astype(F32) + zero_of(w_query_keep)

    kv_grads, grad_k_gain = kv_back(
        kv_parts, key_proj, k_gain, cos2, sin2, scale, [w_query_keep]
    )
    w_out_quarters = plane_spread(part_sum(w_out_parts.reshape(n_groups, -1, width), [kv_parts]))
    pairs = [(w_query_keep, w_query_got)]
    widths = [query_weight.shape[1]]
    if group_dev == 1:
        w_kv_send, w_kv_keep = token_halves(normed_rows, kv_grads, [])
        pairs.append((w_kv_keep, swap_dp(w_kv_send)))
        widths += [key_weight.shape[1], value_weight.shape[1]]
    send, keep = plane_first(pairs, w_out_quarters)

    grad_normed, gain_rows = normed_back(
        grad_q, kv_grads, query_weight, kv_weights, normed_rows, [keep]
    )
    (grad_w_out,) = widen_all(
        w_out_quarters,
        quarter_places(lambda core, b1, b2: jnp.where(core == 0, b1 + 2 * b2, 2 * b1 + b2)),
        [width],
        [],
    )
    small = pack_small(
        experts,
        grad_router,
        gain_rows,
        attn_gain,
        grad_mlp_gain,
        grad_q_gain,
        grad_k_gain,
        [],
    )
    swap_all = lambda rows: lax.all_to_all(rows, ALL_AXES, split_axis=0, concat_axis=0, tiled=True)
    small_parts = swap_all(small.reshape(lax.axis_size(ALL_AXES), -1, width))
    small_own = jnp.sum(small_parts.astype(F32), axis=0).astype(LOW)
    second_send, second_keep = plane_second(send, keep, [grad_normed])
    quarter = plane_last(second_send, second_keep, [output_rows, small_own])
    grad_normed = lax.psum_scatter(grad_normed, "expert", scatter_dimension=0, tiled=True)
    grad_input = input_back(grad_normed, x_low, attn_gain, grad_hidden)
    small_sum = swap_all(jnp.broadcast_to(small_own[None], small_parts.shape))
    small_sum = small_sum.reshape(small.shape).astype(F32)
    quarters = [quarter] + [swap_context(quarter, s) for s in range(1, n_context)]
    d = lax.axis_index("dp")
    turned = lambda core, c: jnp.where(core == 0, 2 * lax.rem(c, 2) + lax.div(c, 2), c)
    places = [4 * core + turned(core, context ^ s) for core in (d, 1 - d) for s in range(n_context)]
    grad_w_query, *more = widen_all(quarters, places, widths, [grad_w_out, grad_input, small_sum])
    if group_dev == 1:
        grad_w_key, grad_w_value = more
    else:
        w_kv = token_dot(normed_rows, kv_grads, [])
        blank = jnp.zeros((width, kv_total), LOW)
        pieces = []
        for part in (w_kv[:, :size], w_kv[:, size:]):
            padded = lax.dynamic_update_slice(blank, part, (0, kv_index * size))
            pieces.append(lax.psum_scatter(padded, "expert", scatter_dimension=1, tiled=True))
        grad_w_key, grad_w_value = (lax.psum(piece, GROUP_AXES).astype(F32) for piece in pieces)
    grad_attn_gain, grad_mlp_gain = small_sum[experts], small_sum[experts + 1]
    grad_q_gain = small_sum[experts + 2, :size]
    grad_k_gain = small_sum[experts + 2, size : 2 * size]
    return (
        output_rows.astype(LOW)[None],
        grad_input[None],
        grad_attn_gain,
        grad_w_query,
        grad_w_key,
        grad_w_value,
        grad_q_gain,
        grad_k_gain,
        grad_w_out,
        grad_mlp_gain,
        small_sum[:experts].T,
        grad_w_gate[None],
        grad_w_up[None],
        grad_w_down[None],
    )


def solution(mesh):
    rows = P("dp", ("context", "expert"), None)
    expert = P(ALL_AXES, None, None)
    columns = P(None, "expert")
    in_specs = (
        rows,
        rows,
        P(),
        columns,
        columns,
        columns,
        P(),
        P(),
        P("expert", None),
        P(),
        P(),
        expert,
        expert,
        expert,
        rows,
        P(),
    )
    out_specs = (
        rows,
        rows,
        P(),
        columns,
        columns,
        columns,
        P(),
        P(),
        P("expert", None),
        P(),
        P(),
        expert,
        expert,
        expert,
    )
    return jax.shard_map(
        on_device, mesh=mesh, in_specs=in_specs, out_specs=out_specs, check_vma=False
    )
```

```python
import functools
import math

import jax
import jax.numpy as jnp
from jax import lax
from jax.experimental import pallas as pl
from jax.experimental.pallas import tpu as pltpu
from jax.sharding import PartitionSpec as P

EPS = 1e-06
THETA = 1000000.0
TILE = 256
PIECE = 128
VMEM_BYTES = 56 * 1024 * 1024
LOG2E = math.log2(math.e)
LOW = jnp.bfloat16
F32 = jnp.float32
ALL_AXES = ("dp", "context", "expert")
GROUP_AXES = ("dp", "context")


def dot_nn(a, b):
    return lax.dot_general(a, b, (((1,), (0,)), ((), ())), preferred_element_type=F32)


def dot_nt(a, b):
    return lax.dot_general(a, b, (((1,), (1,)), ((), ())), preferred_element_type=F32)


def dot_tn(a, b):
    return lax.dot_general(a, b, (((0,), (0,)), ((), ())), preferred_element_type=F32)


def params(**more):
    return pltpu.CompilerParams(vmem_limit_bytes=VMEM_BYTES, **more)


def cost(flops, nbytes, exps=0):
    return pl.CostEstimate(flops=int(flops), bytes_accessed=int(nbytes), transcendentals=int(exps))


def head_forward(u, gain, cos2, sin2):
    rr = lax.rsqrt(jnp.mean(u * u, axis=-1, keepdims=True) + EPS)
    y = u * rr * gain
    return y * cos2 + pltpu.roll(y, 64, 1) * sin2


def head_backward(gy, u, gain, cos2, sin2):
    g = gy * cos2 - pltpu.roll(gy, 64, 1) * sin2
    rr = lax.rsqrt(jnp.mean(u * u, axis=-1, keepdims=True) + EPS)
    n = u * rr
    gn = g * gain
    grad = rr * (gn - n * jnp.mean(gn * n, axis=-1, keepdims=True))
    return grad, jnp.sum(g * n, axis=0, keepdims=True)


def query_kernel(x_ref, w_ref, gain_ref, cos_ref, sin_ref, rot_ref, proj_ref):
    tiles, heads, rows, size = rot_ref.shape
    acc = dot_nn(x_ref[...], w_ref[...])
    for h in range(heads):
        u = acc[:, h * size : (h + 1) * size]
        rot = head_forward(u, gain_ref[...], cos_ref[...], sin_ref[...])
        proj_ref[:, h] = u.reshape(tiles, rows, size)
        rot_ref[:, h] = rot.astype(LOW).reshape(tiles, rows, size)


def project_queries(normed, weight, gain, cos2, sin2):
    block, width = normed.shape
    size = cos2.shape[1]
    heads = weight.shape[1] // size
    tiles = block // TILE
    whole = lambda i: (0, 0)
    per = lambda i: (0, i, 0, 0)
    shape = (tiles, heads, TILE, size)
    return pl.pallas_call(
        query_kernel,
        grid=(heads // 2,),
        in_specs=[
            pl.BlockSpec((block, width), whole),
            pl.BlockSpec((width, 2 * size), lambda i: (0, i)),
            pl.BlockSpec((1, size), whole),
            pl.BlockSpec((block, size), whole),
            pl.BlockSpec((block, size), whole),
        ],
        out_specs=[pl.BlockSpec((tiles, 2, TILE, size), per)] * 2,
        out_shape=[jax.ShapeDtypeStruct(shape, LOW), jax.ShapeDtypeStruct(shape, F32)],
        compiler_params=params(),
        cost_estimate=cost(2 * block * width * heads * size, 12e6),
    )(normed, weight, gain[None], cos2, sin2)


def put_in_order(place, refs, out_ref):
    n = (len(refs) + 1) // 2
    rows = refs[0].shape[0]
    for distance in range(1 - n, n):
        ref = refs[distance + n - 1]
        at = place + distance

        @pl.when(jnp.logical_and(at >= 0, at < n))
        def _():
            out_ref[pl.ds(pl.multiple_of(at * rows, rows), rows), :] = ref[...]


def chunk_list(found):
    n = (len(found) + 1) // 2
    return [found[distance] for distance in range(1 - n, n)]


def key_kernel(factor, n_chunks, place_ref, *refs):
    w_ref, gain_ref, cos_ref, sin_ref, g_ref, mask_ref = refs[n_chunks:-4]
    rows_ref, kv_ref, proj_ref, wide_ref = refs[-4:]
    size = proj_ref.shape[1]
    width = g_ref.shape[1]
    put_in_order(place_ref[0], refs[:n_chunks], rows_ref)
    wide_ref[:, :width] = g_ref[...]
    wide_ref[:, width:] = mask_ref[...].astype(LOW)
    acc = dot_nn(rows_ref[...], w_ref[...])
    u = acc[:, :size]
    rot = head_forward(u, gain_ref[...], cos_ref[...], sin_ref[...])
    proj_ref[...] = u
    kv_ref[:, :size] = (rot * factor).astype(LOW)
    kv_ref[:, size:] = acc[:, size:].astype(LOW)


def full(shape):
    return pl.BlockSpec(shape, lambda *_: (0,) * len(shape))


def project_keys(place, found, weight, gain, cos2, sin2, factor, g, mask):
    chunks = chunk_list(found)
    rows, width = chunks[0].shape
    block, size = cos2.shape
    operands = [*chunks, weight, gain[None], cos2, sin2, g, mask]
    shapes = [
        jax.ShapeDtypeStruct((block, width), LOW),
        jax.ShapeDtypeStruct((block, 2 * size), LOW),
        jax.ShapeDtypeStruct((block, size), F32),
        jax.ShapeDtypeStruct((rows, width + mask.shape[1]), LOW),
    ]
    return pl.pallas_call(
        functools.partial(key_kernel, factor, len(chunks)),
        grid_spec=pltpu.PrefetchScalarGridSpec(
            num_scalar_prefetch=1,
            grid=(1,),
            in_specs=[full(x.shape) for x in operands],
            out_specs=[full(x.shape) for x in shapes],
        ),
        out_shape=shapes,
        compiler_params=params(),
        cost_estimate=cost(4 * block * width * size, 8e6),
    )(place, *operands)


def in_order(last, step):
    lax.fori_loop(0, lax.div(last, 2), lambda p, c: (step([2 * p, 2 * p + 1], False), c)[1], 0)

    @pl.when(lax.rem(last, 2) == 1)
    def _():
        step([last - 1, last], True)

    @pl.when(lax.rem(last, 2) == 0)
    def _():
        step([last], True)


def attend_kernel(qpos_ref, kidx_ref, q_ref, kv_ref, *rest):
    out_ref, inv_ref, acc_ref = rest[-3:]
    heads, rows, size = q_ref.shape[1:]
    acc_ref[...] = jnp.zeros_like(acc_ref)

    def step(places, masked):
        starts = [pl.multiple_of(kidx_ref[place] * rows, rows) for place in places]
        count = len(places) * rows
        keys = jnp.concatenate([kv_ref[pl.ds(start, rows), :size] for start in starts], axis=0)
        values = jnp.concatenate([kv_ref[pl.ds(start, rows), size:] for start in starts], axis=0)
        values = jnp.concatenate([values, jnp.ones((count, size), LOW)], axis=1)
        for h in range(heads):
            for first in range(0, rows, PIECE):
                part = slice(first, first + PIECE)
                e = jnp.exp2(dot_nt(q_ref[0, h, part], keys))
                if masked:
                    qi = lax.broadcasted_iota(jnp.int32, e.shape, 0) + first
                    ki = lax.broadcasted_iota(jnp.int32, e.shape, 1) - (count - rows)
                    e = jnp.where(ki <= qi, e, 0.0)
                acc_ref[h, part] += dot_nn(e.astype(LOW), values)

    in_order(qpos_ref[pl.program_id(0)], step)
    for h in range(heads):
        inv = 1.0 / acc_ref[h, :, size:]
        inv_ref[0, h] = inv
        out_ref[:, h * size : (h + 1) * size] = (acc_ref[h, :, :size] * inv).astype(LOW)


def attend(qpos, kidx, queries, kv, others):
    tiles, heads, rows, size = queries.shape
    seq = kv.shape[0]
    return pl.pallas_call(
        attend_kernel,
        grid_spec=pltpu.PrefetchScalarGridSpec(
            num_scalar_prefetch=2,
            grid=(tiles,),
            in_specs=[
                pl.BlockSpec((1, heads, rows, size), lambda i, a, b: (i, 0, 0, 0)),
                pl.BlockSpec((seq, 2 * size), lambda i, a, b: (0, 0)),
            ]
            + [pl.BlockSpec(memory_space=pl.ANY)] * len(others),
            out_specs=[
                pl.BlockSpec((rows, heads * size), lambda i, a, b: (i, 0)),
                pl.BlockSpec((1, heads, rows, size), lambda i, a, b: (i, 0, 0, 0)),
            ],
            scratch_shapes=[pltpu.VMEM((heads, rows, 2 * size), F32)],
        ),
        out_shape=[
            jax.ShapeDtypeStruct((tiles * rows, heads * size), LOW),
            jax.ShapeDtypeStruct((tiles, heads, rows, size), F32),
        ],
        compiler_params=params(),
        cost_estimate=cost(
            6 * tiles * rows * heads * seq * size, 8e6, tiles * rows * heads * seq
        ),
    )(qpos, kidx, queries, kv, *others)


def grad_out_kernel(rows_ref, w_ref, o_ref, inv_ref, *rest):
    do_ref, centre_ref = rest[-2:]
    tiles, heads, rows, size = do_ref.shape
    acc = dot_nt(rows_ref[...], w_ref[...])
    for t in range(tiles):
        for h in range(heads):
            part = slice(t * rows, (t + 1) * rows), slice(h * size, (h + 1) * size)
            low = (acc[part] * inv_ref[t, h]).astype(LOW)
            do_ref[t, h] = low
            product = low.astype(F32) * o_ref[part].astype(F32)
            centre = jnp.sum(jnp.transpose(product), axis=0, keepdims=True)
            centre_ref[t, h] = jnp.broadcast_to(centre, (8, rows))


def grad_attended(grad_rows, weight, attended, inverse, others):
    tiles, heads, rows, size = inverse.shape
    block, width = grad_rows.shape
    return pl.pallas_call(
        grad_out_kernel,
        grid=(heads // 2,),
        in_specs=[
            pl.BlockSpec((block, width), lambda i: (0, 0)),
            pl.BlockSpec((2 * size, width), lambda i: (i, 0)),
            pl.BlockSpec((block, 2 * size), lambda i: (0, i)),
            pl.BlockSpec((tiles, 2, rows, size), lambda i: (0, i, 0, 0)),
        ]
        + [pl.BlockSpec(memory_space=pl.ANY)] * len(others),
        out_specs=[
            pl.BlockSpec((tiles, 2, rows, size), lambda i: (0, i, 0, 0)),
            pl.BlockSpec((tiles, 2, 8, rows), lambda i: (0, i, 0, 0)),
        ],
        out_shape=[
            jax.ShapeDtypeStruct((tiles, heads, rows, size), LOW),
            jax.ShapeDtypeStruct((tiles, heads, 8, rows), F32),
        ],
        compiler_params=params(),
        cost_estimate=cost(2 * block * width * heads * size, 12e6),
    )(grad_rows, weight, attended, inverse, *others)


def attend_back_kernel(
    qpos_ref,
    kidx_ref,
    q_ref,
    do_ref,
    centre_ref,
    kv_ref,
    proj_ref,
    gain_ref,
    cos_ref,
    sin_ref,
    *rest,
):
    dkv_ref, dq_ref, dgain_ref, acc_ref, e_ref, ds_ref = rest[-6:]
    heads, rows, size = q_ref.shape[1:]

    @pl.when(pl.program_id(0) == 0)
    def _():
        dkv_ref[...] = jnp.zeros_like(dkv_ref)
        dgain_ref[...] = jnp.zeros_like(dgain_ref)

    acc_ref[...] = jnp.zeros_like(acc_ref)

    def step(places, masked):
        starts = [pl.multiple_of(kidx_ref[place] * rows, rows) for place in places]
        count = len(places) * rows
        keys = jnp.concatenate([kv_ref[pl.ds(start, rows), :size] for start in starts], axis=0)
        values = jnp.concatenate([kv_ref[pl.ds(start, rows), size:] for start in starts], axis=0)
        for h in range(heads):
            query, grad = q_ref[0, h], do_ref[0, h]
            centre = centre_ref[0, h, 0:1]
            columns = slice(h * rows, (h + 1) * rows)
            for first in range(0, count, PIECE):
                part = slice(first, first + PIECE)
                e = jnp.exp2(dot_nt(keys[part], query))
                if masked and first >= count - rows:
                    ki = lax.broadcasted_iota(jnp.int32, e.shape, 0) + (first - (count - rows))
                    qi = lax.broadcasted_iota(jnp.int32, e.shape, 1)
                    e = jnp.where(ki <= qi, e, 0.0)
                ds = e * (dot_nt(values[part], grad) - centre)
                e_ref[part, columns] = e.astype(LOW)
                ds_ref[part, columns] = ds.astype(LOW)
            acc_ref[h] += dot_tn(ds_ref[:count, columns], keys)
        dk = dot_nn(ds_ref[:count], q_ref[0].reshape(heads * rows, size))
        dv = dot_nn(e_ref[:count], do_ref[0].reshape(heads * rows, size))
        for k, start in enumerate(starts):
            dkv_ref[pl.ds(start, rows), :size] += dk[k * rows : (k + 1) * rows]
            dkv_ref[pl.ds(start, rows), size:] += dv[k * rows : (k + 1) * rows]

    in_order(qpos_ref[pl.program_id(0)], step)
    total = jnp.zeros((1, size), F32)
    for h in range(heads):
        grad, gain_part = head_backward(
            acc_ref[h] * (1.0 / LOG2E), proj_ref[0, h], gain_ref[...], cos_ref[...], sin_ref[...]
        )
        dq_ref[:, h * size : (h + 1) * size] = grad.astype(LOW)
        total += gain_part
    dgain_ref[...] += total


def attend_back(qpos, kidx, queries, grads, centre, kv, proj, gain, cos2, sin2, others):
    tiles, heads, rows, size = queries.shape
    seq = kv.shape[0]
    per = pl.BlockSpec((1, heads, rows, size), lambda i, a, b: (i, 0, 0, 0))
    flat = lambda i, a, b: (0, 0)
    rowwise = lambda i, a, b: (i, 0)
    return pl.pallas_call(
        attend_back_kernel,
        grid_spec=pltpu.PrefetchScalarGridSpec(
            num_scalar_prefetch=2,
            grid=(tiles,),
            in_specs=[
                per,
                per,
                pl.BlockSpec((1, heads, 8, rows), lambda i, a, b: (i, 0, 0, 0)),
                pl.BlockSpec((seq, 2 * size), flat),
                per,
                pl.BlockSpec((1, size), flat),
                pl.BlockSpec((rows, size), rowwise),
                pl.BlockSpec((rows, size), rowwise),
            ]
            + [pl.BlockSpec(memory_space=pl.ANY)] * len(others),
            out_specs=[
                pl.BlockSpec((seq, 2 * size), flat),
                pl.BlockSpec((rows, heads * size), rowwise),
                pl.BlockSpec((1, size), flat),
            ],
            scratch_shapes=[pltpu.VMEM((heads, rows, size), F32)]
            + [pltpu.VMEM((2 * rows, heads * rows), LOW)] * 2,
        ),
        out_shape=[
            jax.ShapeDtypeStruct((seq, 2 * size), F32),
            jax.ShapeDtypeStruct((tiles * rows, heads * size), LOW),
            jax.ShapeDtypeStruct((1, size), F32),
        ],
        compiler_params=params(),
        cost_estimate=cost(
            15 * tiles * rows * heads * seq * size, 12e6, tiles * rows * heads * seq
        ),
    )(qpos, kidx, queries, grads, centre, kv, proj, gain[None], cos2, sin2, *others)


def out_kernel(a_ref, b_ref, *rest):
    rest[-1][...] = dot_nn(a_ref[...], b_ref[...]).astype(LOW)


def out_dot(a, b, others):
    block, inner = a.shape
    columns = b.shape[1]
    tile = min(columns, 512)
    return pl.pallas_call(
        out_kernel,
        grid=(columns // tile,),
        in_specs=[
            pl.BlockSpec((block, inner), lambda i: (0, 0)),
            pl.BlockSpec((inner, tile), lambda i: (0, i)),
        ]
        + [pl.BlockSpec(memory_space=pl.ANY)] * len(others),
        out_specs=pl.BlockSpec((block, tile), lambda i: (0, i)),
        out_shape=jax.ShapeDtypeStruct((block, columns), LOW),
        compiler_params=params(),
        cost_estimate=cost(2 * block * inner * columns, 8e6),
    )(a, b, *others)


def token_kernel(a_ref, b_ref, *rest):
    rest[-1][...] = dot_tn(a_ref[...], b_ref[...]).astype(LOW)


def token_dot(a, b, others):
    block, rows = a.shape
    columns = b.shape[1]
    tile = min(rows, 512)
    return pl.pallas_call(
        token_kernel,
        grid=(rows // tile,),
        in_specs=[
            pl.BlockSpec((block, tile), lambda i: (0, i)),
            pl.BlockSpec((block, columns), lambda i: (0, 0)),
        ]
        + [pl.BlockSpec(memory_space=pl.ANY)] * len(others),
        out_specs=pl.BlockSpec((tile, columns), lambda i: (i, 0)),
        out_shape=jax.ShapeDtypeStruct((rows, columns), LOW),
        compiler_params=params(),
        cost_estimate=cost(2 * block * rows * columns, 6e6),
    )(a, b, *others)


def halves_kernel(d_ref, a_ref, b_ref, *rest):
    send_ref, keep_ref = rest[-2:]
    product = dot_tn(a_ref[...], b_ref[...]).astype(LOW)

    @pl.when(pl.program_id(0) == 0)
    def _():
        send_ref[...] = product

    @pl.when(pl.program_id(0) == 1)
    def _():
        keep_ref[...] = product


def token_halves(a, b, others):
    block, rows = a.shape
    columns = b.shape[1]
    tiles = 2
    tile = rows // (2 * tiles)
    d = lax.axis_index("dp").astype(jnp.int32)[None]
    half = jax.ShapeDtypeStruct((rows // 2, columns), LOW)
    return pl.pallas_call(
        halves_kernel,
        grid_spec=pltpu.PrefetchScalarGridSpec(
            num_scalar_prefetch=1,
            grid=(2, tiles),
            in_specs=[
                pl.BlockSpec(
                    (block, tile),
                    lambda h, j, d: (0, ((1 - d[0]) * (1 - h) + d[0] * h) * tiles + j),
                ),
                pl.BlockSpec((block, columns), lambda h, j, d: (0, 0)),
            ]
            + [pl.BlockSpec(memory_space=pl.ANY)] * len(others),
            out_specs=[
                pl.BlockSpec((tile, columns), lambda h, j, d: (j * (1 - h) + (tiles - 1) * h, 0)),
                pl.BlockSpec((tile, columns), lambda h, j, d: (j * h, 0)),
            ],
        ),
        out_shape=[half, half],
        compiler_params=params(),
        cost_estimate=cost(2 * block * rows * columns, 6e6),
    )(d, a, b, *others)


def split_low(value):
    high = value.astype(LOW)
    return high, (value - high.astype(F32)).astype(LOW)


def norm_parts(rows):
    rr = lax.rsqrt(jnp.mean(rows * rows, axis=-1, keepdims=True) + EPS)
    return rows * rr, rr


def norm_back(grad, normal, rr, gain):
    weighted = grad * gain
    return rr * (weighted - normal * jnp.mean(weighted * normal, axis=-1, keepdims=True))


def add_all(refs):
    return functools.reduce(jnp.add, [ref[...].astype(F32) for ref in refs])


def pad_rows(rows, count):
    if rows.shape[0] == count:
        return rows
    return jnp.concatenate(
        [rows, jnp.zeros((count - rows.shape[0], rows.shape[1]), rows.dtype)], axis=0
    )


def router_kernel(experts, *refs):
    x_ref, attn_ref, gain_ref, router_ref, mask_ref = refs[:5]
    hidden_ref, mixed_ref, probs_ref = refs[-3:]
    width = x_ref.shape[1]
    lanes = mask_ref.shape[1]
    hidden = add_all([x_ref, attn_ref])
    hidden_ref[...] = hidden
    mixed = (norm_parts(hidden)[0] * gain_ref[...]).astype(LOW)
    mixed_ref[:, :width] = mixed
    logits = dot_nt(mixed, pad_rows(router_ref[...], lanes))
    lane = lax.broadcasted_iota(jnp.int32, logits.shape, 1)
    logits = jnp.where(lane < experts, logits, -1e30)
    weights = jnp.exp(logits - jnp.max(logits, axis=1, keepdims=True))
    probs = weights / jnp.sum(weights, axis=1, keepdims=True)
    probs_ref[...] = probs
    chosen = probs * mask_ref[...]
    high, low = split_low(chosen / jnp.sum(chosen, axis=1, keepdims=True))
    both = high.astype(F32) + pltpu.roll(low.astype(F32), experts, 1)
    mixed_ref[:, width:] = both.astype(LOW)


def route_rows(x, attn, gain, router, mask, experts, others):
    tokens, width = x.shape
    lanes = mask.shape[1]
    operands = [x, attn, gain[None], router, mask]
    shapes = [
        jax.ShapeDtypeStruct((tokens, width), F32),
        jax.ShapeDtypeStruct((tokens, width + lanes), LOW),
        jax.ShapeDtypeStruct((tokens, lanes), F32),
    ]
    return pl.pallas_call(
        functools.partial(router_kernel, experts),
        grid=(1,),
        in_specs=[full(value.shape) for value in operands]
        + [pl.BlockSpec(memory_space=pl.ANY)] * len(others),
        out_specs=[full(shape.shape) for shape in shapes],
        out_shape=shapes,
        compiler_params=params(),
        cost_estimate=cost(2 * tokens * width * lanes, 5e6),
    )(*operands, *others)


def one_hot(slots, count, first):
    groups, tokens = slots.shape
    slot = lax.broadcasted_iota(jnp.int32, (groups, count, tokens), 1).astype(F32)
    same = slots[:, None, :] == slot + float(first)
    return jnp.where(same, 1.0, 0.0).reshape(groups * count, tokens)


def slot_kernel(capacity, meta_ref, col_ref, rows_ref, slots_ref):
    groups, block = slots_ref.shape
    rows, width = rows_ref.shape
    n = rows // groups // capacity
    tokens = block // n
    mask = col_ref[:, width:]
    lanes = mask.shape[1]
    padded = -(-groups // 16) * 16
    group = lax.broadcasted_iota(jnp.int32, (padded, lanes), 0)
    lane = lax.broadcasted_iota(jnp.int32, (padded, lanes), 1)
    wanted = jnp.logical_and(lane == group * n + meta_ref[0], group < groups)
    hits = dot_nt(jnp.where(wanted, 1.0, 0.0).astype(LOW), mask)
    before = lax.broadcasted_iota(jnp.int32, (tokens, tokens), 0)
    after_it = lax.broadcasted_iota(jnp.int32, (tokens, tokens), 1)
    earlier = jnp.where(before < after_it, 1.0, 0.0).astype(LOW)
    for z in range(n):
        hit = hits[:, z * tokens : (z + 1) * tokens]
        rank = dot_nn(hit.astype(LOW), earlier)
        turn = (meta_ref[1 + z] * capacity).astype(F32)
        slot = jnp.where(hit > 0.5, rank + turn, -1.0)
        slots_ref[:, z * tokens : (z + 1) * tokens] = slot[:groups]
    spread = one_hot(slots_ref[...], n * capacity, 0).astype(LOW)
    rows_ref[...] = dot_nn(spread, col_ref[:, :width]).astype(LOW)


def make_slots(meta, col, width, groups, capacity):
    block = col.shape[0]
    n = lax.axis_size("expert")
    shapes = [
        jax.ShapeDtypeStruct((groups * n * capacity, width), LOW),
        jax.ShapeDtypeStruct((groups, block), F32),
    ]
    return pl.pallas_call(
        functools.partial(slot_kernel, capacity),
        grid_spec=pltpu.PrefetchScalarGridSpec(
            num_scalar_prefetch=1,
            grid=(1,),
            in_specs=[full(col.shape)],
            out_specs=[full(shape.shape) for shape in shapes],
        ),
        out_shape=shapes,
        compiler_params=params(),
        cost_estimate=cost(2 * groups * n * capacity * block * width, 8e6),
    )(meta, col)


def table_kernel(capacity, n_half, meta_ref, slots_ref, near_ref, far_ref, near_back_ref, far_back_ref):
    n = 2 * n_half
    tokens = slots_ref.shape[1] // n
    cap_half = n_half * capacity
    for part, (to_ref, back_ref) in enumerate([(near_ref, near_back_ref), (far_ref, far_back_ref)]):
        pieces = []
        for k in range(n_half):
            start = pl.multiple_of(meta_ref[1 + n + part * n_half + k] * tokens, tokens)
            pieces.append(slots_ref[:, pl.ds(start, tokens)])
        spread = one_hot(jnp.concatenate(pieces, axis=1), cap_half, part * cap_half)
        to_ref[...] = spread.astype(LOW)
        back_ref[...] = jnp.transpose(spread).astype(LOW)


def make_tables(meta, slots, n_half, capacity):
    groups, block = slots.shape
    rows = groups * n_half * capacity
    shapes = [jax.ShapeDtypeStruct((rows, block // 2), LOW)] * 2
    shapes += [jax.ShapeDtypeStruct((block // 2, rows), LOW)] * 2
    outs = pl.pallas_call(
        functools.partial(table_kernel, capacity, n_half),
        grid_spec=pltpu.PrefetchScalarGridSpec(
            num_scalar_prefetch=1,
            grid=(1,),
            in_specs=[full(slots.shape)],
            out_specs=[full(shape.shape) for shape in shapes],
        ),
        out_shape=shapes,
        compiler_params=params(),
        cost_estimate=cost(8 * rows * block, 3e6),
    )(meta, slots)
    return outs[:2], outs[2:]


def spread_kernel(choices, place_ref, spread_ref, *refs):
    out_ref, rows_ref = refs[-2:]
    for k, by_place in enumerate(choices):
        for which in sorted(set(by_place)):
            hit = functools.reduce(
                jnp.logical_or,
                [place_ref[0] == i for i, other in enumerate(by_place) if other == which],
            )

            @pl.when(hit)
            def _():
                tokens = refs[which].shape[0]
                rows_ref[k * tokens : (k + 1) * tokens] = refs[which][...]

    out_ref[...] = dot_nn(spread_ref[...], rows_ref[...]).astype(LOW)


def spread_rows(place, spread, found, turns, others):
    n = lax.axis_size("expert")
    order = arrival_order(n)
    distances = sorted({order[i][turn] - i for i in range(n) for turn in turns})
    choices = [[distances.index(order[i][turn] - i) for i in range(n)] for turn in turns]
    chunks = [found[distance] for distance in distances]
    tokens, wide = chunks[0].shape
    rows = spread.shape[0]
    return pl.pallas_call(
        functools.partial(spread_kernel, choices),
        grid_spec=pltpu.PrefetchScalarGridSpec(
            num_scalar_prefetch=1,
            grid=(1,),
            in_specs=[full(spread.shape)]
            + [full(chunk.shape) for chunk in chunks]
            + [pl.BlockSpec(memory_space=pl.ANY)] * len(others),
            out_specs=full((rows, wide)),
            scratch_shapes=[pltpu.VMEM((len(turns) * tokens, wide), LOW)],
        ),
        out_shape=jax.ShapeDtypeStruct((rows, wide), LOW),
        compiler_params=params(),
        cost_estimate=cost(2 * rows * len(turns) * tokens * wide, 5e6),
    )(place, spread, *chunks, *others)


def router_back_kernel(experts, *refs):
    sum_ref, g_ref, hidden_ref, gain_ref, router_ref, mask_ref, probs_ref = refs[:7]
    grad_ref, low_ref, dgain_ref, drouter_ref = refs[-4:]
    width = g_ref.shape[1]
    lanes = mask_ref.shape[1]
    total = sum_ref[...].astype(F32)
    table = total[:, width:]
    mask, probs = mask_ref[...], probs_ref[...]
    grad_gates = (table + pltpu.roll(table, lanes - experts, 1)) * mask
    chosen = probs * mask
    chosen_sum = jnp.sum(chosen, axis=1, keepdims=True)
    mean = jnp.sum(grad_gates * (chosen / chosen_sum), axis=1, keepdims=True)
    centred = mask * (grad_gates - mean) / chosen_sum
    grad_logits = probs * (centred - jnp.sum(centred * chosen, axis=1, keepdims=True))
    high, low = split_low(grad_logits)
    router = pad_rows(router_ref[...], lanes)
    grad = total[:, :width] + dot_nn(high, router) + dot_nn(low, router)
    normal, rr = norm_parts(hidden_ref[...])
    mixed = (normal * gain_ref[...]).astype(LOW)
    drouter_ref[...] = dot_tn(high, mixed) + dot_tn(low, mixed)
    dgain_ref[...] = jnp.sum(grad * normal, axis=0, keepdims=True)
    grad_hidden = g_ref[...].astype(F32) + norm_back(grad, normal, rr, gain_ref[...])
    grad_ref[...] = grad_hidden
    low_ref[...] = grad_hidden.astype(LOW)


def route_back(summed, g, hidden, gain, router, mask, probs, experts, others):
    tokens, width = g.shape
    lanes = mask.shape[1]
    operands = [summed, g, hidden, gain[None], router, mask, probs]
    shapes = [
        jax.ShapeDtypeStruct((tokens, width), F32),
        jax.ShapeDtypeStruct((tokens, width), LOW),
        jax.ShapeDtypeStruct((1, width), F32),
        jax.ShapeDtypeStruct((lanes, width), F32),
    ]
    return pl.pallas_call(
        functools.partial(router_back_kernel, experts),
        grid=(1,),
        in_specs=[full(value.shape) for value in operands]
        + [pl.BlockSpec(memory_space=pl.ANY)] * len(others),
        out_specs=[full(shape.shape) for shape in shapes],
        out_shape=shapes,
        compiler_params=params(),
        cost_estimate=cost(8 * tokens * width * lanes, 8e6),
    )(*operands, *others)


def combine_kernel(meta_ref, table_ref, rows_ref, *rest):
    del meta_ref
    rest[-1][...] = dot_nn(table_ref[...], rows_ref[...]).astype(LOW)


def combine_part(meta, table, rows, first, n, into, others):
    block, slots = table.shape
    wide = rows.shape[1]
    tokens = block // (n // 2)
    return pl.pallas_call(
        combine_kernel,
        grid_spec=pltpu.PrefetchScalarGridSpec(
            num_scalar_prefetch=1,
            grid=(n // 2,),
            in_specs=[
                pl.BlockSpec((tokens, slots), lambda i, m: (i, 0)),
                full(rows.shape),
            ]
            + [pl.BlockSpec(memory_space=pl.ANY)] * (len(into) + len(others)),
            out_specs=pl.BlockSpec((tokens, wide), lambda i, m: (m[1 + n + first + i], 0)),
        ),
        out_shape=jax.ShapeDtypeStruct((n * tokens, wide), LOW),
        input_output_aliases={3: 0} if into else {},
        compiler_params=params(),
        cost_estimate=cost(2 * slots * block * wide, 6e6),
    )(meta, table, rows, *into, *others)


def combine_rows(meta, tables, rows, n_half, others):
    near = combine_part(meta, tables[0], rows[0], 0, 2 * n_half, [], [])
    return combine_part(meta, tables[1], rows[1], n_half, 2 * n_half, [near], others)


def expert_kernel(experts, who_ref, x_ref, gate_ref, up_ref, pull_ref, *rest):
    act_ref, dgate_ref, dup_ref, copy_ref = rest[-4:]
    width = gate_ref.shape[0]
    x = x_ref[:, :width]
    table = x_ref[:, width:].astype(F32)
    lane = lax.broadcasted_iota(jnp.int32, table.shape, 1)
    mine = who_ref[0]
    gate = jnp.sum(
        jnp.where(jnp.logical_or(lane == mine, lane == mine + experts), table, 0.0),
        axis=1,
        keepdims=True,
    )
    pre_gate = dot_nn(x, gate_ref[...])
    pre_up = dot_nn(x, up_ref[...])
    pull = pull_ref[...].reshape(pre_up.shape)
    sig = 1.0 / (1.0 + jnp.exp(-pre_gate))
    silu = pre_gate * sig
    act = silu * pre_up
    act_ref[...] = (act * gate).astype(LOW)
    high, low = split_low(jnp.sum(act * pull, axis=1, keepdims=True))
    pull = pull * gate
    dup = (pull * silu).astype(LOW)
    dgate = (pull * pre_up * (sig * (1.0 + pre_gate * (1.0 - sig)))).astype(LOW)
    dgate_ref[...] = dgate
    dup_ref[...] = dup
    copy_ref[:, :width] = (dot_nt(dgate, gate_ref[...]) + dot_nt(dup, up_ref[...])).astype(LOW)
    back = jnp.where(lane == mine, high.astype(F32), 0.0)
    back = jnp.where(lane == mine + experts, low.astype(F32), back)
    copy_ref[:, width:] = back.astype(LOW)


def run_expert(who, x, w_gate, w_up, pull, part, experts):
    rows, wide = x.shape
    width, hidden = w_gate.shape
    groups, _, slots, _ = pull.shape
    each = groups // 2
    tile = each * slots
    by_rows = lambda columns: pl.BlockSpec((tile, columns), lambda i, p: (i, 0))
    return pl.pallas_call(
        functools.partial(expert_kernel, experts),
        grid_spec=pltpu.PrefetchScalarGridSpec(
            num_scalar_prefetch=1,
            grid=(2,),
            in_specs=[
                by_rows(wide),
                full(w_gate.shape),
                full(w_up.shape),
                pl.BlockSpec((each, 1, slots, hidden), lambda i, p: (i, part, 0, 0)),
            ],
            out_specs=[by_rows(hidden), by_rows(hidden), by_rows(hidden), by_rows(wide)],
        ),
        out_shape=[jax.ShapeDtypeStruct((rows, hidden), LOW)] * 3
        + [jax.ShapeDtypeStruct((rows, wide), LOW)],
        compiler_params=params(),
        cost_estimate=cost(8 * rows * width * hidden, 20e6, rows * hidden),
    )(who, x, w_gate, w_up, pull)


def input_kernel(grad_ref, x_ref, gain_ref, more_ref, out_ref):
    normal, rr = norm_parts(x_ref[...].astype(F32))
    grad = grad_ref[...].astype(F32)
    out_ref[...] = more_ref[...] + norm_back(grad, normal, rr, gain_ref[...])


def input_back(grad, x, gain, more):
    tokens, width = x.shape
    operands = [grad, x, gain[None], more]
    return pl.pallas_call(
        input_kernel,
        grid=(1,),
        in_specs=[full(value.shape) for value in operands],
        out_specs=full(more.shape),
        out_shape=jax.ShapeDtypeStruct((tokens, width), F32),
        compiler_params=params(),
        cost_estimate=cost(20 * tokens * width, 5e6),
    )(*operands)


def kv_back_kernel(factor, parts_ref, proj_ref, gain_ref, cos_ref, sin_ref, *rest):
    grad_ref, dgain_ref = rest[-2:]
    size = proj_ref.shape[1]
    total = parts_ref[0].astype(F32)
    for k in range(1, parts_ref.shape[0]):
        total += parts_ref[k].astype(F32)
    grad, dgain = head_backward(
        total[:, :size] * factor, proj_ref[...], gain_ref[...], cos_ref[...], sin_ref[...]
    )
    grad_ref[:, :size] = grad.astype(LOW)
    grad_ref[:, size:] = total[:, size:].astype(LOW)
    dgain_ref[...] = dgain


def kv_back(parts, proj, gain, cos2, sin2, factor, others):
    block, size = proj.shape
    operands = [parts, proj, gain[None], cos2, sin2]
    shapes = [
        jax.ShapeDtypeStruct((block, 2 * size), LOW),
        jax.ShapeDtypeStruct((1, size), F32),
    ]
    return pl.pallas_call(
        functools.partial(kv_back_kernel, factor),
        grid=(1,),
        in_specs=[full(value.shape) for value in operands]
        + [pl.BlockSpec(memory_space=pl.ANY)] * len(others),
        out_specs=[full(shape.shape) for shape in shapes],
        out_shape=shapes,
        compiler_params=params(),
        cost_estimate=cost(40 * block * size, 5e6),
    )(*operands, *others)


def pair_kernel(a_ref, b_ref, *rest):
    rest[-1][...] = (a_ref[...].astype(F32) + b_ref[...].astype(F32)).astype(LOW)


def pair_sum(a, b, others):
    rows, columns = a.shape
    tiles = 2 if rows % 32 == 0 else 1
    spec = pl.BlockSpec((rows // tiles, columns), lambda i: (i, 0))
    return pl.pallas_call(
        pair_kernel,
        grid=(tiles,),
        in_specs=[spec, spec] + [pl.BlockSpec(memory_space=pl.ANY)] * len(others),
        out_specs=spec,
        out_shape=jax.ShapeDtypeStruct((rows, columns), LOW),
        compiler_params=params(),
        cost_estimate=cost(rows * columns, 6 * rows * columns),
    )(a, b, *others)


def fold_kernel(n_pairs, s_ref, *refs):
    del s_ref
    send_ref, keep_ref = refs[-2:]
    totals = [
        (refs[2 * k][...].astype(F32) + refs[2 * k + 1][...].astype(F32)).astype(LOW)
        for k in range(n_pairs)
    ]
    for half, out_ref in enumerate((send_ref, keep_ref)):

        @pl.when(pl.program_id(0) == half)
        def _():
            first = 0
            for total in totals:
                last = first + total.shape[1]
                out_ref[:, first:last] = total
                first = last


def fold(pairs, bit, others):
    rows = pairs[0][1].shape[0]
    columns = sum(got.shape[1] for _, got in pairs)
    tiles = 2
    tile = rows // (2 * tiles)
    side = lambda h, m: (1 - m[0]) * (1 - h) + m[0] * h
    specs = []
    for _, got in pairs:
        wide = got.shape[1]
        specs += [pl.BlockSpec((tile, wide), lambda h, j, m: (side(h, m) * tiles + j, 0))] * 2
    shape = jax.ShapeDtypeStruct((rows // 2, columns), LOW)
    return pl.pallas_call(
        functools.partial(fold_kernel, len(pairs)),
        grid_spec=pltpu.PrefetchScalarGridSpec(
            num_scalar_prefetch=1,
            grid=(2, tiles),
            in_specs=specs + [pl.BlockSpec(memory_space=pl.ANY)] * len(others),
            out_specs=[
                pl.BlockSpec((tile, columns), lambda h, j, m: (j * (1 - h) + (tiles - 1) * h, 0)),
                pl.BlockSpec((tile, columns), lambda h, j, m: (j * h, 0)),
            ],
        ),
        out_shape=[shape, shape],
        compiler_params=params(),
        cost_estimate=cost(rows * columns, 6 * rows * columns),
    )(
        bit.astype(jnp.int32)[None],
        *[value for pair in pairs for value in pair],
        *others,
    )


def normed_kernel(q_ref, kv_ref, wq_ref, wkv_ref, rows_ref, *rest):
    out_ref, dgain_ref = rest[-2:]
    grad = dot_nt(q_ref[...], wq_ref[...]) + dot_nt(kv_ref[...], wkv_ref[...])
    out_ref[...] = grad.astype(LOW)
    dgain_ref[...] = jnp.sum(grad * rows_ref[...].astype(F32), axis=0, keepdims=True)


def normed_back(grad_q, grad_kv, w_q, w_kv, rows, others):
    block, width = rows.shape
    tile = 512
    column = lambda i: (0, i)
    return pl.pallas_call(
        normed_kernel,
        grid=(width // tile,),
        in_specs=[
            full(grad_q.shape),
            full(grad_kv.shape),
            pl.BlockSpec((tile, w_q.shape[1]), lambda i: (i, 0)),
            pl.BlockSpec((tile, w_kv.shape[1]), lambda i: (i, 0)),
            pl.BlockSpec((block, tile), column),
        ]
        + [pl.BlockSpec(memory_space=pl.ANY)] * len(others),
        out_specs=[pl.BlockSpec((block, tile), column), pl.BlockSpec((1, tile), column)],
        out_shape=[
            jax.ShapeDtypeStruct((block, width), LOW),
            jax.ShapeDtypeStruct((1, width), F32),
        ],
        compiler_params=params(),
        cost_estimate=cost(2 * block * width * (w_q.shape[1] + w_kv.shape[1]), 12e6),
    )(grad_q, grad_kv, w_q, w_kv, rows, *others)


def pack_kernel(experts, router_ref, attn_ref, gain_ref, mlp_ref, q_ref, k_ref, *rest):
    out_ref, rows_ref = rest[-2:]
    size = q_ref.shape[1]
    rows_ref[:experts] = router_ref[:experts]
    rows_ref[experts:] = jnp.zeros_like(rows_ref[experts:])
    rows_ref[experts : experts + 1] = attn_ref[...] / gain_ref[...]
    rows_ref[experts + 1 : experts + 2] = mlp_ref[...]
    rows_ref[experts + 2 : experts + 3, :size] = q_ref[...]
    rows_ref[experts + 2 : experts + 3, size : 2 * size] = k_ref[...]
    out_ref[...] = rows_ref[...].astype(LOW)


def pack_small(experts, router, attn, gain, mlp, q, k, others):
    width = attn.shape[1]
    n = lax.axis_size(ALL_AXES)
    shape = (-(-(experts + 3) // n) * n, width)
    operands = [router, attn, gain[None], mlp, q, k]
    return pl.pallas_call(
        functools.partial(pack_kernel, experts),
        grid=(1,),
        in_specs=[full(value.shape) for value in operands]
        + [pl.BlockSpec(memory_space=pl.ANY)] * len(others),
        out_specs=full(shape),
        out_shape=jax.ShapeDtypeStruct(shape, LOW),
        scratch_shapes=[pltpu.VMEM(shape, F32)],
        compiler_params=params(),
        cost_estimate=cost(shape[0] * width, 6 * shape[0] * width),
    )(*operands, *others)


def part_sum_kernel(parts_ref, *rest):
    total = parts_ref[0].astype(F32)
    for k in range(1, parts_ref.shape[0]):
        total += parts_ref[k].astype(F32)
    rest[-1][...] = total.astype(LOW)


def part_sum(parts, others):
    count, rows, columns = parts.shape
    tiles = 2
    return pl.pallas_call(
        part_sum_kernel,
        grid=(tiles,),
        in_specs=[pl.BlockSpec((count, rows // tiles, columns), lambda i: (0, i, 0))]
        + [pl.BlockSpec(memory_space=pl.ANY)] * len(others),
        out_specs=pl.BlockSpec((rows // tiles, columns), lambda i: (i, 0)),
        out_shape=jax.ShapeDtypeStruct((rows, columns), LOW),
        compiler_params=params(),
        cost_estimate=cost(count * rows * columns, 4 * count * rows * columns),
    )(parts, *others)


def widen_kernel(n_chunks, n_outs, at_ref, *refs):
    del at_ref
    outs = refs[-n_outs:]
    widths = [ref.shape[1] for ref in outs]
    for k in range(n_chunks):

        @pl.when(pl.program_id(0) == k)
        def _():
            first = 0
            for wide, out_ref in zip(widths, outs):
                out_ref[...] = refs[k][:, first : first + wide].astype(F32)
                first += wide


def widen(places, chunks, widths, others):
    rows, columns = chunks[0].shape
    count = len(chunks)
    return pl.pallas_call(
        functools.partial(widen_kernel, count, len(widths)),
        grid_spec=pltpu.PrefetchScalarGridSpec(
            num_scalar_prefetch=1,
            grid=(count,),
            in_specs=[full(chunk.shape) for chunk in chunks]
            + [pl.BlockSpec(memory_space=pl.ANY)] * len(others),
            out_specs=[pl.BlockSpec((rows, wide), lambda i, at: (at[i], 0)) for wide in widths],
        ),
        out_shape=[jax.ShapeDtypeStruct((count * rows, wide), F32) for wide in widths],
        compiler_params=params(),
        cost_estimate=cost(rows * columns, 6 * count * rows * columns),
    )(jnp.stack(places).astype(jnp.int32), *chunks, *others)


def swap_dp(rows):
    return lax.ppermute(rows, "dp", [(0, 1), (1, 0)])


def swap_context(rows, s):
    n = lax.axis_size("context")
    return lax.ppermute(rows, "context", [(i, i ^ s) for i in range(n)])


def plane_turns():
    d, c = lax.axis_index("dp"), lax.axis_index("context")
    low, high = lax.rem(c, 2), lax.div(c, 2)

    def swap(first, second):
        perm = [(i, i ^ first) for i in range(4)] + [(4 + i, 4 + (i ^ second)) for i in range(4)]
        return lambda rows: lax.ppermute(rows, GROUP_AXES, perm)

    return [
        (jnp.where(d == 0, low, high), swap(1, 2)),
        (jnp.where(d == 0, high, low), swap(2, 1)),
    ]


def plane_first(pairs, others):
    (bit_1, _), _ = plane_turns()
    return fold(pairs, bit_1, others)


def plane_second(send, keep, others):
    (_, swap_1), (bit_2, _) = plane_turns()
    return fold([(keep, swap_1(send))], bit_2, others)


def plane_last(send, keep, others):
    _, (_, swap_2) = plane_turns()
    return pair_sum(keep, swap_2(send), others)


def plane_spread(own):
    (_, swap_1), (_, swap_2) = plane_turns()
    second = swap_2(own)
    return [own, second, swap_1(own), swap_1(second)]


def quarter_places(rank):
    d = lax.axis_index("dp")
    c = lax.axis_index("context")
    low, high = lax.rem(c, 2), lax.div(c, 2)
    places = []
    for core in (d, 1 - d):
        bit_1 = jnp.where(core == 0, low, high)
        bit_2 = jnp.where(core == 0, high, low)
        for flip_1, flip_2 in ((0, 0), (0, 1), (1, 0), (1, 1)):
            places.append(4 * core + rank(core, bit_1 ^ flip_1, bit_2 ^ flip_2))
    return places


def widen_all(quarters, places, widths, others):
    return widen(places, quarters + [swap_dp(part) for part in quarters], widths, others)


def arrival_order(n):
    return [sorted(range(n), key=lambda j: (abs(j - i), j)) for i in range(n)]


def choose(index, options):
    distinct = []
    for option in options:
        if option is not None and not any(option is other for other in distinct):
            distinct.append(option)
    result = distinct[0]
    for option in distinct[1:]:
        mask = functools.reduce(
            jnp.logical_or, [index == i for i, other in enumerate(options) if other is option]
        )
        result = jnp.where(mask, option, result)
    return result


def line_gather(chunk):
    return line_steps({0: chunk}, 1, lax.axis_size("expert"))


def line_steps(found, first, stop):
    n = lax.axis_size("expert")
    found = dict(found)
    for s in range(first, stop):
        found[-s] = lax.ppermute(
            found[1 - s], "expert", [(i, i + 1) for i in range(s - 1, n - 1)]
        )
        found[s] = lax.ppermute(found[s - 1], "expert", [(i + 1, i) for i in range(n - s)])
    return found


def context_gather(rows):
    n = lax.axis_size("context")
    c = lax.axis_index("context")
    found = {0: rows}
    for s in range(1, n):
        found[s] = lax.ppermute(rows, "context", [(i, i ^ s) for i in range(n)])
    return jnp.concatenate([choose(c, [found[i ^ j] for i in range(n)]) for j in range(n)], axis=0)


def zero_of(*others):
    return functools.reduce(
        jnp.add,
        [
            lax.slice(other, (0,) * other.ndim, (1,) * other.ndim).reshape(()).astype(F32) * 0.0
            for other in others
        ],
    )


def after(value, *others):
    return (value.astype(F32) + zero_of(*others)).astype(value.dtype)


def on_device(
    layer_input,
    grad_output,
    attn_gain,
    query_weight,
    key_weight,
    value_weight,
    q_gain,
    k_gain,
    output_weight,
    mlp_gain,
    router,
    w_gate,
    w_up,
    w_down,
    routes,
    half_order,
):
    n_context = lax.axis_size("context")
    n_expert = lax.axis_size("expert")
    n_groups = lax.axis_size(GROUP_AXES)
    tok_dev, width = layer_input.shape[1:]
    size = q_gain.shape[0]
    kv_total = key_weight.shape[1] * n_expert
    group_dev = n_expert // (kv_total // size)
    kv_index = lax.axis_index("expert") // group_dev
    block = tok_dev * n_expert
    seq = block * n_context
    half = block // 2
    experts = router.shape[1]
    exp_dev = w_gate.shape[0]
    top = routes.shape[2]
    capacity = max(2, (tok_dev * top * 9 + 8 * experts - 1) // (8 * experts))
    scale = size ** (-0.5)

    seq_rows = jnp.arange(seq, dtype=jnp.int32)
    context = lax.axis_index("context")
    own_halves = lax.dynamic_slice_in_dim(half_order, 2 * context, 2)
    own_pos = (own_halves[:, None] * half + jnp.arange(half, dtype=jnp.int32)[None]).reshape(-1)
    per_half = half // TILE
    tile_pos = (half_order[:, None] * per_half + jnp.arange(per_half, dtype=jnp.int32)).reshape(-1)
    kidx = jnp.sum(
        (tile_pos[None, :] == jnp.arange(seq // TILE, dtype=jnp.int32)[:, None])
        * jnp.arange(seq // TILE, dtype=jnp.int32)[None, :],
        axis=1,
    ).astype(jnp.int32)
    qpos = lax.dynamic_slice_in_dim(tile_pos, context * (block // TILE), block // TILE)
    entry = jnp.arange(size)
    freq = jnp.power(THETA, -(2 * (entry % (size // 2))).astype(F32) / size)
    angles = own_pos.astype(F32)[:, None] * freq[None, :]
    cos2 = jnp.cos(angles)
    sin2 = jnp.sin(angles) * jnp.where(entry < size // 2, -1.0, 1.0)[None, :]

    place = lax.axis_index("expert")
    place_1 = place.astype(jnp.int32)[None]
    lanes = -(-2 * experts // 128) * 128
    mask = jnp.any(
        routes[0][:, :, None] == jnp.arange(lanes, dtype=jnp.int32)[None, None, :], axis=1
    )
    mask_wide = mask.astype(F32)
    router_rows = router.T

    x_low = layer_input[0]
    x_normal, _ = norm_parts(x_low.astype(F32))
    normed_found = line_gather((x_normal * attn_gain).astype(LOW))
    if group_dev == 1:
        kv_weights = jnp.concatenate([key_weight, value_weight], axis=1)
    else:
        key_whole = lax.all_gather(key_weight, "expert", axis=1, tiled=True)
        value_whole = lax.all_gather(value_weight, "expert", axis=1, tiled=True)
        kv_weights = jnp.concatenate(
            [
                lax.dynamic_slice_in_dim(key_whole, kv_index * size, size, 1),
                lax.dynamic_slice_in_dim(value_whole, kv_index * size, size, 1),
            ],
            axis=1,
        )
    grad_low = grad_output[0]
    normed_rows, own_kv, key_proj, grad_wide = project_keys(
        place_1,
        normed_found,
        kv_weights,
        k_gain,
        cos2,
        sin2,
        scale * LOG2E,
        grad_low,
        mask_wide,
    )
    grad_col = lax.all_gather(grad_wide, "expert", axis=0, tiled=True)
    kv_whole = context_gather(own_kv)
    queries, query_proj = project_queries(normed_rows, query_weight, q_gain, cos2, sin2)

    n_half = n_expert // 2
    order_here = jnp.asarray(arrival_order(n_expert), jnp.int32)[place]
    turn_here = jnp.sum(
        (order_here[:, None] == jnp.arange(n_expert, dtype=jnp.int32)[None, :])
        * jnp.arange(n_expert, dtype=jnp.int32)[:, None],
        axis=0,
    ).astype(jnp.int32)
    meta = jnp.concatenate([place_1, turn_here, order_here])
    grad_sent, slots = make_slots(meta, grad_col, width, n_groups, capacity)
    spreads, back_tables = make_tables(meta, slots, n_half, capacity)

    def swap_plane(rows):
        parts = rows.reshape(n_groups, -1, rows.shape[1])
        parts = lax.all_to_all(parts, GROUP_AXES, split_axis=0, concat_axis=0, tiled=True)
        return parts.reshape(rows.shape)

    attended, inverse = attend(qpos, kidx, queries, kv_whole, [])
    attn_part = out_dot(attended, output_weight, [grad_col])
    attn_rows = lax.psum_scatter(attn_part, "expert", scatter_dimension=0, tiled=True)

    grad_x = swap_plane(grad_sent)
    act_pull = dot_nt(grad_x, w_down[0]).reshape(n_groups, 2, n_half * capacity, -1)

    hidden, mixed, probs = route_rows(
        x_low, attn_rows, mlp_gain, router_rows, mask_wide, experts, []
    )

    who = (lax.axis_index(ALL_AXES) * exp_dev).astype(jnp.int32)[None]
    mixed_found = line_gather(mixed)
    near = spread_rows(place_1, spreads[0], mixed_found, range(n_half), [grad_x])
    x_near = swap_plane(near)
    worked_near = run_expert(who, x_near, w_gate[0], w_up[0], act_pull, 0, experts)
    far = spread_rows(place_1, spreads[1], mixed_found, range(n_half, n_expert), [x_near])
    x_far = swap_plane(far)
    worked_far = run_expert(who, x_far, w_gate[0], w_up[0], act_pull, 1, experts)
    xs = [x_near, x_far]
    acts, gate_lows, up_lows, copies = (list(pair) for pair in zip(worked_near, worked_far))
    back_far = swap_plane(copies[1])
    back_near = swap_plane(copies[0])
    join = lambda parts: jnp.concatenate(parts, axis=0)
    x_all = join([x[:, :width] for x in xs])
    grad_w_gate = dot_tn(x_all, join(gate_lows))
    grad_w_up = dot_tn(x_all, join(up_lows))
    grad_by_round = jnp.swapaxes(
        grad_x.reshape(n_groups, 2, n_half * capacity, width), 0, 1
    ).reshape(-1, width)
    grad_w_down = dot_tn(join(acts), grad_by_round)
    copies_col = combine_rows(
        meta, back_tables, [back_near, back_far], n_half, [grad_w_gate, grad_w_up]
    )
    copies_sum = lax.psum_scatter(copies_col, "expert", scatter_dimension=0, tiled=True)

    returned = [dot_nn(act, w_down[0]).astype(LOW) for act in acts]
    returned_near = swap_plane(returned[0])

    grad_hidden, grad_hidden_low, grad_mlp_gain, grad_router = route_back(
        copies_sum,
        grad_low,
        hidden,
        mlp_gain,
        router_rows,
        mask_wide,
        probs,
        experts,
        [returned_near, grad_w_down],
    )

    returned_far = swap_plane(returned[1])
    grad_attn = lax.all_gather(grad_hidden_low, "expert", axis=0, tiled=True)
    grad_o, centre = grad_attended(
        grad_attn, output_weight, attended, inverse, [returned_far]
    )
    combined = combine_rows(meta, back_tables, [returned_near, returned_far], n_half, [])
    output_rows = lax.psum_scatter(combined, "expert", scatter_dimension=0, tiled=True)
    w_out = token_dot(attended, grad_attn, [combined])
    w_out_parts = swap_plane(w_out)
    grad_kv, grad_q, grad_q_gain = attend_back(
        qpos,
        kidx,
        queries,
        grad_o,
        centre,
        kv_whole,
        query_proj,
        q_gain,
        cos2,
        sin2,
        [w_out],
    )
    kv_parts = lax.all_to_all(
        grad_kv.astype(LOW).reshape(n_context, block, 2 * size),
        "context",
        split_axis=0,
        concat_axis=0,
        tiled=True,
    )
    w_query_send, w_query_keep = token_halves(normed_rows, grad_q, [w_out_parts])
    w_query_got = swap_dp(w_query_send)
    output_rows = hidden + output_rows.astype(F32) + zero_of(w_query_keep)

    kv_grads, grad_k_gain = kv_back(
        kv_parts, key_proj, k_gain, cos2, sin2, scale, [w_query_keep]
    )
    w_out_quarters = plane_spread(part_sum(w_out_parts.reshape(n_groups, -1, width), [kv_parts]))
    pairs = [(w_query_keep, w_query_got)]
    widths = [query_weight.shape[1]]
    if group_dev == 1:
        w_kv_send, w_kv_keep = token_halves(normed_rows, kv_grads, [])
        pairs.append((w_kv_keep, swap_dp(w_kv_send)))
        widths += [key_weight.shape[1], value_weight.shape[1]]
    grad_normed, gain_rows = normed_back(
        grad_q, kv_grads, query_weight, kv_weights, normed_rows, []
    )
    send, keep = plane_first(pairs, [*w_out_quarters, grad_normed])
    (grad_w_out,) = widen_all(
        w_out_quarters,
        quarter_places(lambda core, b1, b2: jnp.where(core == 0, b1 + 2 * b2, 2 * b1 + b2)),
        [width],
        [],
    )
    small = pack_small(
        experts,
        grad_router,
        gain_rows,
        attn_gain,
        grad_mlp_gain,
        grad_q_gain,
        grad_k_gain,
        [],
    )
    swap_all = lambda rows: lax.all_to_all(rows, ALL_AXES, split_axis=0, concat_axis=0, tiled=True)
    small_parts = swap_all(small.reshape(lax.axis_size(ALL_AXES), -1, width))
    small_own = jnp.sum(small_parts.astype(F32), axis=0).astype(LOW)
    second_send, second_keep = plane_second(send, keep, [small_own])
    quarter = plane_last(second_send, second_keep, [output_rows])
    grad_normed = lax.psum_scatter(grad_normed, "expert", scatter_dimension=0, tiled=True)
    grad_input = input_back(grad_normed, x_low, attn_gain, grad_hidden)
    small_sum = swap_all(jnp.broadcast_to(small_own[None], small_parts.shape))
    small_sum = small_sum.reshape(small.shape).astype(F32)
    quarters = [quarter] + [swap_context(quarter, s) for s in range(1, n_context)]
    d = lax.axis_index("dp")
    turned = lambda core, c: jnp.where(core == 0, 2 * lax.rem(c, 2) + lax.div(c, 2), c)
    places = [4 * core + turned(core, context ^ s) for core in (d, 1 - d) for s in range(n_context)]
    grad_w_query, *more = widen_all(quarters, places, widths, [grad_w_out, grad_input, small_sum])
    if group_dev == 1:
        grad_w_key, grad_w_value = more
    else:
        w_kv = token_dot(normed_rows, kv_grads, [])
        blank = jnp.zeros((width, kv_total), LOW)
        pieces = []
        for part in (w_kv[:, :size], w_kv[:, size:]):
            padded = lax.dynamic_update_slice(blank, part, (0, kv_index * size))
            pieces.append(lax.psum_scatter(padded, "expert", scatter_dimension=1, tiled=True))
        grad_w_key, grad_w_value = (lax.psum(piece, GROUP_AXES).astype(F32) for piece in pieces)
    grad_attn_gain, grad_mlp_gain = small_sum[experts], small_sum[experts + 1]
    grad_q_gain = small_sum[experts + 2, :size]
    grad_k_gain = small_sum[experts + 2, size : 2 * size]
    return (
        output_rows.astype(LOW)[None],
        grad_input[None],
        grad_attn_gain,
        grad_w_query,
        grad_w_key,
        grad_w_value,
        grad_q_gain,
        grad_k_gain,
        grad_w_out,
        grad_mlp_gain,
        small_sum[:experts].T,
        grad_w_gate[None],
        grad_w_up[None],
        grad_w_down[None],
    )


def solution(mesh):
    rows = P("dp", ("context", "expert"), None)
    expert = P(ALL_AXES, None, None)
    columns = P(None, "expert")
    in_specs = (
        rows,
        rows,
        P(),
        columns,
        columns,
        columns,
        P(),
        P(),
        P("expert", None),
        P(),
        P(),
        expert,
        expert,
        expert,
        rows,
        P(),
    )
    out_specs = (
        rows,
        rows,
        P(),
        columns,
        columns,
        columns,
        P(),
        P(),
        P("expert", None),
        P(),
        P(),
        expert,
        expert,
        expert,
    )
    return jax.shard_map(
        on_device, mesh=mesh, in_specs=in_specs, out_specs=out_specs, check_vma=False
    )
```

```python
import functools
import math

import jax
import jax.numpy as jnp
from jax import lax
from jax.experimental import pallas as pl
from jax.experimental.pallas import tpu as pltpu
from jax.sharding import PartitionSpec as P

EPS = 1e-06
THETA = 1000000.0
TILE = 256
PIECE = 128
VMEM_BYTES = 56 * 1024 * 1024
LOG2E = math.log2(math.e)
LOW = jnp.bfloat16
F32 = jnp.float32
ALL_AXES = ("dp", "context", "expert")
GROUP_AXES = ("dp", "context")


def dot_nn(a, b):
    return lax.dot_general(a, b, (((1,), (0,)), ((), ())), preferred_element_type=F32)


def dot_nt(a, b):
    return lax.dot_general(a, b, (((1,), (1,)), ((), ())), preferred_element_type=F32)


def dot_tn(a, b):
    return lax.dot_general(a, b, (((0,), (0,)), ((), ())), preferred_element_type=F32)


def params(**more):
    return pltpu.CompilerParams(vmem_limit_bytes=VMEM_BYTES, **more)


def cost(flops, nbytes, exps=0):
    return pl.CostEstimate(flops=int(flops), bytes_accessed=int(nbytes), transcendentals=int(exps))


def head_forward(u, gain, cos2, sin2):
    rr = lax.rsqrt(jnp.mean(u * u, axis=-1, keepdims=True) + EPS)
    y = u * rr * gain
    return y * cos2 + pltpu.roll(y, 64, 1) * sin2


def head_backward(gy, u, gain, cos2, sin2):
    g = gy * cos2 - pltpu.roll(gy, 64, 1) * sin2
    rr = lax.rsqrt(jnp.mean(u * u, axis=-1, keepdims=True) + EPS)
    n = u * rr
    gn = g * gain
    grad = rr * (gn - n * jnp.mean(gn * n, axis=-1, keepdims=True))
    return grad, jnp.sum(g * n, axis=0, keepdims=True)


def query_kernel(x_ref, w_ref, gain_ref, cos_ref, sin_ref, rot_ref, proj_ref):
    tiles, heads, rows, size = rot_ref.shape
    acc = dot_nn(x_ref[...], w_ref[...])
    for h in range(heads):
        u = acc[:, h * size : (h + 1) * size]
        rot = head_forward(u, gain_ref[...], cos_ref[...], sin_ref[...])
        proj_ref[:, h] = u.reshape(tiles, rows, size)
        rot_ref[:, h] = rot.astype(LOW).reshape(tiles, rows, size)


def project_queries(normed, weight, gain, cos2, sin2):
    block, width = normed.shape
    size = cos2.shape[1]
    heads = weight.shape[1] // size
    tiles = block // TILE
    whole = lambda i: (0, 0)
    per = lambda i: (0, i, 0, 0)
    shape = (tiles, heads, TILE, size)
    return pl.pallas_call(
        query_kernel,
        grid=(heads // 2,),
        in_specs=[
            pl.BlockSpec((block, width), whole),
            pl.BlockSpec((width, 2 * size), lambda i: (0, i)),
            pl.BlockSpec((1, size), whole),
            pl.BlockSpec((block, size), whole),
            pl.BlockSpec((block, size), whole),
        ],
        out_specs=[pl.BlockSpec((tiles, 2, TILE, size), per)] * 2,
        out_shape=[jax.ShapeDtypeStruct(shape, LOW), jax.ShapeDtypeStruct(shape, F32)],
        compiler_params=params(),
        cost_estimate=cost(2 * block * width * heads * size, 12e6),
    )(normed, weight, gain[None], cos2, sin2)


def put_in_order(place, refs, out_ref):
    n = (len(refs) + 1) // 2
    rows = refs[0].shape[0]
    for distance in range(1 - n, n):
        ref = refs[distance + n - 1]
        at = place + distance

        @pl.when(jnp.logical_and(at >= 0, at < n))
        def _():
            out_ref[pl.ds(pl.multiple_of(at * rows, rows), rows), :] = ref[...]


def chunk_list(found):
    n = (len(found) + 1) // 2
    return [found[distance] for distance in range(1 - n, n)]


def key_kernel(factor, n_chunks, place_ref, *refs):
    w_ref, gain_ref, cos_ref, sin_ref, g_ref, mask_ref = refs[n_chunks:-4]
    rows_ref, kv_ref, proj_ref, wide_ref = refs[-4:]
    size = proj_ref.shape[1]
    width = g_ref.shape[1]
    put_in_order(place_ref[0], refs[:n_chunks], rows_ref)
    wide_ref[:, :width] = g_ref[...]
    wide_ref[:, width:] = mask_ref[...].astype(LOW)
    acc = dot_nn(rows_ref[...], w_ref[...])
    u = acc[:, :size]
    rot = head_forward(u, gain_ref[...], cos_ref[...], sin_ref[...])
    proj_ref[...] = u
    kv_ref[:, :size] = (rot * factor).astype(LOW)
    kv_ref[:, size:] = acc[:, size:].astype(LOW)


def full(shape):
    return pl.BlockSpec(shape, lambda *_: (0,) * len(shape))


def project_keys(place, found, weight, gain, cos2, sin2, factor, g, mask):
    chunks = chunk_list(found)
    rows, width = chunks[0].shape
    block, size = cos2.shape
    operands = [*chunks, weight, gain[None], cos2, sin2, g, mask]
    shapes = [
        jax.ShapeDtypeStruct((block, width), LOW),
        jax.ShapeDtypeStruct((block, 2 * size), LOW),
        jax.ShapeDtypeStruct((block, size), F32),
        jax.ShapeDtypeStruct((rows, width + mask.shape[1]), LOW),
    ]
    return pl.pallas_call(
        functools.partial(key_kernel, factor, len(chunks)),
        grid_spec=pltpu.PrefetchScalarGridSpec(
            num_scalar_prefetch=1,
            grid=(1,),
            in_specs=[full(x.shape) for x in operands],
            out_specs=[full(x.shape) for x in shapes],
        ),
        out_shape=shapes,
        compiler_params=params(),
        cost_estimate=cost(4 * block * width * size, 8e6),
    )(place, *operands)


def in_order(last, step):
    lax.fori_loop(0, lax.div(last, 2), lambda p, c: (step([2 * p, 2 * p + 1], False), c)[1], 0)

    @pl.when(lax.rem(last, 2) == 1)
    def _():
        step([last - 1, last], True)

    @pl.when(lax.rem(last, 2) == 0)
    def _():
        step([last], True)


def attend_kernel(qpos_ref, kidx_ref, q_ref, kv_ref, *rest):
    out_ref, inv_ref, acc_ref = rest[-3:]
    heads, rows, size = q_ref.shape[1:]
    acc_ref[...] = jnp.zeros_like(acc_ref)

    def step(places, masked):
        starts = [pl.multiple_of(kidx_ref[place] * rows, rows) for place in places]
        count = len(places) * rows
        keys = jnp.concatenate([kv_ref[pl.ds(start, rows), :size] for start in starts], axis=0)
        values = jnp.concatenate([kv_ref[pl.ds(start, rows), size:] for start in starts], axis=0)
        values = jnp.concatenate([values, jnp.ones((count, size), LOW)], axis=1)
        for h in range(heads):
            for first in range(0, rows, PIECE):
                part = slice(first, first + PIECE)
                e = jnp.exp2(dot_nt(q_ref[0, h, part], keys))
                if masked:
                    qi = lax.broadcasted_iota(jnp.int32, e.shape, 0) + first
                    ki = lax.broadcasted_iota(jnp.int32, e.shape, 1) - (count - rows)
                    e = jnp.where(ki <= qi, e, 0.0)
                acc_ref[h, part] += dot_nn(e.astype(LOW), values)

    in_order(qpos_ref[pl.program_id(0)], step)
    for h in range(heads):
        inv = 1.0 / acc_ref[h, :, size:]
        inv_ref[0, h] = inv
        out_ref[:, h * size : (h + 1) * size] = (acc_ref[h, :, :size] * inv).astype(LOW)


def attend(qpos, kidx, queries, kv, others):
    tiles, heads, rows, size = queries.shape
    seq = kv.shape[0]
    return pl.pallas_call(
        attend_kernel,
        grid_spec=pltpu.PrefetchScalarGridSpec(
            num_scalar_prefetch=2,
            grid=(tiles,),
            in_specs=[
                pl.BlockSpec((1, heads, rows, size), lambda i, a, b: (i, 0, 0, 0)),
                pl.BlockSpec((seq, 2 * size), lambda i, a, b: (0, 0)),
            ]
            + [pl.BlockSpec(memory_space=pl.ANY)] * len(others),
            out_specs=[
                pl.BlockSpec((rows, heads * size), lambda i, a, b: (i, 0)),
                pl.BlockSpec((1, heads, rows, size), lambda i, a, b: (i, 0, 0, 0)),
            ],
            scratch_shapes=[pltpu.VMEM((heads, rows, 2 * size), F32)],
        ),
        out_shape=[
            jax.ShapeDtypeStruct((tiles * rows, heads * size), LOW),
            jax.ShapeDtypeStruct((tiles, heads, rows, size), F32),
        ],
        compiler_params=params(),
        cost_estimate=cost(
            6 * tiles * rows * heads * seq * size, 8e6, tiles * rows * heads * seq
        ),
    )(qpos, kidx, queries, kv, *others)


def grad_out_kernel(rows_ref, w_ref, o_ref, inv_ref, *rest):
    do_ref, centre_ref = rest[-2:]
    tiles, heads, rows, size = do_ref.shape
    acc = dot_nt(rows_ref[...], w_ref[...])
    for t in range(tiles):
        for h in range(heads):
            part = slice(t * rows, (t + 1) * rows), slice(h * size, (h + 1) * size)
            low = (acc[part] * inv_ref[t, h]).astype(LOW)
            do_ref[t, h] = low
            product = low.astype(F32) * o_ref[part].astype(F32)
            centre = jnp.sum(jnp.transpose(product), axis=0, keepdims=True)
            centre_ref[t, h] = jnp.broadcast_to(centre, (8, rows))


def grad_attended(grad_rows, weight, attended, inverse, others):
    tiles, heads, rows, size = inverse.shape
    block, width = grad_rows.shape
    return pl.pallas_call(
        grad_out_kernel,
        grid=(heads // 2,),
        in_specs=[
            pl.BlockSpec((block, width), lambda i: (0, 0)),
            pl.BlockSpec((2 * size, width), lambda i: (i, 0)),
            pl.BlockSpec((block, 2 * size), lambda i: (0, i)),
            pl.BlockSpec((tiles, 2, rows, size), lambda i: (0, i, 0, 0)),
        ]
        + [pl.BlockSpec(memory_space=pl.ANY)] * len(others),
        out_specs=[
            pl.BlockSpec((tiles, 2, rows, size), lambda i: (0, i, 0, 0)),
            pl.BlockSpec((tiles, 2, 8, rows), lambda i: (0, i, 0, 0)),
        ],
        out_shape=[
            jax.ShapeDtypeStruct((tiles, heads, rows, size), LOW),
            jax.ShapeDtypeStruct((tiles, heads, 8, rows), F32),
        ],
        compiler_params=params(),
        cost_estimate=cost(2 * block * width * heads * size, 12e6),
    )(grad_rows, weight, attended, inverse, *others)


def attend_back_kernel(
    qpos_ref,
    kidx_ref,
    q_ref,
    do_ref,
    centre_ref,
    kv_ref,
    proj_ref,
    gain_ref,
    cos_ref,
    sin_ref,
    *rest,
):
    dkv_ref, dq_ref, dgain_ref, acc_ref, e_ref, ds_ref = rest[-6:]
    heads, rows, size = q_ref.shape[1:]

    @pl.when(pl.program_id(0) == 0)
    def _():
        dkv_ref[...] = jnp.zeros_like(dkv_ref)
        dgain_ref[...] = jnp.zeros_like(dgain_ref)

    acc_ref[...] = jnp.zeros_like(acc_ref)

    def step(places, masked):
        starts = [pl.multiple_of(kidx_ref[place] * rows, rows) for place in places]
        count = len(places) * rows
        keys = jnp.concatenate([kv_ref[pl.ds(start, rows), :size] for start in starts], axis=0)
        values = jnp.concatenate([kv_ref[pl.ds(start, rows), size:] for start in starts], axis=0)
        for h in range(heads):
            query, grad = q_ref[0, h], do_ref[0, h]
            centre = centre_ref[0, h, 0:1]
            columns = slice(h * rows, (h + 1) * rows)
            for first in range(0, count, PIECE):
                part = slice(first, first + PIECE)
                e = jnp.exp2(dot_nt(keys[part], query))
                if masked and first >= count - rows:
                    ki = lax.broadcasted_iota(jnp.int32, e.shape, 0) + (first - (count - rows))
                    qi = lax.broadcasted_iota(jnp.int32, e.shape, 1)
                    e = jnp.where(ki <= qi, e, 0.0)
                ds = e * (dot_nt(values[part], grad) - centre)
                e_ref[part, columns] = e.astype(LOW)
                ds_ref[part, columns] = ds.astype(LOW)
            acc_ref[h] += dot_tn(ds_ref[:count, columns], keys)
        dk = dot_nn(ds_ref[:count], q_ref[0].reshape(heads * rows, size))
        dv = dot_nn(e_ref[:count], do_ref[0].reshape(heads * rows, size))
        for k, start in enumerate(starts):
            dkv_ref[pl.ds(start, rows), :size] += dk[k * rows : (k + 1) * rows]
            dkv_ref[pl.ds(start, rows), size:] += dv[k * rows : (k + 1) * rows]

    in_order(qpos_ref[pl.program_id(0)], step)
    total = jnp.zeros((1, size), F32)
    for h in range(heads):
        grad, gain_part = head_backward(
            acc_ref[h] * (1.0 / LOG2E), proj_ref[0, h], gain_ref[...], cos_ref[...], sin_ref[...]
        )
        dq_ref[:, h * size : (h + 1) * size] = grad.astype(LOW)
        total += gain_part
    dgain_ref[...] += total


def attend_back(qpos, kidx, queries, grads, centre, kv, proj, gain, cos2, sin2, others):
    tiles, heads, rows, size = queries.shape
    seq = kv.shape[0]
    per = pl.BlockSpec((1, heads, rows, size), lambda i, a, b: (i, 0, 0, 0))
    flat = lambda i, a, b: (0, 0)
    rowwise = lambda i, a, b: (i, 0)
    return pl.pallas_call(
        attend_back_kernel,
        grid_spec=pltpu.PrefetchScalarGridSpec(
            num_scalar_prefetch=2,
            grid=(tiles,),
            in_specs=[
                per,
                per,
                pl.BlockSpec((1, heads, 8, rows), lambda i, a, b: (i, 0, 0, 0)),
                pl.BlockSpec((seq, 2 * size), flat),
                per,
                pl.BlockSpec((1, size), flat),
                pl.BlockSpec((rows, size), rowwise),
                pl.BlockSpec((rows, size), rowwise),
            ]
            + [pl.BlockSpec(memory_space=pl.ANY)] * len(others),
            out_specs=[
                pl.BlockSpec((seq, 2 * size), flat),
                pl.BlockSpec((rows, heads * size), rowwise),
                pl.BlockSpec((1, size), flat),
            ],
            scratch_shapes=[pltpu.VMEM((heads, rows, size), F32)]
            + [pltpu.VMEM((2 * rows, heads * rows), LOW)] * 2,
        ),
        out_shape=[
            jax.ShapeDtypeStruct((seq, 2 * size), F32),
            jax.ShapeDtypeStruct((tiles * rows, heads * size), LOW),
            jax.ShapeDtypeStruct((1, size), F32),
        ],
        compiler_params=params(),
        cost_estimate=cost(
            15 * tiles * rows * heads * seq * size, 12e6, tiles * rows * heads * seq
        ),
    )(qpos, kidx, queries, grads, centre, kv, proj, gain[None], cos2, sin2, *others)


def out_kernel(a_ref, b_ref, *rest):
    rest[-1][...] = dot_nn(a_ref[...], b_ref[...]).astype(LOW)


def out_dot(a, b, others):
    block, inner = a.shape
    columns = b.shape[1]
    tile = min(columns, 512)
    return pl.pallas_call(
        out_kernel,
        grid=(columns // tile,),
        in_specs=[
            pl.BlockSpec((block, inner), lambda i: (0, 0)),
            pl.BlockSpec((inner, tile), lambda i: (0, i)),
        ]
        + [pl.BlockSpec(memory_space=pl.ANY)] * len(others),
        out_specs=pl.BlockSpec((block, tile), lambda i: (0, i)),
        out_shape=jax.ShapeDtypeStruct((block, columns), LOW),
        compiler_params=params(),
        cost_estimate=cost(2 * block * inner * columns, 8e6),
    )(a, b, *others)


def token_kernel(a_ref, b_ref, *rest):
    rest[-1][...] = dot_tn(a_ref[...], b_ref[...]).astype(LOW)


def token_dot(a, b, others):
    block, rows = a.shape
    columns = b.shape[1]
    tile = min(rows, 512)
    return pl.pallas_call(
        token_kernel,
        grid=(rows // tile,),
        in_specs=[
            pl.BlockSpec((block, tile), lambda i: (0, i)),
            pl.BlockSpec((block, columns), lambda i: (0, 0)),
        ]
        + [pl.BlockSpec(memory_space=pl.ANY)] * len(others),
        out_specs=pl.BlockSpec((tile, columns), lambda i: (i, 0)),
        out_shape=jax.ShapeDtypeStruct((rows, columns), LOW),
        compiler_params=params(),
        cost_estimate=cost(2 * block * rows * columns, 6e6),
    )(a, b, *others)


def halves_kernel(d_ref, a_ref, b_ref, *rest):
    send_ref, keep_ref = rest[-2:]
    product = dot_tn(a_ref[...], b_ref[...]).astype(LOW)

    @pl.when(pl.program_id(0) == 0)
    def _():
        send_ref[...] = product

    @pl.when(pl.program_id(0) == 1)
    def _():
        keep_ref[...] = product


def token_halves(a, b, others):
    block, rows = a.shape
    columns = b.shape[1]
    tiles = 2 if rows % 512 == 0 else 1
    tile = rows // (2 * tiles)
    d = lax.axis_index("dp").astype(jnp.int32)[None]
    half = jax.ShapeDtypeStruct((rows // 2, columns), LOW)
    return pl.pallas_call(
        halves_kernel,
        grid_spec=pltpu.PrefetchScalarGridSpec(
            num_scalar_prefetch=1,
            grid=(2, tiles),
            in_specs=[
                pl.BlockSpec(
                    (block, tile),
                    lambda h, j, d: (0, ((1 - d[0]) * (1 - h) + d[0] * h) * tiles + j),
                ),
                pl.BlockSpec((block, columns), lambda h, j, d: (0, 0)),
            ]
            + [pl.BlockSpec(memory_space=pl.ANY)] * len(others),
            out_specs=[
                pl.BlockSpec((tile, columns), lambda h, j, d: (j * (1 - h) + (tiles - 1) * h, 0)),
                pl.BlockSpec((tile, columns), lambda h, j, d: (j * h, 0)),
            ],
        ),
        out_shape=[half, half],
        compiler_params=params(),
        cost_estimate=cost(2 * block * rows * columns, 6e6),
    )(d, a, b, *others)


def split_low(value):
    high = value.astype(LOW)
    return high, (value - high.astype(F32)).astype(LOW)


def norm_parts(rows):
    rr = lax.rsqrt(jnp.mean(rows * rows, axis=-1, keepdims=True) + EPS)
    return rows * rr, rr


def norm_back(grad, normal, rr, gain):
    weighted = grad * gain
    return rr * (weighted - normal * jnp.mean(weighted * normal, axis=-1, keepdims=True))


def add_all(refs):
    return functools.reduce(jnp.add, [ref[...].astype(F32) for ref in refs])


def pad_rows(rows, count):
    if rows.shape[0] == count:
        return rows
    return jnp.concatenate(
        [rows, jnp.zeros((count - rows.shape[0], rows.shape[1]), rows.dtype)], axis=0
    )


def router_kernel(experts, *refs):
    x_ref, attn_ref, gain_ref, router_ref, mask_ref = refs[:5]
    hidden_ref, mixed_ref, probs_ref = refs[-3:]
    width = x_ref.shape[1]
    lanes = mask_ref.shape[1]
    hidden = add_all([x_ref, attn_ref])
    hidden_ref[...] = hidden
    mixed = (norm_parts(hidden)[0] * gain_ref[...]).astype(LOW)
    mixed_ref[:, :width] = mixed
    logits = dot_nt(mixed, pad_rows(router_ref[...], lanes))
    lane = lax.broadcasted_iota(jnp.int32, logits.shape, 1)
    logits = jnp.where(lane < experts, logits, -1e30)
    weights = jnp.exp(logits - jnp.max(logits, axis=1, keepdims=True))
    probs = weights / jnp.sum(weights, axis=1, keepdims=True)
    probs_ref[...] = probs
    chosen = probs * mask_ref[...]
    high, low = split_low(chosen / jnp.sum(chosen, axis=1, keepdims=True))
    both = high.astype(F32) + pltpu.roll(low.astype(F32), experts, 1)
    mixed_ref[:, width:] = both.astype(LOW)


def route_rows(x, attn, gain, router, mask, experts, others):
    tokens, width = x.shape
    lanes = mask.shape[1]
    operands = [x, attn, gain[None], router, mask]
    shapes = [
        jax.ShapeDtypeStruct((tokens, width), F32),
        jax.ShapeDtypeStruct((tokens, width + lanes), LOW),
        jax.ShapeDtypeStruct((tokens, lanes), F32),
    ]
    return pl.pallas_call(
        functools.partial(router_kernel, experts),
        grid=(1,),
        in_specs=[full(value.shape) for value in operands]
        + [pl.BlockSpec(memory_space=pl.ANY)] * len(others),
        out_specs=[full(shape.shape) for shape in shapes],
        out_shape=shapes,
        compiler_params=params(),
        cost_estimate=cost(2 * tokens * width * lanes, 5e6),
    )(*operands, *others)


def one_hot(slots, count, first):
    groups, tokens = slots.shape
    slot = lax.broadcasted_iota(jnp.int32, (groups, count, tokens), 1).astype(F32)
    same = slots[:, None, :] == slot + float(first)
    return jnp.where(same, 1.0, 0.0).reshape(groups * count, tokens)


def slot_kernel(capacity, meta_ref, col_ref, rows_ref, slots_ref):
    groups, block = slots_ref.shape
    rows, width = rows_ref.shape
    n = rows // groups // capacity
    tokens = block // n
    mask = col_ref[:, width:]
    lanes = mask.shape[1]
    padded = -(-groups // 16) * 16
    group = lax.broadcasted_iota(jnp.int32, (padded, lanes), 0)
    lane = lax.broadcasted_iota(jnp.int32, (padded, lanes), 1)
    wanted = jnp.logical_and(lane == group * n + meta_ref[0], group < groups)
    hits = dot_nt(jnp.where(wanted, 1.0, 0.0).astype(LOW), mask)
    before = lax.broadcasted_iota(jnp.int32, (tokens, tokens), 0)
    after_it = lax.broadcasted_iota(jnp.int32, (tokens, tokens), 1)
    earlier = jnp.where(before < after_it, 1.0, 0.0).astype(LOW)
    for z in range(n):
        hit = hits[:, z * tokens : (z + 1) * tokens]
        rank = dot_nn(hit.astype(LOW), earlier)
        turn = (meta_ref[1 + z] * capacity).astype(F32)
        slot = jnp.where(hit > 0.5, rank + turn, -1.0)
        slots_ref[:, z * tokens : (z + 1) * tokens] = slot[:groups]
    spread = one_hot(slots_ref[...], n * capacity, 0).astype(LOW)
    rows_ref[...] = dot_nn(spread, col_ref[:, :width]).astype(LOW)


def make_slots(meta, col, width, groups, capacity):
    block = col.shape[0]
    n = lax.axis_size("expert")
    shapes = [
        jax.ShapeDtypeStruct((groups * n * capacity, width), LOW),
        jax.ShapeDtypeStruct((groups, block), F32),
    ]
    return pl.pallas_call(
        functools.partial(slot_kernel, capacity),
        grid_spec=pltpu.PrefetchScalarGridSpec(
            num_scalar_prefetch=1,
            grid=(1,),
            in_specs=[full(col.shape)],
            out_specs=[full(shape.shape) for shape in shapes],
        ),
        out_shape=shapes,
        compiler_params=params(),
        cost_estimate=cost(2 * groups * n * capacity * block * width, 8e6),
    )(meta, col)


def table_kernel(capacity, n_half, meta_ref, slots_ref, near_ref, far_ref, near_back_ref, far_back_ref):
    n = 2 * n_half
    tokens = slots_ref.shape[1] // n
    cap_half = n_half * capacity
    for part, (to_ref, back_ref) in enumerate([(near_ref, near_back_ref), (far_ref, far_back_ref)]):
        pieces = []
        for k in range(n_half):
            start = pl.multiple_of(meta_ref[1 + n + part * n_half + k] * tokens, tokens)
            pieces.append(slots_ref[:, pl.ds(start, tokens)])
        spread = one_hot(jnp.concatenate(pieces, axis=1), cap_half, part * cap_half)
        to_ref[...] = spread.astype(LOW)
        back_ref[...] = jnp.transpose(spread).astype(LOW)


def make_tables(meta, slots, n_half, capacity):
    groups, block = slots.shape
    rows = groups * n_half * capacity
    shapes = [jax.ShapeDtypeStruct((rows, block // 2), LOW)] * 2
    shapes += [jax.ShapeDtypeStruct((block // 2, rows), LOW)] * 2
    outs = pl.pallas_call(
        functools.partial(table_kernel, capacity, n_half),
        grid_spec=pltpu.PrefetchScalarGridSpec(
            num_scalar_prefetch=1,
            grid=(1,),
            in_specs=[full(slots.shape)],
            out_specs=[full(shape.shape) for shape in shapes],
        ),
        out_shape=shapes,
        compiler_params=params(),
        cost_estimate=cost(8 * rows * block, 3e6),
    )(meta, slots)
    return outs[:2], outs[2:]


def spread_kernel(choices, place_ref, spread_ref, *refs):
    out_ref, rows_ref = refs[-2:]
    for k, by_place in enumerate(choices):
        for which in sorted(set(by_place)):
            hit = functools.reduce(
                jnp.logical_or,
                [place_ref[0] == i for i, other in enumerate(by_place) if other == which],
            )

            @pl.when(hit)
            def _():
                tokens = refs[which].shape[0]
                rows_ref[k * tokens : (k + 1) * tokens] = refs[which][...]

    out_ref[...] = dot_nn(spread_ref[...], rows_ref[...]).astype(LOW)


def spread_rows(place, spread, found, turns, others):
    n = lax.axis_size("expert")
    order = arrival_order(n)
    distances = sorted({order[i][turn] - i for i in range(n) for turn in turns})
    choices = [[distances.index(order[i][turn] - i) for i in range(n)] for turn in turns]
    chunks = [found[distance] for distance in distances]
    tokens, wide = chunks[0].shape
    rows = spread.shape[0]
    return pl.pallas_call(
        functools.partial(spread_kernel, choices),
        grid_spec=pltpu.PrefetchScalarGridSpec(
            num_scalar_prefetch=1,
            grid=(1,),
            in_specs=[full(spread.shape)]
            + [full(chunk.shape) for chunk in chunks]
            + [pl.BlockSpec(memory_space=pl.ANY)] * len(others),
            out_specs=full((rows, wide)),
            scratch_shapes=[pltpu.VMEM((len(turns) * tokens, wide), LOW)],
        ),
        out_shape=jax.ShapeDtypeStruct((rows, wide), LOW),
        compiler_params=params(),
        cost_estimate=cost(2 * rows * len(turns) * tokens * wide, 5e6),
    )(place, spread, *chunks, *others)


def router_back_kernel(experts, *refs):
    sum_ref, g_ref, hidden_ref, gain_ref, router_ref, mask_ref, probs_ref = refs[:7]
    grad_ref, low_ref, dgain_ref, drouter_ref = refs[-4:]
    width = g_ref.shape[1]
    lanes = mask_ref.shape[1]
    total = sum_ref[...].astype(F32)
    table = total[:, width:]
    mask, probs = mask_ref[...], probs_ref[...]
    grad_gates = (table + pltpu.roll(table, lanes - experts, 1)) * mask
    chosen = probs * mask
    chosen_sum = jnp.sum(chosen, axis=1, keepdims=True)
    mean = jnp.sum(grad_gates * (chosen / chosen_sum), axis=1, keepdims=True)
    centred = mask * (grad_gates - mean) / chosen_sum
    grad_logits = probs * (centred - jnp.sum(centred * chosen, axis=1, keepdims=True))
    high, low = split_low(grad_logits)
    router = pad_rows(router_ref[...], lanes)
    grad = total[:, :width] + dot_nn(high, router) + dot_nn(low, router)
    normal, rr = norm_parts(hidden_ref[...])
    mixed = (normal * gain_ref[...]).astype(LOW)
    drouter_ref[...] = dot_tn(high, mixed) + dot_tn(low, mixed)
    dgain_ref[...] = jnp.sum(grad * normal, axis=0, keepdims=True)
    grad_hidden = g_ref[...].astype(F32) + norm_back(grad, normal, rr, gain_ref[...])
    grad_ref[...] = grad_hidden
    low_ref[...] = grad_hidden.astype(LOW)


def route_back(summed, g, hidden, gain, router, mask, probs, experts, others):
    tokens, width = g.shape
    lanes = mask.shape[1]
    operands = [summed, g, hidden, gain[None], router, mask, probs]
    shapes = [
        jax.ShapeDtypeStruct((tokens, width), F32),
        jax.ShapeDtypeStruct((tokens, width), LOW),
        jax.ShapeDtypeStruct((1, width), F32),
        jax.ShapeDtypeStruct((lanes, width), F32),
    ]
    return pl.pallas_call(
        functools.partial(router_back_kernel, experts),
        grid=(1,),
        in_specs=[full(value.shape) for value in operands]
        + [pl.BlockSpec(memory_space=pl.ANY)] * len(others),
        out_specs=[full(shape.shape) for shape in shapes],
        out_shape=shapes,
        compiler_params=params(),
        cost_estimate=cost(8 * tokens * width * lanes, 8e6),
    )(*operands, *others)


def combine_kernel(meta_ref, table_ref, rows_ref, *rest):
    del meta_ref
    rest[-1][...] = dot_nn(table_ref[...], rows_ref[...]).astype(LOW)


def combine_part(meta, table, rows, first, n, into, others):
    block, slots = table.shape
    wide = rows.shape[1]
    tokens = block // (n // 2)
    return pl.pallas_call(
        combine_kernel,
        grid_spec=pltpu.PrefetchScalarGridSpec(
            num_scalar_prefetch=1,
            grid=(n // 2,),
            in_specs=[
                pl.BlockSpec((tokens, slots), lambda i, m: (i, 0)),
                full(rows.shape),
            ]
            + [pl.BlockSpec(memory_space=pl.ANY)] * (len(into) + len(others)),
            out_specs=pl.BlockSpec((tokens, wide), lambda i, m: (m[1 + n + first + i], 0)),
        ),
        out_shape=jax.ShapeDtypeStruct((n * tokens, wide), LOW),
        input_output_aliases={3: 0} if into else {},
        compiler_params=params(),
        cost_estimate=cost(2 * slots * block * wide, 6e6),
    )(meta, table, rows, *into, *others)


def combine_rows(meta, tables, rows, n_half, others):
    near = combine_part(meta, tables[0], rows[0], 0, 2 * n_half, [], [])
    return combine_part(meta, tables[1], rows[1], n_half, 2 * n_half, [near], others)


def expert_kernel(experts, who_ref, x_ref, gate_ref, up_ref, pull_ref, *rest):
    act_ref, dgate_ref, dup_ref, copy_ref = rest[-4:]
    width = gate_ref.shape[0]
    x = x_ref[:, :width]
    table = x_ref[:, width:].astype(F32)
    lane = lax.broadcasted_iota(jnp.int32, table.shape, 1)
    mine = who_ref[0]
    gate = jnp.sum(
        jnp.where(jnp.logical_or(lane == mine, lane == mine + experts), table, 0.0),
        axis=1,
        keepdims=True,
    )
    pre_gate = dot_nn(x, gate_ref[...])
    pre_up = dot_nn(x, up_ref[...])
    pull = pull_ref[...].reshape(pre_up.shape)
    sig = 1.0 / (1.0 + jnp.exp(-pre_gate))
    silu = pre_gate * sig
    act = silu * pre_up
    act_ref[...] = (act * gate).astype(LOW)
    high, low = split_low(jnp.sum(act * pull, axis=1, keepdims=True))
    pull = pull * gate
    dup = (pull * silu).astype(LOW)
    dgate = (pull * pre_up * (sig * (1.0 + pre_gate * (1.0 - sig)))).astype(LOW)
    dgate_ref[...] = dgate
    dup_ref[...] = dup
    copy_ref[:, :width] = (dot_nt(dgate, gate_ref[...]) + dot_nt(dup, up_ref[...])).astype(LOW)
    back = jnp.where(lane == mine, high.astype(F32), 0.0)
    back = jnp.where(lane == mine + experts, low.astype(F32), back)
    copy_ref[:, width:] = back.astype(LOW)


def run_expert(who, x, w_gate, w_up, pull, part, experts):
    rows, wide = x.shape
    width, hidden = w_gate.shape
    groups, _, slots, _ = pull.shape
    each = groups // 2
    tile = each * slots
    by_rows = lambda columns: pl.BlockSpec((tile, columns), lambda i, p: (i, 0))
    return pl.pallas_call(
        functools.partial(expert_kernel, experts),
        grid_spec=pltpu.PrefetchScalarGridSpec(
            num_scalar_prefetch=1,
            grid=(2,),
            in_specs=[
                by_rows(wide),
                full(w_gate.shape),
                full(w_up.shape),
                pl.BlockSpec((each, 1, slots, hidden), lambda i, p: (i, part, 0, 0)),
            ],
            out_specs=[by_rows(hidden), by_rows(hidden), by_rows(hidden), by_rows(wide)],
        ),
        out_shape=[jax.ShapeDtypeStruct((rows, hidden), LOW)] * 3
        + [jax.ShapeDtypeStruct((rows, wide), LOW)],
        compiler_params=params(),
        cost_estimate=cost(8 * rows * width * hidden, 20e6, rows * hidden),
    )(who, x, w_gate, w_up, pull)


def input_kernel(grad_ref, x_ref, gain_ref, more_ref, out_ref):
    normal, rr = norm_parts(x_ref[...].astype(F32))
    grad = grad_ref[...].astype(F32)
    out_ref[...] = more_ref[...] + norm_back(grad, normal, rr, gain_ref[...])


def input_back(grad, x, gain, more):
    tokens, width = x.shape
    operands = [grad, x, gain[None], more]
    return pl.pallas_call(
        input_kernel,
        grid=(1,),
        in_specs=[full(value.shape) for value in operands],
        out_specs=full(more.shape),
        out_shape=jax.ShapeDtypeStruct((tokens, width), F32),
        compiler_params=params(),
        cost_estimate=cost(20 * tokens * width, 5e6),
    )(*operands)


def kv_back_kernel(factor, parts_ref, proj_ref, gain_ref, cos_ref, sin_ref, *rest):
    grad_ref, dgain_ref = rest[-2:]
    size = proj_ref.shape[1]
    total = parts_ref[0].astype(F32)
    for k in range(1, parts_ref.shape[0]):
        total += parts_ref[k].astype(F32)
    grad, dgain = head_backward(
        total[:, :size] * factor, proj_ref[...], gain_ref[...], cos_ref[...], sin_ref[...]
    )
    grad_ref[:, :size] = grad.astype(LOW)
    grad_ref[:, size:] = total[:, size:].astype(LOW)
    dgain_ref[...] = dgain


def kv_back(parts, proj, gain, cos2, sin2, factor, others):
    block, size = proj.shape
    operands = [parts, proj, gain[None], cos2, sin2]
    shapes = [
        jax.ShapeDtypeStruct((block, 2 * size), LOW),
        jax.ShapeDtypeStruct((1, size), F32),
    ]
    return pl.pallas_call(
        functools.partial(kv_back_kernel, factor),
        grid=(1,),
        in_specs=[full(value.shape) for value in operands]
        + [pl.BlockSpec(memory_space=pl.ANY)] * len(others),
        out_specs=[full(shape.shape) for shape in shapes],
        out_shape=shapes,
        compiler_params=params(),
        cost_estimate=cost(40 * block * size, 5e6),
    )(*operands, *others)


def pair_kernel(a_ref, b_ref, *rest):
    rest[-1][...] = (a_ref[...].astype(F32) + b_ref[...].astype(F32)).astype(LOW)


def pair_sum(a, b, others):
    rows, columns = a.shape
    tiles = 2 if rows % 32 == 0 else 1
    spec = pl.BlockSpec((rows // tiles, columns), lambda i: (i, 0))
    return pl.pallas_call(
        pair_kernel,
        grid=(tiles,),
        in_specs=[spec, spec] + [pl.BlockSpec(memory_space=pl.ANY)] * len(others),
        out_specs=spec,
        out_shape=jax.ShapeDtypeStruct((rows, columns), LOW),
        compiler_params=params(),
        cost_estimate=cost(rows * columns, 6 * rows * columns),
    )(a, b, *others)


def fold_kernel(n_pairs, s_ref, *refs):
    del s_ref
    send_ref, keep_ref = refs[-2:]
    totals = [
        (refs[2 * k][...].astype(F32) + refs[2 * k + 1][...].astype(F32)).astype(LOW)
        for k in range(n_pairs)
    ]
    for half, out_ref in enumerate((send_ref, keep_ref)):

        @pl.when(pl.program_id(0) == half)
        def _():
            first = 0
            for total in totals:
                last = first + total.shape[1]
                out_ref[:, first:last] = total
                first = last


def fold(pairs, bit, others):
    rows = pairs[0][1].shape[0]
    columns = sum(got.shape[1] for _, got in pairs)
    tiles = 2
    tile = rows // (2 * tiles)
    side = lambda h, m: (1 - m[0]) * (1 - h) + m[0] * h
    specs = []
    for _, got in pairs:
        wide = got.shape[1]
        specs += [pl.BlockSpec((tile, wide), lambda h, j, m: (side(h, m) * tiles + j, 0))] * 2
    shape = jax.ShapeDtypeStruct((rows // 2, columns), LOW)
    return pl.pallas_call(
        functools.partial(fold_kernel, len(pairs)),
        grid_spec=pltpu.PrefetchScalarGridSpec(
            num_scalar_prefetch=1,
            grid=(2, tiles),
            in_specs=specs + [pl.BlockSpec(memory_space=pl.ANY)] * len(others),
            out_specs=[
                pl.BlockSpec((tile, columns), lambda h, j, m: (j * (1 - h) + (tiles - 1) * h, 0)),
                pl.BlockSpec((tile, columns), lambda h, j, m: (j * h, 0)),
            ],
        ),
        out_shape=[shape, shape],
        compiler_params=params(),
        cost_estimate=cost(rows * columns, 6 * rows * columns),
    )(
        bit.astype(jnp.int32)[None],
        *[value for pair in pairs for value in pair],
        *others,
    )


def normed_kernel(q_ref, kv_ref, wq_ref, wkv_ref, rows_ref, *rest):
    out_ref, dgain_ref = rest[-2:]
    grad = dot_nt(q_ref[...], wq_ref[...]) + dot_nt(kv_ref[...], wkv_ref[...])
    out_ref[...] = grad.astype(LOW)
    dgain_ref[...] = jnp.sum(grad * rows_ref[...].astype(F32), axis=0, keepdims=True)


def normed_back(grad_q, grad_kv, w_q, w_kv, rows, others):
    block, width = rows.shape
    tile = 512
    column = lambda i: (0, i)
    return pl.pallas_call(
        normed_kernel,
        grid=(width // tile,),
        in_specs=[
            full(grad_q.shape),
            full(grad_kv.shape),
            pl.BlockSpec((tile, w_q.shape[1]), lambda i: (i, 0)),
            pl.BlockSpec((tile, w_kv.shape[1]), lambda i: (i, 0)),
            pl.BlockSpec((block, tile), column),
        ]
        + [pl.BlockSpec(memory_space=pl.ANY)] * len(others),
        out_specs=[pl.BlockSpec((block, tile), column), pl.BlockSpec((1, tile), column)],
        out_shape=[
            jax.ShapeDtypeStruct((block, width), LOW),
            jax.ShapeDtypeStruct((1, width), F32),
        ],
        compiler_params=params(),
        cost_estimate=cost(2 * block * width * (w_q.shape[1] + w_kv.shape[1]), 12e6),
    )(grad_q, grad_kv, w_q, w_kv, rows, *others)


def pack_kernel(experts, router_ref, attn_ref, gain_ref, mlp_ref, q_ref, k_ref, *rest):
    out_ref, rows_ref = rest[-2:]
    size = q_ref.shape[1]
    rows_ref[:experts] = router_ref[:experts]
    rows_ref[experts:] = jnp.zeros_like(rows_ref[experts:])
    rows_ref[experts : experts + 1] = attn_ref[...] / gain_ref[...]
    rows_ref[experts + 1 : experts + 2] = mlp_ref[...]
    rows_ref[experts + 2 : experts + 3, :size] = q_ref[...]
    rows_ref[experts + 2 : experts + 3, size : 2 * size] = k_ref[...]
    out_ref[...] = rows_ref[...].astype(LOW)


def pack_small(experts, router, attn, gain, mlp, q, k, others):
    width = attn.shape[1]
    n = lax.axis_size(ALL_AXES)
    shape = (-(-(experts + 3) // n) * n, width)
    operands = [router, attn, gain[None], mlp, q, k]
    return pl.pallas_call(
        functools.partial(pack_kernel, experts),
        grid=(1,),
        in_specs=[full(value.shape) for value in operands]
        + [pl.BlockSpec(memory_space=pl.ANY)] * len(others),
        out_specs=full(shape),
        out_shape=jax.ShapeDtypeStruct(shape, LOW),
        scratch_shapes=[pltpu.VMEM(shape, F32)],
        compiler_params=params(),
        cost_estimate=cost(shape[0] * width, 6 * shape[0] * width),
    )(*operands, *others)


def part_sum_kernel(parts_ref, *rest):
    total = parts_ref[0].astype(F32)
    for k in range(1, parts_ref.shape[0]):
        total += parts_ref[k].astype(F32)
    rest[-1][...] = total.astype(LOW)


def part_sum(parts, others):
    count, rows, columns = parts.shape
    tiles = 2
    return pl.pallas_call(
        part_sum_kernel,
        grid=(tiles,),
        in_specs=[pl.BlockSpec((count, rows // tiles, columns), lambda i: (0, i, 0))]
        + [pl.BlockSpec(memory_space=pl.ANY)] * len(others),
        out_specs=pl.BlockSpec((rows // tiles, columns), lambda i: (i, 0)),
        out_shape=jax.ShapeDtypeStruct((rows, columns), LOW),
        compiler_params=params(),
        cost_estimate=cost(count * rows * columns, 4 * count * rows * columns),
    )(parts, *others)


def widen_kernel(n_chunks, n_outs, at_ref, *refs):
    del at_ref
    outs = refs[-n_outs:]
    widths = [ref.shape[1] for ref in outs]
    for k in range(n_chunks):

        @pl.when(pl.program_id(0) == k)
        def _():
            first = 0
            for wide, out_ref in zip(widths, outs):
                out_ref[...] = refs[k][:, first : first + wide].astype(F32)
                first += wide


def widen(places, chunks, widths, others):
    rows, columns = chunks[0].shape
    count = len(chunks)
    return pl.pallas_call(
        functools.partial(widen_kernel, count, len(widths)),
        grid_spec=pltpu.PrefetchScalarGridSpec(
            num_scalar_prefetch=1,
            grid=(count,),
            in_specs=[full(chunk.shape) for chunk in chunks]
            + [pl.BlockSpec(memory_space=pl.ANY)] * len(others),
            out_specs=[pl.BlockSpec((rows, wide), lambda i, at: (at[i], 0)) for wide in widths],
        ),
        out_shape=[jax.ShapeDtypeStruct((count * rows, wide), F32) for wide in widths],
        compiler_params=params(),
        cost_estimate=cost(rows * columns, 6 * count * rows * columns),
    )(jnp.stack(places).astype(jnp.int32), *chunks, *others)


def swap_dp(rows):
    return lax.ppermute(rows, "dp", [(0, 1), (1, 0)])


def swap_context(rows, s):
    n = lax.axis_size("context")
    return lax.ppermute(rows, "context", [(i, i ^ s) for i in range(n)])


def share_context(parts):
    return lax.all_to_all(parts, "context", split_axis=0, concat_axis=0, tiled=True)


def plane_turns():
    d, c = lax.axis_index("dp"), lax.axis_index("context")
    low, high = lax.rem(c, 2), lax.div(c, 2)

    def swap(first, second):
        perm = [(i, i ^ first) for i in range(4)] + [(4 + i, 4 + (i ^ second)) for i in range(4)]
        return lambda rows: lax.ppermute(rows, GROUP_AXES, perm)

    return [
        (jnp.where(d == 0, low, high), swap(1, 2)),
        (jnp.where(d == 0, high, low), swap(2, 1)),
    ]


def plane_first(pairs, others):
    (bit_1, _), _ = plane_turns()
    return fold(pairs, bit_1, others)


def plane_second(send, keep, others):
    (_, swap_1), (bit_2, _) = plane_turns()
    return fold([(keep, swap_1(send))], bit_2, others)


def plane_last(send, keep, others):
    _, (_, swap_2) = plane_turns()
    return pair_sum(keep, swap_2(send), others)


def plane_spread(own):
    (_, swap_1), (_, swap_2) = plane_turns()
    second = swap_2(own)
    return [own, second, swap_1(own), swap_1(second)]


def quarter_places(rank):
    d = lax.axis_index("dp")
    c = lax.axis_index("context")
    low, high = lax.rem(c, 2), lax.div(c, 2)
    places = []
    for core in (d, 1 - d):
        bit_1 = jnp.where(core == 0, low, high)
        bit_2 = jnp.where(core == 0, high, low)
        for flip_1, flip_2 in ((0, 0), (0, 1), (1, 0), (1, 1)):
            places.append(4 * core + rank(core, bit_1 ^ flip_1, bit_2 ^ flip_2))
    return places


def widen_all(quarters, places, widths, others):
    return widen(places, quarters + [swap_dp(part) for part in quarters], widths, others)


def arrival_order(n):
    return [sorted(range(n), key=lambda j: (abs(j - i), j)) for i in range(n)]


def choose(index, options):
    distinct = []
    for option in options:
        if option is not None and not any(option is other for other in distinct):
            distinct.append(option)
    result = distinct[0]
    for option in distinct[1:]:
        mask = functools.reduce(
            jnp.logical_or, [index == i for i, other in enumerate(options) if other is option]
        )
        result = jnp.where(mask, option, result)
    return result


def line_gather(chunk):
    return line_steps({0: chunk}, 1, lax.axis_size("expert"))


def line_steps(found, first, stop):
    n = lax.axis_size("expert")
    found = dict(found)
    for s in range(first, stop):
        found[-s] = lax.ppermute(
            found[1 - s], "expert", [(i, i + 1) for i in range(s - 1, n - 1)]
        )
        found[s] = lax.ppermute(found[s - 1], "expert", [(i + 1, i) for i in range(n - s)])
    return found


def context_gather(rows):
    n = lax.axis_size("context")
    c = lax.axis_index("context")
    found = {0: rows}
    for s in range(1, n):
        found[s] = lax.ppermute(rows, "context", [(i, i ^ s) for i in range(n)])
    return jnp.concatenate([choose(c, [found[i ^ j] for i in range(n)]) for j in range(n)], axis=0)


def zero_of(*others):
    return functools.reduce(
        jnp.add,
        [
            lax.slice(other, (0,) * other.ndim, (1,) * other.ndim).reshape(()).astype(F32) * 0.0
            for other in others
        ],
    )


def after(value, *others):
    return (value.astype(F32) + zero_of(*others)).astype(value.dtype)


def on_device(
    layer_input,
    grad_output,
    attn_gain,
    query_weight,
    key_weight,
    value_weight,
    q_gain,
    k_gain,
    output_weight,
    mlp_gain,
    router,
    w_gate,
    w_up,
    w_down,
    routes,
    half_order,
):
    n_context = lax.axis_size("context")
    n_expert = lax.axis_size("expert")
    n_groups = lax.axis_size(GROUP_AXES)
    tok_dev, width = layer_input.shape[1:]
    size = q_gain.shape[0]
    kv_total = key_weight.shape[1] * n_expert
    group_dev = n_expert // (kv_total // size)
    kv_index = lax.axis_index("expert") // group_dev
    block = tok_dev * n_expert
    seq = block * n_context
    half = block // 2
    experts = router.shape[1]
    exp_dev = w_gate.shape[0]
    top = routes.shape[2]
    capacity = max(2, (tok_dev * top * 9 + 8 * experts - 1) // (8 * experts))
    scale = size ** (-0.5)

    seq_rows = jnp.arange(seq, dtype=jnp.int32)
    context = lax.axis_index("context")
    own_halves = lax.dynamic_slice_in_dim(half_order, 2 * context, 2)
    own_pos = (own_halves[:, None] * half + jnp.arange(half, dtype=jnp.int32)[None]).reshape(-1)
    per_half = half // TILE
    tile_pos = (half_order[:, None] * per_half + jnp.arange(per_half, dtype=jnp.int32)).reshape(-1)
    kidx = jnp.sum(
        (tile_pos[None, :] == jnp.arange(seq // TILE, dtype=jnp.int32)[:, None])
        * jnp.arange(seq // TILE, dtype=jnp.int32)[None, :],
        axis=1,
    ).astype(jnp.int32)
    qpos = lax.dynamic_slice_in_dim(tile_pos, context * (block // TILE), block // TILE)
    entry = jnp.arange(size)
    freq = jnp.power(THETA, -(2 * (entry % (size // 2))).astype(F32) / size)
    angles = own_pos.astype(F32)[:, None] * freq[None, :]
    cos2 = jnp.cos(angles)
    sin2 = jnp.sin(angles) * jnp.where(entry < size // 2, -1.0, 1.0)[None, :]

    place = lax.axis_index("expert")
    place_1 = place.astype(jnp.int32)[None]
    lanes = -(-2 * experts // 128) * 128
    mask = jnp.any(
        routes[0][:, :, None] == jnp.arange(lanes, dtype=jnp.int32)[None, None, :], axis=1
    )
    mask_wide = mask.astype(F32)
    router_rows = router.T

    x_low = layer_input[0]
    x_normal, _ = norm_parts(x_low.astype(F32))
    normed_found = line_gather((x_normal * attn_gain).astype(LOW))
    if group_dev == 1:
        kv_weights = jnp.concatenate([key_weight, value_weight], axis=1)
    else:
        key_whole = lax.all_gather(key_weight, "expert", axis=1, tiled=True)
        value_whole = lax.all_gather(value_weight, "expert", axis=1, tiled=True)
        kv_weights = jnp.concatenate(
            [
                lax.dynamic_slice_in_dim(key_whole, kv_index * size, size, 1),
                lax.dynamic_slice_in_dim(value_whole, kv_index * size, size, 1),
            ],
            axis=1,
        )
    grad_low = grad_output[0]
    normed_rows, own_kv, key_proj, grad_wide = project_keys(
        place_1,
        normed_found,
        kv_weights,
        k_gain,
        cos2,
        sin2,
        scale * LOG2E,
        grad_low,
        mask_wide,
    )
    grad_col = lax.all_gather(grad_wide, "expert", axis=0, tiled=True)
    kv_whole = context_gather(own_kv)
    queries, query_proj = project_queries(normed_rows, query_weight, q_gain, cos2, sin2)

    n_half = n_expert // 2
    order_here = jnp.asarray(arrival_order(n_expert), jnp.int32)[place]
    turn_here = jnp.sum(
        (order_here[:, None] == jnp.arange(n_expert, dtype=jnp.int32)[None, :])
        * jnp.arange(n_expert, dtype=jnp.int32)[:, None],
        axis=0,
    ).astype(jnp.int32)
    meta = jnp.concatenate([place_1, turn_here, order_here])
    grad_sent, slots = make_slots(meta, grad_col, width, n_groups, capacity)
    spreads, back_tables = make_tables(meta, slots, n_half, capacity)

    def swap_plane(rows):
        parts = rows.reshape(n_groups, -1, rows.shape[1])
        parts = lax.all_to_all(parts, GROUP_AXES, split_axis=0, concat_axis=0, tiled=True)
        return parts.reshape(rows.shape)

    attended, inverse = attend(qpos, kidx, queries, kv_whole, [])
    attn_part = out_dot(attended, output_weight, [grad_col])
    attn_rows = lax.psum_scatter(attn_part, "expert", scatter_dimension=0, tiled=True)

    grad_x = swap_plane(grad_sent)
    act_pull = dot_nt(grad_x, w_down[0]).reshape(n_groups, 2, n_half * capacity, -1)

    hidden, mixed, probs = route_rows(
        x_low, attn_rows, mlp_gain, router_rows, mask_wide, experts, []
    )

    who = (lax.axis_index(ALL_AXES) * exp_dev).astype(jnp.int32)[None]
    mixed_found = line_gather(mixed)
    near = spread_rows(place_1, spreads[0], mixed_found, range(n_half), [grad_x])
    x_near = swap_plane(near)
    worked_near = run_expert(who, x_near, w_gate[0], w_up[0], act_pull, 0, experts)
    far = spread_rows(place_1, spreads[1], mixed_found, range(n_half, n_expert), [x_near])
    x_far = swap_plane(far)
    worked_far = run_expert(who, x_far, w_gate[0], w_up[0], act_pull, 1, experts)
    xs = [x_near, x_far]
    acts, gate_lows, up_lows, copies = (list(pair) for pair in zip(worked_near, worked_far))
    back_far = swap_plane(copies[1])
    back_near = swap_plane(copies[0])
    join = lambda parts: jnp.concatenate(parts, axis=0)
    x_all = join([x[:, :width] for x in xs])
    grad_w_gate = dot_tn(x_all, join(gate_lows))
    grad_w_up = dot_tn(x_all, join(up_lows))
    grad_by_round = jnp.swapaxes(
        grad_x.reshape(n_groups, 2, n_half * capacity, width), 0, 1
    ).reshape(-1, width)
    grad_w_down = dot_tn(join(acts), grad_by_round)
    copies_col = combine_rows(
        meta, back_tables, [back_near, back_far], n_half, [grad_w_gate, grad_w_up]
    )
    copies_sum = lax.psum_scatter(copies_col, "expert", scatter_dimension=0, tiled=True)

    returned = [dot_nn(act, w_down[0]).astype(LOW) for act in acts]
    returned_near = swap_plane(returned[0])

    grad_hidden, grad_hidden_low, grad_mlp_gain, grad_router = route_back(
        copies_sum,
        grad_low,
        hidden,
        mlp_gain,
        router_rows,
        mask_wide,
        probs,
        experts,
        [returned_near, grad_w_down],
    )

    returned_far = swap_plane(returned[1])
    grad_attn = lax.all_gather(grad_hidden_low, "expert", axis=0, tiled=True)
    grad_o, centre = grad_attended(
        grad_attn, output_weight, attended, inverse, [returned_far]
    )
    combined = combine_rows(meta, back_tables, [returned_near, returned_far], n_half, [])
    output_rows = lax.psum_scatter(combined, "expert", scatter_dimension=0, tiled=True)
    w_out_send, w_out_keep = token_halves(attended, grad_attn, [combined])
    w_out_half = pair_sum(w_out_keep, swap_dp(w_out_send), [grad_o])
    w_out_parts = share_context(w_out_half.reshape(n_context, -1, width))
    grad_kv, grad_q, grad_q_gain = attend_back(
        qpos,
        kidx,
        queries,
        grad_o,
        centre,
        kv_whole,
        query_proj,
        q_gain,
        cos2,
        sin2,
        [w_out_half],
    )
    kv_parts = share_context(grad_kv.astype(LOW).reshape(n_context, block, 2 * size))
    w_out_own = part_sum(w_out_parts, [grad_kv])
    w_query_send, w_query_keep = token_halves(normed_rows, grad_q, [w_out_own])
    w_query_got = swap_dp(w_query_send)
    output_rows = hidden + output_rows.astype(F32) + zero_of(w_query_keep)

    kv_grads, grad_k_gain = kv_back(
        kv_parts, key_proj, k_gain, cos2, sin2, scale, [w_query_keep]
    )
    w_out_quarters = plane_spread(w_out_own)
    pairs = [(w_query_keep, w_query_got)]
    widths = [query_weight.shape[1]]
    if group_dev == 1:
        w_kv_send, w_kv_keep = token_halves(normed_rows, kv_grads, [])
        pairs.append((w_kv_keep, swap_dp(w_kv_send)))
        widths += [key_weight.shape[1], value_weight.shape[1]]
    grad_normed, gain_rows = normed_back(
        grad_q, kv_grads, query_weight, kv_weights, normed_rows, []
    )
    send, keep = plane_first(pairs, [*w_out_quarters, grad_normed])
    (grad_w_out,) = widen_all(
        w_out_quarters,
        quarter_places(lambda core, b1, b2: jnp.where(core == 0, b1 + 2 * b2, 2 * b1 + b2)),
        [width],
        [],
    )
    small = pack_small(
        experts,
        grad_router,
        gain_rows,
        attn_gain,
        grad_mlp_gain,
        grad_q_gain,
        grad_k_gain,
        [],
    )
    swap_all = lambda rows: lax.all_to_all(rows, ALL_AXES, split_axis=0, concat_axis=0, tiled=True)
    small_parts = swap_all(small.reshape(lax.axis_size(ALL_AXES), -1, width))
    small_own = jnp.sum(small_parts.astype(F32), axis=0).astype(LOW)
    second_send, second_keep = plane_second(send, keep, [small_own])
    quarter = plane_last(second_send, second_keep, [output_rows])
    grad_normed = lax.psum_scatter(grad_normed, "expert", scatter_dimension=0, tiled=True)
    grad_input = input_back(grad_normed, x_low, attn_gain, grad_hidden)
    small_sum = swap_all(jnp.broadcast_to(small_own[None], small_parts.shape))
    small_sum = small_sum.reshape(small.shape).astype(F32) + zero_of(grad_w_out, grad_input)
    quarters = [quarter] + [swap_context(quarter, s) for s in range(1, n_context)]
    d = lax.axis_index("dp")
    turned = lambda core, c: jnp.where(core == 0, 2 * lax.rem(c, 2) + lax.div(c, 2), c)
    places = [4 * core + turned(core, context ^ s) for core in (d, 1 - d) for s in range(n_context)]
    grad_w_query, *more = widen_all(quarters, places, widths, [small_sum])
    if group_dev == 1:
        grad_w_key, grad_w_value = more
    else:
        w_kv = token_dot(normed_rows, kv_grads, [])
        blank = jnp.zeros((width, kv_total), LOW)
        pieces = []
        for part in (w_kv[:, :size], w_kv[:, size:]):
            padded = lax.dynamic_update_slice(blank, part, (0, kv_index * size))
            pieces.append(lax.psum_scatter(padded, "expert", scatter_dimension=1, tiled=True))
        grad_w_key, grad_w_value = (lax.psum(piece, GROUP_AXES).astype(F32) for piece in pieces)
    grad_attn_gain, grad_mlp_gain = small_sum[experts], small_sum[experts + 1]
    grad_q_gain = small_sum[experts + 2, :size]
    grad_k_gain = small_sum[experts + 2, size : 2 * size]
    return (
        output_rows.astype(LOW)[None],
        grad_input[None],
        grad_attn_gain,
        grad_w_query,
        grad_w_key,
        grad_w_value,
        grad_q_gain,
        grad_k_gain,
        grad_w_out,
        grad_mlp_gain,
        small_sum[:experts].T,
        grad_w_gate[None],
        grad_w_up[None],
        grad_w_down[None],
    )


def solution(mesh):
    rows = P("dp", ("context", "expert"), None)
    expert = P(ALL_AXES, None, None)
    columns = P(None, "expert")
    in_specs = (
        rows,
        rows,
        P(),
        columns,
        columns,
        columns,
        P(),
        P(),
        P("expert", None),
        P(),
        P(),
        expert,
        expert,
        expert,
        rows,
        P(),
    )
    out_specs = (
        rows,
        rows,
        P(),
        columns,
        columns,
        columns,
        P(),
        P(),
        P("expert", None),
        P(),
        P(),
        expert,
        expert,
        expert,
    )
    return jax.shard_map(
        on_device, mesh=mesh, in_specs=in_specs, out_specs=out_specs, check_vma=False
    )
```

```python
import functools
import math

import jax
import jax.numpy as jnp
from jax import lax
from jax.experimental import pallas as pl
from jax.experimental.pallas import tpu as pltpu
from jax.sharding import PartitionSpec as P

EPS = 1e-06
THETA = 1000000.0
TILE = 256
PIECE = 128
VMEM_BYTES = 56 * 1024 * 1024
LOG2E = math.log2(math.e)
LOW = jnp.bfloat16
F32 = jnp.float32
ALL_AXES = ("dp", "context", "expert")
GROUP_AXES = ("dp", "context")


def dot_nn(a, b):
    return lax.dot_general(a, b, (((1,), (0,)), ((), ())), preferred_element_type=F32)


def dot_nt(a, b):
    return lax.dot_general(a, b, (((1,), (1,)), ((), ())), preferred_element_type=F32)


def dot_tn(a, b):
    return lax.dot_general(a, b, (((0,), (0,)), ((), ())), preferred_element_type=F32)


def params(**more):
    return pltpu.CompilerParams(vmem_limit_bytes=VMEM_BYTES, **more)


def cost(flops, nbytes, exps=0):
    return pl.CostEstimate(flops=int(flops), bytes_accessed=int(nbytes), transcendentals=int(exps))


def head_forward(u, gain, cos2, sin2):
    rr = lax.rsqrt(jnp.mean(u * u, axis=-1, keepdims=True) + EPS)
    y = u * rr * gain
    return y * cos2 + pltpu.roll(y, 64, 1) * sin2


def head_backward(gy, u, gain, cos2, sin2):
    g = gy * cos2 - pltpu.roll(gy, 64, 1) * sin2
    rr = lax.rsqrt(jnp.mean(u * u, axis=-1, keepdims=True) + EPS)
    n = u * rr
    gn = g * gain
    grad = rr * (gn - n * jnp.mean(gn * n, axis=-1, keepdims=True))
    return grad, jnp.sum(g * n, axis=0, keepdims=True)


def query_kernel(x_ref, w_ref, gain_ref, cos_ref, sin_ref, rot_ref, proj_ref):
    tiles, heads, rows, size = rot_ref.shape
    acc = dot_nn(x_ref[...], w_ref[...])
    for h in range(heads):
        u = acc[:, h * size : (h + 1) * size]
        rot = head_forward(u, gain_ref[...], cos_ref[...], sin_ref[...])
        proj_ref[:, h] = u.reshape(tiles, rows, size)
        rot_ref[:, h] = rot.astype(LOW).reshape(tiles, rows, size)


def project_queries(normed, weight, gain, cos2, sin2):
    block, width = normed.shape
    size = cos2.shape[1]
    heads = weight.shape[1] // size
    tiles = block // TILE
    whole = lambda i: (0, 0)
    per = lambda i: (0, i, 0, 0)
    shape = (tiles, heads, TILE, size)
    return pl.pallas_call(
        query_kernel,
        grid=(heads // 2,),
        in_specs=[
            pl.BlockSpec((block, width), whole),
            pl.BlockSpec((width, 2 * size), lambda i: (0, i)),
            pl.BlockSpec((1, size), whole),
            pl.BlockSpec((block, size), whole),
            pl.BlockSpec((block, size), whole),
        ],
        out_specs=[pl.BlockSpec((tiles, 2, TILE, size), per)] * 2,
        out_shape=[jax.ShapeDtypeStruct(shape, LOW), jax.ShapeDtypeStruct(shape, F32)],
        compiler_params=params(),
        cost_estimate=cost(2 * block * width * heads * size, 12e6),
    )(normed, weight, gain[None], cos2, sin2)


def put_in_order(place, refs, out_ref):
    n = (len(refs) + 1) // 2
    rows = refs[0].shape[0]
    for distance in range(1 - n, n):
        ref = refs[distance + n - 1]
        at = place + distance

        @pl.when(jnp.logical_and(at >= 0, at < n))
        def _():
            out_ref[pl.ds(pl.multiple_of(at * rows, rows), rows), :] = ref[...]


def chunk_list(found):
    n = (len(found) + 1) // 2
    return [found[distance] for distance in range(1 - n, n)]


def key_kernel(factor, n_chunks, place_ref, *refs):
    w_ref, gain_ref, cos_ref, sin_ref, g_ref, mask_ref = refs[n_chunks:-4]
    rows_ref, kv_ref, proj_ref, wide_ref = refs[-4:]
    size = proj_ref.shape[1]
    width = g_ref.shape[1]
    put_in_order(place_ref[0], refs[:n_chunks], rows_ref)
    wide_ref[:, :width] = g_ref[...]
    wide_ref[:, width:] = mask_ref[...].astype(LOW)
    acc = dot_nn(rows_ref[...], w_ref[...])
    u = acc[:, :size]
    rot = head_forward(u, gain_ref[...], cos_ref[...], sin_ref[...])
    proj_ref[...] = u
    kv_ref[:, :size] = (rot * factor).astype(LOW)
    kv_ref[:, size:] = acc[:, size:].astype(LOW)


def full(shape):
    return pl.BlockSpec(shape, lambda *_: (0,) * len(shape))


def project_keys(place, found, weight, gain, cos2, sin2, factor, g, mask):
    chunks = chunk_list(found)
    rows, width = chunks[0].shape
    block, size = cos2.shape
    operands = [*chunks, weight, gain[None], cos2, sin2, g, mask]
    shapes = [
        jax.ShapeDtypeStruct((block, width), LOW),
        jax.ShapeDtypeStruct((block, 2 * size), LOW),
        jax.ShapeDtypeStruct((block, size), F32),
        jax.ShapeDtypeStruct((rows, width + mask.shape[1]), LOW),
    ]
    return pl.pallas_call(
        functools.partial(key_kernel, factor, len(chunks)),
        grid_spec=pltpu.PrefetchScalarGridSpec(
            num_scalar_prefetch=1,
            grid=(1,),
            in_specs=[full(x.shape) for x in operands],
            out_specs=[full(x.shape) for x in shapes],
        ),
        out_shape=shapes,
        compiler_params=params(),
        cost_estimate=cost(4 * block * width * size, 8e6),
    )(place, *operands)


def in_order(last, step):
    lax.fori_loop(0, lax.div(last, 2), lambda p, c: (step([2 * p, 2 * p + 1], False), c)[1], 0)

    @pl.when(lax.rem(last, 2) == 1)
    def _():
        step([last - 1, last], True)

    @pl.when(lax.rem(last, 2) == 0)
    def _():
        step([last], True)


def attend_kernel(qpos_ref, kidx_ref, q_ref, kv_ref, *rest):
    out_ref, inv_ref, acc_ref = rest[-3:]
    heads, rows, size = q_ref.shape[1:]
    acc_ref[...] = jnp.zeros_like(acc_ref)

    def step(places, masked):
        starts = [pl.multiple_of(kidx_ref[place] * rows, rows) for place in places]
        count = len(places) * rows
        keys = jnp.concatenate([kv_ref[pl.ds(start, rows), :size] for start in starts], axis=0)
        values = jnp.concatenate([kv_ref[pl.ds(start, rows), size:] for start in starts], axis=0)
        values = jnp.concatenate([values, jnp.ones((count, size), LOW)], axis=1)
        for h in range(heads):
            for first in range(0, rows, PIECE):
                part = slice(first, first + PIECE)
                e = jnp.exp2(dot_nt(q_ref[0, h, part], keys))
                if masked:
                    qi = lax.broadcasted_iota(jnp.int32, e.shape, 0) + first
                    ki = lax.broadcasted_iota(jnp.int32, e.shape, 1) - (count - rows)
                    e = jnp.where(ki <= qi, e, 0.0)
                acc_ref[h, part] += dot_nn(e.astype(LOW), values)

    in_order(qpos_ref[pl.program_id(0)], step)
    for h in range(heads):
        inv = 1.0 / acc_ref[h, :, size:]
        inv_ref[0, h] = inv
        out_ref[:, h * size : (h + 1) * size] = (acc_ref[h, :, :size] * inv).astype(LOW)


def attend(qpos, kidx, queries, kv, others):
    tiles, heads, rows, size = queries.shape
    seq = kv.shape[0]
    return pl.pallas_call(
        attend_kernel,
        grid_spec=pltpu.PrefetchScalarGridSpec(
            num_scalar_prefetch=2,
            grid=(tiles,),
            in_specs=[
                pl.BlockSpec((1, heads, rows, size), lambda i, a, b: (i, 0, 0, 0)),
                pl.BlockSpec((seq, 2 * size), lambda i, a, b: (0, 0)),
            ]
            + [pl.BlockSpec(memory_space=pl.ANY)] * len(others),
            out_specs=[
                pl.BlockSpec((rows, heads * size), lambda i, a, b: (i, 0)),
                pl.BlockSpec((1, heads, rows, size), lambda i, a, b: (i, 0, 0, 0)),
            ],
            scratch_shapes=[pltpu.VMEM((heads, rows, 2 * size), F32)],
        ),
        out_shape=[
            jax.ShapeDtypeStruct((tiles * rows, heads * size), LOW),
            jax.ShapeDtypeStruct((tiles, heads, rows, size), F32),
        ],
        compiler_params=params(),
        cost_estimate=cost(
            6 * tiles * rows * heads * seq * size, 8e6, tiles * rows * heads * seq
        ),
    )(qpos, kidx, queries, kv, *others)


def grad_out_kernel(rows_ref, w_ref, o_ref, inv_ref, *rest):
    do_ref, centre_ref = rest[-2:]
    tiles, heads, rows, size = do_ref.shape
    acc = dot_nt(rows_ref[...], w_ref[...])
    for t in range(tiles):
        for h in range(heads):
            part = slice(t * rows, (t + 1) * rows), slice(h * size, (h + 1) * size)
            low = (acc[part] * inv_ref[t, h]).astype(LOW)
            do_ref[t, h] = low
            product = low.astype(F32) * o_ref[part].astype(F32)
            centre = jnp.sum(jnp.transpose(product), axis=0, keepdims=True)
            centre_ref[t, h] = jnp.broadcast_to(centre, (8, rows))


def grad_attended(grad_rows, weight, attended, inverse, others):
    tiles, heads, rows, size = inverse.shape
    block, width = grad_rows.shape
    return pl.pallas_call(
        grad_out_kernel,
        grid=(heads // 2,),
        in_specs=[
            pl.BlockSpec((block, width), lambda i: (0, 0)),
            pl.BlockSpec((2 * size, width), lambda i: (i, 0)),
            pl.BlockSpec((block, 2 * size), lambda i: (0, i)),
            pl.BlockSpec((tiles, 2, rows, size), lambda i: (0, i, 0, 0)),
        ]
        + [pl.BlockSpec(memory_space=pl.ANY)] * len(others),
        out_specs=[
            pl.BlockSpec((tiles, 2, rows, size), lambda i: (0, i, 0, 0)),
            pl.BlockSpec((tiles, 2, 8, rows), lambda i: (0, i, 0, 0)),
        ],
        out_shape=[
            jax.ShapeDtypeStruct((tiles, heads, rows, size), LOW),
            jax.ShapeDtypeStruct((tiles, heads, 8, rows), F32),
        ],
        compiler_params=params(),
        cost_estimate=cost(2 * block * width * heads * size, 12e6),
    )(grad_rows, weight, attended, inverse, *others)


def attend_back_kernel(
    qpos_ref,
    kidx_ref,
    q_ref,
    do_ref,
    centre_ref,
    kv_ref,
    kt_ref,
    proj_ref,
    gain_ref,
    cos_ref,
    sin_ref,
    *rest,
):
    dkv_ref, dq_ref, dgain_ref, acc_ref, e_ref, ds_ref = rest[-6:]
    heads, rows, size = q_ref.shape[1:]

    @pl.when(pl.program_id(0) == 0)
    def _():
        dkv_ref[...] = jnp.zeros_like(dkv_ref)
        dgain_ref[...] = jnp.zeros_like(dgain_ref)

    acc_ref[...] = jnp.zeros_like(acc_ref)

    def step(places, masked):
        starts = [pl.multiple_of(kidx_ref[place] * rows, rows) for place in places]
        count = len(places) * rows
        keys = jnp.concatenate([kv_ref[pl.ds(start, rows), :size] for start in starts], axis=0)
        values = jnp.concatenate([kv_ref[pl.ds(start, rows), size:] for start in starts], axis=0)
        keys_t = jnp.concatenate([kt_ref[:, pl.ds(start, rows)] for start in starts], axis=1)
        for h in range(heads):
            query, grad = q_ref[0, h], do_ref[0, h]
            centre = centre_ref[0, h, 0:1]
            columns = slice(h * rows, (h + 1) * rows)
            for first in range(0, count, PIECE):
                part = slice(first, first + PIECE)
                e = jnp.exp2(dot_nt(keys[part], query))
                if masked and first >= count - rows:
                    ki = lax.broadcasted_iota(jnp.int32, e.shape, 0) + (first - (count - rows))
                    qi = lax.broadcasted_iota(jnp.int32, e.shape, 1)
                    e = jnp.where(ki <= qi, e, 0.0)
                ds = e * (dot_nt(values[part], grad) - centre)
                e_ref[part, columns] = e.astype(LOW)
                ds_ref[part, columns] = ds.astype(LOW)
            acc_ref[h] += dot_nn(keys_t, ds_ref[:count, columns])
        dk = dot_nn(ds_ref[:count], q_ref[0].reshape(heads * rows, size))
        dv = dot_nn(e_ref[:count], do_ref[0].reshape(heads * rows, size))
        for k, start in enumerate(starts):
            dkv_ref[pl.ds(start, rows), :size] += dk[k * rows : (k + 1) * rows]
            dkv_ref[pl.ds(start, rows), size:] += dv[k * rows : (k + 1) * rows]

    in_order(qpos_ref[pl.program_id(0)], step)
    total = jnp.zeros((1, size), F32)
    for h in range(heads):
        grad, gain_part = head_backward(
            jnp.transpose(acc_ref[h]) * (1.0 / LOG2E),
            proj_ref[0, h],
            gain_ref[...],
            cos_ref[...],
            sin_ref[...],
        )
        dq_ref[:, h * size : (h + 1) * size] = grad.astype(LOW)
        total += gain_part
    dgain_ref[...] += total


def attend_back(qpos, kidx, queries, grads, centre, kv, keys_t, proj, gain, cos2, sin2, others):
    tiles, heads, rows, size = queries.shape
    seq = kv.shape[0]
    per = pl.BlockSpec((1, heads, rows, size), lambda i, a, b: (i, 0, 0, 0))
    flat = lambda i, a, b: (0, 0)
    rowwise = lambda i, a, b: (i, 0)
    return pl.pallas_call(
        attend_back_kernel,
        grid_spec=pltpu.PrefetchScalarGridSpec(
            num_scalar_prefetch=2,
            grid=(tiles,),
            in_specs=[
                per,
                per,
                pl.BlockSpec((1, heads, 8, rows), lambda i, a, b: (i, 0, 0, 0)),
                pl.BlockSpec((seq, 2 * size), flat),
                pl.BlockSpec((size, seq), flat),
                per,
                pl.BlockSpec((1, size), flat),
                pl.BlockSpec((rows, size), rowwise),
                pl.BlockSpec((rows, size), rowwise),
            ]
            + [pl.BlockSpec(memory_space=pl.ANY)] * len(others),
            out_specs=[
                pl.BlockSpec((seq, 2 * size), flat),
                pl.BlockSpec((rows, heads * size), rowwise),
                pl.BlockSpec((1, size), flat),
            ],
            scratch_shapes=[pltpu.VMEM((heads, size, rows), F32)]
            + [pltpu.VMEM((2 * rows, heads * rows), LOW)] * 2,
        ),
        out_shape=[
            jax.ShapeDtypeStruct((seq, 2 * size), F32),
            jax.ShapeDtypeStruct((tiles * rows, heads * size), LOW),
            jax.ShapeDtypeStruct((1, size), F32),
        ],
        compiler_params=params(),
        cost_estimate=cost(
            15 * tiles * rows * heads * seq * size, 12e6, tiles * rows * heads * seq
        ),
    )(qpos, kidx, queries, grads, centre, kv, keys_t, proj, gain[None], cos2, sin2, *others)


def out_kernel(a_ref, b_ref, *rest):
    rest[-1][...] = dot_nn(a_ref[...], b_ref[...]).astype(LOW)


def out_dot(a, b, others):
    block, inner = a.shape
    columns = b.shape[1]
    tile = min(columns, 512)
    return pl.pallas_call(
        out_kernel,
        grid=(columns // tile,),
        in_specs=[
            pl.BlockSpec((block, inner), lambda i: (0, 0)),
            pl.BlockSpec((inner, tile), lambda i: (0, i)),
        ]
        + [pl.BlockSpec(memory_space=pl.ANY)] * len(others),
        out_specs=pl.BlockSpec((block, tile), lambda i: (0, i)),
        out_shape=jax.ShapeDtypeStruct((block, columns), LOW),
        compiler_params=params(),
        cost_estimate=cost(2 * block * inner * columns, 8e6),
    )(a, b, *others)


def token_kernel(a_ref, b_ref, *rest):
    rest[-1][...] = dot_tn(a_ref[...], b_ref[...]).astype(LOW)


def token_dot(a, b, others):
    block, rows = a.shape
    columns = b.shape[1]
    tile = min(rows, 512)
    return pl.pallas_call(
        token_kernel,
        grid=(rows // tile,),
        in_specs=[
            pl.BlockSpec((block, tile), lambda i: (0, i)),
            pl.BlockSpec((block, columns), lambda i: (0, 0)),
        ]
        + [pl.BlockSpec(memory_space=pl.ANY)] * len(others),
        out_specs=pl.BlockSpec((tile, columns), lambda i: (i, 0)),
        out_shape=jax.ShapeDtypeStruct((rows, columns), LOW),
        compiler_params=params(),
        cost_estimate=cost(2 * block * rows * columns, 6e6),
    )(a, b, *others)


def halves_kernel(d_ref, a_ref, b_ref, *rest):
    send_ref, keep_ref = rest[-2:]
    product = dot_tn(a_ref[...], b_ref[...]).astype(LOW)

    @pl.when(pl.program_id(0) == 0)
    def _():
        send_ref[...] = product

    @pl.when(pl.program_id(0) == 1)
    def _():
        keep_ref[...] = product


def token_halves(a, b, others):
    block, rows = a.shape
    columns = b.shape[1]
    tiles = 2 if rows % 512 == 0 else 1
    tile = rows // (2 * tiles)
    d = lax.axis_index("dp").astype(jnp.int32)[None]
    half = jax.ShapeDtypeStruct((rows // 2, columns), LOW)
    return pl.pallas_call(
        halves_kernel,
        grid_spec=pltpu.PrefetchScalarGridSpec(
            num_scalar_prefetch=1,
            grid=(2, tiles),
            in_specs=[
                pl.BlockSpec(
                    (block, tile),
                    lambda h, j, d: (0, ((1 - d[0]) * (1 - h) + d[0] * h) * tiles + j),
                ),
                pl.BlockSpec((block, columns), lambda h, j, d: (0, 0)),
            ]
            + [pl.BlockSpec(memory_space=pl.ANY)] * len(others),
            out_specs=[
                pl.BlockSpec((tile, columns), lambda h, j, d: (j * (1 - h) + (tiles - 1) * h, 0)),
                pl.BlockSpec((tile, columns), lambda h, j, d: (j * h, 0)),
            ],
        ),
        out_shape=[half, half],
        compiler_params=params(),
        cost_estimate=cost(2 * block * rows * columns, 6e6),
    )(d, a, b, *others)


def split_low(value):
    high = value.astype(LOW)
    return high, (value - high.astype(F32)).astype(LOW)


def norm_parts(rows):
    rr = lax.rsqrt(jnp.mean(rows * rows, axis=-1, keepdims=True) + EPS)
    return rows * rr, rr


def norm_back(grad, normal, rr, gain):
    weighted = grad * gain
    return rr * (weighted - normal * jnp.mean(weighted * normal, axis=-1, keepdims=True))


def add_all(refs):
    return functools.reduce(jnp.add, [ref[...].astype(F32) for ref in refs])


def pad_rows(rows, count):
    if rows.shape[0] == count:
        return rows
    return jnp.concatenate(
        [rows, jnp.zeros((count - rows.shape[0], rows.shape[1]), rows.dtype)], axis=0
    )


def router_kernel(experts, *refs):
    x_ref, attn_ref, gain_ref, router_ref, mask_ref = refs[:5]
    hidden_ref, mixed_ref, probs_ref = refs[-3:]
    width = x_ref.shape[1]
    lanes = mask_ref.shape[1]
    hidden = add_all([x_ref, attn_ref])
    hidden_ref[...] = hidden
    mixed = (norm_parts(hidden)[0] * gain_ref[...]).astype(LOW)
    mixed_ref[:, :width] = mixed
    logits = dot_nt(mixed, pad_rows(router_ref[...], lanes))
    lane = lax.broadcasted_iota(jnp.int32, logits.shape, 1)
    logits = jnp.where(lane < experts, logits, -1e30)
    weights = jnp.exp(logits - jnp.max(logits, axis=1, keepdims=True))
    probs = weights / jnp.sum(weights, axis=1, keepdims=True)
    probs_ref[...] = probs
    chosen = probs * mask_ref[...]
    high, low = split_low(chosen / jnp.sum(chosen, axis=1, keepdims=True))
    both = high.astype(F32) + pltpu.roll(low.astype(F32), experts, 1)
    mixed_ref[:, width:] = both.astype(LOW)


def route_rows(x, attn, gain, router, mask, experts, others):
    tokens, width = x.shape
    lanes = mask.shape[1]
    operands = [x, attn, gain[None], router, mask]
    shapes = [
        jax.ShapeDtypeStruct((tokens, width), F32),
        jax.ShapeDtypeStruct((tokens, width + lanes), LOW),
        jax.ShapeDtypeStruct((tokens, lanes), F32),
    ]
    return pl.pallas_call(
        functools.partial(router_kernel, experts),
        grid=(1,),
        in_specs=[full(value.shape) for value in operands]
        + [pl.BlockSpec(memory_space=pl.ANY)] * len(others),
        out_specs=[full(shape.shape) for shape in shapes],
        out_shape=shapes,
        compiler_params=params(),
        cost_estimate=cost(2 * tokens * width * lanes, 5e6),
    )(*operands, *others)


def one_hot(slots, count, first):
    groups, tokens = slots.shape
    slot = lax.broadcasted_iota(jnp.int32, (groups, count, tokens), 1).astype(F32)
    same = slots[:, None, :] == slot + float(first)
    return jnp.where(same, 1.0, 0.0).reshape(groups * count, tokens)


def slot_kernel(capacity, meta_ref, col_ref, rows_ref, slots_ref):
    groups, block = slots_ref.shape
    rows, width = rows_ref.shape
    n = rows // groups // capacity
    tokens = block // n
    mask = col_ref[:, width:]
    lanes = mask.shape[1]
    padded = -(-groups // 16) * 16
    group = lax.broadcasted_iota(jnp.int32, (padded, lanes), 0)
    lane = lax.broadcasted_iota(jnp.int32, (padded, lanes), 1)
    wanted = jnp.logical_and(lane == group * n + meta_ref[0], group < groups)
    hits = dot_nt(jnp.where(wanted, 1.0, 0.0).astype(LOW), mask)
    before = lax.broadcasted_iota(jnp.int32, (tokens, tokens), 0)
    after_it = lax.broadcasted_iota(jnp.int32, (tokens, tokens), 1)
    earlier = jnp.where(before < after_it, 1.0, 0.0).astype(LOW)
    for z in range(n):
        hit = hits[:, z * tokens : (z + 1) * tokens]
        rank = dot_nn(hit.astype(LOW), earlier)
        turn = (meta_ref[1 + z] * capacity).astype(F32)
        slot = jnp.where(hit > 0.5, rank + turn, -1.0)
        slots_ref[:, z * tokens : (z + 1) * tokens] = slot[:groups]
    spread = one_hot(slots_ref[...], n * capacity, 0).astype(LOW)
    rows_ref[...] = dot_nn(spread, col_ref[:, :width]).astype(LOW)


def make_slots(meta, col, width, groups, capacity):
    block = col.shape[0]
    n = lax.axis_size("expert")
    shapes = [
        jax.ShapeDtypeStruct((groups * n * capacity, width), LOW),
        jax.ShapeDtypeStruct((groups, block), F32),
    ]
    return pl.pallas_call(
        functools.partial(slot_kernel, capacity),
        grid_spec=pltpu.PrefetchScalarGridSpec(
            num_scalar_prefetch=1,
            grid=(1,),
            in_specs=[full(col.shape)],
            out_specs=[full(shape.shape) for shape in shapes],
        ),
        out_shape=shapes,
        compiler_params=params(),
        cost_estimate=cost(2 * groups * n * capacity * block * width, 8e6),
    )(meta, col)


def table_kernel(capacity, n_half, meta_ref, slots_ref, near_ref, far_ref, near_back_ref, far_back_ref):
    n = 2 * n_half
    tokens = slots_ref.shape[1] // n
    cap_half = n_half * capacity
    for part, (to_ref, back_ref) in enumerate([(near_ref, near_back_ref), (far_ref, far_back_ref)]):
        pieces = []
        for k in range(n_half):
            start = pl.multiple_of(meta_ref[1 + n + part * n_half + k] * tokens, tokens)
            pieces.append(slots_ref[:, pl.ds(start, tokens)])
        spread = one_hot(jnp.concatenate(pieces, axis=1), cap_half, part * cap_half)
        to_ref[...] = spread.astype(LOW)
        back_ref[...] = jnp.transpose(spread).astype(LOW)


def make_tables(meta, slots, n_half, capacity):
    groups, block = slots.shape
    rows = groups * n_half * capacity
    shapes = [jax.ShapeDtypeStruct((rows, block // 2), LOW)] * 2
    shapes += [jax.ShapeDtypeStruct((block // 2, rows), LOW)] * 2
    outs = pl.pallas_call(
        functools.partial(table_kernel, capacity, n_half),
        grid_spec=pltpu.PrefetchScalarGridSpec(
            num_scalar_prefetch=1,
            grid=(1,),
            in_specs=[full(slots.shape)],
            out_specs=[full(shape.shape) for shape in shapes],
        ),
        out_shape=shapes,
        compiler_params=params(),
        cost_estimate=cost(8 * rows * block, 3e6),
    )(meta, slots)
    return outs[:2], outs[2:]


def spread_kernel(choices, place_ref, spread_ref, *refs):
    out_ref, rows_ref = refs[-2:]
    for k, by_place in enumerate(choices):
        for which in sorted(set(by_place)):
            hit = functools.reduce(
                jnp.logical_or,
                [place_ref[0] == i for i, other in enumerate(by_place) if other == which],
            )

            @pl.when(hit)
            def _():
                tokens = refs[which].shape[0]
                rows_ref[k * tokens : (k + 1) * tokens] = refs[which][...]

    out_ref[...] = dot_nn(spread_ref[...], rows_ref[...]).astype(LOW)


def spread_rows(place, spread, found, turns, others):
    n = lax.axis_size("expert")
    order = arrival_order(n)
    distances = sorted({order[i][turn] - i for i in range(n) for turn in turns})
    choices = [[distances.index(order[i][turn] - i) for i in range(n)] for turn in turns]
    chunks = [found[distance] for distance in distances]
    tokens, wide = chunks[0].shape
    rows = spread.shape[0]
    return pl.pallas_call(
        functools.partial(spread_kernel, choices),
        grid_spec=pltpu.PrefetchScalarGridSpec(
            num_scalar_prefetch=1,
            grid=(1,),
            in_specs=[full(spread.shape)]
            + [full(chunk.shape) for chunk in chunks]
            + [pl.BlockSpec(memory_space=pl.ANY)] * len(others),
            out_specs=full((rows, wide)),
            scratch_shapes=[pltpu.VMEM((len(turns) * tokens, wide), LOW)],
        ),
        out_shape=jax.ShapeDtypeStruct((rows, wide), LOW),
        compiler_params=params(),
        cost_estimate=cost(2 * rows * len(turns) * tokens * wide, 5e6),
    )(place, spread, *chunks, *others)


def router_back_kernel(experts, *refs):
    sum_ref, g_ref, hidden_ref, gain_ref, router_ref, mask_ref, probs_ref = refs[:7]
    grad_ref, low_ref, dgain_ref, drouter_ref = refs[-4:]
    width = g_ref.shape[1]
    lanes = mask_ref.shape[1]
    total = sum_ref[...].astype(F32)
    table = total[:, width:]
    mask, probs = mask_ref[...], probs_ref[...]
    grad_gates = (table + pltpu.roll(table, lanes - experts, 1)) * mask
    chosen = probs * mask
    chosen_sum = jnp.sum(chosen, axis=1, keepdims=True)
    mean = jnp.sum(grad_gates * (chosen / chosen_sum), axis=1, keepdims=True)
    centred = mask * (grad_gates - mean) / chosen_sum
    grad_logits = probs * (centred - jnp.sum(centred * chosen, axis=1, keepdims=True))
    high, low = split_low(grad_logits)
    router = pad_rows(router_ref[...], lanes)
    grad = total[:, :width] + dot_nn(high, router) + dot_nn(low, router)
    normal, rr = norm_parts(hidden_ref[...])
    mixed = (normal * gain_ref[...]).astype(LOW)
    drouter_ref[...] = dot_tn(high, mixed) + dot_tn(low, mixed)
    dgain_ref[...] = jnp.sum(grad * normal, axis=0, keepdims=True)
    grad_hidden = g_ref[...].astype(F32) + norm_back(grad, normal, rr, gain_ref[...])
    grad_ref[...] = grad_hidden
    low_ref[...] = grad_hidden.astype(LOW)


def route_back(summed, g, hidden, gain, router, mask, probs, experts, others):
    tokens, width = g.shape
    lanes = mask.shape[1]
    operands = [summed, g, hidden, gain[None], router, mask, probs]
    shapes = [
        jax.ShapeDtypeStruct((tokens, width), F32),
        jax.ShapeDtypeStruct((tokens, width), LOW),
        jax.ShapeDtypeStruct((1, width), F32),
        jax.ShapeDtypeStruct((lanes, width), F32),
    ]
    return pl.pallas_call(
        functools.partial(router_back_kernel, experts),
        grid=(1,),
        in_specs=[full(value.shape) for value in operands]
        + [pl.BlockSpec(memory_space=pl.ANY)] * len(others),
        out_specs=[full(shape.shape) for shape in shapes],
        out_shape=shapes,
        compiler_params=params(),
        cost_estimate=cost(8 * tokens * width * lanes, 8e6),
    )(*operands, *others)


def combine_kernel(meta_ref, table_ref, rows_ref, *rest):
    del meta_ref
    rest[-1][...] = dot_nn(table_ref[...], rows_ref[...]).astype(LOW)


def combine_part(meta, table, rows, first, n, into, others):
    block, slots = table.shape
    wide = rows.shape[1]
    tokens = block // (n // 2)
    return pl.pallas_call(
        combine_kernel,
        grid_spec=pltpu.PrefetchScalarGridSpec(
            num_scalar_prefetch=1,
            grid=(n // 2,),
            in_specs=[
                pl.BlockSpec((tokens, slots), lambda i, m: (i, 0)),
                full(rows.shape),
            ]
            + [pl.BlockSpec(memory_space=pl.ANY)] * (len(into) + len(others)),
            out_specs=pl.BlockSpec((tokens, wide), lambda i, m: (m[1 + n + first + i], 0)),
        ),
        out_shape=jax.ShapeDtypeStruct((n * tokens, wide), LOW),
        input_output_aliases={3: 0} if into else {},
        compiler_params=params(),
        cost_estimate=cost(2 * slots * block * wide, 6e6),
    )(meta, table, rows, *into, *others)


def combine_rows(meta, tables, rows, n_half, others):
    near = combine_part(meta, tables[0], rows[0], 0, 2 * n_half, [], [])
    return combine_part(meta, tables[1], rows[1], n_half, 2 * n_half, [near], others)


def expert_kernel(experts, who_ref, x_ref, gate_ref, up_ref, pull_ref, *rest):
    act_ref, dgate_ref, dup_ref, copy_ref = rest[-4:]
    width = gate_ref.shape[0]
    x = x_ref[:, :width]
    table = x_ref[:, width:].astype(F32)
    lane = lax.broadcasted_iota(jnp.int32, table.shape, 1)
    mine = who_ref[0]
    gate = jnp.sum(
        jnp.where(jnp.logical_or(lane == mine, lane == mine + experts), table, 0.0),
        axis=1,
        keepdims=True,
    )
    pre_gate = dot_nn(x, gate_ref[...])
    pre_up = dot_nn(x, up_ref[...])
    pull = pull_ref[...].reshape(pre_up.shape)
    sig = 1.0 / (1.0 + jnp.exp(-pre_gate))
    silu = pre_gate * sig
    act = silu * pre_up
    act_ref[...] = (act * gate).astype(LOW)
    high, low = split_low(jnp.sum(act * pull, axis=1, keepdims=True))
    pull = pull * gate
    dup = (pull * silu).astype(LOW)
    dgate = (pull * pre_up * (sig * (1.0 + pre_gate * (1.0 - sig)))).astype(LOW)
    dgate_ref[...] = dgate
    dup_ref[...] = dup
    copy_ref[:, :width] = (dot_nt(dgate, gate_ref[...]) + dot_nt(dup, up_ref[...])).astype(LOW)
    back = jnp.where(lane == mine, high.astype(F32), 0.0)
    back = jnp.where(lane == mine + experts, low.astype(F32), back)
    copy_ref[:, width:] = back.astype(LOW)


def run_expert(who, x, w_gate, w_up, pull, part, experts):
    rows, wide = x.shape
    width, hidden = w_gate.shape
    groups, _, slots, _ = pull.shape
    each = groups // 2
    tile = each * slots
    by_rows = lambda columns: pl.BlockSpec((tile, columns), lambda i, p: (i, 0))
    return pl.pallas_call(
        functools.partial(expert_kernel, experts),
        grid_spec=pltpu.PrefetchScalarGridSpec(
            num_scalar_prefetch=1,
            grid=(2,),
            in_specs=[
                by_rows(wide),
                full(w_gate.shape),
                full(w_up.shape),
                pl.BlockSpec((each, 1, slots, hidden), lambda i, p: (i, part, 0, 0)),
            ],
            out_specs=[by_rows(hidden), by_rows(hidden), by_rows(hidden), by_rows(wide)],
        ),
        out_shape=[jax.ShapeDtypeStruct((rows, hidden), LOW)] * 3
        + [jax.ShapeDtypeStruct((rows, wide), LOW)],
        compiler_params=params(),
        cost_estimate=cost(8 * rows * width * hidden, 20e6, rows * hidden),
    )(who, x, w_gate, w_up, pull)


def input_kernel(grad_ref, x_ref, gain_ref, more_ref, out_ref):
    normal, rr = norm_parts(x_ref[...].astype(F32))
    grad = grad_ref[...].astype(F32)
    out_ref[...] = more_ref[...] + norm_back(grad, normal, rr, gain_ref[...])


def input_back(grad, x, gain, more):
    tokens, width = x.shape
    operands = [grad, x, gain[None], more]
    return pl.pallas_call(
        input_kernel,
        grid=(1,),
        in_specs=[full(value.shape) for value in operands],
        out_specs=full(more.shape),
        out_shape=jax.ShapeDtypeStruct((tokens, width), F32),
        compiler_params=params(),
        cost_estimate=cost(20 * tokens * width, 5e6),
    )(*operands)


def kv_back_kernel(factor, parts_ref, proj_ref, gain_ref, cos_ref, sin_ref, *rest):
    grad_ref, dgain_ref = rest[-2:]
    size = proj_ref.shape[1]
    total = parts_ref[0].astype(F32)
    for k in range(1, parts_ref.shape[0]):
        total += parts_ref[k].astype(F32)
    grad, dgain = head_backward(
        total[:, :size] * factor, proj_ref[...], gain_ref[...], cos_ref[...], sin_ref[...]
    )
    grad_ref[:, :size] = grad.astype(LOW)
    grad_ref[:, size:] = total[:, size:].astype(LOW)
    dgain_ref[...] = dgain


def kv_back(parts, proj, gain, cos2, sin2, factor, others):
    block, size = proj.shape
    operands = [parts, proj, gain[None], cos2, sin2]
    shapes = [
        jax.ShapeDtypeStruct((block, 2 * size), LOW),
        jax.ShapeDtypeStruct((1, size), F32),
    ]
    return pl.pallas_call(
        functools.partial(kv_back_kernel, factor),
        grid=(1,),
        in_specs=[full(value.shape) for value in operands]
        + [pl.BlockSpec(memory_space=pl.ANY)] * len(others),
        out_specs=[full(shape.shape) for shape in shapes],
        out_shape=shapes,
        compiler_params=params(),
        cost_estimate=cost(40 * block * size, 5e6),
    )(*operands, *others)


def pair_kernel(a_ref, b_ref, *rest):
    rest[-1][...] = (a_ref[...].astype(F32) + b_ref[...].astype(F32)).astype(LOW)


def pair_sum(a, b, others):
    rows, columns = a.shape
    tiles = 2 if rows % 32 == 0 else 1
    spec = pl.BlockSpec((rows // tiles, columns), lambda i: (i, 0))
    return pl.pallas_call(
        pair_kernel,
        grid=(tiles,),
        in_specs=[spec, spec] + [pl.BlockSpec(memory_space=pl.ANY)] * len(others),
        out_specs=spec,
        out_shape=jax.ShapeDtypeStruct((rows, columns), LOW),
        compiler_params=params(),
        cost_estimate=cost(rows * columns, 6 * rows * columns),
    )(a, b, *others)


def fold_kernel(n_pairs, s_ref, *refs):
    del s_ref
    send_ref, keep_ref = refs[-2:]
    totals = [
        (refs[2 * k][...].astype(F32) + refs[2 * k + 1][...].astype(F32)).astype(LOW)
        for k in range(n_pairs)
    ]
    for half, out_ref in enumerate((send_ref, keep_ref)):

        @pl.when(pl.program_id(0) == half)
        def _():
            first = 0
            for total in totals:
                last = first + total.shape[1]
                out_ref[:, first:last] = total
                first = last


def fold(pairs, bit, others):
    rows = pairs[0][1].shape[0]
    columns = sum(got.shape[1] for _, got in pairs)
    tiles = 2
    tile = rows // (2 * tiles)
    side = lambda h, m: (1 - m[0]) * (1 - h) + m[0] * h
    specs = []
    for _, got in pairs:
        wide = got.shape[1]
        specs += [pl.BlockSpec((tile, wide), lambda h, j, m: (side(h, m) * tiles + j, 0))] * 2
    shape = jax.ShapeDtypeStruct((rows // 2, columns), LOW)
    return pl.pallas_call(
        functools.partial(fold_kernel, len(pairs)),
        grid_spec=pltpu.PrefetchScalarGridSpec(
            num_scalar_prefetch=1,
            grid=(2, tiles),
            in_specs=specs + [pl.BlockSpec(memory_space=pl.ANY)] * len(others),
            out_specs=[
                pl.BlockSpec((tile, columns), lambda h, j, m: (j * (1 - h) + (tiles - 1) * h, 0)),
                pl.BlockSpec((tile, columns), lambda h, j, m: (j * h, 0)),
            ],
        ),
        out_shape=[shape, shape],
        compiler_params=params(),
        cost_estimate=cost(rows * columns, 6 * rows * columns),
    )(
        bit.astype(jnp.int32)[None],
        *[value for pair in pairs for value in pair],
        *others,
    )


def normed_kernel(q_ref, kv_ref, wq_ref, wkv_ref, rows_ref, *rest):
    out_ref, dgain_ref = rest[-2:]
    grad = dot_nt(q_ref[...], wq_ref[...]) + dot_nt(kv_ref[...], wkv_ref[...])
    out_ref[...] = grad.astype(LOW)
    dgain_ref[...] = jnp.sum(grad * rows_ref[...].astype(F32), axis=0, keepdims=True)


def normed_back(grad_q, grad_kv, w_q, w_kv, rows, others):
    block, width = rows.shape
    tile = 512
    column = lambda i: (0, i)
    return pl.pallas_call(
        normed_kernel,
        grid=(width // tile,),
        in_specs=[
            full(grad_q.shape),
            full(grad_kv.shape),
            pl.BlockSpec((tile, w_q.shape[1]), lambda i: (i, 0)),
            pl.BlockSpec((tile, w_kv.shape[1]), lambda i: (i, 0)),
            pl.BlockSpec((block, tile), column),
        ]
        + [pl.BlockSpec(memory_space=pl.ANY)] * len(others),
        out_specs=[pl.BlockSpec((block, tile), column), pl.BlockSpec((1, tile), column)],
        out_shape=[
            jax.ShapeDtypeStruct((block, width), LOW),
            jax.ShapeDtypeStruct((1, width), F32),
        ],
        compiler_params=params(),
        cost_estimate=cost(2 * block * width * (w_q.shape[1] + w_kv.shape[1]), 12e6),
    )(grad_q, grad_kv, w_q, w_kv, rows, *others)


def pack_kernel(experts, router_ref, attn_ref, gain_ref, mlp_ref, q_ref, k_ref, *rest):
    out_ref, rows_ref = rest[-2:]
    size = q_ref.shape[1]
    rows_ref[:experts] = router_ref[:experts]
    rows_ref[experts:] = jnp.zeros_like(rows_ref[experts:])
    rows_ref[experts : experts + 1] = attn_ref[...] / gain_ref[...]
    rows_ref[experts + 1 : experts + 2] = mlp_ref[...]
    rows_ref[experts + 2 : experts + 3, :size] = q_ref[...]
    rows_ref[experts + 2 : experts + 3, size : 2 * size] = k_ref[...]
    out_ref[...] = rows_ref[...].astype(LOW)


def pack_small(experts, router, attn, gain, mlp, q, k, others):
    width = attn.shape[1]
    n = lax.axis_size(ALL_AXES)
    shape = (-(-(experts + 3) // n) * n, width)
    operands = [router, attn, gain[None], mlp, q, k]
    return pl.pallas_call(
        functools.partial(pack_kernel, experts),
        grid=(1,),
        in_specs=[full(value.shape) for value in operands]
        + [pl.BlockSpec(memory_space=pl.ANY)] * len(others),
        out_specs=full(shape),
        out_shape=jax.ShapeDtypeStruct(shape, LOW),
        scratch_shapes=[pltpu.VMEM(shape, F32)],
        compiler_params=params(),
        cost_estimate=cost(shape[0] * width, 6 * shape[0] * width),
    )(*operands, *others)


def part_sum_kernel(parts_ref, *rest):
    total = parts_ref[0].astype(F32)
    for k in range(1, parts_ref.shape[0]):
        total += parts_ref[k].astype(F32)
    rest[-1][...] = total.astype(LOW)


def part_sum(parts, others):
    count, rows, columns = parts.shape
    tiles = 2
    return pl.pallas_call(
        part_sum_kernel,
        grid=(tiles,),
        in_specs=[pl.BlockSpec((count, rows // tiles, columns), lambda i: (0, i, 0))]
        + [pl.BlockSpec(memory_space=pl.ANY)] * len(others),
        out_specs=pl.BlockSpec((rows // tiles, columns), lambda i: (i, 0)),
        out_shape=jax.ShapeDtypeStruct((rows, columns), LOW),
        compiler_params=params(),
        cost_estimate=cost(count * rows * columns, 4 * count * rows * columns),
    )(parts, *others)


def widen_kernel(n_chunks, n_outs, at_ref, *refs):
    del at_ref
    outs = refs[-n_outs:]
    widths = [ref.shape[1] for ref in outs]
    for k in range(n_chunks):

        @pl.when(pl.program_id(0) == k)
        def _():
            first = 0
            for wide, out_ref in zip(widths, outs):
                out_ref[...] = refs[k][:, first : first + wide].astype(F32)
                first += wide


def widen(places, chunks, widths, total, into, others):
    rows, columns = chunks[0].shape
    count = len(chunks)
    return pl.pallas_call(
        functools.partial(widen_kernel, count, len(widths)),
        grid_spec=pltpu.PrefetchScalarGridSpec(
            num_scalar_prefetch=1,
            grid=(count,),
            in_specs=[full(chunk.shape) for chunk in chunks]
            + [pl.BlockSpec(memory_space=pl.ANY)] * (len(into) + len(others)),
            out_specs=[pl.BlockSpec((rows, wide), lambda i, at: (at[i], 0)) for wide in widths],
        ),
        out_shape=[jax.ShapeDtypeStruct((total, wide), F32) for wide in widths],
        input_output_aliases={1 + count + k: k for k in range(len(into))},
        compiler_params=params(),
        cost_estimate=cost(rows * columns, 6 * count * rows * columns),
    )(jnp.stack(places).astype(jnp.int32), *chunks, *into, *others)


def swap_dp(rows):
    return lax.ppermute(rows, "dp", [(0, 1), (1, 0)])


def swap_context(rows, s):
    n = lax.axis_size("context")
    return lax.ppermute(rows, "context", [(i, i ^ s) for i in range(n)])


def share_context(parts):
    return lax.all_to_all(parts, "context", split_axis=0, concat_axis=0, tiled=True)


def plane_turns():
    d, c = lax.axis_index("dp"), lax.axis_index("context")
    low, high = lax.rem(c, 2), lax.div(c, 2)

    def swap(first, second):
        perm = [(i, i ^ first) for i in range(4)] + [(4 + i, 4 + (i ^ second)) for i in range(4)]
        return lambda rows: lax.ppermute(rows, GROUP_AXES, perm)

    return [
        (jnp.where(d == 0, low, high), swap(1, 2)),
        (jnp.where(d == 0, high, low), swap(2, 1)),
    ]


def plane_first(pairs, others):
    (bit_1, _), _ = plane_turns()
    return fold(pairs, bit_1, others)


def plane_second(send, keep, others):
    (_, swap_1), (bit_2, _) = plane_turns()
    return fold([(keep, swap_1(send))], bit_2, others)


def plane_last(send, keep, others):
    _, (_, swap_2) = plane_turns()
    return pair_sum(keep, swap_2(send), others)


def plane_spread(own):
    (_, swap_1), (_, swap_2) = plane_turns()
    second = swap_2(own)
    return [own, second, swap_1(own), swap_1(second)]


def quarter_places(rank):
    d = lax.axis_index("dp")
    c = lax.axis_index("context")
    low, high = lax.rem(c, 2), lax.div(c, 2)
    places = []
    for core in (d, 1 - d):
        bit_1 = jnp.where(core == 0, low, high)
        bit_2 = jnp.where(core == 0, high, low)
        for flip_1, flip_2 in ((0, 0), (0, 1), (1, 0), (1, 1)):
            places.append(4 * core + rank(core, bit_1 ^ flip_1, bit_2 ^ flip_2))
    return places


def widen_all(quarters, places, widths, others):
    count = len(quarters)
    total = 2 * count * quarters[0].shape[0]
    swapped = [swap_dp(part) for part in quarters]
    here = widen(places[:count], quarters, widths, total, [], [])
    return widen(places[count:], swapped, widths, total, here, others)


def arrival_order(n):
    return [sorted(range(n), key=lambda j: (abs(j - i), j)) for i in range(n)]


def choose(index, options):
    distinct = []
    for option in options:
        if option is not None and not any(option is other for other in distinct):
            distinct.append(option)
    result = distinct[0]
    for option in distinct[1:]:
        mask = functools.reduce(
            jnp.logical_or, [index == i for i, other in enumerate(options) if other is option]
        )
        result = jnp.where(mask, option, result)
    return result


def line_gather(chunk):
    return line_steps({0: chunk}, 1, lax.axis_size("expert"))


def line_steps(found, first, stop):
    n = lax.axis_size("expert")
    found = dict(found)
    for s in range(first, stop):
        found[-s] = lax.ppermute(
            found[1 - s], "expert", [(i, i + 1) for i in range(s - 1, n - 1)]
        )
        found[s] = lax.ppermute(found[s - 1], "expert", [(i + 1, i) for i in range(n - s)])
    return found


def context_gather(rows):
    n = lax.axis_size("context")
    c = lax.axis_index("context")
    found = {0: rows}
    for s in range(1, n):
        found[s] = lax.ppermute(rows, "context", [(i, i ^ s) for i in range(n)])
    return jnp.concatenate([choose(c, [found[i ^ j] for i in range(n)]) for j in range(n)], axis=0)


def zero_of(*others):
    return functools.reduce(
        jnp.add,
        [
            lax.slice(other, (0,) * other.ndim, (1,) * other.ndim).reshape(()).astype(F32) * 0.0
            for other in others
        ],
    )


def after(value, *others):
    return (value.astype(F32) + zero_of(*others)).astype(value.dtype)


def on_device(
    layer_input,
    grad_output,
    attn_gain,
    query_weight,
    key_weight,
    value_weight,
    q_gain,
    k_gain,
    output_weight,
    mlp_gain,
    router,
    w_gate,
    w_up,
    w_down,
    routes,
    half_order,
):
    n_context = lax.axis_size("context")
    n_expert = lax.axis_size("expert")
    n_groups = lax.axis_size(GROUP_AXES)
    tok_dev, width = layer_input.shape[1:]
    size = q_gain.shape[0]
    kv_total = key_weight.shape[1] * n_expert
    group_dev = n_expert // (kv_total // size)
    kv_index = lax.axis_index("expert") // group_dev
    block = tok_dev * n_expert
    seq = block * n_context
    half = block // 2
    experts = router.shape[1]
    exp_dev = w_gate.shape[0]
    top = routes.shape[2]
    capacity = max(2, (tok_dev * top * 9 + 8 * experts - 1) // (8 * experts))
    scale = size ** (-0.5)

    seq_rows = jnp.arange(seq, dtype=jnp.int32)
    context = lax.axis_index("context")
    own_halves = lax.dynamic_slice_in_dim(half_order, 2 * context, 2)
    own_pos = (own_halves[:, None] * half + jnp.arange(half, dtype=jnp.int32)[None]).reshape(-1)
    per_half = half // TILE
    tile_pos = (half_order[:, None] * per_half + jnp.arange(per_half, dtype=jnp.int32)).reshape(-1)
    kidx = jnp.sum(
        (tile_pos[None, :] == jnp.arange(seq // TILE, dtype=jnp.int32)[:, None])
        * jnp.arange(seq // TILE, dtype=jnp.int32)[None, :],
        axis=1,
    ).astype(jnp.int32)
    qpos = lax.dynamic_slice_in_dim(tile_pos, context * (block // TILE), block // TILE)
    entry = jnp.arange(size)
    freq = jnp.power(THETA, -(2 * (entry % (size // 2))).astype(F32) / size)
    angles = own_pos.astype(F32)[:, None] * freq[None, :]
    cos2 = jnp.cos(angles)
    sin2 = jnp.sin(angles) * jnp.where(entry < size // 2, -1.0, 1.0)[None, :]

    place = lax.axis_index("expert")
    place_1 = place.astype(jnp.int32)[None]
    lanes = -(-2 * experts // 128) * 128
    mask = jnp.any(
        routes[0][:, :, None] == jnp.arange(lanes, dtype=jnp.int32)[None, None, :], axis=1
    )
    mask_wide = mask.astype(F32)
    router_rows = router.T

    x_low = layer_input[0]
    x_normal, _ = norm_parts(x_low.astype(F32))
    normed_found = line_gather((x_normal * attn_gain).astype(LOW))
    if group_dev == 1:
        kv_weights = jnp.concatenate([key_weight, value_weight], axis=1)
    else:
        key_whole = lax.all_gather(key_weight, "expert", axis=1, tiled=True)
        value_whole = lax.all_gather(value_weight, "expert", axis=1, tiled=True)
        kv_weights = jnp.concatenate(
            [
                lax.dynamic_slice_in_dim(key_whole, kv_index * size, size, 1),
                lax.dynamic_slice_in_dim(value_whole, kv_index * size, size, 1),
            ],
            axis=1,
        )
    grad_low = grad_output[0]
    normed_rows, own_kv, key_proj, grad_wide = project_keys(
        place_1,
        normed_found,
        kv_weights,
        k_gain,
        cos2,
        sin2,
        scale * LOG2E,
        grad_low,
        mask_wide,
    )
    grad_col = lax.all_gather(grad_wide, "expert", axis=0, tiled=True)
    kv_whole = context_gather(own_kv)
    queries, query_proj = project_queries(normed_rows, query_weight, q_gain, cos2, sin2)

    n_half = n_expert // 2
    order_here = jnp.asarray(arrival_order(n_expert), jnp.int32)[place]
    turn_here = jnp.sum(
        (order_here[:, None] == jnp.arange(n_expert, dtype=jnp.int32)[None, :])
        * jnp.arange(n_expert, dtype=jnp.int32)[:, None],
        axis=0,
    ).astype(jnp.int32)
    meta = jnp.concatenate([place_1, turn_here, order_here])
    grad_sent, slots = make_slots(meta, grad_col, width, n_groups, capacity)
    spreads, back_tables = make_tables(meta, slots, n_half, capacity)

    def swap_plane(rows):
        parts = rows.reshape(n_groups, -1, rows.shape[1])
        parts = lax.all_to_all(parts, GROUP_AXES, split_axis=0, concat_axis=0, tiled=True)
        return parts.reshape(rows.shape)

    attended, inverse = attend(qpos, kidx, queries, kv_whole, [])
    keys_t = kv_whole[:, :size].T
    attn_part = out_dot(attended, output_weight, [grad_col])
    attn_rows = lax.psum_scatter(attn_part, "expert", scatter_dimension=0, tiled=True)

    grad_x = swap_plane(grad_sent)
    act_pull = dot_nt(grad_x, w_down[0]).reshape(n_groups, 2, n_half * capacity, -1)

    hidden, mixed, probs = route_rows(
        x_low, attn_rows, mlp_gain, router_rows, mask_wide, experts, [keys_t]
    )

    who = (lax.axis_index(ALL_AXES) * exp_dev).astype(jnp.int32)[None]
    mixed_found = line_gather(mixed)
    near = spread_rows(place_1, spreads[0], mixed_found, range(n_half), [grad_x])
    x_near = swap_plane(near)
    worked_near = run_expert(who, x_near, w_gate[0], w_up[0], act_pull, 0, experts)
    far = spread_rows(place_1, spreads[1], mixed_found, range(n_half, n_expert), [x_near])
    x_far = swap_plane(far)
    worked_far = run_expert(who, x_far, w_gate[0], w_up[0], act_pull, 1, experts)
    xs = [x_near, x_far]
    acts, gate_lows, up_lows, copies = (list(pair) for pair in zip(worked_near, worked_far))
    back_far = swap_plane(copies[1])
    back_near = swap_plane(copies[0])
    join = lambda parts: jnp.concatenate(parts, axis=0)
    x_all = join([x[:, :width] for x in xs])
    grad_w_gate = dot_tn(x_all, join(gate_lows))
    grad_w_up = dot_tn(x_all, join(up_lows))
    grad_by_round = jnp.swapaxes(
        grad_x.reshape(n_groups, 2, n_half * capacity, width), 0, 1
    ).reshape(-1, width)
    grad_w_down = dot_tn(join(acts), grad_by_round)
    copies_col = combine_rows(
        meta, back_tables, [back_near, back_far], n_half, [grad_w_gate, grad_w_up]
    )
    copies_sum = lax.psum_scatter(copies_col, "expert", scatter_dimension=0, tiled=True)

    returned = [dot_nn(act, w_down[0]).astype(LOW) for act in acts]
    returned_near = swap_plane(returned[0])

    grad_hidden, grad_hidden_low, grad_mlp_gain, grad_router = route_back(
        copies_sum,
        grad_low,
        hidden,
        mlp_gain,
        router_rows,
        mask_wide,
        probs,
        experts,
        [returned_near, grad_w_down],
    )

    returned_far = swap_plane(returned[1])
    grad_attn = lax.all_gather(grad_hidden_low, "expert", axis=0, tiled=True)
    grad_o, centre = grad_attended(
        grad_attn, output_weight, attended, inverse, [returned_far]
    )
    combined = combine_rows(meta, back_tables, [returned_near, returned_far], n_half, [])
    output_rows = lax.psum_scatter(combined, "expert", scatter_dimension=0, tiled=True)
    w_out_send, w_out_keep = token_halves(attended, grad_attn, [combined])
    w_out_half = pair_sum(w_out_keep, swap_dp(w_out_send), [grad_o])
    w_out_parts = share_context(w_out_half.reshape(n_context, -1, width))
    grad_kv, grad_q, grad_q_gain = attend_back(
        qpos,
        kidx,
        queries,
        grad_o,
        centre,
        kv_whole,
        keys_t,
        query_proj,
        q_gain,
        cos2,
        sin2,
        [w_out_half],
    )
    kv_parts = share_context(grad_kv.astype(LOW).reshape(n_context, block, 2 * size))
    w_out_own = part_sum(w_out_parts, [grad_kv])
    w_query_send, w_query_keep = token_halves(normed_rows, grad_q, [w_out_own])
    w_query_got = swap_dp(w_query_send)
    output_rows = hidden + output_rows.astype(F32) + zero_of(w_query_keep)

    kv_grads, grad_k_gain = kv_back(
        kv_parts, key_proj, k_gain, cos2, sin2, scale, [w_query_keep]
    )
    w_out_quarters = plane_spread(w_out_own)
    pairs = [(w_query_keep, w_query_got)]
    widths = [query_weight.shape[1]]
    if group_dev == 1:
        w_kv_send, w_kv_keep = token_halves(normed_rows, kv_grads, w_out_quarters[1:3])
        pairs.append((w_kv_keep, swap_dp(w_kv_send)))
        widths += [key_weight.shape[1], value_weight.shape[1]]
    grad_normed, gain_rows = normed_back(
        grad_q, kv_grads, query_weight, kv_weights, normed_rows, []
    )
    send, keep = plane_first(pairs, [*w_out_quarters, grad_normed])
    (grad_w_out,) = widen_all(
        w_out_quarters,
        quarter_places(lambda core, b1, b2: jnp.where(core == 0, b1 + 2 * b2, 2 * b1 + b2)),
        [width],
        [],
    )
    small = pack_small(
        experts,
        grad_router,
        gain_rows,
        attn_gain,
        grad_mlp_gain,
        grad_q_gain,
        grad_k_gain,
        [],
    )
    swap_all = lambda rows: lax.all_to_all(rows, ALL_AXES, split_axis=0, concat_axis=0, tiled=True)
    small_parts = swap_all(small.reshape(lax.axis_size(ALL_AXES), -1, width))
    small_own = jnp.sum(small_parts.astype(F32), axis=0).astype(LOW)
    second_send, second_keep = plane_second(send, keep, [small])
    quarter = plane_last(second_send, second_keep, [output_rows, small_own])
    grad_normed = lax.psum_scatter(grad_normed, "expert", scatter_dimension=0, tiled=True)
    grad_input = input_back(grad_normed, x_low, attn_gain, grad_hidden)
    small_sum = swap_all(jnp.broadcast_to(small_own[None], small_parts.shape))
    small_sum = small_sum.reshape(small.shape).astype(F32) + zero_of(grad_w_out, grad_input)
    quarters = [quarter] + [swap_context(quarter, s) for s in range(1, n_context)]
    d = lax.axis_index("dp")
    turned = lambda core, c: jnp.where(core == 0, 2 * lax.rem(c, 2) + lax.div(c, 2), c)
    places = [4 * core + turned(core, context ^ s) for core in (d, 1 - d) for s in range(n_context)]
    grad_w_query, *more = widen_all(quarters, places, widths, [small_sum])
    if group_dev == 1:
        grad_w_key, grad_w_value = more
    else:
        w_kv = token_dot(normed_rows, kv_grads, [])
        blank = jnp.zeros((width, kv_total), LOW)
        pieces = []
        for part in (w_kv[:, :size], w_kv[:, size:]):
            padded = lax.dynamic_update_slice(blank, part, (0, kv_index * size))
            pieces.append(lax.psum_scatter(padded, "expert", scatter_dimension=1, tiled=True))
        grad_w_key, grad_w_value = (lax.psum(piece, GROUP_AXES).astype(F32) for piece in pieces)
    grad_attn_gain, grad_mlp_gain = small_sum[experts], small_sum[experts + 1]
    grad_q_gain = small_sum[experts + 2, :size]
    grad_k_gain = small_sum[experts + 2, size : 2 * size]
    return (
        output_rows.astype(LOW)[None],
        grad_input[None],
        grad_attn_gain,
        grad_w_query,
        grad_w_key,
        grad_w_value,
        grad_q_gain,
        grad_k_gain,
        grad_w_out,
        grad_mlp_gain,
        small_sum[:experts].T,
        grad_w_gate[None],
        grad_w_up[None],
        grad_w_down[None],
    )


def solution(mesh):
    rows = P("dp", ("context", "expert"), None)
    expert = P(ALL_AXES, None, None)
    columns = P(None, "expert")
    in_specs = (
        rows,
        rows,
        P(),
        columns,
        columns,
        columns,
        P(),
        P(),
        P("expert", None),
        P(),
        P(),
        expert,
        expert,
        expert,
        rows,
        P(),
    )
    out_specs = (
        rows,
        rows,
        P(),
        columns,
        columns,
        columns,
        P(),
        P(),
        P("expert", None),
        P(),
        P(),
        expert,
        expert,
        expert,
    )
    return jax.shard_map(
        on_device, mesh=mesh, in_specs=in_specs, out_specs=out_specs, check_vma=False
    )
```

```python
import functools
import math

import jax
import jax.numpy as jnp
from jax import lax
from jax.experimental import pallas as pl
from jax.experimental.pallas import tpu as pltpu
from jax.sharding import PartitionSpec as P

EPS = 1e-06
THETA = 1000000.0
TILE = 256
PIECE = 128
VMEM_BYTES = 56 * 1024 * 1024
LOG2E = math.log2(math.e)
LOW = jnp.bfloat16
F32 = jnp.float32
ALL_AXES = ("dp", "context", "expert")
GROUP_AXES = ("dp", "context")


def dot_nn(a, b):
    return lax.dot_general(a, b, (((1,), (0,)), ((), ())), preferred_element_type=F32)


def dot_nt(a, b):
    return lax.dot_general(a, b, (((1,), (1,)), ((), ())), preferred_element_type=F32)


def dot_tn(a, b):
    return lax.dot_general(a, b, (((0,), (0,)), ((), ())), preferred_element_type=F32)


def params(**more):
    return pltpu.CompilerParams(vmem_limit_bytes=VMEM_BYTES, **more)


def cost(flops, nbytes, exps=0):
    return pl.CostEstimate(flops=int(flops), bytes_accessed=int(nbytes), transcendentals=int(exps))


def head_forward(u, gain, cos2, sin2):
    rr = lax.rsqrt(jnp.mean(u * u, axis=-1, keepdims=True) + EPS)
    y = u * rr * gain
    return y * cos2 + pltpu.roll(y, 64, 1) * sin2


def head_backward(gy, u, gain, cos2, sin2):
    g = gy * cos2 - pltpu.roll(gy, 64, 1) * sin2
    rr = lax.rsqrt(jnp.mean(u * u, axis=-1, keepdims=True) + EPS)
    n = u * rr
    gn = g * gain
    grad = rr * (gn - n * jnp.mean(gn * n, axis=-1, keepdims=True))
    return grad, jnp.sum(g * n, axis=0, keepdims=True)


def query_kernel(x_ref, w_ref, gain_ref, cos_ref, sin_ref, rot_ref, turned_ref, proj_ref):
    tiles, heads, rows, size = rot_ref.shape
    acc = dot_nn(x_ref[...], w_ref[...])
    for h in range(heads):
        u = acc[:, h * size : (h + 1) * size]
        rot = head_forward(u, gain_ref[...], cos_ref[...], sin_ref[...])
        proj_ref[:, h] = u.reshape(tiles, rows, size)
        rot_ref[:, h] = rot.astype(LOW).reshape(tiles, rows, size)
        for t in range(tiles):
            turned_ref[t, h] = jnp.transpose(rot[t * rows : (t + 1) * rows]).astype(LOW)


def project_queries(normed, weight, gain, cos2, sin2):
    block, width = normed.shape
    size = cos2.shape[1]
    heads = weight.shape[1] // size
    tiles = block // TILE
    whole = lambda i: (0, 0)
    per = lambda i: (0, i, 0, 0)
    shape = (tiles, heads, TILE, size)
    return pl.pallas_call(
        query_kernel,
        grid=(heads // 2,),
        in_specs=[
            pl.BlockSpec((block, width), whole),
            pl.BlockSpec((width, 2 * size), lambda i: (0, i)),
            pl.BlockSpec((1, size), whole),
            pl.BlockSpec((block, size), whole),
            pl.BlockSpec((block, size), whole),
        ],
        out_specs=[
            pl.BlockSpec((tiles, 2, TILE, size), per),
            pl.BlockSpec((tiles, 2, size, TILE), per),
            pl.BlockSpec((tiles, 2, TILE, size), per),
        ],
        out_shape=[
            jax.ShapeDtypeStruct(shape, LOW),
            jax.ShapeDtypeStruct((tiles, heads, size, TILE), LOW),
            jax.ShapeDtypeStruct(shape, F32),
        ],
        compiler_params=params(),
        cost_estimate=cost(2 * block * width * heads * size, 12e6),
    )(normed, weight, gain[None], cos2, sin2)


def put_in_order(place, refs, out_ref):
    n = (len(refs) + 1) // 2
    rows = refs[0].shape[0]
    for distance in range(1 - n, n):
        ref = refs[distance + n - 1]
        at = place + distance

        @pl.when(jnp.logical_and(at >= 0, at < n))
        def _():
            out_ref[pl.ds(pl.multiple_of(at * rows, rows), rows), :] = ref[...]


def chunk_list(found):
    n = (len(found) + 1) // 2
    return [found[distance] for distance in range(1 - n, n)]


def key_kernel(factor, n_chunks, place_ref, *refs):
    w_ref, gain_ref, cos_ref, sin_ref, g_ref, mask_ref = refs[n_chunks:-4]
    rows_ref, kv_ref, proj_ref, wide_ref = refs[-4:]
    size = proj_ref.shape[1]
    width = g_ref.shape[1]
    put_in_order(place_ref[0], refs[:n_chunks], rows_ref)
    wide_ref[:, :width] = g_ref[...]
    wide_ref[:, width:] = mask_ref[...].astype(LOW)
    acc = dot_nn(rows_ref[...], w_ref[...])
    u = acc[:, :size]
    rot = head_forward(u, gain_ref[...], cos_ref[...], sin_ref[...])
    proj_ref[...] = u
    kv_ref[:, :size] = (rot * factor).astype(LOW)
    kv_ref[:, size:] = acc[:, size:].astype(LOW)


def full(shape):
    return pl.BlockSpec(shape, lambda *_: (0,) * len(shape))


def project_keys(place, found, weight, gain, cos2, sin2, factor, g, mask):
    chunks = chunk_list(found)
    rows, width = chunks[0].shape
    block, size = cos2.shape
    operands = [*chunks, weight, gain[None], cos2, sin2, g, mask]
    shapes = [
        jax.ShapeDtypeStruct((block, width), LOW),
        jax.ShapeDtypeStruct((block, 2 * size), LOW),
        jax.ShapeDtypeStruct((block, size), F32),
        jax.ShapeDtypeStruct((rows, width + mask.shape[1]), LOW),
    ]
    return pl.pallas_call(
        functools.partial(key_kernel, factor, len(chunks)),
        grid_spec=pltpu.PrefetchScalarGridSpec(
            num_scalar_prefetch=1,
            grid=(1,),
            in_specs=[full(x.shape) for x in operands],
            out_specs=[full(x.shape) for x in shapes],
        ),
        out_shape=shapes,
        compiler_params=params(),
        cost_estimate=cost(4 * block * width * size, 8e6),
    )(place, *operands)


def in_order(last, step):
    lax.fori_loop(0, lax.div(last, 2), lambda p, c: (step([2 * p, 2 * p + 1], False), c)[1], 0)

    @pl.when(lax.rem(last, 2) == 1)
    def _():
        step([last - 1, last], True)

    @pl.when(lax.rem(last, 2) == 0)
    def _():
        step([last], True)


def attend_kernel(qpos_ref, kidx_ref, q_ref, kv_ref, kt_ref, *rest):
    out_ref, inv_ref, acc_ref = rest[-3:]
    heads, rows, size = q_ref.shape[1:]
    acc_ref[...] = jnp.zeros_like(acc_ref)

    def step(places, masked):
        starts = [pl.multiple_of(kidx_ref[place] * rows, rows) for place in places]
        count = len(places) * rows
        keys_t = jnp.concatenate([kt_ref[:, pl.ds(start, rows)] for start in starts], axis=1)
        values = jnp.concatenate([kv_ref[pl.ds(start, rows), size:] for start in starts], axis=0)
        values = jnp.concatenate([values, jnp.ones((count, size), LOW)], axis=1)
        for h in range(heads):
            for first in range(0, rows, PIECE):
                part = slice(first, first + PIECE)
                e = jnp.exp2(dot_nn(q_ref[0, h, part], keys_t))
                if masked:
                    qi = lax.broadcasted_iota(jnp.int32, e.shape, 0) + first
                    ki = lax.broadcasted_iota(jnp.int32, e.shape, 1) - (count - rows)
                    e = jnp.where(ki <= qi, e, 0.0)
                acc_ref[h, part] += dot_nn(e.astype(LOW), values)

    in_order(qpos_ref[pl.program_id(0)], step)
    for h in range(heads):
        inv = 1.0 / acc_ref[h, :, size:]
        inv_ref[0, h] = inv
        out_ref[:, h * size : (h + 1) * size] = (acc_ref[h, :, :size] * inv).astype(LOW)


def attend(qpos, kidx, queries, kv, keys_t, others):
    tiles, heads, rows, size = queries.shape
    seq = kv.shape[0]
    return pl.pallas_call(
        attend_kernel,
        grid_spec=pltpu.PrefetchScalarGridSpec(
            num_scalar_prefetch=2,
            grid=(tiles,),
            in_specs=[
                pl.BlockSpec((1, heads, rows, size), lambda i, a, b: (i, 0, 0, 0)),
                pl.BlockSpec((seq, 2 * size), lambda i, a, b: (0, 0)),
                pl.BlockSpec((size, seq), lambda i, a, b: (0, 0)),
            ]
            + [pl.BlockSpec(memory_space=pl.ANY)] * len(others),
            out_specs=[
                pl.BlockSpec((rows, heads * size), lambda i, a, b: (i, 0)),
                pl.BlockSpec((1, heads, rows, size), lambda i, a, b: (i, 0, 0, 0)),
            ],
            scratch_shapes=[pltpu.VMEM((heads, rows, 2 * size), F32)],
        ),
        out_shape=[
            jax.ShapeDtypeStruct((tiles * rows, heads * size), LOW),
            jax.ShapeDtypeStruct((tiles, heads, rows, size), F32),
        ],
        compiler_params=params(),
        cost_estimate=cost(
            6 * tiles * rows * heads * seq * size, 8e6, tiles * rows * heads * seq
        ),
    )(qpos, kidx, queries, kv, keys_t, *others)


def grad_out_kernel(rows_ref, w_ref, o_ref, inv_ref, *rest):
    do_ref, turned_ref, centre_ref = rest[-3:]
    tiles, heads, rows, size = do_ref.shape
    acc = dot_nt(rows_ref[...], w_ref[...])
    for t in range(tiles):
        for h in range(heads):
            part = slice(t * rows, (t + 1) * rows), slice(h * size, (h + 1) * size)
            scaled = acc[part] * inv_ref[t, h]
            low = scaled.astype(LOW)
            do_ref[t, h] = low
            turned_ref[t, h] = jnp.transpose(scaled).astype(LOW)
            product = low.astype(F32) * o_ref[part].astype(F32)
            centre = jnp.sum(jnp.transpose(product), axis=0, keepdims=True)
            centre_ref[t, h] = jnp.broadcast_to(centre, (8, rows))


def grad_attended(grad_rows, weight, attended, inverse, others):
    tiles, heads, rows, size = inverse.shape
    block, width = grad_rows.shape
    return pl.pallas_call(
        grad_out_kernel,
        grid=(heads // 2,),
        in_specs=[
            pl.BlockSpec((block, width), lambda i: (0, 0)),
            pl.BlockSpec((2 * size, width), lambda i: (i, 0)),
            pl.BlockSpec((block, 2 * size), lambda i: (0, i)),
            pl.BlockSpec((tiles, 2, rows, size), lambda i: (0, i, 0, 0)),
        ]
        + [pl.BlockSpec(memory_space=pl.ANY)] * len(others),
        out_specs=[
            pl.BlockSpec((tiles, 2, rows, size), lambda i: (0, i, 0, 0)),
            pl.BlockSpec((tiles, 2, size, rows), lambda i: (0, i, 0, 0)),
            pl.BlockSpec((tiles, 2, 8, rows), lambda i: (0, i, 0, 0)),
        ],
        out_shape=[
            jax.ShapeDtypeStruct((tiles, heads, rows, size), LOW),
            jax.ShapeDtypeStruct((tiles, heads, size, rows), LOW),
            jax.ShapeDtypeStruct((tiles, heads, 8, rows), F32),
        ],
        compiler_params=params(),
        cost_estimate=cost(2 * block * width * heads * size, 12e6),
    )(grad_rows, weight, attended, inverse, *others)


def attend_back_kernel(
    qpos_ref,
    kidx_ref,
    q_ref,
    qt_ref,
    do_ref,
    dot_ref,
    centre_ref,
    kv_ref,
    kt_ref,
    proj_ref,
    gain_ref,
    cos_ref,
    sin_ref,
    *rest,
):
    dkv_ref, dq_ref, dgain_ref, acc_ref, e_ref, ds_ref = rest[-6:]
    heads, rows, size = q_ref.shape[1:]

    @pl.when(pl.program_id(0) == 0)
    def _():
        dkv_ref[...] = jnp.zeros_like(dkv_ref)
        dgain_ref[...] = jnp.zeros_like(dgain_ref)

    acc_ref[...] = jnp.zeros_like(acc_ref)

    def step(places, masked):
        starts = [pl.multiple_of(kidx_ref[place] * rows, rows) for place in places]
        count = len(places) * rows
        keys = jnp.concatenate([kv_ref[pl.ds(start, rows), :size] for start in starts], axis=0)
        values = jnp.concatenate([kv_ref[pl.ds(start, rows), size:] for start in starts], axis=0)
        keys_t = jnp.concatenate([kt_ref[:, pl.ds(start, rows)] for start in starts], axis=1)
        for h in range(heads):
            query_t, grad_t = qt_ref[0, h], dot_ref[0, h]
            centre = centre_ref[0, h, 0:1]
            columns = slice(h * rows, (h + 1) * rows)
            for first in range(0, count, PIECE):
                part = slice(first, first + PIECE)
                e = jnp.exp2(dot_nn(keys[part], query_t))
                if masked and first >= count - rows:
                    ki = lax.broadcasted_iota(jnp.int32, e.shape, 0) + (first - (count - rows))
                    qi = lax.broadcasted_iota(jnp.int32, e.shape, 1)
                    e = jnp.where(ki <= qi, e, 0.0)
                ds = e * (dot_nn(values[part], grad_t) - centre)
                e_ref[part, columns] = e.astype(LOW)
                ds_ref[part, columns] = ds.astype(LOW)
            acc_ref[h] += dot_nn(keys_t, ds_ref[:count, columns])
        dk = dot_nn(ds_ref[:count], q_ref[0].reshape(heads * rows, size))
        dv = dot_nn(e_ref[:count], do_ref[0].reshape(heads * rows, size))
        for k, start in enumerate(starts):
            dkv_ref[pl.ds(start, rows), :size] += dk[k * rows : (k + 1) * rows]
            dkv_ref[pl.ds(start, rows), size:] += dv[k * rows : (k + 1) * rows]

    in_order(qpos_ref[pl.program_id(0)], step)
    total = jnp.zeros((1, size), F32)
    for h in range(heads):
        grad, gain_part = head_backward(
            jnp.transpose(acc_ref[h]) * (1.0 / LOG2E),
            proj_ref[0, h],
            gain_ref[...],
            cos_ref[...],
            sin_ref[...],
        )
        dq_ref[:, h * size : (h + 1) * size] = grad.astype(LOW)
        total += gain_part
    dgain_ref[...] += total


def attend_back(
    qpos, kidx, queries, queries_t, grads, grads_t, centre, kv, keys_t, proj, gain, cos2, sin2, others
):
    tiles, heads, rows, size = queries.shape
    seq = kv.shape[0]
    per = pl.BlockSpec((1, heads, rows, size), lambda i, a, b: (i, 0, 0, 0))
    turned = pl.BlockSpec((1, heads, size, rows), lambda i, a, b: (i, 0, 0, 0))
    flat = lambda i, a, b: (0, 0)
    rowwise = lambda i, a, b: (i, 0)
    return pl.pallas_call(
        attend_back_kernel,
        grid_spec=pltpu.PrefetchScalarGridSpec(
            num_scalar_prefetch=2,
            grid=(tiles,),
            in_specs=[
                per,
                turned,
                per,
                turned,
                pl.BlockSpec((1, heads, 8, rows), lambda i, a, b: (i, 0, 0, 0)),
                pl.BlockSpec((seq, 2 * size), flat),
                pl.BlockSpec((size, seq), flat),
                per,
                pl.BlockSpec((1, size), flat),
                pl.BlockSpec((rows, size), rowwise),
                pl.BlockSpec((rows, size), rowwise),
            ]
            + [pl.BlockSpec(memory_space=pl.ANY)] * len(others),
            out_specs=[
                pl.BlockSpec((seq, 2 * size), flat),
                pl.BlockSpec((rows, heads * size), rowwise),
                pl.BlockSpec((1, size), flat),
            ],
            scratch_shapes=[pltpu.VMEM((heads, size, rows), F32)]
            + [pltpu.VMEM((2 * rows, heads * rows), LOW)] * 2,
        ),
        out_shape=[
            jax.ShapeDtypeStruct((seq, 2 * size), F32),
            jax.ShapeDtypeStruct((tiles * rows, heads * size), LOW),
            jax.ShapeDtypeStruct((1, size), F32),
        ],
        compiler_params=params(),
        cost_estimate=cost(
            15 * tiles * rows * heads * seq * size, 12e6, tiles * rows * heads * seq
        ),
    )(
        qpos,
        kidx,
        queries,
        queries_t,
        grads,
        grads_t,
        centre,
        kv,
        keys_t,
        proj,
        gain[None],
        cos2,
        sin2,
        *others,
    )


def out_kernel(a_ref, b_ref, *rest):
    rest[-1][...] = dot_nn(a_ref[...], b_ref[...]).astype(LOW)


def out_dot(a, b, others):
    block, inner = a.shape
    columns = b.shape[1]
    tile = min(columns, 512)
    return pl.pallas_call(
        out_kernel,
        grid=(columns // tile,),
        in_specs=[
            pl.BlockSpec((block, inner), lambda i: (0, 0)),
            pl.BlockSpec((inner, tile), lambda i: (0, i)),
        ]
        + [pl.BlockSpec(memory_space=pl.ANY)] * len(others),
        out_specs=pl.BlockSpec((block, tile), lambda i: (0, i)),
        out_shape=jax.ShapeDtypeStruct((block, columns), LOW),
        compiler_params=params(),
        cost_estimate=cost(2 * block * inner * columns, 8e6),
    )(a, b, *others)


def token_kernel(a_ref, b_ref, *rest):
    rest[-1][...] = dot_tn(a_ref[...], b_ref[...]).astype(LOW)


def token_dot(a, b, others):
    block, rows = a.shape
    columns = b.shape[1]
    tile = min(rows, 512)
    return pl.pallas_call(
        token_kernel,
        grid=(rows // tile,),
        in_specs=[
            pl.BlockSpec((block, tile), lambda i: (0, i)),
            pl.BlockSpec((block, columns), lambda i: (0, 0)),
        ]
        + [pl.BlockSpec(memory_space=pl.ANY)] * len(others),
        out_specs=pl.BlockSpec((tile, columns), lambda i: (i, 0)),
        out_shape=jax.ShapeDtypeStruct((rows, columns), LOW),
        compiler_params=params(),
        cost_estimate=cost(2 * block * rows * columns, 6e6),
    )(a, b, *others)


def halves_kernel(d_ref, a_ref, b_ref, *rest):
    send_ref, keep_ref = rest[-2:]
    product = dot_tn(a_ref[...], b_ref[...]).astype(LOW)

    @pl.when(pl.program_id(0) == 0)
    def _():
        send_ref[...] = product

    @pl.when(pl.program_id(0) == 1)
    def _():
        keep_ref[...] = product


def token_halves(a, b, others):
    block, rows = a.shape
    columns = b.shape[1]
    tiles = 2 if rows % 512 == 0 else 1
    tile = rows // (2 * tiles)
    d = lax.axis_index("dp").astype(jnp.int32)[None]
    half = jax.ShapeDtypeStruct((rows // 2, columns), LOW)
    return pl.pallas_call(
        halves_kernel,
        grid_spec=pltpu.PrefetchScalarGridSpec(
            num_scalar_prefetch=1,
            grid=(2, tiles),
            in_specs=[
                pl.BlockSpec(
                    (block, tile),
                    lambda h, j, d: (0, ((1 - d[0]) * (1 - h) + d[0] * h) * tiles + j),
                ),
                pl.BlockSpec((block, columns), lambda h, j, d: (0, 0)),
            ]
            + [pl.BlockSpec(memory_space=pl.ANY)] * len(others),
            out_specs=[
                pl.BlockSpec((tile, columns), lambda h, j, d: (j * (1 - h) + (tiles - 1) * h, 0)),
                pl.BlockSpec((tile, columns), lambda h, j, d: (j * h, 0)),
            ],
        ),
        out_shape=[half, half],
        compiler_params=params(),
        cost_estimate=cost(2 * block * rows * columns, 6e6),
    )(d, a, b, *others)


def split_low(value):
    high = value.astype(LOW)
    return high, (value - high.astype(F32)).astype(LOW)


def norm_parts(rows):
    rr = lax.rsqrt(jnp.mean(rows * rows, axis=-1, keepdims=True) + EPS)
    return rows * rr, rr


def norm_back(grad, normal, rr, gain):
    weighted = grad * gain
    return rr * (weighted - normal * jnp.mean(weighted * normal, axis=-1, keepdims=True))


def add_all(refs):
    return functools.reduce(jnp.add, [ref[...].astype(F32) for ref in refs])


def pad_rows(rows, count):
    if rows.shape[0] == count:
        return rows
    return jnp.concatenate(
        [rows, jnp.zeros((count - rows.shape[0], rows.shape[1]), rows.dtype)], axis=0
    )


def router_kernel(experts, *refs):
    x_ref, attn_ref, gain_ref, router_ref, mask_ref = refs[:5]
    hidden_ref, mixed_ref, probs_ref = refs[-3:]
    width = x_ref.shape[1]
    lanes = mask_ref.shape[1]
    hidden = add_all([x_ref, attn_ref])
    hidden_ref[...] = hidden
    mixed = (norm_parts(hidden)[0] * gain_ref[...]).astype(LOW)
    mixed_ref[:, :width] = mixed
    logits = dot_nt(mixed, pad_rows(router_ref[...], lanes))
    lane = lax.broadcasted_iota(jnp.int32, logits.shape, 1)
    logits = jnp.where(lane < experts, logits, -1e30)
    weights = jnp.exp(logits - jnp.max(logits, axis=1, keepdims=True))
    probs = weights / jnp.sum(weights, axis=1, keepdims=True)
    probs_ref[...] = probs
    chosen = probs * mask_ref[...]
    high, low = split_low(chosen / jnp.sum(chosen, axis=1, keepdims=True))
    both = high.astype(F32) + pltpu.roll(low.astype(F32), experts, 1)
    mixed_ref[:, width:] = both.astype(LOW)


def route_rows(x, attn, gain, router, mask, experts, others):
    tokens, width = x.shape
    lanes = mask.shape[1]
    operands = [x, attn, gain[None], router, mask]
    shapes = [
        jax.ShapeDtypeStruct((tokens, width), F32),
        jax.ShapeDtypeStruct((tokens, width + lanes), LOW),
        jax.ShapeDtypeStruct((tokens, lanes), F32),
    ]
    return pl.pallas_call(
        functools.partial(router_kernel, experts),
        grid=(1,),
        in_specs=[full(value.shape) for value in operands]
        + [pl.BlockSpec(memory_space=pl.ANY)] * len(others),
        out_specs=[full(shape.shape) for shape in shapes],
        out_shape=shapes,
        compiler_params=params(),
        cost_estimate=cost(2 * tokens * width * lanes, 5e6),
    )(*operands, *others)


def one_hot(slots, count, first):
    groups, tokens = slots.shape
    slot = lax.broadcasted_iota(jnp.int32, (groups, count, tokens), 1).astype(F32)
    same = slots[:, None, :] == slot + float(first)
    return jnp.where(same, 1.0, 0.0).reshape(groups * count, tokens)


def slot_kernel(capacity, meta_ref, col_ref, rows_ref, slots_ref):
    groups, block = slots_ref.shape
    rows, width = rows_ref.shape
    n = rows // groups // capacity
    tokens = block // n
    mask = col_ref[:, width:]
    lanes = mask.shape[1]
    padded = -(-groups // 16) * 16
    group = lax.broadcasted_iota(jnp.int32, (padded, lanes), 0)
    lane = lax.broadcasted_iota(jnp.int32, (padded, lanes), 1)
    wanted = jnp.logical_and(lane == group * n + meta_ref[0], group < groups)
    hits = dot_nt(jnp.where(wanted, 1.0, 0.0).astype(LOW), mask)
    before = lax.broadcasted_iota(jnp.int32, (tokens, tokens), 0)
    after_it = lax.broadcasted_iota(jnp.int32, (tokens, tokens), 1)
    earlier = jnp.where(before < after_it, 1.0, 0.0).astype(LOW)
    for z in range(n):
        hit = hits[:, z * tokens : (z + 1) * tokens]
        rank = dot_nn(hit.astype(LOW), earlier)
        turn = (meta_ref[1 + z] * capacity).astype(F32)
        slot = jnp.where(hit > 0.5, rank + turn, -1.0)
        slots_ref[:, z * tokens : (z + 1) * tokens] = slot[:groups]
    spread = one_hot(slots_ref[...], n * capacity, 0).astype(LOW)
    rows_ref[...] = dot_nn(spread, col_ref[:, :width]).astype(LOW)


def make_slots(meta, col, width, groups, capacity):
    block = col.shape[0]
    n = lax.axis_size("expert")
    shapes = [
        jax.ShapeDtypeStruct((groups * n * capacity, width), LOW),
        jax.ShapeDtypeStruct((groups, block), F32),
    ]
    return pl.pallas_call(
        functools.partial(slot_kernel, capacity),
        grid_spec=pltpu.PrefetchScalarGridSpec(
            num_scalar_prefetch=1,
            grid=(1,),
            in_specs=[full(col.shape)],
            out_specs=[full(shape.shape) for shape in shapes],
        ),
        out_shape=shapes,
        compiler_params=params(),
        cost_estimate=cost(2 * groups * n * capacity * block * width, 8e6),
    )(meta, col)


def table_kernel(capacity, n_half, meta_ref, slots_ref, near_ref, far_ref, near_back_ref, far_back_ref):
    n = 2 * n_half
    tokens = slots_ref.shape[1] // n
    cap_half = n_half * capacity
    for part, (to_ref, back_ref) in enumerate([(near_ref, near_back_ref), (far_ref, far_back_ref)]):
        pieces = []
        for k in range(n_half):
            start = pl.multiple_of(meta_ref[1 + n + part * n_half + k] * tokens, tokens)
            pieces.append(slots_ref[:, pl.ds(start, tokens)])
        spread = one_hot(jnp.concatenate(pieces, axis=1), cap_half, part * cap_half)
        to_ref[...] = spread.astype(LOW)
        back_ref[...] = jnp.transpose(spread).astype(LOW)


def make_tables(meta, slots, n_half, capacity):
    groups, block = slots.shape
    rows = groups * n_half * capacity
    shapes = [jax.ShapeDtypeStruct((rows, block // 2), LOW)] * 2
    shapes += [jax.ShapeDtypeStruct((block // 2, rows), LOW)] * 2
    outs = pl.pallas_call(
        functools.partial(table_kernel, capacity, n_half),
        grid_spec=pltpu.PrefetchScalarGridSpec(
            num_scalar_prefetch=1,
            grid=(1,),
            in_specs=[full(slots.shape)],
            out_specs=[full(shape.shape) for shape in shapes],
        ),
        out_shape=shapes,
        compiler_params=params(),
        cost_estimate=cost(8 * rows * block, 3e6),
    )(meta, slots)
    return outs[:2], outs[2:]


def spread_kernel(choices, place_ref, spread_ref, *refs):
    out_ref, rows_ref = refs[-2:]
    for k, by_place in enumerate(choices):
        for which in sorted(set(by_place)):
            hit = functools.reduce(
                jnp.logical_or,
                [place_ref[0] == i for i, other in enumerate(by_place) if other == which],
            )

            @pl.when(hit)
            def _():
                tokens = refs[which].shape[0]
                rows_ref[k * tokens : (k + 1) * tokens] = refs[which][...]

    out_ref[...] = dot_nn(spread_ref[...], rows_ref[...]).astype(LOW)


def spread_rows(place, spread, found, turns, others):
    n = lax.axis_size("expert")
    order = arrival_order(n)
    distances = sorted({order[i][turn] - i for i in range(n) for turn in turns})
    choices = [[distances.index(order[i][turn] - i) for i in range(n)] for turn in turns]
    chunks = [found[distance] for distance in distances]
    tokens, wide = chunks[0].shape
    rows = spread.shape[0]
    return pl.pallas_call(
        functools.partial(spread_kernel, choices),
        grid_spec=pltpu.PrefetchScalarGridSpec(
            num_scalar_prefetch=1,
            grid=(1,),
            in_specs=[full(spread.shape)]
            + [full(chunk.shape) for chunk in chunks]
            + [pl.BlockSpec(memory_space=pl.ANY)] * len(others),
            out_specs=full((rows, wide)),
            scratch_shapes=[pltpu.VMEM((len(turns) * tokens, wide), LOW)],
        ),
        out_shape=jax.ShapeDtypeStruct((rows, wide), LOW),
        compiler_params=params(),
        cost_estimate=cost(2 * rows * len(turns) * tokens * wide, 5e6),
    )(place, spread, *chunks, *others)


def router_back_kernel(experts, *refs):
    sum_ref, g_ref, hidden_ref, gain_ref, router_ref, mask_ref, probs_ref = refs[:7]
    grad_ref, low_ref, dgain_ref, drouter_ref = refs[-4:]
    width = g_ref.shape[1]
    lanes = mask_ref.shape[1]
    total = sum_ref[...].astype(F32)
    table = total[:, width:]
    mask, probs = mask_ref[...], probs_ref[...]
    grad_gates = (table + pltpu.roll(table, lanes - experts, 1)) * mask
    chosen = probs * mask
    chosen_sum = jnp.sum(chosen, axis=1, keepdims=True)
    mean = jnp.sum(grad_gates * (chosen / chosen_sum), axis=1, keepdims=True)
    centred = mask * (grad_gates - mean) / chosen_sum
    grad_logits = probs * (centred - jnp.sum(centred * chosen, axis=1, keepdims=True))
    high, low = split_low(grad_logits)
    router = pad_rows(router_ref[...], lanes)
    grad = total[:, :width] + dot_nn(high, router) + dot_nn(low, router)
    normal, rr = norm_parts(hidden_ref[...])
    mixed = (normal * gain_ref[...]).astype(LOW)
    drouter_ref[...] = dot_tn(high, mixed) + dot_tn(low, mixed)
    dgain_ref[...] = jnp.sum(grad * normal, axis=0, keepdims=True)
    grad_hidden = g_ref[...].astype(F32) + norm_back(grad, normal, rr, gain_ref[...])
    grad_ref[...] = grad_hidden
    low_ref[...] = grad_hidden.astype(LOW)


def route_back(summed, g, hidden, gain, router, mask, probs, experts, others):
    tokens, width = g.shape
    lanes = mask.shape[1]
    operands = [summed, g, hidden, gain[None], router, mask, probs]
    shapes = [
        jax.ShapeDtypeStruct((tokens, width), F32),
        jax.ShapeDtypeStruct((tokens, width), LOW),
        jax.ShapeDtypeStruct((1, width), F32),
        jax.ShapeDtypeStruct((lanes, width), F32),
    ]
    return pl.pallas_call(
        functools.partial(router_back_kernel, experts),
        grid=(1,),
        in_specs=[full(value.shape) for value in operands]
        + [pl.BlockSpec(memory_space=pl.ANY)] * len(others),
        out_specs=[full(shape.shape) for shape in shapes],
        out_shape=shapes,
        compiler_params=params(),
        cost_estimate=cost(8 * tokens * width * lanes, 8e6),
    )(*operands, *others)


def combine_kernel(meta_ref, table_ref, rows_ref, *rest):
    del meta_ref
    rest[-1][...] = dot_nn(table_ref[...], rows_ref[...]).astype(LOW)


def combine_part(meta, table, rows, first, n, into, others):
    block, slots = table.shape
    wide = rows.shape[1]
    tokens = block // (n // 2)
    return pl.pallas_call(
        combine_kernel,
        grid_spec=pltpu.PrefetchScalarGridSpec(
            num_scalar_prefetch=1,
            grid=(n // 2,),
            in_specs=[
                pl.BlockSpec((tokens, slots), lambda i, m: (i, 0)),
                full(rows.shape),
            ]
            + [pl.BlockSpec(memory_space=pl.ANY)] * (len(into) + len(others)),
            out_specs=pl.BlockSpec((tokens, wide), lambda i, m: (m[1 + n + first + i], 0)),
        ),
        out_shape=jax.ShapeDtypeStruct((n * tokens, wide), LOW),
        input_output_aliases={3: 0} if into else {},
        compiler_params=params(),
        cost_estimate=cost(2 * slots * block * wide, 6e6),
    )(meta, table, rows, *into, *others)


def combine_rows(meta, tables, rows, n_half, others):
    near = combine_part(meta, tables[0], rows[0], 0, 2 * n_half, [], [])
    return combine_part(meta, tables[1], rows[1], n_half, 2 * n_half, [near], others)


def expert_kernel(experts, who_ref, x_ref, gate_ref, up_ref, pull_ref, *rest):
    act_ref, dgate_ref, dup_ref, copy_ref = rest[-4:]
    width = gate_ref.shape[0]
    x = x_ref[:, :width]
    table = x_ref[:, width:].astype(F32)
    lane = lax.broadcasted_iota(jnp.int32, table.shape, 1)
    mine = who_ref[0]
    gate = jnp.sum(
        jnp.where(jnp.logical_or(lane == mine, lane == mine + experts), table, 0.0),
        axis=1,
        keepdims=True,
    )
    pre_gate = dot_nn(x, gate_ref[...])
    pre_up = dot_nn(x, up_ref[...])
    pull = pull_ref[...].reshape(pre_up.shape)
    sig = 1.0 / (1.0 + jnp.exp(-pre_gate))
    silu = pre_gate * sig
    act = silu * pre_up
    act_ref[...] = (act * gate).astype(LOW)
    high, low = split_low(jnp.sum(act * pull, axis=1, keepdims=True))
    pull = pull * gate
    dup = (pull * silu).astype(LOW)
    dgate = (pull * pre_up * (sig * (1.0 + pre_gate * (1.0 - sig)))).astype(LOW)
    dgate_ref[...] = dgate
    dup_ref[...] = dup
    copy_ref[:, :width] = (dot_nt(dgate, gate_ref[...]) + dot_nt(dup, up_ref[...])).astype(LOW)
    back = jnp.where(lane == mine, high.astype(F32), 0.0)
    back = jnp.where(lane == mine + experts, low.astype(F32), back)
    copy_ref[:, width:] = back.astype(LOW)


def run_expert(who, x, w_gate, w_up, pull, part, experts):
    rows, wide = x.shape
    width, hidden = w_gate.shape
    groups, _, slots, _ = pull.shape
    each = groups // 2
    tile = each * slots
    by_rows = lambda columns: pl.BlockSpec((tile, columns), lambda i, p: (i, 0))
    return pl.pallas_call(
        functools.partial(expert_kernel, experts),
        grid_spec=pltpu.PrefetchScalarGridSpec(
            num_scalar_prefetch=1,
            grid=(2,),
            in_specs=[
                by_rows(wide),
                full(w_gate.shape),
                full(w_up.shape),
                pl.BlockSpec((each, 1, slots, hidden), lambda i, p: (i, part, 0, 0)),
            ],
            out_specs=[by_rows(hidden), by_rows(hidden), by_rows(hidden), by_rows(wide)],
        ),
        out_shape=[jax.ShapeDtypeStruct((rows, hidden), LOW)] * 3
        + [jax.ShapeDtypeStruct((rows, wide), LOW)],
        compiler_params=params(),
        cost_estimate=cost(8 * rows * width * hidden, 20e6, rows * hidden),
    )(who, x, w_gate, w_up, pull)


def input_kernel(grad_ref, x_ref, gain_ref, more_ref, out_ref):
    normal, rr = norm_parts(x_ref[...].astype(F32))
    grad = grad_ref[...].astype(F32)
    out_ref[...] = more_ref[...] + norm_back(grad, normal, rr, gain_ref[...])


def input_back(grad, x, gain, more):
    tokens, width = x.shape
    operands = [grad, x, gain[None], more]
    return pl.pallas_call(
        input_kernel,
        grid=(1,),
        in_specs=[full(value.shape) for value in operands],
        out_specs=full(more.shape),
        out_shape=jax.ShapeDtypeStruct((tokens, width), F32),
        compiler_params=params(),
        cost_estimate=cost(20 * tokens * width, 5e6),
    )(*operands)


def kv_back_kernel(factor, parts_ref, proj_ref, gain_ref, cos_ref, sin_ref, *rest):
    grad_ref, dgain_ref = rest[-2:]
    size = proj_ref.shape[1]
    total = parts_ref[0].astype(F32)
    for k in range(1, parts_ref.shape[0]):
        total += parts_ref[k].astype(F32)
    grad, dgain = head_backward(
        total[:, :size] * factor, proj_ref[...], gain_ref[...], cos_ref[...], sin_ref[...]
    )
    grad_ref[:, :size] = grad.astype(LOW)
    grad_ref[:, size:] = total[:, size:].astype(LOW)
    dgain_ref[...] = dgain


def kv_back(parts, proj, gain, cos2, sin2, factor, others):
    block, size = proj.shape
    operands = [parts, proj, gain[None], cos2, sin2]
    shapes = [
        jax.ShapeDtypeStruct((block, 2 * size), LOW),
        jax.ShapeDtypeStruct((1, size), F32),
    ]
    return pl.pallas_call(
        functools.partial(kv_back_kernel, factor),
        grid=(1,),
        in_specs=[full(value.shape) for value in operands]
        + [pl.BlockSpec(memory_space=pl.ANY)] * len(others),
        out_specs=[full(shape.shape) for shape in shapes],
        out_shape=shapes,
        compiler_params=params(),
        cost_estimate=cost(40 * block * size, 5e6),
    )(*operands, *others)


def pair_kernel(a_ref, b_ref, *rest):
    rest[-1][...] = (a_ref[...].astype(F32) + b_ref[...].astype(F32)).astype(LOW)


def pair_sum(a, b, others):
    rows, columns = a.shape
    tiles = 2 if rows % 32 == 0 else 1
    spec = pl.BlockSpec((rows // tiles, columns), lambda i: (i, 0))
    return pl.pallas_call(
        pair_kernel,
        grid=(tiles,),
        in_specs=[spec, spec] + [pl.BlockSpec(memory_space=pl.ANY)] * len(others),
        out_specs=spec,
        out_shape=jax.ShapeDtypeStruct((rows, columns), LOW),
        compiler_params=params(),
        cost_estimate=cost(rows * columns, 6 * rows * columns),
    )(a, b, *others)


def fold_kernel(n_pairs, s_ref, *refs):
    del s_ref
    send_ref, keep_ref = refs[-2:]
    totals = [
        (refs[2 * k][...].astype(F32) + refs[2 * k + 1][...].astype(F32)).astype(LOW)
        for k in range(n_pairs)
    ]
    for half, out_ref in enumerate((send_ref, keep_ref)):

        @pl.when(pl.program_id(0) == half)
        def _():
            first = 0
            for total in totals:
                last = first + total.shape[1]
                out_ref[:, first:last] = total
                first = last


def fold(pairs, bit, others):
    rows = pairs[0][1].shape[0]
    columns = sum(got.shape[1] for _, got in pairs)
    tiles = 2
    tile = rows // (2 * tiles)
    side = lambda h, m: (1 - m[0]) * (1 - h) + m[0] * h
    specs = []
    for _, got in pairs:
        wide = got.shape[1]
        specs += [pl.BlockSpec((tile, wide), lambda h, j, m: (side(h, m) * tiles + j, 0))] * 2
    shape = jax.ShapeDtypeStruct((rows // 2, columns), LOW)
    return pl.pallas_call(
        functools.partial(fold_kernel, len(pairs)),
        grid_spec=pltpu.PrefetchScalarGridSpec(
            num_scalar_prefetch=1,
            grid=(2, tiles),
            in_specs=specs + [pl.BlockSpec(memory_space=pl.ANY)] * len(others),
            out_specs=[
                pl.BlockSpec((tile, columns), lambda h, j, m: (j * (1 - h) + (tiles - 1) * h, 0)),
                pl.BlockSpec((tile, columns), lambda h, j, m: (j * h, 0)),
            ],
        ),
        out_shape=[shape, shape],
        compiler_params=params(),
        cost_estimate=cost(rows * columns, 6 * rows * columns),
    )(
        bit.astype(jnp.int32)[None],
        *[value for pair in pairs for value in pair],
        *others,
    )


def normed_kernel(q_ref, kv_ref, wq_ref, wkv_ref, rows_ref, *rest):
    out_ref, dgain_ref = rest[-2:]
    grad = dot_nt(q_ref[...], wq_ref[...]) + dot_nt(kv_ref[...], wkv_ref[...])
    out_ref[...] = grad.astype(LOW)
    dgain_ref[...] = jnp.sum(grad * rows_ref[...].astype(F32), axis=0, keepdims=True)


def normed_back(grad_q, grad_kv, w_q, w_kv, rows, others):
    block, width = rows.shape
    tile = 512
    column = lambda i: (0, i)
    return pl.pallas_call(
        normed_kernel,
        grid=(width // tile,),
        in_specs=[
            full(grad_q.shape),
            full(grad_kv.shape),
            pl.BlockSpec((tile, w_q.shape[1]), lambda i: (i, 0)),
            pl.BlockSpec((tile, w_kv.shape[1]), lambda i: (i, 0)),
            pl.BlockSpec((block, tile), column),
        ]
        + [pl.BlockSpec(memory_space=pl.ANY)] * len(others),
        out_specs=[pl.BlockSpec((block, tile), column), pl.BlockSpec((1, tile), column)],
        out_shape=[
            jax.ShapeDtypeStruct((block, width), LOW),
            jax.ShapeDtypeStruct((1, width), F32),
        ],
        compiler_params=params(),
        cost_estimate=cost(2 * block * width * (w_q.shape[1] + w_kv.shape[1]), 12e6),
    )(grad_q, grad_kv, w_q, w_kv, rows, *others)


def pack_kernel(experts, router_ref, attn_ref, gain_ref, mlp_ref, q_ref, k_ref, *rest):
    out_ref, rows_ref = rest[-2:]
    size = q_ref.shape[1]
    rows_ref[:experts] = router_ref[:experts]
    rows_ref[experts:] = jnp.zeros_like(rows_ref[experts:])
    rows_ref[experts : experts + 1] = attn_ref[...] / gain_ref[...]
    rows_ref[experts + 1 : experts + 2] = mlp_ref[...]
    rows_ref[experts + 2 : experts + 3, :size] = q_ref[...]
    rows_ref[experts + 2 : experts + 3, size : 2 * size] = k_ref[...]
    out_ref[...] = rows_ref[...].astype(LOW)


def pack_small(experts, router, attn, gain, mlp, q, k, others):
    width = attn.shape[1]
    n = lax.axis_size(ALL_AXES)
    shape = (-(-(experts + 3) // n) * n, width)
    operands = [router, attn, gain[None], mlp, q, k]
    return pl.pallas_call(
        functools.partial(pack_kernel, experts),
        grid=(1,),
        in_specs=[full(value.shape) for value in operands]
        + [pl.BlockSpec(memory_space=pl.ANY)] * len(others),
        out_specs=full(shape),
        out_shape=jax.ShapeDtypeStruct(shape, LOW),
        scratch_shapes=[pltpu.VMEM(shape, F32)],
        compiler_params=params(),
        cost_estimate=cost(shape[0] * width, 6 * shape[0] * width),
    )(*operands, *others)


def part_sum_kernel(parts_ref, *rest):
    total = parts_ref[0].astype(F32)
    for k in range(1, parts_ref.shape[0]):
        total += parts_ref[k].astype(F32)
    rest[-1][...] = total.astype(LOW)


def part_sum(parts, others):
    count, rows, columns = parts.shape
    tiles = 2
    return pl.pallas_call(
        part_sum_kernel,
        grid=(tiles,),
        in_specs=[pl.BlockSpec((count, rows // tiles, columns), lambda i: (0, i, 0))]
        + [pl.BlockSpec(memory_space=pl.ANY)] * len(others),
        out_specs=pl.BlockSpec((rows // tiles, columns), lambda i: (i, 0)),
        out_shape=jax.ShapeDtypeStruct((rows, columns), LOW),
        compiler_params=params(),
        cost_estimate=cost(count * rows * columns, 4 * count * rows * columns),
    )(parts, *others)


def widen_kernel(n_chunks, n_outs, at_ref, *refs):
    del at_ref
    outs = refs[-n_outs:]
    widths = [ref.shape[1] for ref in outs]
    for k in range(n_chunks):

        @pl.when(pl.program_id(0) == k)
        def _():
            first = 0
            for wide, out_ref in zip(widths, outs):
                out_ref[...] = refs[k][:, first : first + wide].astype(F32)
                first += wide


def widen(places, chunks, widths, total, others):
    rows, columns = chunks[0].shape
    count = len(chunks)
    return pl.pallas_call(
        functools.partial(widen_kernel, count, len(widths)),
        grid_spec=pltpu.PrefetchScalarGridSpec(
            num_scalar_prefetch=1,
            grid=(count,),
            in_specs=[full(chunk.shape) for chunk in chunks]
            + [pl.BlockSpec(memory_space=pl.ANY)] * len(others),
            out_specs=[pl.BlockSpec((rows, wide), lambda i, at: (at[i], 0)) for wide in widths],
        ),
        out_shape=[jax.ShapeDtypeStruct((total, wide), F32) for wide in widths],
        compiler_params=params(),
        cost_estimate=cost(rows * columns, 6 * count * rows * columns),
    )(jnp.stack(places).astype(jnp.int32), *chunks, *others)


def swap_dp(rows):
    return lax.ppermute(rows, "dp", [(0, 1), (1, 0)])


def swap_context(rows, s):
    n = lax.axis_size("context")
    return lax.ppermute(rows, "context", [(i, i ^ s) for i in range(n)])


def share_context(parts):
    return lax.all_to_all(parts, "context", split_axis=0, concat_axis=0, tiled=True)


def plane_turns():
    d, c = lax.axis_index("dp"), lax.axis_index("context")
    low, high = lax.rem(c, 2), lax.div(c, 2)

    def swap(first, second):
        perm = [(i, i ^ first) for i in range(4)] + [(4 + i, 4 + (i ^ second)) for i in range(4)]
        return lambda rows: lax.ppermute(rows, GROUP_AXES, perm)

    return [
        (jnp.where(d == 0, low, high), swap(1, 2)),
        (jnp.where(d == 0, high, low), swap(2, 1)),
    ]


def plane_first(pairs, others):
    (bit_1, _), _ = plane_turns()
    return fold(pairs, bit_1, others)


def plane_second(send, keep, others):
    (_, swap_1), (bit_2, _) = plane_turns()
    return fold([(keep, swap_1(send))], bit_2, others)


def plane_last(send, keep, others):
    _, (_, swap_2) = plane_turns()
    return pair_sum(keep, swap_2(send), others)


def plane_spread(own):
    (_, swap_1), (_, swap_2) = plane_turns()
    second = swap_2(own)
    return [own, second, swap_1(own), swap_1(second)]


def quarter_places(rank):
    d = lax.axis_index("dp")
    c = lax.axis_index("context")
    low, high = lax.rem(c, 2), lax.div(c, 2)
    places = []
    for core in (d, 1 - d):
        bit_1 = jnp.where(core == 0, low, high)
        bit_2 = jnp.where(core == 0, high, low)
        for flip_1, flip_2 in ((0, 0), (0, 1), (1, 0), (1, 1)):
            places.append(4 * core + rank(core, bit_1 ^ flip_1, bit_2 ^ flip_2))
    return places


def widen_all(quarters, places, widths, others):
    count = len(quarters)
    total = 2 * count * quarters[0].shape[0]
    chunks = quarters + [swap_dp(part) for part in quarters]
    return widen(places, chunks, widths, total, others)


def arrival_order(n):
    return [sorted(range(n), key=lambda j: (abs(j - i), j)) for i in range(n)]


def choose(index, options):
    distinct = []
    for option in options:
        if option is not None and not any(option is other for other in distinct):
            distinct.append(option)
    result = distinct[0]
    for option in distinct[1:]:
        mask = functools.reduce(
            jnp.logical_or, [index == i for i, other in enumerate(options) if other is option]
        )
        result = jnp.where(mask, option, result)
    return result


def line_gather(chunk):
    return line_steps({0: chunk}, 1, lax.axis_size("expert"))


def line_steps(found, first, stop):
    n = lax.axis_size("expert")
    found = dict(found)
    for s in range(first, stop):
        found[-s] = lax.ppermute(
            found[1 - s], "expert", [(i, i + 1) for i in range(s - 1, n - 1)]
        )
        found[s] = lax.ppermute(found[s - 1], "expert", [(i + 1, i) for i in range(n - s)])
    return found


def context_gather(rows):
    n = lax.axis_size("context")
    c = lax.axis_index("context")
    found = {0: rows}
    for s in range(1, n):
        found[s] = lax.ppermute(rows, "context", [(i, i ^ s) for i in range(n)])
    return jnp.concatenate([choose(c, [found[i ^ j] for i in range(n)]) for j in range(n)], axis=0)


def zero_of(*others):
    return functools.reduce(
        jnp.add,
        [
            lax.slice(other, (0,) * other.ndim, (1,) * other.ndim).reshape(()).astype(F32) * 0.0
            for other in others
        ],
    )


def after(value, *others):
    return (value.astype(F32) + zero_of(*others)).astype(value.dtype)


def on_device(
    layer_input,
    grad_output,
    attn_gain,
    query_weight,
    key_weight,
    value_weight,
    q_gain,
    k_gain,
    output_weight,
    mlp_gain,
    router,
    w_gate,
    w_up,
    w_down,
    routes,
    half_order,
):
    n_context = lax.axis_size("context")
    n_expert = lax.axis_size("expert")
    n_groups = lax.axis_size(GROUP_AXES)
    tok_dev, width = layer_input.shape[1:]
    size = q_gain.shape[0]
    kv_total = key_weight.shape[1] * n_expert
    group_dev = n_expert // (kv_total // size)
    kv_index = lax.axis_index("expert") // group_dev
    block = tok_dev * n_expert
    seq = block * n_context
    half = block // 2
    experts = router.shape[1]
    exp_dev = w_gate.shape[0]
    top = routes.shape[2]
    capacity = max(2, (tok_dev * top * 9 + 8 * experts - 1) // (8 * experts))
    scale = size ** (-0.5)

    seq_rows = jnp.arange(seq, dtype=jnp.int32)
    context = lax.axis_index("context")
    own_halves = lax.dynamic_slice_in_dim(half_order, 2 * context, 2)
    own_pos = (own_halves[:, None] * half + jnp.arange(half, dtype=jnp.int32)[None]).reshape(-1)
    per_half = half // TILE
    tile_pos = (half_order[:, None] * per_half + jnp.arange(per_half, dtype=jnp.int32)).reshape(-1)
    kidx = jnp.sum(
        (tile_pos[None, :] == jnp.arange(seq // TILE, dtype=jnp.int32)[:, None])
        * jnp.arange(seq // TILE, dtype=jnp.int32)[None, :],
        axis=1,
    ).astype(jnp.int32)
    qpos = lax.dynamic_slice_in_dim(tile_pos, context * (block // TILE), block // TILE)
    entry = jnp.arange(size)
    freq = jnp.power(THETA, -(2 * (entry % (size // 2))).astype(F32) / size)
    angles = own_pos.astype(F32)[:, None] * freq[None, :]
    cos2 = jnp.cos(angles)
    sin2 = jnp.sin(angles) * jnp.where(entry < size // 2, -1.0, 1.0)[None, :]

    place = lax.axis_index("expert")
    place_1 = place.astype(jnp.int32)[None]
    lanes = -(-2 * experts // 128) * 128
    mask = jnp.any(
        routes[0][:, :, None] == jnp.arange(lanes, dtype=jnp.int32)[None, None, :], axis=1
    )
    mask_wide = mask.astype(F32)
    router_rows = router.T

    x_low = layer_input[0]
    x_normal, _ = norm_parts(x_low.astype(F32))
    normed_found = line_gather((x_normal * attn_gain).astype(LOW))
    if group_dev == 1:
        kv_weights = jnp.concatenate([key_weight, value_weight], axis=1)
    else:
        key_whole = lax.all_gather(key_weight, "expert", axis=1, tiled=True)
        value_whole = lax.all_gather(value_weight, "expert", axis=1, tiled=True)
        kv_weights = jnp.concatenate(
            [
                lax.dynamic_slice_in_dim(key_whole, kv_index * size, size, 1),
                lax.dynamic_slice_in_dim(value_whole, kv_index * size, size, 1),
            ],
            axis=1,
        )
    grad_low = grad_output[0]
    normed_rows, own_kv, key_proj, grad_wide = project_keys(
        place_1,
        normed_found,
        kv_weights,
        k_gain,
        cos2,
        sin2,
        scale * LOG2E,
        grad_low,
        mask_wide,
    )
    grad_col = lax.all_gather(grad_wide, "expert", axis=0, tiled=True)
    kv_whole = context_gather(own_kv)
    queries, queries_t, query_proj = project_queries(normed_rows, query_weight, q_gain, cos2, sin2)

    n_half = n_expert // 2
    order_here = jnp.asarray(arrival_order(n_expert), jnp.int32)[place]
    turn_here = jnp.sum(
        (order_here[:, None] == jnp.arange(n_expert, dtype=jnp.int32)[None, :])
        * jnp.arange(n_expert, dtype=jnp.int32)[:, None],
        axis=0,
    ).astype(jnp.int32)
    meta = jnp.concatenate([place_1, turn_here, order_here])
    grad_sent, slots = make_slots(meta, grad_col, width, n_groups, capacity)
    spreads, back_tables = make_tables(meta, slots, n_half, capacity)

    def swap_plane(rows):
        parts = rows.reshape(n_groups, -1, rows.shape[1])
        parts = lax.all_to_all(parts, GROUP_AXES, split_axis=0, concat_axis=0, tiled=True)
        return parts.reshape(rows.shape)

    keys_t = kv_whole[:, :size].T
    attended, inverse = attend(qpos, kidx, queries, kv_whole, keys_t, [])
    attn_part = out_dot(attended, output_weight, [grad_col])
    attn_rows = lax.psum_scatter(attn_part, "expert", scatter_dimension=0, tiled=True)

    grad_x = swap_plane(grad_sent)
    act_pull = dot_nt(grad_x, w_down[0]).reshape(n_groups, 2, n_half * capacity, -1)

    hidden, mixed, probs = route_rows(
        x_low, attn_rows, mlp_gain, router_rows, mask_wide, experts, []
    )

    who = (lax.axis_index(ALL_AXES) * exp_dev).astype(jnp.int32)[None]
    mixed_found = line_gather(mixed)
    near = spread_rows(place_1, spreads[0], mixed_found, range(n_half), [grad_x])
    x_near = swap_plane(near)
    worked_near = run_expert(who, x_near, w_gate[0], w_up[0], act_pull, 0, experts)
    far = spread_rows(place_1, spreads[1], mixed_found, range(n_half, n_expert), [x_near])
    x_far = swap_plane(far)
    worked_far = run_expert(who, x_far, w_gate[0], w_up[0], act_pull, 1, experts)
    xs = [x_near, x_far]
    acts, gate_lows, up_lows, copies = (list(pair) for pair in zip(worked_near, worked_far))
    back_far = swap_plane(copies[1])
    back_near = swap_plane(copies[0])
    join = lambda parts: jnp.concatenate(parts, axis=0)
    x_all = join([x[:, :width] for x in xs])
    grad_w_gate = dot_tn(x_all, join(gate_lows))
    grad_w_up = dot_tn(x_all, join(up_lows))
    grad_by_round = jnp.swapaxes(
        grad_x.reshape(n_groups, 2, n_half * capacity, width), 0, 1
    ).reshape(-1, width)
    grad_w_down = dot_tn(join(acts), grad_by_round)
    copies_col = combine_rows(
        meta, back_tables, [back_near, back_far], n_half, [grad_w_gate, grad_w_up]
    )
    copies_sum = lax.psum_scatter(copies_col, "expert", scatter_dimension=0, tiled=True)

    returned = [dot_nn(act, w_down[0]).astype(LOW) for act in acts]
    returned_near = swap_plane(returned[0])

    grad_hidden, grad_hidden_low, grad_mlp_gain, grad_router = route_back(
        copies_sum,
        grad_low,
        hidden,
        mlp_gain,
        router_rows,
        mask_wide,
        probs,
        experts,
        [returned_near, grad_w_down],
    )

    returned_far = swap_plane(returned[1])
    grad_attn = lax.all_gather(grad_hidden_low, "expert", axis=0, tiled=True)
    grad_o, grad_o_t, centre = grad_attended(
        grad_attn, output_weight, attended, inverse, [returned_far]
    )
    combined = combine_rows(meta, back_tables, [returned_near, returned_far], n_half, [])
    output_rows = lax.psum_scatter(combined, "expert", scatter_dimension=0, tiled=True)
    w_out_send, w_out_keep = token_halves(attended, grad_attn, [combined])
    w_out_half = pair_sum(w_out_keep, swap_dp(w_out_send), [grad_o])
    w_out_parts = share_context(w_out_half.reshape(n_context, -1, width))
    grad_kv, grad_q, grad_q_gain = attend_back(
        qpos,
        kidx,
        queries,
        queries_t,
        grad_o,
        grad_o_t,
        centre,
        kv_whole,
        keys_t,
        query_proj,
        q_gain,
        cos2,
        sin2,
        [w_out_half],
    )
    kv_parts = share_context(grad_kv.astype(LOW).reshape(n_context, block, 2 * size))
    w_out_own = part_sum(w_out_parts, [grad_kv])
    w_query_send, w_query_keep = token_halves(normed_rows, grad_q, [w_out_own])
    w_query_got = swap_dp(w_query_send)
    output_rows = hidden + output_rows.astype(F32) + zero_of(w_query_keep)

    kv_grads, grad_k_gain = kv_back(
        kv_parts, key_proj, k_gain, cos2, sin2, scale, [w_query_keep]
    )
    w_out_quarters = plane_spread(w_out_own)
    pairs = [(w_query_keep, w_query_got)]
    widths = [query_weight.shape[1]]
    if group_dev == 1:
        w_kv_send, w_kv_keep = token_halves(normed_rows, kv_grads, [])
        pairs.append((w_kv_keep, swap_dp(w_kv_send)))
        widths += [key_weight.shape[1], value_weight.shape[1]]
    grad_normed, gain_rows = normed_back(
        grad_q, kv_grads, query_weight, kv_weights, normed_rows, []
    )
    send, keep = plane_first(pairs, [grad_normed])
    (grad_w_out,) = widen_all(
        w_out_quarters,
        quarter_places(lambda core, b1, b2: jnp.where(core == 0, b1 + 2 * b2, 2 * b1 + b2)),
        [width],
        [],
    )
    small = pack_small(
        experts,
        grad_router,
        gain_rows,
        attn_gain,
        grad_mlp_gain,
        grad_q_gain,
        grad_k_gain,
        [],
    )
    swap_all = lambda rows: lax.all_to_all(rows, ALL_AXES, split_axis=0, concat_axis=0, tiled=True)
    small_parts = swap_all(small.reshape(lax.axis_size(ALL_AXES), -1, width))
    small_own = jnp.sum(small_parts.astype(F32), axis=0).astype(LOW)
    second_send, second_keep = plane_second(send, keep, [small, *w_out_quarters[1:3]])
    quarter = plane_last(second_send, second_keep, [output_rows, small_own])
    grad_normed = lax.psum_scatter(grad_normed, "expert", scatter_dimension=0, tiled=True)
    grad_input = input_back(grad_normed, x_low, attn_gain, grad_hidden)
    small_sum = swap_all(jnp.broadcast_to(small_own[None], small_parts.shape))
    small_sum = small_sum.reshape(small.shape).astype(F32) + zero_of(grad_w_out, grad_input)
    quarters = plane_spread(quarter)
    places = quarter_places(lambda core, b1, b2: 2 * b1 + b2)
    grad_w_query, *more = widen_all(quarters, places, widths, [small_sum])
    if group_dev == 1:
        grad_w_key, grad_w_value = more
    else:
        w_kv = token_dot(normed_rows, kv_grads, [])
        blank = jnp.zeros((width, kv_total), LOW)
        pieces = []
        for part in (w_kv[:, :size], w_kv[:, size:]):
            padded = lax.dynamic_update_slice(blank, part, (0, kv_index * size))
            pieces.append(lax.psum_scatter(padded, "expert", scatter_dimension=1, tiled=True))
        grad_w_key, grad_w_value = (lax.psum(piece, GROUP_AXES).astype(F32) for piece in pieces)
    grad_attn_gain, grad_mlp_gain = small_sum[experts], small_sum[experts + 1]
    grad_q_gain = small_sum[experts + 2, :size]
    grad_k_gain = small_sum[experts + 2, size : 2 * size]
    return (
        output_rows.astype(LOW)[None],
        grad_input[None],
        grad_attn_gain,
        grad_w_query,
        grad_w_key,
        grad_w_value,
        grad_q_gain,
        grad_k_gain,
        grad_w_out,
        grad_mlp_gain,
        small_sum[:experts].T,
        grad_w_gate[None],
        grad_w_up[None],
        grad_w_down[None],
    )


def solution(mesh):
    rows = P("dp", ("context", "expert"), None)
    expert = P(ALL_AXES, None, None)
    columns = P(None, "expert")
    in_specs = (
        rows,
        rows,
        P(),
        columns,
        columns,
        columns,
        P(),
        P(),
        P("expert", None),
        P(),
        P(),
        expert,
        expert,
        expert,
        rows,
        P(),
    )
    out_specs = (
        rows,
        rows,
        P(),
        columns,
        columns,
        columns,
        P(),
        P(),
        P("expert", None),
        P(),
        P(),
        expert,
        expert,
        expert,
    )
    return jax.shard_map(
        on_device, mesh=mesh, in_specs=in_specs, out_specs=out_specs, check_vma=False
    )
```

```python
import functools
import math

import jax
import jax.numpy as jnp
from jax import lax
from jax.experimental import pallas as pl
from jax.experimental.pallas import tpu as pltpu
from jax.sharding import PartitionSpec as P

EPS = 1e-06
THETA = 1000000.0
TILE = 256
PIECE = 128
VMEM_BYTES = 56 * 1024 * 1024
LOG2E = math.log2(math.e)
LOW = jnp.bfloat16
F32 = jnp.float32
ALL_AXES = ("dp", "context", "expert")
GROUP_AXES = ("dp", "context")


def dot_nn(a, b):
    return lax.dot_general(a, b, (((1,), (0,)), ((), ())), preferred_element_type=F32)


def dot_nt(a, b):
    return lax.dot_general(a, b, (((1,), (1,)), ((), ())), preferred_element_type=F32)


def dot_tn(a, b):
    return lax.dot_general(a, b, (((0,), (0,)), ((), ())), preferred_element_type=F32)


def params(**more):
    return pltpu.CompilerParams(vmem_limit_bytes=VMEM_BYTES, **more)


def cost(flops, nbytes, exps=0):
    return pl.CostEstimate(flops=int(flops), bytes_accessed=int(nbytes), transcendentals=int(exps))


def head_forward(u, gain, cos2, sin2):
    rr = lax.rsqrt(jnp.mean(u * u, axis=-1, keepdims=True) + EPS)
    y = u * rr * gain
    return y * cos2 + pltpu.roll(y, 64, 1) * sin2


def head_backward(gy, u, gain, cos2, sin2):
    g = gy * cos2 - pltpu.roll(gy, 64, 1) * sin2
    rr = lax.rsqrt(jnp.mean(u * u, axis=-1, keepdims=True) + EPS)
    n = u * rr
    gn = g * gain
    grad = rr * (gn - n * jnp.mean(gn * n, axis=-1, keepdims=True))
    return grad, jnp.sum(g * n, axis=0, keepdims=True)


def query_kernel(x_ref, w_ref, gain_ref, cos_ref, sin_ref, rot_ref, proj_ref):
    tiles, heads, rows, size = rot_ref.shape
    acc = dot_nn(x_ref[...], w_ref[...])
    for h in range(heads):
        u = acc[:, h * size : (h + 1) * size]
        rot = head_forward(u, gain_ref[...], cos_ref[...], sin_ref[...])
        proj_ref[:, h] = u.reshape(tiles, rows, size)
        rot_ref[:, h] = rot.astype(LOW).reshape(tiles, rows, size)


def project_queries(normed, weight, gain, cos2, sin2):
    block, width = normed.shape
    size = cos2.shape[1]
    heads = weight.shape[1] // size
    tiles = block // TILE
    whole = lambda i: (0, 0)
    per = lambda i: (0, i, 0, 0)
    shape = (tiles, heads, TILE, size)
    return pl.pallas_call(
        query_kernel,
        grid=(heads // 2,),
        in_specs=[
            pl.BlockSpec((block, width), whole),
            pl.BlockSpec((width, 2 * size), lambda i: (0, i)),
            pl.BlockSpec((1, size), whole),
            pl.BlockSpec((block, size), whole),
            pl.BlockSpec((block, size), whole),
        ],
        out_specs=[pl.BlockSpec((tiles, 2, TILE, size), per)] * 2,
        out_shape=[jax.ShapeDtypeStruct(shape, LOW), jax.ShapeDtypeStruct(shape, F32)],
        compiler_params=params(),
        cost_estimate=cost(2 * block * width * heads * size, 12e6),
    )(normed, weight, gain[None], cos2, sin2)


def put_in_order(place, refs, out_ref):
    n = (len(refs) + 1) // 2
    rows = refs[0].shape[0]
    for distance in range(1 - n, n):
        ref = refs[distance + n - 1]
        at = place + distance

        @pl.when(jnp.logical_and(at >= 0, at < n))
        def _():
            out_ref[pl.ds(pl.multiple_of(at * rows, rows), rows), :] = ref[...]


def chunk_list(found):
    n = (len(found) + 1) // 2
    return [found[distance] for distance in range(1 - n, n)]


def key_kernel(factor, n_chunks, place_ref, *refs):
    w_ref, gain_ref, cos_ref, sin_ref, g_ref, mask_ref = refs[n_chunks:-4]
    rows_ref, kv_ref, proj_ref, wide_ref = refs[-4:]
    size = proj_ref.shape[1]
    width = g_ref.shape[1]
    put_in_order(place_ref[0], refs[:n_chunks], rows_ref)
    wide_ref[:, :width] = g_ref[...]
    wide_ref[:, width:] = mask_ref[...].astype(LOW)
    acc = dot_nn(rows_ref[...], w_ref[...])
    u = acc[:, :size]
    rot = head_forward(u, gain_ref[...], cos_ref[...], sin_ref[...])
    proj_ref[...] = u
    kv_ref[:, :size] = (rot * factor).astype(LOW)
    kv_ref[:, size:] = acc[:, size:].astype(LOW)


def full(shape):
    return pl.BlockSpec(shape, lambda *_: (0,) * len(shape))


def project_keys(place, found, weight, gain, cos2, sin2, factor, g, mask):
    chunks = chunk_list(found)
    rows, width = chunks[0].shape
    block, size = cos2.shape
    operands = [*chunks, weight, gain[None], cos2, sin2, g, mask]
    shapes = [
        jax.ShapeDtypeStruct((block, width), LOW),
        jax.ShapeDtypeStruct((block, 2 * size), LOW),
        jax.ShapeDtypeStruct((block, size), F32),
        jax.ShapeDtypeStruct((rows, width + mask.shape[1]), LOW),
    ]
    return pl.pallas_call(
        functools.partial(key_kernel, factor, len(chunks)),
        grid_spec=pltpu.PrefetchScalarGridSpec(
            num_scalar_prefetch=1,
            grid=(1,),
            in_specs=[full(x.shape) for x in operands],
            out_specs=[full(x.shape) for x in shapes],
        ),
        out_shape=shapes,
        compiler_params=params(),
        cost_estimate=cost(4 * block * width * size, 8e6),
    )(place, *operands)


def in_order(last, step):
    lax.fori_loop(0, lax.div(last, 2), lambda p, c: (step([2 * p, 2 * p + 1], False), c)[1], 0)

    @pl.when(lax.rem(last, 2) == 1)
    def _():
        step([last - 1, last], True)

    @pl.when(lax.rem(last, 2) == 0)
    def _():
        step([last], True)


def attend_kernel(qpos_ref, kidx_ref, q_ref, kv_ref, *rest):
    out_ref, inv_ref, acc_ref = rest[-3:]
    heads, rows, size = q_ref.shape[1:]
    acc_ref[...] = jnp.zeros_like(acc_ref)

    def step(places, masked):
        starts = [pl.multiple_of(kidx_ref[place] * rows, rows) for place in places]
        count = len(places) * rows
        keys = jnp.concatenate([kv_ref[pl.ds(start, rows), :size] for start in starts], axis=0)
        values = jnp.concatenate([kv_ref[pl.ds(start, rows), size:] for start in starts], axis=0)
        values = jnp.concatenate([values, jnp.ones((count, size), LOW)], axis=1)
        for h in range(heads):
            for first in range(0, rows, PIECE):
                part = slice(first, first + PIECE)
                e = jnp.exp2(dot_nt(q_ref[0, h, part], keys))
                if masked:
                    qi = lax.broadcasted_iota(jnp.int32, e.shape, 0) + first
                    ki = lax.broadcasted_iota(jnp.int32, e.shape, 1) - (count - rows)
                    e = jnp.where(ki <= qi, e, 0.0)
                acc_ref[h, part] += dot_nn(e.astype(LOW), values)

    in_order(qpos_ref[pl.program_id(0)], step)
    for h in range(heads):
        inv = 1.0 / acc_ref[h, :, size:]
        inv_ref[0, h] = inv
        out_ref[:, h * size : (h + 1) * size] = (acc_ref[h, :, :size] * inv).astype(LOW)


def attend(qpos, kidx, queries, kv, others):
    tiles, heads, rows, size = queries.shape
    seq = kv.shape[0]
    return pl.pallas_call(
        attend_kernel,
        grid_spec=pltpu.PrefetchScalarGridSpec(
            num_scalar_prefetch=2,
            grid=(tiles,),
            in_specs=[
                pl.BlockSpec((1, heads, rows, size), lambda i, a, b: (i, 0, 0, 0)),
                pl.BlockSpec((seq, 2 * size), lambda i, a, b: (0, 0)),
            ]
            + [pl.BlockSpec(memory_space=pl.ANY)] * len(others),
            out_specs=[
                pl.BlockSpec((rows, heads * size), lambda i, a, b: (i, 0)),
                pl.BlockSpec((1, heads, rows, size), lambda i, a, b: (i, 0, 0, 0)),
            ],
            scratch_shapes=[pltpu.VMEM((heads, rows, 2 * size), F32)],
        ),
        out_shape=[
            jax.ShapeDtypeStruct((tiles * rows, heads * size), LOW),
            jax.ShapeDtypeStruct((tiles, heads, rows, size), F32),
        ],
        compiler_params=params(),
        cost_estimate=cost(
            6 * tiles * rows * heads * seq * size, 8e6, tiles * rows * heads * seq
        ),
    )(qpos, kidx, queries, kv, *others)


def grad_out_kernel(rows_ref, w_ref, o_ref, inv_ref, *rest):
    do_ref, centre_ref = rest[-2:]
    tiles, heads, rows, size = do_ref.shape
    acc = dot_nt(rows_ref[...], w_ref[...])
    for t in range(tiles):
        for h in range(heads):
            part = slice(t * rows, (t + 1) * rows), slice(h * size, (h + 1) * size)
            low = (acc[part] * inv_ref[t, h]).astype(LOW)
            do_ref[t, h] = low
            product = low.astype(F32) * o_ref[part].astype(F32)
            centre = jnp.sum(jnp.transpose(product), axis=0, keepdims=True)
            centre_ref[t, h] = jnp.broadcast_to(centre, (8, rows))


def grad_attended(grad_rows, weight, attended, inverse, others):
    tiles, heads, rows, size = inverse.shape
    block, width = grad_rows.shape
    return pl.pallas_call(
        grad_out_kernel,
        grid=(heads // 2,),
        in_specs=[
            pl.BlockSpec((block, width), lambda i: (0, 0)),
            pl.BlockSpec((2 * size, width), lambda i: (i, 0)),
            pl.BlockSpec((block, 2 * size), lambda i: (0, i)),
            pl.BlockSpec((tiles, 2, rows, size), lambda i: (0, i, 0, 0)),
        ]
        + [pl.BlockSpec(memory_space=pl.ANY)] * len(others),
        out_specs=[
            pl.BlockSpec((tiles, 2, rows, size), lambda i: (0, i, 0, 0)),
            pl.BlockSpec((tiles, 2, 8, rows), lambda i: (0, i, 0, 0)),
        ],
        out_shape=[
            jax.ShapeDtypeStruct((tiles, heads, rows, size), LOW),
            jax.ShapeDtypeStruct((tiles, heads, 8, rows), F32),
        ],
        compiler_params=params(),
        cost_estimate=cost(2 * block * width * heads * size, 12e6),
    )(grad_rows, weight, attended, inverse, *others)


def attend_back_kernel(
    qpos_ref,
    kidx_ref,
    q_ref,
    do_ref,
    centre_ref,
    kv_ref,
    kt_ref,
    proj_ref,
    gain_ref,
    cos_ref,
    sin_ref,
    *rest,
):
    dkv_ref, dq_ref, dgain_ref, acc_ref, e_ref, ds_ref = rest[-6:]
    heads, rows, size = q_ref.shape[1:]

    @pl.when(pl.program_id(0) == 0)
    def _():
        dkv_ref[...] = jnp.zeros_like(dkv_ref)
        dgain_ref[...] = jnp.zeros_like(dgain_ref)

    acc_ref[...] = jnp.zeros_like(acc_ref)

    def step(places, masked):
        starts = [pl.multiple_of(kidx_ref[place] * rows, rows) for place in places]
        count = len(places) * rows
        keys = jnp.concatenate([kv_ref[pl.ds(start, rows), :size] for start in starts], axis=0)
        values = jnp.concatenate([kv_ref[pl.ds(start, rows), size:] for start in starts], axis=0)
        keys_t = jnp.concatenate([kt_ref[:, pl.ds(start, rows)] for start in starts], axis=1)
        for h in range(heads):
            query, grad = q_ref[0, h], do_ref[0, h]
            centre = centre_ref[0, h, 0:1]
            columns = slice(h * rows, (h + 1) * rows)
            for first in range(0, count, PIECE):
                part = slice(first, first + PIECE)
                e = jnp.exp2(dot_nt(keys[part], query))
                if masked and first >= count - rows:
                    ki = lax.broadcasted_iota(jnp.int32, e.shape, 0) + (first - (count - rows))
                    qi = lax.broadcasted_iota(jnp.int32, e.shape, 1)
                    e = jnp.where(ki <= qi, e, 0.0)
                ds = e * (dot_nt(values[part], grad) - centre)
                e_ref[part, columns] = e.astype(LOW)
                ds_ref[part, columns] = ds.astype(LOW)
            acc_ref[h] += dot_nn(keys_t, ds_ref[:count, columns])
        dk = dot_nn(ds_ref[:count], q_ref[0].reshape(heads * rows, size))
        dv = dot_nn(e_ref[:count], do_ref[0].reshape(heads * rows, size))
        for k, start in enumerate(starts):
            dkv_ref[pl.ds(start, rows), :size] += dk[k * rows : (k + 1) * rows]
            dkv_ref[pl.ds(start, rows), size:] += dv[k * rows : (k + 1) * rows]

    in_order(qpos_ref[pl.program_id(0)], step)
    total = jnp.zeros((1, size), F32)
    for h in range(heads):
        grad, gain_part = head_backward(
            jnp.transpose(acc_ref[h]) * (1.0 / LOG2E),
            proj_ref[0, h],
            gain_ref[...],
            cos_ref[...],
            sin_ref[...],
        )
        dq_ref[:, h * size : (h + 1) * size] = grad.astype(LOW)
        total += gain_part
    dgain_ref[...] += total


def attend_back(qpos, kidx, queries, grads, centre, kv, keys_t, proj, gain, cos2, sin2, others):
    tiles, heads, rows, size = queries.shape
    seq = kv.shape[0]
    per = pl.BlockSpec((1, heads, rows, size), lambda i, a, b: (i, 0, 0, 0))
    flat = lambda i, a, b: (0, 0)
    rowwise = lambda i, a, b: (i, 0)
    return pl.pallas_call(
        attend_back_kernel,
        grid_spec=pltpu.PrefetchScalarGridSpec(
            num_scalar_prefetch=2,
            grid=(tiles,),
            in_specs=[
                per,
                per,
                pl.BlockSpec((1, heads, 8, rows), lambda i, a, b: (i, 0, 0, 0)),
                pl.BlockSpec((seq, 2 * size), flat),
                pl.BlockSpec((size, seq), flat),
                per,
                pl.BlockSpec((1, size), flat),
                pl.BlockSpec((rows, size), rowwise),
                pl.BlockSpec((rows, size), rowwise),
            ]
            + [pl.BlockSpec(memory_space=pl.ANY)] * len(others),
            out_specs=[
                pl.BlockSpec((seq, 2 * size), flat),
                pl.BlockSpec((rows, heads * size), rowwise),
                pl.BlockSpec((1, size), flat),
            ],
            scratch_shapes=[pltpu.VMEM((heads, size, rows), F32)]
            + [pltpu.VMEM((2 * rows, heads * rows), LOW)] * 2,
        ),
        out_shape=[
            jax.ShapeDtypeStruct((seq, 2 * size), F32),
            jax.ShapeDtypeStruct((tiles * rows, heads * size), LOW),
            jax.ShapeDtypeStruct((1, size), F32),
        ],
        compiler_params=params(),
        cost_estimate=cost(
            15 * tiles * rows * heads * seq * size, 12e6, tiles * rows * heads * seq
        ),
    )(qpos, kidx, queries, grads, centre, kv, keys_t, proj, gain[None], cos2, sin2, *others)


def out_kernel(a_ref, b_ref, *rest):
    rest[-1][...] = dot_nn(a_ref[...], b_ref[...]).astype(LOW)


def out_dot(a, b, others):
    block, inner = a.shape
    columns = b.shape[1]
    tile = min(columns, 512)
    return pl.pallas_call(
        out_kernel,
        grid=(columns // tile,),
        in_specs=[
            pl.BlockSpec((block, inner), lambda i: (0, 0)),
            pl.BlockSpec((inner, tile), lambda i: (0, i)),
        ]
        + [pl.BlockSpec(memory_space=pl.ANY)] * len(others),
        out_specs=pl.BlockSpec((block, tile), lambda i: (0, i)),
        out_shape=jax.ShapeDtypeStruct((block, columns), LOW),
        compiler_params=params(),
        cost_estimate=cost(2 * block * inner * columns, 8e6),
    )(a, b, *others)


def token_kernel(a_ref, b_ref, *rest):
    rest[-1][...] = dot_tn(a_ref[...], b_ref[...]).astype(LOW)


def token_dot(a, b, others):
    block, rows = a.shape
    columns = b.shape[1]
    tile = min(rows, 512)
    return pl.pallas_call(
        token_kernel,
        grid=(rows // tile,),
        in_specs=[
            pl.BlockSpec((block, tile), lambda i: (0, i)),
            pl.BlockSpec((block, columns), lambda i: (0, 0)),
        ]
        + [pl.BlockSpec(memory_space=pl.ANY)] * len(others),
        out_specs=pl.BlockSpec((tile, columns), lambda i: (i, 0)),
        out_shape=jax.ShapeDtypeStruct((rows, columns), LOW),
        compiler_params=params(),
        cost_estimate=cost(2 * block * rows * columns, 6e6),
    )(a, b, *others)


def halves_kernel(d_ref, a_ref, b_ref, *rest):
    send_ref, keep_ref = rest[-2:]
    product = dot_tn(a_ref[...], b_ref[...]).astype(LOW)

    @pl.when(pl.program_id(0) == 0)
    def _():
        send_ref[...] = product

    @pl.when(pl.program_id(0) == 1)
    def _():
        keep_ref[...] = product


def token_halves(a, b, others):
    block, rows = a.shape
    columns = b.shape[1]
    tiles = 2 if rows % 512 == 0 else 1
    tile = rows // (2 * tiles)
    d = lax.axis_index("dp").astype(jnp.int32)[None]
    half = jax.ShapeDtypeStruct((rows // 2, columns), LOW)
    return pl.pallas_call(
        halves_kernel,
        grid_spec=pltpu.PrefetchScalarGridSpec(
            num_scalar_prefetch=1,
            grid=(2, tiles),
            in_specs=[
                pl.BlockSpec(
                    (block, tile),
                    lambda h, j, d: (0, ((1 - d[0]) * (1 - h) + d[0] * h) * tiles + j),
                ),
                pl.BlockSpec((block, columns), lambda h, j, d: (0, 0)),
            ]
            + [pl.BlockSpec(memory_space=pl.ANY)] * len(others),
            out_specs=[
                pl.BlockSpec((tile, columns), lambda h, j, d: (j * (1 - h) + (tiles - 1) * h, 0)),
                pl.BlockSpec((tile, columns), lambda h, j, d: (j * h, 0)),
            ],
        ),
        out_shape=[half, half],
        compiler_params=params(),
        cost_estimate=cost(2 * block * rows * columns, 6e6),
    )(d, a, b, *others)


def split_low(value):
    high = value.astype(LOW)
    return high, (value - high.astype(F32)).astype(LOW)


def norm_parts(rows):
    rr = lax.rsqrt(jnp.mean(rows * rows, axis=-1, keepdims=True) + EPS)
    return rows * rr, rr


def norm_back(grad, normal, rr, gain):
    weighted = grad * gain
    return rr * (weighted - normal * jnp.mean(weighted * normal, axis=-1, keepdims=True))


def add_all(refs):
    return functools.reduce(jnp.add, [ref[...].astype(F32) for ref in refs])


def pad_rows(rows, count):
    if rows.shape[0] == count:
        return rows
    return jnp.concatenate(
        [rows, jnp.zeros((count - rows.shape[0], rows.shape[1]), rows.dtype)], axis=0
    )


def router_kernel(experts, *refs):
    x_ref, attn_ref, gain_ref, router_ref, mask_ref = refs[:5]
    hidden_ref, mixed_ref, probs_ref = refs[-3:]
    width = x_ref.shape[1]
    lanes = mask_ref.shape[1]
    hidden = add_all([x_ref, attn_ref])
    hidden_ref[...] = hidden
    mixed = (norm_parts(hidden)[0] * gain_ref[...]).astype(LOW)
    mixed_ref[:, :width] = mixed
    logits = dot_nt(mixed, pad_rows(router_ref[...], lanes))
    lane = lax.broadcasted_iota(jnp.int32, logits.shape, 1)
    logits = jnp.where(lane < experts, logits, -1e30)
    weights = jnp.exp(logits - jnp.max(logits, axis=1, keepdims=True))
    probs = weights / jnp.sum(weights, axis=1, keepdims=True)
    probs_ref[...] = probs
    chosen = probs * mask_ref[...]
    high, low = split_low(chosen / jnp.sum(chosen, axis=1, keepdims=True))
    both = high.astype(F32) + pltpu.roll(low.astype(F32), experts, 1)
    mixed_ref[:, width:] = both.astype(LOW)


def route_rows(x, attn, gain, router, mask, experts, others):
    tokens, width = x.shape
    lanes = mask.shape[1]
    operands = [x, attn, gain[None], router, mask]
    shapes = [
        jax.ShapeDtypeStruct((tokens, width), F32),
        jax.ShapeDtypeStruct((tokens, width + lanes), LOW),
        jax.ShapeDtypeStruct((tokens, lanes), F32),
    ]
    return pl.pallas_call(
        functools.partial(router_kernel, experts),
        grid=(1,),
        in_specs=[full(value.shape) for value in operands]
        + [pl.BlockSpec(memory_space=pl.ANY)] * len(others),
        out_specs=[full(shape.shape) for shape in shapes],
        out_shape=shapes,
        compiler_params=params(),
        cost_estimate=cost(2 * tokens * width * lanes, 5e6),
    )(*operands, *others)


def one_hot(slots, count, first):
    groups, tokens = slots.shape
    slot = lax.broadcasted_iota(jnp.int32, (groups, count, tokens), 1).astype(F32)
    same = slots[:, None, :] == slot + float(first)
    return jnp.where(same, 1.0, 0.0).reshape(groups * count, tokens)


def slot_kernel(capacity, meta_ref, col_ref, rows_ref, slots_ref):
    groups, block = slots_ref.shape
    rows, width = rows_ref.shape
    n = rows // groups // capacity
    tokens = block // n
    mask = col_ref[:, width:]
    lanes = mask.shape[1]
    padded = -(-groups // 16) * 16
    group = lax.broadcasted_iota(jnp.int32, (padded, lanes), 0)
    lane = lax.broadcasted_iota(jnp.int32, (padded, lanes), 1)
    wanted = jnp.logical_and(lane == group * n + meta_ref[0], group < groups)
    hits = dot_nt(jnp.where(wanted, 1.0, 0.0).astype(LOW), mask)
    before = lax.broadcasted_iota(jnp.int32, (tokens, tokens), 0)
    after_it = lax.broadcasted_iota(jnp.int32, (tokens, tokens), 1)
    earlier = jnp.where(before < after_it, 1.0, 0.0).astype(LOW)
    for z in range(n):
        hit = hits[:, z * tokens : (z + 1) * tokens]
        rank = dot_nn(hit.astype(LOW), earlier)
        turn = (meta_ref[1 + z] * capacity).astype(F32)
        slot = jnp.where(hit > 0.5, rank + turn, -1.0)
        slots_ref[:, z * tokens : (z + 1) * tokens] = slot[:groups]
    spread = one_hot(slots_ref[...], n * capacity, 0).astype(LOW)
    rows_ref[...] = dot_nn(spread, col_ref[:, :width]).astype(LOW)


def make_slots(meta, col, width, groups, capacity):
    block = col.shape[0]
    n = lax.axis_size("expert")
    shapes = [
        jax.ShapeDtypeStruct((groups * n * capacity, width), LOW),
        jax.ShapeDtypeStruct((groups, block), F32),
    ]
    return pl.pallas_call(
        functools.partial(slot_kernel, capacity),
        grid_spec=pltpu.PrefetchScalarGridSpec(
            num_scalar_prefetch=1,
            grid=(1,),
            in_specs=[full(col.shape)],
            out_specs=[full(shape.shape) for shape in shapes],
        ),
        out_shape=shapes,
        compiler_params=params(),
        cost_estimate=cost(2 * groups * n * capacity * block * width, 8e6),
    )(meta, col)


def table_kernel(capacity, n_half, meta_ref, slots_ref, near_ref, far_ref, near_back_ref, far_back_ref):
    n = 2 * n_half
    tokens = slots_ref.shape[1] // n
    cap_half = n_half * capacity
    for part, (to_ref, back_ref) in enumerate([(near_ref, near_back_ref), (far_ref, far_back_ref)]):
        pieces = []
        for k in range(n_half):
            start = pl.multiple_of(meta_ref[1 + n + part * n_half + k] * tokens, tokens)
            pieces.append(slots_ref[:, pl.ds(start, tokens)])
        spread = one_hot(jnp.concatenate(pieces, axis=1), cap_half, part * cap_half)
        to_ref[...] = spread.astype(LOW)
        back_ref[...] = jnp.transpose(spread).astype(LOW)


def make_tables(meta, slots, n_half, capacity):
    groups, block = slots.shape
    rows = groups * n_half * capacity
    shapes = [jax.ShapeDtypeStruct((rows, block // 2), LOW)] * 2
    shapes += [jax.ShapeDtypeStruct((block // 2, rows), LOW)] * 2
    outs = pl.pallas_call(
        functools.partial(table_kernel, capacity, n_half),
        grid_spec=pltpu.PrefetchScalarGridSpec(
            num_scalar_prefetch=1,
            grid=(1,),
            in_specs=[full(slots.shape)],
            out_specs=[full(shape.shape) for shape in shapes],
        ),
        out_shape=shapes,
        compiler_params=params(),
        cost_estimate=cost(8 * rows * block, 3e6),
    )(meta, slots)
    return outs[:2], outs[2:]


def spread_kernel(choices, place_ref, spread_ref, *refs):
    out_ref, rows_ref = refs[-2:]
    for k, by_place in enumerate(choices):
        for which in sorted(set(by_place)):
            hit = functools.reduce(
                jnp.logical_or,
                [place_ref[0] == i for i, other in enumerate(by_place) if other == which],
            )

            @pl.when(hit)
            def _():
                tokens = refs[which].shape[0]
                rows_ref[k * tokens : (k + 1) * tokens] = refs[which][...]

    out_ref[...] = dot_nn(spread_ref[...], rows_ref[...]).astype(LOW)


def spread_rows(place, spread, found, turns, others):
    n = lax.axis_size("expert")
    order = arrival_order(n)
    distances = sorted({order[i][turn] - i for i in range(n) for turn in turns})
    choices = [[distances.index(order[i][turn] - i) for i in range(n)] for turn in turns]
    chunks = [found[distance] for distance in distances]
    tokens, wide = chunks[0].shape
    rows = spread.shape[0]
    return pl.pallas_call(
        functools.partial(spread_kernel, choices),
        grid_spec=pltpu.PrefetchScalarGridSpec(
            num_scalar_prefetch=1,
            grid=(1,),
            in_specs=[full(spread.shape)]
            + [full(chunk.shape) for chunk in chunks]
            + [pl.BlockSpec(memory_space=pl.ANY)] * len(others),
            out_specs=full((rows, wide)),
            scratch_shapes=[pltpu.VMEM((len(turns) * tokens, wide), LOW)],
        ),
        out_shape=jax.ShapeDtypeStruct((rows, wide), LOW),
        compiler_params=params(),
        cost_estimate=cost(2 * rows * len(turns) * tokens * wide, 5e6),
    )(place, spread, *chunks, *others)


def router_back_kernel(experts, *refs):
    sum_ref, g_ref, hidden_ref, gain_ref, router_ref, mask_ref, probs_ref = refs[:7]
    grad_ref, low_ref, dgain_ref, drouter_ref = refs[-4:]
    width = g_ref.shape[1]
    lanes = mask_ref.shape[1]
    total = sum_ref[...].astype(F32)
    table = total[:, width:]
    mask, probs = mask_ref[...], probs_ref[...]
    grad_gates = (table + pltpu.roll(table, lanes - experts, 1)) * mask
    chosen = probs * mask
    chosen_sum = jnp.sum(chosen, axis=1, keepdims=True)
    mean = jnp.sum(grad_gates * (chosen / chosen_sum), axis=1, keepdims=True)
    centred = mask * (grad_gates - mean) / chosen_sum
    grad_logits = probs * (centred - jnp.sum(centred * chosen, axis=1, keepdims=True))
    high, low = split_low(grad_logits)
    router = pad_rows(router_ref[...], lanes)
    grad = total[:, :width] + dot_nn(high, router) + dot_nn(low, router)
    normal, rr = norm_parts(hidden_ref[...])
    mixed = (normal * gain_ref[...]).astype(LOW)
    drouter_ref[...] = dot_tn(high, mixed) + dot_tn(low, mixed)
    dgain_ref[...] = jnp.sum(grad * normal, axis=0, keepdims=True)
    grad_hidden = g_ref[...].astype(F32) + norm_back(grad, normal, rr, gain_ref[...])
    grad_ref[...] = grad_hidden
    low_ref[...] = grad_hidden.astype(LOW)


def route_back(summed, g, hidden, gain, router, mask, probs, experts, others):
    tokens, width = g.shape
    lanes = mask.shape[1]
    operands = [summed, g, hidden, gain[None], router, mask, probs]
    shapes = [
        jax.ShapeDtypeStruct((tokens, width), F32),
        jax.ShapeDtypeStruct((tokens, width), LOW),
        jax.ShapeDtypeStruct((1, width), F32),
        jax.ShapeDtypeStruct((lanes, width), F32),
    ]
    return pl.pallas_call(
        functools.partial(router_back_kernel, experts),
        grid=(1,),
        in_specs=[full(value.shape) for value in operands]
        + [pl.BlockSpec(memory_space=pl.ANY)] * len(others),
        out_specs=[full(shape.shape) for shape in shapes],
        out_shape=shapes,
        compiler_params=params(),
        cost_estimate=cost(8 * tokens * width * lanes, 8e6),
    )(*operands, *others)


def combine_kernel(meta_ref, table_ref, rows_ref, *rest):
    del meta_ref
    rest[-1][...] = dot_nn(table_ref[...], rows_ref[...]).astype(LOW)


def combine_part(meta, table, rows, first, n, into, others):
    block, slots = table.shape
    wide = rows.shape[1]
    tokens = block // (n // 2)
    return pl.pallas_call(
        combine_kernel,
        grid_spec=pltpu.PrefetchScalarGridSpec(
            num_scalar_prefetch=1,
            grid=(n // 2,),
            in_specs=[
                pl.BlockSpec((tokens, slots), lambda i, m: (i, 0)),
                full(rows.shape),
            ]
            + [pl.BlockSpec(memory_space=pl.ANY)] * (len(into) + len(others)),
            out_specs=pl.BlockSpec((tokens, wide), lambda i, m: (m[1 + n + first + i], 0)),
        ),
        out_shape=jax.ShapeDtypeStruct((n * tokens, wide), LOW),
        input_output_aliases={3: 0} if into else {},
        compiler_params=params(),
        cost_estimate=cost(2 * slots * block * wide, 6e6),
    )(meta, table, rows, *into, *others)


def combine_rows(meta, tables, rows, n_half, others):
    near = combine_part(meta, tables[0], rows[0], 0, 2 * n_half, [], [])
    return combine_part(meta, tables[1], rows[1], n_half, 2 * n_half, [near], others)


def expert_kernel(experts, who_ref, x_ref, gate_ref, up_ref, pull_ref, *rest):
    act_ref, dgate_ref, dup_ref, copy_ref = rest[-4:]
    width = gate_ref.shape[0]
    x = x_ref[:, :width]
    table = x_ref[:, width:].astype(F32)
    lane = lax.broadcasted_iota(jnp.int32, table.shape, 1)
    mine = who_ref[0]
    gate = jnp.sum(
        jnp.where(jnp.logical_or(lane == mine, lane == mine + experts), table, 0.0),
        axis=1,
        keepdims=True,
    )
    pre_gate = dot_nn(x, gate_ref[...])
    pre_up = dot_nn(x, up_ref[...])
    pull = pull_ref[...].reshape(pre_up.shape)
    sig = 1.0 / (1.0 + jnp.exp(-pre_gate))
    silu = pre_gate * sig
    act = silu * pre_up
    act_ref[...] = (act * gate).astype(LOW)
    high, low = split_low(jnp.sum(act * pull, axis=1, keepdims=True))
    pull = pull * gate
    dup = (pull * silu).astype(LOW)
    dgate = (pull * pre_up * (sig * (1.0 + pre_gate * (1.0 - sig)))).astype(LOW)
    dgate_ref[...] = dgate
    dup_ref[...] = dup
    copy_ref[:, :width] = (dot_nt(dgate, gate_ref[...]) + dot_nt(dup, up_ref[...])).astype(LOW)
    back = jnp.where(lane == mine, high.astype(F32), 0.0)
    back = jnp.where(lane == mine + experts, low.astype(F32), back)
    copy_ref[:, width:] = back.astype(LOW)


def run_expert(who, x, w_gate, w_up, pull, part, experts):
    rows, wide = x.shape
    width, hidden = w_gate.shape
    groups, _, slots, _ = pull.shape
    each = groups // 2
    tile = each * slots
    by_rows = lambda columns: pl.BlockSpec((tile, columns), lambda i, p: (i, 0))
    return pl.pallas_call(
        functools.partial(expert_kernel, experts),
        grid_spec=pltpu.PrefetchScalarGridSpec(
            num_scalar_prefetch=1,
            grid=(2,),
            in_specs=[
                by_rows(wide),
                full(w_gate.shape),
                full(w_up.shape),
                pl.BlockSpec((each, 1, slots, hidden), lambda i, p: (i, part, 0, 0)),
            ],
            out_specs=[by_rows(hidden), by_rows(hidden), by_rows(hidden), by_rows(wide)],
        ),
        out_shape=[jax.ShapeDtypeStruct((rows, hidden), LOW)] * 3
        + [jax.ShapeDtypeStruct((rows, wide), LOW)],
        compiler_params=params(),
        cost_estimate=cost(8 * rows * width * hidden, 20e6, rows * hidden),
    )(who, x, w_gate, w_up, pull)


def input_kernel(grad_ref, x_ref, gain_ref, more_ref, out_ref):
    normal, rr = norm_parts(x_ref[...].astype(F32))
    grad = grad_ref[...].astype(F32)
    out_ref[...] = more_ref[...] + norm_back(grad, normal, rr, gain_ref[...])


def input_back(grad, x, gain, more):
    tokens, width = x.shape
    operands = [grad, x, gain[None], more]
    return pl.pallas_call(
        input_kernel,
        grid=(1,),
        in_specs=[full(value.shape) for value in operands],
        out_specs=full(more.shape),
        out_shape=jax.ShapeDtypeStruct((tokens, width), F32),
        compiler_params=params(),
        cost_estimate=cost(20 * tokens * width, 5e6),
    )(*operands)


def kv_back_kernel(factor, parts_ref, proj_ref, gain_ref, cos_ref, sin_ref, *rest):
    grad_ref, dgain_ref = rest[-2:]
    size = proj_ref.shape[1]
    total = parts_ref[0].astype(F32)
    for k in range(1, parts_ref.shape[0]):
        total += parts_ref[k].astype(F32)
    grad, dgain = head_backward(
        total[:, :size] * factor, proj_ref[...], gain_ref[...], cos_ref[...], sin_ref[...]
    )
    grad_ref[:, :size] = grad.astype(LOW)
    grad_ref[:, size:] = total[:, size:].astype(LOW)
    dgain_ref[...] = dgain


def kv_back(parts, proj, gain, cos2, sin2, factor, others):
    block, size = proj.shape
    operands = [parts, proj, gain[None], cos2, sin2]
    shapes = [
        jax.ShapeDtypeStruct((block, 2 * size), LOW),
        jax.ShapeDtypeStruct((1, size), F32),
    ]
    return pl.pallas_call(
        functools.partial(kv_back_kernel, factor),
        grid=(1,),
        in_specs=[full(value.shape) for value in operands]
        + [pl.BlockSpec(memory_space=pl.ANY)] * len(others),
        out_specs=[full(shape.shape) for shape in shapes],
        out_shape=shapes,
        compiler_params=params(),
        cost_estimate=cost(40 * block * size, 5e6),
    )(*operands, *others)


def unpack_kernel(experts, small_ref, *rest):
    router_ref, attn_ref, mlp_ref, q_ref, k_ref = rest[-5:]
    rows = small_ref[...].astype(F32)
    size = q_ref.shape[1]
    router_ref[...] = rows[:experts]
    attn_ref[...] = rows[experts : experts + 1]
    mlp_ref[...] = rows[experts + 1 : experts + 2]
    q_ref[...] = rows[experts + 2 : experts + 3, :size]
    k_ref[...] = rows[experts + 2 : experts + 3, size : 2 * size]


def unpack_small(small, experts, size, others):
    width = small.shape[1]
    shapes = [(experts, width), (1, width), (1, width), (1, size), (1, size)]
    return pl.pallas_call(
        functools.partial(unpack_kernel, experts),
        grid=(1,),
        in_specs=[full(small.shape)] + [pl.BlockSpec(memory_space=pl.ANY)] * len(others),
        out_specs=[full(shape) for shape in shapes],
        out_shape=[jax.ShapeDtypeStruct(shape, F32) for shape in shapes],
        compiler_params=params(),
        cost_estimate=cost(experts * width, 6 * experts * width),
    )(small, *others)


def pair_kernel(a_ref, b_ref, *rest):
    rest[-1][...] = (a_ref[...].astype(F32) + b_ref[...].astype(F32)).astype(LOW)


def pair_sum(a, b, others):
    rows, columns = a.shape
    tiles = 2 if rows % 32 == 0 else 1
    spec = pl.BlockSpec((rows // tiles, columns), lambda i: (i, 0))
    return pl.pallas_call(
        pair_kernel,
        grid=(tiles,),
        in_specs=[spec, spec] + [pl.BlockSpec(memory_space=pl.ANY)] * len(others),
        out_specs=spec,
        out_shape=jax.ShapeDtypeStruct((rows, columns), LOW),
        compiler_params=params(),
        cost_estimate=cost(rows * columns, 6 * rows * columns),
    )(a, b, *others)


def fold_kernel(n_pairs, s_ref, *refs):
    del s_ref
    send_ref, keep_ref = refs[-2:]
    totals = [
        (refs[2 * k][...].astype(F32) + refs[2 * k + 1][...].astype(F32)).astype(LOW)
        for k in range(n_pairs)
    ]
    for half, out_ref in enumerate((send_ref, keep_ref)):

        @pl.when(pl.program_id(0) == half)
        def _():
            first = 0
            for total in totals:
                last = first + total.shape[1]
                out_ref[:, first:last] = total
                first = last


def fold(pairs, bit, others):
    rows = pairs[0][1].shape[0]
    columns = sum(got.shape[1] for _, got in pairs)
    tiles = 2
    tile = rows // (2 * tiles)
    side = lambda h, m: (1 - m[0]) * (1 - h) + m[0] * h
    specs = []
    for _, got in pairs:
        wide = got.shape[1]
        specs += [pl.BlockSpec((tile, wide), lambda h, j, m: (side(h, m) * tiles + j, 0))] * 2
    shape = jax.ShapeDtypeStruct((rows // 2, columns), LOW)
    return pl.pallas_call(
        functools.partial(fold_kernel, len(pairs)),
        grid_spec=pltpu.PrefetchScalarGridSpec(
            num_scalar_prefetch=1,
            grid=(2, tiles),
            in_specs=specs + [pl.BlockSpec(memory_space=pl.ANY)] * len(others),
            out_specs=[
                pl.BlockSpec((tile, columns), lambda h, j, m: (j * (1 - h) + (tiles - 1) * h, 0)),
                pl.BlockSpec((tile, columns), lambda h, j, m: (j * h, 0)),
            ],
        ),
        out_shape=[shape, shape],
        compiler_params=params(),
        cost_estimate=cost(rows * columns, 6 * rows * columns),
    )(
        bit.astype(jnp.int32)[None],
        *[value for pair in pairs for value in pair],
        *others,
    )


def normed_kernel(q_ref, kv_ref, wq_ref, wkv_ref, rows_ref, *rest):
    out_ref, dgain_ref = rest[-2:]
    grad = dot_nt(q_ref[...], wq_ref[...]) + dot_nt(kv_ref[...], wkv_ref[...])
    out_ref[...] = grad.astype(LOW)
    dgain_ref[...] = jnp.sum(grad * rows_ref[...].astype(F32), axis=0, keepdims=True)


def normed_back(grad_q, grad_kv, w_q, w_kv, rows, others):
    block, width = rows.shape
    tile = 512
    column = lambda i: (0, i)
    return pl.pallas_call(
        normed_kernel,
        grid=(width // tile,),
        in_specs=[
            full(grad_q.shape),
            full(grad_kv.shape),
            pl.BlockSpec((tile, w_q.shape[1]), lambda i: (i, 0)),
            pl.BlockSpec((tile, w_kv.shape[1]), lambda i: (i, 0)),
            pl.BlockSpec((block, tile), column),
        ]
        + [pl.BlockSpec(memory_space=pl.ANY)] * len(others),
        out_specs=[pl.BlockSpec((block, tile), column), pl.BlockSpec((1, tile), column)],
        out_shape=[
            jax.ShapeDtypeStruct((block, width), LOW),
            jax.ShapeDtypeStruct((1, width), F32),
        ],
        compiler_params=params(),
        cost_estimate=cost(2 * block * width * (w_q.shape[1] + w_kv.shape[1]), 12e6),
    )(grad_q, grad_kv, w_q, w_kv, rows, *others)


def pack_kernel(experts, router_ref, attn_ref, gain_ref, mlp_ref, q_ref, k_ref, *rest):
    out_ref, rows_ref = rest[-2:]
    size = q_ref.shape[1]
    rows_ref[:experts] = router_ref[:experts]
    rows_ref[experts:] = jnp.zeros_like(rows_ref[experts:])
    rows_ref[experts : experts + 1] = attn_ref[...] / gain_ref[...]
    rows_ref[experts + 1 : experts + 2] = mlp_ref[...]
    rows_ref[experts + 2 : experts + 3, :size] = q_ref[...]
    rows_ref[experts + 2 : experts + 3, size : 2 * size] = k_ref[...]
    out_ref[...] = rows_ref[...].astype(LOW)


def pack_small(experts, router, attn, gain, mlp, q, k, others):
    width = attn.shape[1]
    n = lax.axis_size(ALL_AXES)
    shape = (-(-(experts + 3) // n) * n, width)
    operands = [router, attn, gain[None], mlp, q, k]
    return pl.pallas_call(
        functools.partial(pack_kernel, experts),
        grid=(1,),
        in_specs=[full(value.shape) for value in operands]
        + [pl.BlockSpec(memory_space=pl.ANY)] * len(others),
        out_specs=full(shape),
        out_shape=jax.ShapeDtypeStruct(shape, LOW),
        scratch_shapes=[pltpu.VMEM(shape, F32)],
        compiler_params=params(),
        cost_estimate=cost(shape[0] * width, 6 * shape[0] * width),
    )(*operands, *others)


def part_sum_kernel(parts_ref, *rest):
    total = parts_ref[0].astype(F32)
    for k in range(1, parts_ref.shape[0]):
        total += parts_ref[k].astype(F32)
    rest[-1][...] = total.astype(LOW)


def part_sum(parts, others):
    count, rows, columns = parts.shape
    tiles = 2
    return pl.pallas_call(
        part_sum_kernel,
        grid=(tiles,),
        in_specs=[pl.BlockSpec((count, rows // tiles, columns), lambda i: (0, i, 0))]
        + [pl.BlockSpec(memory_space=pl.ANY)] * len(others),
        out_specs=pl.BlockSpec((rows // tiles, columns), lambda i: (i, 0)),
        out_shape=jax.ShapeDtypeStruct((rows, columns), LOW),
        compiler_params=params(),
        cost_estimate=cost(count * rows * columns, 4 * count * rows * columns),
    )(parts, *others)


def widen_kernel(n_chunks, n_outs, at_ref, *refs):
    del at_ref
    outs = refs[-n_outs:]
    widths = [ref.shape[1] for ref in outs]
    for k in range(n_chunks):

        @pl.when(pl.program_id(0) == k)
        def _():
            first = 0
            for wide, out_ref in zip(widths, outs):
                out_ref[...] = refs[k][:, first : first + wide].astype(F32)
                first += wide


def widen(places, chunks, widths, total, others):
    rows, columns = chunks[0].shape
    count = len(chunks)
    return pl.pallas_call(
        functools.partial(widen_kernel, count, len(widths)),
        grid_spec=pltpu.PrefetchScalarGridSpec(
            num_scalar_prefetch=1,
            grid=(count,),
            in_specs=[full(chunk.shape) for chunk in chunks]
            + [pl.BlockSpec(memory_space=pl.ANY)] * len(others),
            out_specs=[pl.BlockSpec((rows, wide), lambda i, at: (at[i], 0)) for wide in widths],
        ),
        out_shape=[jax.ShapeDtypeStruct((total, wide), F32) for wide in widths],
        compiler_params=params(),
        cost_estimate=cost(rows * columns, 6 * count * rows * columns),
    )(jnp.stack(places).astype(jnp.int32), *chunks, *others)


def swap_dp(rows):
    return lax.ppermute(rows, "dp", [(0, 1), (1, 0)])


def swap_context(rows, s):
    n = lax.axis_size("context")
    return lax.ppermute(rows, "context", [(i, i ^ s) for i in range(n)])


def share_context(parts):
    return lax.all_to_all(parts, "context", split_axis=0, concat_axis=0, tiled=True)


def plane_turns():
    d, c = lax.axis_index("dp"), lax.axis_index("context")
    low, high = lax.rem(c, 2), lax.div(c, 2)

    def swap(first, second):
        perm = [(i, i ^ first) for i in range(4)] + [(4 + i, 4 + (i ^ second)) for i in range(4)]
        return lambda rows: lax.ppermute(rows, GROUP_AXES, perm)

    return [
        (jnp.where(d == 0, low, high), swap(1, 2)),
        (jnp.where(d == 0, high, low), swap(2, 1)),
    ]


def plane_first(pairs, others):
    (bit_1, _), _ = plane_turns()
    return fold(pairs, bit_1, others)


def plane_second(send, keep, others):
    (_, swap_1), (bit_2, _) = plane_turns()
    return fold([(keep, swap_1(send))], bit_2, others)


def plane_last(send, keep, others):
    _, (_, swap_2) = plane_turns()
    return pair_sum(keep, swap_2(send), others)


def plane_spread(own):
    (_, swap_1), (_, swap_2) = plane_turns()
    second = swap_2(own)
    return [own, second, swap_1(own), swap_1(second)]


def quarter_places(rank):
    d = lax.axis_index("dp")
    c = lax.axis_index("context")
    low, high = lax.rem(c, 2), lax.div(c, 2)
    places = []
    for core in (d, 1 - d):
        bit_1 = jnp.where(core == 0, low, high)
        bit_2 = jnp.where(core == 0, high, low)
        for flip_1, flip_2 in ((0, 0), (0, 1), (1, 0), (1, 1)):
            places.append(4 * core + rank(core, bit_1 ^ flip_1, bit_2 ^ flip_2))
    return places


def widen_all(quarters, places, widths, others):
    count = len(quarters)
    total = 2 * count * quarters[0].shape[0]
    chunks = quarters + [swap_dp(part) for part in quarters]
    return widen(places, chunks, widths, total, others)


def arrival_order(n):
    return [sorted(range(n), key=lambda j: (abs(j - i), j)) for i in range(n)]


def choose(index, options):
    distinct = []
    for option in options:
        if option is not None and not any(option is other for other in distinct):
            distinct.append(option)
    result = distinct[0]
    for option in distinct[1:]:
        mask = functools.reduce(
            jnp.logical_or, [index == i for i, other in enumerate(options) if other is option]
        )
        result = jnp.where(mask, option, result)
    return result


def line_gather(chunk):
    return line_steps({0: chunk}, 1, lax.axis_size("expert"))


def line_steps(found, first, stop):
    n = lax.axis_size("expert")
    found = dict(found)
    for s in range(first, stop):
        found[-s] = lax.ppermute(
            found[1 - s], "expert", [(i, i + 1) for i in range(s - 1, n - 1)]
        )
        found[s] = lax.ppermute(found[s - 1], "expert", [(i + 1, i) for i in range(n - s)])
    return found


def context_gather(rows):
    n = lax.axis_size("context")
    c = lax.axis_index("context")
    found = {0: rows}
    for s in range(1, n):
        found[s] = lax.ppermute(rows, "context", [(i, i ^ s) for i in range(n)])
    return jnp.concatenate([choose(c, [found[i ^ j] for i in range(n)]) for j in range(n)], axis=0)


def zero_of(*others):
    return functools.reduce(
        jnp.add,
        [
            lax.slice(other, (0,) * other.ndim, (1,) * other.ndim).reshape(()).astype(F32) * 0.0
            for other in others
        ],
    )


def after(value, *others):
    return (value.astype(F32) + zero_of(*others)).astype(value.dtype)


def on_device(
    layer_input,
    grad_output,
    attn_gain,
    query_weight,
    key_weight,
    value_weight,
    q_gain,
    k_gain,
    output_weight,
    mlp_gain,
    router,
    w_gate,
    w_up,
    w_down,
    routes,
    half_order,
):
    n_context = lax.axis_size("context")
    n_expert = lax.axis_size("expert")
    n_groups = lax.axis_size(GROUP_AXES)
    tok_dev, width = layer_input.shape[1:]
    size = q_gain.shape[0]
    kv_total = key_weight.shape[1] * n_expert
    group_dev = n_expert // (kv_total // size)
    kv_index = lax.axis_index("expert") // group_dev
    block = tok_dev * n_expert
    seq = block * n_context
    half = block // 2
    experts = router.shape[1]
    exp_dev = w_gate.shape[0]
    top = routes.shape[2]
    capacity = max(2, (tok_dev * top * 9 + 8 * experts - 1) // (8 * experts))
    scale = size ** (-0.5)

    seq_rows = jnp.arange(seq, dtype=jnp.int32)
    context = lax.axis_index("context")
    own_halves = lax.dynamic_slice_in_dim(half_order, 2 * context, 2)
    own_pos = (own_halves[:, None] * half + jnp.arange(half, dtype=jnp.int32)[None]).reshape(-1)
    per_half = half // TILE
    tile_pos = (half_order[:, None] * per_half + jnp.arange(per_half, dtype=jnp.int32)).reshape(-1)
    kidx = jnp.sum(
        (tile_pos[None, :] == jnp.arange(seq // TILE, dtype=jnp.int32)[:, None])
        * jnp.arange(seq // TILE, dtype=jnp.int32)[None, :],
        axis=1,
    ).astype(jnp.int32)
    qpos = lax.dynamic_slice_in_dim(tile_pos, context * (block // TILE), block // TILE)
    entry = jnp.arange(size)
    freq = jnp.power(THETA, -(2 * (entry % (size // 2))).astype(F32) / size)
    angles = own_pos.astype(F32)[:, None] * freq[None, :]
    cos2 = jnp.cos(angles)
    sin2 = jnp.sin(angles) * jnp.where(entry < size // 2, -1.0, 1.0)[None, :]

    place = lax.axis_index("expert")
    place_1 = place.astype(jnp.int32)[None]
    lanes = -(-2 * experts // 128) * 128
    mask = jnp.any(
        routes[0][:, :, None] == jnp.arange(lanes, dtype=jnp.int32)[None, None, :], axis=1
    )
    mask_wide = mask.astype(F32)
    router_rows = router.T

    x_low = layer_input[0]
    x_normal, _ = norm_parts(x_low.astype(F32))
    normed_found = line_gather((x_normal * attn_gain).astype(LOW))
    if group_dev == 1:
        kv_weights = jnp.concatenate([key_weight, value_weight], axis=1)
    else:
        key_whole = lax.all_gather(key_weight, "expert", axis=1, tiled=True)
        value_whole = lax.all_gather(value_weight, "expert", axis=1, tiled=True)
        kv_weights = jnp.concatenate(
            [
                lax.dynamic_slice_in_dim(key_whole, kv_index * size, size, 1),
                lax.dynamic_slice_in_dim(value_whole, kv_index * size, size, 1),
            ],
            axis=1,
        )
    grad_low = grad_output[0]
    normed_rows, own_kv, key_proj, grad_wide = project_keys(
        place_1,
        normed_found,
        kv_weights,
        k_gain,
        cos2,
        sin2,
        scale * LOG2E,
        grad_low,
        mask_wide,
    )
    grad_col = lax.all_gather(grad_wide, "expert", axis=0, tiled=True)
    kv_whole = context_gather(own_kv)
    queries, query_proj = project_queries(normed_rows, query_weight, q_gain, cos2, sin2)

    n_half = n_expert // 2
    order_here = jnp.asarray(arrival_order(n_expert), jnp.int32)[place]
    turn_here = jnp.sum(
        (order_here[:, None] == jnp.arange(n_expert, dtype=jnp.int32)[None, :])
        * jnp.arange(n_expert, dtype=jnp.int32)[:, None],
        axis=0,
    ).astype(jnp.int32)
    meta = jnp.concatenate([place_1, turn_here, order_here])
    grad_sent, slots = make_slots(meta, grad_col, width, n_groups, capacity)
    spreads, back_tables = make_tables(meta, slots, n_half, capacity)

    def swap_plane(rows):
        parts = rows.reshape(n_groups, -1, rows.shape[1])
        parts = lax.all_to_all(parts, GROUP_AXES, split_axis=0, concat_axis=0, tiled=True)
        return parts.reshape(rows.shape)

    attended, inverse = attend(qpos, kidx, queries, kv_whole, [])
    keys_t = kv_whole[:, :size].T
    attn_part = out_dot(attended, output_weight, [grad_col])
    attn_rows = lax.psum_scatter(attn_part, "expert", scatter_dimension=0, tiled=True)

    grad_x = swap_plane(grad_sent)
    act_pull = dot_nt(grad_x, w_down[0]).reshape(n_groups, 2, n_half * capacity, -1)

    hidden, mixed, probs = route_rows(
        x_low, attn_rows, mlp_gain, router_rows, mask_wide, experts, [keys_t]
    )

    who = (lax.axis_index(ALL_AXES) * exp_dev).astype(jnp.int32)[None]
    mixed_found = line_gather(mixed)
    near = spread_rows(place_1, spreads[0], mixed_found, range(n_half), [grad_x])
    x_near = swap_plane(near)
    worked_near = run_expert(who, x_near, w_gate[0], w_up[0], act_pull, 0, experts)
    far = spread_rows(place_1, spreads[1], mixed_found, range(n_half, n_expert), [x_near])
    x_far = swap_plane(far)
    worked_far = run_expert(who, x_far, w_gate[0], w_up[0], act_pull, 1, experts)
    xs = [x_near, x_far]
    acts, gate_lows, up_lows, copies = (list(pair) for pair in zip(worked_near, worked_far))
    back_far = swap_plane(copies[1])
    back_near = swap_plane(copies[0])
    join = lambda parts: jnp.concatenate(parts, axis=0)
    x_all = join([x[:, :width] for x in xs])
    grad_w_gate = dot_tn(x_all, join(gate_lows))
    grad_w_up = dot_tn(x_all, join(up_lows))
    grad_by_round = jnp.swapaxes(
        grad_x.reshape(n_groups, 2, n_half * capacity, width), 0, 1
    ).reshape(-1, width)
    grad_w_down = dot_tn(join(acts), grad_by_round)
    copies_col = combine_rows(
        meta, back_tables, [back_near, back_far], n_half, [grad_w_gate, grad_w_up]
    )
    copies_sum = lax.psum_scatter(copies_col, "expert", scatter_dimension=0, tiled=True)

    returned = [dot_nn(act, w_down[0]).astype(LOW) for act in acts]
    returned_near = swap_plane(returned[0])

    grad_hidden, grad_hidden_low, grad_mlp_gain, grad_router = route_back(
        copies_sum,
        grad_low,
        hidden,
        mlp_gain,
        router_rows,
        mask_wide,
        probs,
        experts,
        [returned_near, grad_w_down],
    )

    returned_far = swap_plane(returned[1])
    grad_attn = lax.all_gather(grad_hidden_low, "expert", axis=0, tiled=True)
    grad_o, centre = grad_attended(
        grad_attn, output_weight, attended, inverse, [returned_far]
    )
    combined = combine_rows(meta, back_tables, [returned_near, returned_far], n_half, [])
    output_rows = lax.psum_scatter(combined, "expert", scatter_dimension=0, tiled=True)
    w_out_send, w_out_keep = token_halves(attended, grad_attn, [combined])
    w_out_half = pair_sum(w_out_keep, swap_dp(w_out_send), [grad_o])
    w_out_parts = share_context(w_out_half.reshape(n_context, -1, width))
    grad_kv, grad_q, grad_q_gain = attend_back(
        qpos,
        kidx,
        queries,
        grad_o,
        centre,
        kv_whole,
        keys_t,
        query_proj,
        q_gain,
        cos2,
        sin2,
        [w_out_half],
    )
    kv_parts = share_context(grad_kv.astype(LOW).reshape(n_context, block, 2 * size))
    w_out_own = part_sum(w_out_parts, [grad_kv])
    w_query_send, w_query_keep = token_halves(normed_rows, grad_q, [w_out_own])
    w_query_got = swap_dp(w_query_send)
    output_rows = hidden + output_rows.astype(F32) + zero_of(w_query_keep)

    kv_grads, grad_k_gain = kv_back(
        kv_parts, key_proj, k_gain, cos2, sin2, scale, [w_query_keep]
    )
    w_out_quarters = plane_spread(w_out_own)
    pairs = [(w_query_keep, w_query_got)]
    widths = [query_weight.shape[1]]
    if group_dev == 1:
        w_kv_send, w_kv_keep = token_halves(normed_rows, kv_grads, [])
        pairs.append((w_kv_keep, swap_dp(w_kv_send)))
        widths += [key_weight.shape[1], value_weight.shape[1]]
    grad_normed, gain_rows = normed_back(
        grad_q, kv_grads, query_weight, kv_weights, normed_rows, []
    )
    send, keep = plane_first(pairs, [grad_normed])
    (grad_w_out,) = widen_all(
        w_out_quarters,
        quarter_places(lambda core, b1, b2: jnp.where(core == 0, b1 + 2 * b2, 2 * b1 + b2)),
        [width],
        [],
    )
    small = pack_small(
        experts,
        grad_router,
        gain_rows,
        attn_gain,
        grad_mlp_gain,
        grad_q_gain,
        grad_k_gain,
        [],
    )
    swap_all = lambda rows: lax.all_to_all(rows, ALL_AXES, split_axis=0, concat_axis=0, tiled=True)
    small_parts = swap_all(small.reshape(lax.axis_size(ALL_AXES), -1, width))
    small_own = jnp.sum(small_parts.astype(F32), axis=0).astype(LOW)
    second_send, second_keep = plane_second(send, keep, [small_own, *w_out_quarters[1:3]])
    grad_normed = lax.psum_scatter(grad_normed, "expert", scatter_dimension=0, tiled=True)
    grad_input = input_back(grad_normed, x_low, attn_gain, grad_hidden)
    quarter = plane_last(second_send, second_keep, [output_rows, grad_input])
    small_sum = swap_all(jnp.broadcast_to(small_own[None], small_parts.shape))
    grad_router, grad_attn_gain, grad_mlp_gain, grad_q_gain, grad_k_gain = unpack_small(
        small_sum.reshape(small.shape), experts, size, [grad_w_out]
    )
    quarters = plane_spread(quarter)
    places = quarter_places(lambda core, b1, b2: 2 * b1 + b2)
    grad_w_query, *more = widen_all(quarters, places, widths, [grad_router])
    if group_dev == 1:
        grad_w_key, grad_w_value = more
    else:
        w_kv = token_dot(normed_rows, kv_grads, [])
        blank = jnp.zeros((width, kv_total), LOW)
        pieces = []
        for part in (w_kv[:, :size], w_kv[:, size:]):
            padded = lax.dynamic_update_slice(blank, part, (0, kv_index * size))
            pieces.append(lax.psum_scatter(padded, "expert", scatter_dimension=1, tiled=True))
        grad_w_key, grad_w_value = (lax.psum(piece, GROUP_AXES).astype(F32) for piece in pieces)
    return (
        output_rows.astype(LOW)[None],
        grad_input[None],
        grad_attn_gain[0],
        grad_w_query,
        grad_w_key,
        grad_w_value,
        grad_q_gain[0],
        grad_k_gain[0],
        grad_w_out,
        grad_mlp_gain[0],
        grad_router.T,
        grad_w_gate[None],
        grad_w_up[None],
        grad_w_down[None],
    )


def solution(mesh):
    rows = P("dp", ("context", "expert"), None)
    expert = P(ALL_AXES, None, None)
    columns = P(None, "expert")
    in_specs = (
        rows,
        rows,
        P(),
        columns,
        columns,
        columns,
        P(),
        P(),
        P("expert", None),
        P(),
        P(),
        expert,
        expert,
        expert,
        rows,
        P(),
    )
    out_specs = (
        rows,
        rows,
        P(),
        columns,
        columns,
        columns,
        P(),
        P(),
        P("expert", None),
        P(),
        P(),
        expert,
        expert,
        expert,
    )
    return jax.shard_map(
        on_device, mesh=mesh, in_specs=in_specs, out_specs=out_specs, check_vma=False
    )
```

```python
import functools
import math

import jax
import jax.numpy as jnp
from jax import lax
from jax.experimental import pallas as pl
from jax.experimental.pallas import tpu as pltpu
from jax.sharding import PartitionSpec as P

EPS = 1e-06
THETA = 1000000.0
TILE = 256
PIECE = 128
VMEM_BYTES = 56 * 1024 * 1024
LOG2E = math.log2(math.e)
LOW = jnp.bfloat16
F32 = jnp.float32
ALL_AXES = ("dp", "context", "expert")
GROUP_AXES = ("dp", "context")


def dot_nn(a, b):
    return lax.dot_general(a, b, (((1,), (0,)), ((), ())), preferred_element_type=F32)


def dot_nt(a, b):
    return lax.dot_general(a, b, (((1,), (1,)), ((), ())), preferred_element_type=F32)


def dot_tn(a, b):
    return lax.dot_general(a, b, (((0,), (0,)), ((), ())), preferred_element_type=F32)


def params(**more):
    return pltpu.CompilerParams(vmem_limit_bytes=VMEM_BYTES, **more)


def cost(flops, nbytes, exps=0):
    return pl.CostEstimate(flops=int(flops), bytes_accessed=int(nbytes), transcendentals=int(exps))


def head_forward(u, gain, cos2, sin2):
    rr = lax.rsqrt(jnp.mean(u * u, axis=-1, keepdims=True) + EPS)
    y = u * rr * gain
    return y * cos2 + pltpu.roll(y, 64, 1) * sin2


def head_backward(gy, u, gain, cos2, sin2):
    g = gy * cos2 - pltpu.roll(gy, 64, 1) * sin2
    rr = lax.rsqrt(jnp.mean(u * u, axis=-1, keepdims=True) + EPS)
    n = u * rr
    gn = g * gain
    grad = rr * (gn - n * jnp.mean(gn * n, axis=-1, keepdims=True))
    return grad, jnp.sum(g * n, axis=0, keepdims=True)


def query_kernel(x_ref, w_ref, gain_ref, cos_ref, sin_ref, rot_ref, proj_ref):
    tiles, heads, rows, size = rot_ref.shape
    acc = dot_nn(x_ref[...], w_ref[...])
    for h in range(heads):
        u = acc[:, h * size : (h + 1) * size]
        rot = head_forward(u, gain_ref[...], cos_ref[...], sin_ref[...])
        proj_ref[:, h] = u.reshape(tiles, rows, size)
        rot_ref[:, h] = rot.astype(LOW).reshape(tiles, rows, size)


def project_queries(normed, weight, gain, cos2, sin2):
    block, width = normed.shape
    size = cos2.shape[1]
    heads = weight.shape[1] // size
    tiles = block // TILE
    whole = lambda i: (0, 0)
    per = lambda i: (0, i, 0, 0)
    shape = (tiles, heads, TILE, size)
    return pl.pallas_call(
        query_kernel,
        grid=(heads // 2,),
        in_specs=[
            pl.BlockSpec((block, width), whole),
            pl.BlockSpec((width, 2 * size), lambda i: (0, i)),
            pl.BlockSpec((1, size), whole),
            pl.BlockSpec((block, size), whole),
            pl.BlockSpec((block, size), whole),
        ],
        out_specs=[pl.BlockSpec((tiles, 2, TILE, size), per)] * 2,
        out_shape=[jax.ShapeDtypeStruct(shape, LOW), jax.ShapeDtypeStruct(shape, F32)],
        compiler_params=params(),
        cost_estimate=cost(2 * block * width * heads * size, 12e6),
    )(normed, weight, gain[None], cos2, sin2)


def put_in_order(place, refs, out_ref):
    n = (len(refs) + 1) // 2
    rows = refs[0].shape[0]
    for distance in range(1 - n, n):
        ref = refs[distance + n - 1]
        at = place + distance

        @pl.when(jnp.logical_and(at >= 0, at < n))
        def _():
            out_ref[pl.ds(pl.multiple_of(at * rows, rows), rows), :] = ref[...]


def chunk_list(found):
    n = (len(found) + 1) // 2
    return [found[distance] for distance in range(1 - n, n)]


def key_kernel(factor, n_chunks, place_ref, *refs):
    w_ref, gain_ref, cos_ref, sin_ref, g_ref, mask_ref = refs[n_chunks:-4]
    rows_ref, kv_ref, proj_ref, wide_ref = refs[-4:]
    size = proj_ref.shape[1]
    width = g_ref.shape[1]
    put_in_order(place_ref[0], refs[:n_chunks], rows_ref)
    wide_ref[:, :width] = g_ref[...]
    wide_ref[:, width:] = mask_ref[...].astype(LOW)
    acc = dot_nn(rows_ref[...], w_ref[...])
    u = acc[:, :size]
    rot = head_forward(u, gain_ref[...], cos_ref[...], sin_ref[...])
    proj_ref[...] = u
    kv_ref[:, :size] = (rot * factor).astype(LOW)
    kv_ref[:, size:] = acc[:, size:].astype(LOW)


def full(shape):
    return pl.BlockSpec(shape, lambda *_: (0,) * len(shape))


def project_keys(place, found, weight, gain, cos2, sin2, factor, g, mask):
    chunks = chunk_list(found)
    rows, width = chunks[0].shape
    block, size = cos2.shape
    operands = [*chunks, weight, gain[None], cos2, sin2, g, mask]
    shapes = [
        jax.ShapeDtypeStruct((block, width), LOW),
        jax.ShapeDtypeStruct((block, 2 * size), LOW),
        jax.ShapeDtypeStruct((block, size), F32),
        jax.ShapeDtypeStruct((rows, width + mask.shape[1]), LOW),
    ]
    return pl.pallas_call(
        functools.partial(key_kernel, factor, len(chunks)),
        grid_spec=pltpu.PrefetchScalarGridSpec(
            num_scalar_prefetch=1,
            grid=(1,),
            in_specs=[full(x.shape) for x in operands],
            out_specs=[full(x.shape) for x in shapes],
        ),
        out_shape=shapes,
        compiler_params=params(),
        cost_estimate=cost(4 * block * width * size, 8e6),
    )(place, *operands)


def in_order(last, step):
    lax.fori_loop(0, lax.div(last, 2), lambda p, c: (step([2 * p, 2 * p + 1], False), c)[1], 0)

    @pl.when(lax.rem(last, 2) == 1)
    def _():
        step([last - 1, last], True)

    @pl.when(lax.rem(last, 2) == 0)
    def _():
        step([last], True)


def attend_kernel(qpos_ref, kidx_ref, q_ref, kv_ref, *rest):
    out_ref, inv_ref, acc_ref = rest[-3:]
    heads, rows, size = q_ref.shape[1:]
    acc_ref[...] = jnp.zeros_like(acc_ref)

    def step(places, masked):
        starts = [pl.multiple_of(kidx_ref[place] * rows, rows) for place in places]
        count = len(places) * rows
        keys = jnp.concatenate([kv_ref[pl.ds(start, rows), :size] for start in starts], axis=0)
        values = jnp.concatenate([kv_ref[pl.ds(start, rows), size:] for start in starts], axis=0)
        values = jnp.concatenate([values, jnp.ones((count, size), LOW)], axis=1)
        for h in range(heads):
            for first in range(0, rows, PIECE):
                part = slice(first, first + PIECE)
                e = jnp.exp2(dot_nt(q_ref[0, h, part], keys))
                if masked:
                    qi = lax.broadcasted_iota(jnp.int32, e.shape, 0) + first
                    ki = lax.broadcasted_iota(jnp.int32, e.shape, 1) - (count - rows)
                    e = jnp.where(ki <= qi, e, 0.0)
                acc_ref[h, part] += dot_nn(e.astype(LOW), values)

    in_order(qpos_ref[pl.program_id(0)], step)
    for h in range(heads):
        inv = 1.0 / acc_ref[h, :, size:]
        inv_ref[0, h] = inv
        out_ref[:, h * size : (h + 1) * size] = (acc_ref[h, :, :size] * inv).astype(LOW)


def attend(qpos, kidx, queries, kv, others):
    tiles, heads, rows, size = queries.shape
    seq = kv.shape[0]
    return pl.pallas_call(
        attend_kernel,
        grid_spec=pltpu.PrefetchScalarGridSpec(
            num_scalar_prefetch=2,
            grid=(tiles,),
            in_specs=[
                pl.BlockSpec((1, heads, rows, size), lambda i, a, b: (i, 0, 0, 0)),
                pl.BlockSpec((seq, 2 * size), lambda i, a, b: (0, 0)),
            ]
            + [pl.BlockSpec(memory_space=pl.ANY)] * len(others),
            out_specs=[
                pl.BlockSpec((rows, heads * size), lambda i, a, b: (i, 0)),
                pl.BlockSpec((1, heads, rows, size), lambda i, a, b: (i, 0, 0, 0)),
            ],
            scratch_shapes=[pltpu.VMEM((heads, rows, 2 * size), F32)],
        ),
        out_shape=[
            jax.ShapeDtypeStruct((tiles * rows, heads * size), LOW),
            jax.ShapeDtypeStruct((tiles, heads, rows, size), F32),
        ],
        compiler_params=params(),
        cost_estimate=cost(
            6 * tiles * rows * heads * seq * size, 8e6, tiles * rows * heads * seq
        ),
    )(qpos, kidx, queries, kv, *others)


def grad_out_kernel(rows_ref, w_ref, o_ref, inv_ref, *rest):
    do_ref, centre_ref = rest[-2:]
    tiles, heads, rows, size = do_ref.shape
    acc = dot_nt(rows_ref[...], w_ref[...])
    for t in range(tiles):
        for h in range(heads):
            part = slice(t * rows, (t + 1) * rows), slice(h * size, (h + 1) * size)
            low = (acc[part] * inv_ref[t, h]).astype(LOW)
            do_ref[t, h] = low
            product = low.astype(F32) * o_ref[part].astype(F32)
            centre = jnp.sum(jnp.transpose(product), axis=0, keepdims=True)
            centre_ref[t, h] = jnp.broadcast_to(centre, (8, rows))


def grad_attended(grad_rows, weight, attended, inverse, others):
    tiles, heads, rows, size = inverse.shape
    block, width = grad_rows.shape
    return pl.pallas_call(
        grad_out_kernel,
        grid=(heads // 2,),
        in_specs=[
            pl.BlockSpec((block, width), lambda i: (0, 0)),
            pl.BlockSpec((2 * size, width), lambda i: (i, 0)),
            pl.BlockSpec((block, 2 * size), lambda i: (0, i)),
            pl.BlockSpec((tiles, 2, rows, size), lambda i: (0, i, 0, 0)),
        ]
        + [pl.BlockSpec(memory_space=pl.ANY)] * len(others),
        out_specs=[
            pl.BlockSpec((tiles, 2, rows, size), lambda i: (0, i, 0, 0)),
            pl.BlockSpec((tiles, 2, 8, rows), lambda i: (0, i, 0, 0)),
        ],
        out_shape=[
            jax.ShapeDtypeStruct((tiles, heads, rows, size), LOW),
            jax.ShapeDtypeStruct((tiles, heads, 8, rows), F32),
        ],
        compiler_params=params(),
        cost_estimate=cost(2 * block * width * heads * size, 12e6),
    )(grad_rows, weight, attended, inverse, *others)


def attend_back_kernel(
    qpos_ref,
    kidx_ref,
    q_ref,
    do_ref,
    centre_ref,
    kv_ref,
    kt_ref,
    proj_ref,
    gain_ref,
    cos_ref,
    sin_ref,
    *rest,
):
    dkv_ref, dq_ref, dgain_ref, acc_ref, e_ref, ds_ref = rest[-6:]
    heads, rows, size = q_ref.shape[1:]

    @pl.when(pl.program_id(0) == 0)
    def _():
        dkv_ref[...] = jnp.zeros_like(dkv_ref)
        dgain_ref[...] = jnp.zeros_like(dgain_ref)

    acc_ref[...] = jnp.zeros_like(acc_ref)

    def step(places, masked):
        starts = [pl.multiple_of(kidx_ref[place] * rows, rows) for place in places]
        count = len(places) * rows
        keys = jnp.concatenate([kv_ref[pl.ds(start, rows), :size] for start in starts], axis=0)
        values = jnp.concatenate([kv_ref[pl.ds(start, rows), size:] for start in starts], axis=0)
        keys_t = jnp.concatenate([kt_ref[:, pl.ds(start, rows)] for start in starts], axis=1)
        for h in range(heads):
            query, grad = q_ref[0, h], do_ref[0, h]
            centre = centre_ref[0, h, 0:1]
            columns = slice(h * rows, (h + 1) * rows)
            for first in range(0, count, PIECE):
                part = slice(first, first + PIECE)
                e = jnp.exp2(dot_nt(keys[part], query))
                if masked and first >= count - rows:
                    ki = lax.broadcasted_iota(jnp.int32, e.shape, 0) + (first - (count - rows))
                    qi = lax.broadcasted_iota(jnp.int32, e.shape, 1)
                    e = jnp.where(ki <= qi, e, 0.0)
                ds = e * (dot_nt(values[part], grad) - centre)
                e_ref[part, columns] = e.astype(LOW)
                ds_ref[part, columns] = ds.astype(LOW)
            acc_ref[h] += dot_nn(keys_t, ds_ref[:count, columns])
        dk = dot_nn(ds_ref[:count], q_ref[0].reshape(heads * rows, size))
        dv = dot_nn(e_ref[:count], do_ref[0].reshape(heads * rows, size))
        for k, start in enumerate(starts):
            dkv_ref[pl.ds(start, rows), :size] += dk[k * rows : (k + 1) * rows]
            dkv_ref[pl.ds(start, rows), size:] += dv[k * rows : (k + 1) * rows]

    in_order(qpos_ref[pl.program_id(0)], step)
    total = jnp.zeros((1, size), F32)
    for h in range(heads):
        grad, gain_part = head_backward(
            jnp.transpose(acc_ref[h]) * (1.0 / LOG2E),
            proj_ref[0, h],
            gain_ref[...],
            cos_ref[...],
            sin_ref[...],
        )
        dq_ref[:, h * size : (h + 1) * size] = grad.astype(LOW)
        total += gain_part
    dgain_ref[...] += total


def attend_back(qpos, kidx, queries, grads, centre, kv, keys_t, proj, gain, cos2, sin2, others):
    tiles, heads, rows, size = queries.shape
    seq = kv.shape[0]
    per = pl.BlockSpec((1, heads, rows, size), lambda i, a, b: (i, 0, 0, 0))
    flat = lambda i, a, b: (0, 0)
    rowwise = lambda i, a, b: (i, 0)
    return pl.pallas_call(
        attend_back_kernel,
        grid_spec=pltpu.PrefetchScalarGridSpec(
            num_scalar_prefetch=2,
            grid=(tiles,),
            in_specs=[
                per,
                per,
                pl.BlockSpec((1, heads, 8, rows), lambda i, a, b: (i, 0, 0, 0)),
                pl.BlockSpec((seq, 2 * size), flat),
                pl.BlockSpec((size, seq), flat),
                per,
                pl.BlockSpec((1, size), flat),
                pl.BlockSpec((rows, size), rowwise),
                pl.BlockSpec((rows, size), rowwise),
            ]
            + [pl.BlockSpec(memory_space=pl.ANY)] * len(others),
            out_specs=[
                pl.BlockSpec((seq, 2 * size), flat),
                pl.BlockSpec((rows, heads * size), rowwise),
                pl.BlockSpec((1, size), flat),
            ],
            scratch_shapes=[pltpu.VMEM((heads, size, rows), F32)]
            + [pltpu.VMEM((2 * rows, heads * rows), LOW)] * 2,
        ),
        out_shape=[
            jax.ShapeDtypeStruct((seq, 2 * size), F32),
            jax.ShapeDtypeStruct((tiles * rows, heads * size), LOW),
            jax.ShapeDtypeStruct((1, size), F32),
        ],
        compiler_params=params(),
        cost_estimate=cost(
            15 * tiles * rows * heads * seq * size, 12e6, tiles * rows * heads * seq
        ),
    )(qpos, kidx, queries, grads, centre, kv, keys_t, proj, gain[None], cos2, sin2, *others)


def out_kernel(a_ref, b_ref, *rest):
    rest[-1][...] = dot_nn(a_ref[...], b_ref[...]).astype(LOW)


def out_dot(a, b, others):
    block, inner = a.shape
    columns = b.shape[1]
    tile = min(columns, 512)
    return pl.pallas_call(
        out_kernel,
        grid=(columns // tile,),
        in_specs=[
            pl.BlockSpec((block, inner), lambda i: (0, 0)),
            pl.BlockSpec((inner, tile), lambda i: (0, i)),
        ]
        + [pl.BlockSpec(memory_space=pl.ANY)] * len(others),
        out_specs=pl.BlockSpec((block, tile), lambda i: (0, i)),
        out_shape=jax.ShapeDtypeStruct((block, columns), LOW),
        compiler_params=params(),
        cost_estimate=cost(2 * block * inner * columns, 8e6),
    )(a, b, *others)


def token_kernel(a_ref, b_ref, *rest):
    rest[-1][...] = dot_tn(a_ref[...], b_ref[...]).astype(LOW)


def token_dot(a, b, others):
    block, rows = a.shape
    columns = b.shape[1]
    tile = min(rows, 512)
    return pl.pallas_call(
        token_kernel,
        grid=(rows // tile,),
        in_specs=[
            pl.BlockSpec((block, tile), lambda i: (0, i)),
            pl.BlockSpec((block, columns), lambda i: (0, 0)),
        ]
        + [pl.BlockSpec(memory_space=pl.ANY)] * len(others),
        out_specs=pl.BlockSpec((tile, columns), lambda i: (i, 0)),
        out_shape=jax.ShapeDtypeStruct((rows, columns), LOW),
        compiler_params=params(),
        cost_estimate=cost(2 * block * rows * columns, 6e6),
    )(a, b, *others)


def halves_kernel(d_ref, a_ref, b_ref, *rest):
    send_ref, keep_ref = rest[-2:]
    product = dot_tn(a_ref[...], b_ref[...]).astype(LOW)

    @pl.when(pl.program_id(0) == 0)
    def _():
        send_ref[...] = product

    @pl.when(pl.program_id(0) == 1)
    def _():
        keep_ref[...] = product


def token_halves(a, b, others):
    block, rows = a.shape
    columns = b.shape[1]
    tiles = 2 if rows % 512 == 0 else 1
    tile = rows // (2 * tiles)
    d = lax.axis_index("dp").astype(jnp.int32)[None]
    half = jax.ShapeDtypeStruct((rows // 2, columns), LOW)
    return pl.pallas_call(
        halves_kernel,
        grid_spec=pltpu.PrefetchScalarGridSpec(
            num_scalar_prefetch=1,
            grid=(2, tiles),
            in_specs=[
                pl.BlockSpec(
                    (block, tile),
                    lambda h, j, d: (0, ((1 - d[0]) * (1 - h) + d[0] * h) * tiles + j),
                ),
                pl.BlockSpec((block, columns), lambda h, j, d: (0, 0)),
            ]
            + [pl.BlockSpec(memory_space=pl.ANY)] * len(others),
            out_specs=[
                pl.BlockSpec((tile, columns), lambda h, j, d: (j * (1 - h) + (tiles - 1) * h, 0)),
                pl.BlockSpec((tile, columns), lambda h, j, d: (j * h, 0)),
            ],
        ),
        out_shape=[half, half],
        compiler_params=params(),
        cost_estimate=cost(2 * block * rows * columns, 6e6),
    )(d, a, b, *others)


def split_low(value):
    high = value.astype(LOW)
    return high, (value - high.astype(F32)).astype(LOW)


def norm_parts(rows):
    rr = lax.rsqrt(jnp.mean(rows * rows, axis=-1, keepdims=True) + EPS)
    return rows * rr, rr


def norm_back(grad, normal, rr, gain):
    weighted = grad * gain
    return rr * (weighted - normal * jnp.mean(weighted * normal, axis=-1, keepdims=True))


def add_all(refs):
    return functools.reduce(jnp.add, [ref[...].astype(F32) for ref in refs])


def pad_rows(rows, count):
    if rows.shape[0] == count:
        return rows
    return jnp.concatenate(
        [rows, jnp.zeros((count - rows.shape[0], rows.shape[1]), rows.dtype)], axis=0
    )


def router_kernel(experts, *refs):
    x_ref, attn_ref, gain_ref, router_ref, mask_ref = refs[:5]
    hidden_ref, mixed_ref, probs_ref = refs[-3:]
    width = x_ref.shape[1]
    lanes = mask_ref.shape[1]
    hidden = add_all([x_ref, attn_ref])
    hidden_ref[...] = hidden
    mixed = (norm_parts(hidden)[0] * gain_ref[...]).astype(LOW)
    mixed_ref[:, :width] = mixed
    logits = dot_nt(mixed, pad_rows(router_ref[...], lanes))
    lane = lax.broadcasted_iota(jnp.int32, logits.shape, 1)
    logits = jnp.where(lane < experts, logits, -1e30)
    weights = jnp.exp(logits - jnp.max(logits, axis=1, keepdims=True))
    probs = weights / jnp.sum(weights, axis=1, keepdims=True)
    probs_ref[...] = probs
    chosen = probs * mask_ref[...]
    high, low = split_low(chosen / jnp.sum(chosen, axis=1, keepdims=True))
    both = high.astype(F32) + pltpu.roll(low.astype(F32), experts, 1)
    mixed_ref[:, width:] = both.astype(LOW)


def route_rows(x, attn, gain, router, mask, experts, others):
    tokens, width = x.shape
    lanes = mask.shape[1]
    operands = [x, attn, gain[None], router, mask]
    shapes = [
        jax.ShapeDtypeStruct((tokens, width), F32),
        jax.ShapeDtypeStruct((tokens, width + lanes), LOW),
        jax.ShapeDtypeStruct((tokens, lanes), F32),
    ]
    return pl.pallas_call(
        functools.partial(router_kernel, experts),
        grid=(1,),
        in_specs=[full(value.shape) for value in operands]
        + [pl.BlockSpec(memory_space=pl.ANY)] * len(others),
        out_specs=[full(shape.shape) for shape in shapes],
        out_shape=shapes,
        compiler_params=params(),
        cost_estimate=cost(2 * tokens * width * lanes, 5e6),
    )(*operands, *others)


def one_hot(slots, count, first):
    groups, tokens = slots.shape
    slot = lax.broadcasted_iota(jnp.int32, (groups, count, tokens), 1).astype(F32)
    same = slots[:, None, :] == slot + float(first)
    return jnp.where(same, 1.0, 0.0).reshape(groups * count, tokens)


def slot_kernel(capacity, meta_ref, col_ref, rows_ref, slots_ref):
    groups, block = slots_ref.shape
    rows, width = rows_ref.shape
    n = rows // groups // capacity
    tokens = block // n
    mask = col_ref[:, width:]
    lanes = mask.shape[1]
    padded = -(-groups // 16) * 16
    group = lax.broadcasted_iota(jnp.int32, (padded, lanes), 0)
    lane = lax.broadcasted_iota(jnp.int32, (padded, lanes), 1)
    wanted = jnp.logical_and(lane == group * n + meta_ref[0], group < groups)
    hits = dot_nt(jnp.where(wanted, 1.0, 0.0).astype(LOW), mask)
    before = lax.broadcasted_iota(jnp.int32, (tokens, tokens), 0)
    after_it = lax.broadcasted_iota(jnp.int32, (tokens, tokens), 1)
    earlier = jnp.where(before < after_it, 1.0, 0.0).astype(LOW)
    for z in range(n):
        hit = hits[:, z * tokens : (z + 1) * tokens]
        rank = dot_nn(hit.astype(LOW), earlier)
        turn = (meta_ref[1 + z] * capacity).astype(F32)
        slot = jnp.where(hit > 0.5, rank + turn, -1.0)
        slots_ref[:, z * tokens : (z + 1) * tokens] = slot[:groups]
    spread = one_hot(slots_ref[...], n * capacity, 0).astype(LOW)
    rows_ref[...] = dot_nn(spread, col_ref[:, :width]).astype(LOW)


def make_slots(meta, col, width, groups, capacity):
    block = col.shape[0]
    n = lax.axis_size("expert")
    shapes = [
        jax.ShapeDtypeStruct((groups * n * capacity, width), LOW),
        jax.ShapeDtypeStruct((groups, block), F32),
    ]
    return pl.pallas_call(
        functools.partial(slot_kernel, capacity),
        grid_spec=pltpu.PrefetchScalarGridSpec(
            num_scalar_prefetch=1,
            grid=(1,),
            in_specs=[full(col.shape)],
            out_specs=[full(shape.shape) for shape in shapes],
        ),
        out_shape=shapes,
        compiler_params=params(),
        cost_estimate=cost(2 * groups * n * capacity * block * width, 8e6),
    )(meta, col)


def table_kernel(capacity, n_half, meta_ref, slots_ref, near_ref, far_ref, near_back_ref, far_back_ref):
    n = 2 * n_half
    tokens = slots_ref.shape[1] // n
    cap_half = n_half * capacity
    for part, (to_ref, back_ref) in enumerate([(near_ref, near_back_ref), (far_ref, far_back_ref)]):
        pieces = []
        for k in range(n_half):
            start = pl.multiple_of(meta_ref[1 + n + part * n_half + k] * tokens, tokens)
            pieces.append(slots_ref[:, pl.ds(start, tokens)])
        spread = one_hot(jnp.concatenate(pieces, axis=1), cap_half, part * cap_half)
        to_ref[...] = spread.astype(LOW)
        back_ref[...] = jnp.transpose(spread).astype(LOW)


def make_tables(meta, slots, n_half, capacity):
    groups, block = slots.shape
    rows = groups * n_half * capacity
    shapes = [jax.ShapeDtypeStruct((rows, block // 2), LOW)] * 2
    shapes += [jax.ShapeDtypeStruct((block // 2, rows), LOW)] * 2
    outs = pl.pallas_call(
        functools.partial(table_kernel, capacity, n_half),
        grid_spec=pltpu.PrefetchScalarGridSpec(
            num_scalar_prefetch=1,
            grid=(1,),
            in_specs=[full(slots.shape)],
            out_specs=[full(shape.shape) for shape in shapes],
        ),
        out_shape=shapes,
        compiler_params=params(),
        cost_estimate=cost(8 * rows * block, 3e6),
    )(meta, slots)
    return outs[:2], outs[2:]


def spread_kernel(choices, place_ref, spread_ref, *refs):
    out_ref, rows_ref = refs[-2:]
    for k, by_place in enumerate(choices):
        for which in sorted(set(by_place)):
            hit = functools.reduce(
                jnp.logical_or,
                [place_ref[0] == i for i, other in enumerate(by_place) if other == which],
            )

            @pl.when(hit)
            def _():
                tokens = refs[which].shape[0]
                rows_ref[k * tokens : (k + 1) * tokens] = refs[which][...]

    out_ref[...] = dot_nn(spread_ref[...], rows_ref[...]).astype(LOW)


def spread_rows(place, spread, found, turns, others):
    n = lax.axis_size("expert")
    order = arrival_order(n)
    distances = sorted({order[i][turn] - i for i in range(n) for turn in turns})
    choices = [[distances.index(order[i][turn] - i) for i in range(n)] for turn in turns]
    chunks = [found[distance] for distance in distances]
    tokens, wide = chunks[0].shape
    rows = spread.shape[0]
    return pl.pallas_call(
        functools.partial(spread_kernel, choices),
        grid_spec=pltpu.PrefetchScalarGridSpec(
            num_scalar_prefetch=1,
            grid=(1,),
            in_specs=[full(spread.shape)]
            + [full(chunk.shape) for chunk in chunks]
            + [pl.BlockSpec(memory_space=pl.ANY)] * len(others),
            out_specs=full((rows, wide)),
            scratch_shapes=[pltpu.VMEM((len(turns) * tokens, wide), LOW)],
        ),
        out_shape=jax.ShapeDtypeStruct((rows, wide), LOW),
        compiler_params=params(),
        cost_estimate=cost(2 * rows * len(turns) * tokens * wide, 5e6),
    )(place, spread, *chunks, *others)


def router_back_kernel(experts, *refs):
    sum_ref, g_ref, hidden_ref, gain_ref, router_ref, mask_ref, probs_ref = refs[:7]
    grad_ref, low_ref, dgain_ref, drouter_ref = refs[-4:]
    width = g_ref.shape[1]
    lanes = mask_ref.shape[1]
    total = sum_ref[...].astype(F32)
    table = total[:, width:]
    mask, probs = mask_ref[...], probs_ref[...]
    grad_gates = (table + pltpu.roll(table, lanes - experts, 1)) * mask
    chosen = probs * mask
    chosen_sum = jnp.sum(chosen, axis=1, keepdims=True)
    mean = jnp.sum(grad_gates * (chosen / chosen_sum), axis=1, keepdims=True)
    centred = mask * (grad_gates - mean) / chosen_sum
    grad_logits = probs * (centred - jnp.sum(centred * chosen, axis=1, keepdims=True))
    high, low = split_low(grad_logits)
    router = pad_rows(router_ref[...], lanes)
    grad = total[:, :width] + dot_nn(high, router) + dot_nn(low, router)
    normal, rr = norm_parts(hidden_ref[...])
    mixed = (normal * gain_ref[...]).astype(LOW)
    drouter_ref[...] = dot_tn(high, mixed) + dot_tn(low, mixed)
    dgain_ref[...] = jnp.sum(grad * normal, axis=0, keepdims=True)
    grad_hidden = g_ref[...].astype(F32) + norm_back(grad, normal, rr, gain_ref[...])
    grad_ref[...] = grad_hidden
    low_ref[...] = grad_hidden.astype(LOW)


def route_back(summed, g, hidden, gain, router, mask, probs, experts, others):
    tokens, width = g.shape
    lanes = mask.shape[1]
    operands = [summed, g, hidden, gain[None], router, mask, probs]
    shapes = [
        jax.ShapeDtypeStruct((tokens, width), F32),
        jax.ShapeDtypeStruct((tokens, width), LOW),
        jax.ShapeDtypeStruct((1, width), F32),
        jax.ShapeDtypeStruct((lanes, width), F32),
    ]
    return pl.pallas_call(
        functools.partial(router_back_kernel, experts),
        grid=(1,),
        in_specs=[full(value.shape) for value in operands]
        + [pl.BlockSpec(memory_space=pl.ANY)] * len(others),
        out_specs=[full(shape.shape) for shape in shapes],
        out_shape=shapes,
        compiler_params=params(),
        cost_estimate=cost(8 * tokens * width * lanes, 8e6),
    )(*operands, *others)


def combine_kernel(meta_ref, table_ref, rows_ref, *rest):
    del meta_ref
    rest[-1][...] = dot_nn(table_ref[...], rows_ref[...]).astype(LOW)


def combine_part(meta, table, rows, first, n, into, others):
    block, slots = table.shape
    wide = rows.shape[1]
    tokens = block // (n // 2)
    return pl.pallas_call(
        combine_kernel,
        grid_spec=pltpu.PrefetchScalarGridSpec(
            num_scalar_prefetch=1,
            grid=(n // 2,),
            in_specs=[
                pl.BlockSpec((tokens, slots), lambda i, m: (i, 0)),
                full(rows.shape),
            ]
            + [pl.BlockSpec(memory_space=pl.ANY)] * (len(into) + len(others)),
            out_specs=pl.BlockSpec((tokens, wide), lambda i, m: (m[1 + n + first + i], 0)),
        ),
        out_shape=jax.ShapeDtypeStruct((n * tokens, wide), LOW),
        input_output_aliases={3: 0} if into else {},
        compiler_params=params(),
        cost_estimate=cost(2 * slots * block * wide, 6e6),
    )(meta, table, rows, *into, *others)


def combine_rows(meta, tables, rows, n_half, others):
    near = combine_part(meta, tables[0], rows[0], 0, 2 * n_half, [], [])
    return combine_part(meta, tables[1], rows[1], n_half, 2 * n_half, [near], others)


def expert_kernel(experts, who_ref, x_ref, gate_ref, up_ref, pull_ref, *rest):
    act_ref, dgate_ref, dup_ref, copy_ref = rest[-4:]
    width = gate_ref.shape[0]
    x = x_ref[:, :width]
    table = x_ref[:, width:].astype(F32)
    lane = lax.broadcasted_iota(jnp.int32, table.shape, 1)
    mine = who_ref[0]
    gate = jnp.sum(
        jnp.where(jnp.logical_or(lane == mine, lane == mine + experts), table, 0.0),
        axis=1,
        keepdims=True,
    )
    pre_gate = dot_nn(x, gate_ref[...])
    pre_up = dot_nn(x, up_ref[...])
    pull = pull_ref[...].reshape(pre_up.shape)
    sig = 1.0 / (1.0 + jnp.exp(-pre_gate))
    silu = pre_gate * sig
    act = silu * pre_up
    act_ref[...] = (act * gate).astype(LOW)
    high, low = split_low(jnp.sum(act * pull, axis=1, keepdims=True))
    pull = pull * gate
    dup = (pull * silu).astype(LOW)
    dgate = (pull * pre_up * (sig * (1.0 + pre_gate * (1.0 - sig)))).astype(LOW)
    dgate_ref[...] = dgate
    dup_ref[...] = dup
    copy_ref[:, :width] = (dot_nt(dgate, gate_ref[...]) + dot_nt(dup, up_ref[...])).astype(LOW)
    back = jnp.where(lane == mine, high.astype(F32), 0.0)
    back = jnp.where(lane == mine + experts, low.astype(F32), back)
    copy_ref[:, width:] = back.astype(LOW)


def run_expert(who, x, w_gate, w_up, pull, part, experts):
    rows, wide = x.shape
    width, hidden = w_gate.shape
    groups, _, slots, _ = pull.shape
    each = groups // 2
    tile = each * slots
    by_rows = lambda columns: pl.BlockSpec((tile, columns), lambda i, p: (i, 0))
    return pl.pallas_call(
        functools.partial(expert_kernel, experts),
        grid_spec=pltpu.PrefetchScalarGridSpec(
            num_scalar_prefetch=1,
            grid=(2,),
            in_specs=[
                by_rows(wide),
                full(w_gate.shape),
                full(w_up.shape),
                pl.BlockSpec((each, 1, slots, hidden), lambda i, p: (i, part, 0, 0)),
            ],
            out_specs=[by_rows(hidden), by_rows(hidden), by_rows(hidden), by_rows(wide)],
        ),
        out_shape=[jax.ShapeDtypeStruct((rows, hidden), LOW)] * 3
        + [jax.ShapeDtypeStruct((rows, wide), LOW)],
        compiler_params=params(),
        cost_estimate=cost(8 * rows * width * hidden, 20e6, rows * hidden),
    )(who, x, w_gate, w_up, pull)


def input_kernel(grad_ref, x_ref, gain_ref, more_ref, out_ref):
    normal, rr = norm_parts(x_ref[...].astype(F32))
    grad = grad_ref[...].astype(F32)
    out_ref[...] = more_ref[...] + norm_back(grad, normal, rr, gain_ref[...])


def input_back(grad, x, gain, more):
    tokens, width = x.shape
    operands = [grad, x, gain[None], more]
    return pl.pallas_call(
        input_kernel,
        grid=(1,),
        in_specs=[full(value.shape) for value in operands],
        out_specs=full(more.shape),
        out_shape=jax.ShapeDtypeStruct((tokens, width), F32),
        compiler_params=params(),
        cost_estimate=cost(20 * tokens * width, 5e6),
    )(*operands)


def kv_back_kernel(factor, parts_ref, proj_ref, gain_ref, cos_ref, sin_ref, *rest):
    grad_ref, dgain_ref = rest[-2:]
    size = proj_ref.shape[1]
    total = parts_ref[0].astype(F32)
    for k in range(1, parts_ref.shape[0]):
        total += parts_ref[k].astype(F32)
    grad, dgain = head_backward(
        total[:, :size] * factor, proj_ref[...], gain_ref[...], cos_ref[...], sin_ref[...]
    )
    grad_ref[:, :size] = grad.astype(LOW)
    grad_ref[:, size:] = total[:, size:].astype(LOW)
    dgain_ref[...] = dgain


def kv_back(parts, proj, gain, cos2, sin2, factor, others):
    block, size = proj.shape
    operands = [parts, proj, gain[None], cos2, sin2]
    shapes = [
        jax.ShapeDtypeStruct((block, 2 * size), LOW),
        jax.ShapeDtypeStruct((1, size), F32),
    ]
    return pl.pallas_call(
        functools.partial(kv_back_kernel, factor),
        grid=(1,),
        in_specs=[full(value.shape) for value in operands]
        + [pl.BlockSpec(memory_space=pl.ANY)] * len(others),
        out_specs=[full(shape.shape) for shape in shapes],
        out_shape=shapes,
        compiler_params=params(),
        cost_estimate=cost(40 * block * size, 5e6),
    )(*operands, *others)


def unpack_kernel(experts, small_ref, *rest):
    router_ref, attn_ref, mlp_ref, q_ref, k_ref = rest[-5:]
    rows = small_ref[...].astype(F32)
    size = q_ref.shape[1]
    router_ref[...] = rows[:experts]
    attn_ref[...] = rows[experts : experts + 1]
    mlp_ref[...] = rows[experts + 1 : experts + 2]
    q_ref[...] = rows[experts + 2 : experts + 3, :size]
    k_ref[...] = rows[experts + 2 : experts + 3, size : 2 * size]


def unpack_small(small, experts, size, others):
    width = small.shape[1]
    shapes = [(experts, width), (1, width), (1, width), (1, size), (1, size)]
    return pl.pallas_call(
        functools.partial(unpack_kernel, experts),
        grid=(1,),
        in_specs=[full(small.shape)] + [pl.BlockSpec(memory_space=pl.ANY)] * len(others),
        out_specs=[full(shape) for shape in shapes],
        out_shape=[jax.ShapeDtypeStruct(shape, F32) for shape in shapes],
        compiler_params=params(),
        cost_estimate=cost(experts * width, 6 * experts * width),
    )(small, *others)


def pair_kernel(a_ref, b_ref, *rest):
    rest[-1][...] = (a_ref[...].astype(F32) + b_ref[...].astype(F32)).astype(LOW)


def pair_sum(a, b, others):
    rows, columns = a.shape
    tiles = 2 if rows % 32 == 0 else 1
    spec = pl.BlockSpec((rows // tiles, columns), lambda i: (i, 0))
    return pl.pallas_call(
        pair_kernel,
        grid=(tiles,),
        in_specs=[spec, spec] + [pl.BlockSpec(memory_space=pl.ANY)] * len(others),
        out_specs=spec,
        out_shape=jax.ShapeDtypeStruct((rows, columns), LOW),
        compiler_params=params(),
        cost_estimate=cost(rows * columns, 6 * rows * columns),
    )(a, b, *others)


def fold_kernel(n_pairs, s_ref, *refs):
    del s_ref
    send_ref, keep_ref = refs[-2:]
    totals = [
        (refs[2 * k][...].astype(F32) + refs[2 * k + 1][...].astype(F32)).astype(LOW)
        for k in range(n_pairs)
    ]
    for half, out_ref in enumerate((send_ref, keep_ref)):

        @pl.when(pl.program_id(0) == half)
        def _():
            first = 0
            for total in totals:
                last = first + total.shape[1]
                out_ref[:, first:last] = total
                first = last


def fold(pairs, bit, others):
    rows = pairs[0][1].shape[0]
    columns = sum(got.shape[1] for _, got in pairs)
    tiles = 2
    tile = rows // (2 * tiles)
    side = lambda h, m: (1 - m[0]) * (1 - h) + m[0] * h
    specs = []
    for _, got in pairs:
        wide = got.shape[1]
        specs += [pl.BlockSpec((tile, wide), lambda h, j, m: (side(h, m) * tiles + j, 0))] * 2
    shape = jax.ShapeDtypeStruct((rows // 2, columns), LOW)
    return pl.pallas_call(
        functools.partial(fold_kernel, len(pairs)),
        grid_spec=pltpu.PrefetchScalarGridSpec(
            num_scalar_prefetch=1,
            grid=(2, tiles),
            in_specs=specs + [pl.BlockSpec(memory_space=pl.ANY)] * len(others),
            out_specs=[
                pl.BlockSpec((tile, columns), lambda h, j, m: (j * (1 - h) + (tiles - 1) * h, 0)),
                pl.BlockSpec((tile, columns), lambda h, j, m: (j * h, 0)),
            ],
        ),
        out_shape=[shape, shape],
        compiler_params=params(),
        cost_estimate=cost(rows * columns, 6 * rows * columns),
    )(
        bit.astype(jnp.int32)[None],
        *[value for pair in pairs for value in pair],
        *others,
    )


def normed_kernel(q_ref, kv_ref, wq_ref, wkv_ref, rows_ref, *rest):
    out_ref, dgain_ref = rest[-2:]
    grad = dot_nt(q_ref[...], wq_ref[...]) + dot_nt(kv_ref[...], wkv_ref[...])
    out_ref[...] = grad.astype(LOW)
    dgain_ref[...] = jnp.sum(grad * rows_ref[...].astype(F32), axis=0, keepdims=True)


def normed_back(grad_q, grad_kv, w_q, w_kv, rows, others):
    block, width = rows.shape
    tile = 512
    column = lambda i: (0, i)
    return pl.pallas_call(
        normed_kernel,
        grid=(width // tile,),
        in_specs=[
            full(grad_q.shape),
            full(grad_kv.shape),
            pl.BlockSpec((tile, w_q.shape[1]), lambda i: (i, 0)),
            pl.BlockSpec((tile, w_kv.shape[1]), lambda i: (i, 0)),
            pl.BlockSpec((block, tile), column),
        ]
        + [pl.BlockSpec(memory_space=pl.ANY)] * len(others),
        out_specs=[pl.BlockSpec((block, tile), column), pl.BlockSpec((1, tile), column)],
        out_shape=[
            jax.ShapeDtypeStruct((block, width), LOW),
            jax.ShapeDtypeStruct((1, width), F32),
        ],
        compiler_params=params(),
        cost_estimate=cost(2 * block * width * (w_q.shape[1] + w_kv.shape[1]), 12e6),
    )(grad_q, grad_kv, w_q, w_kv, rows, *others)


def pack_kernel(experts, router_ref, attn_ref, gain_ref, mlp_ref, q_ref, k_ref, *rest):
    out_ref, rows_ref = rest[-2:]
    size = q_ref.shape[1]
    rows_ref[:experts] = router_ref[:experts]
    rows_ref[experts:] = jnp.zeros_like(rows_ref[experts:])
    rows_ref[experts : experts + 1] = attn_ref[...] / gain_ref[...]
    rows_ref[experts + 1 : experts + 2] = mlp_ref[...]
    rows_ref[experts + 2 : experts + 3, :size] = q_ref[...]
    rows_ref[experts + 2 : experts + 3, size : 2 * size] = k_ref[...]
    out_ref[...] = rows_ref[...].astype(LOW)


def pack_small(experts, router, attn, gain, mlp, q, k, others):
    width = attn.shape[1]
    n = lax.axis_size(ALL_AXES)
    shape = (-(-(experts + 3) // n) * n, width)
    operands = [router, attn, gain[None], mlp, q, k]
    return pl.pallas_call(
        functools.partial(pack_kernel, experts),
        grid=(1,),
        in_specs=[full(value.shape) for value in operands]
        + [pl.BlockSpec(memory_space=pl.ANY)] * len(others),
        out_specs=full(shape),
        out_shape=jax.ShapeDtypeStruct(shape, LOW),
        scratch_shapes=[pltpu.VMEM(shape, F32)],
        compiler_params=params(),
        cost_estimate=cost(shape[0] * width, 6 * shape[0] * width),
    )(*operands, *others)


def part_sum_kernel(parts_ref, *rest):
    total = parts_ref[0].astype(F32)
    for k in range(1, parts_ref.shape[0]):
        total += parts_ref[k].astype(F32)
    rest[-1][...] = total.astype(LOW)


def part_sum(parts, others):
    count, rows, columns = parts.shape
    tiles = 2
    return pl.pallas_call(
        part_sum_kernel,
        grid=(tiles,),
        in_specs=[pl.BlockSpec((count, rows // tiles, columns), lambda i: (0, i, 0))]
        + [pl.BlockSpec(memory_space=pl.ANY)] * len(others),
        out_specs=pl.BlockSpec((rows // tiles, columns), lambda i: (i, 0)),
        out_shape=jax.ShapeDtypeStruct((rows, columns), LOW),
        compiler_params=params(),
        cost_estimate=cost(count * rows * columns, 4 * count * rows * columns),
    )(parts, *others)


def widen_kernel(n_chunks, n_outs, at_ref, *refs):
    del at_ref
    outs = refs[-n_outs:]
    widths = [ref.shape[1] for ref in outs]
    for k in range(n_chunks):

        @pl.when(pl.program_id(0) == k)
        def _():
            first = 0
            for wide, out_ref in zip(widths, outs):
                out_ref[...] = refs[k][:, first : first + wide].astype(F32)
                first += wide


def widen(places, chunks, widths, total, others):
    rows, columns = chunks[0].shape
    count = len(chunks)
    return pl.pallas_call(
        functools.partial(widen_kernel, count, len(widths)),
        grid_spec=pltpu.PrefetchScalarGridSpec(
            num_scalar_prefetch=1,
            grid=(count,),
            in_specs=[full(chunk.shape) for chunk in chunks]
            + [pl.BlockSpec(memory_space=pl.ANY)] * len(others),
            out_specs=[pl.BlockSpec((rows, wide), lambda i, at: (at[i], 0)) for wide in widths],
        ),
        out_shape=[jax.ShapeDtypeStruct((total, wide), F32) for wide in widths],
        compiler_params=params(),
        cost_estimate=cost(rows * columns, 6 * count * rows * columns),
    )(jnp.stack(places).astype(jnp.int32), *chunks, *others)


def swap_dp(rows):
    return lax.ppermute(rows, "dp", [(0, 1), (1, 0)])


def swap_context(rows, s):
    n = lax.axis_size("context")
    return lax.ppermute(rows, "context", [(i, i ^ s) for i in range(n)])


def share_context(parts):
    return lax.all_to_all(parts, "context", split_axis=0, concat_axis=0, tiled=True)


def plane_turns():
    d, c = lax.axis_index("dp"), lax.axis_index("context")
    low, high = lax.rem(c, 2), lax.div(c, 2)

    def swap(first, second):
        perm = [(i, i ^ first) for i in range(4)] + [(4 + i, 4 + (i ^ second)) for i in range(4)]
        return lambda rows: lax.ppermute(rows, GROUP_AXES, perm)

    return [
        (jnp.where(d == 0, low, high), swap(1, 2)),
        (jnp.where(d == 0, high, low), swap(2, 1)),
    ]


def plane_first(pairs, others):
    (bit_1, _), _ = plane_turns()
    return fold(pairs, bit_1, others)


def plane_second(send, keep, others):
    (_, swap_1), (bit_2, _) = plane_turns()
    return fold([(keep, swap_1(send))], bit_2, others)


def plane_last(send, keep, others):
    _, (_, swap_2) = plane_turns()
    return pair_sum(keep, swap_2(send), others)


def plane_spread(own):
    (_, swap_1), (_, swap_2) = plane_turns()
    second = swap_2(own)
    return [own, second, swap_1(own), swap_1(second)]


def quarter_places(rank):
    d = lax.axis_index("dp")
    c = lax.axis_index("context")
    low, high = lax.rem(c, 2), lax.div(c, 2)
    places = []
    for core in (d, 1 - d):
        bit_1 = jnp.where(core == 0, low, high)
        bit_2 = jnp.where(core == 0, high, low)
        for flip_1, flip_2 in ((0, 0), (0, 1), (1, 0), (1, 1)):
            places.append(4 * core + rank(core, bit_1 ^ flip_1, bit_2 ^ flip_2))
    return places


def widen_all(quarters, places, widths, others):
    count = len(quarters)
    total = 2 * count * quarters[0].shape[0]
    chunks = quarters + [swap_dp(part) for part in quarters]
    return widen(places, chunks, widths, total, others)


def arrival_order(n):
    return [sorted(range(n), key=lambda j: (abs(j - i), j)) for i in range(n)]


def choose(index, options):
    distinct = []
    for option in options:
        if option is not None and not any(option is other for other in distinct):
            distinct.append(option)
    result = distinct[0]
    for option in distinct[1:]:
        mask = functools.reduce(
            jnp.logical_or, [index == i for i, other in enumerate(options) if other is option]
        )
        result = jnp.where(mask, option, result)
    return result


def line_gather(chunk):
    return line_steps({0: chunk}, 1, lax.axis_size("expert"))


def line_steps(found, first, stop):
    n = lax.axis_size("expert")
    found = dict(found)
    for s in range(first, stop):
        found[-s] = lax.ppermute(
            found[1 - s], "expert", [(i, i + 1) for i in range(s - 1, n - 1)]
        )
        found[s] = lax.ppermute(found[s - 1], "expert", [(i + 1, i) for i in range(n - s)])
    return found


def context_gather(rows):
    n = lax.axis_size("context")
    c = lax.axis_index("context")
    found = {0: rows}
    for s in range(1, n):
        found[s] = lax.ppermute(rows, "context", [(i, i ^ s) for i in range(n)])
    return jnp.concatenate([choose(c, [found[i ^ j] for i in range(n)]) for j in range(n)], axis=0)


def zero_of(*others):
    return functools.reduce(
        jnp.add,
        [
            lax.slice(other, (0,) * other.ndim, (1,) * other.ndim).reshape(()).astype(F32) * 0.0
            for other in others
        ],
    )


def after(value, *others):
    return (value.astype(F32) + zero_of(*others)).astype(value.dtype)


def on_device(
    layer_input,
    grad_output,
    attn_gain,
    query_weight,
    key_weight,
    value_weight,
    q_gain,
    k_gain,
    output_weight,
    mlp_gain,
    router,
    w_gate,
    w_up,
    w_down,
    routes,
    half_order,
):
    n_context = lax.axis_size("context")
    n_expert = lax.axis_size("expert")
    n_groups = lax.axis_size(GROUP_AXES)
    tok_dev, width = layer_input.shape[1:]
    size = q_gain.shape[0]
    kv_total = key_weight.shape[1] * n_expert
    group_dev = n_expert // (kv_total // size)
    kv_index = lax.axis_index("expert") // group_dev
    block = tok_dev * n_expert
    seq = block * n_context
    half = block // 2
    experts = router.shape[1]
    exp_dev = w_gate.shape[0]
    top = routes.shape[2]
    capacity = max(2, (tok_dev * top * 9 + 8 * experts - 1) // (8 * experts))
    scale = size ** (-0.5)

    seq_rows = jnp.arange(seq, dtype=jnp.int32)
    context = lax.axis_index("context")
    own_halves = lax.dynamic_slice_in_dim(half_order, 2 * context, 2)
    own_pos = (own_halves[:, None] * half + jnp.arange(half, dtype=jnp.int32)[None]).reshape(-1)
    per_half = half // TILE
    tile_pos = (half_order[:, None] * per_half + jnp.arange(per_half, dtype=jnp.int32)).reshape(-1)
    kidx = jnp.sum(
        (tile_pos[None, :] == jnp.arange(seq // TILE, dtype=jnp.int32)[:, None])
        * jnp.arange(seq // TILE, dtype=jnp.int32)[None, :],
        axis=1,
    ).astype(jnp.int32)
    qpos = lax.dynamic_slice_in_dim(tile_pos, context * (block // TILE), block // TILE)
    entry = jnp.arange(size)
    freq = jnp.power(THETA, -(2 * (entry % (size // 2))).astype(F32) / size)
    angles = own_pos.astype(F32)[:, None] * freq[None, :]
    cos2 = jnp.cos(angles)
    sin2 = jnp.sin(angles) * jnp.where(entry < size // 2, -1.0, 1.0)[None, :]

    place = lax.axis_index("expert")
    place_1 = place.astype(jnp.int32)[None]
    lanes = -(-2 * experts // 128) * 128
    mask = jnp.any(
        routes[0][:, :, None] == jnp.arange(lanes, dtype=jnp.int32)[None, None, :], axis=1
    )
    mask_wide = mask.astype(F32)
    router_rows = router.T

    x_low = layer_input[0]
    x_normal, _ = norm_parts(x_low.astype(F32))
    normed_found = line_gather((x_normal * attn_gain).astype(LOW))
    if group_dev == 1:
        kv_weights = jnp.concatenate([key_weight, value_weight], axis=1)
    else:
        key_whole = lax.all_gather(key_weight, "expert", axis=1, tiled=True)
        value_whole = lax.all_gather(value_weight, "expert", axis=1, tiled=True)
        kv_weights = jnp.concatenate(
            [
                lax.dynamic_slice_in_dim(key_whole, kv_index * size, size, 1),
                lax.dynamic_slice_in_dim(value_whole, kv_index * size, size, 1),
            ],
            axis=1,
        )
    grad_low = grad_output[0]
    normed_rows, own_kv, key_proj, grad_wide = project_keys(
        place_1,
        normed_found,
        kv_weights,
        k_gain,
        cos2,
        sin2,
        scale * LOG2E,
        grad_low,
        mask_wide,
    )
    grad_col = lax.all_gather(grad_wide, "expert", axis=0, tiled=True)
    kv_whole = context_gather(own_kv)
    queries, query_proj = project_queries(normed_rows, query_weight, q_gain, cos2, sin2)

    n_half = n_expert // 2
    order_here = jnp.asarray(arrival_order(n_expert), jnp.int32)[place]
    turn_here = jnp.sum(
        (order_here[:, None] == jnp.arange(n_expert, dtype=jnp.int32)[None, :])
        * jnp.arange(n_expert, dtype=jnp.int32)[:, None],
        axis=0,
    ).astype(jnp.int32)
    meta = jnp.concatenate([place_1, turn_here, order_here])
    grad_sent, slots = make_slots(meta, grad_col, width, n_groups, capacity)
    spreads, back_tables = make_tables(meta, slots, n_half, capacity)

    def swap_plane(rows):
        parts = rows.reshape(n_groups, -1, rows.shape[1])
        parts = lax.all_to_all(parts, GROUP_AXES, split_axis=0, concat_axis=0, tiled=True)
        return parts.reshape(rows.shape)

    attended, inverse = attend(qpos, kidx, queries, kv_whole, [])
    keys_t = kv_whole[:, :size].T
    attn_part = out_dot(attended, output_weight, [grad_col])
    attn_rows = lax.psum_scatter(attn_part, "expert", scatter_dimension=0, tiled=True)

    grad_x = swap_plane(grad_sent)
    act_pull = dot_nt(grad_x, w_down[0]).reshape(n_groups, 2, n_half * capacity, -1)

    hidden, mixed, probs = route_rows(
        x_low, attn_rows, mlp_gain, router_rows, mask_wide, experts, [keys_t]
    )

    who = (lax.axis_index(ALL_AXES) * exp_dev).astype(jnp.int32)[None]
    mixed_found = line_gather(mixed)
    near = spread_rows(place_1, spreads[0], mixed_found, range(n_half), [grad_x])
    x_near = swap_plane(near)
    worked_near = run_expert(who, x_near, w_gate[0], w_up[0], act_pull, 0, experts)
    far = spread_rows(place_1, spreads[1], mixed_found, range(n_half, n_expert), [x_near])
    x_far = swap_plane(far)
    worked_far = run_expert(who, x_far, w_gate[0], w_up[0], act_pull, 1, experts)
    xs = [x_near, x_far]
    acts, gate_lows, up_lows, copies = (list(pair) for pair in zip(worked_near, worked_far))
    back_far = swap_plane(copies[1])
    back_near = swap_plane(copies[0])
    join = lambda parts: jnp.concatenate(parts, axis=0)
    x_all = join([x[:, :width] for x in xs])
    grad_w_gate = dot_tn(x_all, join(gate_lows))
    grad_w_up = dot_tn(x_all, join(up_lows))
    grad_by_round = jnp.swapaxes(
        grad_x.reshape(n_groups, 2, n_half * capacity, width), 0, 1
    ).reshape(-1, width)
    grad_w_down = dot_tn(join(acts), grad_by_round)
    copies_col = combine_rows(
        meta, back_tables, [back_near, back_far], n_half, [grad_w_gate, grad_w_up]
    )
    copies_sum = lax.psum_scatter(copies_col, "expert", scatter_dimension=0, tiled=True)

    returned = [dot_nn(act, w_down[0]).astype(LOW) for act in acts]
    returned_near = swap_plane(returned[0])

    grad_hidden, grad_hidden_low, grad_mlp_gain, grad_router = route_back(
        copies_sum,
        grad_low,
        hidden,
        mlp_gain,
        router_rows,
        mask_wide,
        probs,
        experts,
        [returned_near, grad_w_down],
    )

    returned_far = swap_plane(returned[1])
    grad_attn = lax.all_gather(grad_hidden_low, "expert", axis=0, tiled=True)
    grad_o, centre = grad_attended(
        grad_attn, output_weight, attended, inverse, [returned_far]
    )
    combined = combine_rows(meta, back_tables, [returned_near, returned_far], n_half, [])
    output_rows = lax.psum_scatter(combined, "expert", scatter_dimension=0, tiled=True)
    w_out_send, w_out_keep = token_halves(attended, grad_attn, [combined])
    w_out_half = pair_sum(w_out_keep, swap_dp(w_out_send), [grad_o])
    w_out_parts = share_context(w_out_half.reshape(n_context, -1, width))
    grad_kv, grad_q, grad_q_gain = attend_back(
        qpos,
        kidx,
        queries,
        grad_o,
        centre,
        kv_whole,
        keys_t,
        query_proj,
        q_gain,
        cos2,
        sin2,
        [w_out_half],
    )
    kv_parts = share_context(grad_kv.astype(LOW).reshape(n_context, block, 2 * size))
    w_out_own = part_sum(w_out_parts, [grad_kv])
    w_query_send, w_query_keep = token_halves(normed_rows, grad_q, [w_out_own])
    w_query_got = swap_dp(w_query_send)
    output_rows = hidden + output_rows.astype(F32) + zero_of(w_query_keep)

    kv_grads, grad_k_gain = kv_back(
        kv_parts, key_proj, k_gain, cos2, sin2, scale, [w_query_keep]
    )
    w_out_quarters = plane_spread(w_out_own)
    pairs = [(w_query_keep, w_query_got)]
    widths = [query_weight.shape[1]]
    if group_dev == 1:
        w_kv_send, w_kv_keep = token_halves(normed_rows, kv_grads, [])
        pairs.append((w_kv_keep, swap_dp(w_kv_send)))
        widths += [key_weight.shape[1], value_weight.shape[1]]
    grad_normed, gain_rows = normed_back(
        grad_q, kv_grads, query_weight, kv_weights, normed_rows, []
    )
    send, keep = plane_first(pairs, [grad_normed])
    (grad_w_out,) = widen_all(
        w_out_quarters,
        quarter_places(lambda core, b1, b2: jnp.where(core == 0, b1 + 2 * b2, 2 * b1 + b2)),
        [width],
        [],
    )
    small = pack_small(
        experts,
        grad_router,
        gain_rows,
        attn_gain,
        grad_mlp_gain,
        grad_q_gain,
        grad_k_gain,
        [],
    )
    swap_all = lambda rows: lax.all_to_all(rows, ALL_AXES, split_axis=0, concat_axis=0, tiled=True)
    small_parts = swap_all(small.reshape(lax.axis_size(ALL_AXES), -1, width))
    small_own = jnp.sum(small_parts.astype(F32), axis=0).astype(LOW)
    second_send, second_keep = plane_second(send, keep, [small_own, *w_out_quarters[1:3]])
    grad_normed = lax.psum_scatter(grad_normed, "expert", scatter_dimension=0, tiled=True)
    grad_input = input_back(grad_normed, x_low, attn_gain, grad_hidden)
    small_sum = swap_all(jnp.broadcast_to(small_own[None], small_parts.shape))
    quarter = plane_last(
        second_send, second_keep, [output_rows, grad_input, grad_w_out, small_sum]
    )
    grad_router, grad_attn_gain, grad_mlp_gain, grad_q_gain, grad_k_gain = unpack_small(
        small_sum.reshape(small.shape), experts, size, []
    )
    quarters = plane_spread(quarter)
    places = quarter_places(lambda core, b1, b2: 2 * b1 + b2)
    grad_w_query, *more = widen_all(quarters, places, widths, [grad_router])
    if group_dev == 1:
        grad_w_key, grad_w_value = more
    else:
        w_kv = token_dot(normed_rows, kv_grads, [])
        blank = jnp.zeros((width, kv_total), LOW)
        pieces = []
        for part in (w_kv[:, :size], w_kv[:, size:]):
            padded = lax.dynamic_update_slice(blank, part, (0, kv_index * size))
            pieces.append(lax.psum_scatter(padded, "expert", scatter_dimension=1, tiled=True))
        grad_w_key, grad_w_value = (lax.psum(piece, GROUP_AXES).astype(F32) for piece in pieces)
    return (
        output_rows.astype(LOW)[None],
        grad_input[None],
        grad_attn_gain[0],
        grad_w_query,
        grad_w_key,
        grad_w_value,
        grad_q_gain[0],
        grad_k_gain[0],
        grad_w_out,
        grad_mlp_gain[0],
        grad_router.T,
        grad_w_gate[None],
        grad_w_up[None],
        grad_w_down[None],
    )


def solution(mesh):
    rows = P("dp", ("context", "expert"), None)
    expert = P(ALL_AXES, None, None)
    columns = P(None, "expert")
    in_specs = (
        rows,
        rows,
        P(),
        columns,
        columns,
        columns,
        P(),
        P(),
        P("expert", None),
        P(),
        P(),
        expert,
        expert,
        expert,
        rows,
        P(),
    )
    out_specs = (
        rows,
        rows,
        P(),
        columns,
        columns,
        columns,
        P(),
        P(),
        P("expert", None),
        P(),
        P(),
        expert,
        expert,
        expert,
    )
    return jax.shard_map(
        on_device, mesh=mesh, in_specs=in_specs, out_specs=out_specs, check_vma=False
    )
```

```python
import functools
import math

import jax
import jax.numpy as jnp
from jax import lax
from jax.experimental import pallas as pl
from jax.experimental.pallas import tpu as pltpu
from jax.sharding import PartitionSpec as P

EPS = 1e-06
THETA = 1000000.0
TILE = 256
PIECE = 128
VMEM_BYTES = 56 * 1024 * 1024
LOG2E = math.log2(math.e)
LOW = jnp.bfloat16
F32 = jnp.float32
ALL_AXES = ("dp", "context", "expert")
GROUP_AXES = ("dp", "context")


def dot_nn(a, b):
    return lax.dot_general(a, b, (((1,), (0,)), ((), ())), preferred_element_type=F32)


def dot_nt(a, b):
    return lax.dot_general(a, b, (((1,), (1,)), ((), ())), preferred_element_type=F32)


def dot_tn(a, b):
    return lax.dot_general(a, b, (((0,), (0,)), ((), ())), preferred_element_type=F32)


def params(**more):
    return pltpu.CompilerParams(vmem_limit_bytes=VMEM_BYTES, **more)


def cost(flops, nbytes, exps=0):
    return pl.CostEstimate(flops=int(flops), bytes_accessed=int(nbytes), transcendentals=int(exps))


def head_forward(u, gain, cos2, sin2):
    rr = lax.rsqrt(jnp.mean(u * u, axis=-1, keepdims=True) + EPS)
    y = u * rr * gain
    return y * cos2 + pltpu.roll(y, 64, 1) * sin2


def head_backward(gy, u, gain, cos2, sin2):
    g = gy * cos2 - pltpu.roll(gy, 64, 1) * sin2
    rr = lax.rsqrt(jnp.mean(u * u, axis=-1, keepdims=True) + EPS)
    n = u * rr
    gn = g * gain
    grad = rr * (gn - n * jnp.mean(gn * n, axis=-1, keepdims=True))
    return grad, jnp.sum(g * n, axis=0, keepdims=True)


def query_kernel(x_ref, w_ref, gain_ref, cos_ref, sin_ref, rot_ref, proj_ref):
    tiles, heads, rows, size = rot_ref.shape
    acc = dot_nn(x_ref[...], w_ref[...])
    for h in range(heads):
        u = acc[:, h * size : (h + 1) * size]
        rot = head_forward(u, gain_ref[...], cos_ref[...], sin_ref[...])
        proj_ref[:, h] = u.reshape(tiles, rows, size)
        rot_ref[:, h] = rot.astype(LOW).reshape(tiles, rows, size)


def project_queries(normed, weight, gain, cos2, sin2):
    block, width = normed.shape
    size = cos2.shape[1]
    heads = weight.shape[1] // size
    tiles = block // TILE
    whole = lambda i: (0, 0)
    per = lambda i: (0, i, 0, 0)
    shape = (tiles, heads, TILE, size)
    return pl.pallas_call(
        query_kernel,
        grid=(heads // 2,),
        in_specs=[
            pl.BlockSpec((block, width), whole),
            pl.BlockSpec((width, 2 * size), lambda i: (0, i)),
            pl.BlockSpec((1, size), whole),
            pl.BlockSpec((block, size), whole),
            pl.BlockSpec((block, size), whole),
        ],
        out_specs=[pl.BlockSpec((tiles, 2, TILE, size), per)] * 2,
        out_shape=[jax.ShapeDtypeStruct(shape, LOW), jax.ShapeDtypeStruct(shape, F32)],
        compiler_params=params(),
        cost_estimate=cost(2 * block * width * heads * size, 12e6),
    )(normed, weight, gain[None], cos2, sin2)


def put_in_order(place, refs, out_ref):
    n = (len(refs) + 1) // 2
    rows = refs[0].shape[0]
    for distance in range(1 - n, n):
        ref = refs[distance + n - 1]
        at = place + distance

        @pl.when(jnp.logical_and(at >= 0, at < n))
        def _():
            out_ref[pl.ds(pl.multiple_of(at * rows, rows), rows), :] = ref[...]


def chunk_list(found):
    n = (len(found) + 1) // 2
    return [found[distance] for distance in range(1 - n, n)]


def key_kernel(factor, n_chunks, place_ref, *refs):
    w_ref, gain_ref, cos_ref, sin_ref, g_ref, mask_ref = refs[n_chunks:-4]
    rows_ref, kv_ref, proj_ref, wide_ref = refs[-4:]
    size = proj_ref.shape[1]
    width = g_ref.shape[1]
    put_in_order(place_ref[0], refs[:n_chunks], rows_ref)
    wide_ref[:, :width] = g_ref[...]
    wide_ref[:, width:] = mask_ref[...].astype(LOW)
    acc = dot_nn(rows_ref[...], w_ref[...])
    u = acc[:, :size]
    rot = head_forward(u, gain_ref[...], cos_ref[...], sin_ref[...])
    proj_ref[...] = u
    kv_ref[:, :size] = (rot * factor).astype(LOW)
    kv_ref[:, size:] = acc[:, size:].astype(LOW)


def full(shape):
    return pl.BlockSpec(shape, lambda *_: (0,) * len(shape))


def project_keys(place, found, weight, gain, cos2, sin2, factor, g, mask):
    chunks = chunk_list(found)
    rows, width = chunks[0].shape
    block, size = cos2.shape
    operands = [*chunks, weight, gain[None], cos2, sin2, g, mask]
    shapes = [
        jax.ShapeDtypeStruct((block, width), LOW),
        jax.ShapeDtypeStruct((block, 2 * size), LOW),
        jax.ShapeDtypeStruct((block, size), F32),
        jax.ShapeDtypeStruct((rows, width + mask.shape[1]), LOW),
    ]
    return pl.pallas_call(
        functools.partial(key_kernel, factor, len(chunks)),
        grid_spec=pltpu.PrefetchScalarGridSpec(
            num_scalar_prefetch=1,
            grid=(1,),
            in_specs=[full(x.shape) for x in operands],
            out_specs=[full(x.shape) for x in shapes],
        ),
        out_shape=shapes,
        compiler_params=params(),
        cost_estimate=cost(4 * block * width * size, 8e6),
    )(place, *operands)


def in_order(last, step):
    lax.fori_loop(0, lax.div(last, 2), lambda p, c: (step([2 * p, 2 * p + 1], False), c)[1], 0)

    @pl.when(lax.rem(last, 2) == 1)
    def _():
        step([last - 1, last], True)

    @pl.when(lax.rem(last, 2) == 0)
    def _():
        step([last], True)


def attend_kernel(qpos_ref, kidx_ref, q_ref, kv_ref, *rest):
    out_ref, inv_ref, acc_ref = rest[-3:]
    heads, rows, size = q_ref.shape[1:]
    acc_ref[...] = jnp.zeros_like(acc_ref)

    def step(places, masked):
        starts = [pl.multiple_of(kidx_ref[place] * rows, rows) for place in places]
        count = len(places) * rows
        keys = jnp.concatenate([kv_ref[pl.ds(start, rows), :size] for start in starts], axis=0)
        values = jnp.concatenate([kv_ref[pl.ds(start, rows), size:] for start in starts], axis=0)
        values = jnp.concatenate([values, jnp.ones((count, size), LOW)], axis=1)
        for h in range(heads):
            for first in range(0, rows, PIECE):
                part = slice(first, first + PIECE)
                e = jnp.exp2(dot_nt(q_ref[0, h, part], keys))
                if masked:
                    qi = lax.broadcasted_iota(jnp.int32, e.shape, 0) + first
                    ki = lax.broadcasted_iota(jnp.int32, e.shape, 1) - (count - rows)
                    e = jnp.where(ki <= qi, e, 0.0)
                acc_ref[h, part] += dot_nn(e.astype(LOW), values)

    in_order(qpos_ref[pl.program_id(0)], step)
    for h in range(heads):
        inv = 1.0 / acc_ref[h, :, size:]
        inv_ref[0, h] = inv
        out_ref[:, h * size : (h + 1) * size] = (acc_ref[h, :, :size] * inv).astype(LOW)


def attend(qpos, kidx, queries, kv, others):
    tiles, heads, rows, size = queries.shape
    seq = kv.shape[0]
    return pl.pallas_call(
        attend_kernel,
        grid_spec=pltpu.PrefetchScalarGridSpec(
            num_scalar_prefetch=2,
            grid=(tiles,),
            in_specs=[
                pl.BlockSpec((1, heads, rows, size), lambda i, a, b: (i, 0, 0, 0)),
                pl.BlockSpec((seq, 2 * size), lambda i, a, b: (0, 0)),
            ]
            + [pl.BlockSpec(memory_space=pl.ANY)] * len(others),
            out_specs=[
                pl.BlockSpec((rows, heads * size), lambda i, a, b: (i, 0)),
                pl.BlockSpec((1, heads, rows, size), lambda i, a, b: (i, 0, 0, 0)),
            ],
            scratch_shapes=[pltpu.VMEM((heads, rows, 2 * size), F32)],
        ),
        out_shape=[
            jax.ShapeDtypeStruct((tiles * rows, heads * size), LOW),
            jax.ShapeDtypeStruct((tiles, heads, rows, size), F32),
        ],
        compiler_params=params(),
        cost_estimate=cost(
            6 * tiles * rows * heads * seq * size, 8e6, tiles * rows * heads * seq
        ),
    )(qpos, kidx, queries, kv, *others)


def grad_out_kernel(rows_ref, w_ref, o_ref, inv_ref, *rest):
    do_ref, centre_ref = rest[-2:]
    tiles, heads, rows, size = do_ref.shape
    acc = dot_nt(rows_ref[...], w_ref[...])
    for t in range(tiles):
        for h in range(heads):
            part = slice(t * rows, (t + 1) * rows), slice(h * size, (h + 1) * size)
            low = (acc[part] * inv_ref[t, h]).astype(LOW)
            do_ref[t, h] = low
            product = low.astype(F32) * o_ref[part].astype(F32)
            centre = jnp.sum(jnp.transpose(product), axis=0, keepdims=True)
            centre_ref[t, h] = jnp.broadcast_to(centre, (8, rows))


def grad_attended(grad_rows, weight, attended, inverse, others):
    tiles, heads, rows, size = inverse.shape
    block, width = grad_rows.shape
    return pl.pallas_call(
        grad_out_kernel,
        grid=(heads // 2,),
        in_specs=[
            pl.BlockSpec((block, width), lambda i: (0, 0)),
            pl.BlockSpec((2 * size, width), lambda i: (i, 0)),
            pl.BlockSpec((block, 2 * size), lambda i: (0, i)),
            pl.BlockSpec((tiles, 2, rows, size), lambda i: (0, i, 0, 0)),
        ]
        + [pl.BlockSpec(memory_space=pl.ANY)] * len(others),
        out_specs=[
            pl.BlockSpec((tiles, 2, rows, size), lambda i: (0, i, 0, 0)),
            pl.BlockSpec((tiles, 2, 8, rows), lambda i: (0, i, 0, 0)),
        ],
        out_shape=[
            jax.ShapeDtypeStruct((tiles, heads, rows, size), LOW),
            jax.ShapeDtypeStruct((tiles, heads, 8, rows), F32),
        ],
        compiler_params=params(),
        cost_estimate=cost(2 * block * width * heads * size, 12e6),
    )(grad_rows, weight, attended, inverse, *others)


def attend_back_kernel(
    qpos_ref,
    kidx_ref,
    q_ref,
    do_ref,
    centre_ref,
    kv_ref,
    kt_ref,
    proj_ref,
    gain_ref,
    cos_ref,
    sin_ref,
    *rest,
):
    dkv_ref, dq_ref, dgain_ref, acc_ref, e_ref, ds_ref = rest[-6:]
    heads, rows, size = q_ref.shape[1:]

    @pl.when(pl.program_id(0) == 0)
    def _():
        dkv_ref[...] = jnp.zeros_like(dkv_ref)
        dgain_ref[...] = jnp.zeros_like(dgain_ref)

    acc_ref[...] = jnp.zeros_like(acc_ref)

    def step(places, masked):
        starts = [pl.multiple_of(kidx_ref[place] * rows, rows) for place in places]
        count = len(places) * rows
        keys = jnp.concatenate([kv_ref[pl.ds(start, rows), :size] for start in starts], axis=0)
        values = jnp.concatenate([kv_ref[pl.ds(start, rows), size:] for start in starts], axis=0)
        keys_t = jnp.concatenate([kt_ref[:, pl.ds(start, rows)] for start in starts], axis=1)
        for h in range(heads):
            query, grad = q_ref[0, h], do_ref[0, h]
            centre = centre_ref[0, h, 0:1]
            columns = slice(h * rows, (h + 1) * rows)
            for first in range(0, count, PIECE):
                part = slice(first, first + PIECE)
                e = jnp.exp2(dot_nt(keys[part], query))
                if masked and first >= count - rows:
                    ki = lax.broadcasted_iota(jnp.int32, e.shape, 0) + (first - (count - rows))
                    qi = lax.broadcasted_iota(jnp.int32, e.shape, 1)
                    e = jnp.where(ki <= qi, e, 0.0)
                ds = e * (dot_nt(values[part], grad) - centre)
                e_ref[part, columns] = e.astype(LOW)
                ds_ref[part, columns] = ds.astype(LOW)
            acc_ref[h] += dot_nn(keys_t, ds_ref[:count, columns])
        dk = dot_nn(ds_ref[:count], q_ref[0].reshape(heads * rows, size))
        dv = dot_nn(e_ref[:count], do_ref[0].reshape(heads * rows, size))
        for k, start in enumerate(starts):
            dkv_ref[pl.ds(start, rows), :size] += dk[k * rows : (k + 1) * rows]
            dkv_ref[pl.ds(start, rows), size:] += dv[k * rows : (k + 1) * rows]

    in_order(qpos_ref[pl.program_id(0)], step)
    total = jnp.zeros((1, size), F32)
    for h in range(heads):
        grad, gain_part = head_backward(
            jnp.transpose(acc_ref[h]) * (1.0 / LOG2E),
            proj_ref[0, h],
            gain_ref[...],
            cos_ref[...],
            sin_ref[...],
        )
        dq_ref[:, h * size : (h + 1) * size] = grad.astype(LOW)
        total += gain_part
    dgain_ref[...] += total


def attend_back(qpos, kidx, queries, grads, centre, kv, keys_t, proj, gain, cos2, sin2, others):
    tiles, heads, rows, size = queries.shape
    seq = kv.shape[0]
    per = pl.BlockSpec((1, heads, rows, size), lambda i, a, b: (i, 0, 0, 0))
    flat = lambda i, a, b: (0, 0)
    rowwise = lambda i, a, b: (i, 0)
    return pl.pallas_call(
        attend_back_kernel,
        grid_spec=pltpu.PrefetchScalarGridSpec(
            num_scalar_prefetch=2,
            grid=(tiles,),
            in_specs=[
                per,
                per,
                pl.BlockSpec((1, heads, 8, rows), lambda i, a, b: (i, 0, 0, 0)),
                pl.BlockSpec((seq, 2 * size), flat),
                pl.BlockSpec((size, seq), flat),
                per,
                pl.BlockSpec((1, size), flat),
                pl.BlockSpec((rows, size), rowwise),
                pl.BlockSpec((rows, size), rowwise),
            ]
            + [pl.BlockSpec(memory_space=pl.ANY)] * len(others),
            out_specs=[
                pl.BlockSpec((seq, 2 * size), flat),
                pl.BlockSpec((rows, heads * size), rowwise),
                pl.BlockSpec((1, size), flat),
            ],
            scratch_shapes=[pltpu.VMEM((heads, size, rows), F32)]
            + [pltpu.VMEM((2 * rows, heads * rows), LOW)] * 2,
        ),
        out_shape=[
            jax.ShapeDtypeStruct((seq, 2 * size), F32),
            jax.ShapeDtypeStruct((tiles * rows, heads * size), LOW),
            jax.ShapeDtypeStruct((1, size), F32),
        ],
        compiler_params=params(),
        cost_estimate=cost(
            15 * tiles * rows * heads * seq * size, 12e6, tiles * rows * heads * seq
        ),
    )(qpos, kidx, queries, grads, centre, kv, keys_t, proj, gain[None], cos2, sin2, *others)


def out_kernel(a_ref, b_ref, *rest):
    rest[-1][...] = dot_nn(a_ref[...], b_ref[...]).astype(LOW)


def out_dot(a, b, others):
    block, inner = a.shape
    columns = b.shape[1]
    tile = min(columns, 512)
    return pl.pallas_call(
        out_kernel,
        grid=(columns // tile,),
        in_specs=[
            pl.BlockSpec((block, inner), lambda i: (0, 0)),
            pl.BlockSpec((inner, tile), lambda i: (0, i)),
        ]
        + [pl.BlockSpec(memory_space=pl.ANY)] * len(others),
        out_specs=pl.BlockSpec((block, tile), lambda i: (0, i)),
        out_shape=jax.ShapeDtypeStruct((block, columns), LOW),
        compiler_params=params(),
        cost_estimate=cost(2 * block * inner * columns, 8e6),
    )(a, b, *others)


def token_kernel(a_ref, b_ref, *rest):
    rest[-1][...] = dot_tn(a_ref[...], b_ref[...]).astype(LOW)


def token_dot(a, b, others):
    block, rows = a.shape
    columns = b.shape[1]
    tile = min(rows, 512)
    return pl.pallas_call(
        token_kernel,
        grid=(rows // tile,),
        in_specs=[
            pl.BlockSpec((block, tile), lambda i: (0, i)),
            pl.BlockSpec((block, columns), lambda i: (0, 0)),
        ]
        + [pl.BlockSpec(memory_space=pl.ANY)] * len(others),
        out_specs=pl.BlockSpec((tile, columns), lambda i: (i, 0)),
        out_shape=jax.ShapeDtypeStruct((rows, columns), LOW),
        compiler_params=params(),
        cost_estimate=cost(2 * block * rows * columns, 6e6),
    )(a, b, *others)


def halves_kernel(d_ref, a_ref, b_ref, *rest):
    send_ref, keep_ref = rest[-2:]
    product = dot_tn(a_ref[...], b_ref[...]).astype(LOW)

    @pl.when(pl.program_id(0) == 0)
    def _():
        send_ref[...] = product

    @pl.when(pl.program_id(0) == 1)
    def _():
        keep_ref[...] = product


def token_halves(a, b, others):
    block, rows = a.shape
    columns = b.shape[1]
    tiles = 2 if rows % 512 == 0 else 1
    tile = rows // (2 * tiles)
    d = lax.axis_index("dp").astype(jnp.int32)[None]
    half = jax.ShapeDtypeStruct((rows // 2, columns), LOW)
    return pl.pallas_call(
        halves_kernel,
        grid_spec=pltpu.PrefetchScalarGridSpec(
            num_scalar_prefetch=1,
            grid=(2, tiles),
            in_specs=[
                pl.BlockSpec(
                    (block, tile),
                    lambda h, j, d: (0, ((1 - d[0]) * (1 - h) + d[0] * h) * tiles + j),
                ),
                pl.BlockSpec((block, columns), lambda h, j, d: (0, 0)),
            ]
            + [pl.BlockSpec(memory_space=pl.ANY)] * len(others),
            out_specs=[
                pl.BlockSpec((tile, columns), lambda h, j, d: (j * (1 - h) + (tiles - 1) * h, 0)),
                pl.BlockSpec((tile, columns), lambda h, j, d: (j * h, 0)),
            ],
        ),
        out_shape=[half, half],
        compiler_params=params(),
        cost_estimate=cost(2 * block * rows * columns, 6e6),
    )(d, a, b, *others)


def split_low(value):
    high = value.astype(LOW)
    return high, (value - high.astype(F32)).astype(LOW)


def norm_parts(rows):
    rr = lax.rsqrt(jnp.mean(rows * rows, axis=-1, keepdims=True) + EPS)
    return rows * rr, rr


def norm_back(grad, normal, rr, gain):
    weighted = grad * gain
    return rr * (weighted - normal * jnp.mean(weighted * normal, axis=-1, keepdims=True))


def add_all(refs):
    return functools.reduce(jnp.add, [ref[...].astype(F32) for ref in refs])


def pad_rows(rows, count):
    if rows.shape[0] == count:
        return rows
    return jnp.concatenate(
        [rows, jnp.zeros((count - rows.shape[0], rows.shape[1]), rows.dtype)], axis=0
    )


def router_kernel(experts, *refs):
    x_ref, attn_ref, gain_ref, router_ref, mask_ref = refs[:5]
    hidden_ref, mixed_ref, probs_ref = refs[-3:]
    width = x_ref.shape[1]
    lanes = mask_ref.shape[1]
    hidden = add_all([x_ref, attn_ref])
    hidden_ref[...] = hidden
    mixed = (norm_parts(hidden)[0] * gain_ref[...]).astype(LOW)
    mixed_ref[:, :width] = mixed
    logits = dot_nt(mixed, pad_rows(router_ref[...], lanes))
    lane = lax.broadcasted_iota(jnp.int32, logits.shape, 1)
    logits = jnp.where(lane < experts, logits, -1e30)
    weights = jnp.exp(logits - jnp.max(logits, axis=1, keepdims=True))
    probs = weights / jnp.sum(weights, axis=1, keepdims=True)
    probs_ref[...] = probs
    chosen = probs * mask_ref[...]
    high, low = split_low(chosen / jnp.sum(chosen, axis=1, keepdims=True))
    both = high.astype(F32) + pltpu.roll(low.astype(F32), experts, 1)
    mixed_ref[:, width:] = both.astype(LOW)


def route_rows(x, attn, gain, router, mask, experts, others):
    tokens, width = x.shape
    lanes = mask.shape[1]
    operands = [x, attn, gain[None], router, mask]
    shapes = [
        jax.ShapeDtypeStruct((tokens, width), F32),
        jax.ShapeDtypeStruct((tokens, width + lanes), LOW),
        jax.ShapeDtypeStruct((tokens, lanes), F32),
    ]
    return pl.pallas_call(
        functools.partial(router_kernel, experts),
        grid=(1,),
        in_specs=[full(value.shape) for value in operands]
        + [pl.BlockSpec(memory_space=pl.ANY)] * len(others),
        out_specs=[full(shape.shape) for shape in shapes],
        out_shape=shapes,
        compiler_params=params(),
        cost_estimate=cost(2 * tokens * width * lanes, 5e6),
    )(*operands, *others)


def one_hot(slots, count, first):
    groups, tokens = slots.shape
    slot = lax.broadcasted_iota(jnp.int32, (groups, count, tokens), 1).astype(F32)
    same = slots[:, None, :] == slot + float(first)
    return jnp.where(same, 1.0, 0.0).reshape(groups * count, tokens)


def slot_kernel(capacity, meta_ref, col_ref, rows_ref, slots_ref):
    groups, block = slots_ref.shape
    rows, width = rows_ref.shape
    n = rows // groups // capacity
    tokens = block // n
    mask = col_ref[:, width:]
    lanes = mask.shape[1]
    padded = -(-groups // 16) * 16
    group = lax.broadcasted_iota(jnp.int32, (padded, lanes), 0)
    lane = lax.broadcasted_iota(jnp.int32, (padded, lanes), 1)
    wanted = jnp.logical_and(lane == group * n + meta_ref[0], group < groups)
    hits = dot_nt(jnp.where(wanted, 1.0, 0.0).astype(LOW), mask)
    before = lax.broadcasted_iota(jnp.int32, (tokens, tokens), 0)
    after_it = lax.broadcasted_iota(jnp.int32, (tokens, tokens), 1)
    earlier = jnp.where(before < after_it, 1.0, 0.0).astype(LOW)
    for z in range(n):
        hit = hits[:, z * tokens : (z + 1) * tokens]
        rank = dot_nn(hit.astype(LOW), earlier)
        turn = (meta_ref[1 + z] * capacity).astype(F32)
        slot = jnp.where(hit > 0.5, rank + turn, -1.0)
        slots_ref[:, z * tokens : (z + 1) * tokens] = slot[:groups]
    spread = one_hot(slots_ref[...], n * capacity, 0).astype(LOW)
    rows_ref[...] = dot_nn(spread, col_ref[:, :width]).astype(LOW)


def make_slots(meta, col, width, groups, capacity):
    block = col.shape[0]
    n = lax.axis_size("expert")
    shapes = [
        jax.ShapeDtypeStruct((groups * n * capacity, width), LOW),
        jax.ShapeDtypeStruct((groups, block), F32),
    ]
    return pl.pallas_call(
        functools.partial(slot_kernel, capacity),
        grid_spec=pltpu.PrefetchScalarGridSpec(
            num_scalar_prefetch=1,
            grid=(1,),
            in_specs=[full(col.shape)],
            out_specs=[full(shape.shape) for shape in shapes],
        ),
        out_shape=shapes,
        compiler_params=params(),
        cost_estimate=cost(2 * groups * n * capacity * block * width, 8e6),
    )(meta, col)


def table_kernel(capacity, n_half, meta_ref, slots_ref, near_ref, far_ref, near_back_ref, far_back_ref):
    n = 2 * n_half
    tokens = slots_ref.shape[1] // n
    cap_half = n_half * capacity
    for part, (to_ref, back_ref) in enumerate([(near_ref, near_back_ref), (far_ref, far_back_ref)]):
        pieces = []
        for k in range(n_half):
            start = pl.multiple_of(meta_ref[1 + n + part * n_half + k] * tokens, tokens)
            pieces.append(slots_ref[:, pl.ds(start, tokens)])
        spread = one_hot(jnp.concatenate(pieces, axis=1), cap_half, part * cap_half)
        to_ref[...] = spread.astype(LOW)
        back_ref[...] = jnp.transpose(spread).astype(LOW)


def make_tables(meta, slots, n_half, capacity):
    groups, block = slots.shape
    rows = groups * n_half * capacity
    shapes = [jax.ShapeDtypeStruct((rows, block // 2), LOW)] * 2
    shapes += [jax.ShapeDtypeStruct((block // 2, rows), LOW)] * 2
    outs = pl.pallas_call(
        functools.partial(table_kernel, capacity, n_half),
        grid_spec=pltpu.PrefetchScalarGridSpec(
            num_scalar_prefetch=1,
            grid=(1,),
            in_specs=[full(slots.shape)],
            out_specs=[full(shape.shape) for shape in shapes],
        ),
        out_shape=shapes,
        compiler_params=params(),
        cost_estimate=cost(8 * rows * block, 3e6),
    )(meta, slots)
    return outs[:2], outs[2:]


def spread_kernel(choices, place_ref, spread_ref, *refs):
    out_ref, rows_ref = refs[-2:]
    for k, by_place in enumerate(choices):
        for which in sorted(set(by_place)):
            hit = functools.reduce(
                jnp.logical_or,
                [place_ref[0] == i for i, other in enumerate(by_place) if other == which],
            )

            @pl.when(hit)
            def _():
                tokens = refs[which].shape[0]
                rows_ref[k * tokens : (k + 1) * tokens] = refs[which][...]

    out_ref[...] = dot_nn(spread_ref[...], rows_ref[...]).astype(LOW)


def spread_rows(place, spread, found, turns, others):
    n = lax.axis_size("expert")
    order = arrival_order(n)
    distances = sorted({order[i][turn] - i for i in range(n) for turn in turns})
    choices = [[distances.index(order[i][turn] - i) for i in range(n)] for turn in turns]
    chunks = [found[distance] for distance in distances]
    tokens, wide = chunks[0].shape
    rows = spread.shape[0]
    return pl.pallas_call(
        functools.partial(spread_kernel, choices),
        grid_spec=pltpu.PrefetchScalarGridSpec(
            num_scalar_prefetch=1,
            grid=(1,),
            in_specs=[full(spread.shape)]
            + [full(chunk.shape) for chunk in chunks]
            + [pl.BlockSpec(memory_space=pl.ANY)] * len(others),
            out_specs=full((rows, wide)),
            scratch_shapes=[pltpu.VMEM((len(turns) * tokens, wide), LOW)],
        ),
        out_shape=jax.ShapeDtypeStruct((rows, wide), LOW),
        compiler_params=params(),
        cost_estimate=cost(2 * rows * len(turns) * tokens * wide, 5e6),
    )(place, spread, *chunks, *others)


def router_back_kernel(experts, *refs):
    sum_ref, g_ref, hidden_ref, gain_ref, router_ref, mask_ref, probs_ref = refs[:7]
    grad_ref, low_ref, dgain_ref, drouter_ref = refs[-4:]
    width = g_ref.shape[1]
    lanes = mask_ref.shape[1]
    total = sum_ref[...].astype(F32)
    table = total[:, width:]
    mask, probs = mask_ref[...], probs_ref[...]
    grad_gates = (table + pltpu.roll(table, lanes - experts, 1)) * mask
    chosen = probs * mask
    chosen_sum = jnp.sum(chosen, axis=1, keepdims=True)
    mean = jnp.sum(grad_gates * (chosen / chosen_sum), axis=1, keepdims=True)
    centred = mask * (grad_gates - mean) / chosen_sum
    grad_logits = probs * (centred - jnp.sum(centred * chosen, axis=1, keepdims=True))
    high, low = split_low(grad_logits)
    router = pad_rows(router_ref[...], lanes)
    grad = total[:, :width] + dot_nn(high, router) + dot_nn(low, router)
    normal, rr = norm_parts(hidden_ref[...])
    mixed = (normal * gain_ref[...]).astype(LOW)
    drouter_ref[...] = dot_tn(high, mixed) + dot_tn(low, mixed)
    dgain_ref[...] = jnp.sum(grad * normal, axis=0, keepdims=True)
    grad_hidden = g_ref[...].astype(F32) + norm_back(grad, normal, rr, gain_ref[...])
    grad_ref[...] = grad_hidden
    low_ref[...] = grad_hidden.astype(LOW)


def route_back(summed, g, hidden, gain, router, mask, probs, experts, others):
    tokens, width = g.shape
    lanes = mask.shape[1]
    operands = [summed, g, hidden, gain[None], router, mask, probs]
    shapes = [
        jax.ShapeDtypeStruct((tokens, width), F32),
        jax.ShapeDtypeStruct((tokens, width), LOW),
        jax.ShapeDtypeStruct((1, width), F32),
        jax.ShapeDtypeStruct((lanes, width), F32),
    ]
    return pl.pallas_call(
        functools.partial(router_back_kernel, experts),
        grid=(1,),
        in_specs=[full(value.shape) for value in operands]
        + [pl.BlockSpec(memory_space=pl.ANY)] * len(others),
        out_specs=[full(shape.shape) for shape in shapes],
        out_shape=shapes,
        compiler_params=params(),
        cost_estimate=cost(8 * tokens * width * lanes, 8e6),
    )(*operands, *others)


def combine_kernel(meta_ref, table_ref, rows_ref, *rest):
    del meta_ref
    rest[-1][...] = dot_nn(table_ref[...], rows_ref[...]).astype(LOW)


def combine_part(meta, table, rows, first, n, into, others):
    block, slots = table.shape
    wide = rows.shape[1]
    tokens = block // (n // 2)
    return pl.pallas_call(
        combine_kernel,
        grid_spec=pltpu.PrefetchScalarGridSpec(
            num_scalar_prefetch=1,
            grid=(n // 2,),
            in_specs=[
                pl.BlockSpec((tokens, slots), lambda i, m: (i, 0)),
                full(rows.shape),
            ]
            + [pl.BlockSpec(memory_space=pl.ANY)] * (len(into) + len(others)),
            out_specs=pl.BlockSpec((tokens, wide), lambda i, m: (m[1 + n + first + i], 0)),
        ),
        out_shape=jax.ShapeDtypeStruct((n * tokens, wide), LOW),
        input_output_aliases={3: 0} if into else {},
        compiler_params=params(),
        cost_estimate=cost(2 * slots * block * wide, 6e6),
    )(meta, table, rows, *into, *others)


def combine_rows(meta, tables, rows, n_half, others):
    near = combine_part(meta, tables[0], rows[0], 0, 2 * n_half, [], [])
    return combine_part(meta, tables[1], rows[1], n_half, 2 * n_half, [near], others)


def expert_kernel(experts, who_ref, x_ref, gate_ref, up_ref, pull_ref, *rest):
    act_ref, dgate_ref, dup_ref, copy_ref = rest[-4:]
    width = gate_ref.shape[0]
    x = x_ref[:, :width]
    table = x_ref[:, width:].astype(F32)
    lane = lax.broadcasted_iota(jnp.int32, table.shape, 1)
    mine = who_ref[0]
    gate = jnp.sum(
        jnp.where(jnp.logical_or(lane == mine, lane == mine + experts), table, 0.0),
        axis=1,
        keepdims=True,
    )
    pre_gate = dot_nn(x, gate_ref[...])
    pre_up = dot_nn(x, up_ref[...])
    pull = pull_ref[...].reshape(pre_up.shape)
    sig = 1.0 / (1.0 + jnp.exp(-pre_gate))
    silu = pre_gate * sig
    act = silu * pre_up
    act_ref[...] = (act * gate).astype(LOW)
    high, low = split_low(jnp.sum(act * pull, axis=1, keepdims=True))
    pull = pull * gate
    dup = (pull * silu).astype(LOW)
    dgate = (pull * pre_up * (sig * (1.0 + pre_gate * (1.0 - sig)))).astype(LOW)
    dgate_ref[...] = dgate
    dup_ref[...] = dup
    copy_ref[:, :width] = (dot_nt(dgate, gate_ref[...]) + dot_nt(dup, up_ref[...])).astype(LOW)
    back = jnp.where(lane == mine, high.astype(F32), 0.0)
    back = jnp.where(lane == mine + experts, low.astype(F32), back)
    copy_ref[:, width:] = back.astype(LOW)


def run_expert(who, x, w_gate, w_up, pull, part, experts):
    rows, wide = x.shape
    width, hidden = w_gate.shape
    groups, _, slots, _ = pull.shape
    each = groups // 2
    tile = each * slots
    by_rows = lambda columns: pl.BlockSpec((tile, columns), lambda i, p: (i, 0))
    return pl.pallas_call(
        functools.partial(expert_kernel, experts),
        grid_spec=pltpu.PrefetchScalarGridSpec(
            num_scalar_prefetch=1,
            grid=(2,),
            in_specs=[
                by_rows(wide),
                full(w_gate.shape),
                full(w_up.shape),
                pl.BlockSpec((each, 1, slots, hidden), lambda i, p: (i, part, 0, 0)),
            ],
            out_specs=[by_rows(hidden), by_rows(hidden), by_rows(hidden), by_rows(wide)],
        ),
        out_shape=[jax.ShapeDtypeStruct((rows, hidden), LOW)] * 3
        + [jax.ShapeDtypeStruct((rows, wide), LOW)],
        compiler_params=params(),
        cost_estimate=cost(8 * rows * width * hidden, 20e6, rows * hidden),
    )(who, x, w_gate, w_up, pull)


def input_kernel(grad_ref, x_ref, gain_ref, more_ref, *rest):
    normal, rr = norm_parts(x_ref[...].astype(F32))
    grad = grad_ref[...].astype(F32)
    rest[-1][...] = more_ref[...] + norm_back(grad, normal, rr, gain_ref[...])


def input_back(grad, x, gain, more, others):
    tokens, width = x.shape
    operands = [grad, x, gain[None], more]
    return pl.pallas_call(
        input_kernel,
        grid=(1,),
        in_specs=[full(value.shape) for value in operands]
        + [pl.BlockSpec(memory_space=pl.ANY)] * len(others),
        out_specs=full(more.shape),
        out_shape=jax.ShapeDtypeStruct((tokens, width), F32),
        compiler_params=params(),
        cost_estimate=cost(20 * tokens * width, 5e6),
    )(*operands, *others)


def kv_back_kernel(factor, parts_ref, proj_ref, gain_ref, cos_ref, sin_ref, *rest):
    grad_ref, dgain_ref = rest[-2:]
    size = proj_ref.shape[1]
    total = parts_ref[0].astype(F32)
    for k in range(1, parts_ref.shape[0]):
        total += parts_ref[k].astype(F32)
    grad, dgain = head_backward(
        total[:, :size] * factor, proj_ref[...], gain_ref[...], cos_ref[...], sin_ref[...]
    )
    grad_ref[:, :size] = grad.astype(LOW)
    grad_ref[:, size:] = total[:, size:].astype(LOW)
    dgain_ref[...] = dgain


def kv_back(parts, proj, gain, cos2, sin2, factor, others):
    block, size = proj.shape
    operands = [parts, proj, gain[None], cos2, sin2]
    shapes = [
        jax.ShapeDtypeStruct((block, 2 * size), LOW),
        jax.ShapeDtypeStruct((1, size), F32),
    ]
    return pl.pallas_call(
        functools.partial(kv_back_kernel, factor),
        grid=(1,),
        in_specs=[full(value.shape) for value in operands]
        + [pl.BlockSpec(memory_space=pl.ANY)] * len(others),
        out_specs=[full(shape.shape) for shape in shapes],
        out_shape=shapes,
        compiler_params=params(),
        cost_estimate=cost(40 * block * size, 5e6),
    )(*operands, *others)


def unpack_kernel(experts, small_ref, *rest):
    router_ref, attn_ref, mlp_ref, q_ref, k_ref = rest[-5:]
    rows = small_ref[...].astype(F32)
    size = q_ref.shape[1]
    router_ref[...] = rows[:experts]
    attn_ref[...] = rows[experts : experts + 1]
    mlp_ref[...] = rows[experts + 1 : experts + 2]
    q_ref[...] = rows[experts + 2 : experts + 3, :size]
    k_ref[...] = rows[experts + 2 : experts + 3, size : 2 * size]


def unpack_small(small, experts, size, others):
    width = small.shape[1]
    shapes = [(experts, width), (1, width), (1, width), (1, size), (1, size)]
    return pl.pallas_call(
        functools.partial(unpack_kernel, experts),
        grid=(1,),
        in_specs=[full(small.shape)] + [pl.BlockSpec(memory_space=pl.ANY)] * len(others),
        out_specs=[full(shape) for shape in shapes],
        out_shape=[jax.ShapeDtypeStruct(shape, F32) for shape in shapes],
        compiler_params=params(),
        cost_estimate=cost(experts * width, 6 * experts * width),
    )(small, *others)


def pair_kernel(a_ref, b_ref, *rest):
    rest[-1][...] = (a_ref[...].astype(F32) + b_ref[...].astype(F32)).astype(LOW)


def hold_kernel(a_ref, *rest):
    rest[-1][...] = a_ref[...]


def hold(a, others):
    return pl.pallas_call(
        hold_kernel,
        grid=(1,),
        in_specs=[full(a.shape)] + [pl.BlockSpec(memory_space=pl.ANY)] * len(others),
        out_specs=full(a.shape),
        out_shape=jax.ShapeDtypeStruct(a.shape, a.dtype),
        compiler_params=params(),
        cost_estimate=cost(0, 4 * a.shape[0] * a.shape[1]),
    )(a, *others)


def pair_sum(a, b, others):
    rows, columns = a.shape
    tiles = 2 if rows % 32 == 0 else 1
    spec = pl.BlockSpec((rows // tiles, columns), lambda i: (i, 0))
    return pl.pallas_call(
        pair_kernel,
        grid=(tiles,),
        in_specs=[spec, spec] + [pl.BlockSpec(memory_space=pl.ANY)] * len(others),
        out_specs=spec,
        out_shape=jax.ShapeDtypeStruct((rows, columns), LOW),
        compiler_params=params(),
        cost_estimate=cost(rows * columns, 6 * rows * columns),
    )(a, b, *others)


def fold_kernel(n_pairs, s_ref, *refs):
    del s_ref
    send_ref, keep_ref = refs[-2:]
    totals = [
        (refs[2 * k][...].astype(F32) + refs[2 * k + 1][...].astype(F32)).astype(LOW)
        for k in range(n_pairs)
    ]
    for half, out_ref in enumerate((send_ref, keep_ref)):

        @pl.when(pl.program_id(0) == half)
        def _():
            first = 0
            for total in totals:
                last = first + total.shape[1]
                out_ref[:, first:last] = total
                first = last


def fold(pairs, bit, others):
    rows = pairs[0][1].shape[0]
    columns = sum(got.shape[1] for _, got in pairs)
    tiles = 2
    tile = rows // (2 * tiles)
    side = lambda h, m: (1 - m[0]) * (1 - h) + m[0] * h
    specs = []
    for _, got in pairs:
        wide = got.shape[1]
        specs += [pl.BlockSpec((tile, wide), lambda h, j, m: (side(h, m) * tiles + j, 0))] * 2
    shape = jax.ShapeDtypeStruct((rows // 2, columns), LOW)
    return pl.pallas_call(
        functools.partial(fold_kernel, len(pairs)),
        grid_spec=pltpu.PrefetchScalarGridSpec(
            num_scalar_prefetch=1,
            grid=(2, tiles),
            in_specs=specs + [pl.BlockSpec(memory_space=pl.ANY)] * len(others),
            out_specs=[
                pl.BlockSpec((tile, columns), lambda h, j, m: (j * (1 - h) + (tiles - 1) * h, 0)),
                pl.BlockSpec((tile, columns), lambda h, j, m: (j * h, 0)),
            ],
        ),
        out_shape=[shape, shape],
        compiler_params=params(),
        cost_estimate=cost(rows * columns, 6 * rows * columns),
    )(
        bit.astype(jnp.int32)[None],
        *[value for pair in pairs for value in pair],
        *others,
    )


def normed_kernel(q_ref, kv_ref, wq_ref, wkv_ref, rows_ref, *rest):
    out_ref, dgain_ref = rest[-2:]
    grad = dot_nt(q_ref[...], wq_ref[...]) + dot_nt(kv_ref[...], wkv_ref[...])
    out_ref[...] = grad.astype(LOW)
    dgain_ref[...] = jnp.sum(grad * rows_ref[...].astype(F32), axis=0, keepdims=True)


def normed_back(grad_q, grad_kv, w_q, w_kv, rows, others):
    block, width = rows.shape
    tile = 512
    column = lambda i: (0, i)
    return pl.pallas_call(
        normed_kernel,
        grid=(width // tile,),
        in_specs=[
            full(grad_q.shape),
            full(grad_kv.shape),
            pl.BlockSpec((tile, w_q.shape[1]), lambda i: (i, 0)),
            pl.BlockSpec((tile, w_kv.shape[1]), lambda i: (i, 0)),
            pl.BlockSpec((block, tile), column),
        ]
        + [pl.BlockSpec(memory_space=pl.ANY)] * len(others),
        out_specs=[pl.BlockSpec((block, tile), column), pl.BlockSpec((1, tile), column)],
        out_shape=[
            jax.ShapeDtypeStruct((block, width), LOW),
            jax.ShapeDtypeStruct((1, width), F32),
        ],
        compiler_params=params(),
        cost_estimate=cost(2 * block * width * (w_q.shape[1] + w_kv.shape[1]), 12e6),
    )(grad_q, grad_kv, w_q, w_kv, rows, *others)


def pack_kernel(experts, router_ref, attn_ref, gain_ref, mlp_ref, q_ref, k_ref, *rest):
    out_ref, rows_ref = rest[-2:]
    size = q_ref.shape[1]
    rows_ref[:experts] = router_ref[:experts]
    rows_ref[experts:] = jnp.zeros_like(rows_ref[experts:])
    rows_ref[experts : experts + 1] = attn_ref[...] / gain_ref[...]
    rows_ref[experts + 1 : experts + 2] = mlp_ref[...]
    rows_ref[experts + 2 : experts + 3, :size] = q_ref[...]
    rows_ref[experts + 2 : experts + 3, size : 2 * size] = k_ref[...]
    out_ref[...] = rows_ref[...].astype(LOW)


def pack_small(experts, router, attn, gain, mlp, q, k, others):
    width = attn.shape[1]
    n = lax.axis_size(ALL_AXES)
    shape = (-(-(experts + 3) // n) * n, width)
    operands = [router, attn, gain[None], mlp, q, k]
    return pl.pallas_call(
        functools.partial(pack_kernel, experts),
        grid=(1,),
        in_specs=[full(value.shape) for value in operands]
        + [pl.BlockSpec(memory_space=pl.ANY)] * len(others),
        out_specs=full(shape),
        out_shape=jax.ShapeDtypeStruct(shape, LOW),
        scratch_shapes=[pltpu.VMEM(shape, F32)],
        compiler_params=params(),
        cost_estimate=cost(shape[0] * width, 6 * shape[0] * width),
    )(*operands, *others)


def part_sum_kernel(parts_ref, *rest):
    total = parts_ref[0].astype(F32)
    for k in range(1, parts_ref.shape[0]):
        total += parts_ref[k].astype(F32)
    rest[-1][...] = total.astype(LOW)


def part_sum(parts, others):
    count, rows, columns = parts.shape
    tiles = 2
    return pl.pallas_call(
        part_sum_kernel,
        grid=(tiles,),
        in_specs=[pl.BlockSpec((count, rows // tiles, columns), lambda i: (0, i, 0))]
        + [pl.BlockSpec(memory_space=pl.ANY)] * len(others),
        out_specs=pl.BlockSpec((rows // tiles, columns), lambda i: (i, 0)),
        out_shape=jax.ShapeDtypeStruct((rows, columns), LOW),
        compiler_params=params(),
        cost_estimate=cost(count * rows * columns, 4 * count * rows * columns),
    )(parts, *others)


def widen_kernel(n_chunks, n_outs, at_ref, *refs):
    del at_ref
    outs = refs[-n_outs:]
    widths = [ref.shape[1] for ref in outs]
    for k in range(n_chunks):

        @pl.when(pl.program_id(0) == k)
        def _():
            first = 0
            for wide, out_ref in zip(widths, outs):
                out_ref[...] = refs[k][:, first : first + wide].astype(F32)
                first += wide


def widen(places, chunks, widths, total, others):
    rows, columns = chunks[0].shape
    count = len(chunks)
    return pl.pallas_call(
        functools.partial(widen_kernel, count, len(widths)),
        grid_spec=pltpu.PrefetchScalarGridSpec(
            num_scalar_prefetch=1,
            grid=(count,),
            in_specs=[full(chunk.shape) for chunk in chunks]
            + [pl.BlockSpec(memory_space=pl.ANY)] * len(others),
            out_specs=[pl.BlockSpec((rows, wide), lambda i, at: (at[i], 0)) for wide in widths],
        ),
        out_shape=[jax.ShapeDtypeStruct((total, wide), F32) for wide in widths],
        compiler_params=params(),
        cost_estimate=cost(rows * columns, 6 * count * rows * columns),
    )(jnp.stack(places).astype(jnp.int32), *chunks, *others)


def swap_dp(rows):
    return lax.ppermute(rows, "dp", [(0, 1), (1, 0)])


def swap_context(rows, s):
    n = lax.axis_size("context")
    return lax.ppermute(rows, "context", [(i, i ^ s) for i in range(n)])


def share_context(parts):
    return lax.all_to_all(parts, "context", split_axis=0, concat_axis=0, tiled=True)


def plane_turns():
    d, c = lax.axis_index("dp"), lax.axis_index("context")
    low, high = lax.rem(c, 2), lax.div(c, 2)

    def swap(first, second):
        perm = [(i, i ^ first) for i in range(4)] + [(4 + i, 4 + (i ^ second)) for i in range(4)]
        return lambda rows: lax.ppermute(rows, GROUP_AXES, perm)

    return [
        (jnp.where(d == 0, low, high), swap(1, 2)),
        (jnp.where(d == 0, high, low), swap(2, 1)),
    ]


def plane_first(pairs, others):
    (bit_1, _), _ = plane_turns()
    return fold(pairs, bit_1, others)


def plane_second(send, keep, others):
    (_, swap_1), (bit_2, _) = plane_turns()
    return fold([(keep, swap_1(send))], bit_2, others)


def plane_last(send, keep, others):
    _, (_, swap_2) = plane_turns()
    return pair_sum(keep, swap_2(send), others)


def plane_spread(own):
    (_, swap_1), (_, swap_2) = plane_turns()
    second = swap_2(own)
    return [own, second, swap_1(own), swap_1(second)]


def quarter_places(rank):
    d = lax.axis_index("dp")
    c = lax.axis_index("context")
    low, high = lax.rem(c, 2), lax.div(c, 2)
    places = []
    for core in (d, 1 - d):
        bit_1 = jnp.where(core == 0, low, high)
        bit_2 = jnp.where(core == 0, high, low)
        for flip_1, flip_2 in ((0, 0), (0, 1), (1, 0), (1, 1)):
            places.append(4 * core + rank(core, bit_1 ^ flip_1, bit_2 ^ flip_2))
    return places


def widen_all(quarters, places, widths, others):
    count = len(quarters)
    total = 2 * count * quarters[0].shape[0]
    chunks = quarters + [swap_dp(part) for part in quarters]
    return widen(places, chunks, widths, total, others)


def arrival_order(n):
    return [sorted(range(n), key=lambda j: (abs(j - i), j)) for i in range(n)]


def choose(index, options):
    distinct = []
    for option in options:
        if option is not None and not any(option is other for other in distinct):
            distinct.append(option)
    result = distinct[0]
    for option in distinct[1:]:
        mask = functools.reduce(
            jnp.logical_or, [index == i for i, other in enumerate(options) if other is option]
        )
        result = jnp.where(mask, option, result)
    return result


def line_gather(chunk):
    return line_steps({0: chunk}, 1, lax.axis_size("expert"))


def line_steps(found, first, stop):
    n = lax.axis_size("expert")
    found = dict(found)
    for s in range(first, stop):
        found[-s] = lax.ppermute(
            found[1 - s], "expert", [(i, i + 1) for i in range(s - 1, n - 1)]
        )
        found[s] = lax.ppermute(found[s - 1], "expert", [(i + 1, i) for i in range(n - s)])
    return found


def context_gather(rows):
    n = lax.axis_size("context")
    c = lax.axis_index("context")
    found = {0: rows}
    for s in range(1, n):
        found[s] = lax.ppermute(rows, "context", [(i, i ^ s) for i in range(n)])
    return jnp.concatenate([choose(c, [found[i ^ j] for i in range(n)]) for j in range(n)], axis=0)


def zero_of(*others):
    return functools.reduce(
        jnp.add,
        [
            lax.slice(other, (0,) * other.ndim, (1,) * other.ndim).reshape(()).astype(F32) * 0.0
            for other in others
        ],
    )


def after(value, *others):
    return (value.astype(F32) + zero_of(*others)).astype(value.dtype)


def on_device(
    layer_input,
    grad_output,
    attn_gain,
    query_weight,
    key_weight,
    value_weight,
    q_gain,
    k_gain,
    output_weight,
    mlp_gain,
    router,
    w_gate,
    w_up,
    w_down,
    routes,
    half_order,
):
    n_context = lax.axis_size("context")
    n_expert = lax.axis_size("expert")
    n_groups = lax.axis_size(GROUP_AXES)
    tok_dev, width = layer_input.shape[1:]
    size = q_gain.shape[0]
    kv_total = key_weight.shape[1] * n_expert
    group_dev = n_expert // (kv_total // size)
    kv_index = lax.axis_index("expert") // group_dev
    block = tok_dev * n_expert
    seq = block * n_context
    half = block // 2
    experts = router.shape[1]
    exp_dev = w_gate.shape[0]
    top = routes.shape[2]
    capacity = max(2, (tok_dev * top * 9 + 8 * experts - 1) // (8 * experts))
    scale = size ** (-0.5)

    seq_rows = jnp.arange(seq, dtype=jnp.int32)
    context = lax.axis_index("context")
    own_halves = lax.dynamic_slice_in_dim(half_order, 2 * context, 2)
    own_pos = (own_halves[:, None] * half + jnp.arange(half, dtype=jnp.int32)[None]).reshape(-1)
    per_half = half // TILE
    tile_pos = (half_order[:, None] * per_half + jnp.arange(per_half, dtype=jnp.int32)).reshape(-1)
    kidx = jnp.sum(
        (tile_pos[None, :] == jnp.arange(seq // TILE, dtype=jnp.int32)[:, None])
        * jnp.arange(seq // TILE, dtype=jnp.int32)[None, :],
        axis=1,
    ).astype(jnp.int32)
    qpos = lax.dynamic_slice_in_dim(tile_pos, context * (block // TILE), block // TILE)
    entry = jnp.arange(size)
    freq = jnp.power(THETA, -(2 * (entry % (size // 2))).astype(F32) / size)
    angles = own_pos.astype(F32)[:, None] * freq[None, :]
    cos2 = jnp.cos(angles)
    sin2 = jnp.sin(angles) * jnp.where(entry < size // 2, -1.0, 1.0)[None, :]

    place = lax.axis_index("expert")
    place_1 = place.astype(jnp.int32)[None]
    lanes = -(-2 * experts // 128) * 128
    mask = jnp.any(
        routes[0][:, :, None] == jnp.arange(lanes, dtype=jnp.int32)[None, None, :], axis=1
    )
    mask_wide = mask.astype(F32)
    router_rows = router.T

    x_low = layer_input[0]
    x_normal, _ = norm_parts(x_low.astype(F32))
    normed_found = line_gather((x_normal * attn_gain).astype(LOW))
    if group_dev == 1:
        kv_weights = jnp.concatenate([key_weight, value_weight], axis=1)
    else:
        key_whole = lax.all_gather(key_weight, "expert", axis=1, tiled=True)
        value_whole = lax.all_gather(value_weight, "expert", axis=1, tiled=True)
        kv_weights = jnp.concatenate(
            [
                lax.dynamic_slice_in_dim(key_whole, kv_index * size, size, 1),
                lax.dynamic_slice_in_dim(value_whole, kv_index * size, size, 1),
            ],
            axis=1,
        )
    grad_low = grad_output[0]
    normed_rows, own_kv, key_proj, grad_wide = project_keys(
        place_1,
        normed_found,
        kv_weights,
        k_gain,
        cos2,
        sin2,
        scale * LOG2E,
        grad_low,
        mask_wide,
    )
    grad_col = lax.all_gather(grad_wide, "expert", axis=0, tiled=True)
    kv_whole = context_gather(own_kv)
    queries, query_proj = project_queries(normed_rows, query_weight, q_gain, cos2, sin2)

    n_half = n_expert // 2
    order_here = jnp.asarray(arrival_order(n_expert), jnp.int32)[place]
    turn_here = jnp.sum(
        (order_here[:, None] == jnp.arange(n_expert, dtype=jnp.int32)[None, :])
        * jnp.arange(n_expert, dtype=jnp.int32)[:, None],
        axis=0,
    ).astype(jnp.int32)
    meta = jnp.concatenate([place_1, turn_here, order_here])
    grad_sent, slots = make_slots(meta, grad_col, width, n_groups, capacity)
    spreads, back_tables = make_tables(meta, slots, n_half, capacity)

    def swap_plane(rows):
        parts = rows.reshape(n_groups, -1, rows.shape[1])
        parts = lax.all_to_all(parts, GROUP_AXES, split_axis=0, concat_axis=0, tiled=True)
        return parts.reshape(rows.shape)

    attended, inverse = attend(qpos, kidx, queries, kv_whole, [])
    keys_t = kv_whole[:, :size].T
    attn_part = out_dot(attended, output_weight, [grad_col])
    attn_rows = lax.psum_scatter(attn_part, "expert", scatter_dimension=0, tiled=True)

    grad_x = swap_plane(grad_sent)
    act_pull = dot_nt(grad_x, w_down[0]).reshape(n_groups, 2, n_half * capacity, -1)

    hidden, mixed, probs = route_rows(
        x_low, attn_rows, mlp_gain, router_rows, mask_wide, experts, [keys_t]
    )

    who = (lax.axis_index(ALL_AXES) * exp_dev).astype(jnp.int32)[None]
    mixed_found = line_gather(mixed)
    near = spread_rows(place_1, spreads[0], mixed_found, range(n_half), [grad_x])
    x_near = swap_plane(near)
    worked_near = run_expert(who, x_near, w_gate[0], w_up[0], act_pull, 0, experts)
    far = spread_rows(place_1, spreads[1], mixed_found, range(n_half, n_expert), [x_near])
    x_far = swap_plane(far)
    worked_far = run_expert(who, x_far, w_gate[0], w_up[0], act_pull, 1, experts)
    xs = [x_near, x_far]
    acts, gate_lows, up_lows, copies = (list(pair) for pair in zip(worked_near, worked_far))
    back_far = swap_plane(copies[1])
    back_near = swap_plane(copies[0])
    join = lambda parts: jnp.concatenate(parts, axis=0)
    x_all = join([x[:, :width] for x in xs])
    grad_w_gate = dot_tn(x_all, join(gate_lows))
    grad_w_up = dot_tn(x_all, join(up_lows))
    grad_by_round = jnp.swapaxes(
        grad_x.reshape(n_groups, 2, n_half * capacity, width), 0, 1
    ).reshape(-1, width)
    grad_w_down = dot_tn(join(acts), grad_by_round)
    copies_col = combine_rows(
        meta, back_tables, [back_near, back_far], n_half, [grad_w_gate, grad_w_up]
    )
    copies_sum = lax.psum_scatter(copies_col, "expert", scatter_dimension=0, tiled=True)

    returned = [dot_nn(act, w_down[0]).astype(LOW) for act in acts]
    returned_near = swap_plane(returned[0])

    grad_hidden, grad_hidden_low, grad_mlp_gain, grad_router = route_back(
        copies_sum,
        grad_low,
        hidden,
        mlp_gain,
        router_rows,
        mask_wide,
        probs,
        experts,
        [returned_near, grad_w_down],
    )

    returned_far = swap_plane(returned[1])
    grad_attn = lax.all_gather(grad_hidden_low, "expert", axis=0, tiled=True)
    grad_o, centre = grad_attended(
        grad_attn, output_weight, attended, inverse, [returned_far]
    )
    combined = combine_rows(meta, back_tables, [returned_near, returned_far], n_half, [])
    output_rows = lax.psum_scatter(combined, "expert", scatter_dimension=0, tiled=True)
    w_out_send, w_out_keep = token_halves(attended, grad_attn, [combined])
    w_out_half = pair_sum(w_out_keep, swap_dp(w_out_send), [grad_o])
    w_out_parts = share_context(w_out_half.reshape(n_context, -1, width))
    grad_kv, grad_q, grad_q_gain = attend_back(
        qpos,
        kidx,
        queries,
        grad_o,
        centre,
        kv_whole,
        keys_t,
        query_proj,
        q_gain,
        cos2,
        sin2,
        [w_out_half],
    )
    kv_parts = share_context(grad_kv.astype(LOW).reshape(n_context, block, 2 * size))
    w_out_own = part_sum(w_out_parts, [grad_kv])
    w_query_send, w_query_keep = token_halves(normed_rows, grad_q, [w_out_own])
    w_query_got = swap_dp(w_query_send)
    output_rows = hidden + output_rows.astype(F32) + zero_of(w_query_keep)

    kv_grads, grad_k_gain = kv_back(
        kv_parts, key_proj, k_gain, cos2, sin2, scale, [w_query_keep]
    )
    w_out_quarters = plane_spread(w_out_own)
    pairs = [(w_query_keep, w_query_got)]
    widths = [query_weight.shape[1]]
    if group_dev == 1:
        w_kv_send, w_kv_keep = token_halves(normed_rows, kv_grads, [])
        pairs.append((w_kv_keep, swap_dp(w_kv_send)))
        widths += [key_weight.shape[1], value_weight.shape[1]]
    grad_normed, gain_rows = normed_back(
        grad_q, kv_grads, query_weight, kv_weights, normed_rows, []
    )
    send, keep = plane_first(pairs, [grad_normed])
    small = pack_small(
        experts,
        grad_router,
        gain_rows,
        attn_gain,
        grad_mlp_gain,
        grad_q_gain,
        grad_k_gain,
        [],
    )
    swap_all = lambda rows: lax.all_to_all(rows, ALL_AXES, split_axis=0, concat_axis=0, tiled=True)
    small_parts = swap_all(small.reshape(lax.axis_size(ALL_AXES), -1, width))
    small_own = jnp.sum(small_parts.astype(F32), axis=0).astype(LOW)
    second_send, second_keep = plane_second(send, keep, [small_own, *w_out_quarters[1:3]])
    grad_normed = lax.psum_scatter(grad_normed, "expert", scatter_dimension=0, tiled=True)
    quarter = plane_last(second_send, second_keep, [output_rows])
    grad_input = input_back(grad_normed, x_low, attn_gain, grad_hidden, [quarter])
    (grad_w_out,) = widen_all(
        w_out_quarters,
        quarter_places(lambda core, b1, b2: jnp.where(core == 0, b1 + 2 * b2, 2 * b1 + b2)),
        [width],
        [quarter],
    )
    small_sum = swap_all(jnp.broadcast_to(small_own[None], small_parts.shape))
    grad_router, grad_attn_gain, grad_mlp_gain, grad_q_gain, grad_k_gain = unpack_small(
        small_sum.reshape(small.shape), experts, size, []
    )
    (_, swap_1), (_, swap_2) = plane_turns()
    second = swap_2(quarter)
    held = hold(second, [grad_w_out, grad_input, grad_router])
    quarters = [quarter, second, swap_1(quarter), swap_1(held)]
    places = quarter_places(lambda core, b1, b2: 2 * b1 + b2)
    grad_w_query, *more = widen_all(quarters, places, widths, [])
    if group_dev == 1:
        grad_w_key, grad_w_value = more
    else:
        w_kv = token_dot(normed_rows, kv_grads, [])
        blank = jnp.zeros((width, kv_total), LOW)
        pieces = []
        for part in (w_kv[:, :size], w_kv[:, size:]):
            padded = lax.dynamic_update_slice(blank, part, (0, kv_index * size))
            pieces.append(lax.psum_scatter(padded, "expert", scatter_dimension=1, tiled=True))
        grad_w_key, grad_w_value = (lax.psum(piece, GROUP_AXES).astype(F32) for piece in pieces)
    return (
        output_rows.astype(LOW)[None],
        grad_input[None],
        grad_attn_gain[0],
        grad_w_query,
        grad_w_key,
        grad_w_value,
        grad_q_gain[0],
        grad_k_gain[0],
        grad_w_out,
        grad_mlp_gain[0],
        grad_router.T,
        grad_w_gate[None],
        grad_w_up[None],
        grad_w_down[None],
    )


def solution(mesh):
    rows = P("dp", ("context", "expert"), None)
    expert = P(ALL_AXES, None, None)
    columns = P(None, "expert")
    in_specs = (
        rows,
        rows,
        P(),
        columns,
        columns,
        columns,
        P(),
        P(),
        P("expert", None),
        P(),
        P(),
        expert,
        expert,
        expert,
        rows,
        P(),
    )
    out_specs = (
        rows,
        rows,
        P(),
        columns,
        columns,
        columns,
        P(),
        P(),
        P("expert", None),
        P(),
        P(),
        expert,
        expert,
        expert,
    )
    return jax.shard_map(
        on_device, mesh=mesh, in_specs=in_specs, out_specs=out_specs, check_vma=False
    )
```

```python
import functools
import math

import jax
import jax.numpy as jnp
from jax import lax
from jax.experimental import pallas as pl
from jax.experimental.pallas import tpu as pltpu
from jax.sharding import PartitionSpec as P

EPS = 1e-06
THETA = 1000000.0
TILE = 256
PIECE = 128
VMEM_BYTES = 56 * 1024 * 1024
LOG2E = math.log2(math.e)
LOW = jnp.bfloat16
F32 = jnp.float32
ALL_AXES = ("dp", "context", "expert")
GROUP_AXES = ("dp", "context")


def dot_nn(a, b):
    return lax.dot_general(a, b, (((1,), (0,)), ((), ())), preferred_element_type=F32)


def dot_nt(a, b):
    return lax.dot_general(a, b, (((1,), (1,)), ((), ())), preferred_element_type=F32)


def dot_tn(a, b):
    return lax.dot_general(a, b, (((0,), (0,)), ((), ())), preferred_element_type=F32)


def params(**more):
    return pltpu.CompilerParams(vmem_limit_bytes=VMEM_BYTES, **more)


def cost(flops, nbytes, exps=0):
    return pl.CostEstimate(flops=int(flops), bytes_accessed=int(nbytes), transcendentals=int(exps))


def head_forward(u, gain, cos2, sin2):
    rr = lax.rsqrt(jnp.mean(u * u, axis=-1, keepdims=True) + EPS)
    y = u * rr * gain
    return y * cos2 + pltpu.roll(y, 64, 1) * sin2


def head_backward(gy, u, gain, cos2, sin2):
    g = gy * cos2 - pltpu.roll(gy, 64, 1) * sin2
    rr = lax.rsqrt(jnp.mean(u * u, axis=-1, keepdims=True) + EPS)
    n = u * rr
    gn = g * gain
    grad = rr * (gn - n * jnp.mean(gn * n, axis=-1, keepdims=True))
    return grad, jnp.sum(g * n, axis=0, keepdims=True)


def query_kernel(x_ref, w_ref, gain_ref, cos_ref, sin_ref, rot_ref, proj_ref):
    tiles, heads, rows, size = rot_ref.shape
    acc = dot_nn(x_ref[...], w_ref[...])
    for h in range(heads):
        u = acc[:, h * size : (h + 1) * size]
        rot = head_forward(u, gain_ref[...], cos_ref[...], sin_ref[...])
        proj_ref[:, h] = u.reshape(tiles, rows, size)
        rot_ref[:, h] = rot.astype(LOW).reshape(tiles, rows, size)


def project_queries(normed, weight, gain, cos2, sin2):
    block, width = normed.shape
    size = cos2.shape[1]
    heads = weight.shape[1] // size
    tiles = block // TILE
    whole = lambda i: (0, 0)
    per = lambda i: (0, i, 0, 0)
    shape = (tiles, heads, TILE, size)
    return pl.pallas_call(
        query_kernel,
        grid=(heads // 2,),
        in_specs=[
            pl.BlockSpec((block, width), whole),
            pl.BlockSpec((width, 2 * size), lambda i: (0, i)),
            pl.BlockSpec((1, size), whole),
            pl.BlockSpec((block, size), whole),
            pl.BlockSpec((block, size), whole),
        ],
        out_specs=[pl.BlockSpec((tiles, 2, TILE, size), per)] * 2,
        out_shape=[jax.ShapeDtypeStruct(shape, LOW), jax.ShapeDtypeStruct(shape, F32)],
        compiler_params=params(),
        cost_estimate=cost(2 * block * width * heads * size, 12e6),
    )(normed, weight, gain[None], cos2, sin2)


def put_in_order(place, refs, out_ref):
    n = (len(refs) + 1) // 2
    rows = refs[0].shape[0]
    for distance in range(1 - n, n):
        ref = refs[distance + n - 1]
        at = place + distance

        @pl.when(jnp.logical_and(at >= 0, at < n))
        def _():
            out_ref[pl.ds(pl.multiple_of(at * rows, rows), rows), :] = ref[...]


def chunk_list(found):
    n = (len(found) + 1) // 2
    return [found[distance] for distance in range(1 - n, n)]


def key_kernel(factor, n_chunks, place_ref, *refs):
    w_ref, gain_ref, cos_ref, sin_ref, g_ref, mask_ref = refs[n_chunks:-4]
    rows_ref, kv_ref, proj_ref, wide_ref = refs[-4:]
    size = proj_ref.shape[1]
    width = g_ref.shape[1]
    put_in_order(place_ref[0], refs[:n_chunks], rows_ref)
    wide_ref[:, :width] = g_ref[...]
    wide_ref[:, width:] = mask_ref[...].astype(LOW)
    acc = dot_nn(rows_ref[...], w_ref[...])
    u = acc[:, :size]
    rot = head_forward(u, gain_ref[...], cos_ref[...], sin_ref[...])
    proj_ref[...] = u
    kv_ref[:, :size] = (rot * factor).astype(LOW)
    kv_ref[:, size:] = acc[:, size:].astype(LOW)


def full(shape):
    return pl.BlockSpec(shape, lambda *_: (0,) * len(shape))


def project_keys(place, found, weight, gain, cos2, sin2, factor, g, mask):
    chunks = chunk_list(found)
    rows, width = chunks[0].shape
    block, size = cos2.shape
    operands = [*chunks, weight, gain[None], cos2, sin2, g, mask]
    shapes = [
        jax.ShapeDtypeStruct((block, width), LOW),
        jax.ShapeDtypeStruct((block, 2 * size), LOW),
        jax.ShapeDtypeStruct((block, size), F32),
        jax.ShapeDtypeStruct((rows, width + mask.shape[1]), LOW),
    ]
    return pl.pallas_call(
        functools.partial(key_kernel, factor, len(chunks)),
        grid_spec=pltpu.PrefetchScalarGridSpec(
            num_scalar_prefetch=1,
            grid=(1,),
            in_specs=[full(x.shape) for x in operands],
            out_specs=[full(x.shape) for x in shapes],
        ),
        out_shape=shapes,
        compiler_params=params(),
        cost_estimate=cost(4 * block * width * size, 8e6),
    )(place, *operands)


def in_order(last, step):
    lax.fori_loop(0, lax.div(last, 2), lambda p, c: (step([2 * p, 2 * p + 1], False), c)[1], 0)

    @pl.when(lax.rem(last, 2) == 1)
    def _():
        step([last - 1, last], True)

    @pl.when(lax.rem(last, 2) == 0)
    def _():
        step([last], True)


def attend_kernel(qpos_ref, kidx_ref, q_ref, kv_ref, *rest):
    out_ref, inv_ref, acc_ref = rest[-3:]
    heads, rows, size = q_ref.shape[1:]
    acc_ref[...] = jnp.zeros_like(acc_ref)

    def step(places, masked):
        starts = [pl.multiple_of(kidx_ref[place] * rows, rows) for place in places]
        count = len(places) * rows
        keys = jnp.concatenate([kv_ref[pl.ds(start, rows), :size] for start in starts], axis=0)
        values = jnp.concatenate([kv_ref[pl.ds(start, rows), size:] for start in starts], axis=0)
        values = jnp.concatenate([values, jnp.ones((count, size), LOW)], axis=1)
        for h in range(heads):
            for first in range(0, rows, PIECE):
                part = slice(first, first + PIECE)
                e = jnp.exp2(dot_nt(q_ref[0, h, part], keys))
                if masked:
                    qi = lax.broadcasted_iota(jnp.int32, e.shape, 0) + first
                    ki = lax.broadcasted_iota(jnp.int32, e.shape, 1) - (count - rows)
                    e = jnp.where(ki <= qi, e, 0.0)
                acc_ref[h, part] += dot_nn(e.astype(LOW), values)

    in_order(qpos_ref[pl.program_id(0)], step)
    for h in range(heads):
        inv = 1.0 / acc_ref[h, :, size:]
        inv_ref[0, h] = inv
        out_ref[:, h * size : (h + 1) * size] = (acc_ref[h, :, :size] * inv).astype(LOW)


def attend(qpos, kidx, queries, kv, others):
    tiles, heads, rows, size = queries.shape
    seq = kv.shape[0]
    return pl.pallas_call(
        attend_kernel,
        grid_spec=pltpu.PrefetchScalarGridSpec(
            num_scalar_prefetch=2,
            grid=(tiles,),
            in_specs=[
                pl.BlockSpec((1, heads, rows, size), lambda i, a, b: (i, 0, 0, 0)),
                pl.BlockSpec((seq, 2 * size), lambda i, a, b: (0, 0)),
            ]
            + [pl.BlockSpec(memory_space=pl.ANY)] * len(others),
            out_specs=[
                pl.BlockSpec((rows, heads * size), lambda i, a, b: (i, 0)),
                pl.BlockSpec((1, heads, rows, size), lambda i, a, b: (i, 0, 0, 0)),
            ],
            scratch_shapes=[pltpu.VMEM((heads, rows, 2 * size), F32)],
        ),
        out_shape=[
            jax.ShapeDtypeStruct((tiles * rows, heads * size), LOW),
            jax.ShapeDtypeStruct((tiles, heads, rows, size), F32),
        ],
        compiler_params=params(),
        cost_estimate=cost(
            6 * tiles * rows * heads * seq * size, 8e6, tiles * rows * heads * seq
        ),
    )(qpos, kidx, queries, kv, *others)


def grad_out_kernel(rows_ref, w_ref, o_ref, inv_ref, *rest):
    do_ref, centre_ref = rest[-2:]
    tiles, heads, rows, size = do_ref.shape
    acc = dot_nt(rows_ref[...], w_ref[...])
    for t in range(tiles):
        for h in range(heads):
            part = slice(t * rows, (t + 1) * rows), slice(h * size, (h + 1) * size)
            low = (acc[part] * inv_ref[t, h]).astype(LOW)
            do_ref[t, h] = low
            product = low.astype(F32) * o_ref[part].astype(F32)
            centre = jnp.sum(jnp.transpose(product), axis=0, keepdims=True)
            centre_ref[t, h] = jnp.broadcast_to(centre, (8, rows))


def grad_attended(grad_rows, weight, attended, inverse, others):
    tiles, heads, rows, size = inverse.shape
    block, width = grad_rows.shape
    return pl.pallas_call(
        grad_out_kernel,
        grid=(heads // 2,),
        in_specs=[
            pl.BlockSpec((block, width), lambda i: (0, 0)),
            pl.BlockSpec((2 * size, width), lambda i: (i, 0)),
            pl.BlockSpec((block, 2 * size), lambda i: (0, i)),
            pl.BlockSpec((tiles, 2, rows, size), lambda i: (0, i, 0, 0)),
        ]
        + [pl.BlockSpec(memory_space=pl.ANY)] * len(others),
        out_specs=[
            pl.BlockSpec((tiles, 2, rows, size), lambda i: (0, i, 0, 0)),
            pl.BlockSpec((tiles, 2, 8, rows), lambda i: (0, i, 0, 0)),
        ],
        out_shape=[
            jax.ShapeDtypeStruct((tiles, heads, rows, size), LOW),
            jax.ShapeDtypeStruct((tiles, heads, 8, rows), F32),
        ],
        compiler_params=params(),
        cost_estimate=cost(2 * block * width * heads * size, 12e6),
    )(grad_rows, weight, attended, inverse, *others)


def attend_back_kernel(
    qpos_ref,
    kidx_ref,
    q_ref,
    do_ref,
    centre_ref,
    kv_ref,
    kt_ref,
    proj_ref,
    gain_ref,
    cos_ref,
    sin_ref,
    *rest,
):
    dkv_ref, dq_ref, dgain_ref, acc_ref, e_ref, ds_ref = rest[-6:]
    heads, rows, size = q_ref.shape[1:]

    @pl.when(pl.program_id(0) == 0)
    def _():
        dkv_ref[...] = jnp.zeros_like(dkv_ref)
        dgain_ref[...] = jnp.zeros_like(dgain_ref)

    acc_ref[...] = jnp.zeros_like(acc_ref)

    def step(places, masked):
        starts = [pl.multiple_of(kidx_ref[place] * rows, rows) for place in places]
        count = len(places) * rows
        keys = jnp.concatenate([kv_ref[pl.ds(start, rows), :size] for start in starts], axis=0)
        values = jnp.concatenate([kv_ref[pl.ds(start, rows), size:] for start in starts], axis=0)
        keys_t = jnp.concatenate([kt_ref[:, pl.ds(start, rows)] for start in starts], axis=1)
        for h in range(heads):
            query, grad = q_ref[0, h], do_ref[0, h]
            centre = centre_ref[0, h, 0:1]
            columns = slice(h * rows, (h + 1) * rows)
            for first in range(0, count, PIECE):
                part = slice(first, first + PIECE)
                e = jnp.exp2(dot_nt(keys[part], query))
                if masked and first >= count - rows:
                    ki = lax.broadcasted_iota(jnp.int32, e.shape, 0) + (first - (count - rows))
                    qi = lax.broadcasted_iota(jnp.int32, e.shape, 1)
                    e = jnp.where(ki <= qi, e, 0.0)
                ds = e * (dot_nt(values[part], grad) - centre)
                e_ref[part, columns] = e.astype(LOW)
                ds_ref[part, columns] = ds.astype(LOW)
            acc_ref[h] += dot_nn(keys_t, ds_ref[:count, columns])
        dk = dot_nn(ds_ref[:count], q_ref[0].reshape(heads * rows, size))
        dv = dot_nn(e_ref[:count], do_ref[0].reshape(heads * rows, size))
        for k, start in enumerate(starts):
            dkv_ref[pl.ds(start, rows), :size] += dk[k * rows : (k + 1) * rows]
            dkv_ref[pl.ds(start, rows), size:] += dv[k * rows : (k + 1) * rows]

    in_order(qpos_ref[pl.program_id(0)], step)
    total = jnp.zeros((1, size), F32)
    for h in range(heads):
        grad, gain_part = head_backward(
            jnp.transpose(acc_ref[h]) * (1.0 / LOG2E),
            proj_ref[0, h],
            gain_ref[...],
            cos_ref[...],
            sin_ref[...],
        )
        dq_ref[:, h * size : (h + 1) * size] = grad.astype(LOW)
        total += gain_part
    dgain_ref[...] += total


def attend_back(qpos, kidx, queries, grads, centre, kv, keys_t, proj, gain, cos2, sin2, others):
    tiles, heads, rows, size = queries.shape
    seq = kv.shape[0]
    per = pl.BlockSpec((1, heads, rows, size), lambda i, a, b: (i, 0, 0, 0))
    flat = lambda i, a, b: (0, 0)
    rowwise = lambda i, a, b: (i, 0)
    return pl.pallas_call(
        attend_back_kernel,
        grid_spec=pltpu.PrefetchScalarGridSpec(
            num_scalar_prefetch=2,
            grid=(tiles,),
            in_specs=[
                per,
                per,
                pl.BlockSpec((1, heads, 8, rows), lambda i, a, b: (i, 0, 0, 0)),
                pl.BlockSpec((seq, 2 * size), flat),
                pl.BlockSpec((size, seq), flat),
                per,
                pl.BlockSpec((1, size), flat),
                pl.BlockSpec((rows, size), rowwise),
                pl.BlockSpec((rows, size), rowwise),
            ]
            + [pl.BlockSpec(memory_space=pl.ANY)] * len(others),
            out_specs=[
                pl.BlockSpec((seq, 2 * size), flat),
                pl.BlockSpec((rows, heads * size), rowwise),
                pl.BlockSpec((1, size), flat),
            ],
            scratch_shapes=[pltpu.VMEM((heads, size, rows), F32)]
            + [pltpu.VMEM((2 * rows, heads * rows), LOW)] * 2,
        ),
        out_shape=[
            jax.ShapeDtypeStruct((seq, 2 * size), F32),
            jax.ShapeDtypeStruct((tiles * rows, heads * size), LOW),
            jax.ShapeDtypeStruct((1, size), F32),
        ],
        compiler_params=params(),
        cost_estimate=cost(
            15 * tiles * rows * heads * seq * size, 12e6, tiles * rows * heads * seq
        ),
    )(qpos, kidx, queries, grads, centre, kv, keys_t, proj, gain[None], cos2, sin2, *others)


def out_kernel(a_ref, b_ref, *rest):
    rest[-1][...] = dot_nn(a_ref[...], b_ref[...]).astype(LOW)


def out_dot(a, b, others):
    block, inner = a.shape
    columns = b.shape[1]
    tile = min(columns, 512)
    return pl.pallas_call(
        out_kernel,
        grid=(columns // tile,),
        in_specs=[
            pl.BlockSpec((block, inner), lambda i: (0, 0)),
            pl.BlockSpec((inner, tile), lambda i: (0, i)),
        ]
        + [pl.BlockSpec(memory_space=pl.ANY)] * len(others),
        out_specs=pl.BlockSpec((block, tile), lambda i: (0, i)),
        out_shape=jax.ShapeDtypeStruct((block, columns), LOW),
        compiler_params=params(),
        cost_estimate=cost(2 * block * inner * columns, 8e6),
    )(a, b, *others)


def token_kernel(a_ref, b_ref, *rest):
    rest[-1][...] = dot_tn(a_ref[...], b_ref[...]).astype(LOW)


def token_dot(a, b, others):
    block, rows = a.shape
    columns = b.shape[1]
    tile = min(rows, 512)
    return pl.pallas_call(
        token_kernel,
        grid=(rows // tile,),
        in_specs=[
            pl.BlockSpec((block, tile), lambda i: (0, i)),
            pl.BlockSpec((block, columns), lambda i: (0, 0)),
        ]
        + [pl.BlockSpec(memory_space=pl.ANY)] * len(others),
        out_specs=pl.BlockSpec((tile, columns), lambda i: (i, 0)),
        out_shape=jax.ShapeDtypeStruct((rows, columns), LOW),
        compiler_params=params(),
        cost_estimate=cost(2 * block * rows * columns, 6e6),
    )(a, b, *others)


def halves_kernel(d_ref, a_ref, b_ref, *rest):
    send_ref, keep_ref = rest[-2:]
    product = dot_tn(a_ref[...], b_ref[...]).astype(LOW)

    @pl.when(pl.program_id(0) == 0)
    def _():
        send_ref[...] = product

    @pl.when(pl.program_id(0) == 1)
    def _():
        keep_ref[...] = product


def token_halves(a, b, others):
    block, rows = a.shape
    columns = b.shape[1]
    tiles = 2 if rows % 512 == 0 else 1
    tile = rows // (2 * tiles)
    d = lax.axis_index("dp").astype(jnp.int32)[None]
    half = jax.ShapeDtypeStruct((rows // 2, columns), LOW)
    return pl.pallas_call(
        halves_kernel,
        grid_spec=pltpu.PrefetchScalarGridSpec(
            num_scalar_prefetch=1,
            grid=(2, tiles),
            in_specs=[
                pl.BlockSpec(
                    (block, tile),
                    lambda h, j, d: (0, ((1 - d[0]) * (1 - h) + d[0] * h) * tiles + j),
                ),
                pl.BlockSpec((block, columns), lambda h, j, d: (0, 0)),
            ]
            + [pl.BlockSpec(memory_space=pl.ANY)] * len(others),
            out_specs=[
                pl.BlockSpec((tile, columns), lambda h, j, d: (j * (1 - h) + (tiles - 1) * h, 0)),
                pl.BlockSpec((tile, columns), lambda h, j, d: (j * h, 0)),
            ],
        ),
        out_shape=[half, half],
        compiler_params=params(),
        cost_estimate=cost(2 * block * rows * columns, 6e6),
    )(d, a, b, *others)


def split_low(value):
    high = value.astype(LOW)
    return high, (value - high.astype(F32)).astype(LOW)


def norm_parts(rows):
    rr = lax.rsqrt(jnp.mean(rows * rows, axis=-1, keepdims=True) + EPS)
    return rows * rr, rr


def norm_back(grad, normal, rr, gain):
    weighted = grad * gain
    return rr * (weighted - normal * jnp.mean(weighted * normal, axis=-1, keepdims=True))


def add_all(refs):
    return functools.reduce(jnp.add, [ref[...].astype(F32) for ref in refs])


def pad_rows(rows, count):
    if rows.shape[0] == count:
        return rows
    return jnp.concatenate(
        [rows, jnp.zeros((count - rows.shape[0], rows.shape[1]), rows.dtype)], axis=0
    )


def router_kernel(experts, *refs):
    x_ref, attn_ref, gain_ref, router_ref, mask_ref = refs[:5]
    hidden_ref, mixed_ref, probs_ref = refs[-3:]
    width = x_ref.shape[1]
    lanes = mask_ref.shape[1]
    hidden = add_all([x_ref, attn_ref])
    hidden_ref[...] = hidden
    mixed = (norm_parts(hidden)[0] * gain_ref[...]).astype(LOW)
    mixed_ref[:, :width] = mixed
    logits = dot_nt(mixed, pad_rows(router_ref[...], lanes))
    lane = lax.broadcasted_iota(jnp.int32, logits.shape, 1)
    logits = jnp.where(lane < experts, logits, -1e30)
    weights = jnp.exp(logits - jnp.max(logits, axis=1, keepdims=True))
    probs = weights / jnp.sum(weights, axis=1, keepdims=True)
    probs_ref[...] = probs
    chosen = probs * mask_ref[...]
    high, low = split_low(chosen / jnp.sum(chosen, axis=1, keepdims=True))
    both = high.astype(F32) + pltpu.roll(low.astype(F32), experts, 1)
    mixed_ref[:, width:] = both.astype(LOW)


def route_rows(x, attn, gain, router, mask, experts, others):
    tokens, width = x.shape
    lanes = mask.shape[1]
    operands = [x, attn, gain[None], router, mask]
    shapes = [
        jax.ShapeDtypeStruct((tokens, width), F32),
        jax.ShapeDtypeStruct((tokens, width + lanes), LOW),
        jax.ShapeDtypeStruct((tokens, lanes), F32),
    ]
    return pl.pallas_call(
        functools.partial(router_kernel, experts),
        grid=(1,),
        in_specs=[full(value.shape) for value in operands]
        + [pl.BlockSpec(memory_space=pl.ANY)] * len(others),
        out_specs=[full(shape.shape) for shape in shapes],
        out_shape=shapes,
        compiler_params=params(),
        cost_estimate=cost(2 * tokens * width * lanes, 5e6),
    )(*operands, *others)


def one_hot(slots, count, first):
    groups, tokens = slots.shape
    slot = lax.broadcasted_iota(jnp.int32, (groups, count, tokens), 1).astype(F32)
    same = slots[:, None, :] == slot + float(first)
    return jnp.where(same, 1.0, 0.0).reshape(groups * count, tokens)


def slot_kernel(capacity, meta_ref, col_ref, rows_ref, slots_ref):
    groups, block = slots_ref.shape
    rows, width = rows_ref.shape
    n = rows // groups // capacity
    tokens = block // n
    mask = col_ref[:, width:]
    lanes = mask.shape[1]
    padded = -(-groups // 16) * 16
    group = lax.broadcasted_iota(jnp.int32, (padded, lanes), 0)
    lane = lax.broadcasted_iota(jnp.int32, (padded, lanes), 1)
    wanted = jnp.logical_and(lane == group * n + meta_ref[0], group < groups)
    hits = dot_nt(jnp.where(wanted, 1.0, 0.0).astype(LOW), mask)
    before = lax.broadcasted_iota(jnp.int32, (tokens, tokens), 0)
    after_it = lax.broadcasted_iota(jnp.int32, (tokens, tokens), 1)
    earlier = jnp.where(before < after_it, 1.0, 0.0).astype(LOW)
    for z in range(n):
        hit = hits[:, z * tokens : (z + 1) * tokens]
        rank = dot_nn(hit.astype(LOW), earlier)
        turn = (meta_ref[1 + z] * capacity).astype(F32)
        slot = jnp.where(hit > 0.5, rank + turn, -1.0)
        slots_ref[:, z * tokens : (z + 1) * tokens] = slot[:groups]
    spread = one_hot(slots_ref[...], n * capacity, 0).astype(LOW)
    rows_ref[...] = dot_nn(spread, col_ref[:, :width]).astype(LOW)


def make_slots(meta, col, width, groups, capacity):
    block = col.shape[0]
    n = lax.axis_size("expert")
    shapes = [
        jax.ShapeDtypeStruct((groups * n * capacity, width), LOW),
        jax.ShapeDtypeStruct((groups, block), F32),
    ]
    return pl.pallas_call(
        functools.partial(slot_kernel, capacity),
        grid_spec=pltpu.PrefetchScalarGridSpec(
            num_scalar_prefetch=1,
            grid=(1,),
            in_specs=[full(col.shape)],
            out_specs=[full(shape.shape) for shape in shapes],
        ),
        out_shape=shapes,
        compiler_params=params(),
        cost_estimate=cost(2 * groups * n * capacity * block * width, 8e6),
    )(meta, col)


def table_kernel(capacity, n_half, meta_ref, slots_ref, near_ref, far_ref, near_back_ref, far_back_ref):
    n = 2 * n_half
    tokens = slots_ref.shape[1] // n
    cap_half = n_half * capacity
    for part, (to_ref, back_ref) in enumerate([(near_ref, near_back_ref), (far_ref, far_back_ref)]):
        pieces = []
        for k in range(n_half):
            start = pl.multiple_of(meta_ref[1 + n + part * n_half + k] * tokens, tokens)
            pieces.append(slots_ref[:, pl.ds(start, tokens)])
        spread = one_hot(jnp.concatenate(pieces, axis=1), cap_half, part * cap_half)
        to_ref[...] = spread.astype(LOW)
        back_ref[...] = jnp.transpose(spread).astype(LOW)


def make_tables(meta, slots, n_half, capacity):
    groups, block = slots.shape
    rows = groups * n_half * capacity
    shapes = [jax.ShapeDtypeStruct((rows, block // 2), LOW)] * 2
    shapes += [jax.ShapeDtypeStruct((block // 2, rows), LOW)] * 2
    outs = pl.pallas_call(
        functools.partial(table_kernel, capacity, n_half),
        grid_spec=pltpu.PrefetchScalarGridSpec(
            num_scalar_prefetch=1,
            grid=(1,),
            in_specs=[full(slots.shape)],
            out_specs=[full(shape.shape) for shape in shapes],
        ),
        out_shape=shapes,
        compiler_params=params(),
        cost_estimate=cost(8 * rows * block, 3e6),
    )(meta, slots)
    return outs[:2], outs[2:]


def spread_kernel(choices, place_ref, spread_ref, *refs):
    out_ref, rows_ref = refs[-2:]
    for k, by_place in enumerate(choices):
        for which in sorted(set(by_place)):
            hit = functools.reduce(
                jnp.logical_or,
                [place_ref[0] == i for i, other in enumerate(by_place) if other == which],
            )

            @pl.when(hit)
            def _():
                tokens = refs[which].shape[0]
                rows_ref[k * tokens : (k + 1) * tokens] = refs[which][...]

    out_ref[...] = dot_nn(spread_ref[...], rows_ref[...]).astype(LOW)


def spread_rows(place, spread, found, turns, others):
    n = lax.axis_size("expert")
    order = arrival_order(n)
    distances = sorted({order[i][turn] - i for i in range(n) for turn in turns})
    choices = [[distances.index(order[i][turn] - i) for i in range(n)] for turn in turns]
    chunks = [found[distance] for distance in distances]
    tokens, wide = chunks[0].shape
    rows = spread.shape[0]
    return pl.pallas_call(
        functools.partial(spread_kernel, choices),
        grid_spec=pltpu.PrefetchScalarGridSpec(
            num_scalar_prefetch=1,
            grid=(1,),
            in_specs=[full(spread.shape)]
            + [full(chunk.shape) for chunk in chunks]
            + [pl.BlockSpec(memory_space=pl.ANY)] * len(others),
            out_specs=full((rows, wide)),
            scratch_shapes=[pltpu.VMEM((len(turns) * tokens, wide), LOW)],
        ),
        out_shape=jax.ShapeDtypeStruct((rows, wide), LOW),
        compiler_params=params(),
        cost_estimate=cost(2 * rows * len(turns) * tokens * wide, 5e6),
    )(place, spread, *chunks, *others)


def router_back_kernel(experts, *refs):
    sum_ref, g_ref, hidden_ref, gain_ref, router_ref, mask_ref, probs_ref = refs[:7]
    grad_ref, low_ref, dgain_ref, drouter_ref = refs[-4:]
    width = g_ref.shape[1]
    lanes = mask_ref.shape[1]
    total = sum_ref[...].astype(F32)
    table = total[:, width:]
    mask, probs = mask_ref[...], probs_ref[...]
    grad_gates = (table + pltpu.roll(table, lanes - experts, 1)) * mask
    chosen = probs * mask
    chosen_sum = jnp.sum(chosen, axis=1, keepdims=True)
    mean = jnp.sum(grad_gates * (chosen / chosen_sum), axis=1, keepdims=True)
    centred = mask * (grad_gates - mean) / chosen_sum
    grad_logits = probs * (centred - jnp.sum(centred * chosen, axis=1, keepdims=True))
    high, low = split_low(grad_logits)
    router = pad_rows(router_ref[...], lanes)
    grad = total[:, :width] + dot_nn(high, router) + dot_nn(low, router)
    normal, rr = norm_parts(hidden_ref[...])
    mixed = (normal * gain_ref[...]).astype(LOW)
    drouter_ref[...] = dot_tn(high, mixed) + dot_tn(low, mixed)
    dgain_ref[...] = jnp.sum(grad * normal, axis=0, keepdims=True)
    grad_hidden = g_ref[...].astype(F32) + norm_back(grad, normal, rr, gain_ref[...])
    grad_ref[...] = grad_hidden
    low_ref[...] = grad_hidden.astype(LOW)


def route_back(summed, g, hidden, gain, router, mask, probs, experts, others):
    tokens, width = g.shape
    lanes = mask.shape[1]
    operands = [summed, g, hidden, gain[None], router, mask, probs]
    shapes = [
        jax.ShapeDtypeStruct((tokens, width), F32),
        jax.ShapeDtypeStruct((tokens, width), LOW),
        jax.ShapeDtypeStruct((1, width), F32),
        jax.ShapeDtypeStruct((lanes, width), F32),
    ]
    return pl.pallas_call(
        functools.partial(router_back_kernel, experts),
        grid=(1,),
        in_specs=[full(value.shape) for value in operands]
        + [pl.BlockSpec(memory_space=pl.ANY)] * len(others),
        out_specs=[full(shape.shape) for shape in shapes],
        out_shape=shapes,
        compiler_params=params(),
        cost_estimate=cost(8 * tokens * width * lanes, 8e6),
    )(*operands, *others)


def combine_kernel(meta_ref, table_ref, rows_ref, *rest):
    del meta_ref
    rest[-1][...] = dot_nn(table_ref[...], rows_ref[...]).astype(LOW)


def combine_part(meta, table, rows, first, n, into, others):
    block, slots = table.shape
    wide = rows.shape[1]
    tokens = block // (n // 2)
    return pl.pallas_call(
        combine_kernel,
        grid_spec=pltpu.PrefetchScalarGridSpec(
            num_scalar_prefetch=1,
            grid=(n // 2,),
            in_specs=[
                pl.BlockSpec((tokens, slots), lambda i, m: (i, 0)),
                full(rows.shape),
            ]
            + [pl.BlockSpec(memory_space=pl.ANY)] * (len(into) + len(others)),
            out_specs=pl.BlockSpec((tokens, wide), lambda i, m: (m[1 + n + first + i], 0)),
        ),
        out_shape=jax.ShapeDtypeStruct((n * tokens, wide), LOW),
        input_output_aliases={3: 0} if into else {},
        compiler_params=params(),
        cost_estimate=cost(2 * slots * block * wide, 6e6),
    )(meta, table, rows, *into, *others)


def combine_rows(meta, tables, rows, n_half, others):
    near = combine_part(meta, tables[0], rows[0], 0, 2 * n_half, [], [])
    return combine_part(meta, tables[1], rows[1], n_half, 2 * n_half, [near], others)


def expert_kernel(experts, who_ref, x_ref, gate_ref, up_ref, pull_ref, *rest):
    act_ref, dgate_ref, dup_ref, copy_ref = rest[-4:]
    width = gate_ref.shape[0]
    x = x_ref[:, :width]
    table = x_ref[:, width:].astype(F32)
    lane = lax.broadcasted_iota(jnp.int32, table.shape, 1)
    mine = who_ref[0]
    gate = jnp.sum(
        jnp.where(jnp.logical_or(lane == mine, lane == mine + experts), table, 0.0),
        axis=1,
        keepdims=True,
    )
    pre_gate = dot_nn(x, gate_ref[...])
    pre_up = dot_nn(x, up_ref[...])
    pull = pull_ref[...].reshape(pre_up.shape)
    sig = 1.0 / (1.0 + jnp.exp(-pre_gate))
    silu = pre_gate * sig
    act = silu * pre_up
    act_ref[...] = (act * gate).astype(LOW)
    high, low = split_low(jnp.sum(act * pull, axis=1, keepdims=True))
    pull = pull * gate
    dup = (pull * silu).astype(LOW)
    dgate = (pull * pre_up * (sig * (1.0 + pre_gate * (1.0 - sig)))).astype(LOW)
    dgate_ref[...] = dgate
    dup_ref[...] = dup
    copy_ref[:, :width] = (dot_nt(dgate, gate_ref[...]) + dot_nt(dup, up_ref[...])).astype(LOW)
    back = jnp.where(lane == mine, high.astype(F32), 0.0)
    back = jnp.where(lane == mine + experts, low.astype(F32), back)
    copy_ref[:, width:] = back.astype(LOW)


def run_expert(who, x, w_gate, w_up, pull, part, experts):
    rows, wide = x.shape
    width, hidden = w_gate.shape
    groups, _, slots, _ = pull.shape
    each = groups // 2
    tile = each * slots
    by_rows = lambda columns: pl.BlockSpec((tile, columns), lambda i, p: (i, 0))
    return pl.pallas_call(
        functools.partial(expert_kernel, experts),
        grid_spec=pltpu.PrefetchScalarGridSpec(
            num_scalar_prefetch=1,
            grid=(2,),
            in_specs=[
                by_rows(wide),
                full(w_gate.shape),
                full(w_up.shape),
                pl.BlockSpec((each, 1, slots, hidden), lambda i, p: (i, part, 0, 0)),
            ],
            out_specs=[by_rows(hidden), by_rows(hidden), by_rows(hidden), by_rows(wide)],
        ),
        out_shape=[jax.ShapeDtypeStruct((rows, hidden), LOW)] * 3
        + [jax.ShapeDtypeStruct((rows, wide), LOW)],
        compiler_params=params(),
        cost_estimate=cost(8 * rows * width * hidden, 20e6, rows * hidden),
    )(who, x, w_gate, w_up, pull)


def input_kernel(grad_ref, x_ref, gain_ref, more_ref, out_ref):
    normal, rr = norm_parts(x_ref[...].astype(F32))
    grad = grad_ref[...].astype(F32)
    out_ref[...] = more_ref[...] + norm_back(grad, normal, rr, gain_ref[...])


def input_back(grad, x, gain, more):
    tokens, width = x.shape
    operands = [grad, x, gain[None], more]
    return pl.pallas_call(
        input_kernel,
        grid=(1,),
        in_specs=[full(value.shape) for value in operands],
        out_specs=full(more.shape),
        out_shape=jax.ShapeDtypeStruct((tokens, width), F32),
        compiler_params=params(),
        cost_estimate=cost(20 * tokens * width, 5e6),
    )(*operands)


def kv_back_kernel(factor, parts_ref, proj_ref, gain_ref, cos_ref, sin_ref, *rest):
    grad_ref, dgain_ref = rest[-2:]
    size = proj_ref.shape[1]
    total = parts_ref[0].astype(F32)
    for k in range(1, parts_ref.shape[0]):
        total += parts_ref[k].astype(F32)
    grad, dgain = head_backward(
        total[:, :size] * factor, proj_ref[...], gain_ref[...], cos_ref[...], sin_ref[...]
    )
    grad_ref[:, :size] = grad.astype(LOW)
    grad_ref[:, size:] = total[:, size:].astype(LOW)
    dgain_ref[...] = dgain


def kv_back(parts, proj, gain, cos2, sin2, factor, others):
    block, size = proj.shape
    operands = [parts, proj, gain[None], cos2, sin2]
    shapes = [
        jax.ShapeDtypeStruct((block, 2 * size), LOW),
        jax.ShapeDtypeStruct((1, size), F32),
    ]
    return pl.pallas_call(
        functools.partial(kv_back_kernel, factor),
        grid=(1,),
        in_specs=[full(value.shape) for value in operands]
        + [pl.BlockSpec(memory_space=pl.ANY)] * len(others),
        out_specs=[full(shape.shape) for shape in shapes],
        out_shape=shapes,
        compiler_params=params(),
        cost_estimate=cost(40 * block * size, 5e6),
    )(*operands, *others)


def unpack_kernel(experts, small_ref, *rest):
    router_ref, attn_ref, mlp_ref, q_ref, k_ref = rest[-5:]
    rows = small_ref[...].astype(F32)
    size = q_ref.shape[1]
    router_ref[...] = rows[:experts]
    attn_ref[...] = rows[experts : experts + 1]
    mlp_ref[...] = rows[experts + 1 : experts + 2]
    q_ref[...] = rows[experts + 2 : experts + 3, :size]
    k_ref[...] = rows[experts + 2 : experts + 3, size : 2 * size]


def unpack_small(small, experts, size, others):
    width = small.shape[1]
    shapes = [(experts, width), (1, width), (1, width), (1, size), (1, size)]
    return pl.pallas_call(
        functools.partial(unpack_kernel, experts),
        grid=(1,),
        in_specs=[full(small.shape)] + [pl.BlockSpec(memory_space=pl.ANY)] * len(others),
        out_specs=[full(shape) for shape in shapes],
        out_shape=[jax.ShapeDtypeStruct(shape, F32) for shape in shapes],
        compiler_params=params(),
        cost_estimate=cost(experts * width, 6 * experts * width),
    )(small, *others)


def pair_kernel(a_ref, b_ref, *rest):
    rest[-1][...] = (a_ref[...].astype(F32) + b_ref[...].astype(F32)).astype(LOW)


def pair_sum(a, b, others):
    rows, columns = a.shape
    tiles = 2 if rows % 32 == 0 else 1
    spec = pl.BlockSpec((rows // tiles, columns), lambda i: (i, 0))
    return pl.pallas_call(
        pair_kernel,
        grid=(tiles,),
        in_specs=[spec, spec] + [pl.BlockSpec(memory_space=pl.ANY)] * len(others),
        out_specs=spec,
        out_shape=jax.ShapeDtypeStruct((rows, columns), LOW),
        compiler_params=params(),
        cost_estimate=cost(rows * columns, 6 * rows * columns),
    )(a, b, *others)


def fold_kernel(n_pairs, s_ref, *refs):
    del s_ref
    send_ref, keep_ref = refs[-2:]
    totals = [
        (refs[2 * k][...].astype(F32) + refs[2 * k + 1][...].astype(F32)).astype(LOW)
        for k in range(n_pairs)
    ]
    for half, out_ref in enumerate((send_ref, keep_ref)):

        @pl.when(pl.program_id(0) == half)
        def _():
            first = 0
            for total in totals:
                last = first + total.shape[1]
                out_ref[:, first:last] = total
                first = last


def fold(pairs, bit, others):
    rows = pairs[0][1].shape[0]
    columns = sum(got.shape[1] for _, got in pairs)
    tiles = 2
    tile = rows // (2 * tiles)
    side = lambda h, m: (1 - m[0]) * (1 - h) + m[0] * h
    specs = []
    for _, got in pairs:
        wide = got.shape[1]
        specs += [pl.BlockSpec((tile, wide), lambda h, j, m: (side(h, m) * tiles + j, 0))] * 2
    shape = jax.ShapeDtypeStruct((rows // 2, columns), LOW)
    return pl.pallas_call(
        functools.partial(fold_kernel, len(pairs)),
        grid_spec=pltpu.PrefetchScalarGridSpec(
            num_scalar_prefetch=1,
            grid=(2, tiles),
            in_specs=specs + [pl.BlockSpec(memory_space=pl.ANY)] * len(others),
            out_specs=[
                pl.BlockSpec((tile, columns), lambda h, j, m: (j * (1 - h) + (tiles - 1) * h, 0)),
                pl.BlockSpec((tile, columns), lambda h, j, m: (j * h, 0)),
            ],
        ),
        out_shape=[shape, shape],
        compiler_params=params(),
        cost_estimate=cost(rows * columns, 6 * rows * columns),
    )(
        bit.astype(jnp.int32)[None],
        *[value for pair in pairs for value in pair],
        *others,
    )


def normed_kernel(q_ref, kv_ref, wq_ref, wkv_ref, rows_ref, *rest):
    out_ref, dgain_ref = rest[-2:]
    grad = dot_nt(q_ref[...], wq_ref[...]) + dot_nt(kv_ref[...], wkv_ref[...])
    out_ref[...] = grad.astype(LOW)
    dgain_ref[...] = jnp.sum(grad * rows_ref[...].astype(F32), axis=0, keepdims=True)


def normed_back(grad_q, grad_kv, w_q, w_kv, rows, others):
    block, width = rows.shape
    tile = 512
    column = lambda i: (0, i)
    return pl.pallas_call(
        normed_kernel,
        grid=(width // tile,),
        in_specs=[
            full(grad_q.shape),
            full(grad_kv.shape),
            pl.BlockSpec((tile, w_q.shape[1]), lambda i: (i, 0)),
            pl.BlockSpec((tile, w_kv.shape[1]), lambda i: (i, 0)),
            pl.BlockSpec((block, tile), column),
        ]
        + [pl.BlockSpec(memory_space=pl.ANY)] * len(others),
        out_specs=[pl.BlockSpec((block, tile), column), pl.BlockSpec((1, tile), column)],
        out_shape=[
            jax.ShapeDtypeStruct((block, width), LOW),
            jax.ShapeDtypeStruct((1, width), F32),
        ],
        compiler_params=params(),
        cost_estimate=cost(2 * block * width * (w_q.shape[1] + w_kv.shape[1]), 12e6),
    )(grad_q, grad_kv, w_q, w_kv, rows, *others)


def pack_kernel(experts, router_ref, attn_ref, gain_ref, mlp_ref, q_ref, k_ref, *rest):
    out_ref, rows_ref = rest[-2:]
    size = q_ref.shape[1]
    rows_ref[:experts] = router_ref[:experts]
    rows_ref[experts:] = jnp.zeros_like(rows_ref[experts:])
    rows_ref[experts : experts + 1] = attn_ref[...] / gain_ref[...]
    rows_ref[experts + 1 : experts + 2] = mlp_ref[...]
    rows_ref[experts + 2 : experts + 3, :size] = q_ref[...]
    rows_ref[experts + 2 : experts + 3, size : 2 * size] = k_ref[...]
    out_ref[...] = rows_ref[...].astype(LOW)


def pack_small(experts, router, attn, gain, mlp, q, k, others):
    width = attn.shape[1]
    n = lax.axis_size(ALL_AXES)
    shape = (-(-(experts + 3) // n) * n, width)
    operands = [router, attn, gain[None], mlp, q, k]
    return pl.pallas_call(
        functools.partial(pack_kernel, experts),
        grid=(1,),
        in_specs=[full(value.shape) for value in operands]
        + [pl.BlockSpec(memory_space=pl.ANY)] * len(others),
        out_specs=full(shape),
        out_shape=jax.ShapeDtypeStruct(shape, LOW),
        scratch_shapes=[pltpu.VMEM(shape, F32)],
        compiler_params=params(),
        cost_estimate=cost(shape[0] * width, 6 * shape[0] * width),
    )(*operands, *others)


def part_sum_kernel(parts_ref, *rest):
    total = parts_ref[0].astype(F32)
    for k in range(1, parts_ref.shape[0]):
        total += parts_ref[k].astype(F32)
    rest[-1][...] = total.astype(LOW)


def part_sum(parts, others):
    count, rows, columns = parts.shape
    tiles = 2
    return pl.pallas_call(
        part_sum_kernel,
        grid=(tiles,),
        in_specs=[pl.BlockSpec((count, rows // tiles, columns), lambda i: (0, i, 0))]
        + [pl.BlockSpec(memory_space=pl.ANY)] * len(others),
        out_specs=pl.BlockSpec((rows // tiles, columns), lambda i: (i, 0)),
        out_shape=jax.ShapeDtypeStruct((rows, columns), LOW),
        compiler_params=params(),
        cost_estimate=cost(count * rows * columns, 4 * count * rows * columns),
    )(parts, *others)


def widen_kernel(n_chunks, n_outs, at_ref, *refs):
    del at_ref
    outs = refs[-n_outs:]
    widths = [ref.shape[1] for ref in outs]
    for k in range(n_chunks):

        @pl.when(pl.program_id(0) == k)
        def _():
            first = 0
            for wide, out_ref in zip(widths, outs):
                out_ref[...] = refs[k][:, first : first + wide].astype(F32)
                first += wide


def widen(places, chunks, widths, total, others):
    rows, columns = chunks[0].shape
    count = len(chunks)
    return pl.pallas_call(
        functools.partial(widen_kernel, count, len(widths)),
        grid_spec=pltpu.PrefetchScalarGridSpec(
            num_scalar_prefetch=1,
            grid=(count,),
            in_specs=[full(chunk.shape) for chunk in chunks]
            + [pl.BlockSpec(memory_space=pl.ANY)] * len(others),
            out_specs=[pl.BlockSpec((rows, wide), lambda i, at: (at[i], 0)) for wide in widths],
        ),
        out_shape=[jax.ShapeDtypeStruct((total, wide), F32) for wide in widths],
        compiler_params=params(),
        cost_estimate=cost(rows * columns, 6 * count * rows * columns),
    )(jnp.stack(places).astype(jnp.int32), *chunks, *others)


def swap_dp(rows):
    return lax.ppermute(rows, "dp", [(0, 1), (1, 0)])


def swap_context(rows, s):
    n = lax.axis_size("context")
    return lax.ppermute(rows, "context", [(i, i ^ s) for i in range(n)])


def share_context(parts):
    return lax.all_to_all(parts, "context", split_axis=0, concat_axis=0, tiled=True)


def plane_turns():
    d, c = lax.axis_index("dp"), lax.axis_index("context")
    low, high = lax.rem(c, 2), lax.div(c, 2)

    def swap(first, second):
        perm = [(i, i ^ first) for i in range(4)] + [(4 + i, 4 + (i ^ second)) for i in range(4)]
        return lambda rows: lax.ppermute(rows, GROUP_AXES, perm)

    return [
        (jnp.where(d == 0, low, high), swap(1, 2)),
        (jnp.where(d == 0, high, low), swap(2, 1)),
    ]


def plane_first(pairs, others):
    (bit_1, _), _ = plane_turns()
    return fold(pairs, bit_1, others)


def plane_second(send, keep, others):
    (_, swap_1), (bit_2, _) = plane_turns()
    return fold([(keep, swap_1(send))], bit_2, others)


def plane_last(send, keep, others):
    _, (_, swap_2) = plane_turns()
    return pair_sum(keep, swap_2(send), others)


def plane_spread(own):
    (_, swap_1), (_, swap_2) = plane_turns()
    second = swap_2(own)
    return [own, second, swap_1(own), swap_1(second)]


def quarter_places(rank):
    d = lax.axis_index("dp")
    c = lax.axis_index("context")
    low, high = lax.rem(c, 2), lax.div(c, 2)
    places = []
    for core in (d, 1 - d):
        bit_1 = jnp.where(core == 0, low, high)
        bit_2 = jnp.where(core == 0, high, low)
        for flip_1, flip_2 in ((0, 0), (0, 1), (1, 0), (1, 1)):
            places.append(4 * core + rank(core, bit_1 ^ flip_1, bit_2 ^ flip_2))
    return places


def widen_all(quarters, places, widths, others):
    count = len(quarters)
    total = 2 * count * quarters[0].shape[0]
    chunks = quarters + [swap_dp(part) for part in quarters]
    return widen(places, chunks, widths, total, others)


def arrival_order(n):
    return [sorted(range(n), key=lambda j: (abs(j - i), j)) for i in range(n)]


def choose(index, options):
    distinct = []
    for option in options:
        if option is not None and not any(option is other for other in distinct):
            distinct.append(option)
    result = distinct[0]
    for option in distinct[1:]:
        mask = functools.reduce(
            jnp.logical_or, [index == i for i, other in enumerate(options) if other is option]
        )
        result = jnp.where(mask, option, result)
    return result


def line_gather(chunk):
    return line_steps({0: chunk}, 1, lax.axis_size("expert"))


def line_steps(found, first, stop):
    n = lax.axis_size("expert")
    found = dict(found)
    for s in range(first, stop):
        found[-s] = lax.ppermute(
            found[1 - s], "expert", [(i, i + 1) for i in range(s - 1, n - 1)]
        )
        found[s] = lax.ppermute(found[s - 1], "expert", [(i + 1, i) for i in range(n - s)])
    return found


def context_gather(rows):
    n = lax.axis_size("context")
    c = lax.axis_index("context")
    found = {0: rows}
    for s in range(1, n):
        found[s] = lax.ppermute(rows, "context", [(i, i ^ s) for i in range(n)])
    return jnp.concatenate([choose(c, [found[i ^ j] for i in range(n)]) for j in range(n)], axis=0)


def zero_of(*others):
    return functools.reduce(
        jnp.add,
        [
            lax.slice(other, (0,) * other.ndim, (1,) * other.ndim).reshape(()).astype(F32) * 0.0
            for other in others
        ],
    )


def after(value, *others):
    return (value.astype(F32) + zero_of(*others)).astype(value.dtype)


def on_device(
    layer_input,
    grad_output,
    attn_gain,
    query_weight,
    key_weight,
    value_weight,
    q_gain,
    k_gain,
    output_weight,
    mlp_gain,
    router,
    w_gate,
    w_up,
    w_down,
    routes,
    half_order,
):
    n_context = lax.axis_size("context")
    n_expert = lax.axis_size("expert")
    n_groups = lax.axis_size(GROUP_AXES)
    tok_dev, width = layer_input.shape[1:]
    size = q_gain.shape[0]
    kv_total = key_weight.shape[1] * n_expert
    group_dev = n_expert // (kv_total // size)
    kv_index = lax.axis_index("expert") // group_dev
    block = tok_dev * n_expert
    seq = block * n_context
    half = block // 2
    experts = router.shape[1]
    exp_dev = w_gate.shape[0]
    top = routes.shape[2]
    capacity = max(2, (tok_dev * top * 9 + 8 * experts - 1) // (8 * experts))
    scale = size ** (-0.5)

    seq_rows = jnp.arange(seq, dtype=jnp.int32)
    context = lax.axis_index("context")
    own_halves = lax.dynamic_slice_in_dim(half_order, 2 * context, 2)
    own_pos = (own_halves[:, None] * half + jnp.arange(half, dtype=jnp.int32)[None]).reshape(-1)
    per_half = half // TILE
    tile_pos = (half_order[:, None] * per_half + jnp.arange(per_half, dtype=jnp.int32)).reshape(-1)
    kidx = jnp.sum(
        (tile_pos[None, :] == jnp.arange(seq // TILE, dtype=jnp.int32)[:, None])
        * jnp.arange(seq // TILE, dtype=jnp.int32)[None, :],
        axis=1,
    ).astype(jnp.int32)
    qpos = lax.dynamic_slice_in_dim(tile_pos, context * (block // TILE), block // TILE)
    entry = jnp.arange(size)
    freq = jnp.power(THETA, -(2 * (entry % (size // 2))).astype(F32) / size)
    angles = own_pos.astype(F32)[:, None] * freq[None, :]
    cos2 = jnp.cos(angles)
    sin2 = jnp.sin(angles) * jnp.where(entry < size // 2, -1.0, 1.0)[None, :]

    place = lax.axis_index("expert")
    place_1 = place.astype(jnp.int32)[None]
    lanes = -(-2 * experts // 128) * 128
    mask = jnp.any(
        routes[0][:, :, None] == jnp.arange(lanes, dtype=jnp.int32)[None, None, :], axis=1
    )
    mask_wide = mask.astype(F32)
    router_rows = router.T

    x_low = layer_input[0]
    x_normal, _ = norm_parts(x_low.astype(F32))
    normed_found = line_gather((x_normal * attn_gain).astype(LOW))
    if group_dev == 1:
        kv_weights = jnp.concatenate([key_weight, value_weight], axis=1)
    else:
        key_whole = lax.all_gather(key_weight, "expert", axis=1, tiled=True)
        value_whole = lax.all_gather(value_weight, "expert", axis=1, tiled=True)
        kv_weights = jnp.concatenate(
            [
                lax.dynamic_slice_in_dim(key_whole, kv_index * size, size, 1),
                lax.dynamic_slice_in_dim(value_whole, kv_index * size, size, 1),
            ],
            axis=1,
        )
    grad_low = grad_output[0]
    normed_rows, own_kv, key_proj, grad_wide = project_keys(
        place_1,
        normed_found,
        kv_weights,
        k_gain,
        cos2,
        sin2,
        scale * LOG2E,
        grad_low,
        mask_wide,
    )
    grad_col = lax.all_gather(grad_wide, "expert", axis=0, tiled=True)
    kv_whole = context_gather(own_kv)
    queries, query_proj = project_queries(normed_rows, query_weight, q_gain, cos2, sin2)

    n_half = n_expert // 2
    order_here = jnp.asarray(arrival_order(n_expert), jnp.int32)[place]
    turn_here = jnp.sum(
        (order_here[:, None] == jnp.arange(n_expert, dtype=jnp.int32)[None, :])
        * jnp.arange(n_expert, dtype=jnp.int32)[:, None],
        axis=0,
    ).astype(jnp.int32)
    meta = jnp.concatenate([place_1, turn_here, order_here])
    grad_sent, slots = make_slots(meta, grad_col, width, n_groups, capacity)
    spreads, back_tables = make_tables(meta, slots, n_half, capacity)

    def swap_plane(rows):
        parts = rows.reshape(n_groups, -1, rows.shape[1])
        parts = lax.all_to_all(parts, GROUP_AXES, split_axis=0, concat_axis=0, tiled=True)
        return parts.reshape(rows.shape)

    attended, inverse = attend(qpos, kidx, queries, kv_whole, [])
    keys_t = kv_whole[:, :size].T
    attn_part = out_dot(attended, output_weight, [grad_col])
    attn_rows = lax.psum_scatter(attn_part, "expert", scatter_dimension=0, tiled=True)

    grad_x = swap_plane(grad_sent)
    act_pull = dot_nt(grad_x, w_down[0]).reshape(n_groups, 2, n_half * capacity, -1)

    hidden, mixed, probs = route_rows(
        x_low, attn_rows, mlp_gain, router_rows, mask_wide, experts, [keys_t]
    )

    who = (lax.axis_index(ALL_AXES) * exp_dev).astype(jnp.int32)[None]
    mixed_found = line_gather(mixed)
    near = spread_rows(place_1, spreads[0], mixed_found, range(n_half), [grad_x])
    x_near = swap_plane(near)
    worked_near = run_expert(who, x_near, w_gate[0], w_up[0], act_pull, 0, experts)
    far = spread_rows(place_1, spreads[1], mixed_found, range(n_half, n_expert), [x_near])
    x_far = swap_plane(far)
    worked_far = run_expert(who, x_far, w_gate[0], w_up[0], act_pull, 1, experts)
    xs = [x_near, x_far]
    acts, gate_lows, up_lows, copies = (list(pair) for pair in zip(worked_near, worked_far))
    back_far = swap_plane(copies[1])
    back_near = swap_plane(copies[0])
    join = lambda parts: jnp.concatenate(parts, axis=0)
    x_all = join([x[:, :width] for x in xs])
    grad_w_gate = dot_tn(x_all, join(gate_lows))
    grad_w_up = dot_tn(x_all, join(up_lows))
    grad_by_round = jnp.swapaxes(
        grad_x.reshape(n_groups, 2, n_half * capacity, width), 0, 1
    ).reshape(-1, width)
    grad_w_down = dot_tn(join(acts), grad_by_round)
    copies_col = combine_rows(
        meta, back_tables, [back_near, back_far], n_half, [grad_w_gate, grad_w_up]
    )
    copies_sum = lax.psum_scatter(copies_col, "expert", scatter_dimension=0, tiled=True)

    returned = [dot_nn(act, w_down[0]).astype(LOW) for act in acts]
    returned_near = swap_plane(returned[0])

    grad_hidden, grad_hidden_low, grad_mlp_gain, grad_router = route_back(
        copies_sum,
        grad_low,
        hidden,
        mlp_gain,
        router_rows,
        mask_wide,
        probs,
        experts,
        [returned_near, grad_w_down],
    )

    returned_far = swap_plane(returned[1])
    grad_attn = lax.all_gather(grad_hidden_low, "expert", axis=0, tiled=True)
    grad_o, centre = grad_attended(
        grad_attn, output_weight, attended, inverse, [returned_far]
    )
    combined = combine_rows(meta, back_tables, [returned_near, returned_far], n_half, [])
    output_rows = lax.psum_scatter(combined, "expert", scatter_dimension=0, tiled=True)
    w_out_send, w_out_keep = token_halves(attended, grad_attn, [combined])
    w_out_half = pair_sum(w_out_keep, swap_dp(w_out_send), [grad_o])
    w_out_parts = share_context(w_out_half.reshape(n_context, -1, width))
    grad_kv, grad_q, grad_q_gain = attend_back(
        qpos,
        kidx,
        queries,
        grad_o,
        centre,
        kv_whole,
        keys_t,
        query_proj,
        q_gain,
        cos2,
        sin2,
        [w_out_half],
    )
    kv_parts = share_context(grad_kv.astype(LOW).reshape(n_context, block, 2 * size))
    w_out_own = part_sum(w_out_parts, [grad_kv])
    w_query_send, w_query_keep = token_halves(normed_rows, grad_q, [w_out_own])
    w_query_got = swap_dp(w_query_send)
    output_rows = hidden + output_rows.astype(F32) + zero_of(w_query_keep)

    kv_grads, grad_k_gain = kv_back(
        kv_parts, key_proj, k_gain, cos2, sin2, scale, [w_query_keep]
    )
    w_out_quarters = plane_spread(w_out_own)
    pairs = [(w_query_keep, w_query_got)]
    widths = [query_weight.shape[1]]
    if group_dev == 1:
        w_kv_send, w_kv_keep = token_halves(normed_rows, kv_grads, [])
        pairs.append((w_kv_keep, swap_dp(w_kv_send)))
        widths += [key_weight.shape[1], value_weight.shape[1]]
    grad_normed, gain_rows = normed_back(
        grad_q, kv_grads, query_weight, kv_weights, normed_rows, []
    )
    send, keep = plane_first(pairs, [grad_normed])
    (grad_w_out,) = widen_all(
        w_out_quarters,
        quarter_places(lambda core, b1, b2: jnp.where(core == 0, b1 + 2 * b2, 2 * b1 + b2)),
        [width],
        [],
    )
    small = pack_small(
        experts,
        grad_router,
        gain_rows,
        attn_gain,
        grad_mlp_gain,
        grad_q_gain,
        grad_k_gain,
        [],
    )
    swap_all = lambda rows: lax.all_to_all(rows, ALL_AXES, split_axis=0, concat_axis=0, tiled=True)
    small_parts = swap_all(small.reshape(lax.axis_size(ALL_AXES), -1, width))
    small_own = jnp.sum(small_parts.astype(F32), axis=0).astype(LOW)
    second_send, second_keep = plane_second(
        send, keep, [small_own, output_rows, *w_out_quarters[1:3]]
    )
    grad_normed = lax.psum_scatter(grad_normed, "expert", scatter_dimension=0, tiled=True)
    grad_input = input_back(grad_normed, x_low, attn_gain, grad_hidden)
    small_sum = swap_all(jnp.broadcast_to(small_own[None], small_parts.shape))
    quarter = plane_last(
        second_send, second_keep, [grad_input, grad_w_out, small_sum]
    )
    grad_router, grad_attn_gain, grad_mlp_gain, grad_q_gain, grad_k_gain = unpack_small(
        small_sum.reshape(small.shape), experts, size, []
    )
    quarters = plane_spread(quarter)
    places = quarter_places(lambda core, b1, b2: 2 * b1 + b2)
    grad_w_query, *more = widen_all(quarters, places, widths, [grad_router])
    if group_dev == 1:
        grad_w_key, grad_w_value = more
    else:
        w_kv = token_dot(normed_rows, kv_grads, [])
        blank = jnp.zeros((width, kv_total), LOW)
        pieces = []
        for part in (w_kv[:, :size], w_kv[:, size:]):
            padded = lax.dynamic_update_slice(blank, part, (0, kv_index * size))
            pieces.append(lax.psum_scatter(padded, "expert", scatter_dimension=1, tiled=True))
        grad_w_key, grad_w_value = (lax.psum(piece, GROUP_AXES).astype(F32) for piece in pieces)
    return (
        output_rows.astype(LOW)[None],
        grad_input[None],
        grad_attn_gain[0],
        grad_w_query,
        grad_w_key,
        grad_w_value,
        grad_q_gain[0],
        grad_k_gain[0],
        grad_w_out,
        grad_mlp_gain[0],
        grad_router.T,
        grad_w_gate[None],
        grad_w_up[None],
        grad_w_down[None],
    )


def solution(mesh):
    rows = P("dp", ("context", "expert"), None)
    expert = P(ALL_AXES, None, None)
    columns = P(None, "expert")
    in_specs = (
        rows,
        rows,
        P(),
        columns,
        columns,
        columns,
        P(),
        P(),
        P("expert", None),
        P(),
        P(),
        expert,
        expert,
        expert,
        rows,
        P(),
    )
    out_specs = (
        rows,
        rows,
        P(),
        columns,
        columns,
        columns,
        P(),
        P(),
        P("expert", None),
        P(),
        P(),
        expert,
        expert,
        expert,
    )
    return jax.shard_map(
        on_device, mesh=mesh, in_specs=in_specs, out_specs=out_specs, check_vma=False
    )
```

```python
import functools
import math

import jax
import jax.numpy as jnp
from jax import lax
from jax.experimental import pallas as pl
from jax.experimental.pallas import tpu as pltpu
from jax.sharding import PartitionSpec as P

EPS = 1e-06
THETA = 1000000.0
TILE = 256
PIECE = 128
VMEM_BYTES = 56 * 1024 * 1024
LOG2E = math.log2(math.e)
LOW = jnp.bfloat16
F32 = jnp.float32
ALL_AXES = ("dp", "context", "expert")
GROUP_AXES = ("dp", "context")


def dot_nn(a, b):
    return lax.dot_general(a, b, (((1,), (0,)), ((), ())), preferred_element_type=F32)


def dot_nt(a, b):
    return lax.dot_general(a, b, (((1,), (1,)), ((), ())), preferred_element_type=F32)


def dot_tn(a, b):
    return lax.dot_general(a, b, (((0,), (0,)), ((), ())), preferred_element_type=F32)


def params(**more):
    return pltpu.CompilerParams(vmem_limit_bytes=VMEM_BYTES, **more)


def cost(flops, nbytes, exps=0):
    return pl.CostEstimate(flops=int(flops), bytes_accessed=int(nbytes), transcendentals=int(exps))


def head_forward(u, gain, cos2, sin2):
    rr = lax.rsqrt(jnp.mean(u * u, axis=-1, keepdims=True) + EPS)
    y = u * rr * gain
    return y * cos2 + pltpu.roll(y, 64, 1) * sin2


def head_backward(gy, u, gain, cos2, sin2):
    g = gy * cos2 - pltpu.roll(gy, 64, 1) * sin2
    rr = lax.rsqrt(jnp.mean(u * u, axis=-1, keepdims=True) + EPS)
    n = u * rr
    gn = g * gain
    grad = rr * (gn - n * jnp.mean(gn * n, axis=-1, keepdims=True))
    return grad, jnp.sum(g * n, axis=0, keepdims=True)


def query_kernel(x_ref, w_ref, gain_ref, cos_ref, sin_ref, rot_ref, proj_ref):
    tiles, heads, rows, size = rot_ref.shape
    acc = dot_nn(x_ref[...], w_ref[...])
    for h in range(heads):
        u = acc[:, h * size : (h + 1) * size]
        rot = head_forward(u, gain_ref[...], cos_ref[...], sin_ref[...])
        proj_ref[:, h] = u.reshape(tiles, rows, size)
        rot_ref[:, h] = rot.astype(LOW).reshape(tiles, rows, size)


def project_queries(normed, weight, gain, cos2, sin2):
    block, width = normed.shape
    size = cos2.shape[1]
    heads = weight.shape[1] // size
    tiles = block // TILE
    whole = lambda i: (0, 0)
    per = lambda i: (0, i, 0, 0)
    shape = (tiles, heads, TILE, size)
    return pl.pallas_call(
        query_kernel,
        grid=(heads // 2,),
        in_specs=[
            pl.BlockSpec((block, width), whole),
            pl.BlockSpec((width, 2 * size), lambda i: (0, i)),
            pl.BlockSpec((1, size), whole),
            pl.BlockSpec((block, size), whole),
            pl.BlockSpec((block, size), whole),
        ],
        out_specs=[pl.BlockSpec((tiles, 2, TILE, size), per)] * 2,
        out_shape=[jax.ShapeDtypeStruct(shape, LOW), jax.ShapeDtypeStruct(shape, F32)],
        compiler_params=params(),
        cost_estimate=cost(2 * block * width * heads * size, 12e6),
    )(normed, weight, gain[None], cos2, sin2)


def put_in_order(place, refs, out_ref):
    n = (len(refs) + 1) // 2
    rows = refs[0].shape[0]
    for distance in range(1 - n, n):
        ref = refs[distance + n - 1]
        at = place + distance

        @pl.when(jnp.logical_and(at >= 0, at < n))
        def _():
            out_ref[pl.ds(pl.multiple_of(at * rows, rows), rows), :] = ref[...]


def chunk_list(found):
    n = (len(found) + 1) // 2
    return [found[distance] for distance in range(1 - n, n)]


def key_kernel(factor, n_chunks, place_ref, *refs):
    w_ref, gain_ref, cos_ref, sin_ref, g_ref, mask_ref = refs[n_chunks:-4]
    rows_ref, kv_ref, proj_ref, wide_ref = refs[-4:]
    size = proj_ref.shape[1]
    width = g_ref.shape[1]
    put_in_order(place_ref[0], refs[:n_chunks], rows_ref)
    wide_ref[:, :width] = g_ref[...]
    wide_ref[:, width:] = mask_ref[...].astype(LOW)
    acc = dot_nn(rows_ref[...], w_ref[...])
    u = acc[:, :size]
    rot = head_forward(u, gain_ref[...], cos_ref[...], sin_ref[...])
    proj_ref[...] = u
    kv_ref[:, :size] = (rot * factor).astype(LOW)
    kv_ref[:, size:] = acc[:, size:].astype(LOW)


def full(shape):
    return pl.BlockSpec(shape, lambda *_: (0,) * len(shape))


def project_keys(place, found, weight, gain, cos2, sin2, factor, g, mask):
    chunks = chunk_list(found)
    rows, width = chunks[0].shape
    block, size = cos2.shape
    operands = [*chunks, weight, gain[None], cos2, sin2, g, mask]
    shapes = [
        jax.ShapeDtypeStruct((block, width), LOW),
        jax.ShapeDtypeStruct((block, 2 * size), LOW),
        jax.ShapeDtypeStruct((block, size), F32),
        jax.ShapeDtypeStruct((rows, width + mask.shape[1]), LOW),
    ]
    return pl.pallas_call(
        functools.partial(key_kernel, factor, len(chunks)),
        grid_spec=pltpu.PrefetchScalarGridSpec(
            num_scalar_prefetch=1,
            grid=(1,),
            in_specs=[full(x.shape) for x in operands],
            out_specs=[full(x.shape) for x in shapes],
        ),
        out_shape=shapes,
        compiler_params=params(),
        cost_estimate=cost(4 * block * width * size, 8e6),
    )(place, *operands)


def in_order(last, step):
    lax.fori_loop(0, lax.div(last, 2), lambda p, c: (step([2 * p, 2 * p + 1], False), c)[1], 0)

    @pl.when(lax.rem(last, 2) == 1)
    def _():
        step([last - 1, last], True)

    @pl.when(lax.rem(last, 2) == 0)
    def _():
        step([last], True)


def attend_kernel(qpos_ref, kidx_ref, q_ref, kv_ref, *rest):
    out_ref, inv_ref, acc_ref = rest[-3:]
    heads, rows, size = q_ref.shape[1:]
    acc_ref[...] = jnp.zeros_like(acc_ref)

    def step(places, masked):
        starts = [pl.multiple_of(kidx_ref[place] * rows, rows) for place in places]
        count = len(places) * rows
        keys = jnp.concatenate([kv_ref[pl.ds(start, rows), :size] for start in starts], axis=0)
        values = jnp.concatenate([kv_ref[pl.ds(start, rows), size:] for start in starts], axis=0)
        values = jnp.concatenate([values, jnp.ones((count, size), LOW)], axis=1)
        for h in range(heads):
            for first in range(0, rows, PIECE):
                part = slice(first, first + PIECE)
                e = jnp.exp2(dot_nt(q_ref[0, h, part], keys))
                if masked:
                    qi = lax.broadcasted_iota(jnp.int32, e.shape, 0) + first
                    ki = lax.broadcasted_iota(jnp.int32, e.shape, 1) - (count - rows)
                    e = jnp.where(ki <= qi, e, 0.0)
                acc_ref[h, part] += dot_nn(e.astype(LOW), values)

    in_order(qpos_ref[pl.program_id(0)], step)
    for h in range(heads):
        inv = 1.0 / acc_ref[h, :, size:]
        inv_ref[0, h] = inv
        out_ref[:, h * size : (h + 1) * size] = (acc_ref[h, :, :size] * inv).astype(LOW)


def attend(qpos, kidx, queries, kv, others):
    tiles, heads, rows, size = queries.shape
    seq = kv.shape[0]
    return pl.pallas_call(
        attend_kernel,
        grid_spec=pltpu.PrefetchScalarGridSpec(
            num_scalar_prefetch=2,
            grid=(tiles,),
            in_specs=[
                pl.BlockSpec((1, heads, rows, size), lambda i, a, b: (i, 0, 0, 0)),
                pl.BlockSpec((seq, 2 * size), lambda i, a, b: (0, 0)),
            ]
            + [pl.BlockSpec(memory_space=pl.ANY)] * len(others),
            out_specs=[
                pl.BlockSpec((rows, heads * size), lambda i, a, b: (i, 0)),
                pl.BlockSpec((1, heads, rows, size), lambda i, a, b: (i, 0, 0, 0)),
            ],
            scratch_shapes=[pltpu.VMEM((heads, rows, 2 * size), F32)],
        ),
        out_shape=[
            jax.ShapeDtypeStruct((tiles * rows, heads * size), LOW),
            jax.ShapeDtypeStruct((tiles, heads, rows, size), F32),
        ],
        compiler_params=params(),
        cost_estimate=cost(
            6 * tiles * rows * heads * seq * size, 8e6, tiles * rows * heads * seq
        ),
    )(qpos, kidx, queries, kv, *others)


def grad_out_kernel(rows_ref, w_ref, o_ref, inv_ref, *rest):
    do_ref, centre_ref = rest[-2:]
    tiles, heads, rows, size = do_ref.shape
    acc = dot_nt(rows_ref[...], w_ref[...])
    for t in range(tiles):
        for h in range(heads):
            part = slice(t * rows, (t + 1) * rows), slice(h * size, (h + 1) * size)
            low = (acc[part] * inv_ref[t, h]).astype(LOW)
            do_ref[t, h] = low
            product = low.astype(F32) * o_ref[part].astype(F32)
            centre = jnp.sum(jnp.transpose(product), axis=0, keepdims=True)
            centre_ref[t, h] = jnp.broadcast_to(centre, (8, rows))


def grad_attended(grad_rows, weight, attended, inverse, others):
    tiles, heads, rows, size = inverse.shape
    block, width = grad_rows.shape
    return pl.pallas_call(
        grad_out_kernel,
        grid=(heads // 2,),
        in_specs=[
            pl.BlockSpec((block, width), lambda i: (0, 0)),
            pl.BlockSpec((2 * size, width), lambda i: (i, 0)),
            pl.BlockSpec((block, 2 * size), lambda i: (0, i)),
            pl.BlockSpec((tiles, 2, rows, size), lambda i: (0, i, 0, 0)),
        ]
        + [pl.BlockSpec(memory_space=pl.ANY)] * len(others),
        out_specs=[
            pl.BlockSpec((tiles, 2, rows, size), lambda i: (0, i, 0, 0)),
            pl.BlockSpec((tiles, 2, 8, rows), lambda i: (0, i, 0, 0)),
        ],
        out_shape=[
            jax.ShapeDtypeStruct((tiles, heads, rows, size), LOW),
            jax.ShapeDtypeStruct((tiles, heads, 8, rows), F32),
        ],
        compiler_params=params(),
        cost_estimate=cost(2 * block * width * heads * size, 12e6),
    )(grad_rows, weight, attended, inverse, *others)


def attend_back_kernel(
    qpos_ref,
    kidx_ref,
    q_ref,
    do_ref,
    centre_ref,
    kv_ref,
    kt_ref,
    proj_ref,
    gain_ref,
    cos_ref,
    sin_ref,
    *rest,
):
    dkv_ref, dq_ref, dgain_ref, acc_ref, e_ref, ds_ref = rest[-6:]
    heads, rows, size = q_ref.shape[1:]

    @pl.when(pl.program_id(0) == 0)
    def _():
        dkv_ref[...] = jnp.zeros_like(dkv_ref)
        dgain_ref[...] = jnp.zeros_like(dgain_ref)

    acc_ref[...] = jnp.zeros_like(acc_ref)

    def step(places, masked):
        starts = [pl.multiple_of(kidx_ref[place] * rows, rows) for place in places]
        count = len(places) * rows
        keys = jnp.concatenate([kv_ref[pl.ds(start, rows), :size] for start in starts], axis=0)
        values = jnp.concatenate([kv_ref[pl.ds(start, rows), size:] for start in starts], axis=0)
        keys_t = jnp.concatenate([kt_ref[:, pl.ds(start, rows)] for start in starts], axis=1)
        for h in range(heads):
            query, grad = q_ref[0, h], do_ref[0, h]
            centre = centre_ref[0, h, 0:1]
            columns = slice(h * rows, (h + 1) * rows)
            for first in range(0, count, PIECE):
                part = slice(first, first + PIECE)
                e = jnp.exp2(dot_nt(keys[part], query))
                if masked and first >= count - rows:
                    ki = lax.broadcasted_iota(jnp.int32, e.shape, 0) + (first - (count - rows))
                    qi = lax.broadcasted_iota(jnp.int32, e.shape, 1)
                    e = jnp.where(ki <= qi, e, 0.0)
                ds = e * (dot_nt(values[part], grad) - centre)
                e_ref[part, columns] = e.astype(LOW)
                ds_ref[part, columns] = ds.astype(LOW)
            acc_ref[h] += dot_nn(keys_t, ds_ref[:count, columns])
        dk = dot_nn(ds_ref[:count], q_ref[0].reshape(heads * rows, size))
        dv = dot_nn(e_ref[:count], do_ref[0].reshape(heads * rows, size))
        for k, start in enumerate(starts):
            dkv_ref[pl.ds(start, rows), :size] += dk[k * rows : (k + 1) * rows]
            dkv_ref[pl.ds(start, rows), size:] += dv[k * rows : (k + 1) * rows]

    in_order(qpos_ref[pl.program_id(0)], step)
    total = jnp.zeros((1, size), F32)
    for h in range(heads):
        grad, gain_part = head_backward(
            jnp.transpose(acc_ref[h]) * (1.0 / LOG2E),
            proj_ref[0, h],
            gain_ref[...],
            cos_ref[...],
            sin_ref[...],
        )
        dq_ref[:, h * size : (h + 1) * size] = grad.astype(LOW)
        total += gain_part
    dgain_ref[...] += total


def attend_back(qpos, kidx, queries, grads, centre, kv, keys_t, proj, gain, cos2, sin2, others):
    tiles, heads, rows, size = queries.shape
    seq = kv.shape[0]
    per = pl.BlockSpec((1, heads, rows, size), lambda i, a, b: (i, 0, 0, 0))
    flat = lambda i, a, b: (0, 0)
    rowwise = lambda i, a, b: (i, 0)
    return pl.pallas_call(
        attend_back_kernel,
        grid_spec=pltpu.PrefetchScalarGridSpec(
            num_scalar_prefetch=2,
            grid=(tiles,),
            in_specs=[
                per,
                per,
                pl.BlockSpec((1, heads, 8, rows), lambda i, a, b: (i, 0, 0, 0)),
                pl.BlockSpec((seq, 2 * size), flat),
                pl.BlockSpec((size, seq), flat),
                per,
                pl.BlockSpec((1, size), flat),
                pl.BlockSpec((rows, size), rowwise),
                pl.BlockSpec((rows, size), rowwise),
            ]
            + [pl.BlockSpec(memory_space=pl.ANY)] * len(others),
            out_specs=[
                pl.BlockSpec((seq, 2 * size), flat),
                pl.BlockSpec((rows, heads * size), rowwise),
                pl.BlockSpec((1, size), flat),
            ],
            scratch_shapes=[pltpu.VMEM((heads, size, rows), F32)]
            + [pltpu.VMEM((2 * rows, heads * rows), LOW)] * 2,
        ),
        out_shape=[
            jax.ShapeDtypeStruct((seq, 2 * size), F32),
            jax.ShapeDtypeStruct((tiles * rows, heads * size), LOW),
            jax.ShapeDtypeStruct((1, size), F32),
        ],
        compiler_params=params(),
        cost_estimate=cost(
            15 * tiles * rows * heads * seq * size, 12e6, tiles * rows * heads * seq
        ),
    )(qpos, kidx, queries, grads, centre, kv, keys_t, proj, gain[None], cos2, sin2, *others)


def out_kernel(a_ref, b_ref, *rest):
    rest[-1][...] = dot_nn(a_ref[...], b_ref[...]).astype(LOW)


def out_dot(a, b, others):
    block, inner = a.shape
    columns = b.shape[1]
    tile = min(columns, 512)
    return pl.pallas_call(
        out_kernel,
        grid=(columns // tile,),
        in_specs=[
            pl.BlockSpec((block, inner), lambda i: (0, 0)),
            pl.BlockSpec((inner, tile), lambda i: (0, i)),
        ]
        + [pl.BlockSpec(memory_space=pl.ANY)] * len(others),
        out_specs=pl.BlockSpec((block, tile), lambda i: (0, i)),
        out_shape=jax.ShapeDtypeStruct((block, columns), LOW),
        compiler_params=params(),
        cost_estimate=cost(2 * block * inner * columns, 8e6),
    )(a, b, *others)


def token_kernel(a_ref, b_ref, *rest):
    rest[-1][...] = dot_tn(a_ref[...], b_ref[...]).astype(LOW)


def token_dot(a, b, others):
    block, rows = a.shape
    columns = b.shape[1]
    tile = min(rows, 512)
    return pl.pallas_call(
        token_kernel,
        grid=(rows // tile,),
        in_specs=[
            pl.BlockSpec((block, tile), lambda i: (0, i)),
            pl.BlockSpec((block, columns), lambda i: (0, 0)),
        ]
        + [pl.BlockSpec(memory_space=pl.ANY)] * len(others),
        out_specs=pl.BlockSpec((tile, columns), lambda i: (i, 0)),
        out_shape=jax.ShapeDtypeStruct((rows, columns), LOW),
        compiler_params=params(),
        cost_estimate=cost(2 * block * rows * columns, 6e6),
    )(a, b, *others)


def halves_kernel(d_ref, a_ref, b_ref, *rest):
    send_ref, keep_ref = rest[-2:]
    product = dot_tn(a_ref[...], b_ref[...]).astype(LOW)

    @pl.when(pl.program_id(0) == 0)
    def _():
        send_ref[...] = product

    @pl.when(pl.program_id(0) == 1)
    def _():
        keep_ref[...] = product


def token_halves(a, b, others):
    block, rows = a.shape
    columns = b.shape[1]
    tiles = 2 if rows % 512 == 0 else 1
    tile = rows // (2 * tiles)
    d = lax.axis_index("dp").astype(jnp.int32)[None]
    half = jax.ShapeDtypeStruct((rows // 2, columns), LOW)
    return pl.pallas_call(
        halves_kernel,
        grid_spec=pltpu.PrefetchScalarGridSpec(
            num_scalar_prefetch=1,
            grid=(2, tiles),
            in_specs=[
                pl.BlockSpec(
                    (block, tile),
                    lambda h, j, d: (0, ((1 - d[0]) * (1 - h) + d[0] * h) * tiles + j),
                ),
                pl.BlockSpec((block, columns), lambda h, j, d: (0, 0)),
            ]
            + [pl.BlockSpec(memory_space=pl.ANY)] * len(others),
            out_specs=[
                pl.BlockSpec((tile, columns), lambda h, j, d: (j * (1 - h) + (tiles - 1) * h, 0)),
                pl.BlockSpec((tile, columns), lambda h, j, d: (j * h, 0)),
            ],
        ),
        out_shape=[half, half],
        compiler_params=params(),
        cost_estimate=cost(2 * block * rows * columns, 6e6),
    )(d, a, b, *others)


def split_low(value):
    high = value.astype(LOW)
    return high, (value - high.astype(F32)).astype(LOW)


def norm_parts(rows):
    rr = lax.rsqrt(jnp.mean(rows * rows, axis=-1, keepdims=True) + EPS)
    return rows * rr, rr


def norm_back(grad, normal, rr, gain):
    weighted = grad * gain
    return rr * (weighted - normal * jnp.mean(weighted * normal, axis=-1, keepdims=True))


def add_all(refs):
    return functools.reduce(jnp.add, [ref[...].astype(F32) for ref in refs])


def pad_rows(rows, count):
    if rows.shape[0] == count:
        return rows
    return jnp.concatenate(
        [rows, jnp.zeros((count - rows.shape[0], rows.shape[1]), rows.dtype)], axis=0
    )


def router_kernel(experts, *refs):
    x_ref, attn_ref, gain_ref, router_ref, mask_ref = refs[:5]
    hidden_ref, mixed_ref, probs_ref = refs[-3:]
    width = x_ref.shape[1]
    lanes = mask_ref.shape[1]
    hidden = add_all([x_ref, attn_ref])
    hidden_ref[...] = hidden
    mixed = (norm_parts(hidden)[0] * gain_ref[...]).astype(LOW)
    mixed_ref[:, :width] = mixed
    logits = dot_nt(mixed, pad_rows(router_ref[...], lanes))
    lane = lax.broadcasted_iota(jnp.int32, logits.shape, 1)
    logits = jnp.where(lane < experts, logits, -1e30)
    weights = jnp.exp(logits - jnp.max(logits, axis=1, keepdims=True))
    probs = weights / jnp.sum(weights, axis=1, keepdims=True)
    probs_ref[...] = probs
    chosen = probs * mask_ref[...]
    high, low = split_low(chosen / jnp.sum(chosen, axis=1, keepdims=True))
    both = high.astype(F32) + pltpu.roll(low.astype(F32), experts, 1)
    mixed_ref[:, width:] = both.astype(LOW)


def route_rows(x, attn, gain, router, mask, experts, others):
    tokens, width = x.shape
    lanes = mask.shape[1]
    operands = [x, attn, gain[None], router, mask]
    shapes = [
        jax.ShapeDtypeStruct((tokens, width), F32),
        jax.ShapeDtypeStruct((tokens, width + lanes), LOW),
        jax.ShapeDtypeStruct((tokens, lanes), F32),
    ]
    return pl.pallas_call(
        functools.partial(router_kernel, experts),
        grid=(1,),
        in_specs=[full(value.shape) for value in operands]
        + [pl.BlockSpec(memory_space=pl.ANY)] * len(others),
        out_specs=[full(shape.shape) for shape in shapes],
        out_shape=shapes,
        compiler_params=params(),
        cost_estimate=cost(2 * tokens * width * lanes, 5e6),
    )(*operands, *others)


def one_hot(slots, count, first):
    groups, tokens = slots.shape
    slot = lax.broadcasted_iota(jnp.int32, (groups, count, tokens), 1).astype(F32)
    same = slots[:, None, :] == slot + float(first)
    return jnp.where(same, 1.0, 0.0).reshape(groups * count, tokens)


def slot_kernel(capacity, meta_ref, col_ref, rows_ref, slots_ref):
    groups, block = slots_ref.shape
    rows, width = rows_ref.shape
    n = rows // groups // capacity
    tokens = block // n
    mask = col_ref[:, width:]
    lanes = mask.shape[1]
    padded = -(-groups // 16) * 16
    group = lax.broadcasted_iota(jnp.int32, (padded, lanes), 0)
    lane = lax.broadcasted_iota(jnp.int32, (padded, lanes), 1)
    wanted = jnp.logical_and(lane == group * n + meta_ref[0], group < groups)
    hits = dot_nt(jnp.where(wanted, 1.0, 0.0).astype(LOW), mask)
    before = lax.broadcasted_iota(jnp.int32, (tokens, tokens), 0)
    after_it = lax.broadcasted_iota(jnp.int32, (tokens, tokens), 1)
    earlier = jnp.where(before < after_it, 1.0, 0.0).astype(LOW)
    for z in range(n):
        hit = hits[:, z * tokens : (z + 1) * tokens]
        rank = dot_nn(hit.astype(LOW), earlier)
        turn = (meta_ref[1 + z] * capacity).astype(F32)
        slot = jnp.where(hit > 0.5, rank + turn, -1.0)
        slots_ref[:, z * tokens : (z + 1) * tokens] = slot[:groups]
    spread = one_hot(slots_ref[...], n * capacity, 0).astype(LOW)
    rows_ref[...] = dot_nn(spread, col_ref[:, :width]).astype(LOW)


def make_slots(meta, col, width, groups, capacity):
    block = col.shape[0]
    n = lax.axis_size("expert")
    shapes = [
        jax.ShapeDtypeStruct((groups * n * capacity, width), LOW),
        jax.ShapeDtypeStruct((groups, block), F32),
    ]
    return pl.pallas_call(
        functools.partial(slot_kernel, capacity),
        grid_spec=pltpu.PrefetchScalarGridSpec(
            num_scalar_prefetch=1,
            grid=(1,),
            in_specs=[full(col.shape)],
            out_specs=[full(shape.shape) for shape in shapes],
        ),
        out_shape=shapes,
        compiler_params=params(),
        cost_estimate=cost(2 * groups * n * capacity * block * width, 8e6),
    )(meta, col)


def table_kernel(capacity, n_half, meta_ref, slots_ref, near_ref, far_ref, near_back_ref, far_back_ref):
    n = 2 * n_half
    tokens = slots_ref.shape[1] // n
    cap_half = n_half * capacity
    for part, (to_ref, back_ref) in enumerate([(near_ref, near_back_ref), (far_ref, far_back_ref)]):
        pieces = []
        for k in range(n_half):
            start = pl.multiple_of(meta_ref[1 + n + part * n_half + k] * tokens, tokens)
            pieces.append(slots_ref[:, pl.ds(start, tokens)])
        spread = one_hot(jnp.concatenate(pieces, axis=1), cap_half, part * cap_half)
        to_ref[...] = spread.astype(LOW)
        back_ref[...] = jnp.transpose(spread).astype(LOW)


def make_tables(meta, slots, n_half, capacity):
    groups, block = slots.shape
    rows = groups * n_half * capacity
    shapes = [jax.ShapeDtypeStruct((rows, block // 2), LOW)] * 2
    shapes += [jax.ShapeDtypeStruct((block // 2, rows), LOW)] * 2
    outs = pl.pallas_call(
        functools.partial(table_kernel, capacity, n_half),
        grid_spec=pltpu.PrefetchScalarGridSpec(
            num_scalar_prefetch=1,
            grid=(1,),
            in_specs=[full(slots.shape)],
            out_specs=[full(shape.shape) for shape in shapes],
        ),
        out_shape=shapes,
        compiler_params=params(),
        cost_estimate=cost(8 * rows * block, 3e6),
    )(meta, slots)
    return outs[:2], outs[2:]


def spread_kernel(choices, place_ref, spread_ref, *refs):
    out_ref, rows_ref = refs[-2:]
    for k, by_place in enumerate(choices):
        for which in sorted(set(by_place)):
            hit = functools.reduce(
                jnp.logical_or,
                [place_ref[0] == i for i, other in enumerate(by_place) if other == which],
            )

            @pl.when(hit)
            def _():
                tokens = refs[which].shape[0]
                rows_ref[k * tokens : (k + 1) * tokens] = refs[which][...]

    out_ref[...] = dot_nn(spread_ref[...], rows_ref[...]).astype(LOW)


def spread_rows(place, spread, found, turns, others):
    n = lax.axis_size("expert")
    order = arrival_order(n)
    distances = sorted({order[i][turn] - i for i in range(n) for turn in turns})
    choices = [[distances.index(order[i][turn] - i) for i in range(n)] for turn in turns]
    chunks = [found[distance] for distance in distances]
    tokens, wide = chunks[0].shape
    rows = spread.shape[0]
    return pl.pallas_call(
        functools.partial(spread_kernel, choices),
        grid_spec=pltpu.PrefetchScalarGridSpec(
            num_scalar_prefetch=1,
            grid=(1,),
            in_specs=[full(spread.shape)]
            + [full(chunk.shape) for chunk in chunks]
            + [pl.BlockSpec(memory_space=pl.ANY)] * len(others),
            out_specs=full((rows, wide)),
            scratch_shapes=[pltpu.VMEM((len(turns) * tokens, wide), LOW)],
        ),
        out_shape=jax.ShapeDtypeStruct((rows, wide), LOW),
        compiler_params=params(),
        cost_estimate=cost(2 * rows * len(turns) * tokens * wide, 5e6),
    )(place, spread, *chunks, *others)


def router_back_kernel(experts, *refs):
    sum_ref, g_ref, hidden_ref, gain_ref, router_ref, mask_ref, probs_ref = refs[:7]
    grad_ref, low_ref, dgain_ref, drouter_ref = refs[-4:]
    width = g_ref.shape[1]
    lanes = mask_ref.shape[1]
    total = sum_ref[...].astype(F32)
    table = total[:, width:]
    mask, probs = mask_ref[...], probs_ref[...]
    grad_gates = (table + pltpu.roll(table, lanes - experts, 1)) * mask
    chosen = probs * mask
    chosen_sum = jnp.sum(chosen, axis=1, keepdims=True)
    mean = jnp.sum(grad_gates * (chosen / chosen_sum), axis=1, keepdims=True)
    centred = mask * (grad_gates - mean) / chosen_sum
    grad_logits = probs * (centred - jnp.sum(centred * chosen, axis=1, keepdims=True))
    high, low = split_low(grad_logits)
    router = pad_rows(router_ref[...], lanes)
    grad = total[:, :width] + dot_nn(high, router) + dot_nn(low, router)
    normal, rr = norm_parts(hidden_ref[...])
    mixed = (normal * gain_ref[...]).astype(LOW)
    drouter_ref[...] = dot_tn(high, mixed) + dot_tn(low, mixed)
    dgain_ref[...] = jnp.sum(grad * normal, axis=0, keepdims=True)
    grad_hidden = g_ref[...].astype(F32) + norm_back(grad, normal, rr, gain_ref[...])
    grad_ref[...] = grad_hidden
    low_ref[...] = grad_hidden.astype(LOW)


def route_back(summed, g, hidden, gain, router, mask, probs, experts, others):
    tokens, width = g.shape
    lanes = mask.shape[1]
    operands = [summed, g, hidden, gain[None], router, mask, probs]
    shapes = [
        jax.ShapeDtypeStruct((tokens, width), F32),
        jax.ShapeDtypeStruct((tokens, width), LOW),
        jax.ShapeDtypeStruct((1, width), F32),
        jax.ShapeDtypeStruct((lanes, width), F32),
    ]
    return pl.pallas_call(
        functools.partial(router_back_kernel, experts),
        grid=(1,),
        in_specs=[full(value.shape) for value in operands]
        + [pl.BlockSpec(memory_space=pl.ANY)] * len(others),
        out_specs=[full(shape.shape) for shape in shapes],
        out_shape=shapes,
        compiler_params=params(),
        cost_estimate=cost(8 * tokens * width * lanes, 8e6),
    )(*operands, *others)


def combine_kernel(meta_ref, table_ref, rows_ref, *rest):
    del meta_ref
    rest[-1][...] = dot_nn(table_ref[...], rows_ref[...]).astype(LOW)


def combine_part(meta, table, rows, first, n, into, others):
    block, slots = table.shape
    wide = rows.shape[1]
    tokens = block // (n // 2)
    return pl.pallas_call(
        combine_kernel,
        grid_spec=pltpu.PrefetchScalarGridSpec(
            num_scalar_prefetch=1,
            grid=(n // 2,),
            in_specs=[
                pl.BlockSpec((tokens, slots), lambda i, m: (i, 0)),
                full(rows.shape),
            ]
            + [pl.BlockSpec(memory_space=pl.ANY)] * (len(into) + len(others)),
            out_specs=pl.BlockSpec((tokens, wide), lambda i, m: (m[1 + n + first + i], 0)),
        ),
        out_shape=jax.ShapeDtypeStruct((n * tokens, wide), LOW),
        input_output_aliases={3: 0} if into else {},
        compiler_params=params(),
        cost_estimate=cost(2 * slots * block * wide, 6e6),
    )(meta, table, rows, *into, *others)


def combine_rows(meta, tables, rows, n_half, others):
    near = combine_part(meta, tables[0], rows[0], 0, 2 * n_half, [], [])
    return combine_part(meta, tables[1], rows[1], n_half, 2 * n_half, [near], others)


def expert_kernel(experts, who_ref, x_ref, gate_ref, up_ref, pull_ref, *rest):
    act_ref, dgate_ref, dup_ref, copy_ref = rest[-4:]
    width = gate_ref.shape[0]
    x = x_ref[:, :width]
    table = x_ref[:, width:].astype(F32)
    lane = lax.broadcasted_iota(jnp.int32, table.shape, 1)
    mine = who_ref[0]
    gate = jnp.sum(
        jnp.where(jnp.logical_or(lane == mine, lane == mine + experts), table, 0.0),
        axis=1,
        keepdims=True,
    )
    pre_gate = dot_nn(x, gate_ref[...])
    pre_up = dot_nn(x, up_ref[...])
    pull = pull_ref[...].reshape(pre_up.shape)
    sig = 1.0 / (1.0 + jnp.exp(-pre_gate))
    silu = pre_gate * sig
    act = silu * pre_up
    act_ref[...] = (act * gate).astype(LOW)
    high, low = split_low(jnp.sum(act * pull, axis=1, keepdims=True))
    pull = pull * gate
    dup = (pull * silu).astype(LOW)
    dgate = (pull * pre_up * (sig * (1.0 + pre_gate * (1.0 - sig)))).astype(LOW)
    dgate_ref[...] = dgate
    dup_ref[...] = dup
    copy_ref[:, :width] = (dot_nt(dgate, gate_ref[...]) + dot_nt(dup, up_ref[...])).astype(LOW)
    back = jnp.where(lane == mine, high.astype(F32), 0.0)
    back = jnp.where(lane == mine + experts, low.astype(F32), back)
    copy_ref[:, width:] = back.astype(LOW)


def run_expert(who, x, w_gate, w_up, pull, part, experts):
    rows, wide = x.shape
    width, hidden = w_gate.shape
    groups, _, slots, _ = pull.shape
    each = groups // 2
    tile = each * slots
    by_rows = lambda columns: pl.BlockSpec((tile, columns), lambda i, p: (i, 0))
    return pl.pallas_call(
        functools.partial(expert_kernel, experts),
        grid_spec=pltpu.PrefetchScalarGridSpec(
            num_scalar_prefetch=1,
            grid=(2,),
            in_specs=[
                by_rows(wide),
                full(w_gate.shape),
                full(w_up.shape),
                pl.BlockSpec((each, 1, slots, hidden), lambda i, p: (i, part, 0, 0)),
            ],
            out_specs=[by_rows(hidden), by_rows(hidden), by_rows(hidden), by_rows(wide)],
        ),
        out_shape=[jax.ShapeDtypeStruct((rows, hidden), LOW)] * 3
        + [jax.ShapeDtypeStruct((rows, wide), LOW)],
        compiler_params=params(),
        cost_estimate=cost(8 * rows * width * hidden, 20e6, rows * hidden),
    )(who, x, w_gate, w_up, pull)


def input_kernel(grad_ref, x_ref, gain_ref, more_ref, out_ref):
    normal, rr = norm_parts(x_ref[...].astype(F32))
    grad = grad_ref[...].astype(F32)
    out_ref[...] = more_ref[...] + norm_back(grad, normal, rr, gain_ref[...])


def input_back(grad, x, gain, more):
    tokens, width = x.shape
    operands = [grad, x, gain[None], more]
    return pl.pallas_call(
        input_kernel,
        grid=(1,),
        in_specs=[full(value.shape) for value in operands],
        out_specs=full(more.shape),
        out_shape=jax.ShapeDtypeStruct((tokens, width), F32),
        compiler_params=params(),
        cost_estimate=cost(20 * tokens * width, 5e6),
    )(*operands)


def kv_back_kernel(factor, parts_ref, proj_ref, gain_ref, cos_ref, sin_ref, *rest):
    grad_ref, dgain_ref = rest[-2:]
    size = proj_ref.shape[1]
    total = parts_ref[0].astype(F32)
    for k in range(1, parts_ref.shape[0]):
        total += parts_ref[k].astype(F32)
    grad, dgain = head_backward(
        total[:, :size] * factor, proj_ref[...], gain_ref[...], cos_ref[...], sin_ref[...]
    )
    grad_ref[:, :size] = grad.astype(LOW)
    grad_ref[:, size:] = total[:, size:].astype(LOW)
    dgain_ref[...] = dgain


def kv_back(parts, proj, gain, cos2, sin2, factor, others):
    block, size = proj.shape
    operands = [parts, proj, gain[None], cos2, sin2]
    shapes = [
        jax.ShapeDtypeStruct((block, 2 * size), LOW),
        jax.ShapeDtypeStruct((1, size), F32),
    ]
    return pl.pallas_call(
        functools.partial(kv_back_kernel, factor),
        grid=(1,),
        in_specs=[full(value.shape) for value in operands]
        + [pl.BlockSpec(memory_space=pl.ANY)] * len(others),
        out_specs=[full(shape.shape) for shape in shapes],
        out_shape=shapes,
        compiler_params=params(),
        cost_estimate=cost(40 * block * size, 5e6),
    )(*operands, *others)


def unpack_kernel(experts, small_ref, *rest):
    router_ref, attn_ref, mlp_ref, q_ref, k_ref = rest[-5:]
    rows = small_ref[...].astype(F32)
    size = q_ref.shape[1]
    router_ref[...] = rows[:experts]
    attn_ref[...] = rows[experts : experts + 1]
    mlp_ref[...] = rows[experts + 1 : experts + 2]
    q_ref[...] = rows[experts + 2 : experts + 3, :size]
    k_ref[...] = rows[experts + 2 : experts + 3, size : 2 * size]


def unpack_small(small, experts, size, others):
    width = small.shape[1]
    shapes = [(experts, width), (1, width), (1, width), (1, size), (1, size)]
    return pl.pallas_call(
        functools.partial(unpack_kernel, experts),
        grid=(1,),
        in_specs=[full(small.shape)] + [pl.BlockSpec(memory_space=pl.ANY)] * len(others),
        out_specs=[full(shape) for shape in shapes],
        out_shape=[jax.ShapeDtypeStruct(shape, F32) for shape in shapes],
        compiler_params=params(),
        cost_estimate=cost(experts * width, 6 * experts * width),
    )(small, *others)


def pair_kernel(a_ref, b_ref, *rest):
    rest[-1][...] = (a_ref[...].astype(F32) + b_ref[...].astype(F32)).astype(LOW)


def pair_sum(a, b, others):
    rows, columns = a.shape
    tiles = 2 if rows % 32 == 0 else 1
    spec = pl.BlockSpec((rows // tiles, columns), lambda i: (i, 0))
    return pl.pallas_call(
        pair_kernel,
        grid=(tiles,),
        in_specs=[spec, spec] + [pl.BlockSpec(memory_space=pl.ANY)] * len(others),
        out_specs=spec,
        out_shape=jax.ShapeDtypeStruct((rows, columns), LOW),
        compiler_params=params(),
        cost_estimate=cost(rows * columns, 6 * rows * columns),
    )(a, b, *others)


def fold_kernel(n_pairs, s_ref, *refs):
    del s_ref
    send_ref, keep_ref = refs[-2:]
    totals = [
        (refs[2 * k][...].astype(F32) + refs[2 * k + 1][...].astype(F32)).astype(LOW)
        for k in range(n_pairs)
    ]
    for half, out_ref in enumerate((send_ref, keep_ref)):

        @pl.when(pl.program_id(0) == half)
        def _():
            first = 0
            for total in totals:
                last = first + total.shape[1]
                out_ref[:, first:last] = total
                first = last


def fold(pairs, bit, others):
    rows = pairs[0][1].shape[0]
    columns = sum(got.shape[1] for _, got in pairs)
    tiles = 2
    tile = rows // (2 * tiles)
    side = lambda h, m: (1 - m[0]) * (1 - h) + m[0] * h
    specs = []
    for _, got in pairs:
        wide = got.shape[1]
        specs += [pl.BlockSpec((tile, wide), lambda h, j, m: (side(h, m) * tiles + j, 0))] * 2
    shape = jax.ShapeDtypeStruct((rows // 2, columns), LOW)
    return pl.pallas_call(
        functools.partial(fold_kernel, len(pairs)),
        grid_spec=pltpu.PrefetchScalarGridSpec(
            num_scalar_prefetch=1,
            grid=(2, tiles),
            in_specs=specs + [pl.BlockSpec(memory_space=pl.ANY)] * len(others),
            out_specs=[
                pl.BlockSpec((tile, columns), lambda h, j, m: (j * (1 - h) + (tiles - 1) * h, 0)),
                pl.BlockSpec((tile, columns), lambda h, j, m: (j * h, 0)),
            ],
        ),
        out_shape=[shape, shape],
        compiler_params=params(),
        cost_estimate=cost(rows * columns, 6 * rows * columns),
    )(
        bit.astype(jnp.int32)[None],
        *[value for pair in pairs for value in pair],
        *others,
    )


def normed_kernel(q_ref, kv_ref, wq_ref, wkv_ref, rows_ref, *rest):
    out_ref, dgain_ref = rest[-2:]
    grad = dot_nt(q_ref[...], wq_ref[...]) + dot_nt(kv_ref[...], wkv_ref[...])
    out_ref[...] = grad.astype(LOW)
    dgain_ref[...] = jnp.sum(grad * rows_ref[...].astype(F32), axis=0, keepdims=True)


def normed_back(grad_q, grad_kv, w_q, w_kv, rows, others):
    block, width = rows.shape
    tile = 512
    column = lambda i: (0, i)
    return pl.pallas_call(
        normed_kernel,
        grid=(width // tile,),
        in_specs=[
            full(grad_q.shape),
            full(grad_kv.shape),
            pl.BlockSpec((tile, w_q.shape[1]), lambda i: (i, 0)),
            pl.BlockSpec((tile, w_kv.shape[1]), lambda i: (i, 0)),
            pl.BlockSpec((block, tile), column),
        ]
        + [pl.BlockSpec(memory_space=pl.ANY)] * len(others),
        out_specs=[pl.BlockSpec((block, tile), column), pl.BlockSpec((1, tile), column)],
        out_shape=[
            jax.ShapeDtypeStruct((block, width), LOW),
            jax.ShapeDtypeStruct((1, width), F32),
        ],
        compiler_params=params(),
        cost_estimate=cost(2 * block * width * (w_q.shape[1] + w_kv.shape[1]), 12e6),
    )(grad_q, grad_kv, w_q, w_kv, rows, *others)


def pack_kernel(experts, router_ref, attn_ref, gain_ref, mlp_ref, q_ref, k_ref, *rest):
    out_ref, rows_ref = rest[-2:]
    size = q_ref.shape[1]
    rows_ref[:experts] = router_ref[:experts]
    rows_ref[experts:] = jnp.zeros_like(rows_ref[experts:])
    rows_ref[experts : experts + 1] = attn_ref[...] / gain_ref[...]
    rows_ref[experts + 1 : experts + 2] = mlp_ref[...]
    rows_ref[experts + 2 : experts + 3, :size] = q_ref[...]
    rows_ref[experts + 2 : experts + 3, size : 2 * size] = k_ref[...]
    out_ref[...] = rows_ref[...].astype(LOW)


def pack_small(experts, router, attn, gain, mlp, q, k, others):
    width = attn.shape[1]
    n = lax.axis_size(ALL_AXES)
    shape = (-(-(experts + 3) // n) * n, width)
    operands = [router, attn, gain[None], mlp, q, k]
    return pl.pallas_call(
        functools.partial(pack_kernel, experts),
        grid=(1,),
        in_specs=[full(value.shape) for value in operands]
        + [pl.BlockSpec(memory_space=pl.ANY)] * len(others),
        out_specs=full(shape),
        out_shape=jax.ShapeDtypeStruct(shape, LOW),
        scratch_shapes=[pltpu.VMEM(shape, F32)],
        compiler_params=params(),
        cost_estimate=cost(shape[0] * width, 6 * shape[0] * width),
    )(*operands, *others)


def part_sum_kernel(parts_ref, *rest):
    total = parts_ref[0].astype(F32)
    for k in range(1, parts_ref.shape[0]):
        total += parts_ref[k].astype(F32)
    rest[-1][...] = total.astype(LOW)


def part_sum(parts, others):
    count, rows, columns = parts.shape
    tiles = 2
    return pl.pallas_call(
        part_sum_kernel,
        grid=(tiles,),
        in_specs=[pl.BlockSpec((count, rows // tiles, columns), lambda i: (0, i, 0))]
        + [pl.BlockSpec(memory_space=pl.ANY)] * len(others),
        out_specs=pl.BlockSpec((rows // tiles, columns), lambda i: (i, 0)),
        out_shape=jax.ShapeDtypeStruct((rows, columns), LOW),
        compiler_params=params(),
        cost_estimate=cost(count * rows * columns, 4 * count * rows * columns),
    )(parts, *others)


def widen_kernel(n_chunks, n_outs, at_ref, *refs):
    del at_ref
    outs = refs[-n_outs:]
    widths = [ref.shape[1] for ref in outs]
    for k in range(n_chunks):

        @pl.when(pl.program_id(0) == k)
        def _():
            first = 0
            for wide, out_ref in zip(widths, outs):
                out_ref[...] = refs[k][:, first : first + wide].astype(F32)
                first += wide


def widen(places, chunks, widths, total, others):
    rows, columns = chunks[0].shape
    count = len(chunks)
    return pl.pallas_call(
        functools.partial(widen_kernel, count, len(widths)),
        grid_spec=pltpu.PrefetchScalarGridSpec(
            num_scalar_prefetch=1,
            grid=(count,),
            in_specs=[full(chunk.shape) for chunk in chunks]
            + [pl.BlockSpec(memory_space=pl.ANY)] * len(others),
            out_specs=[pl.BlockSpec((rows, wide), lambda i, at: (at[i], 0)) for wide in widths],
        ),
        out_shape=[jax.ShapeDtypeStruct((total, wide), F32) for wide in widths],
        compiler_params=params(),
        cost_estimate=cost(rows * columns, 6 * count * rows * columns),
    )(jnp.stack(places).astype(jnp.int32), *chunks, *others)


def swap_dp(rows):
    return lax.ppermute(rows, "dp", [(0, 1), (1, 0)])


def swap_context(rows, s):
    n = lax.axis_size("context")
    return lax.ppermute(rows, "context", [(i, i ^ s) for i in range(n)])


def share_context(parts):
    return lax.all_to_all(parts, "context", split_axis=0, concat_axis=0, tiled=True)


def plane_turns():
    d, c = lax.axis_index("dp"), lax.axis_index("context")
    low, high = lax.rem(c, 2), lax.div(c, 2)

    def swap(first, second):
        perm = [(i, i ^ first) for i in range(4)] + [(4 + i, 4 + (i ^ second)) for i in range(4)]
        return lambda rows: lax.ppermute(rows, GROUP_AXES, perm)

    return [
        (jnp.where(d == 0, low, high), swap(1, 2)),
        (jnp.where(d == 0, high, low), swap(2, 1)),
    ]


def plane_first(pairs, others):
    (bit_1, _), _ = plane_turns()
    return fold(pairs, bit_1, others)


def plane_second(send, keep, others):
    (_, swap_1), (bit_2, _) = plane_turns()
    return fold([(keep, swap_1(send))], bit_2, others)


def plane_last(send, keep, others):
    _, (_, swap_2) = plane_turns()
    return pair_sum(keep, swap_2(send), others)


def plane_spread(own):
    (_, swap_1), (_, swap_2) = plane_turns()
    second = swap_2(own)
    return [own, second, swap_1(own), swap_1(second)]


def quarter_places(rank):
    d = lax.axis_index("dp")
    c = lax.axis_index("context")
    low, high = lax.rem(c, 2), lax.div(c, 2)
    places = []
    for core in (d, 1 - d):
        bit_1 = jnp.where(core == 0, low, high)
        bit_2 = jnp.where(core == 0, high, low)
        for flip_1, flip_2 in ((0, 0), (0, 1), (1, 0), (1, 1)):
            places.append(4 * core + rank(core, bit_1 ^ flip_1, bit_2 ^ flip_2))
    return places


def widen_all(quarters, places, widths, others):
    count = len(quarters)
    total = 2 * count * quarters[0].shape[0]
    chunks = quarters + [swap_dp(part) for part in quarters]
    return widen(places, chunks, widths, total, others)


def arrival_order(n):
    return [sorted(range(n), key=lambda j: (abs(j - i), j)) for i in range(n)]


def choose(index, options):
    distinct = []
    for option in options:
        if option is not None and not any(option is other for other in distinct):
            distinct.append(option)
    result = distinct[0]
    for option in distinct[1:]:
        mask = functools.reduce(
            jnp.logical_or, [index == i for i, other in enumerate(options) if other is option]
        )
        result = jnp.where(mask, option, result)
    return result


def line_gather(chunk):
    return line_steps({0: chunk}, 1, lax.axis_size("expert"))


def line_steps(found, first, stop):
    n = lax.axis_size("expert")
    found = dict(found)
    for s in range(first, stop):
        found[-s] = lax.ppermute(
            found[1 - s], "expert", [(i, i + 1) for i in range(s - 1, n - 1)]
        )
        found[s] = lax.ppermute(found[s - 1], "expert", [(i + 1, i) for i in range(n - s)])
    return found


def context_gather(rows):
    n = lax.axis_size("context")
    c = lax.axis_index("context")
    found = {0: rows}
    for s in range(1, n):
        found[s] = lax.ppermute(rows, "context", [(i, i ^ s) for i in range(n)])
    return jnp.concatenate([choose(c, [found[i ^ j] for i in range(n)]) for j in range(n)], axis=0)


def zero_of(*others):
    return functools.reduce(
        jnp.add,
        [
            lax.slice(other, (0,) * other.ndim, (1,) * other.ndim).reshape(()).astype(F32) * 0.0
            for other in others
        ],
    )


def after(value, *others):
    return (value.astype(F32) + zero_of(*others)).astype(value.dtype)


def on_device(
    layer_input,
    grad_output,
    attn_gain,
    query_weight,
    key_weight,
    value_weight,
    q_gain,
    k_gain,
    output_weight,
    mlp_gain,
    router,
    w_gate,
    w_up,
    w_down,
    routes,
    half_order,
):
    n_context = lax.axis_size("context")
    n_expert = lax.axis_size("expert")
    n_groups = lax.axis_size(GROUP_AXES)
    tok_dev, width = layer_input.shape[1:]
    size = q_gain.shape[0]
    kv_total = key_weight.shape[1] * n_expert
    group_dev = n_expert // (kv_total // size)
    kv_index = lax.axis_index("expert") // group_dev
    block = tok_dev * n_expert
    seq = block * n_context
    half = block // 2
    experts = router.shape[1]
    exp_dev = w_gate.shape[0]
    top = routes.shape[2]
    capacity = max(2, (tok_dev * top * 9 + 8 * experts - 1) // (8 * experts))
    scale = size ** (-0.5)

    seq_rows = jnp.arange(seq, dtype=jnp.int32)
    context = lax.axis_index("context")
    own_halves = lax.dynamic_slice_in_dim(half_order, 2 * context, 2)
    own_pos = (own_halves[:, None] * half + jnp.arange(half, dtype=jnp.int32)[None]).reshape(-1)
    per_half = half // TILE
    tile_pos = (half_order[:, None] * per_half + jnp.arange(per_half, dtype=jnp.int32)).reshape(-1)
    kidx = jnp.sum(
        (tile_pos[None, :] == jnp.arange(seq // TILE, dtype=jnp.int32)[:, None])
        * jnp.arange(seq // TILE, dtype=jnp.int32)[None, :],
        axis=1,
    ).astype(jnp.int32)
    qpos = lax.dynamic_slice_in_dim(tile_pos, context * (block // TILE), block // TILE)
    entry = jnp.arange(size)
    freq = jnp.power(THETA, -(2 * (entry % (size // 2))).astype(F32) / size)
    angles = own_pos.astype(F32)[:, None] * freq[None, :]
    cos2 = jnp.cos(angles)
    sin2 = jnp.sin(angles) * jnp.where(entry < size // 2, -1.0, 1.0)[None, :]

    place = lax.axis_index("expert")
    place_1 = place.astype(jnp.int32)[None]
    lanes = -(-2 * experts // 128) * 128
    mask = jnp.any(
        routes[0][:, :, None] == jnp.arange(lanes, dtype=jnp.int32)[None, None, :], axis=1
    )
    mask_wide = mask.astype(F32)
    router_rows = router.T

    x_low = layer_input[0]
    x_normal, _ = norm_parts(x_low.astype(F32))
    normed_found = line_gather((x_normal * attn_gain).astype(LOW))
    if group_dev == 1:
        kv_weights = jnp.concatenate([key_weight, value_weight], axis=1)
    else:
        key_whole = lax.all_gather(key_weight, "expert", axis=1, tiled=True)
        value_whole = lax.all_gather(value_weight, "expert", axis=1, tiled=True)
        kv_weights = jnp.concatenate(
            [
                lax.dynamic_slice_in_dim(key_whole, kv_index * size, size, 1),
                lax.dynamic_slice_in_dim(value_whole, kv_index * size, size, 1),
            ],
            axis=1,
        )
    grad_low = grad_output[0]
    normed_rows, own_kv, key_proj, grad_wide = project_keys(
        place_1,
        normed_found,
        kv_weights,
        k_gain,
        cos2,
        sin2,
        scale * LOG2E,
        grad_low,
        mask_wide,
    )
    grad_col = lax.all_gather(grad_wide, "expert", axis=0, tiled=True)
    kv_whole = context_gather(own_kv)
    queries, query_proj = project_queries(normed_rows, query_weight, q_gain, cos2, sin2)

    n_half = n_expert // 2
    order_here = jnp.asarray(arrival_order(n_expert), jnp.int32)[place]
    turn_here = jnp.sum(
        (order_here[:, None] == jnp.arange(n_expert, dtype=jnp.int32)[None, :])
        * jnp.arange(n_expert, dtype=jnp.int32)[:, None],
        axis=0,
    ).astype(jnp.int32)
    meta = jnp.concatenate([place_1, turn_here, order_here])
    grad_sent, slots = make_slots(meta, grad_col, width, n_groups, capacity)
    spreads, back_tables = make_tables(meta, slots, n_half, capacity)

    def swap_plane(rows):
        parts = rows.reshape(n_groups, -1, rows.shape[1])
        parts = lax.all_to_all(parts, GROUP_AXES, split_axis=0, concat_axis=0, tiled=True)
        return parts.reshape(rows.shape)

    attended, inverse = attend(qpos, kidx, queries, kv_whole, [])
    keys_t = kv_whole[:, :size].T
    attn_part = out_dot(attended, output_weight, [grad_col])
    attn_rows = lax.psum_scatter(attn_part, "expert", scatter_dimension=0, tiled=True)

    grad_x = swap_plane(grad_sent)
    act_pull = dot_nt(grad_x, w_down[0]).reshape(n_groups, 2, n_half * capacity, -1)

    hidden, mixed, probs = route_rows(
        x_low, attn_rows, mlp_gain, router_rows, mask_wide, experts, [keys_t]
    )

    who = (lax.axis_index(ALL_AXES) * exp_dev).astype(jnp.int32)[None]
    mixed_found = line_gather(mixed)
    near = spread_rows(place_1, spreads[0], mixed_found, range(n_half), [grad_x])
    x_near = swap_plane(near)
    worked_near = run_expert(who, x_near, w_gate[0], w_up[0], act_pull, 0, experts)
    far = spread_rows(place_1, spreads[1], mixed_found, range(n_half, n_expert), [x_near])
    x_far = swap_plane(far)
    worked_far = run_expert(who, x_far, w_gate[0], w_up[0], act_pull, 1, experts)
    xs = [x_near, x_far]
    acts, gate_lows, up_lows, copies = (list(pair) for pair in zip(worked_near, worked_far))
    back_far = swap_plane(copies[1])
    back_near = swap_plane(copies[0])
    join = lambda parts: jnp.concatenate(parts, axis=0)
    x_all = join([x[:, :width] for x in xs])
    grad_w_gate = dot_tn(x_all, join(gate_lows))
    grad_w_up = dot_tn(x_all, join(up_lows))
    grad_by_round = jnp.swapaxes(
        grad_x.reshape(n_groups, 2, n_half * capacity, width), 0, 1
    ).reshape(-1, width)
    grad_w_down = dot_tn(join(acts), grad_by_round)
    copies_col = combine_rows(
        meta, back_tables, [back_near, back_far], n_half, [grad_w_gate, grad_w_up]
    )
    copies_sum = lax.psum_scatter(copies_col, "expert", scatter_dimension=0, tiled=True)

    returned = [dot_nn(act, w_down[0]).astype(LOW) for act in acts]
    returned_near = swap_plane(returned[0])

    grad_hidden, grad_hidden_low, grad_mlp_gain, grad_router = route_back(
        copies_sum,
        grad_low,
        hidden,
        mlp_gain,
        router_rows,
        mask_wide,
        probs,
        experts,
        [returned_near, grad_w_down],
    )

    returned_far = swap_plane(returned[1])
    grad_attn = lax.all_gather(grad_hidden_low, "expert", axis=0, tiled=True)
    grad_o, centre = grad_attended(
        grad_attn, output_weight, attended, inverse, [returned_far]
    )
    combined = combine_rows(meta, back_tables, [returned_near, returned_far], n_half, [])
    output_rows = lax.psum_scatter(combined, "expert", scatter_dimension=0, tiled=True)
    w_out_send, w_out_keep = token_halves(attended, grad_attn, [combined])
    w_out_half = pair_sum(w_out_keep, swap_dp(w_out_send), [grad_o])
    w_out_parts = share_context(w_out_half.reshape(n_context, -1, width))
    grad_kv, grad_q, grad_q_gain = attend_back(
        qpos,
        kidx,
        queries,
        grad_o,
        centre,
        kv_whole,
        keys_t,
        query_proj,
        q_gain,
        cos2,
        sin2,
        [w_out_half],
    )
    kv_parts = share_context(grad_kv.astype(LOW).reshape(n_context, block, 2 * size))
    w_out_own = part_sum(w_out_parts, [grad_kv])
    w_query_send, w_query_keep = token_halves(normed_rows, grad_q, [w_out_own])
    w_query_got = swap_dp(w_query_send)
    output_rows = hidden + output_rows.astype(F32) + zero_of(w_query_keep)

    kv_grads, grad_k_gain = kv_back(
        kv_parts, key_proj, k_gain, cos2, sin2, scale, [w_query_keep]
    )
    w_out_quarters = plane_spread(w_out_own)
    pairs = [(w_query_keep, w_query_got)]
    widths = [query_weight.shape[1]]
    if group_dev == 1:
        w_kv_send, w_kv_keep = token_halves(normed_rows, kv_grads, [])
        pairs.append((w_kv_keep, swap_dp(w_kv_send)))
        widths += [key_weight.shape[1], value_weight.shape[1]]
    grad_normed, gain_rows = normed_back(
        grad_q, kv_grads, query_weight, kv_weights, normed_rows, []
    )
    send, keep = plane_first(pairs, [grad_normed])
    (grad_w_out,) = widen_all(
        w_out_quarters,
        quarter_places(lambda core, b1, b2: jnp.where(core == 0, b1 + 2 * b2, 2 * b1 + b2)),
        [width],
        [],
    )
    small = pack_small(
        experts,
        grad_router,
        gain_rows,
        attn_gain,
        grad_mlp_gain,
        grad_q_gain,
        grad_k_gain,
        [],
    )
    swap_all = lambda rows: lax.all_to_all(rows, ALL_AXES, split_axis=0, concat_axis=0, tiled=True)
    small_parts = swap_all(small.reshape(lax.axis_size(ALL_AXES), -1, width))
    small_own = jnp.sum(small_parts.astype(F32), axis=0).astype(LOW)
    second_send, second_keep = plane_second(
        send, keep, [small_own, output_rows, *w_out_quarters[1:3]]
    )
    grad_normed = lax.psum_scatter(grad_normed, "expert", scatter_dimension=0, tiled=True)
    grad_input = input_back(grad_normed, x_low, attn_gain, grad_hidden)
    small_sum = swap_all(jnp.broadcast_to(small_own[None], small_parts.shape))
    quarter = plane_last(
        second_send, second_keep, [grad_input, grad_w_out, small_sum]
    )
    grad_router, grad_attn_gain, grad_mlp_gain, grad_q_gain, grad_k_gain = unpack_small(
        small_sum.reshape(small.shape), experts, size, []
    )
    quarters = plane_spread(quarter)
    places = quarter_places(lambda core, b1, b2: 2 * b1 + b2)
    grad_w_query, *more = widen_all(quarters, places, widths, [])
    if group_dev == 1:
        grad_w_key, grad_w_value = more
    else:
        w_kv = token_dot(normed_rows, kv_grads, [])
        blank = jnp.zeros((width, kv_total), LOW)
        pieces = []
        for part in (w_kv[:, :size], w_kv[:, size:]):
            padded = lax.dynamic_update_slice(blank, part, (0, kv_index * size))
            pieces.append(lax.psum_scatter(padded, "expert", scatter_dimension=1, tiled=True))
        grad_w_key, grad_w_value = (lax.psum(piece, GROUP_AXES).astype(F32) for piece in pieces)
    return (
        output_rows.astype(LOW)[None],
        grad_input[None],
        grad_attn_gain[0],
        grad_w_query,
        grad_w_key,
        grad_w_value,
        grad_q_gain[0],
        grad_k_gain[0],
        grad_w_out,
        grad_mlp_gain[0],
        grad_router.T,
        grad_w_gate[None],
        grad_w_up[None],
        grad_w_down[None],
    )


def solution(mesh):
    rows = P("dp", ("context", "expert"), None)
    expert = P(ALL_AXES, None, None)
    columns = P(None, "expert")
    in_specs = (
        rows,
        rows,
        P(),
        columns,
        columns,
        columns,
        P(),
        P(),
        P("expert", None),
        P(),
        P(),
        expert,
        expert,
        expert,
        rows,
        P(),
    )
    out_specs = (
        rows,
        rows,
        P(),
        columns,
        columns,
        columns,
        P(),
        P(),
        P("expert", None),
        P(),
        P(),
        expert,
        expert,
        expert,
    )
    return jax.shard_map(
        on_device, mesh=mesh, in_specs=in_specs, out_specs=out_specs, check_vma=False
    )
```
